32 devices in a mesh: dp: 16 (over z, y, core), expert: 2 (over x).
Axes of the slice: x: 2, y: 2, z: 4, core: 2. Of those that a mesh axis runs over, the one named last changes fastest.
Arguments:
- tokens: bfloat16 [8192, 1536], P(('dp', 'expert')), may hold values from -6 to 6
- norm1_gain: bfloat16 [1536], P('dp'), may hold values from 0.5 to 1.5
- w_query: bfloat16 [1536, 1536], P('dp'), may hold values from -0.15625 to 0.15625
- w_key: bfloat16 [1536, 256], P('dp'), may hold values from -0.15625 to 0.15625
- w_value: bfloat16 [1536, 256], P('dp'), may hold values from -0.15625 to 0.15625
- w_out: bfloat16 [1536, 1536], P('dp'), may hold values from -0.625 to 0.625
- norm2_gain: bfloat16 [1536], P('dp'), may hold values from 0.5 to 1.5
- w_router: bfloat16 [1536, 8], P('dp'), may hold values from -0.06982422 to 0.06982422
- w_gate: bfloat16 [8, 1536, 768], P('expert'), may hold values from -0.15625 to 0.15625
- w_up: bfloat16 [8, 1536, 768], P('expert'), may hold values from -0.15625 to 0.15625
- w_down: bfloat16 [8, 768, 1536], P('expert'), may hold values from -0.44921875 to 0.44921875
- expert_ids: int32 [8192, 4], P(('dp', 'expert')), may hold values from 0 to 7, all different within a row; in each aligned block of 128 rows (0 to 127, 128 to 255, ...) at most 96 rows name the same one
- prefix_len: int32 [32], P(('dp', 'expert')), may hold values from 25 to 128
- out_grad: bfloat16 [8192, 1536], P(('dp', 'expert')), may hold values from -6 to 6
Outputs:
- block_out: bfloat16 [8192, 1536], P(('dp', 'expert'))
- tokens_grad: bfloat16 [8192, 1536], P(('dp', 'expert'))
- norm1_grad: float32 [1536], P('dp')
- query_grad: float32 [1536, 1536], P('dp')
- key_grad: float32 [1536, 256], P('dp')
- value_grad: float32 [1536, 256], P('dp')
- outproj_grad: float32 [1536, 1536], P('dp')
- norm2_grad: float32 [1536], P('dp')
- router_grad: float32 [1536, 8], P('dp')
- gate_grad: float32 [8, 1536, 768], P('expert', 'dp')
- up_grad: float32 [8, 1536, 768], P('expert', 'dp')
- down_grad: float32 [8, 768, 1536], P('expert', None, 'dp')
The draws below stay inside these ranges and needn't reach their ends.
Inputs may be any that keep to these rules, and one draw needn't show every extreme that they name: `expert_ids`: each row names 4 different experts. Within the rows of one device's micro-batch (aligned blocks of 128 rows) no expert is named by more than 96 rows, and some block reaches 96.
All inputs are finite; a program needn't handle non-finite values.
Results may differ from the reference program's by a relative error of at most 0.024.
Values may be sent and summed in bfloat16 or wider, within the bound.
No kernel may reach another device: no remote copies, remote signals or barrier semaphores. Data moves between devices by JAX's collectives and lax.ppermute only.
A program may use at most 192 MiB of HBM per device.

```python
import math
import jax
import jax.numpy as jnp
import numpy as np
from jax import lax

D = 1536
HQ = 12
HK = 2
HD = 128
FF = 768
TOP = 4
MICRO = 2
SEQ = 256
NSEQ = 32
TOKENS = 8192
EXPERTS = 8
CAP = 96


def touch_ends(array, key, least, largest):
    index_at = [jax.random.randint(jax.random.fold_in(key, axis), (), 0, length) for axis, length in enumerate(array.shape)]
    longest = array.shape.index(max(array.shape))
    neighbour = index_at[:longest] + [(index_at[longest] + 1) % array.shape[longest]] + index_at[longest + 1:]
    return array.at[tuple(index_at)].set(least).at[tuple(neighbour)].set(largest)


def steps_of(own_key, shape, split, smallest, largest):
    def one(dim, parts):
        draws = jax.random.uniform(jax.random.fold_in(jax.random.fold_in(own_key, 6), dim), (parts,), jnp.float32, smallest / len(split), largest / len(split))
        return jnp.repeat(jnp.exp(draws), shape[dim] // parts).reshape((-1,) + (1,) * (len(shape) - dim - 1))

    factor_of = one(*split[0])
    for cut in split[1:]:
        factor_of = factor_of * one(*cut)
    return factor_of


def deal_out(own_key, own, number, rows, number_of, top, most, lean):
    order = jax.random.permutation(own_key, number_of)
    packed, common = portions_of(number_of, rows * top, most, lean, True), portions_of(number_of, rows * top, most, lean, False)
    places = jnp.arange(number_of)

    def named(lengths, offset_by):
        used = int((lengths > 0).sum())
        fixed = max(1, used // 4)
        moved = fixed + (places - fixed + offset_by * (used - fixed)) % max(1, number_of - fixed)
        return jnp.zeros((number_of,), jnp.int32).at[order[jnp.where(places < fixed, places, moved)]].set(jnp.asarray(lengths, jnp.int32))

    lengths = jnp.where(number % 4 == 0, named(packed, number // 4), named(common, number - number // 4 - 1))
    mixed = jax.random.permutation(jax.random.fold_in(own, 3), number_of)
    donor, sink = mixed[0:number_of // 2 * 2:2], mixed[1:number_of // 2 * 2:2]
    room = jnp.minimum(lengths[donor] - 1, most - lengths[sink]) // 2
    room = jnp.where((donor == order[0]) | (sink == order[0]) | (lengths[sink] == 0), 0, jnp.maximum(room, 0))
    moved = jax.random.randint(jax.random.fold_in(own, 4), (number_of // 2,), 0, 1 << 20) % (room + 1)
    lengths = lengths.at[donor].add(-moved).at[sink].add(moved)
    members = jnp.searchsorted(jnp.cumsum(lengths), jnp.arange(rows * top), side="right").astype(jnp.int32)
    listing = members.reshape(top, rows).T
    listing = listing[jax.random.permutation(jax.random.fold_in(own, 1), rows)]
    offset_by = jax.random.randint(jax.random.fold_in(own, 2), (rows, 1), 0, top)
    return jnp.take_along_axis(listing, (jnp.arange(top)[None, :] + offset_by) % top, axis=1)


def portions_of(amount, total, limit, lean, full):
    portions = [(1 << 20) // math.isqrt(rank ** lean) + 1 for rank in range(1, amount + 1)]
    largest = limit if full else min(limit, max(-(-total // amount), total * portions[0] // sum(portions)))
    least = 1 if total - largest >= amount - 1 else 0
    holding, spare = [largest] + [least] * (amount - 1), total - largest - least * (amount - 1)
    while spare > 0:
        candidates = [i for i in range(1, amount) if holding[i] < largest] or [i for i in range(1, amount) if holding[i] < limit]
        pool, budget = sum([portions[i] for i in candidates]), spare
        for i in candidates:
            addition = min(limit - holding[i], max(1, budget * portions[i] // pool), spare)
            holding[i] = holding[i] + addition
            spare = spare - addition
    return np.array(holding)


def noise(rng, shape, width, most, cuts=(), held_as=jnp.bfloat16):
    array = jax.random.normal(rng, shape, jnp.float32) * width
    if len(cuts) > 0:
        array = steps_of(rng, shape, cuts, -0.22, 0.18) * array
    return jnp.clip(array, min=-most, max=most).astype(held_as)


def setup_inputs(seed: int = 0) -> dict:
    keys = jax.random.split(jax.random.key(seed), 15)
    tokens = noise(keys[0], (TOKENS, D), 1.0, 6.0, ((0, 32),))
    norm1_gain = jnp.clip(1.0 + 0.1 * jax.random.normal(keys[1], (D,), jnp.float32), 0.5, 1.5).astype(jnp.bfloat16)
    w_query = noise(keys[2], (D, HQ * HD), D ** -0.5, 0.15625, ((0, 16),))
    w_key = noise(keys[3], (D, HK * HD), D ** -0.5, 0.15625, ((0, 16),))
    w_value = noise(keys[4], (D, HK * HD), D ** -0.5, 0.15625, ((0, 16),))
    w_out = noise(keys[5], (HQ * HD, D), (D // 16) ** -0.5, 0.625, ((0, 16),))
    norm2_gain = jnp.clip(1.0 + 0.1 * jax.random.normal(keys[6], (D,), jnp.float32), 0.5, 1.5).astype(jnp.bfloat16)
    w_router = noise(keys[7], (D, EXPERTS), 0.0128, 0.06982422, ((0, 16),))
    w_gate = noise(keys[8], (EXPERTS, D, FF), D ** -0.5, 0.15625, ((0, 2),))
    w_up = noise(keys[9], (EXPERTS, D, FF), D ** -0.5, 0.15625, ((0, 2),))
    w_down = noise(keys[10], (EXPERTS, FF, D), 0.072, 0.44921875, ((0, 2),))
    expert_ids_keys = jax.random.split(jax.random.fold_in(keys[11], 1), TOKENS // (SEQ // MICRO))
    expert_ids_turns = jax.random.permutation(jax.random.fold_in(keys[11], 3), TOKENS // (SEQ // MICRO))
    expert_ids = jax.vmap(lambda own, number: deal_out(jax.random.fold_in(keys[11], 2), own, number, SEQ // MICRO, EXPERTS, TOP, CAP, 1))(expert_ids_keys, expert_ids_turns).reshape((TOKENS, TOP))
    prefix_len = touch_ends(jax.random.randint(keys[12], (NSEQ,), SEQ // 10, SEQ // 2 + 1), jax.random.fold_in(keys[12], 1), SEQ // 10, (SEQ // 2 + 1) - 1).astype(jnp.int32)
    out_grad = noise(keys[13], (TOKENS, D), 1.0, 6.0, ((0, 32),))
    return dict(tokens=tokens, norm1_gain=norm1_gain, w_query=w_query, w_key=w_key, w_value=w_value, w_out=w_out, norm2_gain=norm2_gain, w_router=w_router, w_gate=w_gate, w_up=w_up, w_down=w_down, expert_ids=expert_ids, prefix_len=prefix_len, out_grad=out_grad)


@jax.custom_vjp
def low(v):
    return lax.optimization_barrier(v.astype(jnp.bfloat16)).astype(jnp.float32)

@jax.custom_vjp
def low_back(v):
    return v

def low_keep(v):
    return (low(v), None)

def low_pass(kept, grad):
    return (grad,)

def back_keep(v):
    return (v, None)

def back_low(kept, grad):
    return (low(grad),)
low.defvjp(low_keep, low_pass)
low_back.defvjp(back_keep, back_low)

def rms_scale(values, gain_vec):
    inverse = lax.rsqrt(lax.optimization_barrier(jnp.mean(values * values, axis=-1, keepdims=True)) + 1e-06)
    return values * inverse * gain_vec

def angles(length, head_size):
    positions = jnp.arange(length).astype(jnp.float32)
    freq_rates = jnp.exp(-(2.0 * jnp.arange(head_size // 2).astype(jnp.float32) / head_size) * math.log(1000000.0))
    angle_tab = positions[:, None] * freq_rates[None, :]
    return (jnp.cos(angle_tab)[:, None, :], jnp.sin(angle_tab)[:, None, :])

def rotary(values, cosine_tab, sine_tab):
    half_dim = values.shape[-1] // 2
    first_half = values[..., :half_dim]
    second_half = values[..., half_dim:]
    return jnp.concatenate([first_half * cosine_tab - second_half * sine_tab, second_half * cosine_tab + first_half * sine_tab], axis=-1)

def block_forward(inputs_f, gain_one, query_w, key_w, value_w, output_w, gain_two, router_w, gate_w, up_w, down_w, ids_block, prefix_block):
    batch_seqs = inputs_f.shape[0]
    highest = lax.Precision.HIGHEST
    cosine_tab, sine_tab = angles(SEQ, HD)
    first_in = low(rms_scale(inputs_f, gain_one))
    query_pre = low_back(jnp.einsum('gsd,de->gse', first_in, query_w, precision=highest).reshape(batch_seqs, SEQ, HQ, HD))
    queries = low(rotary(query_pre, cosine_tab, sine_tab)).reshape(batch_seqs, SEQ, HK, HQ // HK, HD)
    key_pre = low_back(jnp.einsum('gsd,de->gse', first_in, key_w, precision=highest).reshape(batch_seqs, SEQ, HK, HD))
    keys_rot = low(rotary(key_pre, cosine_tab, sine_tab))
    values_r = low(low_back(jnp.einsum('gsd,de->gse', first_in, value_w, precision=highest).reshape(batch_seqs, SEQ, HK, HD)))
    scores = low_back(jnp.einsum('gihrd,gjhd->ghrij', queries, keys_rot, precision=highest) * HD ** (-0.5))
    positions = jnp.arange(SEQ)
    allowed = (positions[None, None, :] <= positions[None, :, None]) | (positions[None, None, :] < prefix_block[:, None, None])
    masked = jnp.where(allowed[:, None, None, :, :], scores, -1e+30)
    prob_low = low(jax.nn.softmax(masked, axis=-1))
    attended = jnp.einsum('ghrij,gjhd->gihrd', prob_low, values_r, precision=highest).reshape(batch_seqs, SEQ, HQ * HD)
    attended = low(low_back(attended))
    resid = inputs_f + low_back(jnp.einsum('gse,ed->gsd', attended, output_w, precision=highest))
    second_in = low(rms_scale(resid, gain_two))
    logits = low_back(jnp.einsum('gsd,de->gse', second_in, router_w, precision=highest))
    onehot = (ids_block[..., None] == jnp.arange(EXPERTS)[None, None, None, :]).astype(jnp.float32)
    chosen = lax.optimization_barrier(jnp.sum(onehot * logits[:, :, None, :], axis=-1))
    gate_probs = jax.nn.softmax(chosen, axis=-1)
    shares = lax.optimization_barrier(jnp.sum(onehot * gate_probs[..., None], axis=2)).reshape(batch_seqs * SEQ, EXPERTS).T
    flat_in = second_in.reshape(batch_seqs * SEQ, D)

    def expert_step(mixture, pieces):
        gate_mat, up_mat, down_mat, share_col = pieces
        gate_pre = low_back(jnp.dot(flat_in, gate_mat, precision=highest))
        up_pre = low_back(jnp.dot(flat_in, up_mat, precision=highest))
        hidden = low(jax.nn.gelu(gate_pre, approximate=True) * up_pre)
        expert_out = low(low_back(jnp.dot(hidden, down_mat, precision=highest)))
        return (mixture + share_col[:, None] * expert_out, None)
    mixture, _ = lax.scan(jax.checkpoint(expert_step), jnp.zeros((batch_seqs * SEQ, D), jnp.float32), (gate_w, up_w, down_w, shares))
    return resid + mixture.reshape(batch_seqs, SEQ, D)

def reference(tokens, norm1_gain, w_query, w_key, w_value, w_out, norm2_gain, w_router, w_gate, w_up, w_down, expert_ids, prefix_len, out_grad):
    group_seqs = math.gcd(NSEQ, max(1, 4096 // SEQ))
    scan_steps = NSEQ // group_seqs
    params = tuple((weight.astype(jnp.float32) for weight in (norm1_gain, w_query, w_key, w_value, w_out, norm2_gain, w_router, w_gate, w_up, w_down)))
    inputs_all = tokens.astype(jnp.float32).reshape(scan_steps, group_seqs, SEQ, D)
    cot_all = out_grad.astype(jnp.float32).reshape(scan_steps, group_seqs, SEQ, D)
    ids_all = expert_ids.reshape(scan_steps, group_seqs, SEQ, TOP)
    prefix_all = prefix_len.reshape(scan_steps, group_seqs)

    def one_step(totals, pieces):
        inputs_blk, cot_blk, ids_blk, prefix_blk = pieces

        def run_block(inputs_f, *weights):
            return block_forward(inputs_f, *weights, ids_blk, prefix_blk)
        result, pullback = jax.vjp(run_block, inputs_blk, *params)
        gradients = pullback(cot_blk)
        totals = tuple((left + right for left, right in zip(totals, gradients[1:])))
        return (totals, (result.astype(jnp.bfloat16), gradients[0].astype(jnp.bfloat16)))
    start_tot = tuple((jnp.zeros_like(weight) for weight in params))
    totals, (results, input_grads) = lax.scan(one_step, start_tot, (inputs_all, cot_all, ids_all, prefix_all))
    return (results.reshape(TOKENS, D), input_grads.reshape(TOKENS, D), totals[0], totals[1], totals[2], totals[3], totals[4], totals[5], totals[6], totals[7], totals[8], totals[9])
```

```python
import math

import jax
import jax.numpy as jnp
from jax import lax
from jax.sharding import PartitionSpec as P

HQ = 12
HK = 2
HD = 128
MICRO = 2
PLANE = ("y", "c", "x")
GROUP = ("z", "y", "c")


def rms_scale(values, gain_vec):
    inverse = lax.rsqrt(jnp.mean(values * values, axis=-1, keepdims=True) + 1e-06)
    return values * inverse * gain_vec


def angles(length, head_size):
    positions = jnp.arange(length).astype(jnp.float32)
    freq_rates = jnp.exp(
        -(2.0 * jnp.arange(head_size // 2).astype(jnp.float32) / head_size) * math.log(1000000.0)
    )
    angle_tab = positions[:, None] * freq_rates[None, :]
    return (jnp.cos(angle_tab)[:, None, :], jnp.sin(angle_tab)[:, None, :])


def rotary(values, cosine_tab, sine_tab):
    half_dim = values.shape[-1] // 2
    first_half = values[..., :half_dim]
    second_half = values[..., half_dim:]
    return jnp.concatenate(
        [
            first_half * cosine_tab - second_half * sine_tab,
            second_half * cosine_tab + first_half * sine_tab,
        ],
        axis=-1,
    )


def expert_act(gate_pre, up_pre):
    return jax.nn.gelu(gate_pre, approximate=True) * up_pre


def left_product(left_mat, right_mat):
    return lax.dot_general(
        left_mat, right_mat, (((0,), (0,)), ((), ())), preferred_element_type=jnp.float32
    )


def gather(block, axes):
    return lax.all_gather(block, axes, axis=0, tiled=True)


def exchange(block, axes):
    return lax.all_to_all(block, axes, split_axis=0, concat_axis=0, tiled=True)


def scatter_sum(block, axes):
    return lax.psum_scatter(block, axes, scatter_dimension=0, tiled=True)


def by_owner(cols, parts):
    rows, total = cols.shape
    return jnp.moveaxis(cols.reshape(rows, parts, total // parts), 1, 0).reshape(
        parts * rows, total // parts
    )


def local(
    tokens,
    norm1_gain,
    w_query,
    w_key,
    w_value,
    w_out,
    norm2_gain,
    w_router,
    w_gate,
    w_up,
    w_down,
    expert_ids,
    prefix_len,
    out_grad,
):
    bf16, f32 = jnp.bfloat16, jnp.float32
    length, model_width = tokens.shape
    shard_rows = w_query.shape[0]
    local_count, _, hidden_width = w_gate.shape
    owners = lax.axis_size("x")
    depth = lax.axis_size("z")
    plane = lax.axis_size(PLANE)
    experts_all = w_router.shape[1]
    top_count = expert_ids.shape[1]
    block_rows = length // MICRO
    capacity = 3 * block_rows * top_count // (2 * experts_all)
    plane_rows = plane * length
    blocks = plane_rows // block_rows
    group_size = HQ // HK
    score_scale = HD ** (-0.5)
    q_cols, kv_cols = w_query.shape[1], w_key.shape[1]
    own_local = lax.axis_index(("y", "c"))
    own_expert = lax.axis_index("x") * local_count + own_local
    own_place = lax.axis_index(PLANE)

    narrow = jnp.concatenate([w_router, norm1_gain[:, None], norm2_gain[:, None]], axis=1)
    narrow = jnp.pad(narrow, ((0, 0), (0, -narrow.shape[1] % 128)))
    packed = gather(jnp.concatenate([w_query, w_key, w_value, narrow], axis=1), GROUP)
    qkv_cols = q_cols + 2 * kv_cols
    qkv_w = packed[:, :qkv_cols]
    router_w = packed[:, qkv_cols : qkv_cols + experts_all]
    gains = packed[:, qkv_cols + experts_all : qkv_cols + experts_all + 2].T.astype(f32)
    gain_one, gain_two = gains[0], gains[1]
    output_w = gather(w_out, GROUP)

    ids_all = gather(expert_ids, PLANE)
    cot_all = gather(out_grad, PLANE)
    chosen_mask = jnp.any(
        ids_all[:, :, None] == jnp.arange(experts_all, dtype=jnp.int32)[None, None, :], axis=1
    )
    own_mask = jnp.any(ids_all == own_expert, axis=1).reshape(blocks, block_rows)
    place = jnp.cumsum(own_mask.astype(jnp.int32), axis=1) - 1
    dispatch = (
        own_mask[:, None, :]
        & (place[:, None, :] == jnp.arange(capacity, dtype=jnp.int32)[None, :, None])
    ).astype(bf16)

    cosine_tab, sine_tab = angles(length, HD)
    inputs_f = tokens.astype(f32)
    first_in = rms_scale(inputs_f, gain_one).astype(bf16)
    qkv = jnp.dot(first_in, qkv_w, preferred_element_type=f32)
    queries = (
        rotary(qkv[:, :q_cols].reshape(length, HQ, HD), cosine_tab, sine_tab)
        .astype(bf16)
        .reshape(length, HK, group_size, HD)
    )
    keys_rot = rotary(
        qkv[:, q_cols : q_cols + kv_cols].reshape(length, HK, HD), cosine_tab, sine_tab
    ).astype(bf16)
    values_b = qkv[:, q_cols + kv_cols :].astype(bf16).reshape(length, HK, HD)
    positions = jnp.arange(length)
    allowed = (positions[None, :] <= positions[:, None]) | (positions[None, :] < prefix_len[0])

    def masked_scores():
        scores = jnp.einsum("ihrd,jhd->hrij", queries, keys_rot, preferred_element_type=f32)
        return jnp.where(allowed, scores * score_scale, -1e30)

    masked = masked_scores()
    row_peak = jnp.max(masked, axis=-1, keepdims=True)
    log_total = row_peak + jnp.log(jnp.sum(jnp.exp(masked - row_peak), axis=-1, keepdims=True))
    prob_bf = jnp.exp(masked - log_total).astype(bf16)
    attended = jnp.einsum("hrij,jhd->ihrd", prob_bf, values_b, preferred_element_type=f32)
    attended = attended.reshape(length, HQ * HD).astype(bf16)
    resid = inputs_f + jnp.dot(attended, output_w, preferred_element_type=f32)
    second_in = rms_scale(resid, gain_two).astype(bf16)

    second_all = gather(second_in, PLANE)
    logits = jnp.dot(second_all, router_w, preferred_element_type=f32)
    gates_all = jax.nn.softmax(jnp.where(chosen_mask, logits, -jnp.inf), axis=-1)
    own_gates = lax.dynamic_index_in_dim(gates_all, own_expert, 1, keepdims=False)
    own_gates = own_gates.reshape(blocks, block_rows)
    gate_rows = jnp.einsum(
        "bct,bt->bc", dispatch.astype(f32), own_gates, precision=lax.Precision.HIGHEST
    )[:, :, None]
    gate_w = lax.dynamic_index_in_dim(w_gate, own_local, 0, keepdims=False)
    up_w = lax.dynamic_index_in_dim(w_up, own_local, 0, keepdims=False)
    down_w = lax.dynamic_index_in_dim(w_down, own_local, 0, keepdims=False)

    def to_rows(array):
        return jnp.einsum(
            "bct,btd->bcd",
            dispatch,
            array.reshape(blocks, block_rows, model_width),
            preferred_element_type=f32,
        ).astype(bf16)

    def to_tokens(rows):
        return (
            jnp.einsum("bct,bcd->btd", dispatch, rows.astype(bf16), preferred_element_type=f32)
            .astype(bf16)
            .reshape(plane_rows, model_width)
        )

    rows_in = to_rows(second_all)
    rows_cot = to_rows(cot_all)
    gate_pre = jnp.einsum("bcd,df->bcf", rows_in, gate_w, preferred_element_type=f32)
    up_pre = jnp.einsum("bcd,df->bcf", rows_in, up_w, preferred_element_type=f32)
    hidden, act_pull = jax.vjp(expert_act, gate_pre, up_pre)
    gated = (gate_rows * hidden).astype(bf16)
    down_part = jnp.einsum("bcd,bcf->df", rows_cot, gated, preferred_element_type=f32)
    down_sum = scatter_sum(down_part.astype(bf16), "z")
    cot_hidden = jnp.einsum("bcd,fd->bcf", rows_cot, down_w, preferred_element_type=f32)
    gate_signal_rows = jnp.sum(hidden * cot_hidden, axis=-1)
    gate_pgrad, up_pgrad = act_pull(gate_rows * cot_hidden)
    gate_pgrad = gate_pgrad.astype(bf16)
    up_pgrad = up_pgrad.astype(bf16)
    gate_part = jnp.einsum("bcd,bcf->df", rows_in, gate_pgrad, preferred_element_type=f32)
    gate_sum = scatter_sum(gate_part.astype(bf16), "z")
    up_part = jnp.einsum("bcd,bcf->df", rows_in, up_pgrad, preferred_element_type=f32)
    up_sum = scatter_sum(up_part.astype(bf16), "z")
    rows_grad = jnp.einsum("bcf,df->bcd", gate_pgrad, gate_w, preferred_element_type=f32)
    rows_grad = rows_grad + jnp.einsum("bcf,df->bcd", up_pgrad, up_w, preferred_element_type=f32)
    second_back = scatter_sum(to_tokens(rows_grad), PLANE).astype(f32)
    gate_signal = jnp.einsum(
        "bct,bc->bt", dispatch.astype(f32), gate_signal_rows, precision=lax.Precision.HIGHEST
    )
    gate_signal = exchange(gate_signal.reshape(plane, length), PLANE)
    gate_signal = jnp.transpose(
        gate_signal.reshape(local_count, owners, length), (2, 1, 0)
    ).reshape(length, experts_all)
    expert_rows = jnp.einsum("bcf,fd->bcd", gated, down_w, preferred_element_type=f32)
    mixture = scatter_sum(to_tokens(expert_rows), PLANE).astype(f32)
    block_out = (resid + mixture).astype(bf16)

    cotangent = out_grad.astype(f32)
    gate_probs = lax.dynamic_slice_in_dim(gates_all, own_place * length, length, 0)
    logit_grad = (
        gate_probs
        * (gate_signal - jnp.sum(gate_probs * gate_signal, axis=-1, keepdims=True))
    ).astype(bf16)
    router_acc = left_product(second_in, logit_grad)
    second_grad = second_back + jnp.dot(logit_grad, router_w.T, preferred_element_type=f32)
    _, norm_two_pull = jax.vjp(rms_scale, resid, gain_two)
    resid_norm_grad, gain_two_grad = norm_two_pull(second_grad)
    resid_grad = cotangent + resid_norm_grad
    branch_grad = resid_grad.astype(bf16)

    attended_all = gather(attended, PLANE)
    branch_cols = exchange(by_owner(branch_grad, plane), PLANE)
    output_part = left_product(attended_all, branch_cols)
    attended_grad = jnp.dot(branch_grad, output_w.T, preferred_element_type=f32).astype(bf16)
    attended_grad = attended_grad.reshape(length, HK, group_size, HD)
    masked = masked_scores()
    prob_full = jnp.exp(masked - log_total)
    prob_bf = prob_full.astype(bf16)
    prob_grad = jnp.einsum("ihrd,jhd->hrij", attended_grad, values_b, preferred_element_type=f32)
    row_inner = jnp.sum(prob_full * prob_grad, axis=-1, keepdims=True)
    score_grad = (prob_full * (prob_grad - row_inner)).astype(bf16)
    query_rot_grad = (
        jnp.einsum("hrij,jhd->ihrd", score_grad, keys_rot, preferred_element_type=f32)
        * score_scale
    )
    query_back = rotary(query_rot_grad.reshape(length, HQ, HD), cosine_tab, -sine_tab)
    query_back = query_back.astype(bf16).reshape(length, HQ * HD)
    key_rot_grad = (
        jnp.einsum("hrij,ihrd->jhd", score_grad, queries, preferred_element_type=f32)
        * score_scale
    )
    key_back = rotary(key_rot_grad, cosine_tab, -sine_tab).astype(bf16).reshape(length, HK * HD)
    value_back = jnp.einsum("hrij,ihrd->jhd", prob_bf, attended_grad, preferred_element_type=f32)
    value_back = value_back.astype(bf16).reshape(length, HK * HD)
    qkv_back = jnp.concatenate([query_back, key_back, value_back], axis=1)
    first_all = gather(first_in, PLANE)
    qkv_part = left_product(first_all, exchange(by_owner(qkv_back, plane), PLANE))
    first_grad = lax.dot_general(
        qkv_back, qkv_w, (((1,), (1,)), ((), ())), preferred_element_type=f32
    )
    _, norm_one_pull = jax.vjp(rms_scale, inputs_f, gain_one)
    input_norm_grad, gain_one_grad = norm_one_pull(first_grad)
    tokens_grad = (resid_grad + input_norm_grad).astype(bf16)

    narrow_part = jnp.concatenate(
        [router_acc, gain_one_grad[:, None], gain_two_grad[:, None]], axis=1
    ).astype(bf16)
    narrow_cols = narrow_part.shape[1]
    narrow_sum = lax.psum(scatter_sum(narrow_part, GROUP), "x").astype(f32)
    dense_part = jnp.concatenate([qkv_part, output_part], axis=1).astype(bf16)
    dense_sum = scatter_sum(dense_part, "z")
    dense_cols = dense_sum.shape[1]
    dense_sum = gather(dense_sum, PLANE).reshape(plane, local_count, shard_rows, dense_cols)
    dense_sum = lax.dynamic_index_in_dim(dense_sum, own_local, 1, keepdims=False).astype(f32)
    dense_sum = jnp.moveaxis(dense_sum, 0, 1)
    qkv_width = qkv_cols // plane
    qkv_sum = dense_sum[:, :, :qkv_width].reshape(shard_rows, qkv_cols)
    output_sum = dense_sum[:, :, qkv_width:].reshape(shard_rows, model_width)

    def placed(total):
        total = exchange(total, ("y", "c"))
        return total.reshape(local_count, shard_rows, hidden_width).astype(f32)

    return (
        block_out,
        tokens_grad,
        narrow_sum[:, experts_all],
        qkv_sum[:, :q_cols],
        qkv_sum[:, q_cols : q_cols + kv_cols],
        qkv_sum[:, q_cols + kv_cols :],
        output_sum,
        narrow_sum[:, experts_all + 1],
        narrow_sum[:, :experts_all],
        placed(gate_sum),
        placed(up_sum),
        jnp.swapaxes(placed(down_sum), 1, 2),
    )


def solution(mesh):
    groups, owners = mesh.shape["dp"], mesh.shape["expert"]
    grid = jax.sharding.Mesh(
        mesh.devices.reshape(groups // 4, 2, 2, owners), ("z", "y", "c", "x")
    )
    rows = P(("z", "y", "c", "x"), None)
    shard, shard_rows = P(GROUP), P(GROUP, None)
    expert = P("x", None, None)
    return jax.shard_map(
        local,
        mesh=grid,
        in_specs=(
            rows,
            shard,
            shard_rows,
            shard_rows,
            shard_rows,
            shard_rows,
            shard,
            shard_rows,
            expert,
            expert,
            expert,
            rows,
            P(("z", "y", "c", "x")),
            rows,
        ),
        out_specs=(
            rows,
            rows,
            shard,
            shard_rows,
            shard_rows,
            shard_rows,
            shard_rows,
            shard,
            shard_rows,
            P("x", GROUP, None),
            P("x", GROUP, None),
            P("x", None, GROUP),
        ),
        check_vma=False,
    )
```

```python
import math

import jax
import jax.numpy as jnp
from jax import lax
from jax.sharding import PartitionSpec as P

HQ = 12
HK = 2
HD = 128
MICRO = 2
PLANE = ("c", "y", "x")
GROUP = ("z", "y", "c")


def rms_scale(values, gain_vec):
    inverse = lax.rsqrt(jnp.mean(values * values, axis=-1, keepdims=True) + 1e-06)
    return values * inverse * gain_vec


def angles(length, head_size):
    positions = jnp.arange(length).astype(jnp.float32)
    freq_rates = jnp.exp(
        -(2.0 * jnp.arange(head_size // 2).astype(jnp.float32) / head_size) * math.log(1000000.0)
    )
    angle_tab = positions[:, None] * freq_rates[None, :]
    return (jnp.cos(angle_tab)[:, None, :], jnp.sin(angle_tab)[:, None, :])


def rotary(values, cosine_tab, sine_tab):
    half_dim = values.shape[-1] // 2
    first_half = values[..., :half_dim]
    second_half = values[..., half_dim:]
    return jnp.concatenate(
        [
            first_half * cosine_tab - second_half * sine_tab,
            second_half * cosine_tab + first_half * sine_tab,
        ],
        axis=-1,
    )


def expert_act(gate_pre, up_pre):
    return jax.nn.gelu(gate_pre, approximate=True) * up_pre


def left_product(left_mat, right_mat):
    return lax.dot_general(
        left_mat, right_mat, (((0,), (0,)), ((), ())), preferred_element_type=jnp.float32
    )


def gather(block, axes):
    return lax.all_gather(block, axes, axis=0, tiled=True)


def exchange(block, axes):
    return lax.all_to_all(block, axes, split_axis=0, concat_axis=0, tiled=True)


def scatter_sum(block, axes):
    return lax.psum_scatter(block, axes, scatter_dimension=0, tiled=True)


def swap(block, axis):
    return lax.ppermute(block, axis, [(0, 1), (1, 0)])


def by_pairs():
    return lax.axis_size("x") == 2


def plane_gather(block):
    if not by_pairs():
        return gather(block, PLANE)
    half = block.shape[0] // 2
    over_c = swap(block, "c")
    over_y = swap(block, "y")
    over_x = swap(block, "x")
    over_both = [swap(over_y[:half], "x"), swap(over_x[half:], "y")]
    others = [over_x, over_y] + over_both
    pieces = [block] + others + [over_c] + [swap(piece, "c") for piece in others]
    return jnp.concatenate(pieces, axis=0)


def late_gather(block, after):
    if not by_pairs():
        block, after = lax.optimization_barrier((block, after))
    return plane_gather(block)


def add(left, right):
    return (left.astype(jnp.float32) + right.astype(jnp.float32)).astype(left.dtype)


def plane_sum(shares):
    if not by_pairs():
        return scatter_sum(shares[0].reshape(-1, shares[0].shape[-1]), PLANE)
    shares = add(shares[0], swap(shares[1], "c"))
    shares = shares.reshape((2, 2) + shares.shape[1:])
    half = shares.shape[2] // 2
    upper = add(shares[:, 0, :half], swap(shares[:, 1, :half], "x"))
    lower = add(shares[0, :, half:], swap(shares[1, :, half:], "y"))
    upper = add(upper[0], swap(upper[1], "y"))
    lower = add(lower[0], swap(lower[1], "x"))
    return jnp.concatenate([upper, lower], axis=0)


def by_distance(array):
    if not by_pairs():
        return array
    shape = array.shape
    array = array.reshape((2, 2, 2) + shape[1:])
    for dim, axis in enumerate(PLANE):
        array = jnp.where(lax.axis_index(axis) == 1, jnp.flip(array, dim), array)
    return array.reshape(shape)


def own_block(array, rows):
    place = 0 if by_pairs() else lax.axis_index(PLANE)
    return lax.dynamic_slice_in_dim(array, place * rows, rows, 0)


def by_source(cols):
    rows, total = cols.shape
    parts = 4 * lax.axis_size("x")
    pieces = jnp.moveaxis(cols.reshape(rows, parts, total // parts), 1, 0)
    return by_distance(exchange(pieces, PLANE)).reshape(parts * rows, total // parts)


def local(
    tokens,
    norm1_gain,
    w_query,
    w_key,
    w_value,
    w_out,
    norm2_gain,
    w_router,
    w_gate,
    w_up,
    w_down,
    expert_ids,
    prefix_len,
    out_grad,
):
    bf16, f32 = jnp.bfloat16, jnp.float32
    length, model_width = tokens.shape
    shard_rows = w_query.shape[0]
    local_count, _, hidden_width = w_gate.shape
    owners = lax.axis_size("x")
    depth = lax.axis_size("z")
    plane = lax.axis_size(PLANE)
    experts_all = w_router.shape[1]
    top_count = expert_ids.shape[1]
    block_rows = length // MICRO
    capacity = 3 * block_rows * top_count // (2 * experts_all)
    plane_rows = plane * length
    blocks = plane_rows // block_rows
    group_size = HQ // HK
    score_scale = HD ** (-0.5)
    q_cols, kv_cols = w_query.shape[1], w_key.shape[1]
    own_local = lax.axis_index(("y", "c"))
    own_expert = lax.axis_index("x") * local_count + own_local

    narrow = jnp.concatenate([w_router, norm1_gain[:, None], norm2_gain[:, None]], axis=1)
    narrow = jnp.pad(narrow, ((0, 0), (0, -narrow.shape[1] % 128)))
    packed = gather(jnp.concatenate([w_query, w_key, w_value, narrow], axis=1), GROUP)
    qkv_cols = q_cols + 2 * kv_cols
    qkv_w = packed[:, :qkv_cols]
    router_w = packed[:, qkv_cols : qkv_cols + experts_all]
    gains = packed[:, qkv_cols + experts_all : qkv_cols + experts_all + 2].T.astype(f32)
    gain_one, gain_two = gains[0], gains[1]
    output_w = gather(w_out, GROUP)

    ids_all = plane_gather(expert_ids)
    cot_all = plane_gather(out_grad)
    chosen_mask = jnp.any(
        ids_all[:, :, None] == jnp.arange(experts_all, dtype=jnp.int32)[None, None, :], axis=1
    )
    own_mask = jnp.any(ids_all == own_expert, axis=1).reshape(blocks, block_rows)
    place = jnp.cumsum(own_mask.astype(jnp.int32), axis=1) - 1
    dispatch = (
        own_mask[:, None, :]
        & (place[:, None, :] == jnp.arange(capacity, dtype=jnp.int32)[None, :, None])
    ).astype(bf16)

    cosine_tab, sine_tab = angles(length, HD)
    inputs_f = tokens.astype(f32)
    first_in = rms_scale(inputs_f, gain_one).astype(bf16)
    qkv = jnp.dot(first_in, qkv_w, preferred_element_type=f32)
    queries = (
        rotary(qkv[:, :q_cols].reshape(length, HQ, HD), cosine_tab, sine_tab)
        .astype(bf16)
        .reshape(length, HK, group_size, HD)
    )
    keys_rot = rotary(
        qkv[:, q_cols : q_cols + kv_cols].reshape(length, HK, HD), cosine_tab, sine_tab
    ).astype(bf16)
    values_b = qkv[:, q_cols + kv_cols :].astype(bf16).reshape(length, HK, HD)
    positions = jnp.arange(length)
    allowed = (positions[None, :] <= positions[:, None]) | (positions[None, :] < prefix_len[0])

    def masked_scores():
        scores = jnp.einsum("ihrd,jhd->hrij", queries, keys_rot, preferred_element_type=f32)
        return jnp.where(allowed, scores * score_scale, -1e30)

    masked = masked_scores()
    row_peak = jnp.max(masked, axis=-1, keepdims=True)
    log_total = row_peak + jnp.log(jnp.sum(jnp.exp(masked - row_peak), axis=-1, keepdims=True))
    prob_bf = jnp.exp(masked - log_total).astype(bf16)
    attended = jnp.einsum("hrij,jhd->ihrd", prob_bf, values_b, preferred_element_type=f32)
    attended = attended.reshape(length, HQ * HD).astype(bf16)
    resid = inputs_f + jnp.dot(attended, output_w, preferred_element_type=f32)
    second_in = rms_scale(resid, gain_two).astype(bf16)

    second_all = plane_gather(second_in)
    logits = jnp.dot(second_all, router_w, preferred_element_type=f32)
    gates_all = jax.nn.softmax(jnp.where(chosen_mask, logits, -jnp.inf), axis=-1)
    own_gates = lax.dynamic_index_in_dim(gates_all, own_expert, 1, keepdims=False)
    own_gates = own_gates.reshape(blocks, block_rows)
    gate_rows = jnp.einsum(
        "bct,bt->bc", dispatch.astype(f32), own_gates, precision=lax.Precision.HIGHEST
    )[:, :, None]
    gate_w = lax.dynamic_index_in_dim(w_gate, own_local, 0, keepdims=False)
    up_w = lax.dynamic_index_in_dim(w_up, own_local, 0, keepdims=False)
    down_w = lax.dynamic_index_in_dim(w_down, own_local, 0, keepdims=False)

    def to_rows(array):
        return jnp.einsum(
            "bct,btd->bcd",
            dispatch,
            array.reshape(blocks, block_rows, model_width),
            preferred_element_type=f32,
        ).astype(bf16)

    def to_tokens(rows):
        def side(part):
            tokens_part = jnp.einsum(
                "bct,bcd->btd", dispatch[part], rows[part].astype(bf16), preferred_element_type=f32
            )
            return tokens_part.astype(bf16).reshape(-1, length, model_width)

        step = blocks // 2 if by_pairs() else blocks
        return [side(slice(at, at + step)) for at in range(0, blocks, step)]

    rows_in = to_rows(second_all)
    rows_cot = to_rows(cot_all)
    gate_pre = jnp.einsum("bcd,df->bcf", rows_in, gate_w, preferred_element_type=f32)
    up_pre = jnp.einsum("bcd,df->bcf", rows_in, up_w, preferred_element_type=f32)
    hidden, act_pull = jax.vjp(expert_act, gate_pre, up_pre)
    gated = (gate_rows * hidden).astype(bf16)
    down_part = jnp.einsum("bcd,bcf->df", rows_cot, gated, preferred_element_type=f32)
    down_sum = scatter_sum(down_part.astype(bf16), "z")
    cot_hidden = jnp.einsum("bcd,fd->bcf", rows_cot, down_w, preferred_element_type=f32)
    gate_signal_rows = jnp.sum(hidden * cot_hidden, axis=-1)
    gate_pgrad, up_pgrad = act_pull(gate_rows * cot_hidden)
    gate_pgrad = gate_pgrad.astype(bf16)
    up_pgrad = up_pgrad.astype(bf16)
    gate_part = jnp.einsum("bcd,bcf->df", rows_in, gate_pgrad, preferred_element_type=f32)
    gate_sum = scatter_sum(gate_part.astype(bf16), "z")
    up_part = jnp.einsum("bcd,bcf->df", rows_in, up_pgrad, preferred_element_type=f32)
    up_sum = scatter_sum(up_part.astype(bf16), "z")
    rows_grad = jnp.einsum("bcf,df->bcd", gate_pgrad, gate_w, preferred_element_type=f32)
    rows_grad = rows_grad + jnp.einsum("bcf,df->bcd", up_pgrad, up_w, preferred_element_type=f32)
    second_back = plane_sum(to_tokens(rows_grad)).astype(f32)
    gate_signal = jnp.einsum(
        "bct,bc->bt", dispatch.astype(f32), gate_signal_rows, precision=lax.Precision.HIGHEST
    )
    gate_signal = exchange(by_distance(gate_signal.reshape(plane, length)), PLANE)
    gate_signal = jnp.transpose(
        gate_signal.reshape(2, 2, owners, length), (3, 2, 1, 0)
    ).reshape(length, experts_all)
    expert_rows = jnp.einsum("bcf,fd->bcd", gated, down_w, preferred_element_type=f32)
    mixture = plane_sum(to_tokens(expert_rows)).astype(f32)
    block_out = (resid + mixture).astype(bf16)

    cotangent = out_grad.astype(f32)
    gate_probs = own_block(gates_all, length)
    logit_grad = (
        gate_probs
        * (gate_signal - jnp.sum(gate_probs * gate_signal, axis=-1, keepdims=True))
    ).astype(bf16)
    router_acc = left_product(second_in, logit_grad)
    second_grad = second_back + jnp.dot(logit_grad, router_w.T, preferred_element_type=f32)
    _, norm_two_pull = jax.vjp(rms_scale, resid, gain_two)
    resid_norm_grad, gain_two_grad = norm_two_pull(second_grad)
    resid_grad = cotangent + resid_norm_grad
    branch_grad = resid_grad.astype(bf16)

    attended_all = late_gather(attended, branch_grad)
    branch_cols = by_source(branch_grad)
    output_part = left_product(attended_all, branch_cols)
    attended_grad = jnp.dot(branch_grad, output_w.T, preferred_element_type=f32).astype(bf16)
    attended_grad = attended_grad.reshape(length, HK, group_size, HD)
    masked = masked_scores()
    prob_full = jnp.exp(masked - log_total)
    prob_bf = prob_full.astype(bf16)
    prob_grad = jnp.einsum("ihrd,jhd->hrij", attended_grad, values_b, preferred_element_type=f32)
    row_inner = jnp.sum(prob_full * prob_grad, axis=-1, keepdims=True)
    score_grad = (prob_full * (prob_grad - row_inner)).astype(bf16)
    query_rot_grad = (
        jnp.einsum("hrij,jhd->ihrd", score_grad, keys_rot, preferred_element_type=f32)
        * score_scale
    )
    query_back = rotary(query_rot_grad.reshape(length, HQ, HD), cosine_tab, -sine_tab)
    query_back = query_back.astype(bf16).reshape(length, HQ * HD)
    key_rot_grad = (
        jnp.einsum("hrij,ihrd->jhd", score_grad, queries, preferred_element_type=f32)
        * score_scale
    )
    key_back = rotary(key_rot_grad, cosine_tab, -sine_tab).astype(bf16).reshape(length, HK * HD)
    value_back = jnp.einsum("hrij,ihrd->jhd", prob_bf, attended_grad, preferred_element_type=f32)
    value_back = value_back.astype(bf16).reshape(length, HK * HD)
    qkv_back = jnp.concatenate([query_back, key_back, value_back], axis=1)
    first_all = late_gather(first_in, output_part)
    qkv_part = left_product(first_all, by_source(qkv_back))
    first_grad = lax.dot_general(
        qkv_back, qkv_w, (((1,), (1,)), ((), ())), preferred_element_type=f32
    )
    _, norm_one_pull = jax.vjp(rms_scale, inputs_f, gain_one)
    input_norm_grad, gain_one_grad = norm_one_pull(first_grad)
    tokens_grad = (resid_grad + input_norm_grad).astype(bf16)

    narrow_part = jnp.concatenate(
        [router_acc, gain_one_grad[:, None], gain_two_grad[:, None]], axis=1
    )
    narrow_cols = -(-narrow_part.shape[1] // owners) * owners
    narrow_part = jnp.pad(narrow_part, ((0, 0), (0, narrow_cols - narrow_part.shape[1])))
    narrow_part = jnp.transpose(
        narrow_part.reshape(depth, 2, 2, shard_rows, owners, narrow_cols // owners),
        (2, 1, 4, 0, 3, 5),
    ).reshape(plane, depth, shard_rows * narrow_cols // owners)
    narrow_part = jnp.sum(exchange(narrow_part, PLANE), axis=0)
    qkv_width = qkv_cols // plane
    dense_cols = qkv_width + model_width // plane
    narrow_len = narrow_part.shape[1]
    narrow_rows = -(-narrow_len // dense_cols)
    narrow_part = jnp.pad(narrow_part, ((0, 0), (0, narrow_rows * dense_cols - narrow_len)))
    pad_rows = -(local_count * shard_rows + narrow_rows) % 8
    dense_part = jnp.concatenate(
        [
            jnp.concatenate([qkv_part, output_part], axis=1).reshape(
                depth, local_count * shard_rows, dense_cols
            ),
            narrow_part.reshape(depth, narrow_rows, dense_cols),
            jnp.zeros((depth, pad_rows, dense_cols), f32),
        ],
        axis=1,
    ).astype(bf16)
    dense_sum = scatter_sum(dense_part.reshape(-1, dense_cols), "z")
    wide_sum = dense_sum[: local_count * shard_rows].reshape(2, 2, 1, shard_rows, dense_cols)
    wide_sum = jnp.broadcast_to(
        jnp.swapaxes(wide_sum, 0, 1), (2, 2, owners, shard_rows, dense_cols)
    ).reshape(plane, shard_rows, dense_cols)
    narrow_sum = dense_sum[local_count * shard_rows :][:narrow_rows]
    narrow_sum = jnp.broadcast_to(narrow_sum[None], (plane, narrow_rows, dense_cols))
    dense_sum = exchange(jnp.concatenate([wide_sum, narrow_sum], axis=1), PLANE)
    wide_sum = jnp.moveaxis(dense_sum[:, :shard_rows].astype(f32), 0, 1)
    qkv_sum = wide_sum[:, :, :qkv_width].reshape(shard_rows, qkv_cols)
    output_sum = wide_sum[:, :, qkv_width:].reshape(shard_rows, model_width)
    narrow_sum = dense_sum[:, shard_rows:].reshape(2, 2, owners, narrow_rows * dense_cols)
    narrow_sum = narrow_sum[lax.axis_index("c"), lax.axis_index("y"), :, :narrow_len]
    narrow_sum = jnp.moveaxis(
        narrow_sum.reshape(owners, shard_rows, narrow_cols // owners), 0, 1
    ).reshape(shard_rows, narrow_cols).astype(f32)

    def placed(total):
        total = exchange(total, ("y", "c"))
        return total.reshape(local_count, shard_rows, hidden_width).astype(f32)

    return (
        block_out,
        tokens_grad,
        narrow_sum[:, experts_all],
        qkv_sum[:, :q_cols],
        qkv_sum[:, q_cols : q_cols + kv_cols],
        qkv_sum[:, q_cols + kv_cols :],
        output_sum,
        narrow_sum[:, experts_all + 1],
        narrow_sum[:, :experts_all],
        placed(gate_sum),
        placed(up_sum),
        jnp.swapaxes(placed(down_sum), 1, 2),
    )


def solution(mesh):
    groups, owners = mesh.shape["dp"], mesh.shape["expert"]
    grid = jax.sharding.Mesh(
        mesh.devices.reshape(groups // 4, 2, 2, owners), ("z", "y", "c", "x")
    )
    rows = P(("z", "y", "c", "x"), None)
    shard, shard_rows = P(GROUP), P(GROUP, None)
    expert = P("x", None, None)
    return jax.shard_map(
        local,
        mesh=grid,
        in_specs=(
            rows,
            shard,
            shard_rows,
            shard_rows,
            shard_rows,
            shard_rows,
            shard,
            shard_rows,
            expert,
            expert,
            expert,
            rows,
            P(("z", "y", "c", "x")),
            rows,
        ),
        out_specs=(
            rows,
            rows,
            shard,
            shard_rows,
            shard_rows,
            shard_rows,
            shard_rows,
            shard,
            shard_rows,
            P("x", GROUP, None),
            P("x", GROUP, None),
            P("x", None, GROUP),
        ),
        check_vma=False,
    )
```

```python
import math

import jax
import jax.numpy as jnp
from jax import lax
from jax.sharding import PartitionSpec as P

HQ = 12
HK = 2
HD = 128
MICRO = 2
PLANE = ("c", "y", "x")
GROUP = ("z", "y", "c")


def rms_scale(values, gain_vec):
    inverse = lax.rsqrt(jnp.mean(values * values, axis=-1, keepdims=True) + 1e-06)
    return values * inverse * gain_vec


def angles(length, head_size):
    positions = jnp.arange(length).astype(jnp.float32)
    freq_rates = jnp.exp(
        -(2.0 * jnp.arange(head_size // 2).astype(jnp.float32) / head_size) * math.log(1000000.0)
    )
    angle_tab = positions[:, None] * freq_rates[None, :]
    return (jnp.cos(angle_tab)[:, None, :], jnp.sin(angle_tab)[:, None, :])


def rotary(values, cosine_tab, sine_tab):
    half_dim = values.shape[-1] // 2
    first_half = values[..., :half_dim]
    second_half = values[..., half_dim:]
    return jnp.concatenate(
        [
            first_half * cosine_tab - second_half * sine_tab,
            second_half * cosine_tab + first_half * sine_tab,
        ],
        axis=-1,
    )


def expert_act(gate_pre, up_pre):
    return jax.nn.gelu(gate_pre, approximate=True) * up_pre


def left_product(left_mat, right_mat):
    return lax.dot_general(
        left_mat, right_mat, (((0,), (0,)), ((), ())), preferred_element_type=jnp.float32
    )


def gather(block, axes):
    return lax.all_gather(block, axes, axis=0, tiled=True)


def exchange(block, axes):
    return lax.all_to_all(block, axes, split_axis=0, concat_axis=0, tiled=True)


def scatter_sum(block, axes):
    return lax.psum_scatter(block, axes, scatter_dimension=0, tiled=True)


def swap(block, axis):
    return lax.ppermute(block, axis, [(0, 1), (1, 0)])


def by_pairs():
    return lax.axis_size("x") == 2


def plane_gather(block):
    if not by_pairs():
        return gather(block, PLANE)
    half = block.shape[0] // 2
    over_c = swap(block, "c")
    over_y = swap(block, "y")
    over_x = swap(block, "x")
    over_both = [swap(over_y[:half], "x"), swap(over_x[half:], "y")]
    others = [over_x, over_y] + over_both
    pieces = [block] + others + [over_c] + [swap(piece, "c") for piece in others]
    return jnp.concatenate(pieces, axis=0)


def late_gather(block, after):
    block, after = lax.optimization_barrier((block, after))
    return plane_gather(block)


def gather_halves(halves):
    _, rows, cols = halves.shape
    depth = lax.axis_size("z")
    if not by_pairs():
        total = gather(jnp.moveaxis(halves, 0, 1), GROUP)
        return jnp.moveaxis(total, 1, 0)
    z, y, c, x = (lax.axis_index(axis) for axis in ("z", "y", "c", "x"))
    own = lax.dynamic_index_in_dim(halves, x, 0, keepdims=False)
    column = jnp.zeros((depth, rows, cols), halves.dtype)
    for k in range(depth):
        piece = own
        if k:
            piece = lax.ppermute(own, "z", [(i, (i + k) % depth) for i in range(depth)])
        column = lax.dynamic_update_index_in_dim(column, piece, (z - k) % depth, 0)
    over_x, over_y = swap(column, "x"), swap(column, "y")
    cut = depth // 2
    near, far = swap(over_y[:cut], "x"), swap(over_x[cut:], "y")
    total = jnp.zeros((2, depth, 2, 2, rows, cols), halves.dtype)
    pieces = ((column, 0, 0, 0), (over_x, 0, 1, 0), (over_y, 0, 0, 1), (near, 0, 1, 1), (far, cut, 1, 1))
    for flip in (0, 1):
        for piece, at, dx, dy in pieces:
            piece = swap(piece, "c") if flip else piece
            start = (x ^ dx, at, y ^ dy, c ^ flip, 0, 0)
            total = lax.dynamic_update_slice(total, piece[None, :, None, None], start)
    return total.reshape(2, -1, cols)


def add(left, right):
    return (left.astype(jnp.float32) + right.astype(jnp.float32)).astype(left.dtype)


def plane_sum(shares):
    if not by_pairs():
        return scatter_sum(shares[0].reshape(-1, shares[0].shape[-1]), PLANE)
    shares = add(shares[0], swap(shares[1], "c"))
    shares = shares.reshape((2, 2) + shares.shape[1:])
    half = shares.shape[2] // 2
    upper = add(shares[:, 0, :half], swap(shares[:, 1, :half], "x"))
    lower = add(shares[0, :, half:], swap(shares[1, :, half:], "y"))
    upper = add(upper[0], swap(upper[1], "y"))
    lower = add(lower[0], swap(lower[1], "x"))
    return jnp.concatenate([upper, lower], axis=0)


def by_distance(array):
    if not by_pairs():
        return array
    shape = array.shape
    array = array.reshape((2, 2, 2) + shape[1:])
    for dim, axis in enumerate(PLANE):
        array = jnp.where(lax.axis_index(axis) == 1, jnp.flip(array, dim), array)
    return array.reshape(shape)


def own_block(array, rows):
    place = 0 if by_pairs() else lax.axis_index(PLANE)
    return lax.dynamic_slice_in_dim(array, place * rows, rows, 0)


def by_source(cols):
    rows, total = cols.shape
    parts = 4 * lax.axis_size("x")
    pieces = jnp.moveaxis(cols.reshape(rows, parts, total // parts), 1, 0)
    return by_distance(exchange(pieces, PLANE)).reshape(parts * rows, total // parts)


def local(
    tokens,
    norm1_gain,
    w_query,
    w_key,
    w_value,
    w_out,
    norm2_gain,
    w_router,
    w_gate,
    w_up,
    w_down,
    expert_ids,
    prefix_len,
    out_grad,
):
    bf16, f32 = jnp.bfloat16, jnp.float32
    length, model_width = tokens.shape
    shard_rows = w_query.shape[0]
    local_count, _, hidden_width = w_gate.shape
    owners = lax.axis_size("x")
    depth = lax.axis_size("z")
    plane = lax.axis_size(PLANE)
    experts_all = w_router.shape[1]
    top_count = expert_ids.shape[1]
    block_rows = length // MICRO
    capacity = 3 * block_rows * top_count // (2 * experts_all)
    plane_rows = plane * length
    blocks = plane_rows // block_rows
    group_size = HQ // HK
    score_scale = HD ** (-0.5)
    q_cols, kv_cols = w_query.shape[1], w_key.shape[1]
    own_local = lax.axis_index(("y", "c"))
    own_expert = lax.axis_index("x") * local_count + own_local

    narrow = jnp.concatenate([w_router, norm1_gain[:, None], norm2_gain[:, None]], axis=1)
    narrow = jnp.pad(narrow, ((0, 0), (0, -narrow.shape[1] % 128)))
    narrow = gather(narrow, GROUP)
    router_w = narrow[:, :experts_all]
    gains = narrow[:, experts_all : experts_all + 2].T.astype(f32)
    gain_one, gain_two = gains[0], gains[1]
    qkv_cols = q_cols + 2 * kv_cols
    q_group = q_cols // HK
    qkv_w = gather_halves(
        jnp.concatenate(
            [
                jnp.moveaxis(part.reshape(shard_rows, HK, -1), 1, 0)
                for part in (w_query, w_key, w_value)
            ],
            axis=2,
        )
    )
    output_w = gather_halves(jnp.moveaxis(w_out.reshape(shard_rows, 2, -1), 1, 0))

    ids_all = plane_gather(expert_ids)
    cot_all = plane_gather(out_grad)
    chosen_mask = jnp.any(
        ids_all[:, :, None] == jnp.arange(experts_all, dtype=jnp.int32)[None, None, :], axis=1
    )
    own_mask = jnp.any(ids_all == own_expert, axis=1).reshape(blocks, block_rows)
    place = jnp.cumsum(own_mask.astype(jnp.int32), axis=1) - 1
    dispatch = (
        own_mask[:, None, :]
        & (place[:, None, :] == jnp.arange(capacity, dtype=jnp.int32)[None, :, None])
    ).astype(bf16)

    cosine_tab, sine_tab = angles(length, HD)
    inputs_f = tokens.astype(f32)
    first_in = rms_scale(inputs_f, gain_one).astype(bf16)
    qkv = jnp.einsum("id,gde->ige", first_in, qkv_w, preferred_element_type=f32)
    queries = (
        rotary(qkv[:, :, :q_group].reshape(length, HQ, HD), cosine_tab, sine_tab)
        .astype(bf16)
        .reshape(length, HK, group_size, HD)
    )
    keys_rot = rotary(qkv[:, :, q_group : q_group + HD], cosine_tab, sine_tab).astype(bf16)
    values_b = qkv[:, :, q_group + HD :].astype(bf16)
    positions = jnp.arange(length)
    allowed = (positions[None, :] <= positions[:, None]) | (positions[None, :] < prefix_len[0])

    def masked_scores():
        scores = jnp.einsum("ihrd,jhd->hrij", queries, keys_rot, preferred_element_type=f32)
        return jnp.where(allowed, scores * score_scale, -1e30)

    masked = masked_scores()
    row_peak = jnp.max(masked, axis=-1, keepdims=True)
    log_total = row_peak + jnp.log(jnp.sum(jnp.exp(masked - row_peak), axis=-1, keepdims=True))
    prob_bf = jnp.exp(masked - log_total).astype(bf16)
    attended = jnp.einsum("hrij,jhd->ihrd", prob_bf, values_b, preferred_element_type=f32)
    attended = attended.reshape(length, HQ * HD).astype(bf16)
    branch = jnp.einsum("ie,hed->ihd", attended, output_w, preferred_element_type=f32)
    resid = inputs_f + branch.reshape(length, model_width)
    second_in = rms_scale(resid, gain_two).astype(bf16)

    second_all = plane_gather(second_in)
    logits = jnp.dot(second_all, router_w, preferred_element_type=f32)
    gates_all = jax.nn.softmax(jnp.where(chosen_mask, logits, -jnp.inf), axis=-1)
    own_gates = lax.dynamic_index_in_dim(gates_all, own_expert, 1, keepdims=False)
    own_gates = own_gates.reshape(blocks, block_rows)
    gate_rows = jnp.einsum(
        "bct,bt->bc", dispatch.astype(f32), own_gates, precision=lax.Precision.HIGHEST
    )[:, :, None]
    gate_w = lax.dynamic_index_in_dim(w_gate, own_local, 0, keepdims=False)
    up_w = lax.dynamic_index_in_dim(w_up, own_local, 0, keepdims=False)
    down_w = lax.dynamic_index_in_dim(w_down, own_local, 0, keepdims=False)

    def to_rows(array):
        return jnp.einsum(
            "bct,btd->bcd",
            dispatch,
            array.reshape(blocks, block_rows, model_width),
            preferred_element_type=f32,
        ).astype(bf16)

    def to_tokens(rows):
        def side(part):
            tokens_part = jnp.einsum(
                "bct,bcd->btd", dispatch[part], rows[part].astype(bf16), preferred_element_type=f32
            )
            return tokens_part.astype(bf16).reshape(-1, length, model_width)

        step = blocks // 2 if by_pairs() else blocks
        return [side(slice(at, at + step)) for at in range(0, blocks, step)]

    rows_in = to_rows(second_all)
    rows_cot = to_rows(cot_all)
    gate_pre = jnp.einsum("bcd,df->bcf", rows_in, gate_w, preferred_element_type=f32)
    up_pre = jnp.einsum("bcd,df->bcf", rows_in, up_w, preferred_element_type=f32)
    hidden, act_pull = jax.vjp(expert_act, gate_pre, up_pre)
    gated = (gate_rows * hidden).astype(bf16)
    down_part = jnp.einsum("bcd,bcf->df", rows_cot, gated, preferred_element_type=f32)
    down_sum = scatter_sum(down_part.astype(bf16), "z")
    cot_hidden = jnp.einsum("bcd,fd->bcf", rows_cot, down_w, preferred_element_type=f32)
    gate_signal_rows = jnp.sum(hidden * cot_hidden, axis=-1)
    gate_pgrad, up_pgrad = act_pull(gate_rows * cot_hidden)
    gate_pgrad = gate_pgrad.astype(bf16)
    up_pgrad = up_pgrad.astype(bf16)
    gate_part = jnp.einsum("bcd,bcf->df", rows_in, gate_pgrad, preferred_element_type=f32)
    gate_sum = scatter_sum(gate_part.astype(bf16), "z")
    up_part = jnp.einsum("bcd,bcf->df", rows_in, up_pgrad, preferred_element_type=f32)
    up_sum = scatter_sum(up_part.astype(bf16), "z")
    rows_grad = jnp.einsum("bcf,df->bcd", gate_pgrad, gate_w, preferred_element_type=f32)
    rows_grad = rows_grad + jnp.einsum("bcf,df->bcd", up_pgrad, up_w, preferred_element_type=f32)
    second_back = plane_sum(to_tokens(rows_grad)).astype(f32)
    gate_signal = jnp.einsum(
        "bct,bc->bt", dispatch.astype(f32), gate_signal_rows, precision=lax.Precision.HIGHEST
    )
    gate_signal = exchange(by_distance(gate_signal.reshape(plane, length)), PLANE)
    gate_signal = jnp.transpose(
        gate_signal.reshape(2, 2, owners, length), (3, 2, 1, 0)
    ).reshape(length, experts_all)
    expert_rows = jnp.einsum("bcf,fd->bcd", gated, down_w, preferred_element_type=f32)
    mixture = plane_sum(to_tokens(expert_rows)).astype(f32)
    block_out = (resid + mixture).astype(bf16)

    cotangent = out_grad.astype(f32)
    gate_probs = own_block(gates_all, length)
    logit_grad = (
        gate_probs
        * (gate_signal - jnp.sum(gate_probs * gate_signal, axis=-1, keepdims=True))
    ).astype(bf16)
    router_acc = left_product(second_in, logit_grad)
    second_grad = second_back + jnp.dot(logit_grad, router_w.T, preferred_element_type=f32)
    _, norm_two_pull = jax.vjp(rms_scale, resid, gain_two)
    resid_norm_grad, gain_two_grad = norm_two_pull(second_grad)
    resid_grad = cotangent + resid_norm_grad
    branch_grad = resid_grad.astype(bf16)

    attended_all = late_gather(attended, second_all if by_pairs() else branch_grad)
    branch_cols = by_source(branch_grad)
    output_part = left_product(attended_all, branch_cols)
    attended_grad = jnp.einsum(
        "ihd,hed->ie", branch_grad.reshape(length, 2, -1), output_w, preferred_element_type=f32
    ).astype(bf16)
    attended_grad = attended_grad.reshape(length, HK, group_size, HD)
    masked = masked_scores()
    prob_full = jnp.exp(masked - log_total)
    prob_bf = prob_full.astype(bf16)
    prob_grad = jnp.einsum("ihrd,jhd->hrij", attended_grad, values_b, preferred_element_type=f32)
    row_inner = jnp.sum(prob_full * prob_grad, axis=-1, keepdims=True)
    score_grad = (prob_full * (prob_grad - row_inner)).astype(bf16)
    query_rot_grad = (
        jnp.einsum("hrij,jhd->ihrd", score_grad, keys_rot, preferred_element_type=f32)
        * score_scale
    )
    query_back = rotary(query_rot_grad.reshape(length, HQ, HD), cosine_tab, -sine_tab)
    query_back = query_back.astype(bf16).reshape(length, HK, q_group)
    key_rot_grad = (
        jnp.einsum("hrij,ihrd->jhd", score_grad, queries, preferred_element_type=f32)
        * score_scale
    )
    key_back = rotary(key_rot_grad, cosine_tab, -sine_tab).astype(bf16)
    value_back = jnp.einsum("hrij,ihrd->jhd", prob_bf, attended_grad, preferred_element_type=f32)
    qkv_back = jnp.concatenate([query_back, key_back, value_back.astype(bf16)], axis=2)
    first_all = late_gather(first_in, second_all if by_pairs() else output_part)
    qkv_part = left_product(first_all, by_source(qkv_back.reshape(length, qkv_cols)))
    first_grad = jnp.einsum("ige,gde->id", qkv_back, qkv_w, preferred_element_type=f32)
    _, norm_one_pull = jax.vjp(rms_scale, inputs_f, gain_one)
    input_norm_grad, gain_one_grad = norm_one_pull(first_grad)
    tokens_grad = (resid_grad + input_norm_grad).astype(bf16)

    narrow_part = jnp.concatenate(
        [router_acc, gain_one_grad[:, None], gain_two_grad[:, None]], axis=1
    )
    narrow_cols = -(-narrow_part.shape[1] // owners) * owners
    narrow_part = jnp.pad(narrow_part, ((0, 0), (0, narrow_cols - narrow_part.shape[1])))
    narrow_part = jnp.transpose(
        narrow_part.reshape(depth, 2, 2, shard_rows, owners, narrow_cols // owners),
        (2, 1, 4, 0, 3, 5),
    ).reshape(plane, depth, shard_rows * narrow_cols // owners)
    narrow_part = jnp.sum(exchange(narrow_part, PLANE), axis=0)
    qkv_width = qkv_cols // plane
    dense_cols = qkv_width + model_width // plane
    narrow_len = narrow_part.shape[1]
    narrow_rows = -(-narrow_len // dense_cols)
    narrow_part = jnp.pad(narrow_part, ((0, 0), (0, narrow_rows * dense_cols - narrow_len)))
    pad_rows = -(local_count * shard_rows + narrow_rows) % 8
    dense_part = jnp.concatenate(
        [
            jnp.concatenate([qkv_part, output_part], axis=1).reshape(
                depth, local_count * shard_rows, dense_cols
            ),
            narrow_part.reshape(depth, narrow_rows, dense_cols),
            jnp.zeros((depth, pad_rows, dense_cols), f32),
        ],
        axis=1,
    ).astype(bf16)
    dense_sum = scatter_sum(dense_part.reshape(-1, dense_cols), "z")
    wide_sum = dense_sum[: local_count * shard_rows].reshape(2, 2, 1, shard_rows, dense_cols)
    wide_sum = jnp.broadcast_to(
        jnp.swapaxes(wide_sum, 0, 1), (2, 2, owners, shard_rows, dense_cols)
    ).reshape(plane, shard_rows, dense_cols)
    narrow_sum = dense_sum[local_count * shard_rows :][:narrow_rows]
    narrow_sum = jnp.broadcast_to(narrow_sum[None], (plane, narrow_rows, dense_cols))
    dense_sum = exchange(jnp.concatenate([wide_sum, narrow_sum], axis=1), PLANE)
    wide_sum = jnp.moveaxis(dense_sum[:, :shard_rows].astype(f32), 0, 1)
    qkv_sum = wide_sum[:, :, :qkv_width].reshape(shard_rows, HK, qkv_cols // HK)
    output_sum = wide_sum[:, :, qkv_width:].reshape(shard_rows, model_width)
    narrow_sum = dense_sum[:, shard_rows:].reshape(2, 2, owners, narrow_rows * dense_cols)
    narrow_sum = narrow_sum[lax.axis_index("c"), lax.axis_index("y"), :, :narrow_len]
    narrow_sum = jnp.moveaxis(
        narrow_sum.reshape(owners, shard_rows, narrow_cols // owners), 0, 1
    ).reshape(shard_rows, narrow_cols).astype(f32)

    def placed(total):
        total = exchange(total, ("y", "c"))
        return total.reshape(local_count, shard_rows, hidden_width).astype(f32)

    return (
        block_out,
        tokens_grad,
        narrow_sum[:, experts_all],
        qkv_sum[:, :, :q_group].reshape(shard_rows, q_cols),
        qkv_sum[:, :, q_group : q_group + HD].reshape(shard_rows, kv_cols),
        qkv_sum[:, :, q_group + HD :].reshape(shard_rows, kv_cols),
        output_sum,
        narrow_sum[:, experts_all + 1],
        narrow_sum[:, :experts_all],
        placed(gate_sum),
        placed(up_sum),
        jnp.swapaxes(placed(down_sum), 1, 2),
    )


def solution(mesh):
    groups, owners = mesh.shape["dp"], mesh.shape["expert"]
    grid = jax.sharding.Mesh(
        mesh.devices.reshape(groups // 4, 2, 2, owners), ("z", "y", "c", "x")
    )
    rows = P(("z", "y", "c", "x"), None)
    shard, shard_rows = P(GROUP), P(GROUP, None)
    expert = P("x", None, None)
    return jax.shard_map(
        local,
        mesh=grid,
        in_specs=(
            rows,
            shard,
            shard_rows,
            shard_rows,
            shard_rows,
            shard_rows,
            shard,
            shard_rows,
            expert,
            expert,
            expert,
            rows,
            P(("z", "y", "c", "x")),
            rows,
        ),
        out_specs=(
            rows,
            rows,
            shard,
            shard_rows,
            shard_rows,
            shard_rows,
            shard_rows,
            shard,
            shard_rows,
            P("x", GROUP, None),
            P("x", GROUP, None),
            P("x", None, GROUP),
        ),
        check_vma=False,
    )
```

```python
import math

import jax
import jax.numpy as jnp
from jax import lax
from jax.sharding import PartitionSpec as P

HQ = 12
HK = 2
HD = 128
MICRO = 2
PLANE = ("y", "c", "x")
GROUP = ("z", "y", "c")


def rms_scale(values, gain_vec):
    inverse = lax.rsqrt(jnp.mean(values * values, axis=-1, keepdims=True) + 1e-06)
    return values * inverse * gain_vec


def angles(length, head_size):
    positions = jnp.arange(length).astype(jnp.float32)
    freq_rates = jnp.exp(
        -(2.0 * jnp.arange(head_size // 2).astype(jnp.float32) / head_size) * math.log(1000000.0)
    )
    angle_tab = positions[:, None] * freq_rates[None, :]
    return (jnp.cos(angle_tab)[:, None, :], jnp.sin(angle_tab)[:, None, :])


def rotary(values, cosine_tab, sine_tab):
    half_dim = values.shape[-1] // 2
    first_half = values[..., :half_dim]
    second_half = values[..., half_dim:]
    return jnp.concatenate(
        [
            first_half * cosine_tab - second_half * sine_tab,
            second_half * cosine_tab + first_half * sine_tab,
        ],
        axis=-1,
    )


def expert_act(gate_pre, up_pre):
    return jax.nn.gelu(gate_pre, approximate=True) * up_pre


def left_product(left_mat, right_mat):
    return lax.dot_general(
        left_mat, right_mat, (((0,), (0,)), ((), ())), preferred_element_type=jnp.float32
    )


def gather(block, axes):
    return lax.all_gather(block, axes, axis=0, tiled=True)


def exchange(block, axes):
    return lax.all_to_all(block, axes, split_axis=0, concat_axis=0, tiled=True)


def scatter_sum(block, axes):
    return lax.psum_scatter(block, axes, scatter_dimension=0, tiled=True)


def swap(block, axis):
    return lax.ppermute(block, axis, [(0, 1), (1, 0)])


def by_pairs():
    return lax.axis_size("x") == 2


def plane_sides(block):
    return swap(block, "x"), swap(block, "y")


def plane_pieces(block, sides=None, before_corner=()):
    half = block.shape[0] // 2
    over_x, over_y = sides or plane_sides(block)
    corner = lax.optimization_barrier((over_y[:half], over_x[half:]) + before_corner)
    others = [over_x, over_y, swap(corner[0], "x"), swap(corner[1], "y")]
    return [block] + others + [swap(block, "c")] + [swap(piece, "c") for piece in others]


def plane_gather(block, sides=None, before_corner=()):
    if not by_pairs():
        return gather(block, PLANE)
    return jnp.concatenate(plane_pieces(block, sides, before_corner), axis=0)


def gather_two(left, right):
    rows = left.shape[0]
    pieces = plane_pieces(jnp.concatenate([left, right], axis=0))
    corners = (3, 4, 8, 9)
    lefts = [piece[:rows] for n, piece in enumerate(pieces) if n not in corners[1::2]]
    rights = [piece[-rows:] for n, piece in enumerate(pieces) if n not in corners[::2]]
    return jnp.concatenate(lefts, axis=0), jnp.concatenate(rights, axis=0)


def small_gather(block):
    if not by_pairs():
        return gather(block, PLANE)
    for axis in ("x", "y", "c"):
        block = jnp.concatenate([block, swap(block, axis)], axis=0)
    return block


def small_group_gather(block, *before_plane):
    if not by_pairs():
        return gather(block, GROUP)
    total = along_z(block)[:, None, None]
    total = after(total, *before_plane)
    for dim, axis in ((1, "y"), (2, "c")):
        other = swap(total, axis)
        last = lax.axis_index(axis) == 1
        pair = [jnp.where(last, other, total), jnp.where(last, total, other)]
        total = jnp.concatenate(pair, axis=dim)
    return total.reshape(-1, block.shape[1])


def after(block, *others):
    return lax.optimization_barrier((block,) + others)[0]


def along_z(block):
    depth = lax.axis_size("z")
    order = jnp.stack(([block] + shifts(block))[::-1] * 2)
    return lax.dynamic_slice_in_dim(order, (depth - 1 - lax.axis_index("z")) % depth, depth, 0)


def column_of(halves):
    own = lax.dynamic_index_in_dim(halves, lax.axis_index("x"), 0, keepdims=False)
    return along_z(own).reshape(-1, halves.shape[2])


def shifts(block):
    depth = lax.axis_size("z")
    return [
        lax.ppermute(block, "z", [(i, (i + k) % depth) for i in range(depth)])
        for k in range(1, depth)
    ]


def weight_sides(column):
    cut = column.shape[0] // 2
    over_x, over_y = plane_sides(column)
    near, far = swap(over_y[:cut], "x"), swap(over_x[cut:], "y")
    return [(column, 0, 0, 0), (over_x, 0, 1, 0), (over_y, 0, 0, 1), (near, 0, 1, 1), (far, cut, 1, 1)]


def whole_weight(sides):
    rows, cols = sides[0][0].shape
    y, c, x = (lax.axis_index(axis) for axis in ("y", "c", "x"))
    total = jnp.zeros((2, 2, 2, rows, cols), sides[0][0].dtype)
    for flip in (0, 1):
        for piece, first, dx, dy in sides:
            piece = swap(piece, "c") if flip else piece
            start = (x ^ dx, y ^ dy, c ^ flip, first, 0)
            total = lax.dynamic_update_slice(total, piece[None, None, None], start)
    return total.reshape(2, -1, cols)


def by_row_order(array):
    if not by_pairs():
        return array
    depth = lax.axis_size("z")
    return jnp.swapaxes(array.reshape(array.shape[0], depth, 4, -1), 1, 2).reshape(array.shape)


def from_row_order(array):
    if not by_pairs():
        return array
    depth = lax.axis_size("z")
    return jnp.swapaxes(array.reshape(array.shape[0], 4, depth, -1), 1, 2).reshape(array.shape)


def all_rows(halves):
    return jnp.moveaxis(gather(jnp.moveaxis(halves, 0, 1), GROUP), 1, 0)


def add(left, right):
    return (left.astype(jnp.float32) + right.astype(jnp.float32)).astype(left.dtype)


def plane_sum(shares):
    if not by_pairs():
        return scatter_sum(shares[0].reshape(-1, shares[0].shape[-1]), PLANE)
    shares = add(shares[0], swap(shares[1], "c"))
    shares = shares.reshape((2, 2) + shares.shape[1:])
    half = shares.shape[2] // 2
    upper = add(shares[:, 0, :half], swap(shares[:, 1, :half], "x"))
    lower = add(shares[0, :, half:], swap(shares[1, :, half:], "y"))
    upper = add(upper[0], swap(upper[1], "y"))
    lower = add(lower[0], swap(lower[1], "x"))
    return jnp.concatenate([upper, lower], axis=0)


def flips(array):
    for dim, axis in enumerate(("c", "y", "x")):
        array = jnp.where(lax.axis_index(axis) == 1, jnp.flip(array, dim), array)
    return array


def to_distance(array):
    if not by_pairs():
        return array
    shape = array.shape
    return flips(jnp.swapaxes(array.reshape((2, 2, 2) + shape[1:]), 0, 1)).reshape(shape)


def to_place(array):
    if not by_pairs():
        return array
    shape = array.shape
    return jnp.swapaxes(flips(array.reshape((2, 2, 2) + shape[1:])), 0, 1).reshape(shape)


def own_block(array, rows):
    place = 0 if by_pairs() else lax.axis_index(PLANE)
    return lax.dynamic_slice_in_dim(array, place * rows, rows, 0)


def by_source(cols):
    rows, total = cols.shape
    parts = 4 * lax.axis_size("x")
    pieces = jnp.moveaxis(cols.reshape(rows, parts, total // parts), 1, 0)
    return to_distance(exchange(pieces, PLANE)).reshape(parts * rows, total // parts)


def local(
    tokens,
    norm1_gain,
    w_query,
    w_key,
    w_value,
    w_out,
    norm2_gain,
    w_router,
    w_gate,
    w_up,
    w_down,
    expert_ids,
    prefix_len,
    out_grad,
):
    bf16, f32 = jnp.bfloat16, jnp.float32
    length, model_width = tokens.shape
    shard_rows = w_query.shape[0]
    local_count, _, hidden_width = w_gate.shape
    owners = lax.axis_size("x")
    depth = lax.axis_size("z")
    plane = lax.axis_size(PLANE)
    experts_all = w_router.shape[1]
    top_count = expert_ids.shape[1]
    block_rows = length // MICRO
    capacity = 3 * block_rows * top_count // (2 * experts_all)
    plane_rows = plane * length
    blocks = plane_rows // block_rows
    group_size = HQ // HK
    score_scale = HD ** (-0.5)
    q_cols, kv_cols = w_query.shape[1], w_key.shape[1]
    own_local = lax.axis_index(("y", "c"))
    own_expert = lax.axis_index("x") * local_count + own_local

    qkv_cols = q_cols + 2 * kv_cols
    q_group = q_cols // HK
    qkv_halves = jnp.concatenate(
        [
            jnp.moveaxis(part.reshape(shard_rows, HK, -1), 1, 0)
            for part in (w_query, w_key, w_value)
        ],
        axis=2,
    )
    out_halves = jnp.moveaxis(w_out.reshape(shard_rows, 2, -1), 1, 0)
    narrow = jnp.concatenate([w_router, norm1_gain[:, None], norm2_gain[:, None]], axis=1)
    if by_pairs():
        cot_sides = plane_sides(out_grad)
        qkv_column = after(column_of(qkv_halves), *cot_sides)
        out_column = column_of(after(out_halves, qkv_column))
        qkv_sides = weight_sides(qkv_column)
        corners = tuple(piece[0] for piece in qkv_sides[3:])
        narrow = small_group_gather(narrow, *corners)
        out_sides = weight_sides(after(out_column, narrow))
        qkv_w = whole_weight(qkv_sides)
        output_w = whole_weight(out_sides)
        corners = tuple(piece[0] for piece in out_sides[3:])
        ids_all = small_gather(after(expert_ids, *corners))
        cot_all = plane_gather(out_grad, cot_sides, corners)
    else:
        narrow = small_group_gather(narrow)
        ids_all = small_gather(expert_ids)
        cot_all = plane_gather(out_grad)
        qkv_w = all_rows(qkv_halves)
        output_w = all_rows(out_halves)
    router_w = narrow[:, :experts_all]
    gains = narrow[:, experts_all : experts_all + 2].T.astype(f32)
    gain_one, gain_two = gains[0], gains[1]

    chosen_mask = jnp.any(
        ids_all[:, :, None] == jnp.arange(experts_all, dtype=jnp.int32)[None, None, :], axis=1
    )
    own_mask = jnp.any(ids_all == own_expert, axis=1).reshape(blocks, block_rows)
    place = jnp.cumsum(own_mask.astype(jnp.int32), axis=1) - 1
    dispatch = (
        own_mask[:, None, :]
        & (place[:, None, :] == jnp.arange(capacity, dtype=jnp.int32)[None, :, None])
    ).astype(bf16)

    cosine_tab, sine_tab = angles(length, HD)
    inputs_f = by_row_order(tokens).astype(f32)
    gain_one = by_row_order(gain_one[None])
    first_in = rms_scale(inputs_f, gain_one).astype(bf16)
    qkv = jnp.einsum("id,gde->ige", first_in, qkv_w, preferred_element_type=f32)
    queries = (
        rotary(qkv[:, :, :q_group].reshape(length, HQ, HD), cosine_tab, sine_tab)
        .astype(bf16)
        .reshape(length, HK, group_size, HD)
    )
    keys_rot = rotary(qkv[:, :, q_group : q_group + HD], cosine_tab, sine_tab).astype(bf16)
    values_b = qkv[:, :, q_group + HD :].astype(bf16)
    positions = jnp.arange(length)
    allowed = (positions[None, :] <= positions[:, None]) | (positions[None, :] < prefix_len[0])
    scores = jnp.einsum("ihrd,jhd->hrij", queries, keys_rot, preferred_element_type=f32)
    masked = jnp.where(allowed, scores * score_scale, -1e30)
    probs = jax.nn.softmax(masked, axis=-1).astype(bf16)
    attended = jnp.einsum("hrij,jhd->ihrd", probs, values_b, preferred_element_type=f32)
    attended = attended.reshape(length, HQ * HD).astype(bf16)
    attended_in = by_row_order(attended)
    branch = [jnp.dot(attended_in, output_w[half], preferred_element_type=f32) for half in (0, 1)]
    resid = tokens.astype(f32) + jnp.concatenate(branch, axis=1)
    second_in = rms_scale(resid, gain_two).astype(bf16)

    second_all = plane_gather(second_in)
    logits = jnp.dot(second_all, router_w, preferred_element_type=f32)
    gates_all = jax.nn.softmax(jnp.where(chosen_mask, logits, -jnp.inf), axis=-1)
    own_gates = lax.dynamic_index_in_dim(gates_all, own_expert, 1, keepdims=False)
    own_gates = own_gates.reshape(blocks, block_rows)
    gate_rows = jnp.einsum(
        "bct,bt->bc", dispatch.astype(f32), own_gates, precision=lax.Precision.HIGHEST
    )[:, :, None]
    gate_w = lax.dynamic_index_in_dim(w_gate, own_local, 0, keepdims=False)
    up_w = lax.dynamic_index_in_dim(w_up, own_local, 0, keepdims=False)
    down_w = lax.dynamic_index_in_dim(w_down, own_local, 0, keepdims=False)

    def to_rows(array):
        return jnp.einsum(
            "bct,btd->bcd",
            dispatch,
            array.reshape(blocks, block_rows, model_width),
            preferred_element_type=f32,
        ).astype(bf16)

    def to_tokens(rows):
        def side(part):
            tokens_part = jnp.einsum(
                "bct,bcd->btd", dispatch[part], rows[part].astype(bf16), preferred_element_type=f32
            )
            return tokens_part.astype(bf16).reshape(-1, length, model_width)

        step = blocks // 2 if by_pairs() else blocks
        return [side(slice(at, at + step)) for at in range(0, blocks, step)]

    rows_in = to_rows(second_all)
    rows_cot = to_rows(cot_all)
    gate_pre = jnp.einsum("bcd,df->bcf", rows_in, gate_w, preferred_element_type=f32)
    up_pre = jnp.einsum("bcd,df->bcf", rows_in, up_w, preferred_element_type=f32)
    hidden, act_pull = jax.vjp(expert_act, gate_pre, up_pre)
    gated = (gate_rows * hidden).astype(bf16)
    down_part = jnp.einsum("bcd,bcf->df", rows_cot, gated, preferred_element_type=f32)
    down_sum = scatter_sum(down_part.astype(bf16), "z")
    cot_hidden = jnp.einsum("bcd,fd->bcf", rows_cot, down_w, preferred_element_type=f32)
    gate_signal_rows = jnp.sum(hidden * cot_hidden, axis=-1)
    gate_pgrad, up_pgrad = act_pull(gate_rows * cot_hidden)
    gate_pgrad = gate_pgrad.astype(bf16)
    up_pgrad = up_pgrad.astype(bf16)
    gate_part = jnp.einsum("bcd,bcf->df", rows_in, gate_pgrad, preferred_element_type=f32)
    gate_sum = scatter_sum(gate_part.astype(bf16), "z")
    up_part = jnp.einsum("bcd,bcf->df", rows_in, up_pgrad, preferred_element_type=f32)
    up_sum = scatter_sum(up_part.astype(bf16), "z")
    rows_grad = jnp.einsum("bcf,df->bcd", gate_pgrad, gate_w, preferred_element_type=f32)
    rows_grad = rows_grad + jnp.einsum("bcf,df->bcd", up_pgrad, up_w, preferred_element_type=f32)
    second_back = plane_sum(to_tokens(rows_grad)).astype(f32)
    gate_signal = jnp.einsum(
        "bct,bc->bt", dispatch.astype(f32), gate_signal_rows, precision=lax.Precision.HIGHEST
    )
    gate_signal = exchange(to_place(gate_signal.reshape(plane, length)), PLANE)
    gate_signal = jnp.transpose(
        gate_signal.reshape(2, 2, owners, length), (3, 2, 0, 1)
    ).reshape(length, experts_all)
    expert_rows = jnp.einsum("bcf,fd->bcd", gated, down_w, preferred_element_type=f32)
    mixture = plane_sum(to_tokens(expert_rows)).astype(f32)
    block_out = (resid + mixture).astype(bf16)

    cotangent = out_grad.astype(f32)
    gate_probs = own_block(gates_all, length)
    logit_grad = (
        gate_probs
        * (gate_signal - jnp.sum(gate_probs * gate_signal, axis=-1, keepdims=True))
    ).astype(bf16)
    router_acc = left_product(second_in, logit_grad)
    second_grad = second_back + jnp.dot(logit_grad, router_w.T, preferred_element_type=f32)
    _, norm_two_pull = jax.vjp(rms_scale, resid, gain_two)
    resid_norm_grad, gain_two_grad = norm_two_pull(second_grad)
    resid_grad = cotangent + resid_norm_grad
    branch_grad = resid_grad.astype(bf16)

    if by_pairs():
        attended_all, first_all = gather_two(
            *lax.optimization_barrier((attended, from_row_order(first_in), second_all))[:2]
        )
    else:
        attended_all = plane_gather(after(attended, branch_grad))
    branch_cols = by_source(branch_grad)
    output_part = left_product(attended_all, branch_cols)
    attended_grad = sum(
        lax.dot_general(
            part, output_w[half], (((1,), (1,)), ((), ())), preferred_element_type=f32
        )
        for half, part in enumerate(jnp.split(branch_grad, 2, axis=1))
    )
    attended_grad = from_row_order(attended_grad.astype(bf16))
    attended_grad = attended_grad.reshape(length, HK, group_size, HD)
    prob_bf = probs
    prob_full = prob_bf.astype(f32)
    prob_grad = jnp.einsum("ihrd,jhd->hrij", attended_grad, values_b, preferred_element_type=f32)
    row_inner = jnp.sum(prob_full * prob_grad, axis=-1, keepdims=True)
    score_grad = (prob_full * (prob_grad - row_inner)).astype(bf16)
    query_rot_grad = (
        jnp.einsum("hrij,jhd->ihrd", score_grad, keys_rot, preferred_element_type=f32)
        * score_scale
    )
    query_back = rotary(query_rot_grad.reshape(length, HQ, HD), cosine_tab, -sine_tab)
    query_back = query_back.astype(bf16).reshape(length, HK, q_group)
    key_rot_grad = (
        jnp.einsum("hrij,ihrd->jhd", score_grad, queries, preferred_element_type=f32)
        * score_scale
    )
    key_back = rotary(key_rot_grad, cosine_tab, -sine_tab).astype(bf16)
    value_back = jnp.einsum("hrij,ihrd->jhd", prob_bf, attended_grad, preferred_element_type=f32)
    qkv_back = jnp.concatenate([query_back, key_back, value_back.astype(bf16)], axis=2)
    if not by_pairs():
        first_all = plane_gather(after(first_in, output_part))
    qkv_part = left_product(first_all, by_source(qkv_back.reshape(length, qkv_cols)))
    first_grad = jnp.einsum("ige,gde->id", qkv_back, qkv_w, preferred_element_type=f32)
    _, norm_one_pull = jax.vjp(rms_scale, inputs_f, gain_one)
    input_norm_grad, gain_one_grad = norm_one_pull(first_grad)
    gain_one_grad = from_row_order(gain_one_grad)[0]
    tokens_grad = (resid_grad + from_row_order(input_norm_grad)).astype(bf16)

    narrow_part = jnp.concatenate(
        [router_acc, gain_one_grad[:, None], gain_two_grad[:, None]], axis=1
    )
    narrow_cols = -(-narrow_part.shape[1] // owners) * owners
    narrow_part = jnp.pad(narrow_part, ((0, 0), (0, narrow_cols - narrow_part.shape[1])))
    narrow_part = jnp.transpose(
        narrow_part.reshape(depth, 2, 2, shard_rows, owners, narrow_cols // owners),
        (1, 2, 4, 0, 3, 5),
    ).reshape(plane, depth, shard_rows * narrow_cols // owners)
    narrow_part = jnp.sum(exchange(narrow_part, PLANE), axis=0)
    qkv_width = qkv_cols // plane
    dense_cols = qkv_width + model_width // plane
    narrow_len = narrow_part.shape[1]
    narrow_rows = -(-narrow_len // dense_cols)
    narrow_part = jnp.pad(narrow_part, ((0, 0), (0, narrow_rows * dense_cols - narrow_len)))
    pad_rows = -(local_count * shard_rows + narrow_rows) % 16
    dense_part = jnp.concatenate(
        [
            jnp.concatenate([qkv_part, output_part], axis=1).reshape(
                depth, local_count * shard_rows, dense_cols
            ),
            narrow_part.reshape(depth, narrow_rows, dense_cols),
            jnp.zeros((depth, pad_rows, dense_cols), f32),
        ],
        axis=1,
    ).astype(bf16)
    dense_sum = scatter_sum(dense_part.reshape(-1, dense_cols), "z")
    wide_sum = dense_sum[: local_count * shard_rows].reshape(2, 2, 1, shard_rows, dense_cols)
    wide_sum = jnp.broadcast_to(wide_sum, (2, 2, owners, shard_rows, dense_cols)).reshape(
        plane, shard_rows, dense_cols
    )
    narrow_sum = dense_sum[local_count * shard_rows :][:narrow_rows]
    narrow_sum = jnp.broadcast_to(narrow_sum[None], (plane, narrow_rows, dense_cols))
    pad_rows = -(shard_rows + narrow_rows) % 16
    padding = jnp.zeros((plane, pad_rows, dense_cols), bf16)
    dense_sum = exchange(jnp.concatenate([wide_sum, narrow_sum, padding], axis=1), PLANE)
    wide_sum = jnp.moveaxis(dense_sum[:, :shard_rows].astype(f32), 0, 1)
    qkv_sum = wide_sum[:, :, :qkv_width].reshape(shard_rows, HK, qkv_cols // HK)
    output_sum = wide_sum[:, :, qkv_width:].reshape(shard_rows, model_width)
    narrow_sum = dense_sum[:, shard_rows : shard_rows + narrow_rows].reshape(
        2, 2, owners, narrow_rows * dense_cols
    )
    narrow_sum = narrow_sum[lax.axis_index("y"), lax.axis_index("c"), :, :narrow_len]
    narrow_sum = jnp.moveaxis(
        narrow_sum.reshape(owners, shard_rows, narrow_cols // owners), 0, 1
    ).reshape(shard_rows, narrow_cols).astype(f32)

    def placed(total):
        total = exchange(total, ("y", "c"))
        return total.reshape(local_count, shard_rows, hidden_width).astype(f32)

    return (
        block_out,
        tokens_grad,
        narrow_sum[:, experts_all],
        qkv_sum[:, :, :q_group].reshape(shard_rows, q_cols),
        qkv_sum[:, :, q_group : q_group + HD].reshape(shard_rows, kv_cols),
        qkv_sum[:, :, q_group + HD :].reshape(shard_rows, kv_cols),
        output_sum,
        narrow_sum[:, experts_all + 1],
        narrow_sum[:, :experts_all],
        placed(gate_sum),
        placed(up_sum),
        jnp.swapaxes(placed(down_sum), 1, 2),
    )


def solution(mesh):
    groups, owners = mesh.shape["dp"], mesh.shape["expert"]
    grid = jax.sharding.Mesh(
        mesh.devices.reshape(groups // 4, 2, 2, owners), ("z", "y", "c", "x")
    )
    rows = P(("z", "y", "c", "x"), None)
    shard, shard_rows = P(GROUP), P(GROUP, None)
    expert = P("x", None, None)
    return jax.shard_map(
        local,
        mesh=grid,
        in_specs=(
            rows,
            shard,
            shard_rows,
            shard_rows,
            shard_rows,
            shard_rows,
            shard,
            shard_rows,
            expert,
            expert,
            expert,
            rows,
            P(("z", "y", "c", "x")),
            rows,
        ),
        out_specs=(
            rows,
            rows,
            shard,
            shard_rows,
            shard_rows,
            shard_rows,
            shard_rows,
            shard,
            shard_rows,
            P("x", GROUP, None),
            P("x", GROUP, None),
            P("x", None, GROUP),
        ),
        check_vma=False,
    )
```

```python
import functools
import math

import jax
import jax.numpy as jnp
from jax import lax
from jax.experimental import pallas as pl
from jax.experimental.pallas import tpu as pltpu
from jax.sharding import PartitionSpec as P

HQ = 12
HK = 2
HD = 128
MICRO = 2
PLANE = ("y", "c", "x")
GROUP = ("z", "y", "c")


def rms_scale(values, gain_vec):
    inverse = lax.rsqrt(jnp.mean(values * values, axis=-1, keepdims=True) + 1e-06)
    return values * inverse * gain_vec


def angles(length, head_size):
    positions = jnp.arange(length).astype(jnp.float32)
    freq_rates = jnp.exp(
        -(2.0 * jnp.arange(head_size // 2).astype(jnp.float32) / head_size) * math.log(1000000.0)
    )
    angle_tab = positions[:, None] * freq_rates[None, :]
    return (jnp.cos(angle_tab)[:, None, :], jnp.sin(angle_tab)[:, None, :])


def rotary(values, cosine_tab, sine_tab):
    half_dim = values.shape[-1] // 2
    first_half = values[..., :half_dim]
    second_half = values[..., half_dim:]
    return jnp.concatenate(
        [
            first_half * cosine_tab - second_half * sine_tab,
            second_half * cosine_tab + first_half * sine_tab,
        ],
        axis=-1,
    )


def expert_act(gate_pre, up_pre):
    return jax.nn.gelu(gate_pre, approximate=True) * up_pre


def left_product(left_mat, right_mat):
    return lax.dot_general(
        left_mat, right_mat, (((0,), (0,)), ((), ())), preferred_element_type=jnp.float32
    )


def gather(block, axes):
    return lax.all_gather(block, axes, axis=0, tiled=True)


def exchange(block, axes):
    return lax.all_to_all(block, axes, split_axis=0, concat_axis=0, tiled=True)


def scatter_sum(block, axes):
    return lax.psum_scatter(block, axes, scatter_dimension=0, tiled=True)


def by_owner(cols, parts):
    rows, total = cols.shape
    return jnp.moveaxis(cols.reshape(rows, parts, total // parts), 1, 0).reshape(
        parts * rows, total // parts
    )


def local_wide(
    tokens,
    norm1_gain,
    w_query,
    w_key,
    w_value,
    w_out,
    norm2_gain,
    w_router,
    w_gate,
    w_up,
    w_down,
    expert_ids,
    prefix_len,
    out_grad,
):
    bf16, f32 = jnp.bfloat16, jnp.float32
    length, model_width = tokens.shape
    shard_rows = w_query.shape[0]
    local_count, _, hidden_width = w_gate.shape
    owners = lax.axis_size("x")
    depth = lax.axis_size("z")
    plane = lax.axis_size(PLANE)
    experts_all = w_router.shape[1]
    top_count = expert_ids.shape[1]
    block_rows = length // MICRO
    capacity = 3 * block_rows * top_count // (2 * experts_all)
    plane_rows = plane * length
    blocks = plane_rows // block_rows
    group_size = HQ // HK
    score_scale = HD ** (-0.5)
    q_cols, kv_cols = w_query.shape[1], w_key.shape[1]
    own_local = lax.axis_index(("y", "c"))
    own_expert = lax.axis_index("x") * local_count + own_local
    own_place = lax.axis_index(PLANE)

    narrow = jnp.concatenate([w_router, norm1_gain[:, None], norm2_gain[:, None]], axis=1)
    narrow = jnp.pad(narrow, ((0, 0), (0, -narrow.shape[1] % 128)))
    packed = gather(jnp.concatenate([w_query, w_key, w_value, narrow], axis=1), GROUP)
    qkv_cols = q_cols + 2 * kv_cols
    qkv_w = packed[:, :qkv_cols]
    router_w = packed[:, qkv_cols : qkv_cols + experts_all]
    gains = packed[:, qkv_cols + experts_all : qkv_cols + experts_all + 2].T.astype(f32)
    gain_one, gain_two = gains[0], gains[1]
    output_w = gather(w_out, GROUP)

    ids_all = gather(expert_ids, PLANE)
    cot_all = gather(out_grad, PLANE)
    chosen_mask = jnp.any(
        ids_all[:, :, None] == jnp.arange(experts_all, dtype=jnp.int32)[None, None, :], axis=1
    )
    own_mask = jnp.any(ids_all == own_expert, axis=1).reshape(blocks, block_rows)
    place = jnp.cumsum(own_mask.astype(jnp.int32), axis=1) - 1
    dispatch = (
        own_mask[:, None, :]
        & (place[:, None, :] == jnp.arange(capacity, dtype=jnp.int32)[None, :, None])
    ).astype(bf16)

    cosine_tab, sine_tab = angles(length, HD)
    inputs_f = tokens.astype(f32)
    first_in = rms_scale(inputs_f, gain_one).astype(bf16)
    qkv = jnp.dot(first_in, qkv_w, preferred_element_type=f32)
    queries = (
        rotary(qkv[:, :q_cols].reshape(length, HQ, HD), cosine_tab, sine_tab)
        .astype(bf16)
        .reshape(length, HK, group_size, HD)
    )
    keys_rot = rotary(
        qkv[:, q_cols : q_cols + kv_cols].reshape(length, HK, HD), cosine_tab, sine_tab
    ).astype(bf16)
    values_b = qkv[:, q_cols + kv_cols :].astype(bf16).reshape(length, HK, HD)
    positions = jnp.arange(length)
    allowed = (positions[None, :] <= positions[:, None]) | (positions[None, :] < prefix_len[0])

    def masked_scores():
        scores = jnp.einsum("ihrd,jhd->hrij", queries, keys_rot, preferred_element_type=f32)
        return jnp.where(allowed, scores * score_scale, -1e30)

    masked = masked_scores()
    row_peak = jnp.max(masked, axis=-1, keepdims=True)
    log_total = row_peak + jnp.log(jnp.sum(jnp.exp(masked - row_peak), axis=-1, keepdims=True))
    prob_bf = jnp.exp(masked - log_total).astype(bf16)
    attended = jnp.einsum("hrij,jhd->ihrd", prob_bf, values_b, preferred_element_type=f32)
    attended = attended.reshape(length, HQ * HD).astype(bf16)
    resid = inputs_f + jnp.dot(attended, output_w, preferred_element_type=f32)
    second_in = rms_scale(resid, gain_two).astype(bf16)

    second_all = gather(second_in, PLANE)
    logits = jnp.dot(second_all, router_w, preferred_element_type=f32)
    gates_all = jax.nn.softmax(jnp.where(chosen_mask, logits, -jnp.inf), axis=-1)
    own_gates = lax.dynamic_index_in_dim(gates_all, own_expert, 1, keepdims=False)
    own_gates = own_gates.reshape(blocks, block_rows)
    gate_rows = jnp.einsum(
        "bct,bt->bc", dispatch.astype(f32), own_gates, precision=lax.Precision.HIGHEST
    )[:, :, None]
    gate_w = lax.dynamic_index_in_dim(w_gate, own_local, 0, keepdims=False)
    up_w = lax.dynamic_index_in_dim(w_up, own_local, 0, keepdims=False)
    down_w = lax.dynamic_index_in_dim(w_down, own_local, 0, keepdims=False)

    def to_rows(array):
        return jnp.einsum(
            "bct,btd->bcd",
            dispatch,
            array.reshape(blocks, block_rows, model_width),
            preferred_element_type=f32,
        ).astype(bf16)

    def to_tokens(rows):
        return (
            jnp.einsum("bct,bcd->btd", dispatch, rows.astype(bf16), preferred_element_type=f32)
            .astype(bf16)
            .reshape(plane_rows, model_width)
        )

    rows_in = to_rows(second_all)
    rows_cot = to_rows(cot_all)
    gate_pre = jnp.einsum("bcd,df->bcf", rows_in, gate_w, preferred_element_type=f32)
    up_pre = jnp.einsum("bcd,df->bcf", rows_in, up_w, preferred_element_type=f32)
    hidden, act_pull = jax.vjp(expert_act, gate_pre, up_pre)
    gated = (gate_rows * hidden).astype(bf16)
    down_part = jnp.einsum("bcd,bcf->df", rows_cot, gated, preferred_element_type=f32)
    down_sum = scatter_sum(down_part.astype(bf16), "z")
    cot_hidden = jnp.einsum("bcd,fd->bcf", rows_cot, down_w, preferred_element_type=f32)
    gate_signal_rows = jnp.sum(hidden * cot_hidden, axis=-1)
    gate_pgrad, up_pgrad = act_pull(gate_rows * cot_hidden)
    gate_pgrad = gate_pgrad.astype(bf16)
    up_pgrad = up_pgrad.astype(bf16)
    gate_part = jnp.einsum("bcd,bcf->df", rows_in, gate_pgrad, preferred_element_type=f32)
    gate_sum = scatter_sum(gate_part.astype(bf16), "z")
    up_part = jnp.einsum("bcd,bcf->df", rows_in, up_pgrad, preferred_element_type=f32)
    up_sum = scatter_sum(up_part.astype(bf16), "z")
    rows_grad = jnp.einsum("bcf,df->bcd", gate_pgrad, gate_w, preferred_element_type=f32)
    rows_grad = rows_grad + jnp.einsum("bcf,df->bcd", up_pgrad, up_w, preferred_element_type=f32)
    second_back = scatter_sum(to_tokens(rows_grad), PLANE).astype(f32)
    gate_signal = jnp.einsum(
        "bct,bc->bt", dispatch.astype(f32), gate_signal_rows, precision=lax.Precision.HIGHEST
    )
    gate_signal = exchange(gate_signal.reshape(plane, length), PLANE)
    gate_signal = jnp.transpose(
        gate_signal.reshape(local_count, owners, length), (2, 1, 0)
    ).reshape(length, experts_all)
    expert_rows = jnp.einsum("bcf,fd->bcd", gated, down_w, preferred_element_type=f32)
    mixture = scatter_sum(to_tokens(expert_rows), PLANE).astype(f32)
    block_out = (resid + mixture).astype(bf16)

    cotangent = out_grad.astype(f32)
    gate_probs = lax.dynamic_slice_in_dim(gates_all, own_place * length, length, 0)
    logit_grad = (
        gate_probs
        * (gate_signal - jnp.sum(gate_probs * gate_signal, axis=-1, keepdims=True))
    ).astype(bf16)
    router_acc = left_product(second_in, logit_grad)
    second_grad = second_back + jnp.dot(logit_grad, router_w.T, preferred_element_type=f32)
    _, norm_two_pull = jax.vjp(rms_scale, resid, gain_two)
    resid_norm_grad, gain_two_grad = norm_two_pull(second_grad)
    resid_grad = cotangent + resid_norm_grad
    branch_grad = resid_grad.astype(bf16)

    attended_all = gather(attended, PLANE)
    branch_cols = exchange(by_owner(branch_grad, plane), PLANE)
    output_part = left_product(attended_all, branch_cols)
    attended_grad = jnp.dot(branch_grad, output_w.T, preferred_element_type=f32).astype(bf16)
    attended_grad = attended_grad.reshape(length, HK, group_size, HD)
    masked = masked_scores()
    prob_full = jnp.exp(masked - log_total)
    prob_bf = prob_full.astype(bf16)
    prob_grad = jnp.einsum("ihrd,jhd->hrij", attended_grad, values_b, preferred_element_type=f32)
    row_inner = jnp.sum(prob_full * prob_grad, axis=-1, keepdims=True)
    score_grad = (prob_full * (prob_grad - row_inner)).astype(bf16)
    query_rot_grad = (
        jnp.einsum("hrij,jhd->ihrd", score_grad, keys_rot, preferred_element_type=f32)
        * score_scale
    )
    query_back = rotary(query_rot_grad.reshape(length, HQ, HD), cosine_tab, -sine_tab)
    query_back = query_back.astype(bf16).reshape(length, HQ * HD)
    key_rot_grad = (
        jnp.einsum("hrij,ihrd->jhd", score_grad, queries, preferred_element_type=f32)
        * score_scale
    )
    key_back = rotary(key_rot_grad, cosine_tab, -sine_tab).astype(bf16).reshape(length, HK * HD)
    value_back = jnp.einsum("hrij,ihrd->jhd", prob_bf, attended_grad, preferred_element_type=f32)
    value_back = value_back.astype(bf16).reshape(length, HK * HD)
    qkv_back = jnp.concatenate([query_back, key_back, value_back], axis=1)
    first_all = gather(first_in, PLANE)
    qkv_part = left_product(first_all, exchange(by_owner(qkv_back, plane), PLANE))
    first_grad = lax.dot_general(
        qkv_back, qkv_w, (((1,), (1,)), ((), ())), preferred_element_type=f32
    )
    _, norm_one_pull = jax.vjp(rms_scale, inputs_f, gain_one)
    input_norm_grad, gain_one_grad = norm_one_pull(first_grad)
    tokens_grad = (resid_grad + input_norm_grad).astype(bf16)

    narrow_part = jnp.concatenate(
        [router_acc, gain_one_grad[:, None], gain_two_grad[:, None]], axis=1
    ).astype(bf16)
    narrow_cols = narrow_part.shape[1]
    narrow_sum = lax.psum(scatter_sum(narrow_part, GROUP), "x").astype(f32)
    dense_part = jnp.concatenate([qkv_part, output_part], axis=1).astype(bf16)
    dense_sum = scatter_sum(dense_part, "z")
    dense_cols = dense_sum.shape[1]
    dense_sum = gather(dense_sum, PLANE).reshape(plane, local_count, shard_rows, dense_cols)
    dense_sum = lax.dynamic_index_in_dim(dense_sum, own_local, 1, keepdims=False).astype(f32)
    dense_sum = jnp.moveaxis(dense_sum, 0, 1)
    qkv_width = qkv_cols // plane
    qkv_sum = dense_sum[:, :, :qkv_width].reshape(shard_rows, qkv_cols)
    output_sum = dense_sum[:, :, qkv_width:].reshape(shard_rows, model_width)

    def placed(total):
        total = exchange(total, ("y", "c"))
        return total.reshape(local_count, shard_rows, hidden_width).astype(f32)

    return (
        block_out,
        tokens_grad,
        narrow_sum[:, experts_all],
        qkv_sum[:, :q_cols],
        qkv_sum[:, q_cols : q_cols + kv_cols],
        qkv_sum[:, q_cols + kv_cols :],
        output_sum,
        narrow_sum[:, experts_all + 1],
        narrow_sum[:, :experts_all],
        placed(gate_sum),
        placed(up_sum),
        jnp.swapaxes(placed(down_sum), 1, 2),
    )


def rounded(values):
    return lax.reduce_precision(values, 8, 7).astype(jnp.bfloat16)


def after(block, *others):
    return lax.optimization_barrier((block,) + others)[0]


def swap(block, axis):
    return lax.ppermute(block, axis, [(0, 1), (1, 0)])


def shifts(block):
    depth = lax.axis_size("z")
    return [
        lax.ppermute(block, "z", [(i, (i + k) % depth) for i in range(depth)])
        for k in range(1, depth)
    ]


def plane_sides(block):
    return swap(block, "x"), swap(block, "y")


def plane_corner(sides, before=()):
    over_x, over_y = sides
    half = over_x.shape[0] // 2
    over_y, over_x = lax.optimization_barrier((over_y[:half], over_x[half:]) + before)[:2]
    return jnp.concatenate([swap(over_y, "x"), swap(over_x, "y")], axis=0)


def plane_pieces(block, sides=None, corner=None):
    sides = plane_sides(block) if sides is None else sides
    corner = plane_corner(sides) if corner is None else corner
    pieces = [block, *sides, corner]
    return pieces + [swap(piece, "c") for piece in pieces]


def small_gather(block):
    for axis in ("x", "y", "c"):
        block = jnp.concatenate([block, swap(block, axis)], axis=0)
    return block


def small_group_gather(block, before_plane):
    depth = lax.axis_size("z")
    order = jnp.stack(([block] + shifts(block))[::-1] * 2)
    start = (depth - 1 - lax.axis_index("z")) % depth
    total = lax.dynamic_slice_in_dim(order, start, depth, 0)[:, None, None]
    total = after(total, before_plane)
    for dim, axis in ((1, "y"), (2, "c")):
        other = swap(total, axis)
        last = lax.axis_index(axis) == 1
        pair = [jnp.where(last, other, total), jnp.where(last, total, other)]
        total = jnp.concatenate(pair, axis=dim)
    return total.reshape(-1, block.shape[1])


def add(left, right):
    return rounded(left.astype(jnp.float32) + right.astype(jnp.float32))


def plane_sum(near, far):
    shares = add(near, swap(far, "c"))
    shares = shares.reshape(2, 2, -1, shares.shape[1])
    half = shares.shape[2] // 2
    upper = add(shares[:, 0, :half], swap(shares[:, 1, :half], "x"))
    lower = add(shares[0, :, half:], swap(shares[1, :, half:], "y"))
    upper, lower = add(upper[0], swap(upper[1], "y")), add(lower[0], swap(lower[1], "x"))
    return upper, lower


def cost(micros):
    return pl.CostEstimate(flops=micros * 10**9, bytes_accessed=micros * 10**6, transcendentals=0)


def dot(left, right, dims=((1,), (0,)), precision=None):
    return lax.dot_general(
        left, right, (dims, ((), ())), precision=precision, preferred_element_type=jnp.float32
    )


WHOLE = pl.BlockSpec(memory_space=pltpu.VMEM)
SCALARS = pl.BlockSpec(memory_space=pltpu.SMEM)


def run_kernel(kernel, micros, at, operands, outs, megabytes=40):
    return pl.pallas_call(
        kernel,
        out_shape=[jax.ShapeDtypeStruct(shape, dtype) for shape, dtype in outs],
        in_specs=[SCALARS] + [WHOLE] * len(operands),
        out_specs=[WHOLE] * len(outs),
        cost_estimate=cost(micros),
        compiler_params=pltpu.CompilerParams(vmem_limit_bytes=megabytes * 2**20),
    )(at, *operands)


def place_pieces(at, refs, weight):
    depth = weight.shape[1]
    for n, ref in enumerate(refs):
        dc, dy, dx = n // 4, n // 2 % 2, n % 2
        for k in range(depth):
            z = lax.rem(at[3] + depth - k, depth)
            weight[at[2] ^ dx, z, at[0] ^ dy, at[1] ^ dc] = ref[k]


def rms_kernel(values, gain):
    inverse = lax.rsqrt(jnp.mean(values * values, axis=-1, keepdims=True) + 1e-06)
    return (values * inverse * gain).astype(jnp.bfloat16)


def rms_back(values, gain, grad):
    inverse = lax.rsqrt(jnp.mean(values * values, axis=-1, keepdims=True) + 1e-06)
    normed = values * inverse
    gain_grad = jnp.sum(grad * normed, axis=0, keepdims=True)
    grad = grad * gain
    along = jnp.mean(grad * normed, axis=-1, keepdims=True)
    return inverse * (grad - normed * along), gain_grad


def turned(values, cosine_tab, sine_tab):
    return values * cosine_tab + pltpu.roll(values, HD // 2, 1) * sine_tab


def attend_kernel(at, tokens, gain, cosine, sine, *refs):
    first_ref, query_ref, key_ref, value_ref, prob_ref, out_ref, weight = refs[8:]
    place_pieces(at, refs[:8], weight)
    length = tokens.shape[0]
    first_in = rms_kernel(tokens[...].astype(jnp.float32), gain[...])
    first_ref[...] = first_in
    rows = lax.broadcasted_iota(jnp.int32, (length, length), 0)
    cols = lax.broadcasted_iota(jnp.int32, (length, length), 1)
    allowed = (cols <= rows) | (cols < at[4])
    cosine_tab, sine_tab = cosine[...], sine[...]
    group_size = HQ // HK
    for group in range(HK):
        matrix = weight[group].reshape(first_in.shape[1], -1)
        qkv = dot(first_in, matrix)
        at_key = group_size * HD
        key = turned(qkv[:, at_key : at_key + HD], cosine_tab, sine_tab).astype(jnp.bfloat16)
        value = qkv[:, at_key + HD :].astype(jnp.bfloat16)
        key_ref[:, group * HD : (group + 1) * HD] = key
        value_ref[:, group * HD : (group + 1) * HD] = value
        for member in range(group_size):
            head = group * group_size + member
            here = slice(head * HD, (head + 1) * HD)
            query = turned(qkv[:, member * HD : (member + 1) * HD], cosine_tab, sine_tab)
            query = query.astype(jnp.bfloat16)
            query_ref[:, here] = query
            scores = dot(query, key, ((1,), (1,)))
            scores = jnp.where(allowed, scores * HD ** (-0.5), -1e30)
            weights = jnp.exp(scores - jnp.max(scores, axis=-1, keepdims=True))
            prob = weights * (1.0 / jnp.sum(weights, axis=-1, keepdims=True))
            prob = prob.astype(jnp.bfloat16)
            prob_ref[head] = prob
            out_ref[:, here] = dot(prob, value).astype(jnp.bfloat16)


def project_kernel(at, tokens, gain, attended, *refs):
    resid_ref, second_ref, weight = refs[8:]
    place_pieces(at, refs[:8], weight)
    heads = attended[...]
    halves = [dot(heads, weight[half].reshape(heads.shape[1], -1)) for half in range(2)]
    resid = tokens[...].astype(jnp.float32) + jnp.concatenate(halves, axis=1)
    resid_ref[...] = resid
    second_ref[...] = rms_kernel(resid, gain[...])


def one_hot(slots, capacity, dtype):
    shape = (capacity, slots.shape[1])
    return (slots == lax.broadcasted_iota(jnp.int32, shape, 0)).astype(jnp.float32).astype(dtype)


def expert_kernel(capacity, at, slots, bias, router, *refs):
    second, cot = refs[:8], refs[8:16]
    gate_w, up_w, down_w = refs[16:19]
    rows_in, rows_cot, gated_ref, gate_back, up_back, signal_ref, gates_ref, gate_rows = refs[19:]
    f32, bf16 = jnp.float32, jnp.bfloat16
    length = second[0].shape[0]
    half = length // 2
    step = pl.program_id(0)

    def take(piece):
        tokens = second[piece][...]
        logits = dot(tokens, router[...]) + bias[piece * length : (piece + 1) * length]
        weights = jnp.exp(logits - jnp.max(logits, axis=-1, keepdims=True))
        gates = weights * (1.0 / jnp.sum(weights, axis=-1, keepdims=True))
        if piece == 0:
            gates_ref[...] = gates
        lanes = lax.broadcasted_iota(jnp.int32, (capacity, gates.shape[1]), 1)
        for part in range(2):
            block = 2 * piece + part
            here = slice(part * half, (part + 1) * half)
            place = pl.ds((block % 4) * capacity, capacity)
            pick = one_hot(slots[block : block + 1], capacity, f32)
            rows_in[place] = dot(pick.astype(bf16), tokens[here]).astype(bf16)
            rows_cot[place] = dot(pick.astype(bf16), cot[piece][here]).astype(bf16)
            picked = dot(pick, gates[here], precision=lax.Precision.HIGHEST)
            picked = jnp.where(lanes == at[5], picked, 0.0)
            gate_rows[place] = jnp.sum(picked, axis=1, keepdims=True)

    def take_two(k):
        take(2 * k)
        take(2 * k + 1)

    for k in range(4):
        pl.when(step == k)(functools.partial(take_two, k))
    gate = gate_rows[...]
    gate_pre = dot(rows_in[...], gate_w[...])
    up_pre = dot(rows_in[...], up_w[...])
    cot_hidden = dot(rows_cot[...], down_w[...], ((1,), (1,)))
    scale = math.sqrt(2.0 / math.pi)
    square = gate_pre * gate_pre
    bent = jnp.tanh(scale * gate_pre * (1.0 + 0.044715 * square))
    open_part = 0.5 * (1.0 + bent)
    active = gate_pre * open_part
    slope = open_part + 0.5 * gate_pre * (1.0 - bent * bent) * scale * (
        1.0 + 3 * 0.044715 * square
    )
    hidden = active * up_pre
    gated_ref[...] = (gate * hidden).astype(bf16)
    signal = jnp.sum(hidden * cot_hidden, axis=1, keepdims=True)
    back = gate * cot_hidden
    gate_back[...] = (back * up_pre * slope).astype(bf16)
    up_back[...] = (back * active).astype(bf16)
    for part in range(4):
        pick = one_hot(slots[pl.ds(4 * step + part, 1)], capacity, f32)
        own = signal[part * capacity : (part + 1) * capacity]
        signal_ref[part : part + 1] = jnp.sum(pick * own, axis=0, keepdims=True)


def own_weight(weight, place):
    return pl.BlockSpec(
        (None,) + weight.shape[1:],
        lambda i, at: (at[place], 0, 0),
        pipeline_mode=pl.Buffered(1),
    )


def run_expert(at, slots, bias, router, second, cot, weights, capacity):
    rows, width, hidden = 4 * capacity, second[0].shape[1], weights[0].shape[2]
    bf16, f32 = jnp.bfloat16, jnp.float32
    lanes = slots.shape[1]
    by_step = [(width, bf16), (width, bf16), (hidden, bf16), (hidden, bf16), (hidden, bf16)]
    return pl.pallas_call(
        functools.partial(expert_kernel, capacity),
        out_shape=[jax.ShapeDtypeStruct((4 * rows, cols), dtype) for cols, dtype in by_step]
        + [
            jax.ShapeDtypeStruct((4, 8, lanes), f32),
            jax.ShapeDtypeStruct((second[0].shape[0], bias.shape[1]), f32),
        ],
        grid_spec=pltpu.PrefetchScalarGridSpec(
            num_scalar_prefetch=1,
            grid=(4,),
            in_specs=[WHOLE] * 19 + [own_weight(weight, 6) for weight in weights],
            out_specs=[pl.BlockSpec((rows, cols), lambda i, at: (i, 0)) for cols, _ in by_step]
            + [
                pl.BlockSpec((None, 8, lanes), lambda i, at: (i, 0, 0)),
                pl.BlockSpec((second[0].shape[0], bias.shape[1]), lambda i, at: (0, 0)),
            ],
            scratch_shapes=[pltpu.VMEM((rows, 1), f32)],
        ),
        cost_estimate=cost(20),
        compiler_params=pltpu.CompilerParams(vmem_limit_bytes=52 * 2**20),
    )(at, slots, bias, router, *second, *cot, *weights)


def spread_kernel(capacity, first, dims, at, slots, *refs):
    out_ref = refs[-1]
    half = len(refs) // 2
    step = pl.program_id(0) + first
    rows = sum(
        dot(left[...], right[...], dims) for left, right in zip(refs[:half], refs[half:-1])
    ).astype(jnp.bfloat16)
    block = slots.shape[1]
    for part in range(4):
        pick = one_hot(slots[pl.ds(4 * step + part, 1)], capacity, jnp.bfloat16)
        own = rows[part * capacity : (part + 1) * capacity]
        tokens = dot(pick, own, ((0,), (0,)))
        out_ref[part * block : (part + 1) * block] = tokens.astype(jnp.bfloat16)


def run_spread(first, dims, micros, at, slots, lefts, weights, width):
    rows = lefts[0].shape[0] // 4
    tokens = 4 * slots.shape[1]
    return pl.pallas_call(
        functools.partial(spread_kernel, rows // 4, first, dims),
        out_shape=jax.ShapeDtypeStruct((2 * tokens, width), jnp.bfloat16),
        grid_spec=pltpu.PrefetchScalarGridSpec(
            num_scalar_prefetch=1,
            grid=(2,),
            in_specs=[WHOLE]
            + [pl.BlockSpec((rows, left.shape[1]), lambda i, at: (i + first, 0)) for left in lefts]
            + [own_weight(weight, 6) for weight in weights],
            out_specs=pl.BlockSpec((tokens, width), lambda i, at: (i, 0)),
        ),
        cost_estimate=cost(micros),
        compiler_params=pltpu.CompilerParams(vmem_limit_bytes=40 * 2**20),
    )(at, slots, *lefts, *weights)


def branch_back_kernel(
    at, upper, lower, resid, gain, second, gates, signal, router, cot, weight, *outs
):
    resid_grad_ref, branch_ref, attended_ref, router_ref, gain_ref = outs
    f32, bf16 = jnp.float32, jnp.bfloat16
    chosen = gates[...]
    logit_grad = chosen * (
        signal[...] - jnp.sum(chosen * signal[...], axis=-1, keepdims=True)
    )
    logit_grad = logit_grad.astype(bf16)
    second_grad = jnp.concatenate([upper[...], lower[...]], axis=0).astype(f32)
    second_grad = second_grad + dot(logit_grad, router[...], ((1,), (1,)))
    norm_grad, gain_grad = rms_back(resid[...], gain[...], second_grad)
    gain_ref[...] = gain_grad
    resid_grad = cot[...].astype(f32) + norm_grad
    resid_grad_ref[...] = resid_grad
    branch = resid_grad.astype(bf16)
    branch_ref[...] = branch
    wide = weight.shape[2]
    attended_ref[...] = (
        dot(branch[:, :wide], weight[0], ((1,), (1,)))
        + dot(branch[:, wide:], weight[1], ((1,), (1,)))
    ).astype(bf16)
    router_ref[...] = dot(second[...], logit_grad, ((0,), (0,)))


def attend_back_kernel(at, attended, probs, queries, keys, values, cosine, sine, back_ref):
    f32, bf16 = jnp.float32, jnp.bfloat16
    cosine_tab, sine_tab = cosine[...], -sine[...]
    group_size = HQ // HK
    width = back_ref.shape[2]
    scale = HD ** (-0.5)

    def put(position, block):
        back_ref[position // width, :, position % width : position % width + HD] = block

    for group in range(HK):
        own = slice(group * HD, (group + 1) * HD)
        key, value = keys[:, own], values[:, own]
        key_grad = value_grad = 0.0
        start = group * (group_size + 2) * HD
        for member in range(group_size):
            head = group * group_size + member
            here = slice(head * HD, (head + 1) * HD)
            out_grad, query, prob = attended[:, here], queries[:, here], probs[head]
            prob_grad = dot(out_grad, value, ((1,), (1,)))
            prob_f = prob.astype(f32)
            inner = jnp.sum(prob_f * prob_grad, axis=-1, keepdims=True)
            score_grad = (prob_f * (prob_grad - inner)).astype(bf16)
            query_grad = turned(dot(score_grad, key) * scale, cosine_tab, sine_tab)
            put(start + member * HD, query_grad.astype(bf16))
            key_grad = key_grad + dot(score_grad, query, ((0,), (0,)))
            value_grad = value_grad + dot(prob, out_grad, ((0,), (0,)))
        key_grad = turned(key_grad * scale, cosine_tab, sine_tab)
        put(start + group_size * HD, key_grad.astype(bf16))
        put(start + (group_size + 1) * HD, value_grad.astype(bf16))


def first_back_kernel(at, back, weight, tokens, gain, resid_grad, tokens_ref, gain_ref):
    f32 = jnp.float32
    parts, _, cols = back.shape
    first_grad = 0.0
    for part in range(parts):
        group, place = divmod(part * cols, weight.shape[2])
        first_grad = first_grad + dot(
            back[part], weight[group, :, place : place + cols], ((1,), (1,))
        )
    norm_grad, gain_grad = rms_back(tokens[...].astype(f32), gain[...], first_grad)
    gain_ref[...] = gain_grad
    tokens_ref[...] = (resid_grad[...] + norm_grad).astype(jnp.bfloat16)


def weight_grad_kernel(at, cols, *refs):
    out_ref = refs[-1]
    total = 0.0
    for n, left in enumerate(refs[:-1]):
        dc, dy, dx = n // 4, n // 2 % 2, n % 2
        place = 4 * (at[0] ^ dy) + 2 * (at[1] ^ dc) + (at[2] ^ dx)
        total = total + dot(left[...], cols[place], ((0,), (0,)))
    out_ref[...] = total.astype(jnp.bfloat16)


def local_pairs(
    tokens,
    norm1_gain,
    w_query,
    w_key,
    w_value,
    w_out,
    norm2_gain,
    w_router,
    w_gate,
    w_up,
    w_down,
    expert_ids,
    prefix_len,
    out_grad,
):
    bf16, f32 = jnp.bfloat16, jnp.float32
    length, model_width = tokens.shape
    shard_rows = w_query.shape[0]
    local_count, _, hidden_width = w_gate.shape
    owners = lax.axis_size("x")
    depth = lax.axis_size("z")
    plane = lax.axis_size(PLANE)
    experts_all = w_router.shape[1]
    block_rows = length // MICRO
    capacity = 3 * block_rows * expert_ids.shape[1] // (2 * experts_all)
    plane_rows = plane * length
    blocks = plane_rows // block_rows
    q_cols, kv_cols = w_query.shape[1], w_key.shape[1]
    qkv_cols = q_cols + 2 * kv_cols
    q_group, out_half = q_cols // HK, model_width // 2
    y, c, x, z = (lax.axis_index(axis) for axis in ("y", "c", "x", "z"))
    own_local = 2 * y + c
    own_expert = x * local_count + own_local
    at = jnp.stack([y, c, x, z, prefix_len[0], own_expert, own_local])

    own_half = jnp.concatenate(
        [
            lax.dynamic_slice_in_dim(part, x * (part.shape[1] // 2), part.shape[1] // 2, 1)
            for part in (w_query, w_key, w_value, w_out)
        ],
        axis=1,
    )
    narrow = jnp.concatenate([w_router, norm1_gain[:, None], norm2_gain[:, None]], axis=1)
    cot_sides = plane_sides(out_grad)
    column = [own_half] + shifts(own_half)
    qkv_half = qkv_cols // 2
    qkv_column = jnp.stack([part[:, :qkv_half] for part in column])
    out_column = jnp.stack([part[:, qkv_half:] for part in column])
    qkv_column = after(qkv_column, *cot_sides)
    qkv_sides = plane_sides(qkv_column)
    qkv_corner = plane_corner(qkv_sides)
    narrow = small_group_gather(narrow, qkv_corner)
    out_sides = plane_sides(after(out_column, narrow))
    out_corner = plane_corner(out_sides)
    qkv_pieces = plane_pieces(qkv_column, qkv_sides, qkv_corner)
    out_pieces = plane_pieces(out_column, out_sides, out_corner)
    ids_all = small_gather(after(expert_ids, out_corner))
    cot_corner = plane_corner(cot_sides, (out_corner,))
    cot_pieces = plane_pieces(out_grad, cot_sides, cot_corner)
    router_w = jnp.pad(narrow[:, :experts_all], ((0, 0), (0, 128 - experts_all)))
    gains = narrow[:, experts_all : experts_all + 2].T.astype(f32)
    gain_one, gain_two = gains[:1], gains[1:]

    expert_range = jnp.arange(128, dtype=jnp.int32)
    chosen_mask = jnp.any(ids_all[:, :, None] == expert_range[None, None, :], axis=1)
    bias = jnp.where(chosen_mask, 0.0, -1e30).astype(f32)
    own_mask = jnp.any(ids_all == own_expert, axis=1).reshape(blocks, block_rows)
    place = jnp.cumsum(own_mask.astype(jnp.int32), axis=1) - 1
    slots = jnp.where(own_mask, place, -1)

    cosine_tab, sine_tab = angles(length, HD)
    cosine_all = jnp.concatenate([cosine_tab, cosine_tab], axis=2)[:, 0]
    sine_all = jnp.concatenate([-sine_tab, sine_tab], axis=2)[:, 0]
    weight_lead = (2, depth, 2, 2, shard_rows)
    first_in, queries, keys_rot, values_b, probs, attended, qkv_w = run_kernel(
        attend_kernel,
        11,
        at,
        (tokens, gain_one, cosine_all, sine_all, *qkv_pieces),
        [
            ((length, model_width), bf16),
            ((length, q_cols), bf16),
            ((length, kv_cols), bf16),
            ((length, kv_cols), bf16),
            ((HQ, length, length), bf16),
            ((length, q_cols), bf16),
            (weight_lead + (qkv_half,), bf16),
        ],
    )
    resid, second_in, output_w = run_kernel(
        project_kernel,
        4,
        at,
        (tokens, gain_two, attended, *out_pieces),
        [
            ((length, model_width), f32),
            ((length, model_width), bf16),
            (weight_lead + (out_half,), bf16),
        ],
    )
    qkv_w = qkv_w.reshape(HK, model_width, qkv_half)
    output_w = output_w.reshape(2, q_cols, out_half)

    second_pieces = plane_pieces(second_in)
    rows_in, rows_cot, gated, gate_back, up_back, signal, gates = run_expert(
        at, slots, bias, router_w, second_pieces, cot_pieces, (w_gate, w_up, w_down), capacity
    )
    down_sum = scatter_sum(left_product(rows_cot, gated).astype(bf16), "z")
    by_rows = ((1,), (1,))
    second_far, second_near = (
        run_spread(
            first, by_rows, 5, at, slots, (gate_back, up_back), (w_gate, w_up), model_width
        )
        for first in (2, 0)
    )
    upper, lower = plane_sum(second_near, second_far)
    gate_sum = scatter_sum(left_product(rows_in, gate_back).astype(bf16), "z")
    up_sum = scatter_sum(left_product(rows_in, up_back).astype(bf16), "z")
    signal = signal[:, :4].reshape(2, 2, 2, length)
    for dim, axis in enumerate(("c", "y", "x")):
        signal = jnp.where(lax.axis_index(axis) == 1, jnp.flip(signal, dim), signal)
    signal = exchange(jnp.swapaxes(signal, 0, 1).reshape(plane, length), PLANE)
    signal = jnp.transpose(signal.reshape(2, 2, owners, length), (3, 2, 0, 1))
    signal = signal.reshape(length, experts_all)
    signal = jnp.pad(signal, ((0, 0), (0, 128 - experts_all)))

    resid_grad, branch_grad, attended_grad, router_acc, gain_two_grad = run_kernel(
        branch_back_kernel,
        6,
        at,
        (upper, lower, resid, gain_two, second_in, gates, signal, router_w, out_grad, output_w),
        [
            ((length, model_width), f32),
            ((length, model_width), bf16),
            ((length, q_cols), bf16),
            ((model_width, 128), f32),
            ((1, model_width), f32),
        ],
    )
    (qkv_back,) = run_kernel(
        attend_back_kernel,
        12,
        at,
        (attended_grad, probs, queries, keys_rot, values_b, cosine_all, sine_all),
        [((plane, length, qkv_cols // plane), bf16)],
    )
    branch_back = jnp.moveaxis(branch_grad.reshape(length, plane, model_width // plane), 1, 0)
    branch_cols = exchange(branch_back, PLANE)
    qkv_cols_back = exchange(qkv_back, PLANE)
    tokens_grad, gain_one_grad = run_kernel(
        first_back_kernel,
        6,
        at,
        (qkv_back, qkv_w, tokens, gain_one, resid_grad),
        [((length, model_width), bf16), ((1, model_width), f32)],
    )

    both = jnp.concatenate(lax.optimization_barrier((attended, first_in, gates))[:2], axis=0)
    both_pieces = plane_pieces(both)
    (output_part,) = run_kernel(
        weight_grad_kernel,
        5,
        at,
        (branch_cols, *[piece[:length] for piece in both_pieces]),
        [((q_cols, model_width // plane), bf16)],
    )
    (qkv_part,) = run_kernel(
        weight_grad_kernel,
        5,
        at,
        (qkv_cols_back, *[piece[length:] for piece in both_pieces]),
        [((model_width, qkv_cols // plane), bf16)],
    )
    narrow_part = jnp.concatenate(
        [router_acc[:, :experts_all], gain_one_grad.T, gain_two_grad.T], axis=1
    )
    narrow_cols = -(-narrow_part.shape[1] // owners) * owners
    narrow_part = jnp.pad(narrow_part, ((0, 0), (0, narrow_cols - narrow_part.shape[1])))
    narrow_part = jnp.transpose(
        narrow_part.reshape(depth, 2, 2, shard_rows, owners, narrow_cols // owners),
        (1, 2, 4, 0, 3, 5),
    ).reshape(plane, depth, shard_rows * narrow_cols // owners)
    narrow_part = jnp.sum(exchange(narrow_part, PLANE), axis=0)
    qkv_width = qkv_cols // plane
    dense_cols = qkv_width + model_width // plane
    narrow_len = narrow_part.shape[1]
    narrow_rows = -(-narrow_len // dense_cols)
    narrow_part = jnp.pad(narrow_part, ((0, 0), (0, narrow_rows * dense_cols - narrow_len)))
    pad_rows = -(local_count * shard_rows + narrow_rows) % 16
    dense_part = jnp.concatenate(
        [
            jnp.concatenate([qkv_part, output_part], axis=1).reshape(
                depth, local_count * shard_rows, dense_cols
            ),
            narrow_part.reshape(depth, narrow_rows, dense_cols).astype(bf16),
            jnp.zeros((depth, pad_rows, dense_cols), bf16),
        ],
        axis=1,
    )
    dense_sum = scatter_sum(dense_part.reshape(-1, dense_cols), "z")
    wide_sum = dense_sum[: local_count * shard_rows].reshape(2, 2, 1, shard_rows, dense_cols)
    wide_sum = jnp.broadcast_to(wide_sum, (2, 2, owners, shard_rows, dense_cols)).reshape(
        plane, shard_rows, dense_cols
    )
    narrow_sum = dense_sum[local_count * shard_rows :][:narrow_rows]
    narrow_sum = jnp.broadcast_to(narrow_sum[None], (plane, narrow_rows, dense_cols))
    pad_rows = -(shard_rows + narrow_rows) % 16
    padding = jnp.zeros((plane, pad_rows, dense_cols), bf16)
    dense_sum = exchange(jnp.concatenate([wide_sum, narrow_sum, padding], axis=1), PLANE)
    wide_sum = jnp.moveaxis(dense_sum[:, :shard_rows].astype(f32), 0, 1)
    qkv_sum = wide_sum[:, :, :qkv_width].reshape(shard_rows, HK, qkv_half)
    output_sum = wide_sum[:, :, qkv_width:].reshape(shard_rows, model_width)
    narrow_sum = dense_sum[:, shard_rows : shard_rows + narrow_rows].reshape(
        2, 2, owners, narrow_rows * dense_cols
    )
    narrow_sum = narrow_sum[y, c, :, :narrow_len].reshape(owners, shard_rows, -1)
    narrow_sum = jnp.moveaxis(narrow_sum, 0, 1).reshape(shard_rows, narrow_cols).astype(f32)

    in_order = ((1,), (0,))
    gated_late = after(gated, attended_grad)
    mixture_far, mixture_near = (
        run_spread(first, in_order, 4, at, slots, (gated_late,), (w_down,), model_width)
        for first in (2, 0)
    )
    mixture = jnp.concatenate(plane_sum(mixture_near, mixture_far), axis=0)
    block_out = (resid + mixture.astype(f32)).astype(bf16)

    def placed(total):
        total = exchange(total, ("y", "c"))
        return total.reshape(local_count, shard_rows, hidden_width).astype(f32)

    return (
        block_out,
        tokens_grad,
        narrow_sum[:, experts_all],
        qkv_sum[:, :, :q_group].reshape(shard_rows, q_cols),
        qkv_sum[:, :, q_group : q_group + HD].reshape(shard_rows, kv_cols),
        qkv_sum[:, :, q_group + HD :].reshape(shard_rows, kv_cols),
        output_sum,
        narrow_sum[:, experts_all + 1],
        narrow_sum[:, :experts_all],
        placed(gate_sum),
        placed(up_sum),
        jnp.swapaxes(placed(down_sum), 1, 2),
    )


def solution(mesh):
    groups, owners = mesh.shape["dp"], mesh.shape["expert"]
    grid = jax.sharding.Mesh(
        mesh.devices.reshape(groups // 4, 2, 2, owners), ("z", "y", "c", "x")
    )
    rows = P(("z", "y", "c", "x"), None)
    shard, shard_rows = P(GROUP), P(GROUP, None)
    expert = P("x", None, None)
    return jax.shard_map(
        local_pairs if owners == 2 else local_wide,
        mesh=grid,
        in_specs=(
            rows,
            shard,
            shard_rows,
            shard_rows,
            shard_rows,
            shard_rows,
            shard,
            shard_rows,
            expert,
            expert,
            expert,
            rows,
            P(("z", "y", "c", "x")),
            rows,
        ),
        out_specs=(
            rows,
            rows,
            shard,
            shard_rows,
            shard_rows,
            shard_rows,
            shard_rows,
            shard,
            shard_rows,
            P("x", GROUP, None),
            P("x", GROUP, None),
            P("x", None, GROUP),
        ),
        check_vma=False,
    )
```

```python
import functools
import math

import jax
import jax.numpy as jnp
from jax import lax
from jax.experimental import pallas as pl
from jax.experimental.pallas import tpu as pltpu
from jax.sharding import PartitionSpec as P

HQ = 12
HK = 2
HD = 128
MICRO = 2
PLANE = ("y", "c", "x")
GROUP = ("z", "y", "c")


def rms_scale(values, gain_vec):
    inverse = lax.rsqrt(jnp.mean(values * values, axis=-1, keepdims=True) + 1e-06)
    return values * inverse * gain_vec


def angles(length, head_size):
    positions = jnp.arange(length).astype(jnp.float32)
    freq_rates = jnp.exp(
        -(2.0 * jnp.arange(head_size // 2).astype(jnp.float32) / head_size) * math.log(1000000.0)
    )
    angle_tab = positions[:, None] * freq_rates[None, :]
    return (jnp.cos(angle_tab)[:, None, :], jnp.sin(angle_tab)[:, None, :])


def rotary(values, cosine_tab, sine_tab):
    half_dim = values.shape[-1] // 2
    first_half = values[..., :half_dim]
    second_half = values[..., half_dim:]
    return jnp.concatenate(
        [
            first_half * cosine_tab - second_half * sine_tab,
            second_half * cosine_tab + first_half * sine_tab,
        ],
        axis=-1,
    )


def expert_act(gate_pre, up_pre):
    return jax.nn.gelu(gate_pre, approximate=True) * up_pre


def left_product(left_mat, right_mat):
    return lax.dot_general(
        left_mat, right_mat, (((0,), (0,)), ((), ())), preferred_element_type=jnp.float32
    )


def gather(block, axes):
    return lax.all_gather(block, axes, axis=0, tiled=True)


def exchange(block, axes):
    return lax.all_to_all(block, axes, split_axis=0, concat_axis=0, tiled=True)


def scatter_sum(block, axes):
    return lax.psum_scatter(block, axes, scatter_dimension=0, tiled=True)


def by_owner(cols, parts):
    rows, total = cols.shape
    return jnp.moveaxis(cols.reshape(rows, parts, total // parts), 1, 0).reshape(
        parts * rows, total // parts
    )


def local_wide(
    tokens,
    norm1_gain,
    w_query,
    w_key,
    w_value,
    w_out,
    norm2_gain,
    w_router,
    w_gate,
    w_up,
    w_down,
    expert_ids,
    prefix_len,
    out_grad,
):
    bf16, f32 = jnp.bfloat16, jnp.float32
    length, model_width = tokens.shape
    shard_rows = w_query.shape[0]
    local_count, _, hidden_width = w_gate.shape
    owners = lax.axis_size("x")
    depth = lax.axis_size("z")
    plane = lax.axis_size(PLANE)
    experts_all = w_router.shape[1]
    top_count = expert_ids.shape[1]
    block_rows = length // MICRO
    capacity = 3 * block_rows * top_count // (2 * experts_all)
    plane_rows = plane * length
    blocks = plane_rows // block_rows
    group_size = HQ // HK
    score_scale = HD ** (-0.5)
    q_cols, kv_cols = w_query.shape[1], w_key.shape[1]
    own_local = lax.axis_index(("y", "c"))
    own_expert = lax.axis_index("x") * local_count + own_local
    own_place = lax.axis_index(PLANE)

    narrow = jnp.concatenate([w_router, norm1_gain[:, None], norm2_gain[:, None]], axis=1)
    narrow = jnp.pad(narrow, ((0, 0), (0, -narrow.shape[1] % 128)))
    packed = gather(jnp.concatenate([w_query, w_key, w_value, narrow], axis=1), GROUP)
    qkv_cols = q_cols + 2 * kv_cols
    qkv_w = packed[:, :qkv_cols]
    router_w = packed[:, qkv_cols : qkv_cols + experts_all]
    gains = packed[:, qkv_cols + experts_all : qkv_cols + experts_all + 2].T.astype(f32)
    gain_one, gain_two = gains[0], gains[1]
    output_w = gather(w_out, GROUP)

    ids_all = gather(expert_ids, PLANE)
    cot_all = gather(out_grad, PLANE)
    chosen_mask = jnp.any(
        ids_all[:, :, None] == jnp.arange(experts_all, dtype=jnp.int32)[None, None, :], axis=1
    )
    own_mask = jnp.any(ids_all == own_expert, axis=1).reshape(blocks, block_rows)
    place = jnp.cumsum(own_mask.astype(jnp.int32), axis=1) - 1
    dispatch = (
        own_mask[:, None, :]
        & (place[:, None, :] == jnp.arange(capacity, dtype=jnp.int32)[None, :, None])
    ).astype(bf16)

    cosine_tab, sine_tab = angles(length, HD)
    inputs_f = tokens.astype(f32)
    first_in = rms_scale(inputs_f, gain_one).astype(bf16)
    qkv = jnp.dot(first_in, qkv_w, preferred_element_type=f32)
    queries = (
        rotary(qkv[:, :q_cols].reshape(length, HQ, HD), cosine_tab, sine_tab)
        .astype(bf16)
        .reshape(length, HK, group_size, HD)
    )
    keys_rot = rotary(
        qkv[:, q_cols : q_cols + kv_cols].reshape(length, HK, HD), cosine_tab, sine_tab
    ).astype(bf16)
    values_b = qkv[:, q_cols + kv_cols :].astype(bf16).reshape(length, HK, HD)
    positions = jnp.arange(length)
    allowed = (positions[None, :] <= positions[:, None]) | (positions[None, :] < prefix_len[0])

    def masked_scores():
        scores = jnp.einsum("ihrd,jhd->hrij", queries, keys_rot, preferred_element_type=f32)
        return jnp.where(allowed, scores * score_scale, -1e30)

    masked = masked_scores()
    row_peak = jnp.max(masked, axis=-1, keepdims=True)
    log_total = row_peak + jnp.log(jnp.sum(jnp.exp(masked - row_peak), axis=-1, keepdims=True))
    prob_bf = jnp.exp(masked - log_total).astype(bf16)
    attended = jnp.einsum("hrij,jhd->ihrd", prob_bf, values_b, preferred_element_type=f32)
    attended = attended.reshape(length, HQ * HD).astype(bf16)
    resid = inputs_f + jnp.dot(attended, output_w, preferred_element_type=f32)
    second_in = rms_scale(resid, gain_two).astype(bf16)

    second_all = gather(second_in, PLANE)
    logits = jnp.dot(second_all, router_w, preferred_element_type=f32)
    gates_all = jax.nn.softmax(jnp.where(chosen_mask, logits, -jnp.inf), axis=-1)
    own_gates = lax.dynamic_index_in_dim(gates_all, own_expert, 1, keepdims=False)
    own_gates = own_gates.reshape(blocks, block_rows)
    gate_rows = jnp.einsum(
        "bct,bt->bc", dispatch.astype(f32), own_gates, precision=lax.Precision.HIGHEST
    )[:, :, None]
    gate_w = lax.dynamic_index_in_dim(w_gate, own_local, 0, keepdims=False)
    up_w = lax.dynamic_index_in_dim(w_up, own_local, 0, keepdims=False)
    down_w = lax.dynamic_index_in_dim(w_down, own_local, 0, keepdims=False)

    def to_rows(array):
        return jnp.einsum(
            "bct,btd->bcd",
            dispatch,
            array.reshape(blocks, block_rows, model_width),
            preferred_element_type=f32,
        ).astype(bf16)

    def to_tokens(rows):
        return (
            jnp.einsum("bct,bcd->btd", dispatch, rows.astype(bf16), preferred_element_type=f32)
            .astype(bf16)
            .reshape(plane_rows, model_width)
        )

    rows_in = to_rows(second_all)
    rows_cot = to_rows(cot_all)
    gate_pre = jnp.einsum("bcd,df->bcf", rows_in, gate_w, preferred_element_type=f32)
    up_pre = jnp.einsum("bcd,df->bcf", rows_in, up_w, preferred_element_type=f32)
    hidden, act_pull = jax.vjp(expert_act, gate_pre, up_pre)
    gated = (gate_rows * hidden).astype(bf16)
    down_part = jnp.einsum("bcd,bcf->df", rows_cot, gated, preferred_element_type=f32)
    down_sum = scatter_sum(down_part.astype(bf16), "z")
    cot_hidden = jnp.einsum("bcd,fd->bcf", rows_cot, down_w, preferred_element_type=f32)
    gate_signal_rows = jnp.sum(hidden * cot_hidden, axis=-1)
    gate_pgrad, up_pgrad = act_pull(gate_rows * cot_hidden)
    gate_pgrad = gate_pgrad.astype(bf16)
    up_pgrad = up_pgrad.astype(bf16)
    gate_part = jnp.einsum("bcd,bcf->df", rows_in, gate_pgrad, preferred_element_type=f32)
    gate_sum = scatter_sum(gate_part.astype(bf16), "z")
    up_part = jnp.einsum("bcd,bcf->df", rows_in, up_pgrad, preferred_element_type=f32)
    up_sum = scatter_sum(up_part.astype(bf16), "z")
    rows_grad = jnp.einsum("bcf,df->bcd", gate_pgrad, gate_w, preferred_element_type=f32)
    rows_grad = rows_grad + jnp.einsum("bcf,df->bcd", up_pgrad, up_w, preferred_element_type=f32)
    second_back = scatter_sum(to_tokens(rows_grad), PLANE).astype(f32)
    gate_signal = jnp.einsum(
        "bct,bc->bt", dispatch.astype(f32), gate_signal_rows, precision=lax.Precision.HIGHEST
    )
    gate_signal = exchange(gate_signal.reshape(plane, length), PLANE)
    gate_signal = jnp.transpose(
        gate_signal.reshape(local_count, owners, length), (2, 1, 0)
    ).reshape(length, experts_all)
    expert_rows = jnp.einsum("bcf,fd->bcd", gated, down_w, preferred_element_type=f32)
    mixture = scatter_sum(to_tokens(expert_rows), PLANE).astype(f32)
    block_out = (resid + mixture).astype(bf16)

    cotangent = out_grad.astype(f32)
    gate_probs = lax.dynamic_slice_in_dim(gates_all, own_place * length, length, 0)
    logit_grad = (
        gate_probs
        * (gate_signal - jnp.sum(gate_probs * gate_signal, axis=-1, keepdims=True))
    ).astype(bf16)
    router_acc = left_product(second_in, logit_grad)
    second_grad = second_back + jnp.dot(logit_grad, router_w.T, preferred_element_type=f32)
    _, norm_two_pull = jax.vjp(rms_scale, resid, gain_two)
    resid_norm_grad, gain_two_grad = norm_two_pull(second_grad)
    resid_grad = cotangent + resid_norm_grad
    branch_grad = resid_grad.astype(bf16)

    attended_all = gather(attended, PLANE)
    branch_cols = exchange(by_owner(branch_grad, plane), PLANE)
    output_part = left_product(attended_all, branch_cols)
    attended_grad = jnp.dot(branch_grad, output_w.T, preferred_element_type=f32).astype(bf16)
    attended_grad = attended_grad.reshape(length, HK, group_size, HD)
    masked = masked_scores()
    prob_full = jnp.exp(masked - log_total)
    prob_bf = prob_full.astype(bf16)
    prob_grad = jnp.einsum("ihrd,jhd->hrij", attended_grad, values_b, preferred_element_type=f32)
    row_inner = jnp.sum(prob_full * prob_grad, axis=-1, keepdims=True)
    score_grad = (prob_full * (prob_grad - row_inner)).astype(bf16)
    query_rot_grad = (
        jnp.einsum("hrij,jhd->ihrd", score_grad, keys_rot, preferred_element_type=f32)
        * score_scale
    )
    query_back = rotary(query_rot_grad.reshape(length, HQ, HD), cosine_tab, -sine_tab)
    query_back = query_back.astype(bf16).reshape(length, HQ * HD)
    key_rot_grad = (
        jnp.einsum("hrij,ihrd->jhd", score_grad, queries, preferred_element_type=f32)
        * score_scale
    )
    key_back = rotary(key_rot_grad, cosine_tab, -sine_tab).astype(bf16).reshape(length, HK * HD)
    value_back = jnp.einsum("hrij,ihrd->jhd", prob_bf, attended_grad, preferred_element_type=f32)
    value_back = value_back.astype(bf16).reshape(length, HK * HD)
    qkv_back = jnp.concatenate([query_back, key_back, value_back], axis=1)
    first_all = gather(first_in, PLANE)
    qkv_part = left_product(first_all, exchange(by_owner(qkv_back, plane), PLANE))
    first_grad = lax.dot_general(
        qkv_back, qkv_w, (((1,), (1,)), ((), ())), preferred_element_type=f32
    )
    _, norm_one_pull = jax.vjp(rms_scale, inputs_f, gain_one)
    input_norm_grad, gain_one_grad = norm_one_pull(first_grad)
    tokens_grad = (resid_grad + input_norm_grad).astype(bf16)

    narrow_part = jnp.concatenate(
        [router_acc, gain_one_grad[:, None], gain_two_grad[:, None]], axis=1
    ).astype(bf16)
    narrow_cols = narrow_part.shape[1]
    narrow_sum = lax.psum(scatter_sum(narrow_part, GROUP), "x").astype(f32)
    dense_part = jnp.concatenate([qkv_part, output_part], axis=1).astype(bf16)
    dense_sum = scatter_sum(dense_part, "z")
    dense_cols = dense_sum.shape[1]
    dense_sum = gather(dense_sum, PLANE).reshape(plane, local_count, shard_rows, dense_cols)
    dense_sum = lax.dynamic_index_in_dim(dense_sum, own_local, 1, keepdims=False).astype(f32)
    dense_sum = jnp.moveaxis(dense_sum, 0, 1)
    qkv_width = qkv_cols // plane
    qkv_sum = dense_sum[:, :, :qkv_width].reshape(shard_rows, qkv_cols)
    output_sum = dense_sum[:, :, qkv_width:].reshape(shard_rows, model_width)

    def placed(total):
        total = exchange(total, ("y", "c"))
        return total.reshape(local_count, shard_rows, hidden_width).astype(f32)

    return (
        block_out,
        tokens_grad,
        narrow_sum[:, experts_all],
        qkv_sum[:, :q_cols],
        qkv_sum[:, q_cols : q_cols + kv_cols],
        qkv_sum[:, q_cols + kv_cols :],
        output_sum,
        narrow_sum[:, experts_all + 1],
        narrow_sum[:, :experts_all],
        placed(gate_sum),
        placed(up_sum),
        jnp.swapaxes(placed(down_sum), 1, 2),
    )


def rounded(values):
    return lax.reduce_precision(values, 8, 7).astype(jnp.bfloat16)


def after(block, *others):
    return lax.optimization_barrier((block,) + others)[0]


def swap(block, axis):
    return lax.ppermute(block, axis, [(0, 1), (1, 0)])


def shifts(block):
    depth = lax.axis_size("z")
    return [
        lax.ppermute(block, "z", [(i, (i + k) % depth) for i in range(depth)])
        for k in range(1, depth)
    ]


def plane_sides(block):
    return swap(block, "x"), swap(block, "y")


def plane_corner(sides, before=()):
    over_x, over_y = sides
    half = over_x.shape[0] // 2
    over_y, over_x = lax.optimization_barrier((over_y[:half], over_x[half:]) + before)[:2]
    return jnp.concatenate([swap(over_y, "x"), swap(over_x, "y")], axis=0)


def plane_pieces(block, sides=None, corner=None):
    sides = plane_sides(block) if sides is None else sides
    corner = plane_corner(sides) if corner is None else corner
    pieces = [block, *sides, corner]
    return pieces + [swap(piece, "c") for piece in pieces]


def small_gather(block):
    for axis in ("x", "y", "c"):
        block = jnp.concatenate([block, swap(block, axis)], axis=0)
    return block


def small_group_gather(block):
    depth = lax.axis_size("z")
    order = jnp.stack(([block] + shifts(block))[::-1] * 2)
    start = (depth - 1 - lax.axis_index("z")) % depth
    total = lax.dynamic_slice_in_dim(order, start, depth, 0)[:, None, None]
    for dim, axis in ((1, "y"), (2, "c")):
        other = swap(total, axis)
        last = lax.axis_index(axis) == 1
        pair = [jnp.where(last, other, total), jnp.where(last, total, other)]
        total = jnp.concatenate(pair, axis=dim)
    return total.reshape(-1, block.shape[1])


def add(left, right):
    return rounded(left.astype(jnp.float32) + right.astype(jnp.float32))


def over_core(near, far):
    return add(near, swap(far, "c"))


def early_sums(over_x, over_y):
    half = over_x.shape[0] // 2
    return swap(over_x[:half], "x"), swap(over_y[half:], "y")


def corner_first(corner):
    half = corner.shape[0] // 2
    return swap(corner[:half], "x"), swap(corner[half:], "y")


def corner_last(over_x, over_y, first):
    half = over_x.shape[0] // 2
    return swap(add(over_y[:half], first[0]), "y"), swap(add(over_x[half:], first[1]), "x")


def cost(micros):
    return pl.CostEstimate(flops=micros * 10**9, bytes_accessed=micros * 10**6, transcendentals=0)


def dot(left, right, dims=((1,), (0,)), precision=None):
    return lax.dot_general(
        left, right, (dims, ((), ())), precision=precision, preferred_element_type=jnp.float32
    )


WHOLE = pl.BlockSpec(memory_space=pltpu.VMEM)
SCALARS = pl.BlockSpec(memory_space=pltpu.SMEM)


def run_kernel(kernel, micros, at, operands, outs, megabytes=40, scratch=()):
    return pl.pallas_call(
        kernel,
        out_shape=[jax.ShapeDtypeStruct(shape, dtype) for shape, dtype in outs],
        in_specs=[SCALARS] + [WHOLE] * len(operands),
        out_specs=[WHOLE] * len(outs),
        scratch_shapes=scratch,
        cost_estimate=cost(micros),
        compiler_params=pltpu.CompilerParams(vmem_limit_bytes=megabytes * 2**20),
    )(at, *operands)


def place_pieces(at, refs, weight):
    depth = weight.shape[1]
    for n, ref in enumerate(refs):
        dc, dy, dx = n // 4, n // 2 % 2, n % 2
        for k in range(depth):
            z = lax.rem(at[3] + depth - k, depth)
            weight[at[2] ^ dx, z, at[0] ^ dy, at[1] ^ dc] = ref[k]


def rms_kernel(values, gain):
    inverse = lax.rsqrt(jnp.mean(values * values, axis=-1, keepdims=True) + 1e-06)
    return (values * inverse * gain).astype(jnp.bfloat16)


def rms_back(values, gain, grad):
    inverse = lax.rsqrt(jnp.mean(values * values, axis=-1, keepdims=True) + 1e-06)
    normed = values * inverse
    gain_grad = jnp.sum(grad * normed, axis=0, keepdims=True)
    grad = grad * gain
    along = jnp.mean(grad * normed, axis=-1, keepdims=True)
    return inverse * (grad - normed * along), gain_grad


def turned(values, cosine_tab, sine_tab):
    return values * cosine_tab + pltpu.roll(values, HD // 2, 1) * sine_tab


def attend_kernel(at, tokens, gain, cosine, sine, *refs):
    first_ref, query_ref, key_ref, value_ref, prob_ref, out_ref, weight = refs[8:]
    place_pieces(at, refs[:8], weight)
    length = tokens.shape[0]
    first_in = rms_kernel(tokens[...].astype(jnp.float32), gain[...])
    first_ref[...] = first_in
    rows = lax.broadcasted_iota(jnp.int32, (length, length), 0)
    cols = lax.broadcasted_iota(jnp.int32, (length, length), 1)
    allowed = (cols <= rows) | (cols < at[4])
    cosine_tab, sine_tab = cosine[...], sine[...]
    group_size = HQ // HK
    for group in range(HK):
        matrix = weight[group].reshape(first_in.shape[1], -1)
        qkv = dot(first_in, matrix)
        at_key = group_size * HD
        key = turned(qkv[:, at_key : at_key + HD], cosine_tab, sine_tab).astype(jnp.bfloat16)
        value = qkv[:, at_key + HD :].astype(jnp.bfloat16)
        key_ref[:, group * HD : (group + 1) * HD] = key
        value_ref[:, group * HD : (group + 1) * HD] = value
        for member in range(group_size):
            head = group * group_size + member
            here = slice(head * HD, (head + 1) * HD)
            query = turned(qkv[:, member * HD : (member + 1) * HD], cosine_tab, sine_tab)
            query = query.astype(jnp.bfloat16)
            query_ref[:, here] = query
            scores = dot(query, key, ((1,), (1,)))
            scores = jnp.where(allowed, scores * HD ** (-0.5), -1e30)
            weights = jnp.exp(scores - jnp.max(scores, axis=-1, keepdims=True))
            prob = weights * (1.0 / jnp.sum(weights, axis=-1, keepdims=True))
            prob = prob.astype(jnp.bfloat16)
            prob_ref[head] = prob
            out_ref[:, here] = dot(prob, value).astype(jnp.bfloat16)


def project_kernel(at, tokens, gain, attended, *refs):
    resid_ref, second_ref, weight = refs[8:]
    place_pieces(at, refs[:8], weight)
    heads = attended[...]
    halves = [dot(heads, weight[half].reshape(heads.shape[1], -1)) for half in range(2)]
    resid = tokens[...].astype(jnp.float32) + jnp.concatenate(halves, axis=1)
    resid_ref[...] = resid
    second_ref[...] = rms_kernel(resid, gain[...])


def one_hot(slots, capacity, dtype):
    shape = (capacity, slots.shape[1])
    return (slots == lax.broadcasted_iota(jnp.int32, shape, 0)).astype(jnp.float32).astype(dtype)


def spread(slots, pieces, capacity, rows, outs):
    rows = rows.astype(jnp.bfloat16)
    block = slots.shape[1]
    for n, piece in enumerate(pieces):
        for part in range(2):
            pick = one_hot(slots[2 * piece + part : 2 * piece + part + 1], capacity, jnp.bfloat16)
            at_row = (2 * n + part) * capacity
            tokens = dot(pick, rows[at_row : at_row + capacity], ((0,), (0,)))
            outs[n][part * block : (part + 1) * block] = tokens.astype(jnp.bfloat16)


def expert_kernel(capacity, pieces, at, slots, bias, router, gate_w, up_w, down_w, *refs):
    count = len(pieces)
    second, cot = refs[:count], refs[count : 2 * count]
    rows_in, rows_cot, gated_ref, gate_back, up_back, signal_ref, gates_ref = refs[
        2 * count : 2 * count + 7
    ]
    backs = refs[2 * count + 7 : -1]
    gate_rows = refs[-1]
    f32, bf16 = jnp.float32, jnp.bfloat16
    length = second[0].shape[0]
    half = length // 2
    for n, piece in enumerate(pieces):
        tokens = second[n][...]
        logits = dot(tokens, router[...]) + bias[piece * length : (piece + 1) * length]
        weights = jnp.exp(logits - jnp.max(logits, axis=-1, keepdims=True))
        gates = weights * (1.0 / jnp.sum(weights, axis=-1, keepdims=True))
        if n == 0:
            gates_ref[...] = gates
        lanes = lax.broadcasted_iota(jnp.int32, (capacity, gates.shape[1]), 1)
        for part in range(2):
            block = 2 * piece + part
            here = slice(part * half, (part + 1) * half)
            place = slice((2 * n + part) * capacity, (2 * n + part + 1) * capacity)
            pick = one_hot(slots[block : block + 1], capacity, f32)
            rows_in[place] = dot(pick.astype(bf16), tokens[here]).astype(bf16)
            rows_cot[place] = dot(pick.astype(bf16), cot[n][here]).astype(bf16)
            picked = dot(pick, gates[here], precision=lax.Precision.HIGHEST)
            picked = jnp.where(lanes == at[5], picked, 0.0)
            gate_rows[place] = jnp.sum(picked, axis=1, keepdims=True)
    gate = gate_rows[...]
    gate_pre = dot(rows_in[...], gate_w[...])
    up_pre = dot(rows_in[...], up_w[...])
    cot_hidden = dot(rows_cot[...], down_w[...], ((1,), (1,)))
    scale = math.sqrt(2.0 / math.pi)
    square = gate_pre * gate_pre
    bent = jnp.tanh(scale * gate_pre * (1.0 + 0.044715 * square))
    open_part = 0.5 * (1.0 + bent)
    active = gate_pre * open_part
    slope = open_part + 0.5 * gate_pre * (1.0 - bent * bent) * scale * (
        1.0 + 3 * 0.044715 * square
    )
    hidden = active * up_pre
    gated_ref[...] = (gate * hidden).astype(bf16)
    signal = jnp.sum(hidden * cot_hidden, axis=1, keepdims=True)
    back = gate * cot_hidden
    gate_back[...] = (back * up_pre * slope).astype(bf16)
    up_back[...] = (back * active).astype(bf16)
    for n in range(2 * count):
        block = 2 * pieces[n // 2] + n % 2
        pick = one_hot(slots[block : block + 1], capacity, f32)
        own = signal[n * capacity : (n + 1) * capacity]
        signal_ref[n : n + 1] = jnp.sum(pick * own, axis=0, keepdims=True)
    by_rows = ((1,), (1,))
    rows = dot(gate_back[...], gate_w[...], by_rows) + dot(up_back[...], up_w[...], by_rows)
    spread(slots, pieces, capacity, rows, backs)


def run_expert(pieces, at, slots, bias, router, weights, second, cot, capacity):
    count = len(pieces)
    rows, lanes = 2 * count * capacity, slots.shape[1]
    (length, width), hidden = second[0].shape, weights[0].shape[1]
    bf16, f32 = jnp.bfloat16, jnp.float32
    outs = [(rows, width)] * 2 + [(rows, hidden)] * 3
    outs = [(shape, bf16) for shape in outs] + [((8, lanes), f32), ((length, lanes), f32)]
    outs = outs + [((length, width), bf16)] * count
    return run_kernel(
        functools.partial(expert_kernel, capacity, pieces),
        6 * count,
        at,
        (slots, bias, router, *weights, *second, *cot),
        outs,
        56,
        [pltpu.VMEM((rows, 1), f32)],
    )


def mixture_kernel(capacity, groups, at, slots, down_w, *refs):
    outs = refs[len(groups) :]
    for pieces, gated in zip(groups, refs):
        rows = dot(gated[...], down_w[...])
        spread(slots, pieces, capacity, rows, [outs[piece] for piece in pieces])


def row_sum_kernel(at, *refs):
    half = len(refs) // 2
    total = sum(
        dot(left[...], right[...], ((0,), (0,))) for left, right in zip(refs[:half], refs[half:-1])
    )
    refs[-1][...] = total.astype(jnp.bfloat16)


def row_sum(at, lefts, rights):
    shape = (lefts[0].shape[1], rights[0].shape[1])
    return run_kernel(row_sum_kernel, 6, at, (*lefts, *rights), [(shape, jnp.bfloat16)], 48)[0]


def branch_back_kernel(
    at, near, far, first_x, first_y, last_y, last_x, resid, gain, second, gates, signal, router, cot, weight, *outs
):
    resid_grad_ref, branch_ref, attended_ref, router_ref, gain_ref = outs
    f32, bf16 = jnp.float32, jnp.bfloat16
    chosen = gates[...]
    logit_grad = chosen * (
        signal[...] - jnp.sum(chosen * signal[...], axis=-1, keepdims=True)
    )
    logit_grad = logit_grad.astype(bf16)
    halves = [first_x[...].astype(f32) + last_y[...], first_y[...].astype(f32) + last_x[...]]
    second_grad = near[...].astype(f32) + far[...] + jnp.concatenate(halves, axis=0)
    second_grad = second_grad + dot(logit_grad, router[...], ((1,), (1,)))
    norm_grad, gain_grad = rms_back(resid[...], gain[...], second_grad)
    gain_ref[...] = gain_grad
    resid_grad = cot[...].astype(f32) + norm_grad
    resid_grad_ref[...] = resid_grad
    branch = resid_grad.astype(bf16)
    branch_ref[...] = branch
    wide = weight.shape[2]
    attended_ref[...] = (
        dot(branch[:, :wide], weight[0], ((1,), (1,)))
        + dot(branch[:, wide:], weight[1], ((1,), (1,)))
    ).astype(bf16)
    router_ref[...] = dot(second[...], logit_grad, ((0,), (0,)))


def attend_back_kernel(at, attended, probs, queries, keys, values, cosine, sine, back_ref):
    f32, bf16 = jnp.float32, jnp.bfloat16
    cosine_tab, sine_tab = cosine[...], -sine[...]
    group_size = HQ // HK
    width = back_ref.shape[2]
    scale = HD ** (-0.5)

    def put(position, block):
        back_ref[position // width, :, position % width : position % width + HD] = block

    for group in range(HK):
        own = slice(group * HD, (group + 1) * HD)
        key, value = keys[:, own], values[:, own]
        key_grad = value_grad = 0.0
        start = group * (group_size + 2) * HD
        for member in range(group_size):
            head = group * group_size + member
            here = slice(head * HD, (head + 1) * HD)
            out_grad, query, prob = attended[:, here], queries[:, here], probs[head]
            prob_grad = dot(out_grad, value, ((1,), (1,)))
            prob_f = prob.astype(f32)
            inner = jnp.sum(prob_f * prob_grad, axis=-1, keepdims=True)
            score_grad = (prob_f * (prob_grad - inner)).astype(bf16)
            query_grad = turned(dot(score_grad, key) * scale, cosine_tab, sine_tab)
            put(start + member * HD, query_grad.astype(bf16))
            key_grad = key_grad + dot(score_grad, query, ((0,), (0,)))
            value_grad = value_grad + dot(prob, out_grad, ((0,), (0,)))
        key_grad = turned(key_grad * scale, cosine_tab, sine_tab)
        put(start + group_size * HD, key_grad.astype(bf16))
        put(start + (group_size + 1) * HD, value_grad.astype(bf16))


def first_back_kernel(at, back, weight, tokens, gain, resid_grad, tokens_ref, gain_ref):
    f32 = jnp.float32
    parts, _, cols = back.shape
    first_grad = 0.0
    for part in range(parts):
        group, place = divmod(part * cols, weight.shape[2])
        first_grad = first_grad + dot(
            back[part], weight[group, :, place : place + cols], ((1,), (1,))
        )
    norm_grad, gain_grad = rms_back(tokens[...].astype(f32), gain[...], first_grad)
    gain_ref[...] = gain_grad
    tokens_ref[...] = (resid_grad[...] + norm_grad).astype(jnp.bfloat16)


def dense_grad_kernel(at, narrow, branch_cols, qkv_cols, *refs):
    pieces, out_ref, held, sems = refs[:8], refs[8], refs[9], refs[10]
    copies = [
        pltpu.make_async_copy(piece, held.at[n], sems.at[n]) for n, piece in enumerate(pieces)
    ]
    for copy in copies:
        copy.start()
    length = branch_cols.shape[1]
    sums = [0.0, 0.0]
    for n, copy in enumerate(copies):
        copy.wait()
        dc, dy, dx = n // 4, n // 2 % 2, n % 2
        place = 4 * (at[0] ^ dy) + 2 * (at[1] ^ dc) + (at[2] ^ dx)
        sums[0] = sums[0] + dot(held[n, length:], qkv_cols[place], ((0,), (0,)))
        sums[1] = sums[1] + dot(held[n, :length], branch_cols[place], ((0,), (0,)))
    depth, rows, _ = out_ref.shape
    wide = rows - narrow.shape[1]
    for z in range(depth):
        here = slice(z * wide, (z + 1) * wide)
        both = jnp.concatenate([part[here] for part in sums], axis=1)
        out_ref[z, :wide] = both.astype(jnp.bfloat16)
        out_ref[z, wide:] = narrow[z]


def local_pairs(
    tokens,
    norm1_gain,
    w_query,
    w_key,
    w_value,
    w_out,
    norm2_gain,
    w_router,
    w_gate,
    w_up,
    w_down,
    expert_ids,
    prefix_len,
    out_grad,
):
    bf16, f32 = jnp.bfloat16, jnp.float32
    length, model_width = tokens.shape
    shard_rows = w_query.shape[0]
    local_count, _, hidden_width = w_gate.shape
    owners = lax.axis_size("x")
    depth = lax.axis_size("z")
    plane = lax.axis_size(PLANE)
    experts_all = w_router.shape[1]
    block_rows = length // MICRO
    capacity = 3 * block_rows * expert_ids.shape[1] // (2 * experts_all)
    plane_rows = plane * length
    blocks = plane_rows // block_rows
    q_cols, kv_cols = w_query.shape[1], w_key.shape[1]
    qkv_cols = q_cols + 2 * kv_cols
    q_group, out_half = q_cols // HK, model_width // 2
    y, c, x, z = (lax.axis_index(axis) for axis in ("y", "c", "x", "z"))
    own_local = 2 * y + c
    own_expert = x * local_count + own_local
    at = jnp.stack([y, c, x, z, prefix_len[0], own_expert, own_local])

    own_half = jnp.concatenate(
        [
            lax.dynamic_slice_in_dim(part, x * (part.shape[1] // 2), part.shape[1] // 2, 1)
            for part in (w_query, w_key, w_value, w_out)
        ],
        axis=1,
    )
    narrow = jnp.concatenate([w_router, norm1_gain[:, None], norm2_gain[:, None]], axis=1)
    narrow = small_group_gather(narrow)
    column = [own_half] + shifts(own_half)
    cot_sides = plane_sides(after(out_grad, narrow))
    qkv_half = qkv_cols // 2
    qkv_column = jnp.stack([part[:, :qkv_half] for part in column])
    out_column = jnp.stack([part[:, qkv_half:] for part in column])
    qkv_column = after(qkv_column, *cot_sides)
    qkv_sides = plane_sides(qkv_column)
    qkv_corner = plane_corner(qkv_sides)
    out_sides = plane_sides(after(out_column, qkv_corner))
    qkv_pieces = plane_pieces(qkv_column, qkv_sides, qkv_corner)
    router_w = jnp.pad(narrow[:, :experts_all], ((0, 0), (0, 128 - experts_all)))
    gains = narrow[:, experts_all : experts_all + 2].T.astype(f32)
    gain_one, gain_two = gains[:1], gains[1:]

    cosine_tab, sine_tab = angles(length, HD)
    cosine_all = jnp.concatenate([cosine_tab, cosine_tab], axis=2)[:, 0]
    sine_all = jnp.concatenate([-sine_tab, sine_tab], axis=2)[:, 0]
    weight_lead = (2, depth, 2, 2, shard_rows)
    first_in, queries, keys_rot, values_b, probs, attended, qkv_w = run_kernel(
        attend_kernel,
        11,
        at,
        (tokens, gain_one, cosine_all, sine_all, *qkv_pieces),
        [
            ((length, model_width), bf16),
            ((length, q_cols), bf16),
            ((length, kv_cols), bf16),
            ((length, kv_cols), bf16),
            ((HQ, length, length), bf16),
            ((length, q_cols), bf16),
            (weight_lead + (qkv_half,), bf16),
        ],
    )
    out_sides = lax.optimization_barrier((*out_sides, attended))[:2]
    out_corner = plane_corner(out_sides)
    out_pieces = plane_pieces(out_column, out_sides, out_corner)
    resid, second_in, output_w = run_kernel(
        project_kernel,
        4,
        at,
        (tokens, gain_two, attended, *out_pieces),
        [
            ((length, model_width), f32),
            ((length, model_width), bf16),
            (weight_lead + (out_half,), bf16),
        ],
    )
    qkv_w = qkv_w.reshape(HK, model_width, qkv_half)
    output_w = output_w.reshape(2, q_cols, out_half)

    ids_all = small_gather(after(expert_ids, out_corner))
    cot_corner = plane_corner(cot_sides, (out_corner,))
    cot_pieces = plane_pieces(out_grad, cot_sides, cot_corner)
    expert_range = jnp.arange(128, dtype=jnp.int32)
    chosen_mask = jnp.any(ids_all[:, :, None] == expert_range[None, None, :], axis=1)
    bias = jnp.where(chosen_mask, 0.0, -1e30).astype(f32)
    own_mask = jnp.any(ids_all == own_expert, axis=1).reshape(blocks, block_rows)
    place = jnp.cumsum(own_mask.astype(jnp.int32), axis=1) - 1
    slots = jnp.where(own_mask, place, -1)

    gate_w, up_w, down_w = (
        lax.dynamic_index_in_dim(weight, own_local, 0, keepdims=False)
        for weight in (w_gate, w_up, w_down)
    )

    expert = functools.partial(
        run_expert,
        at=at,
        slots=slots,
        bias=bias,
        router=router_w,
        weights=(gate_w, up_w, down_w),
        capacity=capacity,
    )
    second_sides = plane_sides(second_in)
    groups = ((0, 4), (1, 5, 2, 6), (3, 7))
    second_pieces = {0: second_in, 4: swap(second_in, "c")}

    def run_group(pieces):
        return expert(
            pieces,
            second=[second_pieces[piece] for piece in pieces],
            cot=[cot_pieces[piece] for piece in pieces],
        )

    stage_own = run_group(groups[0])
    second_sides = lax.optimization_barrier((*second_sides, stage_own[0]))[:2]
    second_corner = plane_corner(second_sides)
    for piece, block in zip((1, 2), second_sides):
        second_pieces[piece], second_pieces[piece + 4] = block, swap(block, "c")
    stage_sides = run_group(groups[1])
    second_corner = after(second_corner, stage_sides[0])
    second_pieces[3], second_pieces[7] = second_corner, swap(second_corner, "c")
    own_near, own_far = stage_own[7:]
    own_far = swap(own_far, "c")
    x_near, x_far, y_near, y_far = stage_sides[7:]
    back_x, back_y = over_core(x_near, x_far), over_core(y_near, y_far)
    first_x, first_y = early_sums(back_x, back_y)
    stage_corner = run_group(groups[2])
    corner = over_core(*stage_corner[7:])
    passed = corner_first(corner)
    stages = (stage_own, stage_sides, stage_corner)

    def expert_grad(left, right, *before):
        lefts = [stage[left] for stage in stages]
        rights = [stage[right] for stage in stages]
        lefts[0] = after(lefts[0], *before)
        return row_sum(at, lefts, rights)

    down_part = expert_grad(1, 2, corner)
    down_sum = scatter_sum(down_part, "z")
    gate_part = expert_grad(0, 3, down_part)
    gate_sum = scatter_sum(gate_part, "z")
    last_y, last_x = corner_last(back_x, back_y, passed)
    up_part = expert_grad(0, 4, gate_part)
    gates = stage_own[6]
    signal = [None] * 8
    for pieces, stage in zip(groups, stages):
        for n, piece in enumerate(pieces):
            signal[piece] = stage[5][2 * n : 2 * n + 2]
    signal = jnp.stack(signal).reshape(2, 2, 2, length)
    for dim, axis in enumerate(("c", "y", "x")):
        signal = jnp.where(lax.axis_index(axis) == 1, jnp.flip(signal, dim), signal)
    signal = exchange(jnp.swapaxes(signal, 0, 1).reshape(plane, length), PLANE)
    signal = jnp.transpose(signal.reshape(2, 2, owners, length), (3, 2, 0, 1))
    signal = signal.reshape(length, experts_all)
    signal = jnp.pad(signal, ((0, 0), (0, 128 - experts_all)))

    resid_grad, branch_grad, attended_grad, router_acc, gain_two_grad = run_kernel(
        branch_back_kernel,
        6,
        at,
        (
            own_near,
            own_far,
            first_x,
            first_y,
            last_y,
            last_x,
            resid,
            gain_two,
            second_in,
            gates,
            signal,
            router_w,
            out_grad,
            output_w,
        ),
        [
            ((length, model_width), f32),
            ((length, model_width), bf16),
            ((length, q_cols), bf16),
            ((model_width, 128), f32),
            ((1, model_width), f32),
        ],
    )
    (qkv_back,) = run_kernel(
        attend_back_kernel,
        12,
        at,
        (attended_grad, probs, queries, keys_rot, values_b, cosine_all, sine_all),
        [((plane, length, qkv_cols // plane), bf16)],
    )
    branch_back = jnp.moveaxis(branch_grad.reshape(length, plane, model_width // plane), 1, 0)
    branch_cols = exchange(branch_back, PLANE)
    qkv_cols_back = exchange(qkv_back, PLANE)
    tokens_grad, gain_one_grad = run_kernel(
        first_back_kernel,
        6,
        at,
        (qkv_back, qkv_w, tokens, gain_one, resid_grad),
        [((length, model_width), bf16), ((1, model_width), f32)],
    )

    both = jnp.concatenate(lax.optimization_barrier((attended, first_in, qkv_back))[:2], axis=0)
    both_pieces = plane_pieces(both)
    narrow_part = jnp.concatenate(
        [router_acc[:, :experts_all], gain_one_grad.T, gain_two_grad.T], axis=1
    )
    narrow_cols = -(-narrow_part.shape[1] // owners) * owners
    narrow_part = jnp.pad(narrow_part, ((0, 0), (0, narrow_cols - narrow_part.shape[1])))
    narrow_part = jnp.transpose(
        narrow_part.reshape(depth, 2, 2, shard_rows, owners, narrow_cols // owners),
        (1, 2, 4, 0, 3, 5),
    ).reshape(plane, depth, shard_rows * narrow_cols // owners)
    narrow_part = jnp.sum(exchange(narrow_part, PLANE), axis=0)
    qkv_width = qkv_cols // plane
    dense_cols = qkv_width + model_width // plane
    narrow_len = narrow_part.shape[1]
    narrow_rows = -(-narrow_len // dense_cols)
    kept_rows = -(-narrow_rows // 16) * 16
    narrow_part = jnp.pad(narrow_part, ((0, 0), (0, kept_rows * dense_cols - narrow_len)))
    wide_rows = local_count * shard_rows
    dense_shape = (depth, wide_rows + kept_rows, dense_cols)
    anywhere = pl.BlockSpec(memory_space=pl.ANY)
    dense_part = pl.pallas_call(
        dense_grad_kernel,
        out_shape=jax.ShapeDtypeStruct(dense_shape, bf16),
        in_specs=[SCALARS] + [WHOLE] * 3 + [anywhere] * 8,
        out_specs=WHOLE,
        scratch_shapes=[
            pltpu.VMEM((plane, 2 * length, model_width), bf16),
            pltpu.SemaphoreType.DMA((plane,)),
        ],
        cost_estimate=cost(7),
        compiler_params=pltpu.CompilerParams(vmem_limit_bytes=48 * 2**20),
    )(
        at,
        narrow_part.reshape(depth, kept_rows, dense_cols).astype(bf16),
        branch_cols,
        qkv_cols_back,
        *both_pieces,
    )
    dense_sum = scatter_sum(dense_part.reshape(-1, dense_cols), "z")
    wide_sum = dense_sum[: local_count * shard_rows].reshape(2, 2, 1, shard_rows, dense_cols)
    wide_sum = jnp.broadcast_to(wide_sum, (2, 2, owners, shard_rows, dense_cols)).reshape(
        plane, shard_rows, dense_cols
    )
    narrow_sum = dense_sum[local_count * shard_rows :][:narrow_rows]
    narrow_sum = jnp.broadcast_to(narrow_sum[None], (plane, narrow_rows, dense_cols))
    pad_rows = -(shard_rows + narrow_rows) % 16
    padding = jnp.zeros((plane, pad_rows, dense_cols), bf16)
    dense_sum = exchange(jnp.concatenate([wide_sum, narrow_sum, padding], axis=1), PLANE)
    wide_sum = jnp.moveaxis(dense_sum[:, :shard_rows].astype(f32), 0, 1)
    qkv_sum = wide_sum[:, :, :qkv_width].reshape(shard_rows, HK, qkv_half)
    output_sum = wide_sum[:, :, qkv_width:].reshape(shard_rows, model_width)
    narrow_sum = dense_sum[:, shard_rows : shard_rows + narrow_rows].reshape(
        2, 2, owners, narrow_rows * dense_cols
    )
    narrow_sum = narrow_sum[y, c, :, :narrow_len].reshape(owners, shard_rows, -1)
    narrow_sum = jnp.moveaxis(narrow_sum, 0, 1).reshape(shard_rows, narrow_cols).astype(f32)

    up_sum = scatter_sum(after(up_part, dense_sum), "z")

    shares = run_kernel(
        functools.partial(mixture_kernel, capacity, groups),
        10,
        at,
        (slots, down_w, after(stage_own[2], both_pieces[3]), stage_sides[2], stage_corner[2]),
        [((length, model_width), bf16)] * plane,
        48,
    )
    mixed = [over_core(near, far) for near, far in zip(shares[:4], shares[4:])]
    early = early_sums(mixed[1], mixed[2])
    last = corner_last(mixed[1], mixed[2], corner_first(mixed[3]))
    mixture = jnp.concatenate(
        [left.astype(f32) + right.astype(f32) for left, right in zip(early, last)], axis=0
    )
    block_out = (resid + (mixture + mixed[0].astype(f32))).astype(bf16)

    def placed(total):
        total = exchange(total, ("y", "c"))
        return total.reshape(local_count, shard_rows, hidden_width).astype(f32)

    return (
        block_out,
        tokens_grad,
        narrow_sum[:, experts_all],
        qkv_sum[:, :, :q_group].reshape(shard_rows, q_cols),
        qkv_sum[:, :, q_group : q_group + HD].reshape(shard_rows, kv_cols),
        qkv_sum[:, :, q_group + HD :].reshape(shard_rows, kv_cols),
        output_sum,
        narrow_sum[:, experts_all + 1],
        narrow_sum[:, :experts_all],
        placed(gate_sum),
        placed(up_sum),
        jnp.swapaxes(placed(down_sum), 1, 2),
    )


def solution(mesh):
    groups, owners = mesh.shape["dp"], mesh.shape["expert"]
    grid = jax.sharding.Mesh(
        mesh.devices.reshape(groups // 4, 2, 2, owners), ("z", "y", "c", "x")
    )
    rows = P(("z", "y", "c", "x"), None)
    shard, shard_rows = P(GROUP), P(GROUP, None)
    expert = P("x", None, None)
    return jax.shard_map(
        local_pairs if owners == 2 else local_wide,
        mesh=grid,
        in_specs=(
            rows,
            shard,
            shard_rows,
            shard_rows,
            shard_rows,
            shard_rows,
            shard,
            shard_rows,
            expert,
            expert,
            expert,
            rows,
            P(("z", "y", "c", "x")),
            rows,
        ),
        out_specs=(
            rows,
            rows,
            shard,
            shard_rows,
            shard_rows,
            shard_rows,
            shard_rows,
            shard,
            shard_rows,
            P("x", GROUP, None),
            P("x", GROUP, None),
            P("x", None, GROUP),
        ),
        check_vma=False,
    )
```

```python
import functools
import math

import jax
import jax.numpy as jnp
from jax import lax
from jax.experimental import pallas as pl
from jax.experimental.pallas import tpu as pltpu
from jax.sharding import PartitionSpec as P

HQ = 12
HK = 2
HD = 128
MICRO = 2
PLANE = ("y", "c", "x")
GROUP = ("z", "y", "c")


def rms_scale(values, gain_vec):
    inverse = lax.rsqrt(jnp.mean(values * values, axis=-1, keepdims=True) + 1e-06)
    return values * inverse * gain_vec


def angles(length, head_size):
    positions = jnp.arange(length).astype(jnp.float32)
    freq_rates = jnp.exp(
        -(2.0 * jnp.arange(head_size // 2).astype(jnp.float32) / head_size) * math.log(1000000.0)
    )
    angle_tab = positions[:, None] * freq_rates[None, :]
    return (jnp.cos(angle_tab)[:, None, :], jnp.sin(angle_tab)[:, None, :])


def rotary(values, cosine_tab, sine_tab):
    half_dim = values.shape[-1] // 2
    first_half = values[..., :half_dim]
    second_half = values[..., half_dim:]
    return jnp.concatenate(
        [
            first_half * cosine_tab - second_half * sine_tab,
            second_half * cosine_tab + first_half * sine_tab,
        ],
        axis=-1,
    )


def expert_act(gate_pre, up_pre):
    return jax.nn.gelu(gate_pre, approximate=True) * up_pre


def left_product(left_mat, right_mat):
    return lax.dot_general(
        left_mat, right_mat, (((0,), (0,)), ((), ())), preferred_element_type=jnp.float32
    )


def gather(block, axes):
    return lax.all_gather(block, axes, axis=0, tiled=True)


def exchange(block, axes):
    return lax.all_to_all(block, axes, split_axis=0, concat_axis=0, tiled=True)


def scatter_sum(block, axes):
    return lax.psum_scatter(block, axes, scatter_dimension=0, tiled=True)


def by_owner(cols, parts):
    rows, total = cols.shape
    return jnp.moveaxis(cols.reshape(rows, parts, total // parts), 1, 0).reshape(
        parts * rows, total // parts
    )


def local_wide(
    tokens,
    norm1_gain,
    w_query,
    w_key,
    w_value,
    w_out,
    norm2_gain,
    w_router,
    w_gate,
    w_up,
    w_down,
    expert_ids,
    prefix_len,
    out_grad,
):
    bf16, f32 = jnp.bfloat16, jnp.float32
    length, model_width = tokens.shape
    shard_rows = w_query.shape[0]
    local_count, _, hidden_width = w_gate.shape
    owners = lax.axis_size("x")
    depth = lax.axis_size("z")
    plane = lax.axis_size(PLANE)
    experts_all = w_router.shape[1]
    top_count = expert_ids.shape[1]
    block_rows = length // MICRO
    capacity = 3 * block_rows * top_count // (2 * experts_all)
    plane_rows = plane * length
    blocks = plane_rows // block_rows
    group_size = HQ // HK
    score_scale = HD ** (-0.5)
    q_cols, kv_cols = w_query.shape[1], w_key.shape[1]
    own_local = lax.axis_index(("y", "c"))
    own_expert = lax.axis_index("x") * local_count + own_local
    own_place = lax.axis_index(PLANE)

    narrow = jnp.concatenate([w_router, norm1_gain[:, None], norm2_gain[:, None]], axis=1)
    narrow = jnp.pad(narrow, ((0, 0), (0, -narrow.shape[1] % 128)))
    packed = gather(jnp.concatenate([w_query, w_key, w_value, narrow], axis=1), GROUP)
    qkv_cols = q_cols + 2 * kv_cols
    qkv_w = packed[:, :qkv_cols]
    router_w = packed[:, qkv_cols : qkv_cols + experts_all]
    gains = packed[:, qkv_cols + experts_all : qkv_cols + experts_all + 2].T.astype(f32)
    gain_one, gain_two = gains[0], gains[1]
    output_w = gather(w_out, GROUP)

    ids_all = gather(expert_ids, PLANE)
    cot_all = gather(out_grad, PLANE)
    chosen_mask = jnp.any(
        ids_all[:, :, None] == jnp.arange(experts_all, dtype=jnp.int32)[None, None, :], axis=1
    )
    own_mask = jnp.any(ids_all == own_expert, axis=1).reshape(blocks, block_rows)
    place = jnp.cumsum(own_mask.astype(jnp.int32), axis=1) - 1
    dispatch = (
        own_mask[:, None, :]
        & (place[:, None, :] == jnp.arange(capacity, dtype=jnp.int32)[None, :, None])
    ).astype(bf16)

    cosine_tab, sine_tab = angles(length, HD)
    inputs_f = tokens.astype(f32)
    first_in = rms_scale(inputs_f, gain_one).astype(bf16)
    qkv = jnp.dot(first_in, qkv_w, preferred_element_type=f32)
    queries = (
        rotary(qkv[:, :q_cols].reshape(length, HQ, HD), cosine_tab, sine_tab)
        .astype(bf16)
        .reshape(length, HK, group_size, HD)
    )
    keys_rot = rotary(
        qkv[:, q_cols : q_cols + kv_cols].reshape(length, HK, HD), cosine_tab, sine_tab
    ).astype(bf16)
    values_b = qkv[:, q_cols + kv_cols :].astype(bf16).reshape(length, HK, HD)
    positions = jnp.arange(length)
    allowed = (positions[None, :] <= positions[:, None]) | (positions[None, :] < prefix_len[0])

    def masked_scores():
        scores = jnp.einsum("ihrd,jhd->hrij", queries, keys_rot, preferred_element_type=f32)
        return jnp.where(allowed, scores * score_scale, -1e30)

    masked = masked_scores()
    row_peak = jnp.max(masked, axis=-1, keepdims=True)
    log_total = row_peak + jnp.log(jnp.sum(jnp.exp(masked - row_peak), axis=-1, keepdims=True))
    prob_bf = jnp.exp(masked - log_total).astype(bf16)
    attended = jnp.einsum("hrij,jhd->ihrd", prob_bf, values_b, preferred_element_type=f32)
    attended = attended.reshape(length, HQ * HD).astype(bf16)
    resid = inputs_f + jnp.dot(attended, output_w, preferred_element_type=f32)
    second_in = rms_scale(resid, gain_two).astype(bf16)

    second_all = gather(second_in, PLANE)
    logits = jnp.dot(second_all, router_w, preferred_element_type=f32)
    gates_all = jax.nn.softmax(jnp.where(chosen_mask, logits, -jnp.inf), axis=-1)
    own_gates = lax.dynamic_index_in_dim(gates_all, own_expert, 1, keepdims=False)
    own_gates = own_gates.reshape(blocks, block_rows)
    gate_rows = jnp.einsum(
        "bct,bt->bc", dispatch.astype(f32), own_gates, precision=lax.Precision.HIGHEST
    )[:, :, None]
    gate_w = lax.dynamic_index_in_dim(w_gate, own_local, 0, keepdims=False)
    up_w = lax.dynamic_index_in_dim(w_up, own_local, 0, keepdims=False)
    down_w = lax.dynamic_index_in_dim(w_down, own_local, 0, keepdims=False)

    def to_rows(array):
        return jnp.einsum(
            "bct,btd->bcd",
            dispatch,
            array.reshape(blocks, block_rows, model_width),
            preferred_element_type=f32,
        ).astype(bf16)

    def to_tokens(rows):
        return (
            jnp.einsum("bct,bcd->btd", dispatch, rows.astype(bf16), preferred_element_type=f32)
            .astype(bf16)
            .reshape(plane_rows, model_width)
        )

    rows_in = to_rows(second_all)
    rows_cot = to_rows(cot_all)
    gate_pre = jnp.einsum("bcd,df->bcf", rows_in, gate_w, preferred_element_type=f32)
    up_pre = jnp.einsum("bcd,df->bcf", rows_in, up_w, preferred_element_type=f32)
    hidden, act_pull = jax.vjp(expert_act, gate_pre, up_pre)
    gated = (gate_rows * hidden).astype(bf16)
    down_part = jnp.einsum("bcd,bcf->df", rows_cot, gated, preferred_element_type=f32)
    down_sum = scatter_sum(down_part.astype(bf16), "z")
    cot_hidden = jnp.einsum("bcd,fd->bcf", rows_cot, down_w, preferred_element_type=f32)
    gate_signal_rows = jnp.sum(hidden * cot_hidden, axis=-1)
    gate_pgrad, up_pgrad = act_pull(gate_rows * cot_hidden)
    gate_pgrad = gate_pgrad.astype(bf16)
    up_pgrad = up_pgrad.astype(bf16)
    gate_part = jnp.einsum("bcd,bcf->df", rows_in, gate_pgrad, preferred_element_type=f32)
    gate_sum = scatter_sum(gate_part.astype(bf16), "z")
    up_part = jnp.einsum("bcd,bcf->df", rows_in, up_pgrad, preferred_element_type=f32)
    up_sum = scatter_sum(up_part.astype(bf16), "z")
    rows_grad = jnp.einsum("bcf,df->bcd", gate_pgrad, gate_w, preferred_element_type=f32)
    rows_grad = rows_grad + jnp.einsum("bcf,df->bcd", up_pgrad, up_w, preferred_element_type=f32)
    second_back = scatter_sum(to_tokens(rows_grad), PLANE).astype(f32)
    gate_signal = jnp.einsum(
        "bct,bc->bt", dispatch.astype(f32), gate_signal_rows, precision=lax.Precision.HIGHEST
    )
    gate_signal = exchange(gate_signal.reshape(plane, length), PLANE)
    gate_signal = jnp.transpose(
        gate_signal.reshape(local_count, owners, length), (2, 1, 0)
    ).reshape(length, experts_all)
    expert_rows = jnp.einsum("bcf,fd->bcd", gated, down_w, preferred_element_type=f32)
    mixture = scatter_sum(to_tokens(expert_rows), PLANE).astype(f32)
    block_out = (resid + mixture).astype(bf16)

    cotangent = out_grad.astype(f32)
    gate_probs = lax.dynamic_slice_in_dim(gates_all, own_place * length, length, 0)
    logit_grad = (
        gate_probs
        * (gate_signal - jnp.sum(gate_probs * gate_signal, axis=-1, keepdims=True))
    ).astype(bf16)
    router_acc = left_product(second_in, logit_grad)
    second_grad = second_back + jnp.dot(logit_grad, router_w.T, preferred_element_type=f32)
    _, norm_two_pull = jax.vjp(rms_scale, resid, gain_two)
    resid_norm_grad, gain_two_grad = norm_two_pull(second_grad)
    resid_grad = cotangent + resid_norm_grad
    branch_grad = resid_grad.astype(bf16)

    attended_all = gather(attended, PLANE)
    branch_cols = exchange(by_owner(branch_grad, plane), PLANE)
    output_part = left_product(attended_all, branch_cols)
    attended_grad = jnp.dot(branch_grad, output_w.T, preferred_element_type=f32).astype(bf16)
    attended_grad = attended_grad.reshape(length, HK, group_size, HD)
    masked = masked_scores()
    prob_full = jnp.exp(masked - log_total)
    prob_bf = prob_full.astype(bf16)
    prob_grad = jnp.einsum("ihrd,jhd->hrij", attended_grad, values_b, preferred_element_type=f32)
    row_inner = jnp.sum(prob_full * prob_grad, axis=-1, keepdims=True)
    score_grad = (prob_full * (prob_grad - row_inner)).astype(bf16)
    query_rot_grad = (
        jnp.einsum("hrij,jhd->ihrd", score_grad, keys_rot, preferred_element_type=f32)
        * score_scale
    )
    query_back = rotary(query_rot_grad.reshape(length, HQ, HD), cosine_tab, -sine_tab)
    query_back = query_back.astype(bf16).reshape(length, HQ * HD)
    key_rot_grad = (
        jnp.einsum("hrij,ihrd->jhd", score_grad, queries, preferred_element_type=f32)
        * score_scale
    )
    key_back = rotary(key_rot_grad, cosine_tab, -sine_tab).astype(bf16).reshape(length, HK * HD)
    value_back = jnp.einsum("hrij,ihrd->jhd", prob_bf, attended_grad, preferred_element_type=f32)
    value_back = value_back.astype(bf16).reshape(length, HK * HD)
    qkv_back = jnp.concatenate([query_back, key_back, value_back], axis=1)
    first_all = gather(first_in, PLANE)
    qkv_part = left_product(first_all, exchange(by_owner(qkv_back, plane), PLANE))
    first_grad = lax.dot_general(
        qkv_back, qkv_w, (((1,), (1,)), ((), ())), preferred_element_type=f32
    )
    _, norm_one_pull = jax.vjp(rms_scale, inputs_f, gain_one)
    input_norm_grad, gain_one_grad = norm_one_pull(first_grad)
    tokens_grad = (resid_grad + input_norm_grad).astype(bf16)

    narrow_part = jnp.concatenate(
        [router_acc, gain_one_grad[:, None], gain_two_grad[:, None]], axis=1
    ).astype(bf16)
    narrow_cols = narrow_part.shape[1]
    narrow_sum = lax.psum(scatter_sum(narrow_part, GROUP), "x").astype(f32)
    dense_part = jnp.concatenate([qkv_part, output_part], axis=1).astype(bf16)
    dense_sum = scatter_sum(dense_part, "z")
    dense_cols = dense_sum.shape[1]
    dense_sum = gather(dense_sum, PLANE).reshape(plane, local_count, shard_rows, dense_cols)
    dense_sum = lax.dynamic_index_in_dim(dense_sum, own_local, 1, keepdims=False).astype(f32)
    dense_sum = jnp.moveaxis(dense_sum, 0, 1)
    qkv_width = qkv_cols // plane
    qkv_sum = dense_sum[:, :, :qkv_width].reshape(shard_rows, qkv_cols)
    output_sum = dense_sum[:, :, qkv_width:].reshape(shard_rows, model_width)

    def placed(total):
        total = exchange(total, ("y", "c"))
        return total.reshape(local_count, shard_rows, hidden_width).astype(f32)

    return (
        block_out,
        tokens_grad,
        narrow_sum[:, experts_all],
        qkv_sum[:, :q_cols],
        qkv_sum[:, q_cols : q_cols + kv_cols],
        qkv_sum[:, q_cols + kv_cols :],
        output_sum,
        narrow_sum[:, experts_all + 1],
        narrow_sum[:, :experts_all],
        placed(gate_sum),
        placed(up_sum),
        jnp.swapaxes(placed(down_sum), 1, 2),
    )


def rounded(values):
    return lax.reduce_precision(values, 8, 7).astype(jnp.bfloat16)


def after(block, *others):
    return lax.optimization_barrier((block,) + others)[0]


def swap(block, axis):
    return lax.ppermute(block, axis, [(0, 1), (1, 0)])


def shifts(block):
    depth = lax.axis_size("z")
    return [
        lax.ppermute(block, "z", [(i, (i + k) % depth) for i in range(depth)])
        for k in range(1, depth)
    ]


def plane_sides(block):
    return swap(block, "x"), swap(block, "y")


def plane_corner(sides, before=()):
    over_x, over_y = sides
    half = over_x.shape[0] // 2
    over_y, over_x = lax.optimization_barrier((over_y[:half], over_x[half:]) + before)[:2]
    return jnp.concatenate([swap(over_y, "x"), swap(over_x, "y")], axis=0)


def plane_pieces(block, sides=None, corner=None):
    sides = plane_sides(block) if sides is None else sides
    corner = plane_corner(sides) if corner is None else corner
    pieces = [block, *sides, corner]
    return pieces + [swap(piece, "c") for piece in pieces]


def small_gather(block):
    for axis in ("x", "y", "c"):
        block = jnp.concatenate([block, swap(block, axis)], axis=0)
    return block


def small_group_gather(block):
    depth = lax.axis_size("z")
    order = jnp.stack(([block] + shifts(block))[::-1] * 2)
    start = (depth - 1 - lax.axis_index("z")) % depth
    total = lax.dynamic_slice_in_dim(order, start, depth, 0)[:, None, None]
    for dim, axis in ((1, "y"), (2, "c")):
        other = swap(total, axis)
        last = lax.axis_index(axis) == 1
        pair = [jnp.where(last, other, total), jnp.where(last, total, other)]
        total = jnp.concatenate(pair, axis=dim)
    return total.reshape(-1, block.shape[1])


def add(left, right):
    return rounded(left.astype(jnp.float32) + right.astype(jnp.float32))


def over_core(near, far):
    return add(near, swap(far, "c"))


def early_sums(over_x, over_y):
    half = over_x.shape[0] // 2
    return swap(over_x[:half], "x"), swap(over_y[half:], "y")


def corner_first(corner):
    half = corner.shape[0] // 2
    return swap(corner[:half], "x"), swap(corner[half:], "y")


def corner_last(over_x, over_y, first):
    half = over_x.shape[0] // 2
    over_y, over_x = add(over_y[:half], first[0]), add(over_x[half:], first[1])
    return swap(over_y, "y"), swap(over_x, "x"), over_x


def cost(micros):
    return pl.CostEstimate(flops=micros * 10**9, bytes_accessed=micros * 10**6, transcendentals=0)


def dot(left, right, dims=((1,), (0,)), precision=None):
    return lax.dot_general(
        left, right, (dims, ((), ())), precision=precision, preferred_element_type=jnp.float32
    )


WHOLE = pl.BlockSpec(memory_space=pltpu.VMEM)
SCALARS = pl.BlockSpec(memory_space=pltpu.SMEM)


def run_kernel(kernel, micros, at, operands, outs, megabytes=40, scratch=()):
    return pl.pallas_call(
        kernel,
        out_shape=[jax.ShapeDtypeStruct(shape, dtype) for shape, dtype in outs],
        in_specs=[SCALARS] + [WHOLE] * len(operands),
        out_specs=[WHOLE] * len(outs),
        scratch_shapes=scratch,
        cost_estimate=cost(micros),
        compiler_params=pltpu.CompilerParams(vmem_limit_bytes=megabytes * 2**20),
    )(at, *operands)


def place_pieces(at, refs, weight):
    depth = weight.shape[1]
    for n, ref in enumerate(refs):
        dc, dy, dx = n // 4, n // 2 % 2, n % 2
        for k in range(depth):
            z = lax.rem(at[3] + depth - k, depth)
            weight[at[2] ^ dx, z, at[0] ^ dy, at[1] ^ dc] = ref[k]


def rms_kernel(values, gain):
    inverse = lax.rsqrt(jnp.mean(values * values, axis=-1, keepdims=True) + 1e-06)
    return (values * inverse * gain).astype(jnp.bfloat16)


def rms_back(values, gain, grad):
    inverse = lax.rsqrt(jnp.mean(values * values, axis=-1, keepdims=True) + 1e-06)
    normed = values * inverse
    gain_grad = jnp.sum(grad * normed, axis=0, keepdims=True)
    grad = grad * gain
    along = jnp.mean(grad * normed, axis=-1, keepdims=True)
    return inverse * (grad - normed * along), gain_grad


def turned(values, cosine_tab, sine_tab):
    return values * cosine_tab + pltpu.roll(values, HD // 2, 1) * sine_tab


def attend_kernel(at, tokens, gain, cosine, sine, *refs):
    first_ref, query_ref, key_ref, value_ref, prob_ref, out_ref, weight = refs[8:]
    place_pieces(at, refs[:8], weight)
    length = tokens.shape[0]
    first_in = rms_kernel(tokens[...].astype(jnp.float32), gain[...])
    first_ref[...] = first_in
    rows = lax.broadcasted_iota(jnp.int32, (length, length), 0)
    cols = lax.broadcasted_iota(jnp.int32, (length, length), 1)
    allowed = (cols <= rows) | (cols < at[4])
    cosine_tab, sine_tab = cosine[...], sine[...]
    group_size = HQ // HK
    for group in range(HK):
        matrix = weight[group].reshape(first_in.shape[1], -1)
        qkv = dot(first_in, matrix)
        at_key = group_size * HD
        key = turned(qkv[:, at_key : at_key + HD], cosine_tab, sine_tab).astype(jnp.bfloat16)
        value = qkv[:, at_key + HD :].astype(jnp.bfloat16)
        key_ref[:, group * HD : (group + 1) * HD] = key
        value_ref[:, group * HD : (group + 1) * HD] = value
        for member in range(group_size):
            head = group * group_size + member
            here = slice(head * HD, (head + 1) * HD)
            query = turned(qkv[:, member * HD : (member + 1) * HD], cosine_tab, sine_tab)
            query = query.astype(jnp.bfloat16)
            query_ref[:, here] = query
            scores = dot(query, key, ((1,), (1,)))
            scores = jnp.where(allowed, scores * HD ** (-0.5), -1e30)
            weights = jnp.exp(scores - jnp.max(scores, axis=-1, keepdims=True))
            prob = weights * (1.0 / jnp.sum(weights, axis=-1, keepdims=True))
            prob = prob.astype(jnp.bfloat16)
            prob_ref[head] = prob
            out_ref[:, here] = dot(prob, value).astype(jnp.bfloat16)


def project_kernel(at, tokens, gain, attended, *refs):
    resid_ref, second_ref, weight = refs[8:]
    place_pieces(at, refs[:8], weight)
    heads = attended[...]
    halves = [dot(heads, weight[half].reshape(heads.shape[1], -1)) for half in range(2)]
    resid = tokens[...].astype(jnp.float32) + jnp.concatenate(halves, axis=1)
    resid_ref[...] = resid
    second_ref[...] = rms_kernel(resid, gain[...])


def one_hot(slots, capacity, dtype):
    shape = (capacity, slots.shape[1])
    return (slots == lax.broadcasted_iota(jnp.int32, shape, 0)).astype(jnp.float32).astype(dtype)


def spread(slots, pieces, capacity, rows, outs):
    rows = rows.astype(jnp.bfloat16)
    block = slots.shape[1]
    for n, piece in enumerate(pieces):
        for part in range(2):
            pick = one_hot(slots[2 * piece + part : 2 * piece + part + 1], capacity, jnp.bfloat16)
            at_row = (2 * n + part) * capacity
            tokens = dot(pick, rows[at_row : at_row + capacity], ((0,), (0,)))
            outs[n][part * block : (part + 1) * block] = tokens.astype(jnp.bfloat16)


def expert_kernel(capacity, pieces, at, slots, bias, router, gate_w, up_w, down_w, *refs):
    count = len(pieces)
    second, cot = refs[:count], refs[count : 2 * count]
    rows_in, rows_cot, gated_ref, gate_back, up_back, gates_ref = refs[2 * count : 2 * count + 6]
    backs = refs[2 * count + 6 : -1]
    gate_rows = refs[-1]
    f32, bf16 = jnp.float32, jnp.bfloat16
    length = second[0].shape[0]
    half = length // 2
    for n, piece in enumerate(pieces):
        tokens = second[n][...]
        logits = dot(tokens, router[...]) + bias[piece * length : (piece + 1) * length]
        weights = jnp.exp(logits - jnp.max(logits, axis=-1, keepdims=True))
        gates = weights * (1.0 / jnp.sum(weights, axis=-1, keepdims=True))
        if n == 0:
            gates_ref[...] = gates
        lanes = lax.broadcasted_iota(jnp.int32, (capacity, gates.shape[1]), 1)
        for part in range(2):
            block = 2 * piece + part
            here = slice(part * half, (part + 1) * half)
            place = slice((2 * n + part) * capacity, (2 * n + part + 1) * capacity)
            pick = one_hot(slots[block : block + 1], capacity, f32)
            rows_in[place] = dot(pick.astype(bf16), tokens[here]).astype(bf16)
            rows_cot[place] = dot(pick.astype(bf16), cot[n][here]).astype(bf16)
            picked = dot(pick, gates[here], precision=lax.Precision.HIGHEST)
            picked = jnp.where(lanes == at[5], picked, 0.0)
            gate_rows[place] = jnp.sum(picked, axis=1, keepdims=True)
    gate = gate_rows[...]
    gate_pre = dot(rows_in[...], gate_w[...])
    up_pre = dot(rows_in[...], up_w[...])
    cot_hidden = dot(rows_cot[...], down_w[...], ((1,), (1,)))
    scale = math.sqrt(2.0 / math.pi)
    square = gate_pre * gate_pre
    bent = jnp.tanh(scale * gate_pre * (1.0 + 0.044715 * square))
    open_part = 0.5 * (1.0 + bent)
    active = gate_pre * open_part
    slope = open_part + 0.5 * gate_pre * (1.0 - bent * bent) * scale * (
        1.0 + 3 * 0.044715 * square
    )
    hidden = active * up_pre
    gated_ref[...] = (gate * hidden).astype(bf16)
    signal = jnp.sum(hidden * cot_hidden, axis=1, keepdims=True)
    back = gate * cot_hidden
    gate_back[...] = (back * up_pre * slope).astype(bf16)
    up_back[...] = (back * active).astype(bf16)
    high = signal.astype(bf16)
    low = (signal - high.astype(f32)).astype(bf16)
    lanes = lax.broadcasted_iota(jnp.int32, (signal.shape[0], bias.shape[1]), 1)
    signal = jnp.where(lanes == at[5], high.astype(f32), 0.0)
    signal = jnp.where(lanes == at[5] + bias.shape[1] // 2, low.astype(f32), signal)
    by_rows = ((1,), (1,))
    rows = dot(gate_back[...], gate_w[...], by_rows) + dot(up_back[...], up_w[...], by_rows)
    spread(slots, pieces, capacity, jnp.concatenate([rows, signal], axis=1), backs)


def run_expert(pieces, at, slots, bias, router, weights, second, cot, capacity):
    count = len(pieces)
    rows = 2 * count * capacity
    (length, width), hidden = second[0].shape, weights[0].shape[1]
    bf16, f32 = jnp.bfloat16, jnp.float32
    outs = [(rows, width)] * 2 + [(rows, hidden)] * 3
    outs = [(shape, bf16) for shape in outs] + [((length, bias.shape[1]), f32)]
    outs = outs + [((length, width + bias.shape[1]), bf16)] * count
    return run_kernel(
        functools.partial(expert_kernel, capacity, pieces),
        6 * count,
        at,
        (slots, bias, router, *weights, *second, *cot),
        outs,
        56,
        [pltpu.VMEM((rows, 1), f32)],
    )


def mixture_kernel(capacity, groups, at, slots, down_w, *refs):
    outs = refs[len(groups) :]
    for pieces, gated in zip(groups, refs):
        rows = dot(gated[...], down_w[...])
        spread(slots, pieces, capacity, rows, [outs[piece] for piece in pieces])


def row_sum_kernel(counts, at, *refs):
    parts = len(counts)
    rights = len(refs) // (parts + 2) - 1
    sources, outs = refs[: parts * (rights + 1)], refs[parts * (rights + 1) : -rights - 2]
    held, sems = refs[-rights - 2 : -1], refs[-1]
    copies = []
    for n, source in enumerate(sources):
        array, part = divmod(n, parts)
        target = held[array].at[pl.ds(sum(counts[:part]), counts[part])]
        copies.append(pltpu.make_async_copy(source, target, sems.at[n]))
        copies[-1].start()
    for copy in copies:
        copy.wait()
    for out, right in zip(outs, held[1:]):
        out[...] = dot(held[0][...], right[...], ((0,), (0,))).astype(jnp.bfloat16)


def row_sums(at, left, *rights):
    counts = [part.shape[0] for part in left]
    widths = [parts[0].shape[1] for parts in (left, *rights)]
    sources = [part for parts in (left, *rights) for part in parts]
    anywhere = pl.BlockSpec(memory_space=pl.ANY)
    return pl.pallas_call(
        functools.partial(row_sum_kernel, counts),
        out_shape=[jax.ShapeDtypeStruct((widths[0], width), jnp.bfloat16) for width in widths[1:]],
        in_specs=[SCALARS] + [anywhere] * len(sources),
        out_specs=[WHOLE] * len(rights),
        scratch_shapes=[pltpu.VMEM((sum(counts), width), jnp.bfloat16) for width in widths]
        + [pltpu.SemaphoreType.DMA((len(sources),))],
        cost_estimate=cost(6 * len(rights)),
        compiler_params=pltpu.CompilerParams(vmem_limit_bytes=40 * 2**20),
    )(at, *sources)


def branch_back_kernel(
    at, near, far, first_x, first_y, last_y, last_x, resid, gain, second, gates, router, cot, weight, *outs
):
    resid_grad_ref, branch_ref, attended_ref, router_ref, gain_ref = outs
    f32, bf16 = jnp.float32, jnp.bfloat16
    halves = [first_x[...].astype(f32) + last_y[...], first_y[...].astype(f32) + last_x[...]]
    total = near[...].astype(f32) + far[...] + jnp.concatenate(halves, axis=0)
    width = resid.shape[1]
    signal = total[:, width:]
    signal = signal + pltpu.roll(signal, signal.shape[1] // 2, 1)
    chosen = gates[...]
    logit_grad = chosen * (signal - jnp.sum(chosen * signal, axis=-1, keepdims=True))
    logit_grad = logit_grad.astype(bf16)
    second_grad = total[:, :width] + dot(logit_grad, router[...], ((1,), (1,)))
    norm_grad, gain_grad = rms_back(resid[...], gain[...], second_grad)
    gain_ref[...] = gain_grad
    resid_grad = cot[...].astype(f32) + norm_grad
    resid_grad_ref[...] = resid_grad
    branch = resid_grad.astype(bf16)
    branch_ref[...] = branch
    wide = weight.shape[2]
    attended_ref[...] = (
        dot(branch[:, :wide], weight[0], ((1,), (1,)))
        + dot(branch[:, wide:], weight[1], ((1,), (1,)))
    ).astype(bf16)
    router_ref[...] = dot(second[...], logit_grad, ((0,), (0,)))


def attend_back_kernel(at, attended, probs, queries, keys, values, cosine, sine, back_ref):
    f32, bf16 = jnp.float32, jnp.bfloat16
    cosine_tab, sine_tab = cosine[...], -sine[...]
    group_size = HQ // HK
    width = back_ref.shape[2]
    scale = HD ** (-0.5)

    def put(position, block):
        back_ref[position // width, :, position % width : position % width + HD] = block

    for group in range(HK):
        own = slice(group * HD, (group + 1) * HD)
        key, value = keys[:, own], values[:, own]
        key_grad = value_grad = 0.0
        start = group * (group_size + 2) * HD
        for member in range(group_size):
            head = group * group_size + member
            here = slice(head * HD, (head + 1) * HD)
            out_grad, query, prob = attended[:, here], queries[:, here], probs[head]
            prob_grad = dot(out_grad, value, ((1,), (1,)))
            prob_f = prob.astype(f32)
            inner = jnp.sum(prob_f * prob_grad, axis=-1, keepdims=True)
            score_grad = (prob_f * (prob_grad - inner)).astype(bf16)
            query_grad = turned(dot(score_grad, key) * scale, cosine_tab, sine_tab)
            put(start + member * HD, query_grad.astype(bf16))
            key_grad = key_grad + dot(score_grad, query, ((0,), (0,)))
            value_grad = value_grad + dot(prob, out_grad, ((0,), (0,)))
        key_grad = turned(key_grad * scale, cosine_tab, sine_tab)
        put(start + group_size * HD, key_grad.astype(bf16))
        put(start + (group_size + 1) * HD, value_grad.astype(bf16))


def first_back_kernel(at, back, weight, tokens, gain, resid_grad, tokens_ref, gain_ref):
    f32 = jnp.float32
    parts, _, cols = back.shape
    first_grad = 0.0
    for part in range(parts):
        group, place = divmod(part * cols, weight.shape[2])
        first_grad = first_grad + dot(
            back[part], weight[group, :, place : place + cols], ((1,), (1,))
        )
    norm_grad, gain_grad = rms_back(tokens[...].astype(f32), gain[...], first_grad)
    gain_ref[...] = gain_grad
    tokens_ref[...] = (resid_grad[...] + norm_grad).astype(jnp.bfloat16)


def dense_grad_kernel(at, narrow, branch_cols, qkv_cols, *refs):
    pieces, out_ref, held, sems = refs[:8], refs[8], refs[9], refs[10]
    copies = [
        pltpu.make_async_copy(piece, held.at[n], sems.at[n]) for n, piece in enumerate(pieces)
    ]
    for copy in copies:
        copy.start()
    length = branch_cols.shape[1]
    sums = [0.0, 0.0]
    for n, copy in enumerate(copies):
        copy.wait()
        dc, dy, dx = n // 4, n // 2 % 2, n % 2
        place = 4 * (at[0] ^ dy) + 2 * (at[1] ^ dc) + (at[2] ^ dx)
        sums[0] = sums[0] + dot(held[n, length:], qkv_cols[place], ((0,), (0,)))
        sums[1] = sums[1] + dot(held[n, :length], branch_cols[place], ((0,), (0,)))
    depth, rows, _ = out_ref.shape
    wide = rows - narrow.shape[1]
    for z in range(depth):
        here = slice(z * wide, (z + 1) * wide)
        both = jnp.concatenate([part[here] for part in sums], axis=1)
        out_ref[z, :wide] = both.astype(jnp.bfloat16)
        out_ref[z, wide:] = narrow[z]


def local_pairs(
    tokens,
    norm1_gain,
    w_query,
    w_key,
    w_value,
    w_out,
    norm2_gain,
    w_router,
    w_gate,
    w_up,
    w_down,
    expert_ids,
    prefix_len,
    out_grad,
):
    bf16, f32 = jnp.bfloat16, jnp.float32
    length, model_width = tokens.shape
    shard_rows = w_query.shape[0]
    local_count, _, hidden_width = w_gate.shape
    owners = lax.axis_size("x")
    depth = lax.axis_size("z")
    plane = lax.axis_size(PLANE)
    experts_all = w_router.shape[1]
    block_rows = length // MICRO
    capacity = 3 * block_rows * expert_ids.shape[1] // (2 * experts_all)
    plane_rows = plane * length
    blocks = plane_rows // block_rows
    q_cols, kv_cols = w_query.shape[1], w_key.shape[1]
    qkv_cols = q_cols + 2 * kv_cols
    q_group, out_half = q_cols // HK, model_width // 2
    y, c, x, z = (lax.axis_index(axis) for axis in ("y", "c", "x", "z"))
    own_local = 2 * y + c
    own_expert = x * local_count + own_local
    at = jnp.stack([y, c, x, z, prefix_len[0], own_expert, own_local])

    own_half = jnp.concatenate(
        [
            lax.dynamic_slice_in_dim(part, x * (part.shape[1] // 2), part.shape[1] // 2, 1)
            for part in (w_query, w_key, w_value, w_out)
        ],
        axis=1,
    )
    narrow = jnp.concatenate([w_router, norm1_gain[:, None], norm2_gain[:, None]], axis=1)
    narrow = small_group_gather(narrow)
    ids_all = small_gather(expert_ids)
    column = [own_half] + shifts(own_half)
    cot_sides = plane_sides(after(out_grad, narrow, ids_all))
    qkv_half = qkv_cols // 2
    qkv_column = jnp.stack([part[:, :qkv_half] for part in column])
    out_column = jnp.stack([part[:, qkv_half:] for part in column])
    qkv_column = after(qkv_column, *cot_sides)
    qkv_sides = plane_sides(qkv_column)
    qkv_corner = plane_corner(qkv_sides)
    out_sides = plane_sides(after(out_column, qkv_corner))
    qkv_pieces = plane_pieces(qkv_column, qkv_sides, qkv_corner)
    router_w = jnp.pad(narrow[:, :experts_all], ((0, 0), (0, 128 - experts_all)))
    gains = narrow[:, experts_all : experts_all + 2].T.astype(f32)
    gain_one, gain_two = gains[:1], gains[1:]

    cosine_tab, sine_tab = angles(length, HD)
    cosine_all = jnp.concatenate([cosine_tab, cosine_tab], axis=2)[:, 0]
    sine_all = jnp.concatenate([-sine_tab, sine_tab], axis=2)[:, 0]
    weight_lead = (2, depth, 2, 2, shard_rows)
    first_in, queries, keys_rot, values_b, probs, attended, qkv_w = run_kernel(
        attend_kernel,
        11,
        at,
        (tokens, gain_one, cosine_all, sine_all, *qkv_pieces),
        [
            ((length, model_width), bf16),
            ((length, q_cols), bf16),
            ((length, kv_cols), bf16),
            ((length, kv_cols), bf16),
            ((HQ, length, length), bf16),
            ((length, q_cols), bf16),
            (weight_lead + (qkv_half,), bf16),
        ],
    )
    out_sides = lax.optimization_barrier((*out_sides, attended))[:2]
    out_corner = plane_corner(out_sides)
    out_pieces = plane_pieces(out_column, out_sides, out_corner)
    resid, second_in, output_w = run_kernel(
        project_kernel,
        4,
        at,
        (tokens, gain_two, attended, *out_pieces),
        [
            ((length, model_width), f32),
            ((length, model_width), bf16),
            (weight_lead + (out_half,), bf16),
        ],
    )
    qkv_w = qkv_w.reshape(HK, model_width, qkv_half)
    output_w = output_w.reshape(2, q_cols, out_half)

    cot_corner = plane_corner(cot_sides, (out_corner,))
    cot_pieces = plane_pieces(out_grad, cot_sides, cot_corner)
    expert_range = jnp.arange(128, dtype=jnp.int32)
    chosen_mask = jnp.any(ids_all[:, :, None] == expert_range[None, None, :], axis=1)
    bias = jnp.where(chosen_mask, 0.0, -1e30).astype(f32)
    own_mask = jnp.any(ids_all == own_expert, axis=1).reshape(blocks, block_rows)
    place = jnp.cumsum(own_mask.astype(jnp.int32), axis=1) - 1
    slots = jnp.where(own_mask, place, -1)

    gate_w, up_w, down_w = (
        lax.dynamic_index_in_dim(weight, own_local, 0, keepdims=False)
        for weight in (w_gate, w_up, w_down)
    )

    expert = functools.partial(
        run_expert,
        at=at,
        slots=slots,
        bias=bias,
        router=router_w,
        weights=(gate_w, up_w, down_w),
        capacity=capacity,
    )
    second_sides = plane_sides(second_in)
    groups = ((0, 4), (1, 5, 2, 6), (3, 7))
    second_pieces = {0: second_in, 4: swap(second_in, "c")}

    def run_group(pieces):
        return expert(
            pieces,
            second=[second_pieces[piece] for piece in pieces],
            cot=[cot_pieces[piece] for piece in pieces],
        )

    stage_own = run_group(groups[0])
    second_sides = lax.optimization_barrier((*second_sides, stage_own[0]))[:2]
    second_corner = plane_corner(second_sides)
    for piece, block in zip((1, 2), second_sides):
        second_pieces[piece], second_pieces[piece + 4] = block, swap(block, "c")
    stage_sides = run_group(groups[1])
    second_corner = after(second_corner, stage_sides[0])
    second_pieces[3], second_pieces[7] = second_corner, swap(second_corner, "c")
    own_near, own_far = stage_own[6:]
    own_far = swap(own_far, "c")
    both = jnp.concatenate(
        lax.optimization_barrier((attended, first_in, second_corner))[:2], axis=0
    )
    both_sides = plane_sides(both)
    x_near, x_far, y_near, y_far = stage_sides[6:]
    back_x, back_y = over_core(x_near, x_far), over_core(y_near, y_far)
    first_x, first_y = early_sums(back_x, back_y)
    stage_corner = run_group(groups[2])
    corner = over_core(*stage_corner[6:])
    passed = corner_first(corner)
    stages = (stage_own, stage_sides, stage_corner)
    rows_in, rows_cot, gated, gate_back, up_back = ([stage[n] for stage in stages] for n in range(5))
    gates = stage_own[5]
    (down_part,) = row_sums(at, [after(rows_cot[0], corner)] + rows_cot[1:], gated)
    down_sum = scatter_sum(down_part, "z")
    passed = lax.optimization_barrier((*passed, down_part))[:2]
    last_y, last_x, sent = corner_last(back_x, back_y, passed)
    gate_part, up_part = row_sums(
        at, [after(rows_in[0], sent)] + rows_in[1:], gate_back, up_back
    )
    gate_sum = scatter_sum(gate_part, "z")
    own_near = after(own_near, gate_part)

    resid_grad, branch_grad, attended_grad, router_acc, gain_two_grad = run_kernel(
        branch_back_kernel,
        6,
        at,
        (
            own_near,
            own_far,
            first_x,
            first_y,
            last_y,
            last_x,
            resid,
            gain_two,
            second_in,
            gates,
            router_w,
            out_grad,
            output_w,
        ),
        [
            ((length, model_width), f32),
            ((length, model_width), bf16),
            ((length, q_cols), bf16),
            ((model_width, 128), f32),
            ((1, model_width), f32),
        ],
    )
    (qkv_back,) = run_kernel(
        attend_back_kernel,
        12,
        at,
        (attended_grad, probs, queries, keys_rot, values_b, cosine_all, sine_all),
        [((plane, length, qkv_cols // plane), bf16)],
    )
    branch_back = jnp.moveaxis(branch_grad.reshape(length, plane, model_width // plane), 1, 0)
    branch_cols = exchange(branch_back, PLANE)
    qkv_cols_back = exchange(qkv_back, PLANE)
    tokens_grad, gain_one_grad = run_kernel(
        first_back_kernel,
        6,
        at,
        (qkv_back, qkv_w, tokens, gain_one, after(resid_grad, branch_cols)),
        [((length, model_width), bf16), ((1, model_width), f32)],
    )

    both_corner = plane_corner(both_sides, (qkv_cols_back,))
    both_pieces = plane_pieces(both, both_sides, both_corner)
    narrow_part = jnp.concatenate(
        [router_acc[:, :experts_all], gain_one_grad.T, gain_two_grad.T], axis=1
    )
    narrow_cols = -(-narrow_part.shape[1] // owners) * owners
    narrow_part = jnp.pad(narrow_part, ((0, 0), (0, narrow_cols - narrow_part.shape[1])))
    narrow_part = jnp.transpose(
        narrow_part.reshape(depth, 2, 2, shard_rows, owners, narrow_cols // owners),
        (1, 2, 4, 0, 3, 5),
    ).reshape(plane, depth, shard_rows * narrow_cols // owners)
    narrow_part = jnp.sum(exchange(narrow_part, PLANE), axis=0)
    qkv_width = qkv_cols // plane
    dense_cols = qkv_width + model_width // plane
    narrow_len = narrow_part.shape[1]
    narrow_rows = -(-narrow_len // dense_cols)
    kept_rows = -(-narrow_rows // 16) * 16
    narrow_part = jnp.pad(narrow_part, ((0, 0), (0, kept_rows * dense_cols - narrow_len)))
    wide_rows = local_count * shard_rows
    dense_shape = (depth, wide_rows + kept_rows, dense_cols)
    anywhere = pl.BlockSpec(memory_space=pl.ANY)
    dense_part = pl.pallas_call(
        dense_grad_kernel,
        out_shape=jax.ShapeDtypeStruct(dense_shape, bf16),
        in_specs=[SCALARS] + [WHOLE] * 3 + [anywhere] * 8,
        out_specs=WHOLE,
        scratch_shapes=[
            pltpu.VMEM((plane, 2 * length, model_width), bf16),
            pltpu.SemaphoreType.DMA((plane,)),
        ],
        cost_estimate=cost(7),
        compiler_params=pltpu.CompilerParams(vmem_limit_bytes=48 * 2**20),
    )(
        at,
        narrow_part.reshape(depth, kept_rows, dense_cols).astype(bf16),
        branch_cols,
        qkv_cols_back,
        *both_pieces,
    )
    dense_sum = scatter_sum(dense_part.reshape(-1, dense_cols), "z")
    wide_sum = dense_sum[: local_count * shard_rows].reshape(2, 2, 1, shard_rows, dense_cols)
    wide_sum = jnp.broadcast_to(wide_sum, (2, 2, owners, shard_rows, dense_cols)).reshape(
        plane, shard_rows, dense_cols
    )
    narrow_sum = dense_sum[local_count * shard_rows :][:narrow_rows]
    narrow_sum = jnp.broadcast_to(narrow_sum[None], (plane, narrow_rows, dense_cols))
    pad_rows = -(shard_rows + narrow_rows) % 16
    padding = jnp.zeros((plane, pad_rows, dense_cols), bf16)
    dense_sum = exchange(jnp.concatenate([wide_sum, narrow_sum, padding], axis=1), PLANE)
    wide_sum = jnp.moveaxis(dense_sum[:, :shard_rows].astype(f32), 0, 1)
    qkv_sum = wide_sum[:, :, :qkv_width].reshape(shard_rows, HK, qkv_half)
    output_sum = wide_sum[:, :, qkv_width:].reshape(shard_rows, model_width)
    narrow_sum = dense_sum[:, shard_rows : shard_rows + narrow_rows].reshape(
        2, 2, owners, narrow_rows * dense_cols
    )
    narrow_sum = narrow_sum[y, c, :, :narrow_len].reshape(owners, shard_rows, -1)
    narrow_sum = jnp.moveaxis(narrow_sum, 0, 1).reshape(shard_rows, narrow_cols).astype(f32)

    up_sum = scatter_sum(after(up_part, dense_sum), "z")

    shares = run_kernel(
        functools.partial(mixture_kernel, capacity, groups),
        10,
        at,
        (slots, down_w, after(gated[0], both_corner), *gated[1:]),
        [((length, model_width), bf16)] * plane,
        48,
    )
    mixed = [over_core(near, far) for near, far in zip(shares[:4], shares[4:])]
    early = early_sums(mixed[1], mixed[2])
    last = corner_last(mixed[1], mixed[2], corner_first(mixed[3]))[:2]
    mixture = jnp.concatenate(
        [left.astype(f32) + right.astype(f32) for left, right in zip(early, last)], axis=0
    )
    block_out = (resid + (mixture + mixed[0].astype(f32))).astype(bf16)

    def placed(total):
        total = exchange(total, ("y", "c"))
        return total.reshape(local_count, shard_rows, hidden_width).astype(f32)

    return (
        block_out,
        tokens_grad,
        narrow_sum[:, experts_all],
        qkv_sum[:, :, :q_group].reshape(shard_rows, q_cols),
        qkv_sum[:, :, q_group : q_group + HD].reshape(shard_rows, kv_cols),
        qkv_sum[:, :, q_group + HD :].reshape(shard_rows, kv_cols),
        output_sum,
        narrow_sum[:, experts_all + 1],
        narrow_sum[:, :experts_all],
        placed(gate_sum),
        placed(up_sum),
        jnp.swapaxes(placed(down_sum), 1, 2),
    )


def solution(mesh):
    groups, owners = mesh.shape["dp"], mesh.shape["expert"]
    grid = jax.sharding.Mesh(
        mesh.devices.reshape(groups // 4, 2, 2, owners), ("z", "y", "c", "x")
    )
    rows = P(("z", "y", "c", "x"), None)
    shard, shard_rows = P(GROUP), P(GROUP, None)
    expert = P("x", None, None)
    return jax.shard_map(
        local_pairs if owners == 2 else local_wide,
        mesh=grid,
        in_specs=(
            rows,
            shard,
            shard_rows,
            shard_rows,
            shard_rows,
            shard_rows,
            shard,
            shard_rows,
            expert,
            expert,
            expert,
            rows,
            P(("z", "y", "c", "x")),
            rows,
        ),
        out_specs=(
            rows,
            rows,
            shard,
            shard_rows,
            shard_rows,
            shard_rows,
            shard_rows,
            shard,
            shard_rows,
            P("x", GROUP, None),
            P("x", GROUP, None),
            P("x", None, GROUP),
        ),
        check_vma=False,
    )
```

```python
import functools
import math

import jax
import jax.numpy as jnp
from jax import lax
from jax.experimental import pallas as pl
from jax.experimental.pallas import tpu as pltpu
from jax.sharding import PartitionSpec as P

HQ = 12
HK = 2
HD = 128
MICRO = 2
PLANE = ("y", "c", "x")
GROUP = ("z", "y", "c")


def rms_scale(values, gain_vec):
    inverse = lax.rsqrt(jnp.mean(values * values, axis=-1, keepdims=True) + 1e-06)
    return values * inverse * gain_vec


def angles(length, head_size):
    positions = jnp.arange(length).astype(jnp.float32)
    freq_rates = jnp.exp(
        -(2.0 * jnp.arange(head_size // 2).astype(jnp.float32) / head_size) * math.log(1000000.0)
    )
    angle_tab = positions[:, None] * freq_rates[None, :]
    return (jnp.cos(angle_tab)[:, None, :], jnp.sin(angle_tab)[:, None, :])


def rotary(values, cosine_tab, sine_tab):
    half_dim = values.shape[-1] // 2
    first_half = values[..., :half_dim]
    second_half = values[..., half_dim:]
    return jnp.concatenate(
        [
            first_half * cosine_tab - second_half * sine_tab,
            second_half * cosine_tab + first_half * sine_tab,
        ],
        axis=-1,
    )


def expert_act(gate_pre, up_pre):
    return jax.nn.gelu(gate_pre, approximate=True) * up_pre


def left_product(left_mat, right_mat):
    return lax.dot_general(
        left_mat, right_mat, (((0,), (0,)), ((), ())), preferred_element_type=jnp.float32
    )


def gather(block, axes):
    return lax.all_gather(block, axes, axis=0, tiled=True)


def exchange(block, axes):
    return lax.all_to_all(block, axes, split_axis=0, concat_axis=0, tiled=True)


def scatter_sum(block, axes):
    return lax.psum_scatter(block, axes, scatter_dimension=0, tiled=True)


def by_owner(cols, parts):
    rows, total = cols.shape
    return jnp.moveaxis(cols.reshape(rows, parts, total // parts), 1, 0).reshape(
        parts * rows, total // parts
    )


def local_wide(
    tokens,
    norm1_gain,
    w_query,
    w_key,
    w_value,
    w_out,
    norm2_gain,
    w_router,
    w_gate,
    w_up,
    w_down,
    expert_ids,
    prefix_len,
    out_grad,
):
    bf16, f32 = jnp.bfloat16, jnp.float32
    length, model_width = tokens.shape
    shard_rows = w_query.shape[0]
    local_count, _, hidden_width = w_gate.shape
    owners = lax.axis_size("x")
    depth = lax.axis_size("z")
    plane = lax.axis_size(PLANE)
    experts_all = w_router.shape[1]
    top_count = expert_ids.shape[1]
    block_rows = length // MICRO
    capacity = 3 * block_rows * top_count // (2 * experts_all)
    plane_rows = plane * length
    blocks = plane_rows // block_rows
    group_size = HQ // HK
    score_scale = HD ** (-0.5)
    q_cols, kv_cols = w_query.shape[1], w_key.shape[1]
    own_local = lax.axis_index(("y", "c"))
    own_expert = lax.axis_index("x") * local_count + own_local
    own_place = lax.axis_index(PLANE)

    narrow = jnp.concatenate([w_router, norm1_gain[:, None], norm2_gain[:, None]], axis=1)
    narrow = jnp.pad(narrow, ((0, 0), (0, -narrow.shape[1] % 128)))
    packed = gather(jnp.concatenate([w_query, w_key, w_value, narrow], axis=1), GROUP)
    qkv_cols = q_cols + 2 * kv_cols
    qkv_w = packed[:, :qkv_cols]
    router_w = packed[:, qkv_cols : qkv_cols + experts_all]
    gains = packed[:, qkv_cols + experts_all : qkv_cols + experts_all + 2].T.astype(f32)
    gain_one, gain_two = gains[0], gains[1]
    output_w = gather(w_out, GROUP)

    ids_all = gather(expert_ids, PLANE)
    cot_all = gather(out_grad, PLANE)
    chosen_mask = jnp.any(
        ids_all[:, :, None] == jnp.arange(experts_all, dtype=jnp.int32)[None, None, :], axis=1
    )
    own_mask = jnp.any(ids_all == own_expert, axis=1).reshape(blocks, block_rows)
    place = jnp.cumsum(own_mask.astype(jnp.int32), axis=1) - 1
    dispatch = (
        own_mask[:, None, :]
        & (place[:, None, :] == jnp.arange(capacity, dtype=jnp.int32)[None, :, None])
    ).astype(bf16)

    cosine_tab, sine_tab = angles(length, HD)
    inputs_f = tokens.astype(f32)
    first_in = rms_scale(inputs_f, gain_one).astype(bf16)
    qkv = jnp.dot(first_in, qkv_w, preferred_element_type=f32)
    queries = (
        rotary(qkv[:, :q_cols].reshape(length, HQ, HD), cosine_tab, sine_tab)
        .astype(bf16)
        .reshape(length, HK, group_size, HD)
    )
    keys_rot = rotary(
        qkv[:, q_cols : q_cols + kv_cols].reshape(length, HK, HD), cosine_tab, sine_tab
    ).astype(bf16)
    values_b = qkv[:, q_cols + kv_cols :].astype(bf16).reshape(length, HK, HD)
    positions = jnp.arange(length)
    allowed = (positions[None, :] <= positions[:, None]) | (positions[None, :] < prefix_len[0])

    def masked_scores():
        scores = jnp.einsum("ihrd,jhd->hrij", queries, keys_rot, preferred_element_type=f32)
        return jnp.where(allowed, scores * score_scale, -1e30)

    masked = masked_scores()
    row_peak = jnp.max(masked, axis=-1, keepdims=True)
    log_total = row_peak + jnp.log(jnp.sum(jnp.exp(masked - row_peak), axis=-1, keepdims=True))
    prob_bf = jnp.exp(masked - log_total).astype(bf16)
    attended = jnp.einsum("hrij,jhd->ihrd", prob_bf, values_b, preferred_element_type=f32)
    attended = attended.reshape(length, HQ * HD).astype(bf16)
    resid = inputs_f + jnp.dot(attended, output_w, preferred_element_type=f32)
    second_in = rms_scale(resid, gain_two).astype(bf16)

    second_all = gather(second_in, PLANE)
    logits = jnp.dot(second_all, router_w, preferred_element_type=f32)
    gates_all = jax.nn.softmax(jnp.where(chosen_mask, logits, -jnp.inf), axis=-1)
    own_gates = lax.dynamic_index_in_dim(gates_all, own_expert, 1, keepdims=False)
    own_gates = own_gates.reshape(blocks, block_rows)
    gate_rows = jnp.einsum(
        "bct,bt->bc", dispatch.astype(f32), own_gates, precision=lax.Precision.HIGHEST
    )[:, :, None]
    gate_w = lax.dynamic_index_in_dim(w_gate, own_local, 0, keepdims=False)
    up_w = lax.dynamic_index_in_dim(w_up, own_local, 0, keepdims=False)
    down_w = lax.dynamic_index_in_dim(w_down, own_local, 0, keepdims=False)

    def to_rows(array):
        return jnp.einsum(
            "bct,btd->bcd",
            dispatch,
            array.reshape(blocks, block_rows, model_width),
            preferred_element_type=f32,
        ).astype(bf16)

    def to_tokens(rows):
        return (
            jnp.einsum("bct,bcd->btd", dispatch, rows.astype(bf16), preferred_element_type=f32)
            .astype(bf16)
            .reshape(plane_rows, model_width)
        )

    rows_in = to_rows(second_all)
    rows_cot = to_rows(cot_all)
    gate_pre = jnp.einsum("bcd,df->bcf", rows_in, gate_w, preferred_element_type=f32)
    up_pre = jnp.einsum("bcd,df->bcf", rows_in, up_w, preferred_element_type=f32)
    hidden, act_pull = jax.vjp(expert_act, gate_pre, up_pre)
    gated = (gate_rows * hidden).astype(bf16)
    down_part = jnp.einsum("bcd,bcf->df", rows_cot, gated, preferred_element_type=f32)
    down_sum = scatter_sum(down_part.astype(bf16), "z")
    cot_hidden = jnp.einsum("bcd,fd->bcf", rows_cot, down_w, preferred_element_type=f32)
    gate_signal_rows = jnp.sum(hidden * cot_hidden, axis=-1)
    gate_pgrad, up_pgrad = act_pull(gate_rows * cot_hidden)
    gate_pgrad = gate_pgrad.astype(bf16)
    up_pgrad = up_pgrad.astype(bf16)
    gate_part = jnp.einsum("bcd,bcf->df", rows_in, gate_pgrad, preferred_element_type=f32)
    gate_sum = scatter_sum(gate_part.astype(bf16), "z")
    up_part = jnp.einsum("bcd,bcf->df", rows_in, up_pgrad, preferred_element_type=f32)
    up_sum = scatter_sum(up_part.astype(bf16), "z")
    rows_grad = jnp.einsum("bcf,df->bcd", gate_pgrad, gate_w, preferred_element_type=f32)
    rows_grad = rows_grad + jnp.einsum("bcf,df->bcd", up_pgrad, up_w, preferred_element_type=f32)
    second_back = scatter_sum(to_tokens(rows_grad), PLANE).astype(f32)
    gate_signal = jnp.einsum(
        "bct,bc->bt", dispatch.astype(f32), gate_signal_rows, precision=lax.Precision.HIGHEST
    )
    gate_signal = exchange(gate_signal.reshape(plane, length), PLANE)
    gate_signal = jnp.transpose(
        gate_signal.reshape(local_count, owners, length), (2, 1, 0)
    ).reshape(length, experts_all)
    expert_rows = jnp.einsum("bcf,fd->bcd", gated, down_w, preferred_element_type=f32)
    mixture = scatter_sum(to_tokens(expert_rows), PLANE).astype(f32)
    block_out = (resid + mixture).astype(bf16)

    cotangent = out_grad.astype(f32)
    gate_probs = lax.dynamic_slice_in_dim(gates_all, own_place * length, length, 0)
    logit_grad = (
        gate_probs
        * (gate_signal - jnp.sum(gate_probs * gate_signal, axis=-1, keepdims=True))
    ).astype(bf16)
    router_acc = left_product(second_in, logit_grad)
    second_grad = second_back + jnp.dot(logit_grad, router_w.T, preferred_element_type=f32)
    _, norm_two_pull = jax.vjp(rms_scale, resid, gain_two)
    resid_norm_grad, gain_two_grad = norm_two_pull(second_grad)
    resid_grad = cotangent + resid_norm_grad
    branch_grad = resid_grad.astype(bf16)

    attended_all = gather(attended, PLANE)
    branch_cols = exchange(by_owner(branch_grad, plane), PLANE)
    output_part = left_product(attended_all, branch_cols)
    attended_grad = jnp.dot(branch_grad, output_w.T, preferred_element_type=f32).astype(bf16)
    attended_grad = attended_grad.reshape(length, HK, group_size, HD)
    masked = masked_scores()
    prob_full = jnp.exp(masked - log_total)
    prob_bf = prob_full.astype(bf16)
    prob_grad = jnp.einsum("ihrd,jhd->hrij", attended_grad, values_b, preferred_element_type=f32)
    row_inner = jnp.sum(prob_full * prob_grad, axis=-1, keepdims=True)
    score_grad = (prob_full * (prob_grad - row_inner)).astype(bf16)
    query_rot_grad = (
        jnp.einsum("hrij,jhd->ihrd", score_grad, keys_rot, preferred_element_type=f32)
        * score_scale
    )
    query_back = rotary(query_rot_grad.reshape(length, HQ, HD), cosine_tab, -sine_tab)
    query_back = query_back.astype(bf16).reshape(length, HQ * HD)
    key_rot_grad = (
        jnp.einsum("hrij,ihrd->jhd", score_grad, queries, preferred_element_type=f32)
        * score_scale
    )
    key_back = rotary(key_rot_grad, cosine_tab, -sine_tab).astype(bf16).reshape(length, HK * HD)
    value_back = jnp.einsum("hrij,ihrd->jhd", prob_bf, attended_grad, preferred_element_type=f32)
    value_back = value_back.astype(bf16).reshape(length, HK * HD)
    qkv_back = jnp.concatenate([query_back, key_back, value_back], axis=1)
    first_all = gather(first_in, PLANE)
    qkv_part = left_product(first_all, exchange(by_owner(qkv_back, plane), PLANE))
    first_grad = lax.dot_general(
        qkv_back, qkv_w, (((1,), (1,)), ((), ())), preferred_element_type=f32
    )
    _, norm_one_pull = jax.vjp(rms_scale, inputs_f, gain_one)
    input_norm_grad, gain_one_grad = norm_one_pull(first_grad)
    tokens_grad = (resid_grad + input_norm_grad).astype(bf16)

    narrow_part = jnp.concatenate(
        [router_acc, gain_one_grad[:, None], gain_two_grad[:, None]], axis=1
    ).astype(bf16)
    narrow_cols = narrow_part.shape[1]
    narrow_sum = lax.psum(scatter_sum(narrow_part, GROUP), "x").astype(f32)
    dense_part = jnp.concatenate([qkv_part, output_part], axis=1).astype(bf16)
    dense_sum = scatter_sum(dense_part, "z")
    dense_cols = dense_sum.shape[1]
    dense_sum = gather(dense_sum, PLANE).reshape(plane, local_count, shard_rows, dense_cols)
    dense_sum = lax.dynamic_index_in_dim(dense_sum, own_local, 1, keepdims=False).astype(f32)
    dense_sum = jnp.moveaxis(dense_sum, 0, 1)
    qkv_width = qkv_cols // plane
    qkv_sum = dense_sum[:, :, :qkv_width].reshape(shard_rows, qkv_cols)
    output_sum = dense_sum[:, :, qkv_width:].reshape(shard_rows, model_width)

    def placed(total):
        total = exchange(total, ("y", "c"))
        return total.reshape(local_count, shard_rows, hidden_width).astype(f32)

    return (
        block_out,
        tokens_grad,
        narrow_sum[:, experts_all],
        qkv_sum[:, :q_cols],
        qkv_sum[:, q_cols : q_cols + kv_cols],
        qkv_sum[:, q_cols + kv_cols :],
        output_sum,
        narrow_sum[:, experts_all + 1],
        narrow_sum[:, :experts_all],
        placed(gate_sum),
        placed(up_sum),
        jnp.swapaxes(placed(down_sum), 1, 2),
    )


def rounded(values):
    return lax.reduce_precision(values, 8, 7).astype(jnp.bfloat16)


def after(block, *others):
    return lax.optimization_barrier((block,) + others)[0]


def swap(block, axis):
    return lax.ppermute(block, axis, [(0, 1), (1, 0)])


def shifts(block):
    depth = lax.axis_size("z")
    return [
        lax.ppermute(block, "z", [(i, (i + k) % depth) for i in range(depth)])
        for k in range(1, depth)
    ]


def plane_sides(block):
    return swap(block, "x"), swap(block, "y")


def plane_corner(sides, before=()):
    over_x, over_y = sides
    half = over_x.shape[0] // 2
    over_y, over_x = lax.optimization_barrier((over_y[:half], over_x[half:]) + before)[:2]
    return jnp.concatenate([swap(over_y, "x"), swap(over_x, "y")], axis=0)


def plane_pieces(block, sides=None, corner=None):
    sides = plane_sides(block) if sides is None else sides
    corner = plane_corner(sides) if corner is None else corner
    pieces = [block, *sides, corner]
    return pieces + [swap(piece, "c") for piece in pieces]


def small_gather(block):
    for axis in ("x", "y", "c"):
        block = jnp.concatenate([block, swap(block, axis)], axis=0)
    return block


def small_group_gather(block):
    depth = lax.axis_size("z")
    order = jnp.stack(([block] + shifts(block))[::-1] * 2)
    start = (depth - 1 - lax.axis_index("z")) % depth
    total = lax.dynamic_slice_in_dim(order, start, depth, 0)[:, None, None]
    for dim, axis in ((1, "y"), (2, "c")):
        other = swap(total, axis)
        last = lax.axis_index(axis) == 1
        pair = [jnp.where(last, other, total), jnp.where(last, total, other)]
        total = jnp.concatenate(pair, axis=dim)
    return total.reshape(-1, block.shape[1])


def add(left, right):
    return rounded(left.astype(jnp.float32) + right.astype(jnp.float32))


def over_core(near, far):
    return add(near, swap(far, "c"))


def early_sums(over_x, over_y):
    half = over_x.shape[0] // 2
    return swap(over_x[:half], "x"), swap(over_y[half:], "y")


def corner_first(corner):
    half = corner.shape[0] // 2
    return swap(corner[:half], "x"), swap(corner[half:], "y")


def corner_last(over_x, over_y, first):
    half = over_x.shape[0] // 2
    over_y, over_x = add(over_y[:half], first[0]), add(over_x[half:], first[1])
    return swap(over_y, "y"), swap(over_x, "x"), over_x


def cost(micros):
    return pl.CostEstimate(flops=micros * 10**9, bytes_accessed=micros * 10**6, transcendentals=0)


def dot(left, right, dims=((1,), (0,)), precision=None):
    return lax.dot_general(
        left, right, (dims, ((), ())), precision=precision, preferred_element_type=jnp.float32
    )


WHOLE = pl.BlockSpec(memory_space=pltpu.VMEM)
SCALARS = pl.BlockSpec(memory_space=pltpu.SMEM)


def run_kernel(kernel, micros, at, operands, outs, megabytes=16, scratch=()):
    return pl.pallas_call(
        kernel,
        out_shape=[jax.ShapeDtypeStruct(shape, dtype) for shape, dtype in outs],
        in_specs=[SCALARS] + [WHOLE] * len(operands),
        out_specs=[WHOLE] * len(outs),
        scratch_shapes=scratch,
        cost_estimate=cost(micros),
        compiler_params=pltpu.CompilerParams(vmem_limit_bytes=megabytes * 2**20),
    )(at, *operands)


def place_pieces(at, refs, weight):
    depth = weight.shape[1]
    for n, ref in enumerate(refs):
        dc, dy, dx = n // 4, n // 2 % 2, n % 2
        for k in range(depth):
            z = lax.rem(at[3] + depth - k, depth)
            weight[at[2] ^ dx, z, at[0] ^ dy, at[1] ^ dc] = ref[k]


def rms_kernel(values, gain):
    inverse = lax.rsqrt(jnp.mean(values * values, axis=-1, keepdims=True) + 1e-06)
    return (values * inverse * gain).astype(jnp.bfloat16)


def rms_back(values, gain, grad):
    inverse = lax.rsqrt(jnp.mean(values * values, axis=-1, keepdims=True) + 1e-06)
    normed = values * inverse
    gain_grad = jnp.sum(grad * normed, axis=0, keepdims=True)
    grad = grad * gain
    along = jnp.mean(grad * normed, axis=-1, keepdims=True)
    return inverse * (grad - normed * along), gain_grad


def turned(values, cosine_tab, sine_tab):
    return values * cosine_tab + pltpu.roll(values, HD // 2, 1) * sine_tab


def attend_kernel(at, tokens, gain, cosine, sine, *refs):
    first_ref, query_ref, key_ref, value_ref, prob_ref, out_ref, weight = refs[8:]
    place_pieces(at, refs[:8], weight)
    length = tokens.shape[0]
    first_in = rms_kernel(tokens[...].astype(jnp.float32), gain[...])
    first_ref[...] = first_in
    rows = lax.broadcasted_iota(jnp.int32, (length, length), 0)
    cols = lax.broadcasted_iota(jnp.int32, (length, length), 1)
    allowed = (cols <= rows) | (cols < at[4])
    cosine_tab, sine_tab = cosine[...], sine[...]
    group_size = HQ // HK
    for group in range(HK):
        matrix = weight[group].reshape(first_in.shape[1], -1)
        qkv = dot(first_in, matrix)
        at_key = group_size * HD
        key = turned(qkv[:, at_key : at_key + HD], cosine_tab, sine_tab).astype(jnp.bfloat16)
        value = qkv[:, at_key + HD :].astype(jnp.bfloat16)
        key_ref[:, group * HD : (group + 1) * HD] = key
        value_ref[:, group * HD : (group + 1) * HD] = value
        for member in range(group_size):
            head = group * group_size + member
            here = slice(head * HD, (head + 1) * HD)
            query = turned(qkv[:, member * HD : (member + 1) * HD], cosine_tab, sine_tab)
            query = query.astype(jnp.bfloat16)
            query_ref[:, here] = query
            scores = dot(query, key, ((1,), (1,)))
            scores = jnp.where(allowed, scores * HD ** (-0.5), -1e30)
            weights = jnp.exp(scores - jnp.max(scores, axis=-1, keepdims=True))
            prob = weights * (1.0 / jnp.sum(weights, axis=-1, keepdims=True))
            prob = prob.astype(jnp.bfloat16)
            prob_ref[head] = prob
            out_ref[:, here] = dot(prob, value).astype(jnp.bfloat16)


def project_kernel(at, tokens, gain, attended, *refs):
    resid_ref, second_ref, weight = refs[8:]
    place_pieces(at, refs[:8], weight)
    heads = attended[...]
    halves = [dot(heads, weight[half].reshape(heads.shape[1], -1)) for half in range(2)]
    resid = tokens[...].astype(jnp.float32) + jnp.concatenate(halves, axis=1)
    resid_ref[...] = resid
    second_ref[...] = rms_kernel(resid, gain[...])


def one_hot(slots, capacity, dtype):
    shape = (capacity, slots.shape[1])
    return (slots == lax.broadcasted_iota(jnp.int32, shape, 0)).astype(jnp.float32).astype(dtype)


def spread(slots, pieces, capacity, rows, outs):
    rows = rows.astype(jnp.bfloat16)
    block = slots.shape[1]
    for n, piece in enumerate(pieces):
        for part in range(2):
            pick = one_hot(slots[2 * piece + part : 2 * piece + part + 1], capacity, jnp.bfloat16)
            at_row = (2 * n + part) * capacity
            tokens = dot(pick, rows[at_row : at_row + capacity], ((0,), (0,)))
            outs[n][part * block : (part + 1) * block] = tokens.astype(jnp.bfloat16)


def expert_kernel(capacity, pieces, at, slots, bias, router, gate_w, up_w, down_w, *refs):
    count = len(pieces)
    second, cot = refs[:count], refs[count : 2 * count]
    rows_in, rows_cot, gated_ref, gate_back, up_back, gates_ref = refs[2 * count : 2 * count + 6]
    backs = refs[2 * count + 6 : -1]
    gate_rows = refs[-1]
    f32, bf16 = jnp.float32, jnp.bfloat16
    length = second[0].shape[0]
    half = length // 2
    for n, piece in enumerate(pieces):
        tokens = second[n][...]
        logits = dot(tokens, router[...]) + bias[piece * length : (piece + 1) * length]
        weights = jnp.exp(logits - jnp.max(logits, axis=-1, keepdims=True))
        gates = weights * (1.0 / jnp.sum(weights, axis=-1, keepdims=True))
        if n == 0:
            gates_ref[...] = gates
        lanes = lax.broadcasted_iota(jnp.int32, (capacity, gates.shape[1]), 1)
        for part in range(2):
            block = 2 * piece + part
            here = slice(part * half, (part + 1) * half)
            place = slice((2 * n + part) * capacity, (2 * n + part + 1) * capacity)
            pick = one_hot(slots[block : block + 1], capacity, f32)
            rows_in[place] = dot(pick.astype(bf16), tokens[here]).astype(bf16)
            rows_cot[place] = dot(pick.astype(bf16), cot[n][here]).astype(bf16)
            picked = dot(pick, gates[here], precision=lax.Precision.HIGHEST)
            picked = jnp.where(lanes == at[5], picked, 0.0)
            gate_rows[place] = jnp.sum(picked, axis=1, keepdims=True)
    gate = gate_rows[...]
    gate_pre = dot(rows_in[...], gate_w[...])
    up_pre = dot(rows_in[...], up_w[...])
    cot_hidden = dot(rows_cot[...], down_w[...], ((1,), (1,)))
    scale = math.sqrt(2.0 / math.pi)
    square = gate_pre * gate_pre
    bent = jnp.tanh(scale * gate_pre * (1.0 + 0.044715 * square))
    open_part = 0.5 * (1.0 + bent)
    active = gate_pre * open_part
    slope = open_part + 0.5 * gate_pre * (1.0 - bent * bent) * scale * (
        1.0 + 3 * 0.044715 * square
    )
    hidden = active * up_pre
    gated_ref[...] = (gate * hidden).astype(bf16)
    signal = jnp.sum(hidden * cot_hidden, axis=1, keepdims=True)
    back = gate * cot_hidden
    gate_back[...] = (back * up_pre * slope).astype(bf16)
    up_back[...] = (back * active).astype(bf16)
    high = signal.astype(bf16)
    low = (signal - high.astype(f32)).astype(bf16)
    lanes = lax.broadcasted_iota(jnp.int32, (signal.shape[0], bias.shape[1]), 1)
    signal = jnp.where(lanes == at[5], high.astype(f32), 0.0)
    signal = jnp.where(lanes == at[5] + bias.shape[1] // 2, low.astype(f32), signal)
    by_rows = ((1,), (1,))
    rows = dot(gate_back[...], gate_w[...], by_rows) + dot(up_back[...], up_w[...], by_rows)
    spread(slots, pieces, capacity, jnp.concatenate([rows, signal], axis=1), backs)


def run_expert(pieces, at, slots, bias, router, weights, second, cot, capacity):
    count = len(pieces)
    rows = 2 * count * capacity
    (length, width), hidden = second[0].shape, weights[0].shape[1]
    bf16, f32 = jnp.bfloat16, jnp.float32
    outs = [(rows, width)] * 2 + [(rows, hidden)] * 3
    outs = [(shape, bf16) for shape in outs] + [((length, bias.shape[1]), f32)]
    outs = outs + [((length, width + bias.shape[1]), bf16)] * count
    return run_kernel(
        functools.partial(expert_kernel, capacity, pieces),
        4 * count,
        at,
        (slots, bias, router, *weights, *second, *cot),
        outs,
        8 + 6 * count,
        [pltpu.VMEM((rows, 1), f32)],
    )


def mixture_kernel(capacity, groups, at, slots, down_w, *refs):
    outs = refs[len(groups) :]
    for pieces, gated in zip(groups, refs):
        rows = dot(gated[...], down_w[...])
        spread(slots, pieces, capacity, rows, [outs[piece] for piece in pieces])


def row_sum_kernel(parts, at, *refs):
    arrays = [
        jnp.concatenate([ref[...] for ref in refs[n : n + parts]], axis=0)
        for n in range(0, len(refs) - len(refs) // (parts + 1), parts)
    ]
    outs = refs[len(arrays) * parts :]
    for out, right in zip(outs, arrays[1:]):
        out[...] = dot(arrays[0], right, ((0,), (0,))).astype(jnp.bfloat16)


def row_sums(at, left, *rights):
    operands = [part for parts in (left, *rights) for part in parts]
    outs = [((left[0].shape[1], right[0].shape[1]), jnp.bfloat16) for right in rights]
    kernel = functools.partial(row_sum_kernel, len(left))
    return run_kernel(kernel, 6 * len(rights), at, operands, outs, 24)


def branch_back_kernel(
    at, near, far, first_x, first_y, last_y, last_x, resid, gain, second, gates, router, cot, weight, *outs
):
    resid_grad_ref, branch_ref, attended_ref, router_ref, gain_ref = outs
    f32, bf16 = jnp.float32, jnp.bfloat16
    halves = [first_x[...].astype(f32) + last_y[...], first_y[...].astype(f32) + last_x[...]]
    total = near[...].astype(f32) + far[...] + jnp.concatenate(halves, axis=0)
    width = resid.shape[1]
    signal = total[:, width:]
    signal = signal + pltpu.roll(signal, signal.shape[1] // 2, 1)
    chosen = gates[...]
    logit_grad = chosen * (signal - jnp.sum(chosen * signal, axis=-1, keepdims=True))
    logit_grad = logit_grad.astype(bf16)
    second_grad = total[:, :width] + dot(logit_grad, router[...], ((1,), (1,)))
    norm_grad, gain_grad = rms_back(resid[...], gain[...], second_grad)
    gain_ref[...] = gain_grad
    resid_grad = cot[...].astype(f32) + norm_grad
    resid_grad_ref[...] = resid_grad
    branch = resid_grad.astype(bf16)
    branch_ref[...] = branch
    wide = weight.shape[2]
    attended_ref[...] = (
        dot(branch[:, :wide], weight[0], ((1,), (1,)))
        + dot(branch[:, wide:], weight[1], ((1,), (1,)))
    ).astype(bf16)
    router_ref[...] = dot(second[...], logit_grad, ((0,), (0,)))


def attend_back_kernel(
    at, attended, probs, queries, keys, values, cosine, sine, branch, back_ref
):
    f32, bf16 = jnp.float32, jnp.bfloat16
    cosine_tab, sine_tab = cosine[...], -sine[...]
    group_size = HQ // HK
    places = back_ref.shape[0]
    branch_width = branch.shape[1] // places
    width = back_ref.shape[2] - branch_width
    for place in range(places):
        here = slice(place * branch_width, (place + 1) * branch_width)
        back_ref[place, :, width:] = branch[:, here]
    scale = HD ** (-0.5)

    def put(position, block):
        back_ref[position // width, :, position % width : position % width + HD] = block

    for group in range(HK):
        own = slice(group * HD, (group + 1) * HD)
        key, value = keys[:, own], values[:, own]
        key_grad = value_grad = 0.0
        start = group * (group_size + 2) * HD
        for member in range(group_size):
            head = group * group_size + member
            here = slice(head * HD, (head + 1) * HD)
            out_grad, query, prob = attended[:, here], queries[:, here], probs[head]
            prob_grad = dot(out_grad, value, ((1,), (1,)))
            prob_f = prob.astype(f32)
            inner = jnp.sum(prob_f * prob_grad, axis=-1, keepdims=True)
            score_grad = (prob_f * (prob_grad - inner)).astype(bf16)
            query_grad = turned(dot(score_grad, key) * scale, cosine_tab, sine_tab)
            put(start + member * HD, query_grad.astype(bf16))
            key_grad = key_grad + dot(score_grad, query, ((0,), (0,)))
            value_grad = value_grad + dot(prob, out_grad, ((0,), (0,)))
        key_grad = turned(key_grad * scale, cosine_tab, sine_tab)
        put(start + group_size * HD, key_grad.astype(bf16))
        put(start + (group_size + 1) * HD, value_grad.astype(bf16))


def first_back_kernel(at, back, weight, tokens, gain, resid_grad, tokens_ref, gain_ref):
    f32 = jnp.float32
    parts = back.shape[0]
    cols = weight.shape[0] * weight.shape[2] // parts
    first_grad = 0.0
    for part in range(parts):
        group, place = divmod(part * cols, weight.shape[2])
        first_grad = first_grad + dot(
            back[part, :, :cols], weight[group, :, place : place + cols], ((1,), (1,))
        )
    norm_grad, gain_grad = rms_back(tokens[...].astype(f32), gain[...], first_grad)
    gain_ref[...] = gain_grad
    tokens_ref[...] = (resid_grad[...] + norm_grad).astype(jnp.bfloat16)


def dense_grad_kernel(at, back, *refs):
    pieces, out_ref, held, sems = refs[:8], refs[8], refs[9], refs[10]
    copies = [
        pltpu.make_async_copy(piece, held.at[n], sems.at[n]) for n, piece in enumerate(pieces)
    ]
    for copy in copies:
        copy.start()
    depth, rows, cols = out_ref.shape
    length = held.shape[1] // 2
    qkv_width = cols - held.shape[2] // back.shape[0]
    narrow = sum(back[place, length:].astype(jnp.float32) for place in range(back.shape[0]))
    sums = [0.0, 0.0]
    for n, copy in enumerate(copies):
        copy.wait()
        dc, dy, dx = n // 4, n // 2 % 2, n % 2
        place = 4 * (at[0] ^ dy) + 2 * (at[1] ^ dc) + (at[2] ^ dx)
        own = back[place, :length]
        sums[0] = sums[0] + dot(held[n, length:], own[:, :qkv_width], ((0,), (0,)))
        sums[1] = sums[1] + dot(held[n, :length], own[:, qkv_width:], ((0,), (0,)))
    wide = held.shape[2] // depth
    each = narrow.shape[0] // depth
    for z in range(depth):
        here = slice(z * wide, (z + 1) * wide)
        both = jnp.concatenate([part[here] for part in sums], axis=1)
        out_ref[z, :wide] = both.astype(jnp.bfloat16)
        kept = [narrow[z * each : (z + 1) * each], jnp.zeros((rows - wide - each, cols), jnp.float32)]
        out_ref[z, wide:] = jnp.concatenate(kept, axis=0).astype(jnp.bfloat16)


def local_pairs(
    tokens,
    norm1_gain,
    w_query,
    w_key,
    w_value,
    w_out,
    norm2_gain,
    w_router,
    w_gate,
    w_up,
    w_down,
    expert_ids,
    prefix_len,
    out_grad,
):
    bf16, f32 = jnp.bfloat16, jnp.float32
    length, model_width = tokens.shape
    shard_rows = w_query.shape[0]
    local_count, _, hidden_width = w_gate.shape
    owners = lax.axis_size("x")
    depth = lax.axis_size("z")
    plane = lax.axis_size(PLANE)
    experts_all = w_router.shape[1]
    block_rows = length // MICRO
    capacity = 3 * block_rows * expert_ids.shape[1] // (2 * experts_all)
    plane_rows = plane * length
    blocks = plane_rows // block_rows
    q_cols, kv_cols = w_query.shape[1], w_key.shape[1]
    qkv_cols = q_cols + 2 * kv_cols
    q_group, out_half = q_cols // HK, model_width // 2
    y, c, x, z = (lax.axis_index(axis) for axis in ("y", "c", "x", "z"))
    own_local = 2 * y + c
    own_expert = x * local_count + own_local
    at = jnp.stack([y, c, x, z, prefix_len[0], own_expert, own_local])

    own_half = jnp.concatenate(
        [
            lax.dynamic_slice_in_dim(part, x * (part.shape[1] // 2), part.shape[1] // 2, 1)
            for part in (w_query, w_key, w_value, w_out)
        ],
        axis=1,
    )
    narrow = jnp.concatenate([w_router, norm1_gain[:, None], norm2_gain[:, None]], axis=1)
    narrow = small_group_gather(narrow)
    ids_all = small_gather(expert_ids)
    column = [own_half] + shifts(own_half)
    cot_sides = plane_sides(out_grad)
    cot_corner = plane_corner(cot_sides)
    gate_w, up_w, down_w = (
        lax.dynamic_index_in_dim(weight, own_local, 0, keepdims=False)
        for weight in (w_gate, w_up, w_down)
    )
    qkv_half = qkv_cols // 2
    qkv_column = jnp.stack([part[:, :qkv_half] for part in column])
    out_column = jnp.stack([part[:, qkv_half:] for part in column])
    qkv_column, out_column, narrow, ids_all, cot_corner, gate_w, up_w, down_w = (
        lax.optimization_barrier(
            (qkv_column, out_column, narrow, ids_all, cot_corner, gate_w, up_w, down_w)
        )
    )
    qkv_sides = plane_sides(qkv_column)
    qkv_corner = plane_corner(qkv_sides)
    out_sides = plane_sides(after(out_column, qkv_corner))
    qkv_pieces = plane_pieces(qkv_column, qkv_sides, qkv_corner)
    cot_pieces = plane_pieces(out_grad, cot_sides, cot_corner)
    router_w = jnp.pad(narrow[:, :experts_all], ((0, 0), (0, 128 - experts_all)))
    gains = narrow[:, experts_all : experts_all + 2].T.astype(f32)
    gain_one, gain_two = gains[:1], gains[1:]

    expert_range = jnp.arange(128, dtype=jnp.int32)
    chosen_mask = jnp.any(ids_all[:, :, None] == expert_range[None, None, :], axis=1)
    bias = jnp.where(chosen_mask, 0.0, -1e30).astype(f32)
    own_mask = jnp.any(ids_all == own_expert, axis=1).reshape(blocks, block_rows)
    place = jnp.cumsum(own_mask.astype(jnp.int32), axis=1) - 1
    slots = jnp.where(own_mask, place, -1)
    gain_one, bias, slots, router_w = lax.optimization_barrier((gain_one, bias, slots, router_w))

    cosine_tab, sine_tab = angles(length, HD)
    cosine_all = jnp.concatenate([cosine_tab, cosine_tab], axis=2)[:, 0]
    sine_all = jnp.concatenate([-sine_tab, sine_tab], axis=2)[:, 0]
    weight_lead = (2, depth, 2, 2, shard_rows)
    first_in, queries, keys_rot, values_b, probs, attended, qkv_w = run_kernel(
        attend_kernel,
        11,
        at,
        (tokens, gain_one, cosine_all, sine_all, *qkv_pieces),
        [
            ((length, model_width), bf16),
            ((length, q_cols), bf16),
            ((length, kv_cols), bf16),
            ((length, kv_cols), bf16),
            ((HQ, length, length), bf16),
            ((length, q_cols), bf16),
            (weight_lead + (qkv_half,), bf16),
        ],
    )
    out_sides = lax.optimization_barrier((*out_sides, attended))[:2]
    out_corner = plane_corner(out_sides)
    out_pieces = plane_pieces(out_column, out_sides, out_corner)
    resid, second_in, output_w = run_kernel(
        project_kernel,
        4,
        at,
        (tokens, gain_two, attended, *out_pieces),
        [
            ((length, model_width), f32),
            ((length, model_width), bf16),
            (weight_lead + (out_half,), bf16),
        ],
    )
    qkv_w = qkv_w.reshape(HK, model_width, qkv_half)
    output_w = output_w.reshape(2, q_cols, out_half)

    expert = functools.partial(
        run_expert,
        at=at,
        slots=slots,
        bias=bias,
        router=router_w,
        weights=(gate_w, up_w, down_w),
        capacity=capacity,
    )
    second_sides = plane_sides(second_in)
    groups = ((0, 4), (1, 5, 2, 6), (3, 7))
    second_pieces = {0: second_in, 4: swap(second_in, "c")}

    def run_group(pieces):
        return expert(
            pieces,
            second=[second_pieces[piece] for piece in pieces],
            cot=[cot_pieces[piece] for piece in pieces],
        )

    stage_own = run_group(groups[0])
    second_sides = lax.optimization_barrier((*second_sides, stage_own[0]))[:2]
    second_corner = plane_corner(second_sides)
    for piece, block in zip((1, 2), second_sides):
        second_pieces[piece], second_pieces[piece + 4] = block, swap(block, "c")
    stage_sides = run_group(groups[1])
    second_corner = after(second_corner, stage_sides[0])
    second_pieces[3], second_pieces[7] = second_corner, swap(second_corner, "c")
    own_near, own_far = stage_own[6:]
    own_far = swap(own_far, "c")
    x_near, x_far, y_near, y_far = stage_sides[6:]
    back_x, back_y = over_core(x_near, x_far), over_core(y_near, y_far)
    first_x, first_y = early_sums(back_x, back_y)
    stage_corner = run_group(groups[2])
    corner = over_core(*stage_corner[6:])
    passed = corner_first(corner)
    stages = (stage_own, stage_sides, stage_corner)
    rows_in, rows_cot, gated, gate_back, up_back = ([stage[n] for stage in stages] for n in range(5))
    gates = stage_own[5]
    (down_part,) = row_sums(at, [after(rows_cot[0], corner)] + rows_cot[1:], gated)
    down_sum = scatter_sum(down_part, "z")
    passed = lax.optimization_barrier((*passed, down_part))[:2]
    last_y, last_x, sent = corner_last(back_x, back_y, passed)
    gate_part, up_part = row_sums(
        at, [after(rows_in[0], sent)] + rows_in[1:], gate_back, up_back
    )
    gate_sum = scatter_sum(after(gate_part, down_sum), "z")
    up_sum = scatter_sum(after(up_part, gate_sum), "z")
    own_near = after(own_near, gate_part)

    resid_grad, branch_grad, attended_grad, router_acc, gain_two_grad = run_kernel(
        branch_back_kernel,
        6,
        at,
        (
            own_near,
            own_far,
            first_x,
            first_y,
            last_y,
            last_x,
            resid,
            gain_two,
            second_in,
            gates,
            router_w,
            out_grad,
            output_w,
        ),
        [
            ((length, model_width), f32),
            ((length, model_width), bf16),
            ((length, q_cols), bf16),
            ((model_width, 128), f32),
            ((1, model_width), f32),
        ],
    )
    qkv_width, branch_width = qkv_cols // plane, model_width // plane
    dense_cols = qkv_width + branch_width
    (back_cols,) = run_kernel(
        attend_back_kernel,
        6,
        at,
        (
            attended_grad,
            probs,
            queries,
            keys_rot,
            values_b,
            cosine_all,
            sine_all,
            branch_grad,
        ),
        [((plane, length, dense_cols), bf16)],
    )
    tokens_grad, gain_one_grad = run_kernel(
        first_back_kernel,
        5,
        at,
        (back_cols, qkv_w, tokens, gain_one, resid_grad),
        [((length, model_width), bf16), ((1, model_width), f32)],
        24,
    )

    both = jnp.concatenate(
        lax.optimization_barrier((attended, first_in, resid_grad))[:2], axis=0
    )
    both_pieces = plane_pieces(both)
    narrow_part = jnp.concatenate(
        [router_acc[:, :experts_all], gain_one_grad.T, gain_two_grad.T], axis=1
    )
    narrow_cols = -(-narrow_part.shape[1] // owners) * owners
    narrow_part = jnp.pad(narrow_part, ((0, 0), (0, narrow_cols - narrow_part.shape[1])))
    narrow_part = jnp.transpose(
        narrow_part.reshape(depth, 2, 2, shard_rows, owners, narrow_cols // owners),
        (1, 2, 4, 0, 3, 5),
    ).reshape(plane, depth, shard_rows * narrow_cols // owners)
    narrow_len = narrow_part.shape[2]
    narrow_rows = -(-narrow_len // dense_cols)
    each_rows = -(-narrow_rows // 4) * 4
    narrow_part = jnp.pad(
        narrow_part, ((0, 0), (0, 0), (0, each_rows * dense_cols - narrow_len))
    ).reshape(plane, depth * each_rows, dense_cols)
    back_cols = exchange(jnp.concatenate([back_cols, narrow_part.astype(bf16)], axis=1), PLANE)
    kept_rows = -(-narrow_rows // 16) * 16
    wide_rows = local_count * shard_rows
    dense_shape = (depth, wide_rows + kept_rows, dense_cols)
    anywhere = pl.BlockSpec(memory_space=pl.ANY)
    dense_part = pl.pallas_call(
        dense_grad_kernel,
        out_shape=jax.ShapeDtypeStruct(dense_shape, bf16),
        in_specs=[SCALARS, WHOLE] + [anywhere] * 8,
        out_specs=WHOLE,
        scratch_shapes=[
            pltpu.VMEM((plane, 2 * length, model_width), bf16),
            pltpu.SemaphoreType.DMA((plane,)),
        ],
        cost_estimate=cost(8),
        compiler_params=pltpu.CompilerParams(vmem_limit_bytes=32 * 2**20),
    )(at, back_cols, *both_pieces)
    dense_part = after(dense_part, up_sum)
    dense_sum = scatter_sum(dense_part.reshape(-1, dense_cols), "z")
    wide_sum = dense_sum[: local_count * shard_rows].reshape(2, 2, 1, shard_rows, dense_cols)
    wide_sum = jnp.broadcast_to(wide_sum, (2, 2, owners, shard_rows, dense_cols)).reshape(
        plane, shard_rows, dense_cols
    )
    narrow_sum = dense_sum[local_count * shard_rows :][:narrow_rows]
    narrow_sum = jnp.broadcast_to(narrow_sum[None], (plane, narrow_rows, dense_cols))
    pad_rows = -(shard_rows + narrow_rows) % 16
    padding = jnp.zeros((plane, pad_rows, dense_cols), bf16)
    dense_sum = exchange(jnp.concatenate([wide_sum, narrow_sum, padding], axis=1), PLANE)
    wide_sum = jnp.moveaxis(dense_sum[:, :shard_rows].astype(f32), 0, 1)
    qkv_sum = wide_sum[:, :, :qkv_width].reshape(shard_rows, HK, qkv_half)
    output_sum = wide_sum[:, :, qkv_width:].reshape(shard_rows, model_width)
    narrow_sum = dense_sum[:, shard_rows : shard_rows + narrow_rows].reshape(
        2, 2, owners, narrow_rows * dense_cols
    )
    narrow_sum = narrow_sum[y, c, :, :narrow_len].reshape(owners, shard_rows, -1)
    narrow_sum = jnp.moveaxis(narrow_sum, 0, 1).reshape(shard_rows, narrow_cols).astype(f32)

    shares = run_kernel(
        functools.partial(mixture_kernel, capacity, groups),
        10,
        at,
        (slots, down_w, after(gated[0], both_pieces[3]), *gated[1:]),
        [((length, model_width), bf16)] * plane,
        24,
    )
    mixed = [over_core(near, far) for near, far in zip(shares[:4], shares[4:])]
    early = early_sums(mixed[1], mixed[2])
    last = corner_last(mixed[1], mixed[2], corner_first(mixed[3]))[:2]
    mixture = jnp.concatenate(
        [left.astype(f32) + right.astype(f32) for left, right in zip(early, last)], axis=0
    )
    block_out = (resid + (mixture + mixed[0].astype(f32))).astype(bf16)

    def placed(total):
        total = exchange(total, ("y", "c"))
        return total.reshape(local_count, shard_rows, hidden_width).astype(f32)

    return (
        block_out,
        tokens_grad,
        narrow_sum[:, experts_all],
        qkv_sum[:, :, :q_group].reshape(shard_rows, q_cols),
        qkv_sum[:, :, q_group : q_group + HD].reshape(shard_rows, kv_cols),
        qkv_sum[:, :, q_group + HD :].reshape(shard_rows, kv_cols),
        output_sum,
        narrow_sum[:, experts_all + 1],
        narrow_sum[:, :experts_all],
        placed(gate_sum),
        placed(up_sum),
        jnp.swapaxes(placed(down_sum), 1, 2),
    )


def solution(mesh):
    groups, owners = mesh.shape["dp"], mesh.shape["expert"]
    grid = jax.sharding.Mesh(
        mesh.devices.reshape(groups // 4, 2, 2, owners), ("z", "y", "c", "x")
    )
    rows = P(("z", "y", "c", "x"), None)
    shard, shard_rows = P(GROUP), P(GROUP, None)
    expert = P("x", None, None)
    return jax.shard_map(
        local_pairs if owners == 2 else local_wide,
        mesh=grid,
        in_specs=(
            rows,
            shard,
            shard_rows,
            shard_rows,
            shard_rows,
            shard_rows,
            shard,
            shard_rows,
            expert,
            expert,
            expert,
            rows,
            P(("z", "y", "c", "x")),
            rows,
        ),
        out_specs=(
            rows,
            rows,
            shard,
            shard_rows,
            shard_rows,
            shard_rows,
            shard_rows,
            shard,
            shard_rows,
            P("x", GROUP, None),
            P("x", GROUP, None),
            P("x", None, GROUP),
        ),
        check_vma=False,
    )
```

```python
import functools
import math

import jax
import jax.numpy as jnp
from jax import lax
from jax.experimental import pallas as pl
from jax.experimental.pallas import tpu as pltpu
from jax.sharding import PartitionSpec as P

HQ = 12
HK = 2
HD = 128
MICRO = 2
PLANE = ("y", "c", "x")
GROUP = ("z", "y", "c")


def rms_scale(values, gain_vec):
    inverse = lax.rsqrt(jnp.mean(values * values, axis=-1, keepdims=True) + 1e-06)
    return values * inverse * gain_vec


def angles(length, head_size):
    positions = jnp.arange(length).astype(jnp.float32)
    freq_rates = jnp.exp(
        -(2.0 * jnp.arange(head_size // 2).astype(jnp.float32) / head_size) * math.log(1000000.0)
    )
    angle_tab = positions[:, None] * freq_rates[None, :]
    return (jnp.cos(angle_tab)[:, None, :], jnp.sin(angle_tab)[:, None, :])


def rotary(values, cosine_tab, sine_tab):
    half_dim = values.shape[-1] // 2
    first_half = values[..., :half_dim]
    second_half = values[..., half_dim:]
    return jnp.concatenate(
        [
            first_half * cosine_tab - second_half * sine_tab,
            second_half * cosine_tab + first_half * sine_tab,
        ],
        axis=-1,
    )


def expert_act(gate_pre, up_pre):
    return jax.nn.gelu(gate_pre, approximate=True) * up_pre


def left_product(left_mat, right_mat):
    return lax.dot_general(
        left_mat, right_mat, (((0,), (0,)), ((), ())), preferred_element_type=jnp.float32
    )


def gather(block, axes):
    return lax.all_gather(block, axes, axis=0, tiled=True)


def exchange(block, axes):
    return lax.all_to_all(block, axes, split_axis=0, concat_axis=0, tiled=True)


def scatter_sum(block, axes):
    return lax.psum_scatter(block, axes, scatter_dimension=0, tiled=True)


def by_owner(cols, parts):
    rows, total = cols.shape
    return jnp.moveaxis(cols.reshape(rows, parts, total // parts), 1, 0).reshape(
        parts * rows, total // parts
    )


def local_wide(
    tokens,
    norm1_gain,
    w_query,
    w_key,
    w_value,
    w_out,
    norm2_gain,
    w_router,
    w_gate,
    w_up,
    w_down,
    expert_ids,
    prefix_len,
    out_grad,
):
    bf16, f32 = jnp.bfloat16, jnp.float32
    length, model_width = tokens.shape
    shard_rows = w_query.shape[0]
    local_count, _, hidden_width = w_gate.shape
    owners = lax.axis_size("x")
    depth = lax.axis_size("z")
    plane = lax.axis_size(PLANE)
    experts_all = w_router.shape[1]
    top_count = expert_ids.shape[1]
    block_rows = length // MICRO
    capacity = 3 * block_rows * top_count // (2 * experts_all)
    plane_rows = plane * length
    blocks = plane_rows // block_rows
    group_size = HQ // HK
    score_scale = HD ** (-0.5)
    q_cols, kv_cols = w_query.shape[1], w_key.shape[1]
    own_local = lax.axis_index(("y", "c"))
    own_expert = lax.axis_index("x") * local_count + own_local
    own_place = lax.axis_index(PLANE)

    narrow = jnp.concatenate([w_router, norm1_gain[:, None], norm2_gain[:, None]], axis=1)
    narrow = jnp.pad(narrow, ((0, 0), (0, -narrow.shape[1] % 128)))
    packed = gather(jnp.concatenate([w_query, w_key, w_value, narrow], axis=1), GROUP)
    qkv_cols = q_cols + 2 * kv_cols
    qkv_w = packed[:, :qkv_cols]
    router_w = packed[:, qkv_cols : qkv_cols + experts_all]
    gains = packed[:, qkv_cols + experts_all : qkv_cols + experts_all + 2].T.astype(f32)
    gain_one, gain_two = gains[0], gains[1]
    output_w = gather(w_out, GROUP)

    ids_all = gather(expert_ids, PLANE)
    cot_all = gather(out_grad, PLANE)
    chosen_mask = jnp.any(
        ids_all[:, :, None] == jnp.arange(experts_all, dtype=jnp.int32)[None, None, :], axis=1
    )
    own_mask = jnp.any(ids_all == own_expert, axis=1).reshape(blocks, block_rows)
    place = jnp.cumsum(own_mask.astype(jnp.int32), axis=1) - 1
    dispatch = (
        own_mask[:, None, :]
        & (place[:, None, :] == jnp.arange(capacity, dtype=jnp.int32)[None, :, None])
    ).astype(bf16)

    cosine_tab, sine_tab = angles(length, HD)
    inputs_f = tokens.astype(f32)
    first_in = rms_scale(inputs_f, gain_one).astype(bf16)
    qkv = jnp.dot(first_in, qkv_w, preferred_element_type=f32)
    queries = (
        rotary(qkv[:, :q_cols].reshape(length, HQ, HD), cosine_tab, sine_tab)
        .astype(bf16)
        .reshape(length, HK, group_size, HD)
    )
    keys_rot = rotary(
        qkv[:, q_cols : q_cols + kv_cols].reshape(length, HK, HD), cosine_tab, sine_tab
    ).astype(bf16)
    values_b = qkv[:, q_cols + kv_cols :].astype(bf16).reshape(length, HK, HD)
    positions = jnp.arange(length)
    allowed = (positions[None, :] <= positions[:, None]) | (positions[None, :] < prefix_len[0])

    def masked_scores():
        scores = jnp.einsum("ihrd,jhd->hrij", queries, keys_rot, preferred_element_type=f32)
        return jnp.where(allowed, scores * score_scale, -1e30)

    masked = masked_scores()
    row_peak = jnp.max(masked, axis=-1, keepdims=True)
    log_total = row_peak + jnp.log(jnp.sum(jnp.exp(masked - row_peak), axis=-1, keepdims=True))
    prob_bf = jnp.exp(masked - log_total).astype(bf16)
    attended = jnp.einsum("hrij,jhd->ihrd", prob_bf, values_b, preferred_element_type=f32)
    attended = attended.reshape(length, HQ * HD).astype(bf16)
    resid = inputs_f + jnp.dot(attended, output_w, preferred_element_type=f32)
    second_in = rms_scale(resid, gain_two).astype(bf16)

    second_all = gather(second_in, PLANE)
    logits = jnp.dot(second_all, router_w, preferred_element_type=f32)
    gates_all = jax.nn.softmax(jnp.where(chosen_mask, logits, -jnp.inf), axis=-1)
    own_gates = lax.dynamic_index_in_dim(gates_all, own_expert, 1, keepdims=False)
    own_gates = own_gates.reshape(blocks, block_rows)
    gate_rows = jnp.einsum(
        "bct,bt->bc", dispatch.astype(f32), own_gates, precision=lax.Precision.HIGHEST
    )[:, :, None]
    gate_w = lax.dynamic_index_in_dim(w_gate, own_local, 0, keepdims=False)
    up_w = lax.dynamic_index_in_dim(w_up, own_local, 0, keepdims=False)
    down_w = lax.dynamic_index_in_dim(w_down, own_local, 0, keepdims=False)

    def to_rows(array):
        return jnp.einsum(
            "bct,btd->bcd",
            dispatch,
            array.reshape(blocks, block_rows, model_width),
            preferred_element_type=f32,
        ).astype(bf16)

    def to_tokens(rows):
        return (
            jnp.einsum("bct,bcd->btd", dispatch, rows.astype(bf16), preferred_element_type=f32)
            .astype(bf16)
            .reshape(plane_rows, model_width)
        )

    rows_in = to_rows(second_all)
    rows_cot = to_rows(cot_all)
    gate_pre = jnp.einsum("bcd,df->bcf", rows_in, gate_w, preferred_element_type=f32)
    up_pre = jnp.einsum("bcd,df->bcf", rows_in, up_w, preferred_element_type=f32)
    hidden, act_pull = jax.vjp(expert_act, gate_pre, up_pre)
    gated = (gate_rows * hidden).astype(bf16)
    down_part = jnp.einsum("bcd,bcf->df", rows_cot, gated, preferred_element_type=f32)
    down_sum = scatter_sum(down_part.astype(bf16), "z")
    cot_hidden = jnp.einsum("bcd,fd->bcf", rows_cot, down_w, preferred_element_type=f32)
    gate_signal_rows = jnp.sum(hidden * cot_hidden, axis=-1)
    gate_pgrad, up_pgrad = act_pull(gate_rows * cot_hidden)
    gate_pgrad = gate_pgrad.astype(bf16)
    up_pgrad = up_pgrad.astype(bf16)
    gate_part = jnp.einsum("bcd,bcf->df", rows_in, gate_pgrad, preferred_element_type=f32)
    gate_sum = scatter_sum(gate_part.astype(bf16), "z")
    up_part = jnp.einsum("bcd,bcf->df", rows_in, up_pgrad, preferred_element_type=f32)
    up_sum = scatter_sum(up_part.astype(bf16), "z")
    rows_grad = jnp.einsum("bcf,df->bcd", gate_pgrad, gate_w, preferred_element_type=f32)
    rows_grad = rows_grad + jnp.einsum("bcf,df->bcd", up_pgrad, up_w, preferred_element_type=f32)
    second_back = scatter_sum(to_tokens(rows_grad), PLANE).astype(f32)
    gate_signal = jnp.einsum(
        "bct,bc->bt", dispatch.astype(f32), gate_signal_rows, precision=lax.Precision.HIGHEST
    )
    gate_signal = exchange(gate_signal.reshape(plane, length), PLANE)
    gate_signal = jnp.transpose(
        gate_signal.reshape(local_count, owners, length), (2, 1, 0)
    ).reshape(length, experts_all)
    expert_rows = jnp.einsum("bcf,fd->bcd", gated, down_w, preferred_element_type=f32)
    mixture = scatter_sum(to_tokens(expert_rows), PLANE).astype(f32)
    block_out = (resid + mixture).astype(bf16)

    cotangent = out_grad.astype(f32)
    gate_probs = lax.dynamic_slice_in_dim(gates_all, own_place * length, length, 0)
    logit_grad = (
        gate_probs
        * (gate_signal - jnp.sum(gate_probs * gate_signal, axis=-1, keepdims=True))
    ).astype(bf16)
    router_acc = left_product(second_in, logit_grad)
    second_grad = second_back + jnp.dot(logit_grad, router_w.T, preferred_element_type=f32)
    _, norm_two_pull = jax.vjp(rms_scale, resid, gain_two)
    resid_norm_grad, gain_two_grad = norm_two_pull(second_grad)
    resid_grad = cotangent + resid_norm_grad
    branch_grad = resid_grad.astype(bf16)

    attended_all = gather(attended, PLANE)
    branch_cols = exchange(by_owner(branch_grad, plane), PLANE)
    output_part = left_product(attended_all, branch_cols)
    attended_grad = jnp.dot(branch_grad, output_w.T, preferred_element_type=f32).astype(bf16)
    attended_grad = attended_grad.reshape(length, HK, group_size, HD)
    masked = masked_scores()
    prob_full = jnp.exp(masked - log_total)
    prob_bf = prob_full.astype(bf16)
    prob_grad = jnp.einsum("ihrd,jhd->hrij", attended_grad, values_b, preferred_element_type=f32)
    row_inner = jnp.sum(prob_full * prob_grad, axis=-1, keepdims=True)
    score_grad = (prob_full * (prob_grad - row_inner)).astype(bf16)
    query_rot_grad = (
        jnp.einsum("hrij,jhd->ihrd", score_grad, keys_rot, preferred_element_type=f32)
        * score_scale
    )
    query_back = rotary(query_rot_grad.reshape(length, HQ, HD), cosine_tab, -sine_tab)
    query_back = query_back.astype(bf16).reshape(length, HQ * HD)
    key_rot_grad = (
        jnp.einsum("hrij,ihrd->jhd", score_grad, queries, preferred_element_type=f32)
        * score_scale
    )
    key_back = rotary(key_rot_grad, cosine_tab, -sine_tab).astype(bf16).reshape(length, HK * HD)
    value_back = jnp.einsum("hrij,ihrd->jhd", prob_bf, attended_grad, preferred_element_type=f32)
    value_back = value_back.astype(bf16).reshape(length, HK * HD)
    qkv_back = jnp.concatenate([query_back, key_back, value_back], axis=1)
    first_all = gather(first_in, PLANE)
    qkv_part = left_product(first_all, exchange(by_owner(qkv_back, plane), PLANE))
    first_grad = lax.dot_general(
        qkv_back, qkv_w, (((1,), (1,)), ((), ())), preferred_element_type=f32
    )
    _, norm_one_pull = jax.vjp(rms_scale, inputs_f, gain_one)
    input_norm_grad, gain_one_grad = norm_one_pull(first_grad)
    tokens_grad = (resid_grad + input_norm_grad).astype(bf16)

    narrow_part = jnp.concatenate(
        [router_acc, gain_one_grad[:, None], gain_two_grad[:, None]], axis=1
    ).astype(bf16)
    narrow_cols = narrow_part.shape[1]
    narrow_sum = lax.psum(scatter_sum(narrow_part, GROUP), "x").astype(f32)
    dense_part = jnp.concatenate([qkv_part, output_part], axis=1).astype(bf16)
    dense_sum = scatter_sum(dense_part, "z")
    dense_cols = dense_sum.shape[1]
    dense_sum = gather(dense_sum, PLANE).reshape(plane, local_count, shard_rows, dense_cols)
    dense_sum = lax.dynamic_index_in_dim(dense_sum, own_local, 1, keepdims=False).astype(f32)
    dense_sum = jnp.moveaxis(dense_sum, 0, 1)
    qkv_width = qkv_cols // plane
    qkv_sum = dense_sum[:, :, :qkv_width].reshape(shard_rows, qkv_cols)
    output_sum = dense_sum[:, :, qkv_width:].reshape(shard_rows, model_width)

    def placed(total):
        total = exchange(total, ("y", "c"))
        return total.reshape(local_count, shard_rows, hidden_width).astype(f32)

    return (
        block_out,
        tokens_grad,
        narrow_sum[:, experts_all],
        qkv_sum[:, :q_cols],
        qkv_sum[:, q_cols : q_cols + kv_cols],
        qkv_sum[:, q_cols + kv_cols :],
        output_sum,
        narrow_sum[:, experts_all + 1],
        narrow_sum[:, :experts_all],
        placed(gate_sum),
        placed(up_sum),
        jnp.swapaxes(placed(down_sum), 1, 2),
    )


def rounded(values):
    return lax.reduce_precision(values, 8, 7).astype(jnp.bfloat16)


def after(block, *others):
    return lax.optimization_barrier((block,) + others)[0]


def swap(block, axis):
    return lax.ppermute(block, axis, [(0, 1), (1, 0)])


def shifts(block):
    depth = lax.axis_size("z")
    return [
        lax.ppermute(block, "z", [(i, (i + k) % depth) for i in range(depth)])
        for k in range(1, depth)
    ]


def plane_sides(block):
    return swap(block, "x"), swap(block, "y")


def plane_corner(sides, before=()):
    over_x, over_y = sides
    half = over_x.shape[0] // 2
    over_y, over_x = lax.optimization_barrier((over_y[:half], over_x[half:]) + before)[:2]
    return jnp.concatenate([swap(over_y, "x"), swap(over_x, "y")], axis=0)


def plane_pieces(block, sides=None, corner=None):
    sides = plane_sides(block) if sides is None else sides
    corner = plane_corner(sides) if corner is None else corner
    pieces = [block, *sides, corner]
    return pieces + [swap(piece, "c") for piece in pieces]


def small_gather(block):
    for axis in ("x", "y", "c"):
        block = jnp.concatenate([block, swap(block, axis)], axis=0)
    return block


def small_group_gather(block):
    depth = lax.axis_size("z")
    order = jnp.stack(([block] + shifts(block))[::-1] * 2)
    start = (depth - 1 - lax.axis_index("z")) % depth
    total = lax.dynamic_slice_in_dim(order, start, depth, 0)[:, None, None]
    for dim, axis in ((1, "y"), (2, "c")):
        other = swap(total, axis)
        last = lax.axis_index(axis) == 1
        pair = [jnp.where(last, other, total), jnp.where(last, total, other)]
        total = jnp.concatenate(pair, axis=dim)
    return total.reshape(-1, block.shape[1])


def add(left, right):
    return rounded(left.astype(jnp.float32) + right.astype(jnp.float32))


def over_core(near, far):
    return add(near, swap(far, "c"))


def early_sums(over_x, over_y):
    half = over_x.shape[0] // 2
    return swap(over_x[:half], "x"), swap(over_y[half:], "y")


def corner_first(corner):
    half = corner.shape[0] // 2
    return swap(corner[:half], "x"), swap(corner[half:], "y")


def corner_last(over_x, over_y, first):
    half = over_x.shape[0] // 2
    over_y, over_x = add(over_y[:half], first[0]), add(over_x[half:], first[1])
    return swap(over_y, "y"), swap(over_x, "x"), over_x


def cost(micros):
    return pl.CostEstimate(flops=micros * 10**9, bytes_accessed=micros * 10**6, transcendentals=0)


def dot(left, right, dims=((1,), (0,)), precision=None):
    return lax.dot_general(
        left, right, (dims, ((), ())), precision=precision, preferred_element_type=jnp.float32
    )


WHOLE = pl.BlockSpec(memory_space=pltpu.VMEM)
IN_HBM = pl.BlockSpec(memory_space=pltpu.HBM)
SCALARS = pl.BlockSpec(memory_space=pltpu.SMEM)


def run_kernel(kernel, micros, at, operands, outs, megabytes=16, scratch=(), hbm_in=0, hbm_out=0):
    return pl.pallas_call(
        kernel,
        out_shape=[jax.ShapeDtypeStruct(shape, dtype) for shape, dtype in outs],
        in_specs=[SCALARS] + [WHOLE] * (len(operands) - hbm_in) + [IN_HBM] * hbm_in,
        out_specs=[WHOLE] * (len(outs) - hbm_out) + [IN_HBM] * hbm_out,
        scratch_shapes=scratch,
        cost_estimate=cost(micros),
        compiler_params=pltpu.CompilerParams(vmem_limit_bytes=megabytes * 2**20),
    )(at, *operands)


def place_pieces(at, refs, weight):
    depth = weight.shape[1]
    for n, ref in enumerate(refs):
        dc, dy, dx = n // 4, n // 2 % 2, n % 2
        for k in range(depth):
            z = lax.rem(at[3] + depth - k, depth)
            weight[at[2] ^ dx, z, at[0] ^ dy, at[1] ^ dc] = ref[k]


def rms_kernel(values, gain):
    inverse = lax.rsqrt(jnp.mean(values * values, axis=-1, keepdims=True) + 1e-06)
    return (values * inverse * gain).astype(jnp.bfloat16)


def rms_back(values, gain, grad):
    inverse = lax.rsqrt(jnp.mean(values * values, axis=-1, keepdims=True) + 1e-06)
    normed = values * inverse
    gain_grad = jnp.sum(grad * normed, axis=0, keepdims=True)
    grad = grad * gain
    along = jnp.mean(grad * normed, axis=-1, keepdims=True)
    return inverse * (grad - normed * along), gain_grad


def turned(values, cosine_tab, sine_tab):
    return values * cosine_tab + pltpu.roll(values, HD // 2, 1) * sine_tab


def attend_kernel(at, tokens, gain, cosine, sine, *refs):
    first_ref, query_ref, key_ref, value_ref, out_ref = refs[8:13]
    prob_out, weight_out, prob_ref, weight, sems = refs[13:]
    place_pieces(at, refs[:8], weight)
    copies = [pltpu.make_async_copy(weight, weight_out, sems.at[HK])]
    copies[0].start()
    length = tokens.shape[0]
    first_in = rms_kernel(tokens[...].astype(jnp.float32), gain[...])
    first_ref[...] = first_in
    rows = lax.broadcasted_iota(jnp.int32, (length, length), 0)
    cols = lax.broadcasted_iota(jnp.int32, (length, length), 1)
    allowed = (cols <= rows) | (cols < at[4])
    cosine_tab, sine_tab = cosine[...], sine[...]
    group_size = HQ // HK
    for group in range(HK):
        matrix = weight[group].reshape(first_in.shape[1], -1)
        qkv = dot(first_in, matrix)
        at_key = group_size * HD
        key = turned(qkv[:, at_key : at_key + HD], cosine_tab, sine_tab).astype(jnp.bfloat16)
        value = qkv[:, at_key + HD :].astype(jnp.bfloat16)
        key_ref[:, group * HD : (group + 1) * HD] = key
        value_ref[:, group * HD : (group + 1) * HD] = value
        for member in range(group_size):
            head = group * group_size + member
            here = slice(head * HD, (head + 1) * HD)
            query = turned(qkv[:, member * HD : (member + 1) * HD], cosine_tab, sine_tab)
            query = query.astype(jnp.bfloat16)
            query_ref[:, here] = query
            scores = dot(query, key, ((1,), (1,)))
            scores = jnp.where(allowed, scores * HD ** (-0.5), -1e30)
            weights = jnp.exp(scores - jnp.max(scores, axis=-1, keepdims=True))
            prob = weights * (1.0 / jnp.sum(weights, axis=-1, keepdims=True))
            prob = prob.astype(jnp.bfloat16)
            prob_ref[head] = prob
            out_ref[:, here] = dot(prob, value).astype(jnp.bfloat16)
        here = pl.ds(group * group_size, group_size)
        copies.append(
            pltpu.make_async_copy(prob_ref.at[here], prob_out.at[here], sems.at[group])
        )
        copies[-1].start()
    for copy in copies:
        copy.wait()


def project_kernel(at, tokens, gain, attended, *refs):
    resid_ref, second_ref, weight_out, weight, sem = refs[8:]
    place_pieces(at, refs[:8], weight)
    copy = pltpu.make_async_copy(weight, weight_out, sem)
    copy.start()
    heads = attended[...]
    halves = [dot(heads, weight[half].reshape(heads.shape[1], -1)) for half in range(2)]
    resid = tokens[...].astype(jnp.float32) + jnp.concatenate(halves, axis=1)
    resid_ref[...] = resid
    second_ref[...] = rms_kernel(resid, gain[...])
    copy.wait()


def one_hot(slots, capacity, dtype):
    shape = (capacity, slots.shape[1])
    return (slots == lax.broadcasted_iota(jnp.int32, shape, 0)).astype(jnp.float32).astype(dtype)


def slots_of(ids, expert, start, rows):
    named = jnp.any(ids[:, start : start + rows] == expert, axis=0, keepdims=True)
    named = named.astype(jnp.float32)
    before = lax.broadcasted_iota(jnp.int32, (rows, rows), 0)
    upto = lax.broadcasted_iota(jnp.int32, (rows, rows), 1)
    counts = dot(named.astype(jnp.bfloat16), (before <= upto).astype(jnp.float32).astype(jnp.bfloat16))
    return jnp.where(named > 0.0, counts - 1.0, -1.0).astype(jnp.int32)


def spread(picks, capacity, rows, outs):
    rows = rows.astype(jnp.bfloat16)
    block = picks[0].shape[1]
    for n in range(len(picks) // 2):
        for part in range(2):
            pick = picks[2 * n + part]
            at_row = (2 * n + part) * capacity
            tokens = dot(pick, rows[at_row : at_row + capacity], ((0,), (0,)))
            outs[n][part * block : (part + 1) * block] = tokens.astype(jnp.bfloat16)


def expert_kernel(capacity, pieces, at, ids, ids_turned, router, *refs):
    count = len(pieces)
    second, cot = refs[:count], refs[count : 2 * count]
    sources = refs[2 * count : 2 * count + 3]
    rows_in, rows_cot, gated_ref, gate_back, up_back, gates_ref = refs[2 * count + 3 : 2 * count + 9]
    backs = refs[2 * count + 9 : -5]
    gate_w, up_w, down_w, gate_rows, sems = refs[-5:]
    copies = [
        pltpu.make_async_copy(source.at[at[6]], target, sems.at[n])
        for n, (source, target) in enumerate(zip(sources, (gate_w, up_w, down_w)))
    ]
    for copy in copies:
        copy.start()
    f32, bf16 = jnp.float32, jnp.bfloat16
    length, width = second[0].shape
    wide = router.shape[1]
    half = length // 2
    picks = []
    for n, piece in enumerate(pieces):
        tokens = second[n][...]
        experts = lax.broadcasted_iota(jnp.int32, (length, wide), 1)
        named = ids[piece * length : (piece + 1) * length]
        chosen = functools.reduce(
            jnp.logical_or, [named[:, k : k + 1] == experts for k in range(named.shape[1])]
        )
        logits = jnp.where(chosen, dot(tokens, router[...]), -1e30)
        weights = jnp.exp(logits - jnp.max(logits, axis=-1, keepdims=True))
        gates = weights * (1.0 / jnp.sum(weights, axis=-1, keepdims=True))
        if n == 0:
            gates_ref[...] = gates
        lanes = lax.broadcasted_iota(jnp.int32, (capacity, wide), 1)
        for part in range(2):
            here = slice(part * half, (part + 1) * half)
            place = slice((2 * n + part) * capacity, (2 * n + part + 1) * capacity)
            slots = slots_of(ids_turned, at[5], piece * length + part * half, half)
            pick = one_hot(slots, capacity, f32)
            picks.append(pick.astype(bf16))
            rows_in[place] = dot(picks[-1], tokens[here]).astype(bf16)
            rows_cot[place] = dot(picks[-1], cot[n][here]).astype(bf16)
            picked = dot(pick, gates[here], precision=lax.Precision.HIGHEST)
            picked = jnp.where(lanes == at[5], picked, 0.0)
            gate_rows[place] = jnp.sum(picked, axis=1, keepdims=True)
    gate = gate_rows[...]
    copies[0].wait()
    gate_pre = dot(rows_in[...], gate_w[...])
    copies[1].wait()
    up_pre = dot(rows_in[...], up_w[...])
    copies[2].wait()
    cot_hidden = dot(rows_cot[...], down_w[...], ((1,), (1,)))
    scale = math.sqrt(2.0 / math.pi)
    square = gate_pre * gate_pre
    bent = jnp.tanh(scale * gate_pre * (1.0 + 0.044715 * square))
    open_part = 0.5 * (1.0 + bent)
    active = gate_pre * open_part
    slope = open_part + 0.5 * gate_pre * (1.0 - bent * bent) * scale * (
        1.0 + 3 * 0.044715 * square
    )
    hidden = active * up_pre
    gated_ref[...] = (gate * hidden).astype(bf16)
    signal = jnp.sum(hidden * cot_hidden, axis=1, keepdims=True)
    back = gate * cot_hidden
    gate_back[...] = (back * up_pre * slope).astype(bf16)
    up_back[...] = (back * active).astype(bf16)
    high = signal.astype(bf16)
    low = (signal - high.astype(f32)).astype(bf16)
    lanes = lax.broadcasted_iota(jnp.int32, (signal.shape[0], wide), 1)
    signal = jnp.where(lanes == at[5], high.astype(f32), 0.0)
    signal = jnp.where(lanes == at[5] + wide // 2, low.astype(f32), signal)
    by_rows = ((1,), (1,))
    rows = dot(gate_back[...], gate_w[...], by_rows) + dot(up_back[...], up_w[...], by_rows)
    spread(picks, capacity, jnp.concatenate([rows, signal], axis=1), backs)


def run_expert(pieces, at, ids, ids_turned, router, weights, second, cot, capacity):
    count = len(pieces)
    rows, wide = 2 * count * capacity, router.shape[1]
    (length, width), hidden = second[0].shape, weights[0].shape[2]
    bf16, f32 = jnp.bfloat16, jnp.float32
    outs = [(rows, width)] * 2 + [(rows, hidden)] * 3
    outs = [(shape, bf16) for shape in outs] + [((length, wide), f32)]
    outs = outs + [((length, width + wide), bf16)] * count
    return run_kernel(
        functools.partial(expert_kernel, capacity, pieces),
        4 * count,
        at,
        (ids, ids_turned, router, *second, *cot, *weights),
        outs,
        15 + 6 * count,
        [pltpu.VMEM(weight.shape[1:], bf16) for weight in weights]
        + [pltpu.VMEM((rows, 1), f32), pltpu.SemaphoreType.DMA((3,))],
        hbm_in=3,
    )


def mixture_kernel(capacity, groups, at, ids_turned, *refs):
    gated, source, down_w, sem = refs[: len(groups)], refs[len(groups)], refs[-2], refs[-1]
    outs = refs[len(groups) + 1 : -2]
    copy = pltpu.make_async_copy(source.at[at[6]], down_w, sem)
    copy.start()
    copy.wait()
    length = outs[0].shape[0]
    for pieces, rows in zip(groups, gated):
        picks = []
        for piece in pieces:
            for part in range(2):
                start = piece * length + part * length // 2
                slots = slots_of(ids_turned, at[5], start, length // 2)
                picks.append(one_hot(slots, capacity, jnp.bfloat16))
        spread(picks, capacity, dot(rows[...], down_w[...]), [outs[piece] for piece in pieces])


def row_sum_kernel(parts, at, *refs):
    arrays = [
        jnp.concatenate([ref[...] for ref in refs[n : n + parts]], axis=0)
        for n in range(0, len(refs) - 1, parts)
    ]
    out = refs[-1]
    rows = out.shape[2]
    for n, right in enumerate(arrays[1:]):
        total = dot(arrays[0], right, ((0,), (0,))).astype(jnp.bfloat16)
        for owner in range(out.shape[0]):
            out[owner, n] = total[owner * rows : (owner + 1) * rows]


def row_sums(at, shard_rows, left, *rights):
    operands = [part for parts in (left, *rights) for part in parts]
    rows, cols = left[0].shape[1], rights[0][0].shape[1]
    shape = (rows // shard_rows, len(rights), shard_rows, cols)
    kernel = functools.partial(row_sum_kernel, len(left))
    (total,) = run_kernel(kernel, 4 * len(rights), at, operands, [(shape, jnp.bfloat16)], 24)
    return total


def branch_back_kernel(
    at, near, far, first_x, first_y, last_y, last_x, resid, gain, second, gates, router, cot, weight, *outs
):
    resid_grad_ref, branch_ref, attended_ref, router_ref, gain_ref = outs
    f32, bf16 = jnp.float32, jnp.bfloat16
    halves = [first_x[...].astype(f32) + last_y[...], first_y[...].astype(f32) + last_x[...]]
    total = near[...].astype(f32) + far[...] + jnp.concatenate(halves, axis=0)
    width = resid.shape[1]
    signal = total[:, width:]
    signal = signal + pltpu.roll(signal, signal.shape[1] // 2, 1)
    chosen = gates[...]
    logit_grad = chosen * (signal - jnp.sum(chosen * signal, axis=-1, keepdims=True))
    logit_grad = logit_grad.astype(bf16)
    second_grad = total[:, :width] + dot(logit_grad, router[...], ((1,), (1,)))
    norm_grad, gain_grad = rms_back(resid[...], gain[...], second_grad)
    gain_ref[...] = gain_grad
    resid_grad = cot[...].astype(f32) + norm_grad
    resid_grad_ref[...] = resid_grad
    branch = resid_grad.astype(bf16)
    branch_ref[...] = branch
    wide = weight.shape[2]
    attended_ref[...] = (
        dot(branch[:, :wide], weight[0], ((1,), (1,)))
        + dot(branch[:, wide:], weight[1], ((1,), (1,)))
    ).astype(bf16)
    router_ref[...] = dot(second[...], logit_grad, ((0,), (0,)))


def attend_back_kernel(
    at, attended, probs, queries, keys, values, cosine, sine, branch, back_ref
):
    f32, bf16 = jnp.float32, jnp.bfloat16
    cosine_tab, sine_tab = cosine[...], -sine[...]
    group_size = HQ // HK
    places = back_ref.shape[0]
    branch_width = branch.shape[1] // places
    width = back_ref.shape[2] - branch_width
    for place in range(places):
        here = slice(place * branch_width, (place + 1) * branch_width)
        back_ref[place, :, width:] = branch[:, here]
    scale = HD ** (-0.5)

    def put(position, block):
        back_ref[position // width, :, position % width : position % width + HD] = block

    for group in range(HK):
        own = slice(group * HD, (group + 1) * HD)
        key, value = keys[:, own], values[:, own]
        key_grad = value_grad = 0.0
        start = group * (group_size + 2) * HD
        for member in range(group_size):
            head = group * group_size + member
            here = slice(head * HD, (head + 1) * HD)
            out_grad, query, prob = attended[:, here], queries[:, here], probs[head]
            prob_grad = dot(out_grad, value, ((1,), (1,)))
            prob_f = prob.astype(f32)
            inner = jnp.sum(prob_f * prob_grad, axis=-1, keepdims=True)
            score_grad = (prob_f * (prob_grad - inner)).astype(bf16)
            query_grad = turned(dot(score_grad, key) * scale, cosine_tab, sine_tab)
            put(start + member * HD, query_grad.astype(bf16))
            key_grad = key_grad + dot(score_grad, query, ((0,), (0,)))
            value_grad = value_grad + dot(prob, out_grad, ((0,), (0,)))
        key_grad = turned(key_grad * scale, cosine_tab, sine_tab)
        put(start + group_size * HD, key_grad.astype(bf16))
        put(start + (group_size + 1) * HD, value_grad.astype(bf16))


def first_back_kernel(at, back, weight, tokens, gain, resid_grad, tokens_ref, gain_ref):
    f32 = jnp.float32
    parts = back.shape[0]
    cols = weight.shape[0] * weight.shape[2] // parts
    first_grad = 0.0
    for part in range(parts):
        group, place = divmod(part * cols, weight.shape[2])
        first_grad = first_grad + dot(
            back[part, :, :cols], weight[group, :, place : place + cols], ((1,), (1,))
        )
    norm_grad, gain_grad = rms_back(tokens[...].astype(f32), gain[...], first_grad)
    gain_ref[...] = gain_grad
    tokens_ref[...] = (resid_grad[...] + norm_grad).astype(jnp.bfloat16)


def dense_grad_kernel(at, back, *refs):
    pieces, out_ref, held, sems = refs[:8], refs[8], refs[9], refs[10]
    copies = [
        pltpu.make_async_copy(piece, held.at[n], sems.at[n]) for n, piece in enumerate(pieces)
    ]
    for copy in copies:
        copy.start()
    depth, rows, cols = out_ref.shape
    length = held.shape[1] // 2
    qkv_width = cols - held.shape[2] // back.shape[0]
    narrow = sum(back[place, length:].astype(jnp.float32) for place in range(back.shape[0]))
    sums = [0.0, 0.0]
    for n, copy in enumerate(copies):
        copy.wait()
        dc, dy, dx = n // 4, n // 2 % 2, n % 2
        place = 4 * (at[0] ^ dy) + 2 * (at[1] ^ dc) + (at[2] ^ dx)
        own = back[place, :length]
        sums[0] = sums[0] + dot(held[n, length:], own[:, :qkv_width], ((0,), (0,)))
        sums[1] = sums[1] + dot(held[n, :length], own[:, qkv_width:], ((0,), (0,)))
    wide = held.shape[2] // depth
    each = narrow.shape[0] // depth
    for z in range(depth):
        here = slice(z * wide, (z + 1) * wide)
        both = jnp.concatenate([part[here] for part in sums], axis=1)
        out_ref[z, :wide] = both.astype(jnp.bfloat16)
        kept = [narrow[z * each : (z + 1) * each], jnp.zeros((rows - wide - each, cols), jnp.float32)]
        out_ref[z, wide:] = jnp.concatenate(kept, axis=0).astype(jnp.bfloat16)


def local_pairs(
    tokens,
    norm1_gain,
    w_query,
    w_key,
    w_value,
    w_out,
    norm2_gain,
    w_router,
    w_gate,
    w_up,
    w_down,
    expert_ids,
    prefix_len,
    out_grad,
):
    bf16, f32 = jnp.bfloat16, jnp.float32
    length, model_width = tokens.shape
    shard_rows = w_query.shape[0]
    local_count, _, hidden_width = w_gate.shape
    owners = lax.axis_size("x")
    depth = lax.axis_size("z")
    plane = lax.axis_size(PLANE)
    experts_all = w_router.shape[1]
    block_rows = length // MICRO
    capacity = 3 * block_rows * expert_ids.shape[1] // (2 * experts_all)
    plane_rows = plane * length
    blocks = plane_rows // block_rows
    q_cols, kv_cols = w_query.shape[1], w_key.shape[1]
    qkv_cols = q_cols + 2 * kv_cols
    q_group, out_half = q_cols // HK, model_width // 2
    y, c, x, z = (lax.axis_index(axis) for axis in ("y", "c", "x", "z"))
    own_local = 2 * y + c
    own_expert = x * local_count + own_local
    at = jnp.stack([y, c, x, z, prefix_len[0], own_expert, own_local])

    own_half = jnp.concatenate(
        [
            lax.dynamic_slice_in_dim(part, x * (part.shape[1] // 2), part.shape[1] // 2, 1)
            for part in (w_query, w_key, w_value, w_out)
        ],
        axis=1,
    )
    narrow = jnp.concatenate([w_router, norm1_gain[:, None], norm2_gain[:, None]], axis=1)
    narrow = small_group_gather(narrow)
    ids_all = small_gather(expert_ids)
    column = [own_half] + shifts(own_half)
    cot_sides = plane_sides(after(out_grad, narrow, ids_all))
    qkv_half = qkv_cols // 2
    qkv_column = jnp.stack([part[:, :qkv_half] for part in column])
    out_column = jnp.stack([part[:, qkv_half:] for part in column])
    qkv_column, out_column = lax.optimization_barrier((qkv_column, out_column, *cot_sides))[:2]
    qkv_sides = plane_sides(qkv_column)
    qkv_corner = plane_corner(qkv_sides)
    out_sides = plane_sides(after(out_column, qkv_corner))
    qkv_pieces = plane_pieces(qkv_column, qkv_sides, qkv_corner)
    router_w = jnp.pad(narrow[:, :experts_all], ((0, 0), (0, 128 - experts_all)))
    gains = narrow[:, experts_all : experts_all + 2].T.astype(f32)
    gain_one, gain_two = gains[:1], gains[1:]

    ids_turned = ids_all.T
    gain_one, ids_all, ids_turned, router_w = lax.optimization_barrier(
        (gain_one, ids_all, ids_turned, router_w)
    )

    cosine_tab, sine_tab = angles(length, HD)
    cosine_all = jnp.concatenate([cosine_tab, cosine_tab], axis=2)[:, 0]
    sine_all = jnp.concatenate([-sine_tab, sine_tab], axis=2)[:, 0]
    weight_lead = (2, depth, 2, 2, shard_rows)
    first_in, queries, keys_rot, values_b, attended, probs, qkv_w = run_kernel(
        attend_kernel,
        11,
        at,
        (tokens, gain_one, cosine_all, sine_all, *qkv_pieces),
        [
            ((length, model_width), bf16),
            ((length, q_cols), bf16),
            ((length, kv_cols), bf16),
            ((length, kv_cols), bf16),
            ((length, q_cols), bf16),
            ((HQ, length, length), bf16),
            (weight_lead + (qkv_half,), bf16),
        ],
        28,
        [
            pltpu.VMEM((HQ, length, length), bf16),
            pltpu.VMEM(weight_lead + (qkv_half,), bf16),
            pltpu.SemaphoreType.DMA((HK + 1,)),
        ],
        hbm_out=2,
    )
    out_sides = lax.optimization_barrier((*out_sides, attended))[:2]
    out_corner = plane_corner(out_sides)
    cot_corner = plane_corner(cot_sides, (out_corner,))
    out_pieces = plane_pieces(out_column, out_sides, out_corner)
    cot_pieces = plane_pieces(out_grad, cot_sides, cot_corner)
    resid, second_in, output_w = run_kernel(
        project_kernel,
        4,
        at,
        (tokens, after(gain_two, cot_corner), attended, *out_pieces),
        [
            ((length, model_width), f32),
            ((length, model_width), bf16),
            (weight_lead + (out_half,), bf16),
        ],
        20,
        [pltpu.VMEM(weight_lead + (out_half,), bf16), pltpu.SemaphoreType.DMA],
        hbm_out=1,
    )
    qkv_w = qkv_w.reshape(HK, model_width, qkv_half)
    output_w = output_w.reshape(2, q_cols, out_half)

    expert = functools.partial(
        run_expert,
        at=at,
        ids=ids_all,
        ids_turned=ids_turned,
        router=router_w,
        weights=(w_gate, w_up, w_down),
        capacity=capacity,
    )
    second_sides = plane_sides(second_in)
    groups = ((0, 4), (1, 5, 2, 6), (3, 7))
    second_pieces = {0: second_in, 4: swap(second_in, "c")}

    def run_group(pieces):
        return expert(
            pieces,
            second=[second_pieces[piece] for piece in pieces],
            cot=[cot_pieces[piece] for piece in pieces],
        )

    stage_own = run_group(groups[0])
    second_sides = lax.optimization_barrier((*second_sides, stage_own[0]))[:2]
    second_corner = plane_corner(second_sides)
    for piece, block in zip((1, 2), second_sides):
        second_pieces[piece], second_pieces[piece + 4] = block, swap(block, "c")
    stage_sides = run_group(groups[1])
    second_corner = after(second_corner, stage_sides[0])
    second_pieces[3], second_pieces[7] = second_corner, swap(second_corner, "c")
    own_near, own_far = stage_own[6:]
    own_far = swap(own_far, "c")
    x_near, x_far, y_near, y_far = stage_sides[6:]
    back_x, back_y = over_core(x_near, x_far), over_core(y_near, y_far)
    first_x, first_y = early_sums(back_x, back_y)
    stage_corner = run_group(groups[2])
    corner = over_core(*stage_corner[6:])
    passed = corner_first(corner)
    stages = (stage_own, stage_sides, stage_corner)
    rows_in, rows_cot, gated, gate_back, up_back = ([stage[n] for stage in stages] for n in range(5))
    gates = stage_own[5]
    down_part = row_sums(at, shard_rows, [after(rows_cot[0], corner)] + rows_cot[1:], gated)
    down_sum = scatter_sum(down_part, "z")
    passed = lax.optimization_barrier((*passed, down_part))[:2]
    last_y, last_x, sent = corner_last(back_x, back_y, passed)
    gate_up_part = row_sums(
        at, shard_rows, [after(rows_in[0], sent)] + rows_in[1:], gate_back, up_back
    )
    gate_up_sum = scatter_sum(gate_up_part, "z")
    own_near = after(own_near, gate_up_part)

    resid_grad, branch_grad, attended_grad, router_acc, gain_two_grad = run_kernel(
        branch_back_kernel,
        6,
        at,
        (
            own_near,
            own_far,
            first_x,
            first_y,
            last_y,
            last_x,
            resid,
            gain_two,
            second_in,
            gates,
            router_w,
            out_grad,
            output_w,
        ),
        [
            ((length, model_width), f32),
            ((length, model_width), bf16),
            ((length, q_cols), bf16),
            ((model_width, 128), f32),
            ((1, model_width), f32),
        ],
    )
    qkv_width, branch_width = qkv_cols // plane, model_width // plane
    dense_cols = qkv_width + branch_width
    (back_cols,) = run_kernel(
        attend_back_kernel,
        6,
        at,
        (
            attended_grad,
            probs,
            queries,
            keys_rot,
            values_b,
            cosine_all,
            sine_all,
            branch_grad,
        ),
        [((plane, length, dense_cols), bf16)],
    )
    tokens_grad, gain_one_grad = run_kernel(
        first_back_kernel,
        5,
        at,
        (back_cols, qkv_w, tokens, gain_one, resid_grad),
        [((length, model_width), bf16), ((1, model_width), f32)],
        24,
    )

    both = jnp.concatenate(
        lax.optimization_barrier((attended, first_in, resid_grad))[:2], axis=0
    )
    both_sides = plane_sides(both)
    narrow_part = jnp.concatenate(
        [router_acc[:, :experts_all], gain_one_grad.T, gain_two_grad.T], axis=1
    )
    narrow_cols = -(-narrow_part.shape[1] // owners) * owners
    narrow_part = jnp.pad(narrow_part, ((0, 0), (0, narrow_cols - narrow_part.shape[1])))
    narrow_part = jnp.transpose(
        narrow_part.reshape(depth, 2, 2, shard_rows, owners, narrow_cols // owners),
        (1, 2, 4, 0, 3, 5),
    ).reshape(plane, depth, shard_rows * narrow_cols // owners)
    narrow_len = narrow_part.shape[2]
    narrow_rows = -(-narrow_len // dense_cols)
    each_rows = -(-narrow_rows // 4) * 4
    narrow_part = jnp.pad(
        narrow_part, ((0, 0), (0, 0), (0, each_rows * dense_cols - narrow_len))
    ).reshape(plane, depth * each_rows, dense_cols)
    back_cols = exchange(jnp.concatenate([back_cols, narrow_part.astype(bf16)], axis=1), PLANE)
    both_corner = plane_corner(both_sides, (back_cols,))
    both_pieces = plane_pieces(both, both_sides, both_corner)
    kept_rows = -(-narrow_rows // 16) * 16
    wide_rows = local_count * shard_rows
    dense_shape = (depth, wide_rows + kept_rows, dense_cols)
    dense_part = pl.pallas_call(
        dense_grad_kernel,
        out_shape=jax.ShapeDtypeStruct(dense_shape, bf16),
        in_specs=[SCALARS, WHOLE] + [IN_HBM] * 8,
        out_specs=WHOLE,
        scratch_shapes=[
            pltpu.VMEM((plane, 2 * length, model_width), bf16),
            pltpu.SemaphoreType.DMA((plane,)),
        ],
        cost_estimate=cost(8),
        compiler_params=pltpu.CompilerParams(vmem_limit_bytes=32 * 2**20),
    )(at, back_cols, *both_pieces)
    dense_sum = scatter_sum(dense_part.reshape(-1, dense_cols), "z")
    wide_sum = dense_sum[: local_count * shard_rows].reshape(2, 2, 1, shard_rows, dense_cols)
    wide_sum = jnp.broadcast_to(wide_sum, (2, 2, owners, shard_rows, dense_cols)).reshape(
        plane, shard_rows, dense_cols
    )
    narrow_sum = dense_sum[local_count * shard_rows :][:narrow_rows]
    narrow_sum = jnp.broadcast_to(narrow_sum[None], (plane, narrow_rows, dense_cols))
    pad_rows = -(shard_rows + narrow_rows) % 16
    padding = jnp.zeros((plane, pad_rows, dense_cols), bf16)
    dense_sum = exchange(jnp.concatenate([wide_sum, narrow_sum, padding], axis=1), PLANE)
    wide_sum = jnp.moveaxis(dense_sum[:, :shard_rows].astype(f32), 0, 1)
    qkv_sum = wide_sum[:, :, :qkv_width].reshape(shard_rows, HK, qkv_half)
    output_sum = wide_sum[:, :, qkv_width:].reshape(shard_rows, model_width)
    narrow_sum = dense_sum[:, shard_rows : shard_rows + narrow_rows].reshape(
        2, 2, owners, narrow_rows * dense_cols
    )
    narrow_sum = narrow_sum[y, c, :, :narrow_len].reshape(owners, shard_rows, -1)
    narrow_sum = jnp.moveaxis(narrow_sum, 0, 1).reshape(shard_rows, narrow_cols).astype(f32)

    shares = run_kernel(
        functools.partial(mixture_kernel, capacity, groups),
        10,
        at,
        (ids_turned, after(gated[0], both_corner), *gated[1:], w_down),
        [((length, model_width), bf16)] * plane,
        24,
        [pltpu.VMEM(w_down.shape[1:], bf16), pltpu.SemaphoreType.DMA],
        hbm_in=1,
    )
    mixed = [over_core(near, far) for near, far in zip(shares[:4], shares[4:])]
    early = early_sums(mixed[1], mixed[2])
    last = corner_last(mixed[1], mixed[2], corner_first(mixed[3]))[:2]
    mixture = jnp.concatenate(
        [left.astype(f32) + right.astype(f32) for left, right in zip(early, last)], axis=0
    )
    block_out = (resid + (mixture + mixed[0].astype(f32))).astype(bf16)

    down_grad = exchange(down_sum, ("y", "c"))[:, 0].astype(f32)
    gate_up_grad = exchange(gate_up_sum, ("y", "c")).astype(f32)

    return (
        block_out,
        tokens_grad,
        narrow_sum[:, experts_all],
        qkv_sum[:, :, :q_group].reshape(shard_rows, q_cols),
        qkv_sum[:, :, q_group : q_group + HD].reshape(shard_rows, kv_cols),
        qkv_sum[:, :, q_group + HD :].reshape(shard_rows, kv_cols),
        output_sum,
        narrow_sum[:, experts_all + 1],
        narrow_sum[:, :experts_all],
        gate_up_grad[:, 0],
        gate_up_grad[:, 1],
        jnp.swapaxes(down_grad, 1, 2),
    )


def solution(mesh):
    groups, owners = mesh.shape["dp"], mesh.shape["expert"]
    grid = jax.sharding.Mesh(
        mesh.devices.reshape(groups // 4, 2, 2, owners), ("z", "y", "c", "x")
    )
    rows = P(("z", "y", "c", "x"), None)
    shard, shard_rows = P(GROUP), P(GROUP, None)
    expert = P("x", None, None)
    return jax.shard_map(
        local_pairs if owners == 2 else local_wide,
        mesh=grid,
        in_specs=(
            rows,
            shard,
            shard_rows,
            shard_rows,
            shard_rows,
            shard_rows,
            shard,
            shard_rows,
            expert,
            expert,
            expert,
            rows,
            P(("z", "y", "c", "x")),
            rows,
        ),
        out_specs=(
            rows,
            rows,
            shard,
            shard_rows,
            shard_rows,
            shard_rows,
            shard_rows,
            shard,
            shard_rows,
            P("x", GROUP, None),
            P("x", GROUP, None),
            P("x", None, GROUP),
        ),
        check_vma=False,
    )
```

```python
import functools
import math

import jax
import jax.numpy as jnp
from jax import lax
from jax.experimental import pallas as pl
from jax.experimental.pallas import tpu as pltpu
from jax.sharding import PartitionSpec as P

HQ = 12
HK = 2
HD = 128
MICRO = 2
PLANE = ("y", "c", "x")
GROUP = ("z", "y", "c")


def rms_scale(values, gain_vec):
    inverse = lax.rsqrt(jnp.mean(values * values, axis=-1, keepdims=True) + 1e-06)
    return values * inverse * gain_vec


def angles(length, head_size):
    positions = jnp.arange(length).astype(jnp.float32)
    freq_rates = jnp.exp(
        -(2.0 * jnp.arange(head_size // 2).astype(jnp.float32) / head_size) * math.log(1000000.0)
    )
    angle_tab = positions[:, None] * freq_rates[None, :]
    return (jnp.cos(angle_tab)[:, None, :], jnp.sin(angle_tab)[:, None, :])


def rotary(values, cosine_tab, sine_tab):
    half_dim = values.shape[-1] // 2
    first_half = values[..., :half_dim]
    second_half = values[..., half_dim:]
    return jnp.concatenate(
        [
            first_half * cosine_tab - second_half * sine_tab,
            second_half * cosine_tab + first_half * sine_tab,
        ],
        axis=-1,
    )


def expert_act(gate_pre, up_pre):
    return jax.nn.gelu(gate_pre, approximate=True) * up_pre


def left_product(left_mat, right_mat):
    return lax.dot_general(
        left_mat, right_mat, (((0,), (0,)), ((), ())), preferred_element_type=jnp.float32
    )


def gather(block, axes):
    return lax.all_gather(block, axes, axis=0, tiled=True)


def exchange(block, axes):
    return lax.all_to_all(block, axes, split_axis=0, concat_axis=0, tiled=True)


def scatter_sum(block, axes):
    return lax.psum_scatter(block, axes, scatter_dimension=0, tiled=True)


def by_owner(cols, parts):
    rows, total = cols.shape
    return jnp.moveaxis(cols.reshape(rows, parts, total // parts), 1, 0).reshape(
        parts * rows, total // parts
    )


def local_wide(
    tokens,
    norm1_gain,
    w_query,
    w_key,
    w_value,
    w_out,
    norm2_gain,
    w_router,
    w_gate,
    w_up,
    w_down,
    expert_ids,
    prefix_len,
    out_grad,
):
    bf16, f32 = jnp.bfloat16, jnp.float32
    length, model_width = tokens.shape
    shard_rows = w_query.shape[0]
    local_count, _, hidden_width = w_gate.shape
    owners = lax.axis_size("x")
    depth = lax.axis_size("z")
    plane = lax.axis_size(PLANE)
    experts_all = w_router.shape[1]
    top_count = expert_ids.shape[1]
    block_rows = length // MICRO
    capacity = 3 * block_rows * top_count // (2 * experts_all)
    plane_rows = plane * length
    blocks = plane_rows // block_rows
    group_size = HQ // HK
    score_scale = HD ** (-0.5)
    q_cols, kv_cols = w_query.shape[1], w_key.shape[1]
    own_local = lax.axis_index(("y", "c"))
    own_expert = lax.axis_index("x") * local_count + own_local
    own_place = lax.axis_index(PLANE)

    narrow = jnp.concatenate([w_router, norm1_gain[:, None], norm2_gain[:, None]], axis=1)
    narrow = jnp.pad(narrow, ((0, 0), (0, -narrow.shape[1] % 128)))
    packed = gather(jnp.concatenate([w_query, w_key, w_value, narrow], axis=1), GROUP)
    qkv_cols = q_cols + 2 * kv_cols
    qkv_w = packed[:, :qkv_cols]
    router_w = packed[:, qkv_cols : qkv_cols + experts_all]
    gains = packed[:, qkv_cols + experts_all : qkv_cols + experts_all + 2].T.astype(f32)
    gain_one, gain_two = gains[0], gains[1]
    output_w = gather(w_out, GROUP)

    ids_all = gather(expert_ids, PLANE)
    cot_all = gather(out_grad, PLANE)
    chosen_mask = jnp.any(
        ids_all[:, :, None] == jnp.arange(experts_all, dtype=jnp.int32)[None, None, :], axis=1
    )
    own_mask = jnp.any(ids_all == own_expert, axis=1).reshape(blocks, block_rows)
    place = jnp.cumsum(own_mask.astype(jnp.int32), axis=1) - 1
    dispatch = (
        own_mask[:, None, :]
        & (place[:, None, :] == jnp.arange(capacity, dtype=jnp.int32)[None, :, None])
    ).astype(bf16)

    cosine_tab, sine_tab = angles(length, HD)
    inputs_f = tokens.astype(f32)
    first_in = rms_scale(inputs_f, gain_one).astype(bf16)
    qkv = jnp.dot(first_in, qkv_w, preferred_element_type=f32)
    queries = (
        rotary(qkv[:, :q_cols].reshape(length, HQ, HD), cosine_tab, sine_tab)
        .astype(bf16)
        .reshape(length, HK, group_size, HD)
    )
    keys_rot = rotary(
        qkv[:, q_cols : q_cols + kv_cols].reshape(length, HK, HD), cosine_tab, sine_tab
    ).astype(bf16)
    values_b = qkv[:, q_cols + kv_cols :].astype(bf16).reshape(length, HK, HD)
    positions = jnp.arange(length)
    allowed = (positions[None, :] <= positions[:, None]) | (positions[None, :] < prefix_len[0])

    def masked_scores():
        scores = jnp.einsum("ihrd,jhd->hrij", queries, keys_rot, preferred_element_type=f32)
        return jnp.where(allowed, scores * score_scale, -1e30)

    masked = masked_scores()
    row_peak = jnp.max(masked, axis=-1, keepdims=True)
    log_total = row_peak + jnp.log(jnp.sum(jnp.exp(masked - row_peak), axis=-1, keepdims=True))
    prob_bf = jnp.exp(masked - log_total).astype(bf16)
    attended = jnp.einsum("hrij,jhd->ihrd", prob_bf, values_b, preferred_element_type=f32)
    attended = attended.reshape(length, HQ * HD).astype(bf16)
    resid = inputs_f + jnp.dot(attended, output_w, preferred_element_type=f32)
    second_in = rms_scale(resid, gain_two).astype(bf16)

    second_all = gather(second_in, PLANE)
    logits = jnp.dot(second_all, router_w, preferred_element_type=f32)
    gates_all = jax.nn.softmax(jnp.where(chosen_mask, logits, -jnp.inf), axis=-1)
    own_gates = lax.dynamic_index_in_dim(gates_all, own_expert, 1, keepdims=False)
    own_gates = own_gates.reshape(blocks, block_rows)
    gate_rows = jnp.einsum(
        "bct,bt->bc", dispatch.astype(f32), own_gates, precision=lax.Precision.HIGHEST
    )[:, :, None]
    gate_w = lax.dynamic_index_in_dim(w_gate, own_local, 0, keepdims=False)
    up_w = lax.dynamic_index_in_dim(w_up, own_local, 0, keepdims=False)
    down_w = lax.dynamic_index_in_dim(w_down, own_local, 0, keepdims=False)

    def to_rows(array):
        return jnp.einsum(
            "bct,btd->bcd",
            dispatch,
            array.reshape(blocks, block_rows, model_width),
            preferred_element_type=f32,
        ).astype(bf16)

    def to_tokens(rows):
        return (
            jnp.einsum("bct,bcd->btd", dispatch, rows.astype(bf16), preferred_element_type=f32)
            .astype(bf16)
            .reshape(plane_rows, model_width)
        )

    rows_in = to_rows(second_all)
    rows_cot = to_rows(cot_all)
    gate_pre = jnp.einsum("bcd,df->bcf", rows_in, gate_w, preferred_element_type=f32)
    up_pre = jnp.einsum("bcd,df->bcf", rows_in, up_w, preferred_element_type=f32)
    hidden, act_pull = jax.vjp(expert_act, gate_pre, up_pre)
    gated = (gate_rows * hidden).astype(bf16)
    down_part = jnp.einsum("bcd,bcf->df", rows_cot, gated, preferred_element_type=f32)
    down_sum = scatter_sum(down_part.astype(bf16), "z")
    cot_hidden = jnp.einsum("bcd,fd->bcf", rows_cot, down_w, preferred_element_type=f32)
    gate_signal_rows = jnp.sum(hidden * cot_hidden, axis=-1)
    gate_pgrad, up_pgrad = act_pull(gate_rows * cot_hidden)
    gate_pgrad = gate_pgrad.astype(bf16)
    up_pgrad = up_pgrad.astype(bf16)
    gate_part = jnp.einsum("bcd,bcf->df", rows_in, gate_pgrad, preferred_element_type=f32)
    gate_sum = scatter_sum(gate_part.astype(bf16), "z")
    up_part = jnp.einsum("bcd,bcf->df", rows_in, up_pgrad, preferred_element_type=f32)
    up_sum = scatter_sum(up_part.astype(bf16), "z")
    rows_grad = jnp.einsum("bcf,df->bcd", gate_pgrad, gate_w, preferred_element_type=f32)
    rows_grad = rows_grad + jnp.einsum("bcf,df->bcd", up_pgrad, up_w, preferred_element_type=f32)
    second_back = scatter_sum(to_tokens(rows_grad), PLANE).astype(f32)
    gate_signal = jnp.einsum(
        "bct,bc->bt", dispatch.astype(f32), gate_signal_rows, precision=lax.Precision.HIGHEST
    )
    gate_signal = exchange(gate_signal.reshape(plane, length), PLANE)
    gate_signal = jnp.transpose(
        gate_signal.reshape(local_count, owners, length), (2, 1, 0)
    ).reshape(length, experts_all)
    expert_rows = jnp.einsum("bcf,fd->bcd", gated, down_w, preferred_element_type=f32)
    mixture = scatter_sum(to_tokens(expert_rows), PLANE).astype(f32)
    block_out = (resid + mixture).astype(bf16)

    cotangent = out_grad.astype(f32)
    gate_probs = lax.dynamic_slice_in_dim(gates_all, own_place * length, length, 0)
    logit_grad = (
        gate_probs
        * (gate_signal - jnp.sum(gate_probs * gate_signal, axis=-1, keepdims=True))
    ).astype(bf16)
    router_acc = left_product(second_in, logit_grad)
    second_grad = second_back + jnp.dot(logit_grad, router_w.T, preferred_element_type=f32)
    _, norm_two_pull = jax.vjp(rms_scale, resid, gain_two)
    resid_norm_grad, gain_two_grad = norm_two_pull(second_grad)
    resid_grad = cotangent + resid_norm_grad
    branch_grad = resid_grad.astype(bf16)

    attended_all = gather(attended, PLANE)
    branch_cols = exchange(by_owner(branch_grad, plane), PLANE)
    output_part = left_product(attended_all, branch_cols)
    attended_grad = jnp.dot(branch_grad, output_w.T, preferred_element_type=f32).astype(bf16)
    attended_grad = attended_grad.reshape(length, HK, group_size, HD)
    masked = masked_scores()
    prob_full = jnp.exp(masked - log_total)
    prob_bf = prob_full.astype(bf16)
    prob_grad = jnp.einsum("ihrd,jhd->hrij", attended_grad, values_b, preferred_element_type=f32)
    row_inner = jnp.sum(prob_full * prob_grad, axis=-1, keepdims=True)
    score_grad = (prob_full * (prob_grad - row_inner)).astype(bf16)
    query_rot_grad = (
        jnp.einsum("hrij,jhd->ihrd", score_grad, keys_rot, preferred_element_type=f32)
        * score_scale
    )
    query_back = rotary(query_rot_grad.reshape(length, HQ, HD), cosine_tab, -sine_tab)
    query_back = query_back.astype(bf16).reshape(length, HQ * HD)
    key_rot_grad = (
        jnp.einsum("hrij,ihrd->jhd", score_grad, queries, preferred_element_type=f32)
        * score_scale
    )
    key_back = rotary(key_rot_grad, cosine_tab, -sine_tab).astype(bf16).reshape(length, HK * HD)
    value_back = jnp.einsum("hrij,ihrd->jhd", prob_bf, attended_grad, preferred_element_type=f32)
    value_back = value_back.astype(bf16).reshape(length, HK * HD)
    qkv_back = jnp.concatenate([query_back, key_back, value_back], axis=1)
    first_all = gather(first_in, PLANE)
    qkv_part = left_product(first_all, exchange(by_owner(qkv_back, plane), PLANE))
    first_grad = lax.dot_general(
        qkv_back, qkv_w, (((1,), (1,)), ((), ())), preferred_element_type=f32
    )
    _, norm_one_pull = jax.vjp(rms_scale, inputs_f, gain_one)
    input_norm_grad, gain_one_grad = norm_one_pull(first_grad)
    tokens_grad = (resid_grad + input_norm_grad).astype(bf16)

    narrow_part = jnp.concatenate(
        [router_acc, gain_one_grad[:, None], gain_two_grad[:, None]], axis=1
    ).astype(bf16)
    narrow_cols = narrow_part.shape[1]
    narrow_sum = lax.psum(scatter_sum(narrow_part, GROUP), "x").astype(f32)
    dense_part = jnp.concatenate([qkv_part, output_part], axis=1).astype(bf16)
    dense_sum = scatter_sum(dense_part, "z")
    dense_cols = dense_sum.shape[1]
    dense_sum = gather(dense_sum, PLANE).reshape(plane, local_count, shard_rows, dense_cols)
    dense_sum = lax.dynamic_index_in_dim(dense_sum, own_local, 1, keepdims=False).astype(f32)
    dense_sum = jnp.moveaxis(dense_sum, 0, 1)
    qkv_width = qkv_cols // plane
    qkv_sum = dense_sum[:, :, :qkv_width].reshape(shard_rows, qkv_cols)
    output_sum = dense_sum[:, :, qkv_width:].reshape(shard_rows, model_width)

    def placed(total):
        total = exchange(total, ("y", "c"))
        return total.reshape(local_count, shard_rows, hidden_width).astype(f32)

    return (
        block_out,
        tokens_grad,
        narrow_sum[:, experts_all],
        qkv_sum[:, :q_cols],
        qkv_sum[:, q_cols : q_cols + kv_cols],
        qkv_sum[:, q_cols + kv_cols :],
        output_sum,
        narrow_sum[:, experts_all + 1],
        narrow_sum[:, :experts_all],
        placed(gate_sum),
        placed(up_sum),
        jnp.swapaxes(placed(down_sum), 1, 2),
    )


def rounded(values):
    return lax.reduce_precision(values, 8, 7).astype(jnp.bfloat16)


def after(block, *others):
    return lax.optimization_barrier((block,) + others)[0]


def swap(block, axis):
    return lax.ppermute(block, axis, [(0, 1), (1, 0)])


def shifts(block):
    depth = lax.axis_size("z")
    return [
        lax.ppermute(block, "z", [(i, (i + k) % depth) for i in range(depth)])
        for k in range(1, depth)
    ]


def plane_sides(block):
    return swap(block, "x"), swap(block, "y")


def plane_corner(sides, before=(), later=()):
    over_x, over_y = sides
    half = over_x.shape[0] // 2
    over_y, over_x = lax.optimization_barrier((over_y[:half], over_x[half:]) + before)[:2]
    parts = (swap(over_y, "x"), swap(over_x, "y"))
    return jnp.concatenate(lax.optimization_barrier(parts + later)[:2], axis=0)


def plane_pieces(block, sides=None, corner=None):
    sides = plane_sides(block) if sides is None else sides
    corner = plane_corner(sides) if corner is None else corner
    pieces = [block, *sides, corner]
    return pieces + [swap(piece, "c") for piece in pieces]


def small_gather(block):
    for axis in ("x", "y", "c"):
        block = jnp.concatenate([block, swap(block, axis)], axis=0)
    return block


def small_group_gather(block):
    depth = lax.axis_size("z")
    order = jnp.stack(([block] + shifts(block))[::-1] * 2)
    start = (depth - 1 - lax.axis_index("z")) % depth
    total = lax.dynamic_slice_in_dim(order, start, depth, 0)[:, None, None]
    for dim, axis in ((1, "y"), (2, "c")):
        other = swap(total, axis)
        last = lax.axis_index(axis) == 1
        pair = [jnp.where(last, other, total), jnp.where(last, total, other)]
        total = jnp.concatenate(pair, axis=dim)
    return total.reshape(-1, block.shape[1])


def add(left, right):
    return rounded(left.astype(jnp.float32) + right.astype(jnp.float32))


def over_core(near, far):
    return add(near, swap(far, "c"))


def early_sums(over_x, over_y):
    half = over_x.shape[0] // 2
    return swap(over_x[:half], "x"), swap(over_y[half:], "y")


def corner_first(corner):
    half = corner.shape[0] // 2
    return swap(corner[:half], "x"), swap(corner[half:], "y")


def corner_last(over_x, over_y, first):
    half = over_x.shape[0] // 2
    over_y, over_x = add(over_y[:half], first[0]), add(over_x[half:], first[1])
    return swap(over_y, "y"), swap(over_x, "x"), over_x


def cost(micros):
    return pl.CostEstimate(flops=micros * 10**9, bytes_accessed=micros * 10**6, transcendentals=0)


def dot(left, right, dims=((1,), (0,)), precision=None):
    return lax.dot_general(
        left, right, (dims, ((), ())), precision=precision, preferred_element_type=jnp.float32
    )


WHOLE = pl.BlockSpec(memory_space=pltpu.VMEM)
IN_HBM = pl.BlockSpec(memory_space=pltpu.HBM)
SCALARS = pl.BlockSpec(memory_space=pltpu.SMEM)


def run_kernel(kernel, micros, at, operands, outs, megabytes=16, scratch=(), hbm_in=0, hbm_out=0):
    return pl.pallas_call(
        kernel,
        out_shape=[jax.ShapeDtypeStruct(shape, dtype) for shape, dtype in outs],
        in_specs=[SCALARS] + [WHOLE] * (len(operands) - hbm_in) + [IN_HBM] * hbm_in,
        out_specs=[WHOLE] * (len(outs) - hbm_out) + [IN_HBM] * hbm_out,
        scratch_shapes=scratch,
        cost_estimate=cost(micros),
        compiler_params=pltpu.CompilerParams(vmem_limit_bytes=megabytes * 2**20),
    )(at, *operands)


def place_pieces(at, refs, weight):
    depth = weight.shape[1]
    for n, ref in enumerate(refs):
        dc, dy, dx = n // 4, n // 2 % 2, n % 2
        for k in range(depth):
            z = lax.rem(at[3] + depth - k, depth)
            weight[at[2] ^ dx, z, at[0] ^ dy, at[1] ^ dc] = ref[k]


def rms_kernel(values, gain):
    inverse = lax.rsqrt(jnp.mean(values * values, axis=-1, keepdims=True) + 1e-06)
    return (values * inverse * gain).astype(jnp.bfloat16)


def rms_back(values, gain, grad):
    inverse = lax.rsqrt(jnp.mean(values * values, axis=-1, keepdims=True) + 1e-06)
    normed = values * inverse
    gain_grad = jnp.sum(grad * normed, axis=0, keepdims=True)
    grad = grad * gain
    along = jnp.mean(grad * normed, axis=-1, keepdims=True)
    return inverse * (grad - normed * along), gain_grad


def turned(values, cosine_tab, sine_tab):
    return values * cosine_tab + pltpu.roll(values, HD // 2, 1) * sine_tab


def attend_kernel(at, tokens, gain, cosine, sine, *refs):
    first_ref, query_ref, key_ref, value_ref, out_ref = refs[8:13]
    prob_out, weight_out, prob_ref, weight, sems = refs[13:]
    place_pieces(at, refs[:8], weight)
    copies = [pltpu.make_async_copy(weight, weight_out, sems.at[HK])]
    copies[0].start()
    length = tokens.shape[0]
    first_in = rms_kernel(tokens[...].astype(jnp.float32), gain[...])
    first_ref[...] = first_in
    rows = lax.broadcasted_iota(jnp.int32, (length, length), 0)
    cols = lax.broadcasted_iota(jnp.int32, (length, length), 1)
    allowed = (cols <= rows) | (cols < at[4])
    cosine_tab, sine_tab = cosine[...], sine[...]
    group_size = HQ // HK
    for group in range(HK):
        matrix = weight[group].reshape(first_in.shape[1], -1)
        qkv = dot(first_in, matrix)
        at_key = group_size * HD
        key = turned(qkv[:, at_key : at_key + HD], cosine_tab, sine_tab).astype(jnp.bfloat16)
        value = qkv[:, at_key + HD :].astype(jnp.bfloat16)
        key_ref[:, group * HD : (group + 1) * HD] = key
        value_ref[:, group * HD : (group + 1) * HD] = value
        for member in range(group_size):
            head = group * group_size + member
            here = slice(head * HD, (head + 1) * HD)
            query = turned(qkv[:, member * HD : (member + 1) * HD], cosine_tab, sine_tab)
            query = query.astype(jnp.bfloat16)
            query_ref[:, here] = query
            scores = dot(query, key, ((1,), (1,)))
            scores = jnp.where(allowed, scores * HD ** (-0.5), -1e30)
            weights = jnp.exp(scores - jnp.max(scores, axis=-1, keepdims=True))
            prob = weights * (1.0 / jnp.sum(weights, axis=-1, keepdims=True))
            prob = prob.astype(jnp.bfloat16)
            prob_ref[head] = prob
            out_ref[:, here] = dot(prob, value).astype(jnp.bfloat16)
        here = pl.ds(group * group_size, group_size)
        copies.append(
            pltpu.make_async_copy(prob_ref.at[here], prob_out.at[here], sems.at[group])
        )
        copies[-1].start()
    for copy in copies:
        copy.wait()


def project_kernel(at, tokens, gain, attended, *refs):
    resid_ref, second_ref, weight_out, weight, sem = refs[8:]
    place_pieces(at, refs[:8], weight)
    copy = pltpu.make_async_copy(weight, weight_out, sem)
    copy.start()
    heads = attended[...]
    halves = [dot(heads, weight[half].reshape(heads.shape[1], -1)) for half in range(2)]
    resid = tokens[...].astype(jnp.float32) + jnp.concatenate(halves, axis=1)
    resid_ref[...] = resid
    second_ref[...] = rms_kernel(resid, gain[...])
    copy.wait()


def one_hot(slots, capacity, dtype):
    shape = (capacity, slots.shape[1])
    return (slots == lax.broadcasted_iota(jnp.int32, shape, 0)).astype(jnp.float32).astype(dtype)


def slots_of(ids, expert, start, rows):
    named = jnp.any(ids[:, start : start + rows] == expert, axis=0, keepdims=True)
    named = named.astype(jnp.float32)
    before = lax.broadcasted_iota(jnp.int32, (rows, rows), 0)
    upto = lax.broadcasted_iota(jnp.int32, (rows, rows), 1)
    counts = dot(named.astype(jnp.bfloat16), (before <= upto).astype(jnp.float32).astype(jnp.bfloat16))
    return jnp.where(named > 0.0, counts - 1.0, -1.0).astype(jnp.int32)


def spread(picks, capacity, rows, outs):
    rows = rows.astype(jnp.bfloat16)
    block = picks[0].shape[1]
    for n in range(len(picks) // 2):
        for part in range(2):
            pick = picks[2 * n + part]
            at_row = (2 * n + part) * capacity
            tokens = dot(pick, rows[at_row : at_row + capacity], ((0,), (0,)))
            outs[n][part * block : (part + 1) * block] = tokens.astype(jnp.bfloat16)


def expert_kernel(capacity, pieces, at, ids, ids_turned, router, *refs):
    count = len(pieces)
    second, cot = refs[:count], refs[count : 2 * count]
    gate_w, up_w, down_w = refs[2 * count : 2 * count + 3]
    rows_in, rows_cot, gated_ref, gate_back, up_back, gates_ref = refs[2 * count + 3 : 2 * count + 9]
    backs, gate_rows = refs[2 * count + 9 : -1], refs[-1]
    f32, bf16 = jnp.float32, jnp.bfloat16
    length, width = second[0].shape
    wide = router.shape[1]
    half = length // 2
    picks = []
    for n, piece in enumerate(pieces):
        tokens = second[n][...]
        experts = lax.broadcasted_iota(jnp.int32, (length, wide), 1)
        named = ids[piece * length : (piece + 1) * length]
        chosen = functools.reduce(
            jnp.logical_or, [named[:, k : k + 1] == experts for k in range(named.shape[1])]
        )
        logits = jnp.where(chosen, dot(tokens, router[...]), -1e30)
        weights = jnp.exp(logits - jnp.max(logits, axis=-1, keepdims=True))
        gates = weights * (1.0 / jnp.sum(weights, axis=-1, keepdims=True))
        if n == 0:
            gates_ref[...] = gates
        lanes = lax.broadcasted_iota(jnp.int32, (capacity, wide), 1)
        for part in range(2):
            here = slice(part * half, (part + 1) * half)
            place = slice((2 * n + part) * capacity, (2 * n + part + 1) * capacity)
            slots = slots_of(ids_turned, at[5], piece * length + part * half, half)
            pick = one_hot(slots, capacity, f32)
            picks.append(pick.astype(bf16))
            rows_in[place] = dot(picks[-1], tokens[here]).astype(bf16)
            rows_cot[place] = dot(picks[-1], cot[n][here]).astype(bf16)
            picked = dot(pick, gates[here], precision=lax.Precision.HIGHEST)
            picked = jnp.where(lanes == at[5], picked, 0.0)
            gate_rows[place] = jnp.sum(picked, axis=1, keepdims=True)
    gate = gate_rows[...]
    gate_pre = dot(rows_in[...], gate_w[...])
    up_pre = dot(rows_in[...], up_w[...])
    cot_hidden = dot(rows_cot[...], down_w[...], ((1,), (1,)))
    scale = math.sqrt(2.0 / math.pi)
    square = gate_pre * gate_pre
    bent = jnp.tanh(scale * gate_pre * (1.0 + 0.044715 * square))
    open_part = 0.5 * (1.0 + bent)
    active = gate_pre * open_part
    slope = open_part + 0.5 * gate_pre * (1.0 - bent * bent) * scale * (
        1.0 + 3 * 0.044715 * square
    )
    hidden = active * up_pre
    gated_ref[...] = (gate * hidden).astype(bf16)
    signal = jnp.sum(hidden * cot_hidden, axis=1, keepdims=True)
    back = gate * cot_hidden
    gate_back[...] = (back * up_pre * slope).astype(bf16)
    up_back[...] = (back * active).astype(bf16)
    high = signal.astype(bf16)
    low = (signal - high.astype(f32)).astype(bf16)
    lanes = lax.broadcasted_iota(jnp.int32, (signal.shape[0], wide), 1)
    signal = jnp.where(lanes == at[5], high.astype(f32), 0.0)
    signal = jnp.where(lanes == at[5] + wide // 2, low.astype(f32), signal)
    by_rows = ((1,), (1,))
    rows = dot(gate_back[...], gate_w[...], by_rows) + dot(up_back[...], up_w[...], by_rows)
    spread(picks, capacity, jnp.concatenate([rows, signal], axis=1), backs)


def run_expert(pieces, at, ids, ids_turned, router, weights, second, cot, capacity):
    count = len(pieces)
    rows, wide = 2 * count * capacity, router.shape[1]
    (length, width), hidden = second[0].shape, weights[0].shape[1]
    bf16, f32 = jnp.bfloat16, jnp.float32
    outs = [(rows, width)] * 2 + [(rows, hidden)] * 3
    outs = [(shape, bf16) for shape in outs] + [((length, wide), f32)]
    outs = outs + [((length, width + wide), bf16)] * count
    return run_kernel(
        functools.partial(expert_kernel, capacity, pieces),
        4 * count,
        at,
        (ids, ids_turned, router, *second, *cot, *weights),
        outs,
        8 + 6 * count,
        [pltpu.VMEM((rows, 1), f32)],
    )


def mixture_kernel(capacity, groups, at, ids_turned, *refs):
    gated, down_w, outs = refs[: len(groups)], refs[len(groups)], refs[len(groups) + 1 :]
    length = outs[0].shape[0]
    for pieces, rows in zip(groups, gated):
        picks = []
        for piece in pieces:
            for part in range(2):
                start = piece * length + part * length // 2
                slots = slots_of(ids_turned, at[5], start, length // 2)
                picks.append(one_hot(slots, capacity, jnp.bfloat16))
        spread(picks, capacity, dot(rows[...], down_w[...]), [outs[piece] for piece in pieces])


def row_sum_kernel(parts, at, *refs):
    arrays = [
        jnp.concatenate([ref[...] for ref in refs[n : n + parts]], axis=0)
        for n in range(0, len(refs) - len(refs) // (parts + 1), parts)
    ]
    outs = refs[len(arrays) * parts :]
    for out, right in zip(outs, arrays[1:]):
        out[...] = dot(arrays[0], right, ((0,), (0,))).astype(jnp.bfloat16)


def row_sums(at, left, *rights):
    operands = [part for parts in (left, *rights) for part in parts]
    outs = [((left[0].shape[1], right[0].shape[1]), jnp.bfloat16) for right in rights]
    kernel = functools.partial(row_sum_kernel, len(left))
    return run_kernel(kernel, 4 * len(rights), at, operands, outs, 24)


def branch_back_kernel(
    at, near, far, first_x, first_y, last_y, last_x, resid, gain, second, gates, router, cot, weight, *outs
):
    resid_grad_ref, branch_ref, attended_ref, router_ref, gain_ref = outs
    f32, bf16 = jnp.float32, jnp.bfloat16
    halves = [first_x[...].astype(f32) + last_y[...], first_y[...].astype(f32) + last_x[...]]
    total = near[...].astype(f32) + far[...] + jnp.concatenate(halves, axis=0)
    width = resid.shape[1]
    signal = total[:, width:]
    signal = signal + pltpu.roll(signal, signal.shape[1] // 2, 1)
    chosen = gates[...]
    logit_grad = chosen * (signal - jnp.sum(chosen * signal, axis=-1, keepdims=True))
    logit_grad = logit_grad.astype(bf16)
    second_grad = total[:, :width] + dot(logit_grad, router[...], ((1,), (1,)))
    norm_grad, gain_grad = rms_back(resid[...], gain[...], second_grad)
    gain_ref[...] = gain_grad
    resid_grad = cot[...].astype(f32) + norm_grad
    resid_grad_ref[...] = resid_grad
    branch = resid_grad.astype(bf16)
    branch_ref[...] = branch
    wide = weight.shape[2]
    attended_ref[...] = (
        dot(branch[:, :wide], weight[0], ((1,), (1,)))
        + dot(branch[:, wide:], weight[1], ((1,), (1,)))
    ).astype(bf16)
    router_ref[...] = dot(second[...], logit_grad, ((0,), (0,)))


def attend_back_kernel(
    at, attended, probs, queries, keys, values, cosine, sine, branch, back_ref
):
    f32, bf16 = jnp.float32, jnp.bfloat16
    cosine_tab, sine_tab = cosine[...], -sine[...]
    group_size = HQ // HK
    places = back_ref.shape[0]
    branch_width = branch.shape[1] // places
    width = back_ref.shape[2] - branch_width
    for place in range(places):
        here = slice(place * branch_width, (place + 1) * branch_width)
        back_ref[place, :, width:] = branch[:, here]
    scale = HD ** (-0.5)

    def put(position, block):
        back_ref[position // width, :, position % width : position % width + HD] = block

    for group in range(HK):
        own = slice(group * HD, (group + 1) * HD)
        key, value = keys[:, own], values[:, own]
        key_grad = value_grad = 0.0
        start = group * (group_size + 2) * HD
        for member in range(group_size):
            head = group * group_size + member
            here = slice(head * HD, (head + 1) * HD)
            out_grad, query, prob = attended[:, here], queries[:, here], probs[head]
            prob_grad = dot(out_grad, value, ((1,), (1,)))
            prob_f = prob.astype(f32)
            inner = jnp.sum(prob_f * prob_grad, axis=-1, keepdims=True)
            score_grad = (prob_f * (prob_grad - inner)).astype(bf16)
            query_grad = turned(dot(score_grad, key) * scale, cosine_tab, sine_tab)
            put(start + member * HD, query_grad.astype(bf16))
            key_grad = key_grad + dot(score_grad, query, ((0,), (0,)))
            value_grad = value_grad + dot(prob, out_grad, ((0,), (0,)))
        key_grad = turned(key_grad * scale, cosine_tab, sine_tab)
        put(start + group_size * HD, key_grad.astype(bf16))
        put(start + (group_size + 1) * HD, value_grad.astype(bf16))


def first_back_kernel(at, back, weight, tokens, gain, resid_grad, tokens_ref, gain_ref):
    f32 = jnp.float32
    parts = back.shape[0]
    cols = weight.shape[0] * weight.shape[2] // parts
    first_grad = 0.0
    for part in range(parts):
        group, place = divmod(part * cols, weight.shape[2])
        first_grad = first_grad + dot(
            back[part, :, :cols], weight[group, :, place : place + cols], ((1,), (1,))
        )
    norm_grad, gain_grad = rms_back(tokens[...].astype(f32), gain[...], first_grad)
    gain_ref[...] = gain_grad
    tokens_ref[...] = (resid_grad[...] + norm_grad).astype(jnp.bfloat16)


def dense_grad_kernel(at, back, *refs):
    pieces, out_ref, held, sems = refs[:8], refs[8], refs[9], refs[10]
    copies = [
        pltpu.make_async_copy(piece, held.at[n], sems.at[n]) for n, piece in enumerate(pieces)
    ]
    for copy in copies:
        copy.start()
    depth, rows, cols = out_ref.shape
    length = held.shape[1] // 2
    qkv_width = cols - held.shape[2] // back.shape[0]
    narrow = sum(back[place, length:].astype(jnp.float32) for place in range(back.shape[0]))
    sums = [0.0, 0.0]
    for n, copy in enumerate(copies):
        copy.wait()
        dc, dy, dx = n // 4, n // 2 % 2, n % 2
        place = 4 * (at[0] ^ dy) + 2 * (at[1] ^ dc) + (at[2] ^ dx)
        own = back[place, :length]
        sums[0] = sums[0] + dot(held[n, length:], own[:, :qkv_width], ((0,), (0,)))
        sums[1] = sums[1] + dot(held[n, :length], own[:, qkv_width:], ((0,), (0,)))
    wide = held.shape[2] // depth
    each = narrow.shape[0] // depth
    for z in range(depth):
        here = slice(z * wide, (z + 1) * wide)
        both = jnp.concatenate([part[here] for part in sums], axis=1)
        out_ref[z, :wide] = both.astype(jnp.bfloat16)
        kept = [narrow[z * each : (z + 1) * each], jnp.zeros((rows - wide - each, cols), jnp.float32)]
        out_ref[z, wide:] = jnp.concatenate(kept, axis=0).astype(jnp.bfloat16)


def local_pairs(
    tokens,
    norm1_gain,
    w_query,
    w_key,
    w_value,
    w_out,
    norm2_gain,
    w_router,
    w_gate,
    w_up,
    w_down,
    expert_ids,
    prefix_len,
    out_grad,
):
    bf16, f32 = jnp.bfloat16, jnp.float32
    length, model_width = tokens.shape
    shard_rows = w_query.shape[0]
    local_count, _, hidden_width = w_gate.shape
    owners = lax.axis_size("x")
    depth = lax.axis_size("z")
    plane = lax.axis_size(PLANE)
    experts_all = w_router.shape[1]
    block_rows = length // MICRO
    capacity = 3 * block_rows * expert_ids.shape[1] // (2 * experts_all)
    plane_rows = plane * length
    blocks = plane_rows // block_rows
    q_cols, kv_cols = w_query.shape[1], w_key.shape[1]
    qkv_cols = q_cols + 2 * kv_cols
    q_group, out_half = q_cols // HK, model_width // 2
    y, c, x, z = (lax.axis_index(axis) for axis in ("y", "c", "x", "z"))
    own_local = 2 * y + c
    own_expert = x * local_count + own_local
    at = jnp.stack([y, c, x, z, prefix_len[0], own_expert, own_local])

    own_half = jnp.concatenate(
        [
            lax.dynamic_slice_in_dim(part, x * (part.shape[1] // 2), part.shape[1] // 2, 1)
            for part in (w_query, w_key, w_value, w_out)
        ],
        axis=1,
    )
    narrow = jnp.concatenate([w_router, norm1_gain[:, None], norm2_gain[:, None]], axis=1)
    narrow = small_group_gather(narrow)
    ids_all = small_gather(expert_ids)
    column = [own_half] + shifts(own_half)
    cot_sides = plane_sides(after(out_grad, narrow, ids_all))
    qkv_half = qkv_cols // 2
    qkv_column = jnp.stack([part[:, :qkv_half] for part in column])
    out_column = jnp.stack([part[:, qkv_half:] for part in column])
    gate_w, up_w, down_w = (
        lax.dynamic_index_in_dim(weight, own_local, 0, keepdims=False)
        for weight in (w_gate, w_up, w_down)
    )
    qkv_column, out_column, gate_w, up_w, down_w = lax.optimization_barrier(
        (qkv_column, out_column, gate_w, up_w, down_w, *cot_sides)
    )[:5]
    qkv_sides = plane_sides(qkv_column)
    qkv_corner = plane_corner(qkv_sides)
    out_sides = plane_sides(after(out_column, qkv_corner))
    qkv_pieces = plane_pieces(qkv_column, qkv_sides, qkv_corner)
    router_w = jnp.pad(narrow[:, :experts_all], ((0, 0), (0, 128 - experts_all)))
    gains = narrow[:, experts_all : experts_all + 2].T.astype(f32)
    gain_one, gain_two = gains[:1], gains[1:]

    ids_turned = ids_all.T
    gain_one, ids_all, ids_turned, router_w = lax.optimization_barrier(
        (gain_one, ids_all, ids_turned, router_w)
    )

    cosine_tab, sine_tab = angles(length, HD)
    cosine_all = jnp.concatenate([cosine_tab, cosine_tab], axis=2)[:, 0]
    sine_all = jnp.concatenate([-sine_tab, sine_tab], axis=2)[:, 0]
    weight_lead = (2, depth, 2, 2, shard_rows)
    first_in, queries, keys_rot, values_b, attended, probs, qkv_w = run_kernel(
        attend_kernel,
        11,
        at,
        (tokens, gain_one, cosine_all, sine_all, *qkv_pieces),
        [
            ((length, model_width), bf16),
            ((length, q_cols), bf16),
            ((length, kv_cols), bf16),
            ((length, kv_cols), bf16),
            ((length, q_cols), bf16),
            ((HQ, length, length), bf16),
            (weight_lead + (qkv_half,), bf16),
        ],
        48,
        [
            pltpu.VMEM((HQ, length, length), bf16),
            pltpu.VMEM(weight_lead + (qkv_half,), bf16),
            pltpu.SemaphoreType.DMA((HK + 1,)),
        ],
        hbm_out=2,
    )
    out_sides = lax.optimization_barrier((*out_sides, attended))[:2]
    out_corner = plane_corner(out_sides)
    cot_corner = plane_corner(cot_sides)
    out_pieces = plane_pieces(out_column, out_sides, out_corner)
    cot_pieces = plane_pieces(out_grad, cot_sides, cot_corner)
    resid, second_in, output_w = run_kernel(
        project_kernel,
        4,
        at,
        (tokens, after(gain_two, cot_corner), attended, *out_pieces),
        [
            ((length, model_width), f32),
            ((length, model_width), bf16),
            (weight_lead + (out_half,), bf16),
        ],
        50,
        [pltpu.VMEM(weight_lead + (out_half,), bf16), pltpu.SemaphoreType.DMA],
        hbm_out=1,
    )
    qkv_w = qkv_w.reshape(HK, model_width, qkv_half)
    output_w = output_w.reshape(2, q_cols, out_half)

    expert = functools.partial(
        run_expert,
        at=at,
        ids=ids_all,
        ids_turned=ids_turned,
        router=router_w,
        weights=(gate_w, up_w, down_w),
        capacity=capacity,
    )
    second_sides = plane_sides(second_in)
    groups = ((0, 4), (1, 5, 2, 6), (3, 7))
    second_pieces = {0: second_in, 4: swap(second_in, "c")}

    def run_group(pieces):
        return expert(
            pieces,
            second=[second_pieces[piece] for piece in pieces],
            cot=[cot_pieces[piece] for piece in pieces],
        )

    stage_own = run_group(groups[0])
    second_sides = lax.optimization_barrier((*second_sides, stage_own[0]))[:2]
    for piece, block in zip((1, 2), second_sides):
        second_pieces[piece], second_pieces[piece + 4] = block, swap(block, "c")
    stage_sides = run_group(groups[1])
    second_corner = plane_corner(second_sides, later=(stage_sides[0],))
    second_pieces[3], second_pieces[7] = second_corner, swap(second_corner, "c")
    own_near, own_far = stage_own[6:]
    own_far = swap(own_far, "c")
    x_near, x_far, y_near, y_far = stage_sides[6:]
    back_x, back_y = over_core(x_near, x_far), over_core(y_near, y_far)
    first_x, first_y = early_sums(back_x, back_y)
    stage_corner = run_group(groups[2])
    corner = over_core(*stage_corner[6:])
    passed = corner_first(corner)
    stages = (stage_own, stage_sides, stage_corner)
    rows_in, rows_cot, gated, gate_back, up_back = ([stage[n] for stage in stages] for n in range(5))
    gates = stage_own[5]
    (down_part,) = row_sums(at, [after(rows_cot[0], corner)] + rows_cot[1:], gated)
    down_sum = scatter_sum(down_part, "z")
    passed = lax.optimization_barrier((*passed, down_part))[:2]
    last_y, last_x, sent = corner_last(back_x, back_y, passed)
    gate_part, up_part = row_sums(
        at, [after(rows_in[0], sent)] + rows_in[1:], gate_back, up_back
    )
    gate_sum, up_sum = scatter_sum(gate_part, "z"), scatter_sum(up_part, "z")
    own_near = after(own_near, gate_part)

    resid_grad, branch_grad, attended_grad, router_acc, gain_two_grad = run_kernel(
        branch_back_kernel,
        6,
        at,
        (
            own_near,
            own_far,
            first_x,
            first_y,
            last_y,
            last_x,
            resid,
            gain_two,
            second_in,
            gates,
            router_w,
            out_grad,
            output_w,
        ),
        [
            ((length, model_width), f32),
            ((length, model_width), bf16),
            ((length, q_cols), bf16),
            ((model_width, 128), f32),
            ((1, model_width), f32),
        ],
    )
    qkv_width, branch_width = qkv_cols // plane, model_width // plane
    dense_cols = qkv_width + branch_width
    (back_cols,) = run_kernel(
        attend_back_kernel,
        6,
        at,
        (
            attended_grad,
            probs,
            queries,
            keys_rot,
            values_b,
            cosine_all,
            sine_all,
            branch_grad,
        ),
        [((plane, length, dense_cols), bf16)],
    )
    tokens_grad, gain_one_grad = run_kernel(
        first_back_kernel,
        5,
        at,
        (back_cols, qkv_w, tokens, gain_one, resid_grad),
        [((length, model_width), bf16), ((1, model_width), f32)],
        24,
    )

    both = jnp.concatenate(
        lax.optimization_barrier((attended, first_in, resid_grad))[:2], axis=0
    )
    both_sides = plane_sides(both)
    narrow_part = jnp.concatenate(
        [router_acc[:, :experts_all], gain_one_grad.T, gain_two_grad.T], axis=1
    )
    narrow_cols = -(-narrow_part.shape[1] // owners) * owners
    narrow_part = jnp.pad(narrow_part, ((0, 0), (0, narrow_cols - narrow_part.shape[1])))
    narrow_part = jnp.transpose(
        narrow_part.reshape(depth, 2, 2, shard_rows, owners, narrow_cols // owners),
        (1, 2, 4, 0, 3, 5),
    ).reshape(plane, depth, shard_rows * narrow_cols // owners)
    narrow_len = narrow_part.shape[2]
    narrow_rows = -(-narrow_len // dense_cols)
    each_rows = -(-narrow_rows // 4) * 4
    narrow_part = jnp.pad(
        narrow_part, ((0, 0), (0, 0), (0, each_rows * dense_cols - narrow_len))
    ).reshape(plane, depth * each_rows, dense_cols)
    back_cols = jnp.concatenate([back_cols, narrow_part.astype(bf16)], axis=1)
    back_cols = exchange(after(back_cols, down_sum), PLANE)
    both_corner = plane_corner(both_sides, (back_cols,))
    both_pieces = plane_pieces(both, both_sides, both_corner)
    kept_rows = -(-narrow_rows // 16) * 16
    wide_rows = local_count * shard_rows
    dense_shape = (depth, wide_rows + kept_rows, dense_cols)
    dense_part = pl.pallas_call(
        dense_grad_kernel,
        out_shape=jax.ShapeDtypeStruct(dense_shape, bf16),
        in_specs=[SCALARS, WHOLE] + [IN_HBM] * 8,
        out_specs=WHOLE,
        scratch_shapes=[
            pltpu.VMEM((plane, 2 * length, model_width), bf16),
            pltpu.SemaphoreType.DMA((plane,)),
        ],
        cost_estimate=cost(8),
        compiler_params=pltpu.CompilerParams(vmem_limit_bytes=32 * 2**20),
    )(at, after(back_cols, gate_sum), *both_pieces)
    dense_part = after(dense_part, up_sum)
    dense_sum = scatter_sum(dense_part.reshape(-1, dense_cols), "z")
    wide_sum = dense_sum[: local_count * shard_rows].reshape(2, 2, 1, shard_rows, dense_cols)
    wide_sum = jnp.broadcast_to(wide_sum, (2, 2, owners, shard_rows, dense_cols)).reshape(
        plane, shard_rows, dense_cols
    )
    narrow_sum = dense_sum[local_count * shard_rows :][:narrow_rows]
    narrow_sum = jnp.broadcast_to(narrow_sum[None], (plane, narrow_rows, dense_cols))
    pad_rows = -(shard_rows + narrow_rows) % 16
    padding = jnp.zeros((plane, pad_rows, dense_cols), bf16)
    dense_sum = exchange(jnp.concatenate([wide_sum, narrow_sum, padding], axis=1), PLANE)
    wide_sum = jnp.moveaxis(dense_sum[:, :shard_rows].astype(f32), 0, 1)
    qkv_sum = wide_sum[:, :, :qkv_width].reshape(shard_rows, HK, qkv_half)
    output_sum = wide_sum[:, :, qkv_width:].reshape(shard_rows, model_width)
    narrow_sum = dense_sum[:, shard_rows : shard_rows + narrow_rows].reshape(
        2, 2, owners, narrow_rows * dense_cols
    )
    narrow_sum = narrow_sum[y, c, :, :narrow_len].reshape(owners, shard_rows, -1)
    narrow_sum = jnp.moveaxis(narrow_sum, 0, 1).reshape(shard_rows, narrow_cols).astype(f32)

    shares = run_kernel(
        functools.partial(mixture_kernel, capacity, groups),
        10,
        at,
        (ids_turned, after(gated[0], both_corner), *gated[1:], down_w),
        [((length, model_width), bf16)] * plane,
        24,
    )
    mixed = [over_core(near, far) for near, far in zip(shares[:4], shares[4:])]
    early = early_sums(mixed[1], mixed[2])
    last = corner_last(mixed[1], mixed[2], corner_first(mixed[3]))[:2]
    mixture = jnp.concatenate(
        [left.astype(f32) + right.astype(f32) for left, right in zip(early, last)], axis=0
    )
    block_out = (resid + (mixture + mixed[0].astype(f32))).astype(bf16)

    def placed(total):
        total = exchange(total, ("y", "c"))
        return total.reshape(local_count, shard_rows, hidden_width).astype(f32)

    return (
        block_out,
        tokens_grad,
        narrow_sum[:, experts_all],
        qkv_sum[:, :, :q_group].reshape(shard_rows, q_cols),
        qkv_sum[:, :, q_group : q_group + HD].reshape(shard_rows, kv_cols),
        qkv_sum[:, :, q_group + HD :].reshape(shard_rows, kv_cols),
        output_sum,
        narrow_sum[:, experts_all + 1],
        narrow_sum[:, :experts_all],
        placed(gate_sum),
        placed(up_sum),
        jnp.swapaxes(placed(down_sum), 1, 2),
    )


def solution(mesh):
    groups, owners = mesh.shape["dp"], mesh.shape["expert"]
    grid = jax.sharding.Mesh(
        mesh.devices.reshape(groups // 4, 2, 2, owners), ("z", "y", "c", "x")
    )
    rows = P(("z", "y", "c", "x"), None)
    shard, shard_rows = P(GROUP), P(GROUP, None)
    expert = P("x", None, None)
    return jax.shard_map(
        local_pairs if owners == 2 else local_wide,
        mesh=grid,
        in_specs=(
            rows,
            shard,
            shard_rows,
            shard_rows,
            shard_rows,
            shard_rows,
            shard,
            shard_rows,
            expert,
            expert,
            expert,
            rows,
            P(("z", "y", "c", "x")),
            rows,
        ),
        out_specs=(
            rows,
            rows,
            shard,
            shard_rows,
            shard_rows,
            shard_rows,
            shard_rows,
            shard,
            shard_rows,
            P("x", GROUP, None),
            P("x", GROUP, None),
            P("x", None, GROUP),
        ),
        check_vma=False,
    )
```

```python
import functools
import math

import jax
import jax.numpy as jnp
from jax import lax
from jax.experimental import pallas as pl
from jax.experimental.pallas import tpu as pltpu
from jax.sharding import PartitionSpec as P

HQ = 12
HK = 2
HD = 128
MICRO = 2
PLANE = ("y", "c", "x")
GROUP = ("z", "y", "c")


def rms_scale(values, gain_vec):
    inverse = lax.rsqrt(jnp.mean(values * values, axis=-1, keepdims=True) + 1e-06)
    return values * inverse * gain_vec


def angles(length, head_size):
    positions = jnp.arange(length).astype(jnp.float32)
    freq_rates = jnp.exp(
        -(2.0 * jnp.arange(head_size // 2).astype(jnp.float32) / head_size) * math.log(1000000.0)
    )
    angle_tab = positions[:, None] * freq_rates[None, :]
    return (jnp.cos(angle_tab)[:, None, :], jnp.sin(angle_tab)[:, None, :])


def rotary(values, cosine_tab, sine_tab):
    half_dim = values.shape[-1] // 2
    first_half = values[..., :half_dim]
    second_half = values[..., half_dim:]
    return jnp.concatenate(
        [
            first_half * cosine_tab - second_half * sine_tab,
            second_half * cosine_tab + first_half * sine_tab,
        ],
        axis=-1,
    )


def expert_act(gate_pre, up_pre):
    return jax.nn.gelu(gate_pre, approximate=True) * up_pre


def left_product(left_mat, right_mat):
    return lax.dot_general(
        left_mat, right_mat, (((0,), (0,)), ((), ())), preferred_element_type=jnp.float32
    )


def gather(block, axes):
    return lax.all_gather(block, axes, axis=0, tiled=True)


def exchange(block, axes):
    return lax.all_to_all(block, axes, split_axis=0, concat_axis=0, tiled=True)


def scatter_sum(block, axes):
    return lax.psum_scatter(block, axes, scatter_dimension=0, tiled=True)


def by_owner(cols, parts):
    rows, total = cols.shape
    return jnp.moveaxis(cols.reshape(rows, parts, total // parts), 1, 0).reshape(
        parts * rows, total // parts
    )


def local_wide(
    tokens,
    norm1_gain,
    w_query,
    w_key,
    w_value,
    w_out,
    norm2_gain,
    w_router,
    w_gate,
    w_up,
    w_down,
    expert_ids,
    prefix_len,
    out_grad,
):
    bf16, f32 = jnp.bfloat16, jnp.float32
    length, model_width = tokens.shape
    shard_rows = w_query.shape[0]
    local_count, _, hidden_width = w_gate.shape
    owners = lax.axis_size("x")
    depth = lax.axis_size("z")
    plane = lax.axis_size(PLANE)
    experts_all = w_router.shape[1]
    top_count = expert_ids.shape[1]
    block_rows = length // MICRO
    capacity = 3 * block_rows * top_count // (2 * experts_all)
    plane_rows = plane * length
    blocks = plane_rows // block_rows
    group_size = HQ // HK
    score_scale = HD ** (-0.5)
    q_cols, kv_cols = w_query.shape[1], w_key.shape[1]
    own_local = lax.axis_index(("y", "c"))
    own_expert = lax.axis_index("x") * local_count + own_local
    own_place = lax.axis_index(PLANE)

    narrow = jnp.concatenate([w_router, norm1_gain[:, None], norm2_gain[:, None]], axis=1)
    narrow = jnp.pad(narrow, ((0, 0), (0, -narrow.shape[1] % 128)))
    packed = gather(jnp.concatenate([w_query, w_key, w_value, narrow], axis=1), GROUP)
    qkv_cols = q_cols + 2 * kv_cols
    qkv_w = packed[:, :qkv_cols]
    router_w = packed[:, qkv_cols : qkv_cols + experts_all]
    gains = packed[:, qkv_cols + experts_all : qkv_cols + experts_all + 2].T.astype(f32)
    gain_one, gain_two = gains[0], gains[1]
    output_w = gather(w_out, GROUP)

    ids_all = gather(expert_ids, PLANE)
    cot_all = gather(out_grad, PLANE)
    chosen_mask = jnp.any(
        ids_all[:, :, None] == jnp.arange(experts_all, dtype=jnp.int32)[None, None, :], axis=1
    )
    own_mask = jnp.any(ids_all == own_expert, axis=1).reshape(blocks, block_rows)
    place = jnp.cumsum(own_mask.astype(jnp.int32), axis=1) - 1
    dispatch = (
        own_mask[:, None, :]
        & (place[:, None, :] == jnp.arange(capacity, dtype=jnp.int32)[None, :, None])
    ).astype(bf16)

    cosine_tab, sine_tab = angles(length, HD)
    inputs_f = tokens.astype(f32)
    first_in = rms_scale(inputs_f, gain_one).astype(bf16)
    qkv = jnp.dot(first_in, qkv_w, preferred_element_type=f32)
    queries = (
        rotary(qkv[:, :q_cols].reshape(length, HQ, HD), cosine_tab, sine_tab)
        .astype(bf16)
        .reshape(length, HK, group_size, HD)
    )
    keys_rot = rotary(
        qkv[:, q_cols : q_cols + kv_cols].reshape(length, HK, HD), cosine_tab, sine_tab
    ).astype(bf16)
    values_b = qkv[:, q_cols + kv_cols :].astype(bf16).reshape(length, HK, HD)
    positions = jnp.arange(length)
    allowed = (positions[None, :] <= positions[:, None]) | (positions[None, :] < prefix_len[0])

    def masked_scores():
        scores = jnp.einsum("ihrd,jhd->hrij", queries, keys_rot, preferred_element_type=f32)
        return jnp.where(allowed, scores * score_scale, -1e30)

    masked = masked_scores()
    row_peak = jnp.max(masked, axis=-1, keepdims=True)
    log_total = row_peak + jnp.log(jnp.sum(jnp.exp(masked - row_peak), axis=-1, keepdims=True))
    prob_bf = jnp.exp(masked - log_total).astype(bf16)
    attended = jnp.einsum("hrij,jhd->ihrd", prob_bf, values_b, preferred_element_type=f32)
    attended = attended.reshape(length, HQ * HD).astype(bf16)
    resid = inputs_f + jnp.dot(attended, output_w, preferred_element_type=f32)
    second_in = rms_scale(resid, gain_two).astype(bf16)

    second_all = gather(second_in, PLANE)
    logits = jnp.dot(second_all, router_w, preferred_element_type=f32)
    gates_all = jax.nn.softmax(jnp.where(chosen_mask, logits, -jnp.inf), axis=-1)
    own_gates = lax.dynamic_index_in_dim(gates_all, own_expert, 1, keepdims=False)
    own_gates = own_gates.reshape(blocks, block_rows)
    gate_rows = jnp.einsum(
        "bct,bt->bc", dispatch.astype(f32), own_gates, precision=lax.Precision.HIGHEST
    )[:, :, None]
    gate_w = lax.dynamic_index_in_dim(w_gate, own_local, 0, keepdims=False)
    up_w = lax.dynamic_index_in_dim(w_up, own_local, 0, keepdims=False)
    down_w = lax.dynamic_index_in_dim(w_down, own_local, 0, keepdims=False)

    def to_rows(array):
        return jnp.einsum(
            "bct,btd->bcd",
            dispatch,
            array.reshape(blocks, block_rows, model_width),
            preferred_element_type=f32,
        ).astype(bf16)

    def to_tokens(rows):
        return (
            jnp.einsum("bct,bcd->btd", dispatch, rows.astype(bf16), preferred_element_type=f32)
            .astype(bf16)
            .reshape(plane_rows, model_width)
        )

    rows_in = to_rows(second_all)
    rows_cot = to_rows(cot_all)
    gate_pre = jnp.einsum("bcd,df->bcf", rows_in, gate_w, preferred_element_type=f32)
    up_pre = jnp.einsum("bcd,df->bcf", rows_in, up_w, preferred_element_type=f32)
    hidden, act_pull = jax.vjp(expert_act, gate_pre, up_pre)
    gated = (gate_rows * hidden).astype(bf16)
    down_part = jnp.einsum("bcd,bcf->df", rows_cot, gated, preferred_element_type=f32)
    down_sum = scatter_sum(down_part.astype(bf16), "z")
    cot_hidden = jnp.einsum("bcd,fd->bcf", rows_cot, down_w, preferred_element_type=f32)
    gate_signal_rows = jnp.sum(hidden * cot_hidden, axis=-1)
    gate_pgrad, up_pgrad = act_pull(gate_rows * cot_hidden)
    gate_pgrad = gate_pgrad.astype(bf16)
    up_pgrad = up_pgrad.astype(bf16)
    gate_part = jnp.einsum("bcd,bcf->df", rows_in, gate_pgrad, preferred_element_type=f32)
    gate_sum = scatter_sum(gate_part.astype(bf16), "z")
    up_part = jnp.einsum("bcd,bcf->df", rows_in, up_pgrad, preferred_element_type=f32)
    up_sum = scatter_sum(up_part.astype(bf16), "z")
    rows_grad = jnp.einsum("bcf,df->bcd", gate_pgrad, gate_w, preferred_element_type=f32)
    rows_grad = rows_grad + jnp.einsum("bcf,df->bcd", up_pgrad, up_w, preferred_element_type=f32)
    second_back = scatter_sum(to_tokens(rows_grad), PLANE).astype(f32)
    gate_signal = jnp.einsum(
        "bct,bc->bt", dispatch.astype(f32), gate_signal_rows, precision=lax.Precision.HIGHEST
    )
    gate_signal = exchange(gate_signal.reshape(plane, length), PLANE)
    gate_signal = jnp.transpose(
        gate_signal.reshape(local_count, owners, length), (2, 1, 0)
    ).reshape(length, experts_all)
    expert_rows = jnp.einsum("bcf,fd->bcd", gated, down_w, preferred_element_type=f32)
    mixture = scatter_sum(to_tokens(expert_rows), PLANE).astype(f32)
    block_out = (resid + mixture).astype(bf16)

    cotangent = out_grad.astype(f32)
    gate_probs = lax.dynamic_slice_in_dim(gates_all, own_place * length, length, 0)
    logit_grad = (
        gate_probs
        * (gate_signal - jnp.sum(gate_probs * gate_signal, axis=-1, keepdims=True))
    ).astype(bf16)
    router_acc = left_product(second_in, logit_grad)
    second_grad = second_back + jnp.dot(logit_grad, router_w.T, preferred_element_type=f32)
    _, norm_two_pull = jax.vjp(rms_scale, resid, gain_two)
    resid_norm_grad, gain_two_grad = norm_two_pull(second_grad)
    resid_grad = cotangent + resid_norm_grad
    branch_grad = resid_grad.astype(bf16)

    attended_all = gather(attended, PLANE)
    branch_cols = exchange(by_owner(branch_grad, plane), PLANE)
    output_part = left_product(attended_all, branch_cols)
    attended_grad = jnp.dot(branch_grad, output_w.T, preferred_element_type=f32).astype(bf16)
    attended_grad = attended_grad.reshape(length, HK, group_size, HD)
    masked = masked_scores()
    prob_full = jnp.exp(masked - log_total)
    prob_bf = prob_full.astype(bf16)
    prob_grad = jnp.einsum("ihrd,jhd->hrij", attended_grad, values_b, preferred_element_type=f32)
    row_inner = jnp.sum(prob_full * prob_grad, axis=-1, keepdims=True)
    score_grad = (prob_full * (prob_grad - row_inner)).astype(bf16)
    query_rot_grad = (
        jnp.einsum("hrij,jhd->ihrd", score_grad, keys_rot, preferred_element_type=f32)
        * score_scale
    )
    query_back = rotary(query_rot_grad.reshape(length, HQ, HD), cosine_tab, -sine_tab)
    query_back = query_back.astype(bf16).reshape(length, HQ * HD)
    key_rot_grad = (
        jnp.einsum("hrij,ihrd->jhd", score_grad, queries, preferred_element_type=f32)
        * score_scale
    )
    key_back = rotary(key_rot_grad, cosine_tab, -sine_tab).astype(bf16).reshape(length, HK * HD)
    value_back = jnp.einsum("hrij,ihrd->jhd", prob_bf, attended_grad, preferred_element_type=f32)
    value_back = value_back.astype(bf16).reshape(length, HK * HD)
    qkv_back = jnp.concatenate([query_back, key_back, value_back], axis=1)
    first_all = gather(first_in, PLANE)
    qkv_part = left_product(first_all, exchange(by_owner(qkv_back, plane), PLANE))
    first_grad = lax.dot_general(
        qkv_back, qkv_w, (((1,), (1,)), ((), ())), preferred_element_type=f32
    )
    _, norm_one_pull = jax.vjp(rms_scale, inputs_f, gain_one)
    input_norm_grad, gain_one_grad = norm_one_pull(first_grad)
    tokens_grad = (resid_grad + input_norm_grad).astype(bf16)

    narrow_part = jnp.concatenate(
        [router_acc, gain_one_grad[:, None], gain_two_grad[:, None]], axis=1
    ).astype(bf16)
    narrow_cols = narrow_part.shape[1]
    narrow_sum = lax.psum(scatter_sum(narrow_part, GROUP), "x").astype(f32)
    dense_part = jnp.concatenate([qkv_part, output_part], axis=1).astype(bf16)
    dense_sum = scatter_sum(dense_part, "z")
    dense_cols = dense_sum.shape[1]
    dense_sum = gather(dense_sum, PLANE).reshape(plane, local_count, shard_rows, dense_cols)
    dense_sum = lax.dynamic_index_in_dim(dense_sum, own_local, 1, keepdims=False).astype(f32)
    dense_sum = jnp.moveaxis(dense_sum, 0, 1)
    qkv_width = qkv_cols // plane
    qkv_sum = dense_sum[:, :, :qkv_width].reshape(shard_rows, qkv_cols)
    output_sum = dense_sum[:, :, qkv_width:].reshape(shard_rows, model_width)

    def placed(total):
        total = exchange(total, ("y", "c"))
        return total.reshape(local_count, shard_rows, hidden_width).astype(f32)

    return (
        block_out,
        tokens_grad,
        narrow_sum[:, experts_all],
        qkv_sum[:, :q_cols],
        qkv_sum[:, q_cols : q_cols + kv_cols],
        qkv_sum[:, q_cols + kv_cols :],
        output_sum,
        narrow_sum[:, experts_all + 1],
        narrow_sum[:, :experts_all],
        placed(gate_sum),
        placed(up_sum),
        jnp.swapaxes(placed(down_sum), 1, 2),
    )


def rounded(values):
    return lax.reduce_precision(values, 8, 7).astype(jnp.bfloat16)


def after(block, *others):
    return lax.optimization_barrier((block,) + others)[0]


def swap(block, axis):
    return lax.ppermute(block, axis, [(0, 1), (1, 0)])


def shifts(block):
    depth = lax.axis_size("z")
    return [
        lax.ppermute(block, "z", [(i, (i + k) % depth) for i in range(depth)])
        for k in range(1, depth)
    ]


def plane_sides(block):
    return swap(block, "x"), swap(block, "y")


def plane_corner(sides, before=(), later=()):
    over_x, over_y = sides
    half = over_x.shape[0] // 2
    over_y, over_x = lax.optimization_barrier((over_y[:half], over_x[half:]) + before)[:2]
    parts = (swap(over_y, "x"), swap(over_x, "y"))
    return jnp.concatenate(lax.optimization_barrier(parts + later)[:2], axis=0)


def plane_pieces(block, sides=None, corner=None):
    sides = plane_sides(block) if sides is None else sides
    corner = plane_corner(sides) if corner is None else corner
    pieces = [block, *sides, corner]
    return pieces + [swap(piece, "c") for piece in pieces]


def small_gather(block):
    for axis in ("x", "y", "c"):
        block = jnp.concatenate([block, swap(block, axis)], axis=1)
    return block


def small_group_gather(block):
    depth = lax.axis_size("z")
    order = jnp.stack(([block] + shifts(block))[::-1] * 2)
    start = (depth - 1 - lax.axis_index("z")) % depth
    total = lax.dynamic_slice_in_dim(order, start, depth, 0)[:, None, None]
    for dim, axis in ((1, "y"), (2, "c")):
        other = swap(total, axis)
        last = lax.axis_index(axis) == 1
        pair = [jnp.where(last, other, total), jnp.where(last, total, other)]
        total = jnp.concatenate(pair, axis=dim)
    return total.reshape(-1, block.shape[1])


def add(left, right):
    return rounded(left.astype(jnp.float32) + right.astype(jnp.float32))


def over_core(near, far):
    return add(near, swap(far, "c"))


def early_sums(over_x, over_y):
    half = over_x.shape[0] // 2
    return swap(over_x[:half], "x"), swap(over_y[half:], "y")


def corner_first(corner):
    half = corner.shape[0] // 2
    return swap(corner[:half], "x"), swap(corner[half:], "y")


def corner_last(over_x, over_y, first):
    half = over_x.shape[0] // 2
    over_y, over_x = add(over_y[:half], first[0]), add(over_x[half:], first[1])
    return swap(over_y, "y"), swap(over_x, "x"), over_x


def cost(micros):
    return pl.CostEstimate(flops=micros * 10**9, bytes_accessed=micros * 10**6, transcendentals=0)


def dot(left, right, dims=((1,), (0,)), precision=None):
    return lax.dot_general(
        left, right, (dims, ((), ())), precision=precision, preferred_element_type=jnp.float32
    )


WHOLE = pl.BlockSpec(memory_space=pltpu.VMEM)
IN_HBM = pl.BlockSpec(memory_space=pltpu.HBM)
SCALARS = pl.BlockSpec(memory_space=pltpu.SMEM)


def run_kernel(kernel, micros, at, operands, outs, megabytes=16, scratch=(), hbm_in=0, hbm_out=0):
    return pl.pallas_call(
        kernel,
        out_shape=[jax.ShapeDtypeStruct(shape, dtype) for shape, dtype in outs],
        in_specs=[SCALARS] + [WHOLE] * (len(operands) - hbm_in) + [IN_HBM] * hbm_in,
        out_specs=[WHOLE] * (len(outs) - hbm_out) + [IN_HBM] * hbm_out,
        scratch_shapes=scratch,
        cost_estimate=cost(micros),
        compiler_params=pltpu.CompilerParams(vmem_limit_bytes=megabytes * 2**20),
    )(at, *operands)


def place_pieces(at, refs, weight):
    depth = weight.shape[1]
    for n, ref in enumerate(refs):
        dc, dy, dx = n // 4, n // 2 % 2, n % 2
        for k in range(depth):
            z = lax.rem(at[3] + depth - k, depth)
            weight[at[2] ^ dx, z, at[0] ^ dy, at[1] ^ dc] = ref[k]


def rms_kernel(values, gain):
    inverse = lax.rsqrt(jnp.mean(values * values, axis=-1, keepdims=True) + 1e-06)
    return (values * inverse * gain).astype(jnp.bfloat16)


def rms_back(values, gain, grad):
    inverse = lax.rsqrt(jnp.mean(values * values, axis=-1, keepdims=True) + 1e-06)
    normed = values * inverse
    gain_grad = jnp.sum(grad * normed, axis=0, keepdims=True)
    grad = grad * gain
    along = jnp.mean(grad * normed, axis=-1, keepdims=True)
    return inverse * (grad - normed * along), gain_grad


def turned(values, cosine_tab, sine_tab):
    return values * cosine_tab + pltpu.roll(values, HD // 2, 1) * sine_tab


def attend_kernel(at, tokens, gain, cosine, sine, *refs):
    first_ref, query_ref, key_ref, value_ref, out_ref = refs[8:13]
    prob_out, weight_out, prob_ref, weight, sems = refs[13:]
    place_pieces(at, refs[:8], weight)
    copies = [pltpu.make_async_copy(weight, weight_out, sems.at[HK])]
    copies[0].start()
    length = tokens.shape[0]
    first_in = rms_kernel(tokens[...].astype(jnp.float32), gain[...])
    first_ref[...] = first_in
    rows = lax.broadcasted_iota(jnp.int32, (length, length), 0)
    cols = lax.broadcasted_iota(jnp.int32, (length, length), 1)
    allowed = (cols <= rows) | (cols < at[4])
    cosine_tab, sine_tab = cosine[...], sine[...]
    group_size = HQ // HK
    for group in range(HK):
        matrix = weight[group].reshape(first_in.shape[1], -1)
        qkv = dot(first_in, matrix)
        at_key = group_size * HD
        key = turned(qkv[:, at_key : at_key + HD], cosine_tab, sine_tab).astype(jnp.bfloat16)
        value = qkv[:, at_key + HD :].astype(jnp.bfloat16)
        key_ref[:, group * HD : (group + 1) * HD] = key
        value_ref[:, group * HD : (group + 1) * HD] = value
        for member in range(group_size):
            head = group * group_size + member
            here = slice(head * HD, (head + 1) * HD)
            query = turned(qkv[:, member * HD : (member + 1) * HD], cosine_tab, sine_tab)
            query = query.astype(jnp.bfloat16)
            query_ref[:, here] = query
            scores = dot(query, key, ((1,), (1,)))
            scores = jnp.where(allowed, scores * HD ** (-0.5), -1e30)
            weights = jnp.exp(scores - jnp.max(scores, axis=-1, keepdims=True))
            prob = weights * (1.0 / jnp.sum(weights, axis=-1, keepdims=True))
            prob = prob.astype(jnp.bfloat16)
            prob_ref[head] = prob
            out_ref[:, here] = dot(prob, value).astype(jnp.bfloat16)
        here = pl.ds(group * group_size, group_size)
        copies.append(
            pltpu.make_async_copy(prob_ref.at[here], prob_out.at[here], sems.at[group])
        )
        copies[-1].start()
    for copy in copies:
        copy.wait()


def project_kernel(at, tokens, gain, attended, *refs):
    resid_ref, second_ref, weight_out, weight, sem = refs[8:]
    place_pieces(at, refs[:8], weight)
    copy = pltpu.make_async_copy(weight, weight_out, sem)
    copy.start()
    heads = attended[...]
    halves = [dot(heads, weight[half].reshape(heads.shape[1], -1)) for half in range(2)]
    resid = tokens[...].astype(jnp.float32) + jnp.concatenate(halves, axis=1)
    resid_ref[...] = resid
    second_ref[...] = rms_kernel(resid, gain[...])
    copy.wait()


def one_hot(slots, capacity, dtype):
    shape = (capacity, slots.shape[1])
    return (slots == lax.broadcasted_iota(jnp.int32, shape, 0)).astype(jnp.float32).astype(dtype)


def slots_of(ids, expert, start, rows):
    named = jnp.any(ids[:, start : start + rows] == expert, axis=0, keepdims=True)
    named = named.astype(jnp.float32)
    before = lax.broadcasted_iota(jnp.int32, (rows, rows), 0)
    upto = lax.broadcasted_iota(jnp.int32, (rows, rows), 1)
    counts = dot(named.astype(jnp.bfloat16), (before <= upto).astype(jnp.float32).astype(jnp.bfloat16))
    return jnp.where(named > 0.0, counts - 1.0, -1.0).astype(jnp.int32)


def spread(picks, capacity, rows, outs):
    rows = rows.astype(jnp.bfloat16)
    block = picks[0].shape[1]
    for n in range(len(picks) // 2):
        for part in range(2):
            pick = picks[2 * n + part]
            at_row = (2 * n + part) * capacity
            tokens = dot(pick, rows[at_row : at_row + capacity], ((0,), (0,)))
            outs[n][part * block : (part + 1) * block] = tokens.astype(jnp.bfloat16)


def expert_kernel(capacity, pieces, at, ids, router, *refs):
    count = len(pieces)
    second, cot = refs[:count], refs[count : 2 * count]
    gate_w, up_w, down_w = refs[2 * count : 2 * count + 3]
    rows_in, rows_cot, gated_ref, gate_back, up_back, gates_ref = refs[2 * count + 3 : 2 * count + 9]
    backs, gate_rows = refs[2 * count + 9 : -1], refs[-1]
    f32, bf16 = jnp.float32, jnp.bfloat16
    length, width = second[0].shape
    wide = router.shape[1]
    half = length // 2
    picks = []
    experts = lax.broadcasted_iota(jnp.int32, (wide, length), 0)
    for n, piece in enumerate(pieces):
        tokens = second[n][...]
        named = ids[:, piece * length : (piece + 1) * length]
        chosen = functools.reduce(
            jnp.logical_or, [named[k : k + 1] == experts for k in range(named.shape[0])]
        )
        logits = jnp.where(chosen, dot(router[...], tokens, ((0,), (1,))), -1e30)
        weights = jnp.exp(logits - jnp.max(logits, axis=0, keepdims=True))
        gates = weights * (1.0 / jnp.sum(weights, axis=0, keepdims=True))
        if n == 0:
            gates_ref[...] = gates
        own = jnp.sum(jnp.where(experts == at[5], gates, 0.0), axis=0, keepdims=True)
        for part in range(2):
            here = slice(part * half, (part + 1) * half)
            place = slice((2 * n + part) * capacity, (2 * n + part + 1) * capacity)
            slots = slots_of(ids, at[5], piece * length + part * half, half)
            pick = one_hot(slots, capacity, f32)
            picks.append(pick.astype(bf16))
            rows_in[place] = dot(picks[-1], tokens[here]).astype(bf16)
            rows_cot[place] = dot(picks[-1], cot[n][here]).astype(bf16)
            gate_rows[place] = jnp.sum(pick * own[:, here], axis=1, keepdims=True)
    gate = gate_rows[...]
    gate_pre = dot(rows_in[...], gate_w[...])
    up_pre = dot(rows_in[...], up_w[...])
    cot_hidden = dot(rows_cot[...], down_w[...], ((1,), (1,)))
    scale = math.sqrt(2.0 / math.pi)
    square = gate_pre * gate_pre
    bent = jnp.tanh(scale * gate_pre * (1.0 + 0.044715 * square))
    open_part = 0.5 * (1.0 + bent)
    active = gate_pre * open_part
    slope = open_part + 0.5 * gate_pre * (1.0 - bent * bent) * scale * (
        1.0 + 3 * 0.044715 * square
    )
    hidden = active * up_pre
    gated_ref[...] = (gate * hidden).astype(bf16)
    signal = jnp.sum(hidden * cot_hidden, axis=1, keepdims=True)
    back = gate * cot_hidden
    gate_back[...] = (back * up_pre * slope).astype(bf16)
    up_back[...] = (back * active).astype(bf16)
    high = signal.astype(bf16)
    low = (signal - high.astype(f32)).astype(bf16)
    lanes = lax.broadcasted_iota(jnp.int32, (signal.shape[0], wide), 1)
    signal = jnp.where(lanes == at[5], high.astype(f32), 0.0)
    signal = jnp.where(lanes == at[5] + wide // 2, low.astype(f32), signal)
    by_rows = ((1,), (1,))
    rows = dot(gate_back[...], gate_w[...], by_rows) + dot(up_back[...], up_w[...], by_rows)
    spread(picks, capacity, jnp.concatenate([rows, signal], axis=1), backs)


def run_expert(pieces, at, ids, router, weights, second, cot, capacity):
    count = len(pieces)
    rows, wide = 2 * count * capacity, router.shape[1]
    (length, width), hidden = second[0].shape, weights[0].shape[1]
    bf16, f32 = jnp.bfloat16, jnp.float32
    outs = [(rows, width)] * 2 + [(rows, hidden)] * 3
    outs = [(shape, bf16) for shape in outs] + [((wide, length), f32)]
    outs = outs + [((length, width + wide), bf16)] * count
    return run_kernel(
        functools.partial(expert_kernel, capacity, pieces),
        4 * count,
        at,
        (ids, router, *second, *cot, *weights),
        outs,
        6 + 4 * count,
        [pltpu.VMEM((rows, 1), f32)],
    )


def mixture_kernel(capacity, groups, at, ids, *refs):
    gated, down_w, outs = refs[: len(groups)], refs[len(groups)], refs[len(groups) + 1 :]
    length = outs[0].shape[0]
    for pieces, rows in zip(groups, gated):
        picks = []
        for piece in pieces:
            for part in range(2):
                start = piece * length + part * length // 2
                slots = slots_of(ids, at[5], start, length // 2)
                picks.append(one_hot(slots, capacity, jnp.bfloat16))
        spread(picks, capacity, dot(rows[...], down_w[...]), [outs[piece] for piece in pieces])


def row_sum_kernel(parts, at, *refs):
    arrays = [
        jnp.concatenate([ref[...] for ref in refs[n : n + parts]], axis=0)
        for n in range(0, len(refs) - len(refs) // (parts + 1), parts)
    ]
    outs = refs[len(arrays) * parts :]
    for out, right in zip(outs, arrays[1:]):
        out[...] = dot(arrays[0], right, ((0,), (0,))).astype(jnp.bfloat16)


def row_sums(at, left, *rights):
    operands = [part for parts in (left, *rights) for part in parts]
    outs = [((left[0].shape[1], right[0].shape[1]), jnp.bfloat16) for right in rights]
    kernel = functools.partial(row_sum_kernel, len(left))
    return run_kernel(kernel, 4 * len(rights), at, operands, outs, 24)


def branch_back_kernel(
    at, near, far, first_x, first_y, last_y, last_x, resid, gain, second, gates, router, cot, weight, *outs
):
    resid_grad_ref, branch_ref, attended_ref, router_ref, gain_ref = outs
    f32, bf16 = jnp.float32, jnp.bfloat16
    halves = [first_x[...].astype(f32) + last_y[...], first_y[...].astype(f32) + last_x[...]]
    total = near[...].astype(f32) + far[...] + jnp.concatenate(halves, axis=0)
    width = resid.shape[1]
    signal = total[:, width:]
    signal = signal + pltpu.roll(signal, signal.shape[1] // 2, 1)
    chosen = gates[...].T
    logit_grad = chosen * (signal - jnp.sum(chosen * signal, axis=-1, keepdims=True))
    logit_grad = logit_grad.astype(bf16)
    second_grad = total[:, :width] + dot(logit_grad, router[...], ((1,), (1,)))
    norm_grad, gain_grad = rms_back(resid[...], gain[...], second_grad)
    gain_ref[...] = gain_grad
    resid_grad = cot[...].astype(f32) + norm_grad
    resid_grad_ref[...] = resid_grad
    branch = resid_grad.astype(bf16)
    branch_ref[...] = branch
    wide = weight.shape[2]
    attended_ref[...] = (
        dot(branch[:, :wide], weight[0], ((1,), (1,)))
        + dot(branch[:, wide:], weight[1], ((1,), (1,)))
    ).astype(bf16)
    router_ref[...] = dot(second[...], logit_grad, ((0,), (0,)))


def attend_back_kernel(
    at, attended, probs, queries, keys, values, cosine, sine, branch, back_ref
):
    f32, bf16 = jnp.float32, jnp.bfloat16
    cosine_tab, sine_tab = cosine[...], -sine[...]
    group_size = HQ // HK
    places = back_ref.shape[0]
    branch_width = branch.shape[1] // places
    width = back_ref.shape[2] - branch_width
    for place in range(places):
        here = slice(place * branch_width, (place + 1) * branch_width)
        back_ref[place, :, width:] = branch[:, here]
    scale = HD ** (-0.5)

    def put(position, block):
        back_ref[position // width, :, position % width : position % width + HD] = block

    for group in range(HK):
        own = slice(group * HD, (group + 1) * HD)
        key, value = keys[:, own], values[:, own]
        key_grad = value_grad = 0.0
        start = group * (group_size + 2) * HD
        for member in range(group_size):
            head = group * group_size + member
            here = slice(head * HD, (head + 1) * HD)
            out_grad, query, prob = attended[:, here], queries[:, here], probs[head]
            prob_grad = dot(out_grad, value, ((1,), (1,)))
            prob_f = prob.astype(f32)
            inner = jnp.sum(prob_f * prob_grad, axis=-1, keepdims=True)
            score_grad = (prob_f * (prob_grad - inner)).astype(bf16)
            query_grad = turned(dot(score_grad, key) * scale, cosine_tab, sine_tab)
            put(start + member * HD, query_grad.astype(bf16))
            key_grad = key_grad + dot(score_grad, query, ((0,), (0,)))
            value_grad = value_grad + dot(prob, out_grad, ((0,), (0,)))
        key_grad = turned(key_grad * scale, cosine_tab, sine_tab)
        put(start + group_size * HD, key_grad.astype(bf16))
        put(start + (group_size + 1) * HD, value_grad.astype(bf16))


def first_back_kernel(at, back, weight, tokens, gain, resid_grad, tokens_ref, gain_ref):
    f32 = jnp.float32
    parts = back.shape[0]
    cols = weight.shape[0] * weight.shape[2] // parts
    first_grad = 0.0
    for part in range(parts):
        group, place = divmod(part * cols, weight.shape[2])
        first_grad = first_grad + dot(
            back[part, :, :cols], weight[group, :, place : place + cols], ((1,), (1,))
        )
    norm_grad, gain_grad = rms_back(tokens[...].astype(f32), gain[...], first_grad)
    gain_ref[...] = gain_grad
    tokens_ref[...] = (resid_grad[...] + norm_grad).astype(jnp.bfloat16)


def dense_grad_kernel(at, back, *refs):
    pieces, out_ref, held, sems = refs[:8], refs[8], refs[9], refs[10]
    copies = [
        pltpu.make_async_copy(piece, held.at[n], sems.at[n]) for n, piece in enumerate(pieces)
    ]
    for copy in copies:
        copy.start()
    depth, rows, cols = out_ref.shape
    length = held.shape[1] // 2
    qkv_width = cols - held.shape[2] // back.shape[0]
    narrow = sum(back[place, length:].astype(jnp.float32) for place in range(back.shape[0]))
    sums = [0.0, 0.0]
    for n, copy in enumerate(copies):
        copy.wait()
        dc, dy, dx = n // 4, n // 2 % 2, n % 2
        place = 4 * (at[0] ^ dy) + 2 * (at[1] ^ dc) + (at[2] ^ dx)
        own = back[place, :length]
        sums[0] = sums[0] + dot(held[n, length:], own[:, :qkv_width], ((0,), (0,)))
        sums[1] = sums[1] + dot(held[n, :length], own[:, qkv_width:], ((0,), (0,)))
    wide = held.shape[2] // depth
    each = narrow.shape[0] // depth
    for z in range(depth):
        here = slice(z * wide, (z + 1) * wide)
        both = jnp.concatenate([part[here] for part in sums], axis=1)
        out_ref[z, :wide] = both.astype(jnp.bfloat16)
        kept = [narrow[z * each : (z + 1) * each], jnp.zeros((rows - wide - each, cols), jnp.float32)]
        out_ref[z, wide:] = jnp.concatenate(kept, axis=0).astype(jnp.bfloat16)


def finish_kernel(at, sums, query_ref, key_ref, value_ref, output_ref):
    places, _, cols = sums.shape
    rows, out_width = query_ref.shape[0], output_ref.shape[1] // places
    width = cols - out_width
    for place in range(places):
        block = sums[place, :rows].astype(jnp.float32)
        output_ref[:, place * out_width : (place + 1) * out_width] = block[:, width:]
        for at_col in range(0, width, HD):
            group, head = divmod((place * width + at_col) // HD, HQ // HK + 2)
            part = block[:, at_col : at_col + HD]
            if head < HQ // HK:
                start = (group * (HQ // HK) + head) * HD
                query_ref[:, start : start + HD] = part
            elif head == HQ // HK:
                key_ref[:, group * HD : (group + 1) * HD] = part
            else:
                value_ref[:, group * HD : (group + 1) * HD] = part


def local_pairs(
    tokens,
    norm1_gain,
    w_query,
    w_key,
    w_value,
    w_out,
    norm2_gain,
    w_router,
    w_gate,
    w_up,
    w_down,
    expert_ids,
    prefix_len,
    out_grad,
):
    bf16, f32 = jnp.bfloat16, jnp.float32
    length, model_width = tokens.shape
    shard_rows = w_query.shape[0]
    local_count, _, hidden_width = w_gate.shape
    owners = lax.axis_size("x")
    depth = lax.axis_size("z")
    plane = lax.axis_size(PLANE)
    experts_all = w_router.shape[1]
    block_rows = length // MICRO
    capacity = 3 * block_rows * expert_ids.shape[1] // (2 * experts_all)
    plane_rows = plane * length
    blocks = plane_rows // block_rows
    q_cols, kv_cols = w_query.shape[1], w_key.shape[1]
    qkv_cols = q_cols + 2 * kv_cols
    q_group, out_half = q_cols // HK, model_width // 2
    y, c, x, z = (lax.axis_index(axis) for axis in ("y", "c", "x", "z"))
    own_local = 2 * y + c
    own_expert = x * local_count + own_local
    at = jnp.stack([y, c, x, z, prefix_len[0], own_expert, own_local])

    own_half = jnp.concatenate(
        [
            lax.dynamic_slice_in_dim(part, x * (part.shape[1] // 2), part.shape[1] // 2, 1)
            for part in (w_query, w_key, w_value, w_out)
        ],
        axis=1,
    )
    narrow = jnp.concatenate([w_router, norm1_gain[:, None], norm2_gain[:, None]], axis=1)
    narrow = jnp.pad(narrow, ((0, 0), (0, 128 - narrow.shape[1])))
    router_w = small_group_gather(narrow)
    ids_all = small_gather(expert_ids.T)
    column = [own_half] + shifts(own_half)
    cot_sides = plane_sides(after(out_grad, router_w, ids_all))
    qkv_half = qkv_cols // 2
    qkv_column = jnp.stack([part[:, :qkv_half] for part in column])
    out_column = jnp.stack([part[:, qkv_half:] for part in column])
    qkv_column, out_column = lax.optimization_barrier((qkv_column, out_column, *cot_sides))[:2]
    sliced = after(own_local, column[-1])
    gate_w, up_w, down_w = (
        lax.dynamic_index_in_dim(weight, sliced, 0, keepdims=False)
        for weight in (w_gate, w_up, w_down)
    )
    qkv_sides = plane_sides(qkv_column)
    qkv_corner = plane_corner(qkv_sides)
    out_sides = plane_sides(after(out_column, *qkv_sides))
    qkv_pieces = plane_pieces(qkv_column, qkv_sides, qkv_corner)
    gains = router_w[:, experts_all : experts_all + 2].T.astype(f32)
    gain_one, gain_two = gains[:1], gains[1:]
    gain_one, gate_w, up_w, down_w = lax.optimization_barrier((gain_one, gate_w, up_w, down_w))

    cosine_tab, sine_tab = angles(length, HD)
    cosine_all = jnp.concatenate([cosine_tab, cosine_tab], axis=2)[:, 0]
    sine_all = jnp.concatenate([-sine_tab, sine_tab], axis=2)[:, 0]
    weight_lead = (2, depth, 2, 2, shard_rows)
    first_in, queries, keys_rot, values_b, attended, probs, qkv_w = run_kernel(
        attend_kernel,
        11,
        at,
        (tokens, gain_one, cosine_all, sine_all, *qkv_pieces),
        [
            ((length, model_width), bf16),
            ((length, q_cols), bf16),
            ((length, kv_cols), bf16),
            ((length, kv_cols), bf16),
            ((length, q_cols), bf16),
            ((HQ, length, length), bf16),
            (weight_lead + (qkv_half,), bf16),
        ],
        48,
        [
            pltpu.VMEM((HQ, length, length), bf16),
            pltpu.VMEM(weight_lead + (qkv_half,), bf16),
            pltpu.SemaphoreType.DMA((HK + 1,)),
        ],
        hbm_out=2,
    )
    out_sides = lax.optimization_barrier((*out_sides, attended))[:2]
    out_corner = plane_corner(out_sides)
    cot_corner = plane_corner(cot_sides)
    out_pieces = plane_pieces(out_column, out_sides, out_corner)
    cot_pieces = plane_pieces(out_grad, cot_sides, cot_corner)
    resid, second_in, output_w = run_kernel(
        project_kernel,
        4,
        at,
        (tokens, after(gain_two, cot_corner), attended, *out_pieces),
        [
            ((length, model_width), f32),
            ((length, model_width), bf16),
            (weight_lead + (out_half,), bf16),
        ],
        44,
        [pltpu.VMEM(weight_lead + (out_half,), bf16), pltpu.SemaphoreType.DMA],
        hbm_out=1,
    )
    qkv_w = qkv_w.reshape(HK, model_width, qkv_half)
    output_w = output_w.reshape(2, q_cols, out_half)

    expert = functools.partial(
        run_expert,
        at=at,
        ids=ids_all,
        router=router_w,
        weights=(gate_w, up_w, down_w),
        capacity=capacity,
    )
    second_sides = plane_sides(second_in)
    groups = ((0, 4), (1, 5, 2, 6), (3, 7))
    second_pieces = {0: second_in, 4: swap(second_in, "c")}

    def run_group(pieces):
        return expert(
            pieces,
            second=[second_pieces[piece] for piece in pieces],
            cot=[cot_pieces[piece] for piece in pieces],
        )

    stage_own = run_group(groups[0])
    second_sides = lax.optimization_barrier((*second_sides, stage_own[0]))[:2]
    for piece, block in zip((1, 2), second_sides):
        second_pieces[piece], second_pieces[piece + 4] = block, swap(block, "c")
    stage_sides = run_group(groups[1])
    second_corner = plane_corner(second_sides, later=(stage_sides[0],))
    second_pieces[3], second_pieces[7] = second_corner, swap(second_corner, "c")
    own_near, own_far = stage_own[6:]
    own_far = swap(own_far, "c")
    x_near, x_far, y_near, y_far = stage_sides[6:]
    back_x, back_y = over_core(x_near, x_far), over_core(y_near, y_far)
    first_x, first_y = early_sums(back_x, back_y)
    stage_corner = run_group(groups[2])
    corner = over_core(*stage_corner[6:])
    passed = corner_first(corner)
    stages = (stage_own, stage_sides, stage_corner)
    rows_in, rows_cot, gated, gate_back, up_back = ([stage[n] for stage in stages] for n in range(5))
    gates = stage_own[5]
    (down_part,) = row_sums(at, [after(rows_cot[0], corner)] + rows_cot[1:], gated)
    down_sum = scatter_sum(down_part, "z")
    passed = lax.optimization_barrier((*passed, down_part))[:2]
    last_y, last_x, sent = corner_last(back_x, back_y, passed)
    gate_part, up_part = row_sums(
        at, [after(rows_in[0], sent)] + rows_in[1:], gate_back, up_back
    )
    gate_sum, up_sum = scatter_sum(gate_part, "z"), scatter_sum(up_part, "z")
    own_near = after(own_near, gate_part)

    resid_grad, branch_grad, attended_grad, router_acc, gain_two_grad = run_kernel(
        branch_back_kernel,
        6,
        at,
        (
            own_near,
            own_far,
            first_x,
            first_y,
            last_y,
            last_x,
            resid,
            gain_two,
            second_in,
            gates,
            router_w,
            out_grad,
            output_w,
        ),
        [
            ((length, model_width), f32),
            ((length, model_width), bf16),
            ((length, q_cols), bf16),
            ((model_width, 128), f32),
            ((1, model_width), f32),
        ],
    )
    qkv_width, branch_width = qkv_cols // plane, model_width // plane
    dense_cols = qkv_width + branch_width
    (back_cols,) = run_kernel(
        attend_back_kernel,
        6,
        at,
        (
            attended_grad,
            probs,
            queries,
            keys_rot,
            values_b,
            cosine_all,
            sine_all,
            branch_grad,
        ),
        [((plane, length, dense_cols), bf16)],
    )
    tokens_grad, gain_one_grad = run_kernel(
        first_back_kernel,
        5,
        at,
        (back_cols, qkv_w, tokens, gain_one, resid_grad),
        [((length, model_width), bf16), ((1, model_width), f32)],
        24,
    )

    both = jnp.concatenate(
        lax.optimization_barrier((attended, first_in, last_y, last_x))[:2], axis=0
    )
    both_sides = plane_sides(both)
    narrow_part = jnp.concatenate(
        [router_acc[:, :experts_all], gain_one_grad.T, gain_two_grad.T], axis=1
    )
    narrow_cols = -(-narrow_part.shape[1] // owners) * owners
    narrow_part = jnp.pad(narrow_part, ((0, 0), (0, narrow_cols - narrow_part.shape[1])))
    narrow_part = jnp.transpose(
        narrow_part.reshape(depth, 2, 2, shard_rows, owners, narrow_cols // owners),
        (1, 2, 4, 0, 3, 5),
    ).reshape(plane, depth, shard_rows * narrow_cols // owners)
    narrow_len = narrow_part.shape[2]
    narrow_rows = -(-narrow_len // dense_cols)
    each_rows = -(-narrow_rows // 4) * 4
    narrow_part = jnp.pad(
        narrow_part, ((0, 0), (0, 0), (0, each_rows * dense_cols - narrow_len))
    ).reshape(plane, depth * each_rows, dense_cols)
    back_cols = jnp.concatenate([back_cols, narrow_part.astype(bf16)], axis=1)
    back_cols = exchange(after(back_cols, down_sum, *both_sides), PLANE)
    both_corner = plane_corner(both_sides)
    both_pieces = plane_pieces(both, both_sides, both_corner)
    kept_rows = -(-narrow_rows // 16) * 16
    wide_rows = local_count * shard_rows
    dense_shape = (depth, wide_rows + kept_rows, dense_cols)
    dense_part = pl.pallas_call(
        dense_grad_kernel,
        out_shape=jax.ShapeDtypeStruct(dense_shape, bf16),
        in_specs=[SCALARS, WHOLE] + [IN_HBM] * 8,
        out_specs=WHOLE,
        scratch_shapes=[
            pltpu.VMEM((plane, 2 * length, model_width), bf16),
            pltpu.SemaphoreType.DMA((plane,)),
        ],
        cost_estimate=cost(8),
        compiler_params=pltpu.CompilerParams(vmem_limit_bytes=32 * 2**20),
    )(at, after(back_cols, gate_sum), *both_pieces)
    dense_part = after(dense_part, up_sum)
    dense_sum = scatter_sum(dense_part.reshape(-1, dense_cols), "z")
    wide_sum = dense_sum[: local_count * shard_rows].reshape(2, 2, 1, shard_rows, dense_cols)
    wide_sum = jnp.broadcast_to(wide_sum, (2, 2, owners, shard_rows, dense_cols)).reshape(
        plane, shard_rows, dense_cols
    )
    narrow_sum = dense_sum[local_count * shard_rows :][:narrow_rows]
    narrow_sum = jnp.broadcast_to(narrow_sum[None], (plane, narrow_rows, dense_cols))
    pad_rows = -(shard_rows + narrow_rows) % 16
    padding = jnp.zeros((plane, pad_rows, dense_cols), bf16)
    dense_sum = exchange(jnp.concatenate([wide_sum, narrow_sum, padding], axis=1), PLANE)
    query_grad, key_grad, value_grad, output_grad = run_kernel(
        finish_kernel,
        2,
        at,
        (dense_sum,),
        [
            ((shard_rows, q_cols), f32),
            ((shard_rows, kv_cols), f32),
            ((shard_rows, kv_cols), f32),
            ((shard_rows, model_width), f32),
        ],
    )
    narrow_sum = dense_sum[:, shard_rows : shard_rows + narrow_rows].reshape(
        2, 2, owners, narrow_rows * dense_cols
    )
    narrow_sum = narrow_sum[y, c, :, :narrow_len].reshape(owners, shard_rows, -1)
    narrow_sum = jnp.moveaxis(narrow_sum, 0, 1).reshape(shard_rows, narrow_cols).astype(f32)

    shares = run_kernel(
        functools.partial(mixture_kernel, capacity, groups),
        10,
        at,
        (ids_all, after(gated[0], dense_part), *gated[1:], down_w),
        [((length, model_width), bf16)] * plane,
        24,
    )
    mixed = [over_core(near, far) for near, far in zip(shares[:4], shares[4:])]
    early = early_sums(mixed[1], mixed[2])
    last = corner_last(mixed[1], mixed[2], corner_first(mixed[3]))[:2]
    mixture = jnp.concatenate(
        [left.astype(f32) + right.astype(f32) for left, right in zip(early, last)], axis=0
    )
    block_out = (resid + (mixture + mixed[0].astype(f32))).astype(bf16)

    def placed(total):
        total = exchange(total, ("y", "c"))
        return total.reshape(local_count, shard_rows, hidden_width).astype(f32)

    return (
        block_out,
        tokens_grad,
        narrow_sum[:, experts_all],
        query_grad,
        key_grad,
        value_grad,
        output_grad,
        narrow_sum[:, experts_all + 1],
        narrow_sum[:, :experts_all],
        placed(after(gate_sum, dense_part)),
        placed(up_sum),
        jnp.swapaxes(placed(after(down_sum, dense_part)), 1, 2),
    )


def solution(mesh):
    groups, owners = mesh.shape["dp"], mesh.shape["expert"]
    grid = jax.sharding.Mesh(
        mesh.devices.reshape(groups // 4, 2, 2, owners), ("z", "y", "c", "x")
    )
    rows = P(("z", "y", "c", "x"), None)
    shard, shard_rows = P(GROUP), P(GROUP, None)
    expert = P("x", None, None)
    return jax.shard_map(
        local_pairs if owners == 2 else local_wide,
        mesh=grid,
        in_specs=(
            rows,
            shard,
            shard_rows,
            shard_rows,
            shard_rows,
            shard_rows,
            shard,
            shard_rows,
            expert,
            expert,
            expert,
            rows,
            P(("z", "y", "c", "x")),
            rows,
        ),
        out_specs=(
            rows,
            rows,
            shard,
            shard_rows,
            shard_rows,
            shard_rows,
            shard_rows,
            shard,
            shard_rows,
            P("x", GROUP, None),
            P("x", GROUP, None),
            P("x", None, GROUP),
        ),
        check_vma=False,
    )
```

```python
import functools
import math

import jax
import jax.numpy as jnp
from jax import lax
from jax.experimental import pallas as pl
from jax.experimental.pallas import tpu as pltpu
from jax.sharding import PartitionSpec as P

HQ = 12
HK = 2
HD = 128
MICRO = 2
PLANE = ("y", "c", "x")
GROUP = ("z", "y", "c")


def rms_scale(values, gain_vec):
    inverse = lax.rsqrt(jnp.mean(values * values, axis=-1, keepdims=True) + 1e-06)
    return values * inverse * gain_vec


def angles(length, head_size):
    positions = jnp.arange(length).astype(jnp.float32)
    freq_rates = jnp.exp(
        -(2.0 * jnp.arange(head_size // 2).astype(jnp.float32) / head_size) * math.log(1000000.0)
    )
    angle_tab = positions[:, None] * freq_rates[None, :]
    return (jnp.cos(angle_tab)[:, None, :], jnp.sin(angle_tab)[:, None, :])


def rotary(values, cosine_tab, sine_tab):
    half_dim = values.shape[-1] // 2
    first_half = values[..., :half_dim]
    second_half = values[..., half_dim:]
    return jnp.concatenate(
        [
            first_half * cosine_tab - second_half * sine_tab,
            second_half * cosine_tab + first_half * sine_tab,
        ],
        axis=-1,
    )


def expert_act(gate_pre, up_pre):
    return jax.nn.gelu(gate_pre, approximate=True) * up_pre


def left_product(left_mat, right_mat):
    return lax.dot_general(
        left_mat, right_mat, (((0,), (0,)), ((), ())), preferred_element_type=jnp.float32
    )


def gather(block, axes):
    return lax.all_gather(block, axes, axis=0, tiled=True)


def exchange(block, axes):
    return lax.all_to_all(block, axes, split_axis=0, concat_axis=0, tiled=True)


def scatter_sum(block, axes):
    return lax.psum_scatter(block, axes, scatter_dimension=0, tiled=True)


def by_owner(cols, parts):
    rows, total = cols.shape
    return jnp.moveaxis(cols.reshape(rows, parts, total // parts), 1, 0).reshape(
        parts * rows, total // parts
    )


def local_wide(
    tokens,
    norm1_gain,
    w_query,
    w_key,
    w_value,
    w_out,
    norm2_gain,
    w_router,
    w_gate,
    w_up,
    w_down,
    expert_ids,
    prefix_len,
    out_grad,
):
    bf16, f32 = jnp.bfloat16, jnp.float32
    length, model_width = tokens.shape
    shard_rows = w_query.shape[0]
    local_count, _, hidden_width = w_gate.shape
    owners = lax.axis_size("x")
    depth = lax.axis_size("z")
    plane = lax.axis_size(PLANE)
    experts_all = w_router.shape[1]
    top_count = expert_ids.shape[1]
    block_rows = length // MICRO
    capacity = 3 * block_rows * top_count // (2 * experts_all)
    plane_rows = plane * length
    blocks = plane_rows // block_rows
    group_size = HQ // HK
    score_scale = HD ** (-0.5)
    q_cols, kv_cols = w_query.shape[1], w_key.shape[1]
    own_local = lax.axis_index(("y", "c"))
    own_expert = lax.axis_index("x") * local_count + own_local
    own_place = lax.axis_index(PLANE)

    narrow = jnp.concatenate([w_router, norm1_gain[:, None], norm2_gain[:, None]], axis=1)
    narrow = jnp.pad(narrow, ((0, 0), (0, -narrow.shape[1] % 128)))
    packed = gather(jnp.concatenate([w_query, w_key, w_value, narrow], axis=1), GROUP)
    qkv_cols = q_cols + 2 * kv_cols
    qkv_w = packed[:, :qkv_cols]
    router_w = packed[:, qkv_cols : qkv_cols + experts_all]
    gains = packed[:, qkv_cols + experts_all : qkv_cols + experts_all + 2].T.astype(f32)
    gain_one, gain_two = gains[0], gains[1]
    output_w = gather(w_out, GROUP)

    ids_all = gather(expert_ids, PLANE)
    cot_all = gather(out_grad, PLANE)
    chosen_mask = jnp.any(
        ids_all[:, :, None] == jnp.arange(experts_all, dtype=jnp.int32)[None, None, :], axis=1
    )
    own_mask = jnp.any(ids_all == own_expert, axis=1).reshape(blocks, block_rows)
    place = jnp.cumsum(own_mask.astype(jnp.int32), axis=1) - 1
    dispatch = (
        own_mask[:, None, :]
        & (place[:, None, :] == jnp.arange(capacity, dtype=jnp.int32)[None, :, None])
    ).astype(bf16)

    cosine_tab, sine_tab = angles(length, HD)
    inputs_f = tokens.astype(f32)
    first_in = rms_scale(inputs_f, gain_one).astype(bf16)
    qkv = jnp.dot(first_in, qkv_w, preferred_element_type=f32)
    queries = (
        rotary(qkv[:, :q_cols].reshape(length, HQ, HD), cosine_tab, sine_tab)
        .astype(bf16)
        .reshape(length, HK, group_size, HD)
    )
    keys_rot = rotary(
        qkv[:, q_cols : q_cols + kv_cols].reshape(length, HK, HD), cosine_tab, sine_tab
    ).astype(bf16)
    values_b = qkv[:, q_cols + kv_cols :].astype(bf16).reshape(length, HK, HD)
    positions = jnp.arange(length)
    allowed = (positions[None, :] <= positions[:, None]) | (positions[None, :] < prefix_len[0])

    def masked_scores():
        scores = jnp.einsum("ihrd,jhd->hrij", queries, keys_rot, preferred_element_type=f32)
        return jnp.where(allowed, scores * score_scale, -1e30)

    masked = masked_scores()
    row_peak = jnp.max(masked, axis=-1, keepdims=True)
    log_total = row_peak + jnp.log(jnp.sum(jnp.exp(masked - row_peak), axis=-1, keepdims=True))
    prob_bf = jnp.exp(masked - log_total).astype(bf16)
    attended = jnp.einsum("hrij,jhd->ihrd", prob_bf, values_b, preferred_element_type=f32)
    attended = attended.reshape(length, HQ * HD).astype(bf16)
    resid = inputs_f + jnp.dot(attended, output_w, preferred_element_type=f32)
    second_in = rms_scale(resid, gain_two).astype(bf16)

    second_all = gather(second_in, PLANE)
    logits = jnp.dot(second_all, router_w, preferred_element_type=f32)
    gates_all = jax.nn.softmax(jnp.where(chosen_mask, logits, -jnp.inf), axis=-1)
    own_gates = lax.dynamic_index_in_dim(gates_all, own_expert, 1, keepdims=False)
    own_gates = own_gates.reshape(blocks, block_rows)
    gate_rows = jnp.einsum(
        "bct,bt->bc", dispatch.astype(f32), own_gates, precision=lax.Precision.HIGHEST
    )[:, :, None]
    gate_w = lax.dynamic_index_in_dim(w_gate, own_local, 0, keepdims=False)
    up_w = lax.dynamic_index_in_dim(w_up, own_local, 0, keepdims=False)
    down_w = lax.dynamic_index_in_dim(w_down, own_local, 0, keepdims=False)

    def to_rows(array):
        return jnp.einsum(
            "bct,btd->bcd",
            dispatch,
            array.reshape(blocks, block_rows, model_width),
            preferred_element_type=f32,
        ).astype(bf16)

    def to_tokens(rows):
        return (
            jnp.einsum("bct,bcd->btd", dispatch, rows.astype(bf16), preferred_element_type=f32)
            .astype(bf16)
            .reshape(plane_rows, model_width)
        )

    rows_in = to_rows(second_all)
    rows_cot = to_rows(cot_all)
    gate_pre = jnp.einsum("bcd,df->bcf", rows_in, gate_w, preferred_element_type=f32)
    up_pre = jnp.einsum("bcd,df->bcf", rows_in, up_w, preferred_element_type=f32)
    hidden, act_pull = jax.vjp(expert_act, gate_pre, up_pre)
    gated = (gate_rows * hidden).astype(bf16)
    down_part = jnp.einsum("bcd,bcf->df", rows_cot, gated, preferred_element_type=f32)
    down_sum = scatter_sum(down_part.astype(bf16), "z")
    cot_hidden = jnp.einsum("bcd,fd->bcf", rows_cot, down_w, preferred_element_type=f32)
    gate_signal_rows = jnp.sum(hidden * cot_hidden, axis=-1)
    gate_pgrad, up_pgrad = act_pull(gate_rows * cot_hidden)
    gate_pgrad = gate_pgrad.astype(bf16)
    up_pgrad = up_pgrad.astype(bf16)
    gate_part = jnp.einsum("bcd,bcf->df", rows_in, gate_pgrad, preferred_element_type=f32)
    gate_sum = scatter_sum(gate_part.astype(bf16), "z")
    up_part = jnp.einsum("bcd,bcf->df", rows_in, up_pgrad, preferred_element_type=f32)
    up_sum = scatter_sum(up_part.astype(bf16), "z")
    rows_grad = jnp.einsum("bcf,df->bcd", gate_pgrad, gate_w, preferred_element_type=f32)
    rows_grad = rows_grad + jnp.einsum("bcf,df->bcd", up_pgrad, up_w, preferred_element_type=f32)
    second_back = scatter_sum(to_tokens(rows_grad), PLANE).astype(f32)
    gate_signal = jnp.einsum(
        "bct,bc->bt", dispatch.astype(f32), gate_signal_rows, precision=lax.Precision.HIGHEST
    )
    gate_signal = exchange(gate_signal.reshape(plane, length), PLANE)
    gate_signal = jnp.transpose(
        gate_signal.reshape(local_count, owners, length), (2, 1, 0)
    ).reshape(length, experts_all)
    expert_rows = jnp.einsum("bcf,fd->bcd", gated, down_w, preferred_element_type=f32)
    mixture = scatter_sum(to_tokens(expert_rows), PLANE).astype(f32)
    block_out = (resid + mixture).astype(bf16)

    cotangent = out_grad.astype(f32)
    gate_probs = lax.dynamic_slice_in_dim(gates_all, own_place * length, length, 0)
    logit_grad = (
        gate_probs
        * (gate_signal - jnp.sum(gate_probs * gate_signal, axis=-1, keepdims=True))
    ).astype(bf16)
    router_acc = left_product(second_in, logit_grad)
    second_grad = second_back + jnp.dot(logit_grad, router_w.T, preferred_element_type=f32)
    _, norm_two_pull = jax.vjp(rms_scale, resid, gain_two)
    resid_norm_grad, gain_two_grad = norm_two_pull(second_grad)
    resid_grad = cotangent + resid_norm_grad
    branch_grad = resid_grad.astype(bf16)

    attended_all = gather(attended, PLANE)
    branch_cols = exchange(by_owner(branch_grad, plane), PLANE)
    output_part = left_product(attended_all, branch_cols)
    attended_grad = jnp.dot(branch_grad, output_w.T, preferred_element_type=f32).astype(bf16)
    attended_grad = attended_grad.reshape(length, HK, group_size, HD)
    masked = masked_scores()
    prob_full = jnp.exp(masked - log_total)
    prob_bf = prob_full.astype(bf16)
    prob_grad = jnp.einsum("ihrd,jhd->hrij", attended_grad, values_b, preferred_element_type=f32)
    row_inner = jnp.sum(prob_full * prob_grad, axis=-1, keepdims=True)
    score_grad = (prob_full * (prob_grad - row_inner)).astype(bf16)
    query_rot_grad = (
        jnp.einsum("hrij,jhd->ihrd", score_grad, keys_rot, preferred_element_type=f32)
        * score_scale
    )
    query_back = rotary(query_rot_grad.reshape(length, HQ, HD), cosine_tab, -sine_tab)
    query_back = query_back.astype(bf16).reshape(length, HQ * HD)
    key_rot_grad = (
        jnp.einsum("hrij,ihrd->jhd", score_grad, queries, preferred_element_type=f32)
        * score_scale
    )
    key_back = rotary(key_rot_grad, cosine_tab, -sine_tab).astype(bf16).reshape(length, HK * HD)
    value_back = jnp.einsum("hrij,ihrd->jhd", prob_bf, attended_grad, preferred_element_type=f32)
    value_back = value_back.astype(bf16).reshape(length, HK * HD)
    qkv_back = jnp.concatenate([query_back, key_back, value_back], axis=1)
    first_all = gather(first_in, PLANE)
    qkv_part = left_product(first_all, exchange(by_owner(qkv_back, plane), PLANE))
    first_grad = lax.dot_general(
        qkv_back, qkv_w, (((1,), (1,)), ((), ())), preferred_element_type=f32
    )
    _, norm_one_pull = jax.vjp(rms_scale, inputs_f, gain_one)
    input_norm_grad, gain_one_grad = norm_one_pull(first_grad)
    tokens_grad = (resid_grad + input_norm_grad).astype(bf16)

    narrow_part = jnp.concatenate(
        [router_acc, gain_one_grad[:, None], gain_two_grad[:, None]], axis=1
    ).astype(bf16)
    narrow_cols = narrow_part.shape[1]
    narrow_sum = lax.psum(scatter_sum(narrow_part, GROUP), "x").astype(f32)
    dense_part = jnp.concatenate([qkv_part, output_part], axis=1).astype(bf16)
    dense_sum = scatter_sum(dense_part, "z")
    dense_cols = dense_sum.shape[1]
    dense_sum = gather(dense_sum, PLANE).reshape(plane, local_count, shard_rows, dense_cols)
    dense_sum = lax.dynamic_index_in_dim(dense_sum, own_local, 1, keepdims=False).astype(f32)
    dense_sum = jnp.moveaxis(dense_sum, 0, 1)
    qkv_width = qkv_cols // plane
    qkv_sum = dense_sum[:, :, :qkv_width].reshape(shard_rows, qkv_cols)
    output_sum = dense_sum[:, :, qkv_width:].reshape(shard_rows, model_width)

    def placed(total):
        total = exchange(total, ("y", "c"))
        return total.reshape(local_count, shard_rows, hidden_width).astype(f32)

    return (
        block_out,
        tokens_grad,
        narrow_sum[:, experts_all],
        qkv_sum[:, :q_cols],
        qkv_sum[:, q_cols : q_cols + kv_cols],
        qkv_sum[:, q_cols + kv_cols :],
        output_sum,
        narrow_sum[:, experts_all + 1],
        narrow_sum[:, :experts_all],
        placed(gate_sum),
        placed(up_sum),
        jnp.swapaxes(placed(down_sum), 1, 2),
    )


def rounded(values):
    return lax.reduce_precision(values, 8, 7).astype(jnp.bfloat16)


def after(block, *others):
    return lax.optimization_barrier((block,) + others)[0]


def swap(block, axis):
    return lax.ppermute(block, axis, [(0, 1), (1, 0)])


def shifts(block):
    depth = lax.axis_size("z")
    return [
        lax.ppermute(block, "z", [(i, (i + k) % depth) for i in range(depth)])
        for k in range(1, depth)
    ]


def plane_sides(block):
    return swap(block, "x"), swap(block, "y")


def plane_corner(sides, before=(), later=()):
    over_x, over_y = sides
    half = over_x.shape[0] // 2
    over_y, over_x = lax.optimization_barrier((over_y[:half], over_x[half:]) + before)[:2]
    parts = (swap(over_y, "x"), swap(over_x, "y"))
    return jnp.concatenate(lax.optimization_barrier(parts + later)[:2], axis=0)


def plane_pieces(block, sides=None, corner=None):
    sides = plane_sides(block) if sides is None else sides
    corner = plane_corner(sides) if corner is None else corner
    pieces = [block, *sides, corner]
    return pieces + [swap(piece, "c") for piece in pieces]


def small_gather(block):
    for axis in ("x", "y", "c"):
        block = jnp.concatenate([block, swap(block, axis)], axis=1)
    return block


def small_group_gather(block):
    depth = lax.axis_size("z")
    order = jnp.stack(([block] + shifts(block))[::-1] * 2)
    start = (depth - 1 - lax.axis_index("z")) % depth
    total = lax.dynamic_slice_in_dim(order, start, depth, 0)[:, None, None]
    for dim, axis in ((1, "y"), (2, "c")):
        other = swap(total, axis)
        last = lax.axis_index(axis) == 1
        pair = [jnp.where(last, other, total), jnp.where(last, total, other)]
        total = jnp.concatenate(pair, axis=dim)
    return total.reshape(-1, block.shape[1])


def add(left, right):
    return rounded(left.astype(jnp.float32) + right.astype(jnp.float32))


def over_core(near, far):
    return add(near, swap(far, "c"))


def early_sums(over_x, over_y):
    half = over_x.shape[0] // 2
    return swap(over_x[:half], "x"), swap(over_y[half:], "y")


def corner_first(corner):
    half = corner.shape[0] // 2
    return swap(corner[:half], "x"), swap(corner[half:], "y")


def corner_last(over_x, over_y, first):
    half = over_x.shape[0] // 2
    over_y, over_x = add(over_y[:half], first[0]), add(over_x[half:], first[1])
    return swap(over_y, "y"), swap(over_x, "x"), over_y, over_x


def cost(micros):
    return pl.CostEstimate(flops=micros * 10**9, bytes_accessed=micros * 10**6, transcendentals=0)


def dot(left, right, dims=((1,), (0,)), precision=None):
    return lax.dot_general(
        left, right, (dims, ((), ())), precision=precision, preferred_element_type=jnp.float32
    )


WHOLE = pl.BlockSpec(memory_space=pltpu.VMEM)
IN_HBM = pl.BlockSpec(memory_space=pltpu.HBM)
SCALARS = pl.BlockSpec(memory_space=pltpu.SMEM)


def run_kernel(kernel, micros, at, operands, outs, megabytes=16, scratch=(), hbm_in=0, hbm_out=0):
    return pl.pallas_call(
        kernel,
        out_shape=[jax.ShapeDtypeStruct(shape, dtype) for shape, dtype in outs],
        in_specs=[SCALARS] + [WHOLE] * (len(operands) - hbm_in) + [IN_HBM] * hbm_in,
        out_specs=[WHOLE] * (len(outs) - hbm_out) + [IN_HBM] * hbm_out,
        scratch_shapes=scratch,
        cost_estimate=cost(micros),
        compiler_params=pltpu.CompilerParams(vmem_limit_bytes=megabytes * 2**20),
    )(at, *operands)


def place_pieces(at, refs, weight):
    depth = weight.shape[1]
    for n, ref in enumerate(refs):
        dc, dy, dx = n // 4, n // 2 % 2, n % 2
        for k in range(depth):
            z = lax.rem(at[3] + depth - k, depth)
            weight[at[2] ^ dx, z, at[0] ^ dy, at[1] ^ dc] = ref[k]


def rms_kernel(values, gain):
    inverse = lax.rsqrt(jnp.mean(values * values, axis=-1, keepdims=True) + 1e-06)
    return (values * inverse * gain).astype(jnp.bfloat16)


def rms_back(values, gain, grad):
    inverse = lax.rsqrt(jnp.mean(values * values, axis=-1, keepdims=True) + 1e-06)
    normed = values * inverse
    gain_grad = jnp.sum(grad * normed, axis=0, keepdims=True)
    grad = grad * gain
    along = jnp.mean(grad * normed, axis=-1, keepdims=True)
    return inverse * (grad - normed * along), gain_grad


def turned(values, cosine_tab, sine_tab):
    return values * cosine_tab + pltpu.roll(values, HD // 2, 1) * sine_tab


def attend_kernel(at, tokens, gain, cosine, sine, *refs):
    first_ref, query_ref, key_ref, value_ref, out_ref = refs[8:13]
    prob_out, weight_out, prob_ref, weight, sems = refs[13:]
    place_pieces(at, refs[:8], weight)
    copies = [pltpu.make_async_copy(weight, weight_out, sems.at[HK])]
    copies[0].start()
    length = tokens.shape[0]
    first_in = rms_kernel(tokens[...].astype(jnp.float32), gain[...])
    first_ref[...] = first_in
    rows = lax.broadcasted_iota(jnp.int32, (length, length), 0)
    cols = lax.broadcasted_iota(jnp.int32, (length, length), 1)
    allowed = (cols <= rows) | (cols < at[4])
    cosine_tab, sine_tab = cosine[...], sine[...]
    group_size = HQ // HK
    for group in range(HK):
        matrix = weight[group].reshape(first_in.shape[1], -1)
        qkv = dot(first_in, matrix)
        at_key = group_size * HD
        key = turned(qkv[:, at_key : at_key + HD], cosine_tab, sine_tab).astype(jnp.bfloat16)
        value = qkv[:, at_key + HD :].astype(jnp.bfloat16)
        key_ref[:, group * HD : (group + 1) * HD] = key
        value_ref[:, group * HD : (group + 1) * HD] = value
        for member in range(group_size):
            head = group * group_size + member
            here = slice(head * HD, (head + 1) * HD)
            query = turned(qkv[:, member * HD : (member + 1) * HD], cosine_tab, sine_tab)
            query = query.astype(jnp.bfloat16)
            query_ref[:, here] = query
            scores = dot(query, key, ((1,), (1,)))
            scores = jnp.where(allowed, scores * HD ** (-0.5), -1e30)
            weights = jnp.exp(scores - jnp.max(scores, axis=-1, keepdims=True))
            prob = weights * (1.0 / jnp.sum(weights, axis=-1, keepdims=True))
            prob = prob.astype(jnp.bfloat16)
            prob_ref[head] = prob
            out_ref[:, here] = dot(prob, value).astype(jnp.bfloat16)
        here = pl.ds(group * group_size, group_size)
        copies.append(
            pltpu.make_async_copy(prob_ref.at[here], prob_out.at[here], sems.at[group])
        )
        copies[-1].start()
    for copy in copies:
        copy.wait()


def project_kernel(at, tokens, gain, attended, *refs):
    resid_ref, second_ref, weight_out, weight, sem = refs[8:]
    place_pieces(at, refs[:8], weight)
    copy = pltpu.make_async_copy(weight, weight_out, sem)
    copy.start()
    heads = attended[...]
    halves = [dot(heads, weight[half].reshape(heads.shape[1], -1)) for half in range(2)]
    resid = tokens[...].astype(jnp.float32) + jnp.concatenate(halves, axis=1)
    resid_ref[...] = resid
    second_ref[...] = rms_kernel(resid, gain[...])
    copy.wait()


def one_hot(slots, capacity, dtype):
    shape = (capacity, slots.shape[1])
    return (slots == lax.broadcasted_iota(jnp.int32, shape, 0)).astype(jnp.float32).astype(dtype)


def slots_of(ids, expert, start, rows):
    named = jnp.any(ids[:, start : start + rows] == expert, axis=0, keepdims=True)
    named = named.astype(jnp.float32)
    before = lax.broadcasted_iota(jnp.int32, (rows, rows), 0)
    upto = lax.broadcasted_iota(jnp.int32, (rows, rows), 1)
    counts = dot(named.astype(jnp.bfloat16), (before <= upto).astype(jnp.float32).astype(jnp.bfloat16))
    return jnp.where(named > 0.0, counts - 1.0, -1.0).astype(jnp.int32)


def spread(picks, capacity, rows, outs):
    rows = rows.astype(jnp.bfloat16)
    block = picks[0].shape[1]
    for n in range(len(picks) // 2):
        for part in range(2):
            pick = picks[2 * n + part]
            at_row = (2 * n + part) * capacity
            tokens = dot(pick, rows[at_row : at_row + capacity], ((0,), (0,)))
            outs[n][part * block : (part + 1) * block] = tokens.astype(jnp.bfloat16)


def expert_kernel(capacity, pieces, at, ids, router, *refs):
    count = len(pieces)
    second, cot = refs[:count], refs[count : 2 * count]
    gate_w, up_w, down_w = refs[2 * count : 2 * count + 3]
    rows_in, rows_cot, gated_ref, gate_back, up_back, gates_ref = refs[2 * count + 3 : 2 * count + 9]
    backs, gate_rows = refs[2 * count + 9 : -1], refs[-1]
    f32, bf16 = jnp.float32, jnp.bfloat16
    length, width = second[0].shape
    wide = router.shape[1]
    half = length // 2
    picks = []
    experts = lax.broadcasted_iota(jnp.int32, (wide, length), 0)
    for n, piece in enumerate(pieces):
        tokens = second[n][...]
        named = ids[:, piece * length : (piece + 1) * length]
        chosen = functools.reduce(
            jnp.logical_or, [named[k : k + 1] == experts for k in range(named.shape[0])]
        )
        logits = jnp.where(chosen, dot(router[...], tokens, ((0,), (1,))), -1e30)
        weights = jnp.exp(logits - jnp.max(logits, axis=0, keepdims=True))
        gates = weights * (1.0 / jnp.sum(weights, axis=0, keepdims=True))
        if n == 0:
            gates_ref[...] = gates
        own = jnp.sum(jnp.where(experts == at[5], gates, 0.0), axis=0, keepdims=True)
        for part in range(2):
            here = slice(part * half, (part + 1) * half)
            place = slice((2 * n + part) * capacity, (2 * n + part + 1) * capacity)
            slots = slots_of(ids, at[5], piece * length + part * half, half)
            pick = one_hot(slots, capacity, f32)
            picks.append(pick.astype(bf16))
            rows_in[place] = dot(picks[-1], tokens[here]).astype(bf16)
            rows_cot[place] = dot(picks[-1], cot[n][here]).astype(bf16)
            gate_rows[place] = jnp.sum(pick * own[:, here], axis=1, keepdims=True)
    gate = gate_rows[...]
    gate_pre = dot(rows_in[...], gate_w[...])
    up_pre = dot(rows_in[...], up_w[...])
    cot_hidden = dot(rows_cot[...], down_w[...], ((1,), (1,)))
    scale = math.sqrt(2.0 / math.pi)
    square = gate_pre * gate_pre
    bent = jnp.tanh(scale * gate_pre * (1.0 + 0.044715 * square))
    open_part = 0.5 * (1.0 + bent)
    active = gate_pre * open_part
    slope = open_part + 0.5 * gate_pre * (1.0 - bent * bent) * scale * (
        1.0 + 3 * 0.044715 * square
    )
    hidden = active * up_pre
    gated_ref[...] = (gate * hidden).astype(bf16)
    signal = jnp.sum(hidden * cot_hidden, axis=1, keepdims=True)
    back = gate * cot_hidden
    gate_back[...] = (back * up_pre * slope).astype(bf16)
    up_back[...] = (back * active).astype(bf16)
    high = signal.astype(bf16)
    low = (signal - high.astype(f32)).astype(bf16)
    lanes = lax.broadcasted_iota(jnp.int32, (signal.shape[0], wide), 1)
    signal = jnp.where(lanes == at[5], high.astype(f32), 0.0)
    signal = jnp.where(lanes == at[5] + wide // 2, low.astype(f32), signal)
    by_rows = ((1,), (1,))
    rows = dot(gate_back[...], gate_w[...], by_rows) + dot(up_back[...], up_w[...], by_rows)
    spread(picks, capacity, jnp.concatenate([rows, signal], axis=1), backs)


def run_expert(pieces, at, ids, router, weights, second, cot, capacity):
    count = len(pieces)
    rows, wide = 2 * count * capacity, router.shape[1]
    (length, width), hidden = second[0].shape, weights[0].shape[1]
    bf16, f32 = jnp.bfloat16, jnp.float32
    outs = [(rows, width)] * 2 + [(rows, hidden)] * 3
    outs = [(shape, bf16) for shape in outs] + [((wide, length), f32)]
    outs = outs + [((length, width + wide), bf16)] * count
    return run_kernel(
        functools.partial(expert_kernel, capacity, pieces),
        4 * count,
        at,
        (ids, router, *second, *cot, *weights),
        outs,
        6 + 4 * count,
        [pltpu.VMEM((rows, 1), f32)],
    )


def mixture_kernel(capacity, groups, at, ids, *refs):
    gated, down_w, outs = refs[: len(groups)], refs[len(groups)], refs[len(groups) + 1 :]
    length = outs[0].shape[0]
    for pieces, rows in zip(groups, gated):
        picks = []
        for piece in pieces:
            for part in range(2):
                start = piece * length + part * length // 2
                slots = slots_of(ids, at[5], start, length // 2)
                picks.append(one_hot(slots, capacity, jnp.bfloat16))
        spread(picks, capacity, dot(rows[...], down_w[...]), [outs[piece] for piece in pieces])


def row_sum_kernel(parts, at, *refs):
    arrays = [
        jnp.concatenate([ref[...] for ref in refs[n : n + parts]], axis=0)
        for n in range(0, len(refs) - len(refs) // (parts + 1), parts)
    ]
    outs = refs[len(arrays) * parts :]
    for out, right in zip(outs, arrays[1:]):
        out[...] = dot(arrays[0], right, ((0,), (0,))).astype(jnp.bfloat16)


def row_sums(at, left, *rights):
    operands = [part for parts in (left, *rights) for part in parts]
    outs = [((left[0].shape[1], right[0].shape[1]), jnp.bfloat16) for right in rights]
    kernel = functools.partial(row_sum_kernel, len(left))
    return run_kernel(kernel, 4 * len(rights), at, operands, outs, 24 if len(rights) == 1 else 56)


def branch_back_kernel(
    at, near, far, first_x, first_y, last_y, last_x, resid, gain, second, gates, router, cot, weight, *outs
):
    resid_grad_ref, branch_ref, attended_ref, router_ref, gain_ref = outs
    f32, bf16 = jnp.float32, jnp.bfloat16
    halves = [first_x[...].astype(f32) + last_y[...], first_y[...].astype(f32) + last_x[...]]
    total = near[...].astype(f32) + far[...] + jnp.concatenate(halves, axis=0)
    width = resid.shape[1]
    signal = total[:, width:]
    signal = signal + pltpu.roll(signal, signal.shape[1] // 2, 1)
    chosen = gates[...].T
    logit_grad = chosen * (signal - jnp.sum(chosen * signal, axis=-1, keepdims=True))
    logit_grad = logit_grad.astype(bf16)
    second_grad = total[:, :width] + dot(logit_grad, router[...], ((1,), (1,)))
    norm_grad, gain_grad = rms_back(resid[...], gain[...], second_grad)
    gain_ref[...] = gain_grad
    resid_grad = cot[...].astype(f32) + norm_grad
    resid_grad_ref[...] = resid_grad
    branch = resid_grad.astype(bf16)
    branch_ref[...] = branch
    wide = weight.shape[2]
    attended_ref[...] = (
        dot(branch[:, :wide], weight[0], ((1,), (1,)))
        + dot(branch[:, wide:], weight[1], ((1,), (1,)))
    ).astype(bf16)
    router_ref[...] = dot(second[...], logit_grad, ((0,), (0,)))


def attend_back_kernel(
    at, attended, probs, queries, keys, values, cosine, sine, branch, back_ref
):
    f32, bf16 = jnp.float32, jnp.bfloat16
    cosine_tab, sine_tab = cosine[...], -sine[...]
    group_size = HQ // HK
    places = back_ref.shape[0]
    branch_width = branch.shape[1] // places
    width = back_ref.shape[2] - branch_width
    for place in range(places):
        here = slice(place * branch_width, (place + 1) * branch_width)
        back_ref[place, :, width:] = branch[:, here]
    scale = HD ** (-0.5)

    def put(position, block):
        back_ref[position // width, :, position % width : position % width + HD] = block

    for group in range(HK):
        own = slice(group * HD, (group + 1) * HD)
        key, value = keys[:, own], values[:, own]
        key_grad = value_grad = 0.0
        start = group * (group_size + 2) * HD
        for member in range(group_size):
            head = group * group_size + member
            here = slice(head * HD, (head + 1) * HD)
            out_grad, query, prob = attended[:, here], queries[:, here], probs[head]
            prob_grad = dot(out_grad, value, ((1,), (1,)))
            prob_f = prob.astype(f32)
            inner = jnp.sum(prob_f * prob_grad, axis=-1, keepdims=True)
            score_grad = (prob_f * (prob_grad - inner)).astype(bf16)
            query_grad = turned(dot(score_grad, key) * scale, cosine_tab, sine_tab)
            put(start + member * HD, query_grad.astype(bf16))
            key_grad = key_grad + dot(score_grad, query, ((0,), (0,)))
            value_grad = value_grad + dot(prob, out_grad, ((0,), (0,)))
        key_grad = turned(key_grad * scale, cosine_tab, sine_tab)
        put(start + group_size * HD, key_grad.astype(bf16))
        put(start + (group_size + 1) * HD, value_grad.astype(bf16))


def first_back_kernel(at, back, weight, tokens, gain, resid_grad, tokens_ref, gain_ref):
    f32 = jnp.float32
    parts = back.shape[0]
    cols = weight.shape[0] * weight.shape[2] // parts
    first_grad = 0.0
    for part in range(parts):
        group, place = divmod(part * cols, weight.shape[2])
        first_grad = first_grad + dot(
            back[part, :, :cols], weight[group, :, place : place + cols], ((1,), (1,))
        )
    norm_grad, gain_grad = rms_back(tokens[...].astype(f32), gain[...], first_grad)
    gain_ref[...] = gain_grad
    tokens_ref[...] = (resid_grad[...] + norm_grad).astype(jnp.bfloat16)


def dense_grad_kernel(at, narrow, back, *refs):
    pieces, out_ref, held, sems = refs[:8], refs[8], refs[9], refs[10]
    copies = [
        pltpu.make_async_copy(piece, held.at[n], sems.at[n]) for n, piece in enumerate(pieces)
    ]
    for copy in copies:
        copy.start()
    depth, rows, cols = out_ref.shape
    length = held.shape[1] // 2
    qkv_width = cols - held.shape[2] // back.shape[0]
    narrow = sum(narrow[place].astype(jnp.float32) for place in range(narrow.shape[0]))
    sums = [0.0, 0.0]
    for n, copy in enumerate(copies):
        copy.wait()
        dc, dy, dx = n // 4, n // 2 % 2, n % 2
        place = 4 * (at[0] ^ dy) + 2 * (at[1] ^ dc) + (at[2] ^ dx)
        own = back[place]
        sums[0] = sums[0] + dot(held[n, length:], own[:, :qkv_width], ((0,), (0,)))
        sums[1] = sums[1] + dot(held[n, :length], own[:, qkv_width:], ((0,), (0,)))
    wide = held.shape[2] // depth
    each = narrow.shape[0] // depth
    for z in range(depth):
        here = slice(z * wide, (z + 1) * wide)
        both = jnp.concatenate([part[here] for part in sums], axis=1)
        out_ref[z, :wide] = both.astype(jnp.bfloat16)
        kept = [narrow[z * each : (z + 1) * each], jnp.zeros((rows - wide - each, cols), jnp.float32)]
        out_ref[z, wide:] = jnp.concatenate(kept, axis=0).astype(jnp.bfloat16)


def finish_kernel(at, sums, query_ref, key_ref, value_ref, output_ref):
    places, _, cols = sums.shape
    rows, out_width = query_ref.shape[0], output_ref.shape[1] // places
    width = cols - out_width
    for place in range(places):
        block = sums[place, :rows].astype(jnp.float32)
        output_ref[:, place * out_width : (place + 1) * out_width] = block[:, width:]
        for at_col in range(0, width, HD):
            group, head = divmod((place * width + at_col) // HD, HQ // HK + 2)
            part = block[:, at_col : at_col + HD]
            if head < HQ // HK:
                start = (group * (HQ // HK) + head) * HD
                query_ref[:, start : start + HD] = part
            elif head == HQ // HK:
                key_ref[:, group * HD : (group + 1) * HD] = part
            else:
                value_ref[:, group * HD : (group + 1) * HD] = part


def local_pairs(
    tokens,
    norm1_gain,
    w_query,
    w_key,
    w_value,
    w_out,
    norm2_gain,
    w_router,
    w_gate,
    w_up,
    w_down,
    expert_ids,
    prefix_len,
    out_grad,
):
    bf16, f32 = jnp.bfloat16, jnp.float32
    length, model_width = tokens.shape
    shard_rows = w_query.shape[0]
    local_count, _, hidden_width = w_gate.shape
    owners = lax.axis_size("x")
    depth = lax.axis_size("z")
    plane = lax.axis_size(PLANE)
    experts_all = w_router.shape[1]
    block_rows = length // MICRO
    capacity = 3 * block_rows * expert_ids.shape[1] // (2 * experts_all)
    plane_rows = plane * length
    blocks = plane_rows // block_rows
    q_cols, kv_cols = w_query.shape[1], w_key.shape[1]
    qkv_cols = q_cols + 2 * kv_cols
    q_group, out_half = q_cols // HK, model_width // 2
    y, c, x, z = (lax.axis_index(axis) for axis in ("y", "c", "x", "z"))
    own_local = 2 * y + c
    own_expert = x * local_count + own_local
    at = jnp.stack([y, c, x, z, prefix_len[0], own_expert, own_local])

    own_half = jnp.concatenate(
        [
            lax.dynamic_slice_in_dim(part, x * (part.shape[1] // 2), part.shape[1] // 2, 1)
            for part in (w_query, w_key, w_value, w_out)
        ],
        axis=1,
    )
    narrow = jnp.concatenate([w_router, norm1_gain[:, None], norm2_gain[:, None]], axis=1)
    narrow = jnp.pad(narrow, ((0, 0), (0, 128 - narrow.shape[1])))
    router_w = small_group_gather(narrow)
    ids_all = small_gather(expert_ids.T)
    column = [own_half] + shifts(own_half)
    cot_sides = plane_sides(after(out_grad, router_w, ids_all))
    qkv_half = qkv_cols // 2
    qkv_column = jnp.stack([part[:, :qkv_half] for part in column])
    out_column = jnp.stack([part[:, qkv_half:] for part in column])
    qkv_column, out_column = lax.optimization_barrier((qkv_column, out_column, *cot_sides))[:2]
    sliced = after(own_local, column[-1])
    gate_w, up_w, down_w = (
        lax.dynamic_index_in_dim(weight, sliced, 0, keepdims=False)
        for weight in (w_gate, w_up, w_down)
    )
    qkv_sides = plane_sides(qkv_column)
    qkv_corner = plane_corner(qkv_sides, (gate_w, up_w, down_w))
    out_sides = plane_sides(after(out_column, *qkv_sides))
    qkv_pieces = plane_pieces(qkv_column, qkv_sides, qkv_corner)
    gains = router_w[:, experts_all : experts_all + 2].T.astype(f32)
    gain_one, gain_two = gains[:1], gains[1:]

    cosine_tab, sine_tab = angles(length, HD)
    cosine_all = jnp.concatenate([cosine_tab, cosine_tab], axis=2)[:, 0]
    sine_all = jnp.concatenate([-sine_tab, sine_tab], axis=2)[:, 0]
    weight_lead = (2, depth, 2, 2, shard_rows)
    first_in, queries, keys_rot, values_b, attended, probs, qkv_w = run_kernel(
        attend_kernel,
        11,
        at,
        (tokens, gain_one, cosine_all, sine_all, *qkv_pieces),
        [
            ((length, model_width), bf16),
            ((length, q_cols), bf16),
            ((length, kv_cols), bf16),
            ((length, kv_cols), bf16),
            ((length, q_cols), bf16),
            ((HQ, length, length), bf16),
            (weight_lead + (qkv_half,), bf16),
        ],
        48,
        [
            pltpu.VMEM((HQ, length, length), bf16),
            pltpu.VMEM(weight_lead + (qkv_half,), bf16),
            pltpu.SemaphoreType.DMA((HK + 1,)),
        ],
        hbm_out=2,
    )
    out_sides = lax.optimization_barrier((*out_sides, attended))[:2]
    out_corner = plane_corner(out_sides)
    cot_corner = plane_corner(cot_sides)
    out_pieces = plane_pieces(out_column, out_sides, out_corner)
    cot_pieces = plane_pieces(out_grad, cot_sides, cot_corner)
    resid, second_in, output_w = run_kernel(
        project_kernel,
        4,
        at,
        (tokens, after(gain_two, cot_corner), attended, *out_pieces),
        [
            ((length, model_width), f32),
            ((length, model_width), bf16),
            (weight_lead + (out_half,), bf16),
        ],
        44,
        [pltpu.VMEM(weight_lead + (out_half,), bf16), pltpu.SemaphoreType.DMA],
        hbm_out=1,
    )
    qkv_w = qkv_w.reshape(HK, model_width, qkv_half)
    output_w = output_w.reshape(2, q_cols, out_half)

    expert = functools.partial(
        run_expert,
        at=at,
        ids=ids_all,
        router=router_w,
        weights=(gate_w, up_w, down_w),
        capacity=capacity,
    )
    second_sides = plane_sides(second_in)
    groups = ((0, 4), (1, 5, 2, 6), (3, 7))
    second_pieces = {0: second_in, 4: swap(second_in, "c")}

    def run_group(pieces):
        return expert(
            pieces,
            second=[second_pieces[piece] for piece in pieces],
            cot=[cot_pieces[piece] for piece in pieces],
        )

    stage_own = run_group(groups[0])
    second_sides = lax.optimization_barrier((*second_sides, stage_own[0]))[:2]
    for piece, block in zip((1, 2), second_sides):
        second_pieces[piece], second_pieces[piece + 4] = block, swap(block, "c")
    stage_sides = run_group(groups[1])
    second_corner = plane_corner(second_sides, later=(stage_sides[0],))
    second_pieces[3], second_pieces[7] = second_corner, swap(second_corner, "c")
    own_near, own_far = stage_own[6:]
    own_far = swap(own_far, "c")
    x_near, x_far, y_near, y_far = stage_sides[6:]
    back_x, back_y = over_core(x_near, x_far), over_core(y_near, y_far)
    first_x, first_y = early_sums(back_x, back_y)
    stage_corner = run_group(groups[2])
    corner = over_core(*stage_corner[6:])
    passed = corner_first(corner)
    stages = (stage_own, stage_sides, stage_corner)
    rows_in, rows_cot, gated, gate_back, up_back = ([stage[n] for stage in stages] for n in range(5))
    gates = stage_own[5]
    own_near, own_far, first_x, first_y, corner, first_rows = lax.optimization_barrier(
        (own_near, own_far, first_x, first_y, corner, rows_cot[0])
    )
    (down_part,) = row_sums(at, [first_rows] + rows_cot[1:], gated)
    down_sum = scatter_sum(down_part, "z")
    passed = lax.optimization_barrier((*passed, down_part))[:2]
    last_y, last_x, *sent = corner_last(back_x, back_y, passed)
    gate_part, up_part = row_sums(
        at, [after(rows_in[0], *sent)] + rows_in[1:], gate_back, up_back
    )
    gate_sum, up_sum = scatter_sum(gate_part, "z"), scatter_sum(up_part, "z")
    own_near = after(own_near, gate_part)

    resid_grad, branch_grad, attended_grad, router_acc, gain_two_grad = run_kernel(
        branch_back_kernel,
        6,
        at,
        (
            own_near,
            own_far,
            first_x,
            first_y,
            last_y,
            last_x,
            resid,
            gain_two,
            second_in,
            gates,
            router_w,
            out_grad,
            output_w,
        ),
        [
            ((length, model_width), f32),
            ((length, model_width), bf16),
            ((length, q_cols), bf16),
            ((model_width, 128), f32),
            ((1, model_width), f32),
        ],
        56,
    )
    qkv_width, branch_width = qkv_cols // plane, model_width // plane
    dense_cols = qkv_width + branch_width
    (back_cols,) = run_kernel(
        attend_back_kernel,
        6,
        at,
        (
            attended_grad,
            probs,
            queries,
            keys_rot,
            values_b,
            cosine_all,
            sine_all,
            branch_grad,
        ),
        [((plane, length, dense_cols), bf16)],
        56,
    )
    tokens_grad, gain_one_grad = run_kernel(
        first_back_kernel,
        5,
        at,
        (back_cols, qkv_w, tokens, gain_one, resid_grad),
        [((length, model_width), bf16), ((1, model_width), f32)],
        56,
    )

    both = jnp.concatenate(
        lax.optimization_barrier((attended, first_in, last_y, last_x))[:2], axis=0
    )
    both_sides = plane_sides(both)
    narrow_part = jnp.concatenate(
        [router_acc[:, :experts_all], gain_one_grad.T, gain_two_grad.T], axis=1
    )
    narrow_cols = -(-narrow_part.shape[1] // owners) * owners
    narrow_part = jnp.pad(narrow_part, ((0, 0), (0, narrow_cols - narrow_part.shape[1])))
    narrow_part = jnp.transpose(
        narrow_part.reshape(depth, 2, 2, shard_rows, owners, narrow_cols // owners),
        (1, 2, 4, 0, 3, 5),
    ).reshape(plane, depth, shard_rows * narrow_cols // owners)
    narrow_len = narrow_part.shape[2]
    narrow_rows = -(-narrow_len // dense_cols)
    each_rows = -(-narrow_rows // 4) * 4
    narrow_part = jnp.pad(
        narrow_part, ((0, 0), (0, 0), (0, each_rows * dense_cols - narrow_len))
    ).reshape(plane, depth * each_rows, dense_cols)
    back_cols = exchange(after(back_cols, down_sum), PLANE)
    narrow_part = exchange(narrow_part.astype(bf16), PLANE)
    both_corner = plane_corner(both_sides, (back_cols,))
    both_pieces = plane_pieces(both, both_sides, both_corner)
    kept_rows = -(-narrow_rows // 16) * 16
    wide_rows = local_count * shard_rows
    dense_shape = (depth, wide_rows + kept_rows, dense_cols)
    dense_part = pl.pallas_call(
        dense_grad_kernel,
        out_shape=jax.ShapeDtypeStruct(dense_shape, bf16),
        in_specs=[SCALARS, WHOLE, WHOLE] + [IN_HBM] * 8,
        out_specs=WHOLE,
        scratch_shapes=[
            pltpu.VMEM((plane, 2 * length, model_width), bf16),
            pltpu.SemaphoreType.DMA((plane,)),
        ],
        cost_estimate=cost(8),
        compiler_params=pltpu.CompilerParams(vmem_limit_bytes=32 * 2**20),
    )(at, narrow_part, after(back_cols, gate_sum), *both_pieces)
    dense_part = after(dense_part, up_sum)
    dense_sum = scatter_sum(dense_part.reshape(-1, dense_cols), "z")
    wide_sum = dense_sum[: local_count * shard_rows].reshape(2, 2, 1, shard_rows, dense_cols)
    wide_sum = jnp.broadcast_to(wide_sum, (2, 2, owners, shard_rows, dense_cols)).reshape(
        plane, shard_rows, dense_cols
    )
    narrow_sum = dense_sum[local_count * shard_rows :][:narrow_rows]
    narrow_sum = jnp.broadcast_to(narrow_sum[None], (plane, narrow_rows, dense_cols))
    pad_rows = -(shard_rows + narrow_rows) % 16
    padding = jnp.zeros((plane, pad_rows, dense_cols), bf16)
    dense_sum = exchange(jnp.concatenate([wide_sum, narrow_sum, padding], axis=1), PLANE)
    query_grad, key_grad, value_grad, output_grad = run_kernel(
        finish_kernel,
        2,
        at,
        (dense_sum,),
        [
            ((shard_rows, q_cols), f32),
            ((shard_rows, kv_cols), f32),
            ((shard_rows, kv_cols), f32),
            ((shard_rows, model_width), f32),
        ],
    )
    narrow_sum = dense_sum[:, shard_rows : shard_rows + narrow_rows].reshape(
        2, 2, owners, narrow_rows * dense_cols
    )
    narrow_sum = narrow_sum[y, c, :, :narrow_len].reshape(owners, shard_rows, -1)
    narrow_sum = jnp.moveaxis(narrow_sum, 0, 1).reshape(shard_rows, narrow_cols).astype(f32)

    shares = run_kernel(
        functools.partial(mixture_kernel, capacity, groups),
        10,
        at,
        (ids_all, after(gated[0], both_corner), *gated[1:], down_w),
        [((length, model_width), bf16)] * plane,
        56,
    )
    mixed = [over_core(near, far) for near, far in zip(shares[:4], shares[4:])]
    early = early_sums(mixed[1], mixed[2])
    last = corner_last(mixed[1], mixed[2], corner_first(mixed[3]))[:2]
    mixture = jnp.concatenate(
        [left.astype(f32) + right.astype(f32) for left, right in zip(early, last)], axis=0
    )
    block_out = (resid + (mixture + mixed[0].astype(f32))).astype(bf16)

    def placed(total):
        total = exchange(total, ("y", "c"))
        return total.reshape(local_count, shard_rows, hidden_width).astype(f32)

    return (
        block_out,
        tokens_grad,
        narrow_sum[:, experts_all],
        query_grad,
        key_grad,
        value_grad,
        output_grad,
        narrow_sum[:, experts_all + 1],
        narrow_sum[:, :experts_all],
        placed(after(gate_sum, dense_part)),
        placed(after(up_sum, dense_part)),
        jnp.swapaxes(placed(after(down_sum, dense_part)), 1, 2),
    )


def solution(mesh):
    groups, owners = mesh.shape["dp"], mesh.shape["expert"]
    grid = jax.sharding.Mesh(
        mesh.devices.reshape(groups // 4, 2, 2, owners), ("z", "y", "c", "x")
    )
    rows = P(("z", "y", "c", "x"), None)
    shard, shard_rows = P(GROUP), P(GROUP, None)
    expert = P("x", None, None)
    return jax.shard_map(
        local_pairs if owners == 2 else local_wide,
        mesh=grid,
        in_specs=(
            rows,
            shard,
            shard_rows,
            shard_rows,
            shard_rows,
            shard_rows,
            shard,
            shard_rows,
            expert,
            expert,
            expert,
            rows,
            P(("z", "y", "c", "x")),
            rows,
        ),
        out_specs=(
            rows,
            rows,
            shard,
            shard_rows,
            shard_rows,
            shard_rows,
            shard_rows,
            shard,
            shard_rows,
            P("x", GROUP, None),
            P("x", GROUP, None),
            P("x", None, GROUP),
        ),
        check_vma=False,
    )
```

```python
import functools
import math

import jax
import jax.numpy as jnp
from jax import lax
from jax.experimental import pallas as pl
from jax.experimental.pallas import tpu as pltpu
from jax.sharding import PartitionSpec as P

HQ = 12
HK = 2
HD = 128
MICRO = 2
PLANE = ("y", "c", "x")
GROUP = ("z", "y", "c")


def rms_scale(values, gain_vec):
    inverse = lax.rsqrt(jnp.mean(values * values, axis=-1, keepdims=True) + 1e-06)
    return values * inverse * gain_vec


def angles(length, head_size):
    positions = jnp.arange(length).astype(jnp.float32)
    freq_rates = jnp.exp(
        -(2.0 * jnp.arange(head_size // 2).astype(jnp.float32) / head_size) * math.log(1000000.0)
    )
    angle_tab = positions[:, None] * freq_rates[None, :]
    return (jnp.cos(angle_tab)[:, None, :], jnp.sin(angle_tab)[:, None, :])


def rotary(values, cosine_tab, sine_tab):
    half_dim = values.shape[-1] // 2
    first_half = values[..., :half_dim]
    second_half = values[..., half_dim:]
    return jnp.concatenate(
        [
            first_half * cosine_tab - second_half * sine_tab,
            second_half * cosine_tab + first_half * sine_tab,
        ],
        axis=-1,
    )


def expert_act(gate_pre, up_pre):
    return jax.nn.gelu(gate_pre, approximate=True) * up_pre


def left_product(left_mat, right_mat):
    return lax.dot_general(
        left_mat, right_mat, (((0,), (0,)), ((), ())), preferred_element_type=jnp.float32
    )


def gather(block, axes):
    return lax.all_gather(block, axes, axis=0, tiled=True)


def exchange(block, axes):
    return lax.all_to_all(block, axes, split_axis=0, concat_axis=0, tiled=True)


def scatter_sum(block, axes):
    return lax.psum_scatter(block, axes, scatter_dimension=0, tiled=True)


def by_owner(cols, parts):
    rows, total = cols.shape
    return jnp.moveaxis(cols.reshape(rows, parts, total // parts), 1, 0).reshape(
        parts * rows, total // parts
    )


def local_wide(
    tokens,
    norm1_gain,
    w_query,
    w_key,
    w_value,
    w_out,
    norm2_gain,
    w_router,
    w_gate,
    w_up,
    w_down,
    expert_ids,
    prefix_len,
    out_grad,
):
    bf16, f32 = jnp.bfloat16, jnp.float32
    length, model_width = tokens.shape
    shard_rows = w_query.shape[0]
    local_count, _, hidden_width = w_gate.shape
    owners = lax.axis_size("x")
    depth = lax.axis_size("z")
    plane = lax.axis_size(PLANE)
    experts_all = w_router.shape[1]
    top_count = expert_ids.shape[1]
    block_rows = length // MICRO
    capacity = 3 * block_rows * top_count // (2 * experts_all)
    plane_rows = plane * length
    blocks = plane_rows // block_rows
    group_size = HQ // HK
    score_scale = HD ** (-0.5)
    q_cols, kv_cols = w_query.shape[1], w_key.shape[1]
    own_local = lax.axis_index(("y", "c"))
    own_expert = lax.axis_index("x") * local_count + own_local
    own_place = lax.axis_index(PLANE)

    narrow = jnp.concatenate([w_router, norm1_gain[:, None], norm2_gain[:, None]], axis=1)
    narrow = jnp.pad(narrow, ((0, 0), (0, -narrow.shape[1] % 128)))
    packed = gather(jnp.concatenate([w_query, w_key, w_value, narrow], axis=1), GROUP)
    qkv_cols = q_cols + 2 * kv_cols
    qkv_w = packed[:, :qkv_cols]
    router_w = packed[:, qkv_cols : qkv_cols + experts_all]
    gains = packed[:, qkv_cols + experts_all : qkv_cols + experts_all + 2].T.astype(f32)
    gain_one, gain_two = gains[0], gains[1]
    output_w = gather(w_out, GROUP)

    ids_all = gather(expert_ids, PLANE)
    cot_all = gather(out_grad, PLANE)
    chosen_mask = jnp.any(
        ids_all[:, :, None] == jnp.arange(experts_all, dtype=jnp.int32)[None, None, :], axis=1
    )
    own_mask = jnp.any(ids_all == own_expert, axis=1).reshape(blocks, block_rows)
    place = jnp.cumsum(own_mask.astype(jnp.int32), axis=1) - 1
    dispatch = (
        own_mask[:, None, :]
        & (place[:, None, :] == jnp.arange(capacity, dtype=jnp.int32)[None, :, None])
    ).astype(bf16)

    cosine_tab, sine_tab = angles(length, HD)
    inputs_f = tokens.astype(f32)
    first_in = rms_scale(inputs_f, gain_one).astype(bf16)
    qkv = jnp.dot(first_in, qkv_w, preferred_element_type=f32)
    queries = (
        rotary(qkv[:, :q_cols].reshape(length, HQ, HD), cosine_tab, sine_tab)
        .astype(bf16)
        .reshape(length, HK, group_size, HD)
    )
    keys_rot = rotary(
        qkv[:, q_cols : q_cols + kv_cols].reshape(length, HK, HD), cosine_tab, sine_tab
    ).astype(bf16)
    values_b = qkv[:, q_cols + kv_cols :].astype(bf16).reshape(length, HK, HD)
    positions = jnp.arange(length)
    allowed = (positions[None, :] <= positions[:, None]) | (positions[None, :] < prefix_len[0])

    def masked_scores():
        scores = jnp.einsum("ihrd,jhd->hrij", queries, keys_rot, preferred_element_type=f32)
        return jnp.where(allowed, scores * score_scale, -1e30)

    masked = masked_scores()
    row_peak = jnp.max(masked, axis=-1, keepdims=True)
    log_total = row_peak + jnp.log(jnp.sum(jnp.exp(masked - row_peak), axis=-1, keepdims=True))
    prob_bf = jnp.exp(masked - log_total).astype(bf16)
    attended = jnp.einsum("hrij,jhd->ihrd", prob_bf, values_b, preferred_element_type=f32)
    attended = attended.reshape(length, HQ * HD).astype(bf16)
    resid = inputs_f + jnp.dot(attended, output_w, preferred_element_type=f32)
    second_in = rms_scale(resid, gain_two).astype(bf16)

    second_all = gather(second_in, PLANE)
    logits = jnp.dot(second_all, router_w, preferred_element_type=f32)
    gates_all = jax.nn.softmax(jnp.where(chosen_mask, logits, -jnp.inf), axis=-1)
    own_gates = lax.dynamic_index_in_dim(gates_all, own_expert, 1, keepdims=False)
    own_gates = own_gates.reshape(blocks, block_rows)
    gate_rows = jnp.einsum(
        "bct,bt->bc", dispatch.astype(f32), own_gates, precision=lax.Precision.HIGHEST
    )[:, :, None]
    gate_w = lax.dynamic_index_in_dim(w_gate, own_local, 0, keepdims=False)
    up_w = lax.dynamic_index_in_dim(w_up, own_local, 0, keepdims=False)
    down_w = lax.dynamic_index_in_dim(w_down, own_local, 0, keepdims=False)

    def to_rows(array):
        return jnp.einsum(
            "bct,btd->bcd",
            dispatch,
            array.reshape(blocks, block_rows, model_width),
            preferred_element_type=f32,
        ).astype(bf16)

    def to_tokens(rows):
        return (
            jnp.einsum("bct,bcd->btd", dispatch, rows.astype(bf16), preferred_element_type=f32)
            .astype(bf16)
            .reshape(plane_rows, model_width)
        )

    rows_in = to_rows(second_all)
    rows_cot = to_rows(cot_all)
    gate_pre = jnp.einsum("bcd,df->bcf", rows_in, gate_w, preferred_element_type=f32)
    up_pre = jnp.einsum("bcd,df->bcf", rows_in, up_w, preferred_element_type=f32)
    hidden, act_pull = jax.vjp(expert_act, gate_pre, up_pre)
    gated = (gate_rows * hidden).astype(bf16)
    down_part = jnp.einsum("bcd,bcf->df", rows_cot, gated, preferred_element_type=f32)
    down_sum = scatter_sum(down_part.astype(bf16), "z")
    cot_hidden = jnp.einsum("bcd,fd->bcf", rows_cot, down_w, preferred_element_type=f32)
    gate_signal_rows = jnp.sum(hidden * cot_hidden, axis=-1)
    gate_pgrad, up_pgrad = act_pull(gate_rows * cot_hidden)
    gate_pgrad = gate_pgrad.astype(bf16)
    up_pgrad = up_pgrad.astype(bf16)
    gate_part = jnp.einsum("bcd,bcf->df", rows_in, gate_pgrad, preferred_element_type=f32)
    gate_sum = scatter_sum(gate_part.astype(bf16), "z")
    up_part = jnp.einsum("bcd,bcf->df", rows_in, up_pgrad, preferred_element_type=f32)
    up_sum = scatter_sum(up_part.astype(bf16), "z")
    rows_grad = jnp.einsum("bcf,df->bcd", gate_pgrad, gate_w, preferred_element_type=f32)
    rows_grad = rows_grad + jnp.einsum("bcf,df->bcd", up_pgrad, up_w, preferred_element_type=f32)
    second_back = scatter_sum(to_tokens(rows_grad), PLANE).astype(f32)
    gate_signal = jnp.einsum(
        "bct,bc->bt", dispatch.astype(f32), gate_signal_rows, precision=lax.Precision.HIGHEST
    )
    gate_signal = exchange(gate_signal.reshape(plane, length), PLANE)
    gate_signal = jnp.transpose(
        gate_signal.reshape(local_count, owners, length), (2, 1, 0)
    ).reshape(length, experts_all)
    expert_rows = jnp.einsum("bcf,fd->bcd", gated, down_w, preferred_element_type=f32)
    mixture = scatter_sum(to_tokens(expert_rows), PLANE).astype(f32)
    block_out = (resid + mixture).astype(bf16)

    cotangent = out_grad.astype(f32)
    gate_probs = lax.dynamic_slice_in_dim(gates_all, own_place * length, length, 0)
    logit_grad = (
        gate_probs
        * (gate_signal - jnp.sum(gate_probs * gate_signal, axis=-1, keepdims=True))
    ).astype(bf16)
    router_acc = left_product(second_in, logit_grad)
    second_grad = second_back + jnp.dot(logit_grad, router_w.T, preferred_element_type=f32)
    _, norm_two_pull = jax.vjp(rms_scale, resid, gain_two)
    resid_norm_grad, gain_two_grad = norm_two_pull(second_grad)
    resid_grad = cotangent + resid_norm_grad
    branch_grad = resid_grad.astype(bf16)

    attended_all = gather(attended, PLANE)
    branch_cols = exchange(by_owner(branch_grad, plane), PLANE)
    output_part = left_product(attended_all, branch_cols)
    attended_grad = jnp.dot(branch_grad, output_w.T, preferred_element_type=f32).astype(bf16)
    attended_grad = attended_grad.reshape(length, HK, group_size, HD)
    masked = masked_scores()
    prob_full = jnp.exp(masked - log_total)
    prob_bf = prob_full.astype(bf16)
    prob_grad = jnp.einsum("ihrd,jhd->hrij", attended_grad, values_b, preferred_element_type=f32)
    row_inner = jnp.sum(prob_full * prob_grad, axis=-1, keepdims=True)
    score_grad = (prob_full * (prob_grad - row_inner)).astype(bf16)
    query_rot_grad = (
        jnp.einsum("hrij,jhd->ihrd", score_grad, keys_rot, preferred_element_type=f32)
        * score_scale
    )
    query_back = rotary(query_rot_grad.reshape(length, HQ, HD), cosine_tab, -sine_tab)
    query_back = query_back.astype(bf16).reshape(length, HQ * HD)
    key_rot_grad = (
        jnp.einsum("hrij,ihrd->jhd", score_grad, queries, preferred_element_type=f32)
        * score_scale
    )
    key_back = rotary(key_rot_grad, cosine_tab, -sine_tab).astype(bf16).reshape(length, HK * HD)
    value_back = jnp.einsum("hrij,ihrd->jhd", prob_bf, attended_grad, preferred_element_type=f32)
    value_back = value_back.astype(bf16).reshape(length, HK * HD)
    qkv_back = jnp.concatenate([query_back, key_back, value_back], axis=1)
    first_all = gather(first_in, PLANE)
    qkv_part = left_product(first_all, exchange(by_owner(qkv_back, plane), PLANE))
    first_grad = lax.dot_general(
        qkv_back, qkv_w, (((1,), (1,)), ((), ())), preferred_element_type=f32
    )
    _, norm_one_pull = jax.vjp(rms_scale, inputs_f, gain_one)
    input_norm_grad, gain_one_grad = norm_one_pull(first_grad)
    tokens_grad = (resid_grad + input_norm_grad).astype(bf16)

    narrow_part = jnp.concatenate(
        [router_acc, gain_one_grad[:, None], gain_two_grad[:, None]], axis=1
    ).astype(bf16)
    narrow_cols = narrow_part.shape[1]
    narrow_sum = lax.psum(scatter_sum(narrow_part, GROUP), "x").astype(f32)
    dense_part = jnp.concatenate([qkv_part, output_part], axis=1).astype(bf16)
    dense_sum = scatter_sum(dense_part, "z")
    dense_cols = dense_sum.shape[1]
    dense_sum = gather(dense_sum, PLANE).reshape(plane, local_count, shard_rows, dense_cols)
    dense_sum = lax.dynamic_index_in_dim(dense_sum, own_local, 1, keepdims=False).astype(f32)
    dense_sum = jnp.moveaxis(dense_sum, 0, 1)
    qkv_width = qkv_cols // plane
    qkv_sum = dense_sum[:, :, :qkv_width].reshape(shard_rows, qkv_cols)
    output_sum = dense_sum[:, :, qkv_width:].reshape(shard_rows, model_width)

    def placed(total):
        total = exchange(total, ("y", "c"))
        return total.reshape(local_count, shard_rows, hidden_width).astype(f32)

    return (
        block_out,
        tokens_grad,
        narrow_sum[:, experts_all],
        qkv_sum[:, :q_cols],
        qkv_sum[:, q_cols : q_cols + kv_cols],
        qkv_sum[:, q_cols + kv_cols :],
        output_sum,
        narrow_sum[:, experts_all + 1],
        narrow_sum[:, :experts_all],
        placed(gate_sum),
        placed(up_sum),
        jnp.swapaxes(placed(down_sum), 1, 2),
    )


def rounded(values):
    return lax.reduce_precision(values, 8, 7).astype(jnp.bfloat16)


def after(block, *others):
    return lax.optimization_barrier((block,) + others)[0]


def swap(block, axis):
    return lax.ppermute(block, axis, [(0, 1), (1, 0)])


def shifts(block):
    depth = lax.axis_size("z")
    return [
        lax.ppermute(block, "z", [(i, (i + k) % depth) for i in range(depth)])
        for k in range(1, depth)
    ]


def plane_sides(block):
    return swap(block, "x"), swap(block, "y")


def plane_corner(sides, before=(), later=()):
    over_x, over_y = sides
    half = over_x.shape[0] // 2
    over_y, over_x = lax.optimization_barrier((over_y[:half], over_x[half:]) + before)[:2]
    parts = (swap(over_y, "x"), swap(over_x, "y"))
    return jnp.concatenate(lax.optimization_barrier(parts + later)[:2], axis=0)


def plane_pieces(block, sides=None, corner=None):
    sides = plane_sides(block) if sides is None else sides
    corner = plane_corner(sides) if corner is None else corner
    pieces = [block, *sides, corner]
    return pieces + [swap(piece, "c") for piece in pieces]


def small_gather(block):
    for axis in ("x", "y", "c"):
        block = jnp.concatenate([block, swap(block, axis)], axis=1)
    return block


def small_group_gather(block):
    depth = lax.axis_size("z")
    order = jnp.stack(([block] + shifts(block))[::-1] * 2)
    start = (depth - 1 - lax.axis_index("z")) % depth
    total = lax.dynamic_slice_in_dim(order, start, depth, 0)[:, None, None]
    for dim, axis in ((1, "y"), (2, "c")):
        other = swap(total, axis)
        last = lax.axis_index(axis) == 1
        pair = [jnp.where(last, other, total), jnp.where(last, total, other)]
        total = jnp.concatenate(pair, axis=dim)
    return total.reshape(-1, block.shape[1])


def add(left, right):
    return rounded(left.astype(jnp.float32) + right.astype(jnp.float32))


def over_core(near, far):
    return add(near, swap(far, "c"))


def early_sums(over_x, over_y):
    half = over_x.shape[0] // 2
    return swap(over_x[:half], "x"), swap(over_y[half:], "y")


def corner_first(corner):
    half = corner.shape[0] // 2
    return swap(corner[:half], "x"), swap(corner[half:], "y")


def corner_last(over_x, over_y, first):
    half = over_x.shape[0] // 2
    over_y, over_x = add(over_y[:half], first[0]), add(over_x[half:], first[1])
    return swap(over_y, "y"), swap(over_x, "x"), over_y, over_x


def cost(micros):
    return pl.CostEstimate(flops=micros * 10**9, bytes_accessed=micros * 10**6, transcendentals=0)


def dot(left, right, dims=((1,), (0,)), precision=None):
    return lax.dot_general(
        left, right, (dims, ((), ())), precision=precision, preferred_element_type=jnp.float32
    )


WHOLE = pl.BlockSpec(memory_space=pltpu.VMEM)
IN_HBM = pl.BlockSpec(memory_space=pltpu.HBM)
SCALARS = pl.BlockSpec(memory_space=pltpu.SMEM)


def run_kernel(kernel, micros, at, operands, outs, megabytes=16, scratch=(), hbm_in=0, hbm_out=0):
    return pl.pallas_call(
        kernel,
        out_shape=[jax.ShapeDtypeStruct(shape, dtype) for shape, dtype in outs],
        in_specs=[SCALARS] + [WHOLE] * (len(operands) - hbm_in) + [IN_HBM] * hbm_in,
        out_specs=[WHOLE] * (len(outs) - hbm_out) + [IN_HBM] * hbm_out,
        scratch_shapes=scratch,
        cost_estimate=cost(micros),
        compiler_params=pltpu.CompilerParams(vmem_limit_bytes=megabytes * 2**20),
    )(at, *operands)


def place_pieces(at, refs, weight):
    depth = weight.shape[1]
    for n, ref in enumerate(refs):
        dc, dy, dx = n // 4, n // 2 % 2, n % 2
        for k in range(depth):
            z = lax.rem(at[3] + depth - k, depth)
            weight[at[2] ^ dx, z, at[0] ^ dy, at[1] ^ dc] = ref[k]


def rms_kernel(values, gain):
    inverse = lax.rsqrt(jnp.mean(values * values, axis=-1, keepdims=True) + 1e-06)
    return (values * inverse * gain).astype(jnp.bfloat16)


def rms_back(values, gain, grad):
    inverse = lax.rsqrt(jnp.mean(values * values, axis=-1, keepdims=True) + 1e-06)
    normed = values * inverse
    gain_grad = jnp.sum(grad * normed, axis=0, keepdims=True)
    grad = grad * gain
    along = jnp.mean(grad * normed, axis=-1, keepdims=True)
    return inverse * (grad - normed * along), gain_grad


def turned(values, cosine_tab, sine_tab):
    return values * cosine_tab + pltpu.roll(values, HD // 2, 1) * sine_tab


def attend_kernel(at, tokens, gain, cosine, sine, *refs):
    first_ref, query_ref, key_ref, value_ref, out_ref = refs[8:13]
    prob_out, weight_out, prob_ref, weight, sems = refs[13:]
    place_pieces(at, refs[:8], weight)
    copies = [pltpu.make_async_copy(weight, weight_out, sems.at[HK])]
    copies[0].start()
    length = tokens.shape[0]
    first_in = rms_kernel(tokens[...].astype(jnp.float32), gain[...])
    first_ref[...] = first_in
    rows = lax.broadcasted_iota(jnp.int32, (length, length), 0)
    cols = lax.broadcasted_iota(jnp.int32, (length, length), 1)
    allowed = (cols <= rows) | (cols < at[4])
    cosine_tab, sine_tab = cosine[...], sine[...]
    group_size = HQ // HK
    for group in range(HK):
        matrix = weight[group].reshape(first_in.shape[1], -1)
        qkv = dot(first_in, matrix)
        at_key = group_size * HD
        key = turned(qkv[:, at_key : at_key + HD], cosine_tab, sine_tab).astype(jnp.bfloat16)
        value = qkv[:, at_key + HD :].astype(jnp.bfloat16)
        key_ref[:, group * HD : (group + 1) * HD] = key
        value_ref[:, group * HD : (group + 1) * HD] = value
        for member in range(group_size):
            head = group * group_size + member
            here = slice(head * HD, (head + 1) * HD)
            query = turned(qkv[:, member * HD : (member + 1) * HD], cosine_tab, sine_tab)
            query = query.astype(jnp.bfloat16)
            query_ref[:, here] = query
            scores = dot(query, key, ((1,), (1,)))
            scores = jnp.where(allowed, scores * HD ** (-0.5), -1e30)
            weights = jnp.exp(scores - jnp.max(scores, axis=-1, keepdims=True))
            prob = weights * (1.0 / jnp.sum(weights, axis=-1, keepdims=True))
            prob = prob.astype(jnp.bfloat16)
            prob_ref[head] = prob
            out_ref[:, here] = dot(prob, value).astype(jnp.bfloat16)
        here = pl.ds(group * group_size, group_size)
        copies.append(
            pltpu.make_async_copy(prob_ref.at[here], prob_out.at[here], sems.at[group])
        )
        copies[-1].start()
    for copy in copies:
        copy.wait()


def project_kernel(at, tokens, gain, attended, *refs):
    resid_ref, second_ref, weight_out, weight, sem = refs[8:]
    place_pieces(at, refs[:8], weight)
    copy = pltpu.make_async_copy(weight, weight_out, sem)
    copy.start()
    heads = attended[...]
    halves = [dot(heads, weight[half].reshape(heads.shape[1], -1)) for half in range(2)]
    resid = tokens[...].astype(jnp.float32) + jnp.concatenate(halves, axis=1)
    resid_ref[...] = resid
    second_ref[...] = rms_kernel(resid, gain[...])
    copy.wait()


def one_hot(slots, capacity, dtype):
    shape = (capacity, slots.shape[1])
    return (slots == lax.broadcasted_iota(jnp.int32, shape, 0)).astype(jnp.float32).astype(dtype)


def slots_of(ids, expert, start, rows):
    named = jnp.any(ids[:, start : start + rows] == expert, axis=0, keepdims=True)
    named = named.astype(jnp.float32)
    before = lax.broadcasted_iota(jnp.int32, (rows, rows), 0)
    upto = lax.broadcasted_iota(jnp.int32, (rows, rows), 1)
    counts = dot(named.astype(jnp.bfloat16), (before <= upto).astype(jnp.float32).astype(jnp.bfloat16))
    return jnp.where(named > 0.0, counts - 1.0, -1.0).astype(jnp.int32)


def spread(picks, capacity, rows, outs):
    rows = rows.astype(jnp.bfloat16)
    block = picks[0].shape[1]
    for n in range(len(picks) // 2):
        for part in range(2):
            pick = picks[2 * n + part]
            at_row = (2 * n + part) * capacity
            tokens = dot(pick, rows[at_row : at_row + capacity], ((0,), (0,)))
            outs[n][part * block : (part + 1) * block] = tokens.astype(jnp.bfloat16)


def expert_kernel(capacity, pieces, at, ids, router, *refs):
    count = len(pieces)
    second, cot = refs[:count], refs[count : 2 * count]
    gate_w, up_w, down_w = refs[2 * count : 2 * count + 3]
    rows_in, rows_cot, gated_ref, gate_back, up_back, gates_ref = refs[2 * count + 3 : 2 * count + 9]
    backs, gate_rows = refs[2 * count + 9 : -1], refs[-1]
    f32, bf16 = jnp.float32, jnp.bfloat16
    length, width = second[0].shape
    wide = router.shape[1]
    half = length // 2
    picks = []
    experts = lax.broadcasted_iota(jnp.int32, (wide, length), 0)
    for n, piece in enumerate(pieces):
        tokens = second[n][...]
        named = ids[:, piece * length : (piece + 1) * length]
        chosen = functools.reduce(
            jnp.logical_or, [named[k : k + 1] == experts for k in range(named.shape[0])]
        )
        logits = jnp.where(chosen, dot(router[...], tokens, ((0,), (1,))), -1e30)
        weights = jnp.exp(logits - jnp.max(logits, axis=0, keepdims=True))
        gates = weights * (1.0 / jnp.sum(weights, axis=0, keepdims=True))
        if n == 0:
            gates_ref[...] = gates
        own = jnp.sum(jnp.where(experts == at[5], gates, 0.0), axis=0, keepdims=True)
        for part in range(2):
            here = slice(part * half, (part + 1) * half)
            place = slice((2 * n + part) * capacity, (2 * n + part + 1) * capacity)
            slots = slots_of(ids, at[5], piece * length + part * half, half)
            pick = one_hot(slots, capacity, f32)
            picks.append(pick.astype(bf16))
            rows_in[place] = dot(picks[-1], tokens[here]).astype(bf16)
            rows_cot[place] = dot(picks[-1], cot[n][here]).astype(bf16)
            gate_rows[place] = jnp.sum(pick * own[:, here], axis=1, keepdims=True)
    gate = gate_rows[...]
    gate_pre = dot(rows_in[...], gate_w[...])
    up_pre = dot(rows_in[...], up_w[...])
    cot_hidden = dot(rows_cot[...], down_w[...], ((1,), (1,)))
    scale = math.sqrt(2.0 / math.pi)
    square = gate_pre * gate_pre
    bent = jnp.tanh(scale * gate_pre * (1.0 + 0.044715 * square))
    open_part = 0.5 * (1.0 + bent)
    active = gate_pre * open_part
    slope = open_part + 0.5 * gate_pre * (1.0 - bent * bent) * scale * (
        1.0 + 3 * 0.044715 * square
    )
    hidden = active * up_pre
    gated_ref[...] = (gate * hidden).astype(bf16)
    signal = jnp.sum(hidden * cot_hidden, axis=1, keepdims=True)
    back = gate * cot_hidden
    gate_back[...] = (back * up_pre * slope).astype(bf16)
    up_back[...] = (back * active).astype(bf16)
    high = signal.astype(bf16)
    low = (signal - high.astype(f32)).astype(bf16)
    lanes = lax.broadcasted_iota(jnp.int32, (signal.shape[0], wide), 1)
    signal = jnp.where(lanes == at[5], high.astype(f32), 0.0)
    signal = jnp.where(lanes == at[5] + wide // 2, low.astype(f32), signal)
    by_rows = ((1,), (1,))
    rows = dot(gate_back[...], gate_w[...], by_rows) + dot(up_back[...], up_w[...], by_rows)
    spread(picks, capacity, jnp.concatenate([rows, signal], axis=1), backs)


def run_expert(pieces, at, ids, router, weights, second, cot, capacity):
    count = len(pieces)
    rows, wide = 2 * count * capacity, router.shape[1]
    (length, width), hidden = second[0].shape, weights[0].shape[1]
    bf16, f32 = jnp.bfloat16, jnp.float32
    outs = [(rows, width)] * 2 + [(rows, hidden)] * 3
    outs = [(shape, bf16) for shape in outs] + [((wide, length), f32)]
    outs = outs + [((length, width + wide), bf16)] * count
    return run_kernel(
        functools.partial(expert_kernel, capacity, pieces),
        4 * count,
        at,
        (ids, router, *second, *cot, *weights),
        outs,
        6 + 4 * count,
        [pltpu.VMEM((rows, 1), f32)],
    )


def mixture_kernel(capacity, groups, at, ids, *refs):
    gated, down_w, outs = refs[: len(groups)], refs[len(groups)], refs[len(groups) + 1 :]
    length = outs[0].shape[0]
    for pieces, rows in zip(groups, gated):
        picks = []
        for piece in pieces:
            for part in range(2):
                start = piece * length + part * length // 2
                slots = slots_of(ids, at[5], start, length // 2)
                picks.append(one_hot(slots, capacity, jnp.bfloat16))
        spread(picks, capacity, dot(rows[...], down_w[...]), [outs[piece] for piece in pieces])


def row_sum_kernel(parts, at, *refs):
    arrays = [
        jnp.concatenate([ref[...] for ref in refs[n : n + parts]], axis=0)
        for n in range(0, len(refs) - len(refs) // (parts + 1), parts)
    ]
    outs = refs[len(arrays) * parts :]
    for out, right in zip(outs, arrays[1:]):
        out[...] = dot(arrays[0], right, ((0,), (0,))).astype(jnp.bfloat16)


def row_sums(at, left, *rights):
    operands = [part for parts in (left, *rights) for part in parts]
    outs = [((left[0].shape[1], right[0].shape[1]), jnp.bfloat16) for right in rights]
    kernel = functools.partial(row_sum_kernel, len(left))
    return run_kernel(kernel, 4 * len(rights), at, operands, outs, 24 if len(rights) == 1 else 56)


def branch_back_kernel(
    at, near, far, first_x, first_y, last_y, last_x, resid, gain, second, gates, router, cot, weight, *outs
):
    resid_grad_ref, branch_ref, attended_ref, router_ref, gain_ref = outs
    f32, bf16 = jnp.float32, jnp.bfloat16
    halves = [first_x[...].astype(f32) + last_y[...], first_y[...].astype(f32) + last_x[...]]
    total = near[...].astype(f32) + far[...] + jnp.concatenate(halves, axis=0)
    width = resid.shape[1]
    signal = total[:, width:]
    signal = signal + pltpu.roll(signal, signal.shape[1] // 2, 1)
    chosen = gates[...].T
    logit_grad = chosen * (signal - jnp.sum(chosen * signal, axis=-1, keepdims=True))
    logit_grad = logit_grad.astype(bf16)
    second_grad = total[:, :width] + dot(logit_grad, router[...], ((1,), (1,)))
    norm_grad, gain_grad = rms_back(resid[...], gain[...], second_grad)
    gain_ref[...] = gain_grad
    resid_grad = cot[...].astype(f32) + norm_grad
    resid_grad_ref[...] = resid_grad
    branch = resid_grad.astype(bf16)
    branch_ref[...] = branch
    wide = weight.shape[2]
    attended_ref[...] = (
        dot(branch[:, :wide], weight[0], ((1,), (1,)))
        + dot(branch[:, wide:], weight[1], ((1,), (1,)))
    ).astype(bf16)
    router_ref[...] = dot(second[...], logit_grad, ((0,), (0,)))


def attend_back_kernel(
    at, attended, probs, queries, keys, values, cosine, sine, branch, back_ref
):
    f32, bf16 = jnp.float32, jnp.bfloat16
    cosine_tab, sine_tab = cosine[...], -sine[...]
    group_size = HQ // HK
    places, length = back_ref.shape[0], branch.shape[0]
    branch_width = branch.shape[1] // places
    width = back_ref.shape[2] - branch_width
    for place in range(places):
        here = slice(place * branch_width, (place + 1) * branch_width)
        back_ref[place, :length, width:] = branch[:, here]
        back_ref[place, length:] = jnp.zeros((back_ref.shape[1] - length, back_ref.shape[2]), bf16)
    scale = HD ** (-0.5)

    def put(position, block):
        back_ref[position // width, :length, position % width : position % width + HD] = block

    for group in range(HK):
        own = slice(group * HD, (group + 1) * HD)
        key, value = keys[:, own], values[:, own]
        key_grad = value_grad = 0.0
        start = group * (group_size + 2) * HD
        for member in range(group_size):
            head = group * group_size + member
            here = slice(head * HD, (head + 1) * HD)
            out_grad, query, prob = attended[:, here], queries[:, here], probs[head]
            prob_grad = dot(out_grad, value, ((1,), (1,)))
            prob_f = prob.astype(f32)
            inner = jnp.sum(prob_f * prob_grad, axis=-1, keepdims=True)
            score_grad = (prob_f * (prob_grad - inner)).astype(bf16)
            query_grad = turned(dot(score_grad, key) * scale, cosine_tab, sine_tab)
            put(start + member * HD, query_grad.astype(bf16))
            key_grad = key_grad + dot(score_grad, query, ((0,), (0,)))
            value_grad = value_grad + dot(prob, out_grad, ((0,), (0,)))
        key_grad = turned(key_grad * scale, cosine_tab, sine_tab)
        put(start + group_size * HD, key_grad.astype(bf16))
        put(start + (group_size + 1) * HD, value_grad.astype(bf16))


def first_back_kernel(at, back, weight, tokens, gain, resid_grad, tokens_ref, gain_ref):
    f32 = jnp.float32
    parts = back.shape[0]
    cols = weight.shape[0] * weight.shape[2] // parts
    first_grad = 0.0
    for part in range(parts):
        group, place = divmod(part * cols, weight.shape[2])
        first_grad = first_grad + dot(
            back[part, : tokens.shape[0], :cols], weight[group, :, place : place + cols], ((1,), (1,))
        )
    norm_grad, gain_grad = rms_back(tokens[...].astype(f32), gain[...], first_grad)
    gain_ref[...] = gain_grad
    tokens_ref[...] = (resid_grad[...] + norm_grad).astype(jnp.bfloat16)


def dense_grad_kernel(at, narrow, back, *refs):
    pieces, out_ref, held, sems = refs[:8], refs[8], refs[9], refs[10]
    copies = [
        pltpu.make_async_copy(piece, held.at[n], sems.at[n]) for n, piece in enumerate(pieces)
    ]
    for copy in copies:
        copy.start()
    depth, rows, cols = out_ref.shape
    length = held.shape[1] // 2
    qkv_width = cols - held.shape[2] // back.shape[0]
    narrow = sum(narrow[place].astype(jnp.float32) for place in range(narrow.shape[0]))
    sums = [0.0, 0.0]
    for n, copy in enumerate(copies):
        copy.wait()
        dc, dy, dx = n // 4, n // 2 % 2, n % 2
        place = 4 * (at[0] ^ dy) + 2 * (at[1] ^ dc) + (at[2] ^ dx)
        own = back[place, :length]
        sums[0] = sums[0] + dot(held[n, length:], own[:, :qkv_width], ((0,), (0,)))
        sums[1] = sums[1] + dot(held[n, :length], own[:, qkv_width:], ((0,), (0,)))
    wide = held.shape[2] // depth
    each = narrow.shape[0] // depth
    for z in range(depth):
        here = slice(z * wide, (z + 1) * wide)
        both = jnp.concatenate([part[here] for part in sums], axis=1)
        out_ref[z, :wide] = both.astype(jnp.bfloat16)
        kept = [narrow[z * each : (z + 1) * each], jnp.zeros((rows - wide - each, cols), jnp.float32)]
        out_ref[z, wide:] = jnp.concatenate(kept, axis=0).astype(jnp.bfloat16)


def finish_kernel(at, sums, query_ref, key_ref, value_ref, output_ref):
    places, _, cols = sums.shape
    rows, out_width = query_ref.shape[0], output_ref.shape[1] // places
    width = cols - out_width
    for place in range(places):
        block = sums[place, :rows].astype(jnp.float32)
        output_ref[:, place * out_width : (place + 1) * out_width] = block[:, width:]
        for at_col in range(0, width, HD):
            group, head = divmod((place * width + at_col) // HD, HQ // HK + 2)
            part = block[:, at_col : at_col + HD]
            if head < HQ // HK:
                start = (group * (HQ // HK) + head) * HD
                query_ref[:, start : start + HD] = part
            elif head == HQ // HK:
                key_ref[:, group * HD : (group + 1) * HD] = part
            else:
                value_ref[:, group * HD : (group + 1) * HD] = part


def local_pairs(
    tokens,
    norm1_gain,
    w_query,
    w_key,
    w_value,
    w_out,
    norm2_gain,
    w_router,
    w_gate,
    w_up,
    w_down,
    expert_ids,
    prefix_len,
    out_grad,
):
    bf16, f32 = jnp.bfloat16, jnp.float32
    length, model_width = tokens.shape
    shard_rows = w_query.shape[0]
    local_count, _, hidden_width = w_gate.shape
    owners = lax.axis_size("x")
    depth = lax.axis_size("z")
    plane = lax.axis_size(PLANE)
    experts_all = w_router.shape[1]
    block_rows = length // MICRO
    capacity = 3 * block_rows * expert_ids.shape[1] // (2 * experts_all)
    plane_rows = plane * length
    blocks = plane_rows // block_rows
    q_cols, kv_cols = w_query.shape[1], w_key.shape[1]
    qkv_cols = q_cols + 2 * kv_cols
    q_group, out_half = q_cols // HK, model_width // 2
    y, c, x, z = (lax.axis_index(axis) for axis in ("y", "c", "x", "z"))
    own_local = 2 * y + c
    own_expert = x * local_count + own_local
    at = jnp.stack([y, c, x, z, prefix_len[0], own_expert, own_local])

    own_half = jnp.concatenate(
        [
            lax.dynamic_slice_in_dim(part, x * (part.shape[1] // 2), part.shape[1] // 2, 1)
            for part in (w_query, w_key, w_value, w_out)
        ],
        axis=1,
    )
    narrow = jnp.concatenate([w_router, norm1_gain[:, None], norm2_gain[:, None]], axis=1)
    narrow = jnp.pad(narrow, ((0, 0), (0, 128 - narrow.shape[1])))
    router_w = small_group_gather(narrow)
    ids_all = small_gather(expert_ids.T)
    column = [own_half] + shifts(own_half)
    cot_sides = plane_sides(after(out_grad, router_w, ids_all))
    qkv_half = qkv_cols // 2
    qkv_column = jnp.stack([part[:, :qkv_half] for part in column])
    out_column = jnp.stack([part[:, qkv_half:] for part in column])
    qkv_column, out_column = lax.optimization_barrier((qkv_column, out_column, *cot_sides))[:2]
    sliced = after(own_local, column[-1])
    gate_w, up_w, down_w = (
        lax.dynamic_index_in_dim(weight, sliced, 0, keepdims=False)
        for weight in (w_gate, w_up, w_down)
    )
    qkv_sides = plane_sides(qkv_column)
    gains = router_w[:, experts_all : experts_all + 2].T.astype(f32)
    gain_one, gain_two = gains[:1], gains[1:]
    qkv_corner = plane_corner(qkv_sides, (gate_w, up_w, down_w, gain_one, gain_two))
    out_sides = plane_sides(after(out_column, *qkv_sides))
    qkv_pieces = plane_pieces(qkv_column, qkv_sides, qkv_corner)
    cosine_tab, sine_tab = angles(length, HD)
    cosine_all = jnp.concatenate([cosine_tab, cosine_tab], axis=2)[:, 0]
    sine_all = jnp.concatenate([-sine_tab, sine_tab], axis=2)[:, 0]
    weight_lead = (2, depth, 2, 2, shard_rows)
    first_in, queries, keys_rot, values_b, attended, probs, qkv_w = run_kernel(
        attend_kernel,
        11,
        at,
        (tokens, gain_one, cosine_all, sine_all, *qkv_pieces),
        [
            ((length, model_width), bf16),
            ((length, q_cols), bf16),
            ((length, kv_cols), bf16),
            ((length, kv_cols), bf16),
            ((length, q_cols), bf16),
            ((HQ, length, length), bf16),
            (weight_lead + (qkv_half,), bf16),
        ],
        28,
        [
            pltpu.VMEM((HQ, length, length), bf16),
            pltpu.VMEM(weight_lead + (qkv_half,), bf16),
            pltpu.SemaphoreType.DMA((HK + 1,)),
        ],
        hbm_out=2,
    )
    out_sides = lax.optimization_barrier((*out_sides, attended))[:2]
    out_corner = plane_corner(out_sides)
    cot_corner = plane_corner(cot_sides)
    out_pieces = plane_pieces(out_column, out_sides, out_corner)
    cot_pieces = plane_pieces(out_grad, cot_sides, cot_corner)
    resid, second_in, output_w = run_kernel(
        project_kernel,
        4,
        at,
        (tokens, after(gain_two, cot_corner), attended, *out_pieces),
        [
            ((length, model_width), f32),
            ((length, model_width), bf16),
            (weight_lead + (out_half,), bf16),
        ],
        44,
        [pltpu.VMEM(weight_lead + (out_half,), bf16), pltpu.SemaphoreType.DMA],
        hbm_out=1,
    )
    qkv_w = qkv_w.reshape(HK, model_width, qkv_half)
    output_w = output_w.reshape(2, q_cols, out_half)

    expert = functools.partial(
        run_expert,
        at=at,
        ids=ids_all,
        router=router_w,
        weights=(gate_w, up_w, down_w),
        capacity=capacity,
    )
    second_sides = plane_sides(second_in)
    groups = ((0, 4), (1, 5, 2, 6), (3, 7))
    second_pieces = {0: second_in, 4: swap(second_in, "c")}

    def run_group(pieces):
        return expert(
            pieces,
            second=[second_pieces[piece] for piece in pieces],
            cot=[cot_pieces[piece] for piece in pieces],
        )

    stage_own = run_group(groups[0])
    second_sides = lax.optimization_barrier((*second_sides, stage_own[0]))[:2]
    for piece, block in zip((1, 2), second_sides):
        second_pieces[piece], second_pieces[piece + 4] = block, swap(block, "c")
    stage_sides = run_group(groups[1])
    second_corner = plane_corner(second_sides, later=(stage_sides[0],))
    second_pieces[3], second_pieces[7] = second_corner, swap(second_corner, "c")
    own_near, own_far = stage_own[6:]
    own_far = swap(own_far, "c")
    x_near, x_far, y_near, y_far = stage_sides[6:]
    back_x, back_y = over_core(x_near, x_far), over_core(y_near, y_far)
    first_x, first_y = early_sums(back_x, back_y)
    stage_corner = run_group(groups[2])
    corner = over_core(*stage_corner[6:])
    passed = corner_first(corner)
    stages = (stage_own, stage_sides, stage_corner)
    rows_in, rows_cot, gated, gate_back, up_back = ([stage[n] for stage in stages] for n in range(5))
    gates = stage_own[5]
    (down_part,) = row_sums(at, [after(rows_cot[0], corner)] + rows_cot[1:], gated)
    down_sum = scatter_sum(down_part, "z")
    passed = lax.optimization_barrier((*passed, down_part))[:2]
    last_y, last_x, *sent = corner_last(back_x, back_y, passed)
    gate_part, up_part = row_sums(
        at, [after(rows_in[0], *sent, first_x, first_y, own_far)] + rows_in[1:], gate_back, up_back
    )
    gate_sum, up_sum = scatter_sum(gate_part, "z"), scatter_sum(up_part, "z")
    own_near = after(own_near, gate_part)

    resid_grad, branch_grad, attended_grad, router_acc, gain_two_grad = run_kernel(
        branch_back_kernel,
        6,
        at,
        (
            own_near,
            own_far,
            first_x,
            first_y,
            last_y,
            last_x,
            resid,
            gain_two,
            second_in,
            gates,
            router_w,
            out_grad,
            output_w,
        ),
        [
            ((length, model_width), f32),
            ((length, model_width), bf16),
            ((length, q_cols), bf16),
            ((model_width, 128), f32),
            ((1, model_width), f32),
        ],
        56,
    )
    qkv_width, branch_width = qkv_cols // plane, model_width // plane
    dense_cols = qkv_width + branch_width
    (back_cols,) = run_kernel(
        attend_back_kernel,
        6,
        at,
        (
            attended_grad,
            probs,
            queries,
            keys_rot,
            values_b,
            cosine_all,
            sine_all,
            branch_grad,
        ),
        [((plane, length + 16, dense_cols), bf16)],
        56,
    )
    tokens_grad, gain_one_grad = run_kernel(
        first_back_kernel,
        5,
        at,
        (back_cols, qkv_w, tokens, gain_one, resid_grad),
        [((length, model_width), bf16), ((1, model_width), f32)],
        24,
    )

    both = jnp.concatenate(
        lax.optimization_barrier((attended, first_in, last_y, last_x))[:2], axis=0
    )
    both_sides = plane_sides(both)
    narrow_part = jnp.concatenate(
        [router_acc[:, :experts_all], gain_one_grad.T, gain_two_grad.T], axis=1
    )
    narrow_cols = -(-narrow_part.shape[1] // owners) * owners
    narrow_part = jnp.pad(narrow_part, ((0, 0), (0, narrow_cols - narrow_part.shape[1])))
    narrow_part = jnp.transpose(
        narrow_part.reshape(depth, 2, 2, shard_rows, owners, narrow_cols // owners),
        (1, 2, 4, 0, 3, 5),
    ).reshape(plane, depth, shard_rows * narrow_cols // owners)
    narrow_len = narrow_part.shape[2]
    narrow_rows = -(-narrow_len // dense_cols)
    each_rows = -(-narrow_rows // 4) * 4
    narrow_part = jnp.pad(
        narrow_part, ((0, 0), (0, 0), (0, each_rows * dense_cols - narrow_len))
    ).reshape(plane, depth * each_rows, dense_cols)
    back_cols = exchange(after(back_cols, down_sum, *both_sides), PLANE)
    narrow_part = exchange(narrow_part.astype(bf16), PLANE)
    both_corner = plane_corner(both_sides, (back_cols, gain_one_grad))
    both_pieces = plane_pieces(both, both_sides, both_corner)
    def placed(total):
        total = exchange(total, ("y", "c"))
        return total.reshape(local_count, shard_rows, hidden_width).astype(f32)

    down_grad = placed(down_sum)
    kept_rows = -(-narrow_rows // 16) * 16
    wide_rows = local_count * shard_rows
    dense_shape = (depth, wide_rows + kept_rows, dense_cols)
    dense_part = pl.pallas_call(
        dense_grad_kernel,
        out_shape=jax.ShapeDtypeStruct(dense_shape, bf16),
        in_specs=[SCALARS, WHOLE, WHOLE] + [IN_HBM] * 8,
        out_specs=WHOLE,
        scratch_shapes=[
            pltpu.VMEM((plane, 2 * length, model_width), bf16),
            pltpu.SemaphoreType.DMA((plane,)),
        ],
        cost_estimate=cost(8),
        compiler_params=pltpu.CompilerParams(vmem_limit_bytes=32 * 2**20),
    )(at, narrow_part, after(back_cols, up_sum, down_grad), *both_pieces)
    dense_sum = scatter_sum(dense_part.reshape(-1, dense_cols), "z")
    wide_sum = dense_sum[: local_count * shard_rows].reshape(2, 2, 1, shard_rows, dense_cols)
    wide_sum = jnp.broadcast_to(wide_sum, (2, 2, owners, shard_rows, dense_cols)).reshape(
        plane, shard_rows, dense_cols
    )
    narrow_sum = dense_sum[local_count * shard_rows :][:narrow_rows]
    narrow_sum = jnp.broadcast_to(narrow_sum[None], (plane, narrow_rows, dense_cols))
    pad_rows = -(shard_rows + narrow_rows) % 16
    padding = jnp.zeros((plane, pad_rows, dense_cols), bf16)
    dense_sum = exchange(jnp.concatenate([wide_sum, narrow_sum, padding], axis=1), PLANE)
    query_grad, key_grad, value_grad, output_grad = run_kernel(
        finish_kernel,
        2,
        at,
        (dense_sum,),
        [
            ((shard_rows, q_cols), f32),
            ((shard_rows, kv_cols), f32),
            ((shard_rows, kv_cols), f32),
            ((shard_rows, model_width), f32),
        ],
    )
    narrow_sum = dense_sum[:, shard_rows : shard_rows + narrow_rows].reshape(
        2, 2, owners, narrow_rows * dense_cols
    )
    narrow_sum = narrow_sum[y, c, :, :narrow_len].reshape(owners, shard_rows, -1)
    narrow_sum = jnp.moveaxis(narrow_sum, 0, 1).reshape(shard_rows, narrow_cols).astype(f32)

    shares = run_kernel(
        functools.partial(mixture_kernel, capacity, groups),
        10,
        at,
        (ids_all, after(gated[0], both_corner), *gated[1:], down_w),
        [((length, model_width), bf16)] * plane,
        56,
    )
    mixed = [over_core(near, far) for near, far in zip(shares[:4], shares[4:])]
    early = early_sums(mixed[1], mixed[2])
    last = corner_last(mixed[1], mixed[2], corner_first(mixed[3]))[:2]
    mixture = jnp.concatenate(
        [left.astype(f32) + right.astype(f32) for left, right in zip(early, last)], axis=0
    )
    block_out = (resid + (mixture + mixed[0].astype(f32))).astype(bf16)

    return (
        block_out,
        tokens_grad,
        narrow_sum[:, experts_all],
        query_grad,
        key_grad,
        value_grad,
        output_grad,
        narrow_sum[:, experts_all + 1],
        narrow_sum[:, :experts_all],
        placed(after(gate_sum, dense_part)),
        placed(after(up_sum, dense_part)),
        jnp.swapaxes(down_grad, 1, 2),
    )


def solution(mesh):
    groups, owners = mesh.shape["dp"], mesh.shape["expert"]
    grid = jax.sharding.Mesh(
        mesh.devices.reshape(groups // 4, 2, 2, owners), ("z", "y", "c", "x")
    )
    rows = P(("z", "y", "c", "x"), None)
    shard, shard_rows = P(GROUP), P(GROUP, None)
    expert = P("x", None, None)
    return jax.shard_map(
        local_pairs if owners == 2 else local_wide,
        mesh=grid,
        in_specs=(
            rows,
            shard,
            shard_rows,
            shard_rows,
            shard_rows,
            shard_rows,
            shard,
            shard_rows,
            expert,
            expert,
            expert,
            rows,
            P(("z", "y", "c", "x")),
            rows,
        ),
        out_specs=(
            rows,
            rows,
            shard,
            shard_rows,
            shard_rows,
            shard_rows,
            shard_rows,
            shard,
            shard_rows,
            P("x", GROUP, None),
            P("x", GROUP, None),
            P("x", None, GROUP),
        ),
        check_vma=False,
    )
```

```python
import functools
import math

import jax
import jax.numpy as jnp
from jax import lax
from jax.experimental import pallas as pl
from jax.experimental.pallas import tpu as pltpu
from jax.sharding import PartitionSpec as P

HQ = 12
HK = 2
HD = 128
MICRO = 2
PLANE = ("y", "c", "x")
GROUP = ("z", "y", "c")


def rms_scale(values, gain_vec):
    inverse = lax.rsqrt(jnp.mean(values * values, axis=-1, keepdims=True) + 1e-06)
    return values * inverse * gain_vec


def angles(length, head_size):
    positions = jnp.arange(length).astype(jnp.float32)
    freq_rates = jnp.exp(
        -(2.0 * jnp.arange(head_size // 2).astype(jnp.float32) / head_size) * math.log(1000000.0)
    )
    angle_tab = positions[:, None] * freq_rates[None, :]
    return (jnp.cos(angle_tab)[:, None, :], jnp.sin(angle_tab)[:, None, :])


def rotary(values, cosine_tab, sine_tab):
    half_dim = values.shape[-1] // 2
    first_half = values[..., :half_dim]
    second_half = values[..., half_dim:]
    return jnp.concatenate(
        [
            first_half * cosine_tab - second_half * sine_tab,
            second_half * cosine_tab + first_half * sine_tab,
        ],
        axis=-1,
    )


def expert_act(gate_pre, up_pre):
    return jax.nn.gelu(gate_pre, approximate=True) * up_pre


def left_product(left_mat, right_mat):
    return lax.dot_general(
        left_mat, right_mat, (((0,), (0,)), ((), ())), preferred_element_type=jnp.float32
    )


def gather(block, axes):
    return lax.all_gather(block, axes, axis=0, tiled=True)


def exchange(block, axes):
    return lax.all_to_all(block, axes, split_axis=0, concat_axis=0, tiled=True)


def scatter_sum(block, axes):
    return lax.psum_scatter(block, axes, scatter_dimension=0, tiled=True)


def by_owner(cols, parts):
    rows, total = cols.shape
    return jnp.moveaxis(cols.reshape(rows, parts, total // parts), 1, 0).reshape(
        parts * rows, total // parts
    )


def local_wide(
    tokens,
    norm1_gain,
    w_query,
    w_key,
    w_value,
    w_out,
    norm2_gain,
    w_router,
    w_gate,
    w_up,
    w_down,
    expert_ids,
    prefix_len,
    out_grad,
):
    bf16, f32 = jnp.bfloat16, jnp.float32
    length, model_width = tokens.shape
    shard_rows = w_query.shape[0]
    local_count, _, hidden_width = w_gate.shape
    owners = lax.axis_size("x")
    depth = lax.axis_size("z")
    plane = lax.axis_size(PLANE)
    experts_all = w_router.shape[1]
    top_count = expert_ids.shape[1]
    block_rows = length // MICRO
    capacity = 3 * block_rows * top_count // (2 * experts_all)
    plane_rows = plane * length
    blocks = plane_rows // block_rows
    group_size = HQ // HK
    score_scale = HD ** (-0.5)
    q_cols, kv_cols = w_query.shape[1], w_key.shape[1]
    own_local = lax.axis_index(("y", "c"))
    own_expert = lax.axis_index("x") * local_count + own_local
    own_place = lax.axis_index(PLANE)

    narrow = jnp.concatenate([w_router, norm1_gain[:, None], norm2_gain[:, None]], axis=1)
    narrow = jnp.pad(narrow, ((0, 0), (0, -narrow.shape[1] % 128)))
    packed = gather(jnp.concatenate([w_query, w_key, w_value, narrow], axis=1), GROUP)
    qkv_cols = q_cols + 2 * kv_cols
    qkv_w = packed[:, :qkv_cols]
    router_w = packed[:, qkv_cols : qkv_cols + experts_all]
    gains = packed[:, qkv_cols + experts_all : qkv_cols + experts_all + 2].T.astype(f32)
    gain_one, gain_two = gains[0], gains[1]
    output_w = gather(w_out, GROUP)

    ids_all = gather(expert_ids, PLANE)
    cot_all = gather(out_grad, PLANE)
    chosen_mask = jnp.any(
        ids_all[:, :, None] == jnp.arange(experts_all, dtype=jnp.int32)[None, None, :], axis=1
    )
    own_mask = jnp.any(ids_all == own_expert, axis=1).reshape(blocks, block_rows)
    place = jnp.cumsum(own_mask.astype(jnp.int32), axis=1) - 1
    dispatch = (
        own_mask[:, None, :]
        & (place[:, None, :] == jnp.arange(capacity, dtype=jnp.int32)[None, :, None])
    ).astype(bf16)

    cosine_tab, sine_tab = angles(length, HD)
    inputs_f = tokens.astype(f32)
    first_in = rms_scale(inputs_f, gain_one).astype(bf16)
    qkv = jnp.dot(first_in, qkv_w, preferred_element_type=f32)
    queries = (
        rotary(qkv[:, :q_cols].reshape(length, HQ, HD), cosine_tab, sine_tab)
        .astype(bf16)
        .reshape(length, HK, group_size, HD)
    )
    keys_rot = rotary(
        qkv[:, q_cols : q_cols + kv_cols].reshape(length, HK, HD), cosine_tab, sine_tab
    ).astype(bf16)
    values_b = qkv[:, q_cols + kv_cols :].astype(bf16).reshape(length, HK, HD)
    positions = jnp.arange(length)
    allowed = (positions[None, :] <= positions[:, None]) | (positions[None, :] < prefix_len[0])

    def masked_scores():
        scores = jnp.einsum("ihrd,jhd->hrij", queries, keys_rot, preferred_element_type=f32)
        return jnp.where(allowed, scores * score_scale, -1e30)

    masked = masked_scores()
    row_peak = jnp.max(masked, axis=-1, keepdims=True)
    log_total = row_peak + jnp.log(jnp.sum(jnp.exp(masked - row_peak), axis=-1, keepdims=True))
    prob_bf = jnp.exp(masked - log_total).astype(bf16)
    attended = jnp.einsum("hrij,jhd->ihrd", prob_bf, values_b, preferred_element_type=f32)
    attended = attended.reshape(length, HQ * HD).astype(bf16)
    resid = inputs_f + jnp.dot(attended, output_w, preferred_element_type=f32)
    second_in = rms_scale(resid, gain_two).astype(bf16)

    second_all = gather(second_in, PLANE)
    logits = jnp.dot(second_all, router_w, preferred_element_type=f32)
    gates_all = jax.nn.softmax(jnp.where(chosen_mask, logits, -jnp.inf), axis=-1)
    own_gates = lax.dynamic_index_in_dim(gates_all, own_expert, 1, keepdims=False)
    own_gates = own_gates.reshape(blocks, block_rows)
    gate_rows = jnp.einsum(
        "bct,bt->bc", dispatch.astype(f32), own_gates, precision=lax.Precision.HIGHEST
    )[:, :, None]
    gate_w = lax.dynamic_index_in_dim(w_gate, own_local, 0, keepdims=False)
    up_w = lax.dynamic_index_in_dim(w_up, own_local, 0, keepdims=False)
    down_w = lax.dynamic_index_in_dim(w_down, own_local, 0, keepdims=False)

    def to_rows(array):
        return jnp.einsum(
            "bct,btd->bcd",
            dispatch,
            array.reshape(blocks, block_rows, model_width),
            preferred_element_type=f32,
        ).astype(bf16)

    def to_tokens(rows):
        return (
            jnp.einsum("bct,bcd->btd", dispatch, rows.astype(bf16), preferred_element_type=f32)
            .astype(bf16)
            .reshape(plane_rows, model_width)
        )

    rows_in = to_rows(second_all)
    rows_cot = to_rows(cot_all)
    gate_pre = jnp.einsum("bcd,df->bcf", rows_in, gate_w, preferred_element_type=f32)
    up_pre = jnp.einsum("bcd,df->bcf", rows_in, up_w, preferred_element_type=f32)
    hidden, act_pull = jax.vjp(expert_act, gate_pre, up_pre)
    gated = (gate_rows * hidden).astype(bf16)
    down_part = jnp.einsum("bcd,bcf->df", rows_cot, gated, preferred_element_type=f32)
    down_sum = scatter_sum(down_part.astype(bf16), "z")
    cot_hidden = jnp.einsum("bcd,fd->bcf", rows_cot, down_w, preferred_element_type=f32)
    gate_signal_rows = jnp.sum(hidden * cot_hidden, axis=-1)
    gate_pgrad, up_pgrad = act_pull(gate_rows * cot_hidden)
    gate_pgrad = gate_pgrad.astype(bf16)
    up_pgrad = up_pgrad.astype(bf16)
    gate_part = jnp.einsum("bcd,bcf->df", rows_in, gate_pgrad, preferred_element_type=f32)
    gate_sum = scatter_sum(gate_part.astype(bf16), "z")
    up_part = jnp.einsum("bcd,bcf->df", rows_in, up_pgrad, preferred_element_type=f32)
    up_sum = scatter_sum(up_part.astype(bf16), "z")
    rows_grad = jnp.einsum("bcf,df->bcd", gate_pgrad, gate_w, preferred_element_type=f32)
    rows_grad = rows_grad + jnp.einsum("bcf,df->bcd", up_pgrad, up_w, preferred_element_type=f32)
    second_back = scatter_sum(to_tokens(rows_grad), PLANE).astype(f32)
    gate_signal = jnp.einsum(
        "bct,bc->bt", dispatch.astype(f32), gate_signal_rows, precision=lax.Precision.HIGHEST
    )
    gate_signal = exchange(gate_signal.reshape(plane, length), PLANE)
    gate_signal = jnp.transpose(
        gate_signal.reshape(local_count, owners, length), (2, 1, 0)
    ).reshape(length, experts_all)
    expert_rows = jnp.einsum("bcf,fd->bcd", gated, down_w, preferred_element_type=f32)
    mixture = scatter_sum(to_tokens(expert_rows), PLANE).astype(f32)
    block_out = (resid + mixture).astype(bf16)

    cotangent = out_grad.astype(f32)
    gate_probs = lax.dynamic_slice_in_dim(gates_all, own_place * length, length, 0)
    logit_grad = (
        gate_probs
        * (gate_signal - jnp.sum(gate_probs * gate_signal, axis=-1, keepdims=True))
    ).astype(bf16)
    router_acc = left_product(second_in, logit_grad)
    second_grad = second_back + jnp.dot(logit_grad, router_w.T, preferred_element_type=f32)
    _, norm_two_pull = jax.vjp(rms_scale, resid, gain_two)
    resid_norm_grad, gain_two_grad = norm_two_pull(second_grad)
    resid_grad = cotangent + resid_norm_grad
    branch_grad = resid_grad.astype(bf16)

    attended_all = gather(attended, PLANE)
    branch_cols = exchange(by_owner(branch_grad, plane), PLANE)
    output_part = left_product(attended_all, branch_cols)
    attended_grad = jnp.dot(branch_grad, output_w.T, preferred_element_type=f32).astype(bf16)
    attended_grad = attended_grad.reshape(length, HK, group_size, HD)
    masked = masked_scores()
    prob_full = jnp.exp(masked - log_total)
    prob_bf = prob_full.astype(bf16)
    prob_grad = jnp.einsum("ihrd,jhd->hrij", attended_grad, values_b, preferred_element_type=f32)
    row_inner = jnp.sum(prob_full * prob_grad, axis=-1, keepdims=True)
    score_grad = (prob_full * (prob_grad - row_inner)).astype(bf16)
    query_rot_grad = (
        jnp.einsum("hrij,jhd->ihrd", score_grad, keys_rot, preferred_element_type=f32)
        * score_scale
    )
    query_back = rotary(query_rot_grad.reshape(length, HQ, HD), cosine_tab, -sine_tab)
    query_back = query_back.astype(bf16).reshape(length, HQ * HD)
    key_rot_grad = (
        jnp.einsum("hrij,ihrd->jhd", score_grad, queries, preferred_element_type=f32)
        * score_scale
    )
    key_back = rotary(key_rot_grad, cosine_tab, -sine_tab).astype(bf16).reshape(length, HK * HD)
    value_back = jnp.einsum("hrij,ihrd->jhd", prob_bf, attended_grad, preferred_element_type=f32)
    value_back = value_back.astype(bf16).reshape(length, HK * HD)
    qkv_back = jnp.concatenate([query_back, key_back, value_back], axis=1)
    first_all = gather(first_in, PLANE)
    qkv_part = left_product(first_all, exchange(by_owner(qkv_back, plane), PLANE))
    first_grad = lax.dot_general(
        qkv_back, qkv_w, (((1,), (1,)), ((), ())), preferred_element_type=f32
    )
    _, norm_one_pull = jax.vjp(rms_scale, inputs_f, gain_one)
    input_norm_grad, gain_one_grad = norm_one_pull(first_grad)
    tokens_grad = (resid_grad + input_norm_grad).astype(bf16)

    narrow_part = jnp.concatenate(
        [router_acc, gain_one_grad[:, None], gain_two_grad[:, None]], axis=1
    ).astype(bf16)
    narrow_cols = narrow_part.shape[1]
    narrow_sum = lax.psum(scatter_sum(narrow_part, GROUP), "x").astype(f32)
    dense_part = jnp.concatenate([qkv_part, output_part], axis=1).astype(bf16)
    dense_sum = scatter_sum(dense_part, "z")
    dense_cols = dense_sum.shape[1]
    dense_sum = gather(dense_sum, PLANE).reshape(plane, local_count, shard_rows, dense_cols)
    dense_sum = lax.dynamic_index_in_dim(dense_sum, own_local, 1, keepdims=False).astype(f32)
    dense_sum = jnp.moveaxis(dense_sum, 0, 1)
    qkv_width = qkv_cols // plane
    qkv_sum = dense_sum[:, :, :qkv_width].reshape(shard_rows, qkv_cols)
    output_sum = dense_sum[:, :, qkv_width:].reshape(shard_rows, model_width)

    def placed(total):
        total = exchange(total, ("y", "c"))
        return total.reshape(local_count, shard_rows, hidden_width).astype(f32)

    return (
        block_out,
        tokens_grad,
        narrow_sum[:, experts_all],
        qkv_sum[:, :q_cols],
        qkv_sum[:, q_cols : q_cols + kv_cols],
        qkv_sum[:, q_cols + kv_cols :],
        output_sum,
        narrow_sum[:, experts_all + 1],
        narrow_sum[:, :experts_all],
        placed(gate_sum),
        placed(up_sum),
        jnp.swapaxes(placed(down_sum), 1, 2),
    )


def rounded(values):
    return lax.reduce_precision(values, 8, 7).astype(jnp.bfloat16)


def after(block, *others):
    return lax.optimization_barrier((block,) + others)[0]


def swap(block, axis):
    return lax.ppermute(block, axis, [(0, 1), (1, 0)])


def shifts(block):
    depth = lax.axis_size("z")
    return [
        lax.ppermute(block, "z", [(i, (i + k) % depth) for i in range(depth)])
        for k in range(1, depth)
    ]


def plane_sides(block):
    return swap(block, "x"), swap(block, "y")


def plane_corner(sides, before=(), later=()):
    over_x, over_y = sides
    half = over_x.shape[0] // 2
    over_y, over_x = lax.optimization_barrier((over_y[:half], over_x[half:]) + before)[:2]
    parts = (swap(over_y, "x"), swap(over_x, "y"))
    return jnp.concatenate(lax.optimization_barrier(parts + later)[:2], axis=0)


def plane_pieces(block, sides=None, corner=None):
    sides = plane_sides(block) if sides is None else sides
    corner = plane_corner(sides) if corner is None else corner
    pieces = [block, *sides, corner]
    return pieces + [swap(piece, "c") for piece in pieces]


def small_gather(block):
    for axis in ("x", "y", "c"):
        block = jnp.concatenate([block, swap(block, axis)], axis=1)
    return block


def small_group_gather(block):
    depth = lax.axis_size("z")
    order = jnp.stack(([block] + shifts(block))[::-1] * 2)
    start = (depth - 1 - lax.axis_index("z")) % depth
    total = lax.dynamic_slice_in_dim(order, start, depth, 0)[:, None, None]
    for dim, axis in ((1, "y"), (2, "c")):
        other = swap(total, axis)
        last = lax.axis_index(axis) == 1
        pair = [jnp.where(last, other, total), jnp.where(last, total, other)]
        total = jnp.concatenate(pair, axis=dim)
    return total.reshape(-1, block.shape[1])


def add(left, right):
    return rounded(left.astype(jnp.float32) + right.astype(jnp.float32))


def over_core(near, far):
    return add(near, swap(far, "c"))


def early_sums(over_x, over_y):
    half = over_x.shape[0] // 2
    return swap(over_x[:half], "x"), swap(over_y[half:], "y")


def corner_first(corner):
    half = corner.shape[0] // 2
    return swap(corner[:half], "x"), swap(corner[half:], "y")


def corner_last(over_x, over_y, first):
    half = over_x.shape[0] // 2
    over_y, over_x = add(over_y[:half], first[0]), add(over_x[half:], first[1])
    return swap(over_y, "y"), swap(over_x, "x"), over_y, over_x


def cost(micros):
    return pl.CostEstimate(flops=micros * 10**9, bytes_accessed=micros * 10**6, transcendentals=0)


def dot(left, right, dims=((1,), (0,)), precision=None):
    return lax.dot_general(
        left, right, (dims, ((), ())), precision=precision, preferred_element_type=jnp.float32
    )


WHOLE = pl.BlockSpec(memory_space=pltpu.VMEM)
IN_HBM = pl.BlockSpec(memory_space=pltpu.HBM)
SCALARS = pl.BlockSpec(memory_space=pltpu.SMEM)


def run_kernel(kernel, micros, at, operands, outs, megabytes=16, scratch=(), hbm_in=0, hbm_out=0):
    return pl.pallas_call(
        kernel,
        out_shape=[jax.ShapeDtypeStruct(shape, dtype) for shape, dtype in outs],
        in_specs=[SCALARS] + [WHOLE] * (len(operands) - hbm_in) + [IN_HBM] * hbm_in,
        out_specs=[WHOLE] * (len(outs) - hbm_out) + [IN_HBM] * hbm_out,
        scratch_shapes=scratch,
        cost_estimate=cost(micros),
        compiler_params=pltpu.CompilerParams(vmem_limit_bytes=megabytes * 2**20),
    )(at, *operands)


def place_pieces(at, refs, weight):
    depth = weight.shape[1]
    for n, ref in enumerate(refs):
        dc, dy, dx = n // 4, n // 2 % 2, n % 2
        for k in range(depth):
            z = lax.rem(at[3] + depth - k, depth)
            weight[at[2] ^ dx, z, at[0] ^ dy, at[1] ^ dc] = ref[k]


def rms_kernel(values, gain):
    inverse = lax.rsqrt(jnp.mean(values * values, axis=-1, keepdims=True) + 1e-06)
    return (values * inverse * gain).astype(jnp.bfloat16)


def rms_back(values, gain, grad):
    inverse = lax.rsqrt(jnp.mean(values * values, axis=-1, keepdims=True) + 1e-06)
    normed = values * inverse
    gain_grad = jnp.sum(grad * normed, axis=0, keepdims=True)
    grad = grad * gain
    along = jnp.mean(grad * normed, axis=-1, keepdims=True)
    return inverse * (grad - normed * along), gain_grad


def turned(values, cosine_tab, sine_tab):
    return values * cosine_tab + pltpu.roll(values, HD // 2, 1) * sine_tab


def attend_kernel(at, tokens, gain, cosine, sine, *refs):
    first_ref, query_ref, key_ref, value_ref, out_ref = refs[8:13]
    prob_out, weight_out, prob_ref, weight, sems = refs[13:]
    place_pieces(at, refs[:8], weight)
    copies = [pltpu.make_async_copy(weight, weight_out, sems.at[HK])]
    copies[0].start()
    length = tokens.shape[0]
    first_in = rms_kernel(tokens[...].astype(jnp.float32), gain[...])
    first_ref[...] = first_in
    rows = lax.broadcasted_iota(jnp.int32, (length, length), 0)
    cols = lax.broadcasted_iota(jnp.int32, (length, length), 1)
    allowed = (cols <= rows) | (cols < at[4])
    cosine_tab, sine_tab = cosine[...], sine[...]
    group_size = HQ // HK
    for group in range(HK):
        matrix = weight[group].reshape(first_in.shape[1], -1)
        qkv = dot(first_in, matrix)
        at_key = group_size * HD
        key = turned(qkv[:, at_key : at_key + HD], cosine_tab, sine_tab).astype(jnp.bfloat16)
        value = qkv[:, at_key + HD :].astype(jnp.bfloat16)
        key_ref[:, group * HD : (group + 1) * HD] = key
        value_ref[:, group * HD : (group + 1) * HD] = value
        for member in range(group_size):
            head = group * group_size + member
            here = slice(head * HD, (head + 1) * HD)
            query = turned(qkv[:, member * HD : (member + 1) * HD], cosine_tab, sine_tab)
            query = query.astype(jnp.bfloat16)
            query_ref[:, here] = query
            scores = dot(query, key, ((1,), (1,)))
            scores = jnp.where(allowed, scores * HD ** (-0.5), -1e30)
            weights = jnp.exp(scores - jnp.max(scores, axis=-1, keepdims=True))
            prob = weights * (1.0 / jnp.sum(weights, axis=-1, keepdims=True))
            prob = prob.astype(jnp.bfloat16)
            prob_ref[head] = prob
            out_ref[:, here] = dot(prob, value).astype(jnp.bfloat16)
        here = pl.ds(group * group_size, group_size)
        copies.append(
            pltpu.make_async_copy(prob_ref.at[here], prob_out.at[here], sems.at[group])
        )
        copies[-1].start()
    for copy in copies:
        copy.wait()


def project_kernel(at, tokens, gain, attended, *refs):
    resid_ref, second_ref, weight_out, weight, sem = refs[8:]
    place_pieces(at, refs[:8], weight)
    copy = pltpu.make_async_copy(weight, weight_out, sem)
    copy.start()
    heads = attended[...]
    halves = [dot(heads, weight[half].reshape(heads.shape[1], -1)) for half in range(2)]
    resid = tokens[...].astype(jnp.float32) + jnp.concatenate(halves, axis=1)
    resid_ref[...] = resid
    second_ref[...] = rms_kernel(resid, gain[...])
    copy.wait()


def one_hot(slots, capacity, dtype):
    shape = (capacity, slots.shape[1])
    return (slots == lax.broadcasted_iota(jnp.int32, shape, 0)).astype(jnp.float32).astype(dtype)


def slots_of(ids, expert, start, rows):
    named = jnp.any(ids[:, start : start + rows] == expert, axis=0, keepdims=True)
    named = named.astype(jnp.float32)
    before = lax.broadcasted_iota(jnp.int32, (rows, rows), 0)
    upto = lax.broadcasted_iota(jnp.int32, (rows, rows), 1)
    counts = dot(named.astype(jnp.bfloat16), (before <= upto).astype(jnp.float32).astype(jnp.bfloat16))
    return jnp.where(named > 0.0, counts - 1.0, -1.0).astype(jnp.int32)


def spread(picks, capacity, rows, outs):
    rows = rows.astype(jnp.bfloat16)
    block = picks[0].shape[1]
    for n in range(len(picks) // 2):
        for part in range(2):
            pick = picks[2 * n + part]
            at_row = (2 * n + part) * capacity
            tokens = dot(pick, rows[at_row : at_row + capacity], ((0,), (0,)))
            outs[n][part * block : (part + 1) * block] = tokens.astype(jnp.bfloat16)


def expert_kernel(capacity, pieces, at, ids, router, *refs):
    count = len(pieces)
    second, cot = refs[:count], refs[count : 2 * count]
    gate_w, up_w, down_w = refs[2 * count : 2 * count + 3]
    rows_in, rows_cot, gated_ref, gate_back, up_back, gates_ref = refs[2 * count + 3 : 2 * count + 9]
    backs, gate_rows = refs[2 * count + 9 : -1], refs[-1]
    f32, bf16 = jnp.float32, jnp.bfloat16
    length, width = second[0].shape
    wide = router.shape[1]
    half = length // 2
    picks = []
    experts = lax.broadcasted_iota(jnp.int32, (wide, length), 0)
    for n, piece in enumerate(pieces):
        tokens = second[n][...]
        named = ids[:, piece * length : (piece + 1) * length]
        chosen = functools.reduce(
            jnp.logical_or, [named[k : k + 1] == experts for k in range(named.shape[0])]
        )
        logits = jnp.where(chosen, dot(router[...], tokens, ((0,), (1,))), -1e30)
        weights = jnp.exp(logits - jnp.max(logits, axis=0, keepdims=True))
        gates = weights * (1.0 / jnp.sum(weights, axis=0, keepdims=True))
        if n == 0:
            gates_ref[...] = gates
        own = jnp.sum(jnp.where(experts == at[5], gates, 0.0), axis=0, keepdims=True)
        for part in range(2):
            here = slice(part * half, (part + 1) * half)
            place = slice((2 * n + part) * capacity, (2 * n + part + 1) * capacity)
            slots = slots_of(ids, at[5], piece * length + part * half, half)
            pick = one_hot(slots, capacity, f32)
            picks.append(pick.astype(bf16))
            rows_in[place] = dot(picks[-1], tokens[here]).astype(bf16)
            rows_cot[place] = dot(picks[-1], cot[n][here]).astype(bf16)
            gate_rows[place] = jnp.sum(pick * own[:, here], axis=1, keepdims=True)
    gate = gate_rows[...]
    gate_pre = dot(rows_in[...], gate_w[...])
    up_pre = dot(rows_in[...], up_w[...])
    cot_hidden = dot(rows_cot[...], down_w[...], ((1,), (1,)))
    scale = math.sqrt(2.0 / math.pi)
    square = gate_pre * gate_pre
    bent = jnp.tanh(scale * gate_pre * (1.0 + 0.044715 * square))
    open_part = 0.5 * (1.0 + bent)
    active = gate_pre * open_part
    slope = open_part + 0.5 * gate_pre * (1.0 - bent * bent) * scale * (
        1.0 + 3 * 0.044715 * square
    )
    hidden = active * up_pre
    gated_ref[...] = (gate * hidden).astype(bf16)
    signal = jnp.sum(hidden * cot_hidden, axis=1, keepdims=True)
    back = gate * cot_hidden
    gate_back[...] = (back * up_pre * slope).astype(bf16)
    up_back[...] = (back * active).astype(bf16)
    high = signal.astype(bf16)
    low = (signal - high.astype(f32)).astype(bf16)
    lanes = lax.broadcasted_iota(jnp.int32, (signal.shape[0], wide), 1)
    signal = jnp.where(lanes == at[5], high.astype(f32), 0.0)
    signal = jnp.where(lanes == at[5] + wide // 2, low.astype(f32), signal)
    by_rows = ((1,), (1,))
    rows = dot(gate_back[...], gate_w[...], by_rows) + dot(up_back[...], up_w[...], by_rows)
    spread(picks, capacity, jnp.concatenate([rows, signal], axis=1), backs)


def run_expert(pieces, at, ids, router, weights, second, cot, capacity):
    count = len(pieces)
    rows, wide = 2 * count * capacity, router.shape[1]
    (length, width), hidden = second[0].shape, weights[0].shape[1]
    bf16, f32 = jnp.bfloat16, jnp.float32
    outs = [(rows, width)] * 2 + [(rows, hidden)] * 3
    outs = [(shape, bf16) for shape in outs] + [((wide, length), f32)]
    outs = outs + [((length, width + wide), bf16)] * count
    return run_kernel(
        functools.partial(expert_kernel, capacity, pieces),
        4 * count,
        at,
        (ids, router, *second, *cot, *weights),
        outs,
        6 + 4 * count,
        [pltpu.VMEM((rows, 1), f32)],
    )


def mixture_kernel(capacity, groups, at, ids, *refs):
    gated, down_w, outs = refs[: len(groups)], refs[len(groups)], refs[len(groups) + 1 :]
    length = outs[0].shape[0]
    for pieces, rows in zip(groups, gated):
        picks = []
        for piece in pieces:
            for part in range(2):
                start = piece * length + part * length // 2
                slots = slots_of(ids, at[5], start, length // 2)
                picks.append(one_hot(slots, capacity, jnp.bfloat16))
        spread(picks, capacity, dot(rows[...], down_w[...]), [outs[piece] for piece in pieces])


def row_sum_kernel(parts, at, *refs):
    arrays = [
        jnp.concatenate([ref[...] for ref in refs[n : n + parts]], axis=0)
        for n in range(0, len(refs) - len(refs) // (parts + 1), parts)
    ]
    outs = refs[len(arrays) * parts :]
    for out, right in zip(outs, arrays[1:]):
        out[...] = dot(arrays[0], right, ((0,), (0,))).astype(jnp.bfloat16)


def row_sums(at, left, *rights):
    operands = [part for parts in (left, *rights) for part in parts]
    outs = [((left[0].shape[1], right[0].shape[1]), jnp.bfloat16) for right in rights]
    kernel = functools.partial(row_sum_kernel, len(left))
    return run_kernel(kernel, 4 * len(rights), at, operands, outs, 24 if len(rights) == 1 else 56)


def branch_back_kernel(
    at, near, far, first_x, first_y, last_y, last_x, resid, gain, second, gates, router, cot, weight, *outs
):
    resid_grad_ref, branch_ref, attended_ref, router_ref, gain_ref = outs
    f32, bf16 = jnp.float32, jnp.bfloat16
    halves = [first_x[...].astype(f32) + last_y[...], first_y[...].astype(f32) + last_x[...]]
    total = near[...].astype(f32) + far[...] + jnp.concatenate(halves, axis=0)
    width = resid.shape[1]
    signal = total[:, width:]
    signal = signal + pltpu.roll(signal, signal.shape[1] // 2, 1)
    chosen = gates[...].T
    logit_grad = chosen * (signal - jnp.sum(chosen * signal, axis=-1, keepdims=True))
    logit_grad = logit_grad.astype(bf16)
    second_grad = total[:, :width] + dot(logit_grad, router[...], ((1,), (1,)))
    norm_grad, gain_grad = rms_back(resid[...], gain[...], second_grad)
    gain_ref[...] = gain_grad
    resid_grad = cot[...].astype(f32) + norm_grad
    resid_grad_ref[...] = resid_grad
    branch = resid_grad.astype(bf16)
    branch_ref[...] = branch
    wide = weight.shape[2]
    attended_ref[...] = (
        dot(branch[:, :wide], weight[0], ((1,), (1,)))
        + dot(branch[:, wide:], weight[1], ((1,), (1,)))
    ).astype(bf16)
    router_ref[...] = dot(second[...], logit_grad, ((0,), (0,)))


def attend_back_kernel(
    at, attended, probs, queries, keys, values, cosine, sine, branch, back_ref
):
    f32, bf16 = jnp.float32, jnp.bfloat16
    cosine_tab, sine_tab = cosine[...], -sine[...]
    group_size = HQ // HK
    places, length = back_ref.shape[0], branch.shape[0]
    branch_width = branch.shape[1] // places
    width = back_ref.shape[2] - branch_width
    for place in range(places):
        here = slice(place * branch_width, (place + 1) * branch_width)
        back_ref[place, :length, width:] = branch[:, here]
        back_ref[place, length:] = jnp.zeros((back_ref.shape[1] - length, back_ref.shape[2]), bf16)
    scale = HD ** (-0.5)

    def put(position, block):
        back_ref[position // width, :length, position % width : position % width + HD] = block

    for group in range(HK):
        own = slice(group * HD, (group + 1) * HD)
        key, value = keys[:, own], values[:, own]
        key_grad = value_grad = 0.0
        start = group * (group_size + 2) * HD
        for member in range(group_size):
            head = group * group_size + member
            here = slice(head * HD, (head + 1) * HD)
            out_grad, query, prob = attended[:, here], queries[:, here], probs[head]
            prob_grad = dot(out_grad, value, ((1,), (1,)))
            prob_f = prob.astype(f32)
            inner = jnp.sum(prob_f * prob_grad, axis=-1, keepdims=True)
            score_grad = (prob_f * (prob_grad - inner)).astype(bf16)
            query_grad = turned(dot(score_grad, key) * scale, cosine_tab, sine_tab)
            put(start + member * HD, query_grad.astype(bf16))
            key_grad = key_grad + dot(score_grad, query, ((0,), (0,)))
            value_grad = value_grad + dot(prob, out_grad, ((0,), (0,)))
        key_grad = turned(key_grad * scale, cosine_tab, sine_tab)
        put(start + group_size * HD, key_grad.astype(bf16))
        put(start + (group_size + 1) * HD, value_grad.astype(bf16))


def first_back_kernel(at, back, weight, tokens, gain, resid_grad, tokens_ref, gain_ref):
    f32 = jnp.float32
    parts = back.shape[0]
    cols = weight.shape[0] * weight.shape[2] // parts
    first_grad = 0.0
    for part in range(parts):
        group, place = divmod(part * cols, weight.shape[2])
        first_grad = first_grad + dot(
            back[part, : tokens.shape[0], :cols], weight[group, :, place : place + cols], ((1,), (1,))
        )
    norm_grad, gain_grad = rms_back(tokens[...].astype(f32), gain[...], first_grad)
    gain_ref[...] = gain_grad
    tokens_ref[...] = (resid_grad[...] + norm_grad).astype(jnp.bfloat16)


def dense_grad_kernel(at, back, *refs):
    pieces, out_ref, held, sems = refs[:8], refs[8], refs[9], refs[10]
    copies = [
        pltpu.make_async_copy(piece, held.at[n], sems.at[n]) for n, piece in enumerate(pieces)
    ]
    for copy in copies:
        copy.start()
    depth, rows, cols = out_ref.shape
    length = held.shape[1] // 2
    qkv_width = cols - held.shape[2] // back.shape[0]
    narrow = sum(back[place, length:].astype(jnp.float32) for place in range(back.shape[0]))
    sums = [0.0, 0.0]
    for n, copy in enumerate(copies):
        copy.wait()
        dc, dy, dx = n // 4, n // 2 % 2, n % 2
        place = 4 * (at[0] ^ dy) + 2 * (at[1] ^ dc) + (at[2] ^ dx)
        own = back[place, :length]
        sums[0] = sums[0] + dot(held[n, length:], own[:, :qkv_width], ((0,), (0,)))
        sums[1] = sums[1] + dot(held[n, :length], own[:, qkv_width:], ((0,), (0,)))
    wide = held.shape[2] // depth
    each = 4
    for z in range(depth):
        here = slice(z * wide, (z + 1) * wide)
        both = jnp.concatenate([part[here] for part in sums], axis=1)
        out_ref[z, :wide] = both.astype(jnp.bfloat16)
        kept = [narrow[z * each : (z + 1) * each], jnp.zeros((rows - wide - each, cols), jnp.float32)]
        out_ref[z, wide:] = jnp.concatenate(kept, axis=0).astype(jnp.bfloat16)


def finish_kernel(at, sums, query_ref, key_ref, value_ref, output_ref):
    places, _, cols = sums.shape
    rows, out_width = query_ref.shape[0], output_ref.shape[1] // places
    width = cols - out_width
    for place in range(places):
        block = sums[place, :rows].astype(jnp.float32)
        output_ref[:, place * out_width : (place + 1) * out_width] = block[:, width:]
        for at_col in range(0, width, HD):
            group, head = divmod((place * width + at_col) // HD, HQ // HK + 2)
            part = block[:, at_col : at_col + HD]
            if head < HQ // HK:
                start = (group * (HQ // HK) + head) * HD
                query_ref[:, start : start + HD] = part
            elif head == HQ // HK:
                key_ref[:, group * HD : (group + 1) * HD] = part
            else:
                value_ref[:, group * HD : (group + 1) * HD] = part


def local_pairs(
    tokens,
    norm1_gain,
    w_query,
    w_key,
    w_value,
    w_out,
    norm2_gain,
    w_router,
    w_gate,
    w_up,
    w_down,
    expert_ids,
    prefix_len,
    out_grad,
):
    bf16, f32 = jnp.bfloat16, jnp.float32
    length, model_width = tokens.shape
    shard_rows = w_query.shape[0]
    local_count, _, hidden_width = w_gate.shape
    owners = lax.axis_size("x")
    depth = lax.axis_size("z")
    plane = lax.axis_size(PLANE)
    experts_all = w_router.shape[1]
    block_rows = length // MICRO
    capacity = 3 * block_rows * expert_ids.shape[1] // (2 * experts_all)
    plane_rows = plane * length
    blocks = plane_rows // block_rows
    q_cols, kv_cols = w_query.shape[1], w_key.shape[1]
    qkv_cols = q_cols + 2 * kv_cols
    q_group, out_half = q_cols // HK, model_width // 2
    y, c, x, z = (lax.axis_index(axis) for axis in ("y", "c", "x", "z"))
    own_local = 2 * y + c
    own_expert = x * local_count + own_local
    at = jnp.stack([y, c, x, z, prefix_len[0], own_expert, own_local])

    own_half = jnp.concatenate(
        [
            lax.dynamic_slice_in_dim(part, x * (part.shape[1] // 2), part.shape[1] // 2, 1)
            for part in (w_query, w_key, w_value, w_out)
        ],
        axis=1,
    )
    narrow = jnp.concatenate([w_router, norm1_gain[:, None], norm2_gain[:, None]], axis=1)
    narrow = jnp.pad(narrow, ((0, 0), (0, 128 - narrow.shape[1])))
    router_w = small_group_gather(narrow)
    ids_all = small_gather(expert_ids.T)
    column = [own_half] + shifts(own_half)
    cot_sides = plane_sides(after(out_grad, router_w, ids_all))
    qkv_half = qkv_cols // 2
    qkv_column = jnp.stack([part[:, :qkv_half] for part in column])
    out_column = jnp.stack([part[:, qkv_half:] for part in column])
    qkv_column, out_column = lax.optimization_barrier((qkv_column, out_column, *cot_sides))[:2]
    sliced = after(own_local, column[-1])
    gate_w, up_w, down_w = (
        lax.dynamic_index_in_dim(weight, sliced, 0, keepdims=False)
        for weight in (w_gate, w_up, w_down)
    )
    qkv_sides = plane_sides(qkv_column)
    gains = router_w[:, experts_all : experts_all + 2].T.astype(f32)
    gain_one, gain_two = gains[:1], gains[1:]
    qkv_corner = plane_corner(qkv_sides, (gate_w, up_w, down_w, gain_one, gain_two))
    out_sides = plane_sides(after(out_column, *qkv_sides))
    qkv_pieces = plane_pieces(qkv_column, qkv_sides, qkv_corner)
    cosine_tab, sine_tab = angles(length, HD)
    cosine_all = jnp.concatenate([cosine_tab, cosine_tab], axis=2)[:, 0]
    sine_all = jnp.concatenate([-sine_tab, sine_tab], axis=2)[:, 0]
    weight_lead = (2, depth, 2, 2, shard_rows)
    first_in, queries, keys_rot, values_b, attended, probs, qkv_w = run_kernel(
        attend_kernel,
        11,
        at,
        (tokens, gain_one, cosine_all, sine_all, *qkv_pieces),
        [
            ((length, model_width), bf16),
            ((length, q_cols), bf16),
            ((length, kv_cols), bf16),
            ((length, kv_cols), bf16),
            ((length, q_cols), bf16),
            ((HQ, length, length), bf16),
            (weight_lead + (qkv_half,), bf16),
        ],
        28,
        [
            pltpu.VMEM((HQ, length, length), bf16),
            pltpu.VMEM(weight_lead + (qkv_half,), bf16),
            pltpu.SemaphoreType.DMA((HK + 1,)),
        ],
        hbm_out=2,
    )
    out_sides = lax.optimization_barrier((*out_sides, attended))[:2]
    out_corner = plane_corner(out_sides)
    cot_corner = plane_corner(cot_sides)
    out_pieces = plane_pieces(out_column, out_sides, out_corner)
    cot_pieces = plane_pieces(out_grad, cot_sides, cot_corner)
    resid, second_in, output_w = run_kernel(
        project_kernel,
        4,
        at,
        (tokens, after(gain_two, cot_corner), attended, *out_pieces),
        [
            ((length, model_width), f32),
            ((length, model_width), bf16),
            (weight_lead + (out_half,), bf16),
        ],
        44,
        [pltpu.VMEM(weight_lead + (out_half,), bf16), pltpu.SemaphoreType.DMA],
        hbm_out=1,
    )
    qkv_w = qkv_w.reshape(HK, model_width, qkv_half)
    output_w = output_w.reshape(2, q_cols, out_half)

    expert = functools.partial(
        run_expert,
        at=at,
        ids=ids_all,
        router=router_w,
        weights=(gate_w, up_w, down_w),
        capacity=capacity,
    )
    second_sides = plane_sides(second_in)
    groups = ((0, 4), (1, 5, 2, 6), (3, 7))
    second_pieces = {0: second_in, 4: swap(second_in, "c")}

    def run_group(pieces):
        return expert(
            pieces,
            second=[second_pieces[piece] for piece in pieces],
            cot=[cot_pieces[piece] for piece in pieces],
        )

    stage_own = run_group(groups[0])
    second_sides = lax.optimization_barrier((*second_sides, stage_own[0]))[:2]
    for piece, block in zip((1, 2), second_sides):
        second_pieces[piece], second_pieces[piece + 4] = block, swap(block, "c")
    stage_sides = run_group(groups[1])
    second_corner = plane_corner(second_sides, later=(stage_sides[0],))
    second_pieces[3], second_pieces[7] = second_corner, swap(second_corner, "c")
    own_near, own_far = stage_own[6:]
    own_far = swap(own_far, "c")
    x_near, x_far, y_near, y_far = stage_sides[6:]
    back_x, back_y = over_core(x_near, x_far), over_core(y_near, y_far)
    first_x, first_y = early_sums(back_x, back_y)
    stage_corner = run_group(groups[2])
    corner = over_core(*stage_corner[6:])
    passed = corner_first(corner)
    stages = (stage_own, stage_sides, stage_corner)
    rows_in, rows_cot, gated, gate_back, up_back = ([stage[n] for stage in stages] for n in range(5))
    gates = stage_own[5]
    last_y, last_x, *sent = corner_last(back_x, back_y, passed)
    (down_part,) = row_sums(
        at, [after(rows_cot[0], *sent, first_x, first_y)] + rows_cot[1:], gated
    )
    down_sum = scatter_sum(down_part, "z")
    gate_part, up_part = row_sums(
        at, [after(rows_in[0], down_part, own_far)] + rows_in[1:], gate_back, up_back
    )
    gate_sum = scatter_sum(gate_part, "z")
    own_near = after(own_near, gate_part)

    resid_grad, branch_grad, attended_grad, router_acc, gain_two_grad = run_kernel(
        branch_back_kernel,
        6,
        at,
        (
            own_near,
            own_far,
            first_x,
            first_y,
            last_y,
            last_x,
            resid,
            gain_two,
            second_in,
            gates,
            router_w,
            out_grad,
            output_w,
        ),
        [
            ((length, model_width), f32),
            ((length, model_width), bf16),
            ((length, q_cols), bf16),
            ((model_width, 128), f32),
            ((1, model_width), f32),
        ],
        56,
    )
    qkv_width, branch_width = qkv_cols // plane, model_width // plane
    dense_cols = qkv_width + branch_width
    (back_cols,) = run_kernel(
        attend_back_kernel,
        6,
        at,
        (
            attended_grad,
            probs,
            queries,
            keys_rot,
            values_b,
            cosine_all,
            sine_all,
            branch_grad,
        ),
        [((plane, length + 16, dense_cols), bf16)],
        56,
    )
    tokens_grad, gain_one_grad = run_kernel(
        first_back_kernel,
        5,
        at,
        (back_cols, qkv_w, tokens, gain_one, resid_grad),
        [((length, model_width), bf16), ((1, model_width), f32)],
        24,
    )

    both = jnp.concatenate(
        lax.optimization_barrier((attended, first_in, last_y, last_x))[:2], axis=0
    )
    both_sides = plane_sides(both)
    narrow_part = jnp.concatenate(
        [router_acc[:, :experts_all], gain_one_grad.T, gain_two_grad.T], axis=1
    )
    narrow_cols = -(-narrow_part.shape[1] // owners) * owners
    narrow_part = jnp.pad(narrow_part, ((0, 0), (0, narrow_cols - narrow_part.shape[1])))
    narrow_part = jnp.transpose(
        narrow_part.reshape(depth, 2, 2, shard_rows, owners, narrow_cols // owners),
        (1, 2, 4, 0, 3, 5),
    ).reshape(plane, depth, shard_rows * narrow_cols // owners)
    narrow_len = narrow_part.shape[2]
    narrow_rows = -(-narrow_len // dense_cols)
    each_rows = -(-narrow_rows // 4) * 4
    narrow_part = jnp.pad(
        narrow_part, ((0, 0), (0, 0), (0, each_rows * dense_cols - narrow_len))
    ).reshape(plane, depth * each_rows, dense_cols)
    narrow_part = jnp.pad(
        narrow_part.astype(bf16), ((0, 0), (0, 16 - depth * each_rows), (0, 0))
    )
    back_cols = lax.dynamic_update_slice(back_cols, narrow_part, (0, length, 0))
    back_cols = exchange(after(back_cols, down_sum, *both_sides), PLANE)
    both_corner = plane_corner(both_sides, (back_cols,))
    both_pieces = plane_pieces(both, both_sides, both_corner)
    def placed(total):
        total = exchange(total, ("y", "c"))
        return total.reshape(local_count, shard_rows, hidden_width).astype(f32)

    down_grad, gate_grad = placed(down_sum), placed(gate_sum)
    kept_rows = -(-narrow_rows // 16) * 16
    wide_rows = local_count * shard_rows
    dense_shape = (depth, wide_rows + kept_rows, dense_cols)
    dense_part = pl.pallas_call(
        dense_grad_kernel,
        out_shape=jax.ShapeDtypeStruct(dense_shape, bf16),
        in_specs=[SCALARS, WHOLE] + [IN_HBM] * 8,
        out_specs=WHOLE,
        scratch_shapes=[
            pltpu.VMEM((plane, 2 * length, model_width), bf16),
            pltpu.SemaphoreType.DMA((plane,)),
        ],
        cost_estimate=cost(8),
        compiler_params=pltpu.CompilerParams(vmem_limit_bytes=32 * 2**20),
    )(at, after(back_cols, down_grad), *both_pieces)
    dense_part = after(dense_part, gate_sum)
    dense_sum = scatter_sum(dense_part.reshape(-1, dense_cols), "z")
    wide_sum = dense_sum[: local_count * shard_rows].reshape(2, 2, 1, shard_rows, dense_cols)
    wide_sum = jnp.broadcast_to(wide_sum, (2, 2, owners, shard_rows, dense_cols)).reshape(
        plane, shard_rows, dense_cols
    )
    narrow_sum = dense_sum[local_count * shard_rows :][:narrow_rows]
    narrow_sum = jnp.broadcast_to(narrow_sum[None], (plane, narrow_rows, dense_cols))
    pad_rows = -(shard_rows + narrow_rows) % 16
    padding = jnp.zeros((plane, pad_rows, dense_cols), bf16)
    dense_sum = exchange(jnp.concatenate([wide_sum, narrow_sum, padding], axis=1), PLANE)
    query_grad, key_grad, value_grad, output_grad = run_kernel(
        finish_kernel,
        2,
        at,
        (dense_sum,),
        [
            ((shard_rows, q_cols), f32),
            ((shard_rows, kv_cols), f32),
            ((shard_rows, kv_cols), f32),
            ((shard_rows, model_width), f32),
        ],
    )
    narrow_sum = dense_sum[:, shard_rows : shard_rows + narrow_rows].reshape(
        2, 2, owners, narrow_rows * dense_cols
    )
    narrow_sum = narrow_sum[y, c, :, :narrow_len].reshape(owners, shard_rows, -1)
    narrow_sum = jnp.moveaxis(narrow_sum, 0, 1).reshape(shard_rows, narrow_cols).astype(f32)

    up_sum = scatter_sum(after(up_part, dense_sum), "z")

    shares = run_kernel(
        functools.partial(mixture_kernel, capacity, groups),
        10,
        at,
        (ids_all, after(gated[0], *both_sides), *gated[1:], down_w),
        [((length, model_width), bf16)] * plane,
        56,
    )
    mixed = [over_core(near, far) for near, far in zip(shares[:4], shares[4:])]
    early = early_sums(mixed[1], mixed[2])
    last = corner_last(mixed[1], mixed[2], corner_first(mixed[3]))[:2]
    mixture = jnp.concatenate(
        [left.astype(f32) + right.astype(f32) for left, right in zip(early, last)], axis=0
    )
    block_out = (resid + (mixture + mixed[0].astype(f32))).astype(bf16)

    return (
        block_out,
        tokens_grad,
        narrow_sum[:, experts_all],
        query_grad,
        key_grad,
        value_grad,
        output_grad,
        narrow_sum[:, experts_all + 1],
        narrow_sum[:, :experts_all],
        gate_grad,
        placed(up_sum),
        jnp.swapaxes(down_grad, 1, 2),
    )


def solution(mesh):
    groups, owners = mesh.shape["dp"], mesh.shape["expert"]
    grid = jax.sharding.Mesh(
        mesh.devices.reshape(groups // 4, 2, 2, owners), ("z", "y", "c", "x")
    )
    rows = P(("z", "y", "c", "x"), None)
    shard, shard_rows = P(GROUP), P(GROUP, None)
    expert = P("x", None, None)
    return jax.shard_map(
        local_pairs if owners == 2 else local_wide,
        mesh=grid,
        in_specs=(
            rows,
            shard,
            shard_rows,
            shard_rows,
            shard_rows,
            shard_rows,
            shard,
            shard_rows,
            expert,
            expert,
            expert,
            rows,
            P(("z", "y", "c", "x")),
            rows,
        ),
        out_specs=(
            rows,
            rows,
            shard,
            shard_rows,
            shard_rows,
            shard_rows,
            shard_rows,
            shard,
            shard_rows,
            P("x", GROUP, None),
            P("x", GROUP, None),
            P("x", None, GROUP),
        ),
        check_vma=False,
    )
```

```python
import functools
import math

import jax
import jax.numpy as jnp
from jax import lax
from jax.experimental import pallas as pl
from jax.experimental.pallas import tpu as pltpu
from jax.sharding import PartitionSpec as P

HQ = 12
HK = 2
HD = 128
MICRO = 2
PLANE = ("y", "c", "x")
GROUP = ("z", "y", "c")


def rms_scale(values, gain_vec):
    inverse = lax.rsqrt(jnp.mean(values * values, axis=-1, keepdims=True) + 1e-06)
    return values * inverse * gain_vec


def angles(length, head_size):
    positions = jnp.arange(length).astype(jnp.float32)
    freq_rates = jnp.exp(
        -(2.0 * jnp.arange(head_size // 2).astype(jnp.float32) / head_size) * math.log(1000000.0)
    )
    angle_tab = positions[:, None] * freq_rates[None, :]
    return (jnp.cos(angle_tab)[:, None, :], jnp.sin(angle_tab)[:, None, :])


def rotary(values, cosine_tab, sine_tab):
    half_dim = values.shape[-1] // 2
    first_half = values[..., :half_dim]
    second_half = values[..., half_dim:]
    return jnp.concatenate(
        [
            first_half * cosine_tab - second_half * sine_tab,
            second_half * cosine_tab + first_half * sine_tab,
        ],
        axis=-1,
    )


def expert_act(gate_pre, up_pre):
    return jax.nn.gelu(gate_pre, approximate=True) * up_pre


def left_product(left_mat, right_mat):
    return lax.dot_general(
        left_mat, right_mat, (((0,), (0,)), ((), ())), preferred_element_type=jnp.float32
    )


def gather(block, axes):
    return lax.all_gather(block, axes, axis=0, tiled=True)


def exchange(block, axes):
    return lax.all_to_all(block, axes, split_axis=0, concat_axis=0, tiled=True)


def scatter_sum(block, axes):
    return lax.psum_scatter(block, axes, scatter_dimension=0, tiled=True)


def by_owner(cols, parts):
    rows, total = cols.shape
    return jnp.moveaxis(cols.reshape(rows, parts, total // parts), 1, 0).reshape(
        parts * rows, total // parts
    )


def local_wide(
    tokens,
    norm1_gain,
    w_query,
    w_key,
    w_value,
    w_out,
    norm2_gain,
    w_router,
    w_gate,
    w_up,
    w_down,
    expert_ids,
    prefix_len,
    out_grad,
):
    bf16, f32 = jnp.bfloat16, jnp.float32
    length, model_width = tokens.shape
    shard_rows = w_query.shape[0]
    local_count, _, hidden_width = w_gate.shape
    owners = lax.axis_size("x")
    depth = lax.axis_size("z")
    plane = lax.axis_size(PLANE)
    experts_all = w_router.shape[1]
    top_count = expert_ids.shape[1]
    block_rows = length // MICRO
    capacity = 3 * block_rows * top_count // (2 * experts_all)
    plane_rows = plane * length
    blocks = plane_rows // block_rows
    group_size = HQ // HK
    score_scale = HD ** (-0.5)
    q_cols, kv_cols = w_query.shape[1], w_key.shape[1]
    own_local = lax.axis_index(("y", "c"))
    own_expert = lax.axis_index("x") * local_count + own_local
    own_place = lax.axis_index(PLANE)

    narrow = jnp.concatenate([w_router, norm1_gain[:, None], norm2_gain[:, None]], axis=1)
    narrow = jnp.pad(narrow, ((0, 0), (0, -narrow.shape[1] % 128)))
    packed = gather(jnp.concatenate([w_query, w_key, w_value, narrow], axis=1), GROUP)
    qkv_cols = q_cols + 2 * kv_cols
    qkv_w = packed[:, :qkv_cols]
    router_w = packed[:, qkv_cols : qkv_cols + experts_all]
    gains = packed[:, qkv_cols + experts_all : qkv_cols + experts_all + 2].T.astype(f32)
    gain_one, gain_two = gains[0], gains[1]
    output_w = gather(w_out, GROUP)

    ids_all = gather(expert_ids, PLANE)
    cot_all = gather(out_grad, PLANE)
    chosen_mask = jnp.any(
        ids_all[:, :, None] == jnp.arange(experts_all, dtype=jnp.int32)[None, None, :], axis=1
    )
    own_mask = jnp.any(ids_all == own_expert, axis=1).reshape(blocks, block_rows)
    place = jnp.cumsum(own_mask.astype(jnp.int32), axis=1) - 1
    dispatch = (
        own_mask[:, None, :]
        & (place[:, None, :] == jnp.arange(capacity, dtype=jnp.int32)[None, :, None])
    ).astype(bf16)

    cosine_tab, sine_tab = angles(length, HD)
    inputs_f = tokens.astype(f32)
    first_in = rms_scale(inputs_f, gain_one).astype(bf16)
    qkv = jnp.dot(first_in, qkv_w, preferred_element_type=f32)
    queries = (
        rotary(qkv[:, :q_cols].reshape(length, HQ, HD), cosine_tab, sine_tab)
        .astype(bf16)
        .reshape(length, HK, group_size, HD)
    )
    keys_rot = rotary(
        qkv[:, q_cols : q_cols + kv_cols].reshape(length, HK, HD), cosine_tab, sine_tab
    ).astype(bf16)
    values_b = qkv[:, q_cols + kv_cols :].astype(bf16).reshape(length, HK, HD)
    positions = jnp.arange(length)
    allowed = (positions[None, :] <= positions[:, None]) | (positions[None, :] < prefix_len[0])

    def masked_scores():
        scores = jnp.einsum("ihrd,jhd->hrij", queries, keys_rot, preferred_element_type=f32)
        return jnp.where(allowed, scores * score_scale, -1e30)

    masked = masked_scores()
    row_peak = jnp.max(masked, axis=-1, keepdims=True)
    log_total = row_peak + jnp.log(jnp.sum(jnp.exp(masked - row_peak), axis=-1, keepdims=True))
    prob_bf = jnp.exp(masked - log_total).astype(bf16)
    attended = jnp.einsum("hrij,jhd->ihrd", prob_bf, values_b, preferred_element_type=f32)
    attended = attended.reshape(length, HQ * HD).astype(bf16)
    resid = inputs_f + jnp.dot(attended, output_w, preferred_element_type=f32)
    second_in = rms_scale(resid, gain_two).astype(bf16)

    second_all = gather(second_in, PLANE)
    logits = jnp.dot(second_all, router_w, preferred_element_type=f32)
    gates_all = jax.nn.softmax(jnp.where(chosen_mask, logits, -jnp.inf), axis=-1)
    own_gates = lax.dynamic_index_in_dim(gates_all, own_expert, 1, keepdims=False)
    own_gates = own_gates.reshape(blocks, block_rows)
    gate_rows = jnp.einsum(
        "bct,bt->bc", dispatch.astype(f32), own_gates, precision=lax.Precision.HIGHEST
    )[:, :, None]
    gate_w = lax.dynamic_index_in_dim(w_gate, own_local, 0, keepdims=False)
    up_w = lax.dynamic_index_in_dim(w_up, own_local, 0, keepdims=False)
    down_w = lax.dynamic_index_in_dim(w_down, own_local, 0, keepdims=False)

    def to_rows(array):
        return jnp.einsum(
            "bct,btd->bcd",
            dispatch,
            array.reshape(blocks, block_rows, model_width),
            preferred_element_type=f32,
        ).astype(bf16)

    def to_tokens(rows):
        return (
            jnp.einsum("bct,bcd->btd", dispatch, rows.astype(bf16), preferred_element_type=f32)
            .astype(bf16)
            .reshape(plane_rows, model_width)
        )

    rows_in = to_rows(second_all)
    rows_cot = to_rows(cot_all)
    gate_pre = jnp.einsum("bcd,df->bcf", rows_in, gate_w, preferred_element_type=f32)
    up_pre = jnp.einsum("bcd,df->bcf", rows_in, up_w, preferred_element_type=f32)
    hidden, act_pull = jax.vjp(expert_act, gate_pre, up_pre)
    gated = (gate_rows * hidden).astype(bf16)
    down_part = jnp.einsum("bcd,bcf->df", rows_cot, gated, preferred_element_type=f32)
    down_sum = scatter_sum(down_part.astype(bf16), "z")
    cot_hidden = jnp.einsum("bcd,fd->bcf", rows_cot, down_w, preferred_element_type=f32)
    gate_signal_rows = jnp.sum(hidden * cot_hidden, axis=-1)
    gate_pgrad, up_pgrad = act_pull(gate_rows * cot_hidden)
    gate_pgrad = gate_pgrad.astype(bf16)
    up_pgrad = up_pgrad.astype(bf16)
    gate_part = jnp.einsum("bcd,bcf->df", rows_in, gate_pgrad, preferred_element_type=f32)
    gate_sum = scatter_sum(gate_part.astype(bf16), "z")
    up_part = jnp.einsum("bcd,bcf->df", rows_in, up_pgrad, preferred_element_type=f32)
    up_sum = scatter_sum(up_part.astype(bf16), "z")
    rows_grad = jnp.einsum("bcf,df->bcd", gate_pgrad, gate_w, preferred_element_type=f32)
    rows_grad = rows_grad + jnp.einsum("bcf,df->bcd", up_pgrad, up_w, preferred_element_type=f32)
    second_back = scatter_sum(to_tokens(rows_grad), PLANE).astype(f32)
    gate_signal = jnp.einsum(
        "bct,bc->bt", dispatch.astype(f32), gate_signal_rows, precision=lax.Precision.HIGHEST
    )
    gate_signal = exchange(gate_signal.reshape(plane, length), PLANE)
    gate_signal = jnp.transpose(
        gate_signal.reshape(local_count, owners, length), (2, 1, 0)
    ).reshape(length, experts_all)
    expert_rows = jnp.einsum("bcf,fd->bcd", gated, down_w, preferred_element_type=f32)
    mixture = scatter_sum(to_tokens(expert_rows), PLANE).astype(f32)
    block_out = (resid + mixture).astype(bf16)

    cotangent = out_grad.astype(f32)
    gate_probs = lax.dynamic_slice_in_dim(gates_all, own_place * length, length, 0)
    logit_grad = (
        gate_probs
        * (gate_signal - jnp.sum(gate_probs * gate_signal, axis=-1, keepdims=True))
    ).astype(bf16)
    router_acc = left_product(second_in, logit_grad)
    second_grad = second_back + jnp.dot(logit_grad, router_w.T, preferred_element_type=f32)
    _, norm_two_pull = jax.vjp(rms_scale, resid, gain_two)
    resid_norm_grad, gain_two_grad = norm_two_pull(second_grad)
    resid_grad = cotangent + resid_norm_grad
    branch_grad = resid_grad.astype(bf16)

    attended_all = gather(attended, PLANE)
    branch_cols = exchange(by_owner(branch_grad, plane), PLANE)
    output_part = left_product(attended_all, branch_cols)
    attended_grad = jnp.dot(branch_grad, output_w.T, preferred_element_type=f32).astype(bf16)
    attended_grad = attended_grad.reshape(length, HK, group_size, HD)
    masked = masked_scores()
    prob_full = jnp.exp(masked - log_total)
    prob_bf = prob_full.astype(bf16)
    prob_grad = jnp.einsum("ihrd,jhd->hrij", attended_grad, values_b, preferred_element_type=f32)
    row_inner = jnp.sum(prob_full * prob_grad, axis=-1, keepdims=True)
    score_grad = (prob_full * (prob_grad - row_inner)).astype(bf16)
    query_rot_grad = (
        jnp.einsum("hrij,jhd->ihrd", score_grad, keys_rot, preferred_element_type=f32)
        * score_scale
    )
    query_back = rotary(query_rot_grad.reshape(length, HQ, HD), cosine_tab, -sine_tab)
    query_back = query_back.astype(bf16).reshape(length, HQ * HD)
    key_rot_grad = (
        jnp.einsum("hrij,ihrd->jhd", score_grad, queries, preferred_element_type=f32)
        * score_scale
    )
    key_back = rotary(key_rot_grad, cosine_tab, -sine_tab).astype(bf16).reshape(length, HK * HD)
    value_back = jnp.einsum("hrij,ihrd->jhd", prob_bf, attended_grad, preferred_element_type=f32)
    value_back = value_back.astype(bf16).reshape(length, HK * HD)
    qkv_back = jnp.concatenate([query_back, key_back, value_back], axis=1)
    first_all = gather(first_in, PLANE)
    qkv_part = left_product(first_all, exchange(by_owner(qkv_back, plane), PLANE))
    first_grad = lax.dot_general(
        qkv_back, qkv_w, (((1,), (1,)), ((), ())), preferred_element_type=f32
    )
    _, norm_one_pull = jax.vjp(rms_scale, inputs_f, gain_one)
    input_norm_grad, gain_one_grad = norm_one_pull(first_grad)
    tokens_grad = (resid_grad + input_norm_grad).astype(bf16)

    narrow_part = jnp.concatenate(
        [router_acc, gain_one_grad[:, None], gain_two_grad[:, None]], axis=1
    ).astype(bf16)
    narrow_cols = narrow_part.shape[1]
    narrow_sum = lax.psum(scatter_sum(narrow_part, GROUP), "x").astype(f32)
    dense_part = jnp.concatenate([qkv_part, output_part], axis=1).astype(bf16)
    dense_sum = scatter_sum(dense_part, "z")
    dense_cols = dense_sum.shape[1]
    dense_sum = gather(dense_sum, PLANE).reshape(plane, local_count, shard_rows, dense_cols)
    dense_sum = lax.dynamic_index_in_dim(dense_sum, own_local, 1, keepdims=False).astype(f32)
    dense_sum = jnp.moveaxis(dense_sum, 0, 1)
    qkv_width = qkv_cols // plane
    qkv_sum = dense_sum[:, :, :qkv_width].reshape(shard_rows, qkv_cols)
    output_sum = dense_sum[:, :, qkv_width:].reshape(shard_rows, model_width)

    def placed(total):
        total = exchange(total, ("y", "c"))
        return total.reshape(local_count, shard_rows, hidden_width).astype(f32)

    return (
        block_out,
        tokens_grad,
        narrow_sum[:, experts_all],
        qkv_sum[:, :q_cols],
        qkv_sum[:, q_cols : q_cols + kv_cols],
        qkv_sum[:, q_cols + kv_cols :],
        output_sum,
        narrow_sum[:, experts_all + 1],
        narrow_sum[:, :experts_all],
        placed(gate_sum),
        placed(up_sum),
        jnp.swapaxes(placed(down_sum), 1, 2),
    )


def rounded(values):
    return lax.reduce_precision(values, 8, 7).astype(jnp.bfloat16)


def after(block, *others):
    return lax.optimization_barrier((block,) + others)[0]


def swap(block, axis):
    return lax.ppermute(block, axis, [(0, 1), (1, 0)])


def shifts(block):
    depth = lax.axis_size("z")
    return [
        lax.ppermute(block, "z", [(i, (i + k) % depth) for i in range(depth)])
        for k in range(1, depth)
    ]


def plane_sides(block):
    return swap(block, "x"), swap(block, "y")


def plane_corner(sides, before=(), later=()):
    over_x, over_y = sides
    half = over_x.shape[0] // 2
    over_y, over_x = lax.optimization_barrier((over_y[:half], over_x[half:]) + before)[:2]
    parts = (swap(over_y, "x"), swap(over_x, "y"))
    return jnp.concatenate(lax.optimization_barrier(parts + later)[:2], axis=0)


def plane_pieces(block, sides=None, corner=None):
    sides = plane_sides(block) if sides is None else sides
    corner = plane_corner(sides) if corner is None else corner
    pieces = [block, *sides, corner]
    return pieces + [swap(piece, "c") for piece in pieces]


def small_gather(block):
    for axis in ("x", "y", "c"):
        block = jnp.concatenate([block, swap(block, axis)], axis=1)
    return block


def small_group_gather(block):
    depth = lax.axis_size("z")
    order = jnp.stack(([block] + shifts(block))[::-1] * 2)
    start = (depth - 1 - lax.axis_index("z")) % depth
    total = lax.dynamic_slice_in_dim(order, start, depth, 0)[:, None, None]
    for dim, axis in ((1, "y"), (2, "c")):
        other = swap(total, axis)
        last = lax.axis_index(axis) == 1
        pair = [jnp.where(last, other, total), jnp.where(last, total, other)]
        total = jnp.concatenate(pair, axis=dim)
    return total.reshape(-1, block.shape[1])


def add(left, right):
    return rounded(left.astype(jnp.float32) + right.astype(jnp.float32))


def over_core(near, far):
    return add(near, swap(far, "c"))


def early_sums(over_x, over_y):
    half = over_x.shape[0] // 2
    return swap(over_x[:half], "x"), swap(over_y[half:], "y")


def corner_first(corner):
    half = corner.shape[0] // 2
    return swap(corner[:half], "x"), swap(corner[half:], "y")


def corner_last(over_x, over_y, first):
    half = over_x.shape[0] // 2
    over_y, over_x = add(over_y[:half], first[0]), add(over_x[half:], first[1])
    return swap(over_y, "y"), swap(over_x, "x"), over_y, over_x


def cost(micros):
    return pl.CostEstimate(flops=micros * 10**9, bytes_accessed=micros * 10**6, transcendentals=0)


def dot(left, right, dims=((1,), (0,)), precision=None):
    return lax.dot_general(
        left, right, (dims, ((), ())), precision=precision, preferred_element_type=jnp.float32
    )


WHOLE = pl.BlockSpec(memory_space=pltpu.VMEM)
IN_HBM = pl.BlockSpec(memory_space=pltpu.HBM)
SCALARS = pl.BlockSpec(memory_space=pltpu.SMEM)


def run_kernel(kernel, micros, at, operands, outs, megabytes=16, scratch=(), hbm_in=0, hbm_out=0):
    return pl.pallas_call(
        kernel,
        out_shape=[jax.ShapeDtypeStruct(shape, dtype) for shape, dtype in outs],
        in_specs=[SCALARS] + [WHOLE] * (len(operands) - hbm_in) + [IN_HBM] * hbm_in,
        out_specs=[WHOLE] * (len(outs) - hbm_out) + [IN_HBM] * hbm_out,
        scratch_shapes=scratch,
        cost_estimate=cost(micros),
        compiler_params=pltpu.CompilerParams(vmem_limit_bytes=megabytes * 2**20),
    )(at, *operands)


def place_pieces(at, refs, weight):
    depth = weight.shape[1]
    for n, ref in enumerate(refs):
        dc, dy, dx = n // 4, n // 2 % 2, n % 2
        for k in range(depth):
            z = lax.rem(at[3] + depth - k, depth)
            weight[at[2] ^ dx, z, at[0] ^ dy, at[1] ^ dc] = ref[k]


def rms_kernel(values, gain):
    inverse = lax.rsqrt(jnp.mean(values * values, axis=-1, keepdims=True) + 1e-06)
    return (values * inverse * gain).astype(jnp.bfloat16)


def rms_back(values, gain, grad):
    inverse = lax.rsqrt(jnp.mean(values * values, axis=-1, keepdims=True) + 1e-06)
    normed = values * inverse
    gain_grad = jnp.sum(grad * normed, axis=0, keepdims=True)
    grad = grad * gain
    along = jnp.mean(grad * normed, axis=-1, keepdims=True)
    return inverse * (grad - normed * along), gain_grad


def turned(values, cosine_tab, sine_tab):
    return values * cosine_tab + pltpu.roll(values, HD // 2, 1) * sine_tab


def attend_kernel(at, tokens, gain, cosine, sine, *refs):
    first_ref, query_ref, key_ref, value_ref, out_ref = refs[8:13]
    prob_out, weight_out, prob_ref, weight, sems = refs[13:]
    place_pieces(at, refs[:8], weight)
    copies = [pltpu.make_async_copy(weight, weight_out, sems.at[HK])]
    copies[0].start()
    length = tokens.shape[0]
    first_in = rms_kernel(tokens[...].astype(jnp.float32), gain[...])
    first_ref[...] = first_in
    rows = lax.broadcasted_iota(jnp.int32, (length, length), 0)
    cols = lax.broadcasted_iota(jnp.int32, (length, length), 1)
    allowed = (cols <= rows) | (cols < at[4])
    cosine_tab, sine_tab = cosine[...], sine[...]
    group_size = HQ // HK
    for group in range(HK):
        matrix = weight[group].reshape(first_in.shape[1], -1)
        qkv = dot(first_in, matrix)
        at_key = group_size * HD
        key = turned(qkv[:, at_key : at_key + HD], cosine_tab, sine_tab).astype(jnp.bfloat16)
        value = qkv[:, at_key + HD :].astype(jnp.bfloat16)
        key_ref[:, group * HD : (group + 1) * HD] = key
        value_ref[:, group * HD : (group + 1) * HD] = value
        for member in range(group_size):
            head = group * group_size + member
            here = slice(head * HD, (head + 1) * HD)
            query = turned(qkv[:, member * HD : (member + 1) * HD], cosine_tab, sine_tab)
            query = query.astype(jnp.bfloat16)
            query_ref[:, here] = query
            scores = dot(query, key, ((1,), (1,)))
            scores = jnp.where(allowed, scores * HD ** (-0.5), -1e30)
            weights = jnp.exp(scores - jnp.max(scores, axis=-1, keepdims=True))
            prob = weights * (1.0 / jnp.sum(weights, axis=-1, keepdims=True))
            prob = prob.astype(jnp.bfloat16)
            prob_ref[head] = prob
            out_ref[:, here] = dot(prob, value).astype(jnp.bfloat16)
        here = pl.ds(group * group_size, group_size)
        copies.append(
            pltpu.make_async_copy(prob_ref.at[here], prob_out.at[here], sems.at[group])
        )
        copies[-1].start()
    for copy in copies:
        copy.wait()


def project_kernel(at, tokens, gain, attended, *refs):
    resid_ref, second_ref, weight_out, weight, sem = refs[8:]
    place_pieces(at, refs[:8], weight)
    copy = pltpu.make_async_copy(weight, weight_out, sem)
    copy.start()
    heads = attended[...]
    halves = [dot(heads, weight[half].reshape(heads.shape[1], -1)) for half in range(2)]
    resid = tokens[...].astype(jnp.float32) + jnp.concatenate(halves, axis=1)
    resid_ref[...] = resid
    second_ref[...] = rms_kernel(resid, gain[...])
    copy.wait()


def one_hot(slots, capacity, dtype):
    shape = (capacity, slots.shape[1])
    return (slots == lax.broadcasted_iota(jnp.int32, shape, 0)).astype(jnp.float32).astype(dtype)


def slots_of(ids, expert, start, rows):
    named = jnp.any(ids[:, start : start + rows] == expert, axis=0, keepdims=True)
    named = named.astype(jnp.float32)
    before = lax.broadcasted_iota(jnp.int32, (rows, rows), 0)
    upto = lax.broadcasted_iota(jnp.int32, (rows, rows), 1)
    counts = dot(named.astype(jnp.bfloat16), (before <= upto).astype(jnp.float32).astype(jnp.bfloat16))
    return jnp.where(named > 0.0, counts - 1.0, -1.0).astype(jnp.int32)


def spread(picks, capacity, rows, outs):
    rows = rows.astype(jnp.bfloat16)
    block = picks[0].shape[1]
    for n in range(len(picks) // 2):
        for part in range(2):
            pick = picks[2 * n + part]
            at_row = (2 * n + part) * capacity
            tokens = dot(pick, rows[at_row : at_row + capacity], ((0,), (0,)))
            outs[n][part * block : (part + 1) * block] = tokens.astype(jnp.bfloat16)


def expert_kernel(capacity, pieces, earlier, at, ids, router, *refs):
    count = len(pieces)
    second, cot = refs[:count], refs[count : 2 * count]
    gate_w, up_w, down_w = refs[2 * count : 2 * count + 3]
    before = refs[2 * count + 3 : 2 * count + 3 + 2 * earlier]
    refs = refs[2 * count + 3 + 2 * earlier :]
    rows_in, rows_cot, gated_ref, gate_back, up_back, gates_ref = refs[:6]
    backs, gate_rows = refs[6 : 6 + count], refs[-1]
    f32, bf16 = jnp.float32, jnp.bfloat16
    length, width = second[0].shape
    wide = router.shape[1]
    half = length // 2
    picks = []
    experts = lax.broadcasted_iota(jnp.int32, (wide, length), 0)
    for n, piece in enumerate(pieces):
        tokens = second[n][...]
        named = ids[:, piece * length : (piece + 1) * length]
        chosen = functools.reduce(
            jnp.logical_or, [named[k : k + 1] == experts for k in range(named.shape[0])]
        )
        logits = jnp.where(chosen, dot(router[...], tokens, ((0,), (1,))), -1e30)
        weights = jnp.exp(logits - jnp.max(logits, axis=0, keepdims=True))
        gates = weights * (1.0 / jnp.sum(weights, axis=0, keepdims=True))
        if n == 0:
            gates_ref[...] = gates
        own = jnp.sum(jnp.where(experts == at[5], gates, 0.0), axis=0, keepdims=True)
        for part in range(2):
            here = slice(part * half, (part + 1) * half)
            place = slice((2 * n + part) * capacity, (2 * n + part + 1) * capacity)
            slots = slots_of(ids, at[5], piece * length + part * half, half)
            pick = one_hot(slots, capacity, f32)
            picks.append(pick.astype(bf16))
            rows_in[place] = dot(picks[-1], tokens[here]).astype(bf16)
            rows_cot[place] = dot(picks[-1], cot[n][here]).astype(bf16)
            gate_rows[place] = jnp.sum(pick * own[:, here], axis=1, keepdims=True)
    gate = gate_rows[...]
    gate_pre = dot(rows_in[...], gate_w[...])
    up_pre = dot(rows_in[...], up_w[...])
    cot_hidden = dot(rows_cot[...], down_w[...], ((1,), (1,)))
    scale = math.sqrt(2.0 / math.pi)
    square = gate_pre * gate_pre
    bent = jnp.tanh(scale * gate_pre * (1.0 + 0.044715 * square))
    open_part = 0.5 * (1.0 + bent)
    active = gate_pre * open_part
    slope = open_part + 0.5 * gate_pre * (1.0 - bent * bent) * scale * (
        1.0 + 3 * 0.044715 * square
    )
    hidden = active * up_pre
    gated_ref[...] = (gate * hidden).astype(bf16)
    signal = jnp.sum(hidden * cot_hidden, axis=1, keepdims=True)
    back = gate * cot_hidden
    gate_back[...] = (back * up_pre * slope).astype(bf16)
    up_back[...] = (back * active).astype(bf16)
    high = signal.astype(bf16)
    low = (signal - high.astype(f32)).astype(bf16)
    lanes = lax.broadcasted_iota(jnp.int32, (signal.shape[0], wide), 1)
    signal = jnp.where(lanes == at[5], high.astype(f32), 0.0)
    signal = jnp.where(lanes == at[5] + wide // 2, low.astype(f32), signal)
    by_rows = ((1,), (1,))
    rows = dot(gate_back[...], gate_w[...], by_rows) + dot(up_back[...], up_w[...], by_rows)
    spread(picks, capacity, jnp.concatenate([rows, signal], axis=1), backs)
    if earlier:
        lefts = [ref[...] for ref in (*before[:earlier], rows_cot)]
        rights = [ref[...] for ref in (*before[earlier:], gated_ref)]
        total = dot(jnp.concatenate(lefts, axis=0), jnp.concatenate(rights, axis=0), ((0,), (0,)))
        refs[6 + count][...] = total.astype(bf16)


def run_expert(pieces, at, ids, router, weights, second, cot, capacity, before=()):
    count = len(pieces)
    rows, wide = 2 * count * capacity, router.shape[1]
    (length, width), hidden = second[0].shape, weights[0].shape[1]
    bf16, f32 = jnp.bfloat16, jnp.float32
    outs = [(rows, width)] * 2 + [(rows, hidden)] * 3
    outs = [(shape, bf16) for shape in outs] + [((wide, length), f32)]
    outs = outs + [((length, width + wide), bf16)] * count
    if before:
        outs = outs + [((width, hidden), bf16)]
    return run_kernel(
        functools.partial(expert_kernel, capacity, pieces, len(before) // 2),
        4 * count,
        at,
        (ids, router, *second, *cot, *weights, *before),
        outs,
        6 + 4 * count + 5 * len(before) // 2,
        [pltpu.VMEM((rows, 1), f32)],
    )


def mixture_kernel(capacity, groups, at, ids, *refs):
    gated, down_w, outs = refs[: len(groups)], refs[len(groups)], refs[len(groups) + 1 :]
    length = outs[0].shape[0]
    for pieces, rows in zip(groups, gated):
        picks = []
        for piece in pieces:
            for part in range(2):
                start = piece * length + part * length // 2
                slots = slots_of(ids, at[5], start, length // 2)
                picks.append(one_hot(slots, capacity, jnp.bfloat16))
        spread(picks, capacity, dot(rows[...], down_w[...]), [outs[piece] for piece in pieces])


def row_sum_kernel(parts, at, *refs):
    arrays = [
        jnp.concatenate([ref[...] for ref in refs[n : n + parts]], axis=0)
        for n in range(0, len(refs) - len(refs) // (parts + 1), parts)
    ]
    outs = refs[len(arrays) * parts :]
    for out, right in zip(outs, arrays[1:]):
        out[...] = dot(arrays[0], right, ((0,), (0,))).astype(jnp.bfloat16)


def row_sums(at, left, *rights):
    operands = [part for parts in (left, *rights) for part in parts]
    outs = [((left[0].shape[1], right[0].shape[1]), jnp.bfloat16) for right in rights]
    kernel = functools.partial(row_sum_kernel, len(left))
    return run_kernel(kernel, 4 * len(rights), at, operands, outs, 24 if len(rights) == 1 else 56)


def branch_back_kernel(
    at, near, far, first_x, first_y, last_y, last_x, resid, gain, second, gates, router, cot, weight, *outs
):
    resid_grad_ref, branch_ref, attended_ref, router_ref, gain_ref = outs
    f32, bf16 = jnp.float32, jnp.bfloat16
    halves = [first_x[...].astype(f32) + last_y[...], first_y[...].astype(f32) + last_x[...]]
    total = near[...].astype(f32) + far[...] + jnp.concatenate(halves, axis=0)
    width = resid.shape[1]
    signal = total[:, width:]
    signal = signal + pltpu.roll(signal, signal.shape[1] // 2, 1)
    chosen = gates[...].T
    logit_grad = chosen * (signal - jnp.sum(chosen * signal, axis=-1, keepdims=True))
    logit_grad = logit_grad.astype(bf16)
    second_grad = total[:, :width] + dot(logit_grad, router[...], ((1,), (1,)))
    norm_grad, gain_grad = rms_back(resid[...], gain[...], second_grad)
    gain_ref[...] = gain_grad
    resid_grad = cot[...].astype(f32) + norm_grad
    resid_grad_ref[...] = resid_grad
    branch = resid_grad.astype(bf16)
    branch_ref[...] = branch
    wide = weight.shape[2]
    attended_ref[...] = (
        dot(branch[:, :wide], weight[0], ((1,), (1,)))
        + dot(branch[:, wide:], weight[1], ((1,), (1,)))
    ).astype(bf16)
    router_ref[...] = dot(second[...], logit_grad, ((0,), (0,)))


def attend_back_kernel(
    at, attended, probs, queries, keys, values, cosine, sine, branch, back_ref
):
    f32, bf16 = jnp.float32, jnp.bfloat16
    cosine_tab, sine_tab = cosine[...], -sine[...]
    group_size = HQ // HK
    places, length = back_ref.shape[0], branch.shape[0]
    branch_width = branch.shape[1] // places
    width = back_ref.shape[2] - branch_width
    for place in range(places):
        here = slice(place * branch_width, (place + 1) * branch_width)
        back_ref[place, :length, width:] = branch[:, here]
        back_ref[place, length:] = jnp.zeros((back_ref.shape[1] - length, back_ref.shape[2]), bf16)
    scale = HD ** (-0.5)

    def put(position, block):
        back_ref[position // width, :length, position % width : position % width + HD] = block

    for group in range(HK):
        own = slice(group * HD, (group + 1) * HD)
        key, value = keys[:, own], values[:, own]
        key_grad = value_grad = 0.0
        start = group * (group_size + 2) * HD
        for member in range(group_size):
            head = group * group_size + member
            here = slice(head * HD, (head + 1) * HD)
            out_grad, query, prob = attended[:, here], queries[:, here], probs[head]
            prob_grad = dot(out_grad, value, ((1,), (1,)))
            prob_f = prob.astype(f32)
            inner = jnp.sum(prob_f * prob_grad, axis=-1, keepdims=True)
            score_grad = (prob_f * (prob_grad - inner)).astype(bf16)
            query_grad = turned(dot(score_grad, key) * scale, cosine_tab, sine_tab)
            put(start + member * HD, query_grad.astype(bf16))
            key_grad = key_grad + dot(score_grad, query, ((0,), (0,)))
            value_grad = value_grad + dot(prob, out_grad, ((0,), (0,)))
        key_grad = turned(key_grad * scale, cosine_tab, sine_tab)
        put(start + group_size * HD, key_grad.astype(bf16))
        put(start + (group_size + 1) * HD, value_grad.astype(bf16))


def first_back_kernel(at, back, weight, tokens, gain, resid_grad, tokens_ref, gain_ref):
    f32 = jnp.float32
    parts = back.shape[0]
    cols = weight.shape[0] * weight.shape[2] // parts
    first_grad = 0.0
    for part in range(parts):
        group, place = divmod(part * cols, weight.shape[2])
        first_grad = first_grad + dot(
            back[part, : tokens.shape[0], :cols], weight[group, :, place : place + cols], ((1,), (1,))
        )
    norm_grad, gain_grad = rms_back(tokens[...].astype(f32), gain[...], first_grad)
    gain_ref[...] = gain_grad
    tokens_ref[...] = (resid_grad[...] + norm_grad).astype(jnp.bfloat16)


def dense_grad_kernel(at, back, *refs):
    pieces, out_ref, held, sems = refs[:8], refs[8], refs[9], refs[10]
    copies = [
        pltpu.make_async_copy(piece, held.at[n], sems.at[n]) for n, piece in enumerate(pieces)
    ]
    for copy in copies:
        copy.start()
    depth, rows, cols = out_ref.shape
    length = held.shape[1] // 2
    qkv_width = cols - held.shape[2] // back.shape[0]
    narrow = sum(back[place, length:].astype(jnp.float32) for place in range(back.shape[0]))
    sums = [0.0, 0.0]
    for n, copy in enumerate(copies):
        copy.wait()
        dc, dy, dx = n // 4, n // 2 % 2, n % 2
        place = 4 * (at[0] ^ dy) + 2 * (at[1] ^ dc) + (at[2] ^ dx)
        own = back[place, :length]
        sums[0] = sums[0] + dot(held[n, length:], own[:, :qkv_width], ((0,), (0,)))
        sums[1] = sums[1] + dot(held[n, :length], own[:, qkv_width:], ((0,), (0,)))
    wide = held.shape[2] // depth
    each = 4
    for z in range(depth):
        here = slice(z * wide, (z + 1) * wide)
        both = jnp.concatenate([part[here] for part in sums], axis=1)
        out_ref[z, :wide] = both.astype(jnp.bfloat16)
        kept = [narrow[z * each : (z + 1) * each], jnp.zeros((rows - wide - each, cols), jnp.float32)]
        out_ref[z, wide:] = jnp.concatenate(kept, axis=0).astype(jnp.bfloat16)


def finish_kernel(at, sums, query_ref, key_ref, value_ref, output_ref):
    places, _, cols = sums.shape
    rows, out_width = query_ref.shape[0], output_ref.shape[1] // places
    width = cols - out_width
    for place in range(places):
        block = sums[place, :rows].astype(jnp.float32)
        output_ref[:, place * out_width : (place + 1) * out_width] = block[:, width:]
        for at_col in range(0, width, HD):
            group, head = divmod((place * width + at_col) // HD, HQ // HK + 2)
            part = block[:, at_col : at_col + HD]
            if head < HQ // HK:
                start = (group * (HQ // HK) + head) * HD
                query_ref[:, start : start + HD] = part
            elif head == HQ // HK:
                key_ref[:, group * HD : (group + 1) * HD] = part
            else:
                value_ref[:, group * HD : (group + 1) * HD] = part


def local_pairs(
    tokens,
    norm1_gain,
    w_query,
    w_key,
    w_value,
    w_out,
    norm2_gain,
    w_router,
    w_gate,
    w_up,
    w_down,
    expert_ids,
    prefix_len,
    out_grad,
):
    bf16, f32 = jnp.bfloat16, jnp.float32
    length, model_width = tokens.shape
    shard_rows = w_query.shape[0]
    local_count, _, hidden_width = w_gate.shape
    owners = lax.axis_size("x")
    depth = lax.axis_size("z")
    plane = lax.axis_size(PLANE)
    experts_all = w_router.shape[1]
    block_rows = length // MICRO
    capacity = 3 * block_rows * expert_ids.shape[1] // (2 * experts_all)
    plane_rows = plane * length
    blocks = plane_rows // block_rows
    q_cols, kv_cols = w_query.shape[1], w_key.shape[1]
    qkv_cols = q_cols + 2 * kv_cols
    q_group, out_half = q_cols // HK, model_width // 2
    y, c, x, z = (lax.axis_index(axis) for axis in ("y", "c", "x", "z"))
    own_local = 2 * y + c
    own_expert = x * local_count + own_local
    at = jnp.stack([y, c, x, z, prefix_len[0], own_expert, own_local])

    own_half = jnp.concatenate(
        [
            lax.dynamic_slice_in_dim(part, x * (part.shape[1] // 2), part.shape[1] // 2, 1)
            for part in (w_query, w_key, w_value, w_out)
        ],
        axis=1,
    )
    narrow = jnp.concatenate([w_router, norm1_gain[:, None], norm2_gain[:, None]], axis=1)
    narrow = jnp.pad(narrow, ((0, 0), (0, 128 - narrow.shape[1])))
    router_w = small_group_gather(narrow)
    ids_all = small_gather(expert_ids.T)
    column = [own_half] + shifts(own_half)
    cot_sides = plane_sides(after(out_grad, router_w, ids_all))
    qkv_half = qkv_cols // 2
    qkv_column = jnp.stack([part[:, :qkv_half] for part in column])
    out_column = jnp.stack([part[:, qkv_half:] for part in column])
    qkv_column, out_column = lax.optimization_barrier((qkv_column, out_column, *cot_sides))[:2]
    sliced = after(own_local, column[-1])
    gate_w, up_w, down_w = (
        lax.dynamic_index_in_dim(weight, sliced, 0, keepdims=False)
        for weight in (w_gate, w_up, w_down)
    )
    qkv_sides = plane_sides(qkv_column)
    gains = router_w[:, experts_all : experts_all + 2].T.astype(f32)
    gain_one, gain_two = gains[:1], gains[1:]
    qkv_corner = plane_corner(qkv_sides, (gate_w, up_w, down_w, gain_one, gain_two))
    out_sides = plane_sides(after(out_column, *qkv_sides))
    qkv_pieces = plane_pieces(qkv_column, qkv_sides, qkv_corner)
    cosine_tab, sine_tab = angles(length, HD)
    cosine_all = jnp.concatenate([cosine_tab, cosine_tab], axis=2)[:, 0]
    sine_all = jnp.concatenate([-sine_tab, sine_tab], axis=2)[:, 0]
    weight_lead = (2, depth, 2, 2, shard_rows)
    first_in, queries, keys_rot, values_b, attended, probs, qkv_w = run_kernel(
        attend_kernel,
        11,
        at,
        (tokens, gain_one, cosine_all, sine_all, *qkv_pieces),
        [
            ((length, model_width), bf16),
            ((length, q_cols), bf16),
            ((length, kv_cols), bf16),
            ((length, kv_cols), bf16),
            ((length, q_cols), bf16),
            ((HQ, length, length), bf16),
            (weight_lead + (qkv_half,), bf16),
        ],
        28,
        [
            pltpu.VMEM((HQ, length, length), bf16),
            pltpu.VMEM(weight_lead + (qkv_half,), bf16),
            pltpu.SemaphoreType.DMA((HK + 1,)),
        ],
        hbm_out=2,
    )
    out_sides = lax.optimization_barrier((*out_sides, attended))[:2]
    out_corner = plane_corner(out_sides)
    cot_corner = plane_corner(cot_sides)
    out_pieces = plane_pieces(out_column, out_sides, out_corner)
    cot_pieces = plane_pieces(out_grad, cot_sides, cot_corner)
    resid, second_in, output_w = run_kernel(
        project_kernel,
        4,
        at,
        (tokens, after(gain_two, cot_corner), attended, *out_pieces),
        [
            ((length, model_width), f32),
            ((length, model_width), bf16),
            (weight_lead + (out_half,), bf16),
        ],
        44,
        [pltpu.VMEM(weight_lead + (out_half,), bf16), pltpu.SemaphoreType.DMA],
        hbm_out=1,
    )
    qkv_w = qkv_w.reshape(HK, model_width, qkv_half)
    output_w = output_w.reshape(2, q_cols, out_half)

    expert = functools.partial(
        run_expert,
        at=at,
        ids=ids_all,
        router=router_w,
        weights=(gate_w, up_w, down_w),
        capacity=capacity,
    )
    second_sides = plane_sides(second_in)
    groups = ((0, 4), (1, 5, 2, 6), (3, 7))
    second_pieces = {0: second_in, 4: swap(second_in, "c")}

    def run_group(pieces, before=()):
        return expert(
            pieces,
            before=before,
            second=[second_pieces[piece] for piece in pieces],
            cot=[cot_pieces[piece] for piece in pieces],
        )

    stage_own = run_group(groups[0])
    second_sides = lax.optimization_barrier((*second_sides, stage_own[0]))[:2]
    for piece, block in zip((1, 2), second_sides):
        second_pieces[piece], second_pieces[piece + 4] = block, swap(block, "c")
    stage_sides = run_group(groups[1])
    second_corner = plane_corner(second_sides, later=(stage_sides[0],))
    second_pieces[3], second_pieces[7] = second_corner, swap(second_corner, "c")
    own_near, own_far = stage_own[6:]
    own_far = swap(own_far, "c")
    x_near, x_far, y_near, y_far = stage_sides[6:]
    back_x, back_y = over_core(x_near, x_far), over_core(y_near, y_far)
    first_x, first_y = early_sums(back_x, back_y)
    two = (stage_own, stage_sides)
    stage_corner = run_group(groups[2], [stage[1] for stage in two] + [stage[2] for stage in two])
    *stage_corner, down_part = stage_corner
    corner = over_core(*stage_corner[6:])
    passed = corner_first(corner)
    stages = (stage_own, stage_sides, stage_corner)
    rows_in, rows_cot, gated, gate_back, up_back = ([stage[n] for stage in stages] for n in range(5))
    gates = stage_own[5]
    last_y, last_x, *sent = corner_last(back_x, back_y, passed)
    down_sum = scatter_sum(down_part, "z")
    gate_part, up_part = row_sums(
        at, [after(rows_in[0], *sent, own_far)] + rows_in[1:], gate_back, up_back
    )
    gate_sum, up_sum = scatter_sum(gate_part, "z"), scatter_sum(up_part, "z")
    own_near = after(own_near, gate_part)

    resid_grad, branch_grad, attended_grad, router_acc, gain_two_grad = run_kernel(
        branch_back_kernel,
        6,
        at,
        (
            own_near,
            own_far,
            first_x,
            first_y,
            last_y,
            last_x,
            resid,
            gain_two,
            second_in,
            gates,
            router_w,
            out_grad,
            output_w,
        ),
        [
            ((length, model_width), f32),
            ((length, model_width), bf16),
            ((length, q_cols), bf16),
            ((model_width, 128), f32),
            ((1, model_width), f32),
        ],
        56,
    )
    qkv_width, branch_width = qkv_cols // plane, model_width // plane
    dense_cols = qkv_width + branch_width
    (back_cols,) = run_kernel(
        attend_back_kernel,
        6,
        at,
        (
            attended_grad,
            probs,
            queries,
            keys_rot,
            values_b,
            cosine_all,
            sine_all,
            branch_grad,
        ),
        [((plane, length + 16, dense_cols), bf16)],
        56,
    )
    tokens_grad, gain_one_grad = run_kernel(
        first_back_kernel,
        5,
        at,
        (back_cols, qkv_w, tokens, gain_one, resid_grad),
        [((length, model_width), bf16), ((1, model_width), f32)],
        24,
    )

    both = jnp.concatenate(
        lax.optimization_barrier((attended, first_in, last_y, last_x))[:2], axis=0
    )
    both_sides = plane_sides(both)
    narrow_part = jnp.concatenate(
        [router_acc[:, :experts_all], gain_one_grad.T, gain_two_grad.T], axis=1
    )
    narrow_cols = -(-narrow_part.shape[1] // owners) * owners
    narrow_part = jnp.pad(narrow_part, ((0, 0), (0, narrow_cols - narrow_part.shape[1])))
    narrow_part = jnp.transpose(
        narrow_part.reshape(depth, 2, 2, shard_rows, owners, narrow_cols // owners),
        (1, 2, 4, 0, 3, 5),
    ).reshape(plane, depth, shard_rows * narrow_cols // owners)
    narrow_len = narrow_part.shape[2]
    narrow_rows = -(-narrow_len // dense_cols)
    each_rows = -(-narrow_rows // 4) * 4
    narrow_part = jnp.pad(
        narrow_part, ((0, 0), (0, 0), (0, each_rows * dense_cols - narrow_len))
    ).reshape(plane, depth * each_rows, dense_cols)
    narrow_part = jnp.pad(
        narrow_part.astype(bf16), ((0, 0), (0, 16 - depth * each_rows), (0, 0))
    )
    back_cols = lax.dynamic_update_slice(back_cols, narrow_part, (0, length, 0))
    back_cols = exchange(after(back_cols, down_sum, *both_sides), PLANE)
    shares = run_kernel(
        functools.partial(mixture_kernel, capacity, groups),
        10,
        at,
        (ids_all, after(gated[0], *both_sides), *gated[1:], down_w),
        [((length, model_width), bf16)] * plane,
        56,
    )
    sides, shares = lax.optimization_barrier((both_sides, shares))
    both_corner = plane_corner(sides, (back_cols,))
    both_pieces = plane_pieces(both, both_sides, both_corner)
    def placed(total):
        total = exchange(total, ("y", "c"))
        return total.reshape(local_count, shard_rows, hidden_width).astype(f32)

    down_grad, gate_grad = placed(down_sum), placed(gate_sum)
    back_cols, down_grad = lax.optimization_barrier((back_cols, down_grad))
    kept_rows = -(-narrow_rows // 16) * 16
    wide_rows = local_count * shard_rows
    dense_shape = (depth, wide_rows + kept_rows, dense_cols)
    dense_part = pl.pallas_call(
        dense_grad_kernel,
        out_shape=jax.ShapeDtypeStruct(dense_shape, bf16),
        in_specs=[SCALARS, WHOLE] + [IN_HBM] * 8,
        out_specs=WHOLE,
        scratch_shapes=[
            pltpu.VMEM((plane, 2 * length, model_width), bf16),
            pltpu.SemaphoreType.DMA((plane,)),
        ],
        cost_estimate=cost(8),
        compiler_params=pltpu.CompilerParams(vmem_limit_bytes=32 * 2**20),
    )(at, back_cols, *both_pieces)
    dense_part, gate_grad, up_sum = lax.optimization_barrier((dense_part, gate_grad, up_sum))
    dense_sum = scatter_sum(dense_part.reshape(-1, dense_cols), "z")
    mixed = [over_core(near, far) for near, far in zip(shares[:4], shares[4:])]
    early = early_sums(mixed[1], mixed[2])
    last = corner_last(mixed[1], mixed[2], corner_first(mixed[3]))[:2]
    mixture = jnp.concatenate(
        [left.astype(f32) + right.astype(f32) for left, right in zip(early, last)], axis=0
    )
    block_out = (resid + (mixture + mixed[0].astype(f32))).astype(bf16)

    dense_sum, up_grad, block_out = lax.optimization_barrier(
        (dense_sum, placed(up_sum), block_out)
    )
    wide_sum = dense_sum[: local_count * shard_rows].reshape(2, 2, 1, shard_rows, dense_cols)
    wide_sum = jnp.broadcast_to(wide_sum, (2, 2, owners, shard_rows, dense_cols)).reshape(
        plane, shard_rows, dense_cols
    )
    narrow_sum = dense_sum[local_count * shard_rows :][:narrow_rows]
    narrow_sum = jnp.broadcast_to(narrow_sum[None], (plane, narrow_rows, dense_cols))
    pad_rows = -(shard_rows + narrow_rows) % 16
    padding = jnp.zeros((plane, pad_rows, dense_cols), bf16)
    dense_sum = exchange(jnp.concatenate([wide_sum, narrow_sum, padding], axis=1), PLANE)
    query_grad, key_grad, value_grad, output_grad = run_kernel(
        finish_kernel,
        2,
        at,
        (dense_sum,),
        [
            ((shard_rows, q_cols), f32),
            ((shard_rows, kv_cols), f32),
            ((shard_rows, kv_cols), f32),
            ((shard_rows, model_width), f32),
        ],
    )
    narrow_sum = dense_sum[:, shard_rows : shard_rows + narrow_rows].reshape(
        2, 2, owners, narrow_rows * dense_cols
    )
    narrow_sum = narrow_sum[y, c, :, :narrow_len].reshape(owners, shard_rows, -1)
    narrow_sum = jnp.moveaxis(narrow_sum, 0, 1).reshape(shard_rows, narrow_cols).astype(f32)

    return (
        block_out,
        tokens_grad,
        narrow_sum[:, experts_all],
        query_grad,
        key_grad,
        value_grad,
        output_grad,
        narrow_sum[:, experts_all + 1],
        narrow_sum[:, :experts_all],
        gate_grad,
        up_grad,
        jnp.swapaxes(down_grad, 1, 2),
    )


def solution(mesh):
    groups, owners = mesh.shape["dp"], mesh.shape["expert"]
    grid = jax.sharding.Mesh(
        mesh.devices.reshape(groups // 4, 2, 2, owners), ("z", "y", "c", "x")
    )
    rows = P(("z", "y", "c", "x"), None)
    shard, shard_rows = P(GROUP), P(GROUP, None)
    expert = P("x", None, None)
    return jax.shard_map(
        local_pairs if owners == 2 else local_wide,
        mesh=grid,
        in_specs=(
            rows,
            shard,
            shard_rows,
            shard_rows,
            shard_rows,
            shard_rows,
            shard,
            shard_rows,
            expert,
            expert,
            expert,
            rows,
            P(("z", "y", "c", "x")),
            rows,
        ),
        out_specs=(
            rows,
            rows,
            shard,
            shard_rows,
            shard_rows,
            shard_rows,
            shard_rows,
            shard,
            shard_rows,
            P("x", GROUP, None),
            P("x", GROUP, None),
            P("x", None, GROUP),
        ),
        check_vma=False,
    )
```

```python
import functools
import math

import jax
import jax.numpy as jnp
from jax import lax
from jax.experimental import pallas as pl
from jax.experimental.pallas import tpu as pltpu
from jax.sharding import PartitionSpec as P

HQ = 12
HK = 2
HD = 128
MICRO = 2
PLANE = ("y", "c", "x")
GROUP = ("z", "y", "c")


def rms_scale(values, gain_vec):
    inverse = lax.rsqrt(jnp.mean(values * values, axis=-1, keepdims=True) + 1e-06)
    return values * inverse * gain_vec


def angles(length, head_size):
    positions = jnp.arange(length).astype(jnp.float32)
    freq_rates = jnp.exp(
        -(2.0 * jnp.arange(head_size // 2).astype(jnp.float32) / head_size) * math.log(1000000.0)
    )
    angle_tab = positions[:, None] * freq_rates[None, :]
    return (jnp.cos(angle_tab)[:, None, :], jnp.sin(angle_tab)[:, None, :])


def rotary(values, cosine_tab, sine_tab):
    half_dim = values.shape[-1] // 2
    first_half = values[..., :half_dim]
    second_half = values[..., half_dim:]
    return jnp.concatenate(
        [
            first_half * cosine_tab - second_half * sine_tab,
            second_half * cosine_tab + first_half * sine_tab,
        ],
        axis=-1,
    )


def expert_act(gate_pre, up_pre):
    return jax.nn.gelu(gate_pre, approximate=True) * up_pre


def left_product(left_mat, right_mat):
    return lax.dot_general(
        left_mat, right_mat, (((0,), (0,)), ((), ())), preferred_element_type=jnp.float32
    )


def gather(block, axes):
    return lax.all_gather(block, axes, axis=0, tiled=True)


def exchange(block, axes):
    return lax.all_to_all(block, axes, split_axis=0, concat_axis=0, tiled=True)


def scatter_sum(block, axes):
    return lax.psum_scatter(block, axes, scatter_dimension=0, tiled=True)


def by_owner(cols, parts):
    rows, total = cols.shape
    return jnp.moveaxis(cols.reshape(rows, parts, total // parts), 1, 0).reshape(
        parts * rows, total // parts
    )


def local_wide(
    tokens,
    norm1_gain,
    w_query,
    w_key,
    w_value,
    w_out,
    norm2_gain,
    w_router,
    w_gate,
    w_up,
    w_down,
    expert_ids,
    prefix_len,
    out_grad,
):
    bf16, f32 = jnp.bfloat16, jnp.float32
    length, model_width = tokens.shape
    shard_rows = w_query.shape[0]
    local_count, _, hidden_width = w_gate.shape
    owners = lax.axis_size("x")
    depth = lax.axis_size("z")
    plane = lax.axis_size(PLANE)
    experts_all = w_router.shape[1]
    top_count = expert_ids.shape[1]
    block_rows = length // MICRO
    capacity = 3 * block_rows * top_count // (2 * experts_all)
    plane_rows = plane * length
    blocks = plane_rows // block_rows
    group_size = HQ // HK
    score_scale = HD ** (-0.5)
    q_cols, kv_cols = w_query.shape[1], w_key.shape[1]
    own_local = lax.axis_index(("y", "c"))
    own_expert = lax.axis_index("x") * local_count + own_local
    own_place = lax.axis_index(PLANE)

    narrow = jnp.concatenate([w_router, norm1_gain[:, None], norm2_gain[:, None]], axis=1)
    narrow = jnp.pad(narrow, ((0, 0), (0, -narrow.shape[1] % 128)))
    packed = gather(jnp.concatenate([w_query, w_key, w_value, narrow], axis=1), GROUP)
    qkv_cols = q_cols + 2 * kv_cols
    qkv_w = packed[:, :qkv_cols]
    router_w = packed[:, qkv_cols : qkv_cols + experts_all]
    gains = packed[:, qkv_cols + experts_all : qkv_cols + experts_all + 2].T.astype(f32)
    gain_one, gain_two = gains[0], gains[1]
    output_w = gather(w_out, GROUP)

    ids_all = gather(expert_ids, PLANE)
    cot_all = gather(out_grad, PLANE)
    chosen_mask = jnp.any(
        ids_all[:, :, None] == jnp.arange(experts_all, dtype=jnp.int32)[None, None, :], axis=1
    )
    own_mask = jnp.any(ids_all == own_expert, axis=1).reshape(blocks, block_rows)
    place = jnp.cumsum(own_mask.astype(jnp.int32), axis=1) - 1
    dispatch = (
        own_mask[:, None, :]
        & (place[:, None, :] == jnp.arange(capacity, dtype=jnp.int32)[None, :, None])
    ).astype(bf16)

    cosine_tab, sine_tab = angles(length, HD)
    inputs_f = tokens.astype(f32)
    first_in = rms_scale(inputs_f, gain_one).astype(bf16)
    qkv = jnp.dot(first_in, qkv_w, preferred_element_type=f32)
    queries = (
        rotary(qkv[:, :q_cols].reshape(length, HQ, HD), cosine_tab, sine_tab)
        .astype(bf16)
        .reshape(length, HK, group_size, HD)
    )
    keys_rot = rotary(
        qkv[:, q_cols : q_cols + kv_cols].reshape(length, HK, HD), cosine_tab, sine_tab
    ).astype(bf16)
    values_b = qkv[:, q_cols + kv_cols :].astype(bf16).reshape(length, HK, HD)
    positions = jnp.arange(length)
    allowed = (positions[None, :] <= positions[:, None]) | (positions[None, :] < prefix_len[0])

    def masked_scores():
        scores = jnp.einsum("ihrd,jhd->hrij", queries, keys_rot, preferred_element_type=f32)
        return jnp.where(allowed, scores * score_scale, -1e30)

    masked = masked_scores()
    row_peak = jnp.max(masked, axis=-1, keepdims=True)
    log_total = row_peak + jnp.log(jnp.sum(jnp.exp(masked - row_peak), axis=-1, keepdims=True))
    prob_bf = jnp.exp(masked - log_total).astype(bf16)
    attended = jnp.einsum("hrij,jhd->ihrd", prob_bf, values_b, preferred_element_type=f32)
    attended = attended.reshape(length, HQ * HD).astype(bf16)
    resid = inputs_f + jnp.dot(attended, output_w, preferred_element_type=f32)
    second_in = rms_scale(resid, gain_two).astype(bf16)

    second_all = gather(second_in, PLANE)
    logits = jnp.dot(second_all, router_w, preferred_element_type=f32)
    gates_all = jax.nn.softmax(jnp.where(chosen_mask, logits, -jnp.inf), axis=-1)
    own_gates = lax.dynamic_index_in_dim(gates_all, own_expert, 1, keepdims=False)
    own_gates = own_gates.reshape(blocks, block_rows)
    gate_rows = jnp.einsum(
        "bct,bt->bc", dispatch.astype(f32), own_gates, precision=lax.Precision.HIGHEST
    )[:, :, None]
    gate_w = lax.dynamic_index_in_dim(w_gate, own_local, 0, keepdims=False)
    up_w = lax.dynamic_index_in_dim(w_up, own_local, 0, keepdims=False)
    down_w = lax.dynamic_index_in_dim(w_down, own_local, 0, keepdims=False)

    def to_rows(array):
        return jnp.einsum(
            "bct,btd->bcd",
            dispatch,
            array.reshape(blocks, block_rows, model_width),
            preferred_element_type=f32,
        ).astype(bf16)

    def to_tokens(rows):
        return (
            jnp.einsum("bct,bcd->btd", dispatch, rows.astype(bf16), preferred_element_type=f32)
            .astype(bf16)
            .reshape(plane_rows, model_width)
        )

    rows_in = to_rows(second_all)
    rows_cot = to_rows(cot_all)
    gate_pre = jnp.einsum("bcd,df->bcf", rows_in, gate_w, preferred_element_type=f32)
    up_pre = jnp.einsum("bcd,df->bcf", rows_in, up_w, preferred_element_type=f32)
    hidden, act_pull = jax.vjp(expert_act, gate_pre, up_pre)
    gated = (gate_rows * hidden).astype(bf16)
    down_part = jnp.einsum("bcd,bcf->df", rows_cot, gated, preferred_element_type=f32)
    down_sum = scatter_sum(down_part.astype(bf16), "z")
    cot_hidden = jnp.einsum("bcd,fd->bcf", rows_cot, down_w, preferred_element_type=f32)
    gate_signal_rows = jnp.sum(hidden * cot_hidden, axis=-1)
    gate_pgrad, up_pgrad = act_pull(gate_rows * cot_hidden)
    gate_pgrad = gate_pgrad.astype(bf16)
    up_pgrad = up_pgrad.astype(bf16)
    gate_part = jnp.einsum("bcd,bcf->df", rows_in, gate_pgrad, preferred_element_type=f32)
    gate_sum = scatter_sum(gate_part.astype(bf16), "z")
    up_part = jnp.einsum("bcd,bcf->df", rows_in, up_pgrad, preferred_element_type=f32)
    up_sum = scatter_sum(up_part.astype(bf16), "z")
    rows_grad = jnp.einsum("bcf,df->bcd", gate_pgrad, gate_w, preferred_element_type=f32)
    rows_grad = rows_grad + jnp.einsum("bcf,df->bcd", up_pgrad, up_w, preferred_element_type=f32)
    second_back = scatter_sum(to_tokens(rows_grad), PLANE).astype(f32)
    gate_signal = jnp.einsum(
        "bct,bc->bt", dispatch.astype(f32), gate_signal_rows, precision=lax.Precision.HIGHEST
    )
    gate_signal = exchange(gate_signal.reshape(plane, length), PLANE)
    gate_signal = jnp.transpose(
        gate_signal.reshape(local_count, owners, length), (2, 1, 0)
    ).reshape(length, experts_all)
    expert_rows = jnp.einsum("bcf,fd->bcd", gated, down_w, preferred_element_type=f32)
    mixture = scatter_sum(to_tokens(expert_rows), PLANE).astype(f32)
    block_out = (resid + mixture).astype(bf16)

    cotangent = out_grad.astype(f32)
    gate_probs = lax.dynamic_slice_in_dim(gates_all, own_place * length, length, 0)
    logit_grad = (
        gate_probs
        * (gate_signal - jnp.sum(gate_probs * gate_signal, axis=-1, keepdims=True))
    ).astype(bf16)
    router_acc = left_product(second_in, logit_grad)
    second_grad = second_back + jnp.dot(logit_grad, router_w.T, preferred_element_type=f32)
    _, norm_two_pull = jax.vjp(rms_scale, resid, gain_two)
    resid_norm_grad, gain_two_grad = norm_two_pull(second_grad)
    resid_grad = cotangent + resid_norm_grad
    branch_grad = resid_grad.astype(bf16)

    attended_all = gather(attended, PLANE)
    branch_cols = exchange(by_owner(branch_grad, plane), PLANE)
    output_part = left_product(attended_all, branch_cols)
    attended_grad = jnp.dot(branch_grad, output_w.T, preferred_element_type=f32).astype(bf16)
    attended_grad = attended_grad.reshape(length, HK, group_size, HD)
    masked = masked_scores()
    prob_full = jnp.exp(masked - log_total)
    prob_bf = prob_full.astype(bf16)
    prob_grad = jnp.einsum("ihrd,jhd->hrij", attended_grad, values_b, preferred_element_type=f32)
    row_inner = jnp.sum(prob_full * prob_grad, axis=-1, keepdims=True)
    score_grad = (prob_full * (prob_grad - row_inner)).astype(bf16)
    query_rot_grad = (
        jnp.einsum("hrij,jhd->ihrd", score_grad, keys_rot, preferred_element_type=f32)
        * score_scale
    )
    query_back = rotary(query_rot_grad.reshape(length, HQ, HD), cosine_tab, -sine_tab)
    query_back = query_back.astype(bf16).reshape(length, HQ * HD)
    key_rot_grad = (
        jnp.einsum("hrij,ihrd->jhd", score_grad, queries, preferred_element_type=f32)
        * score_scale
    )
    key_back = rotary(key_rot_grad, cosine_tab, -sine_tab).astype(bf16).reshape(length, HK * HD)
    value_back = jnp.einsum("hrij,ihrd->jhd", prob_bf, attended_grad, preferred_element_type=f32)
    value_back = value_back.astype(bf16).reshape(length, HK * HD)
    qkv_back = jnp.concatenate([query_back, key_back, value_back], axis=1)
    first_all = gather(first_in, PLANE)
    qkv_part = left_product(first_all, exchange(by_owner(qkv_back, plane), PLANE))
    first_grad = lax.dot_general(
        qkv_back, qkv_w, (((1,), (1,)), ((), ())), preferred_element_type=f32
    )
    _, norm_one_pull = jax.vjp(rms_scale, inputs_f, gain_one)
    input_norm_grad, gain_one_grad = norm_one_pull(first_grad)
    tokens_grad = (resid_grad + input_norm_grad).astype(bf16)

    narrow_part = jnp.concatenate(
        [router_acc, gain_one_grad[:, None], gain_two_grad[:, None]], axis=1
    ).astype(bf16)
    narrow_cols = narrow_part.shape[1]
    narrow_sum = lax.psum(scatter_sum(narrow_part, GROUP), "x").astype(f32)
    dense_part = jnp.concatenate([qkv_part, output_part], axis=1).astype(bf16)
    dense_sum = scatter_sum(dense_part, "z")
    dense_cols = dense_sum.shape[1]
    dense_sum = gather(dense_sum, PLANE).reshape(plane, local_count, shard_rows, dense_cols)
    dense_sum = lax.dynamic_index_in_dim(dense_sum, own_local, 1, keepdims=False).astype(f32)
    dense_sum = jnp.moveaxis(dense_sum, 0, 1)
    qkv_width = qkv_cols // plane
    qkv_sum = dense_sum[:, :, :qkv_width].reshape(shard_rows, qkv_cols)
    output_sum = dense_sum[:, :, qkv_width:].reshape(shard_rows, model_width)

    def placed(total):
        total = exchange(total, ("y", "c"))
        return total.reshape(local_count, shard_rows, hidden_width).astype(f32)

    return (
        block_out,
        tokens_grad,
        narrow_sum[:, experts_all],
        qkv_sum[:, :q_cols],
        qkv_sum[:, q_cols : q_cols + kv_cols],
        qkv_sum[:, q_cols + kv_cols :],
        output_sum,
        narrow_sum[:, experts_all + 1],
        narrow_sum[:, :experts_all],
        placed(gate_sum),
        placed(up_sum),
        jnp.swapaxes(placed(down_sum), 1, 2),
    )


def rounded(values):
    return lax.reduce_precision(values, 8, 7).astype(jnp.bfloat16)


def after(block, *others):
    return lax.optimization_barrier((block,) + others)[0]


def swap(block, axis):
    return lax.ppermute(block, axis, [(0, 1), (1, 0)])


def shifts(block):
    depth = lax.axis_size("z")
    return [
        lax.ppermute(block, "z", [(i, (i + k) % depth) for i in range(depth)])
        for k in range(1, depth)
    ]


def plane_sides(block):
    return swap(block, "x"), swap(block, "y")


def plane_corner(sides, before=(), later=()):
    over_x, over_y = sides
    half = over_x.shape[0] // 2
    over_y, over_x = lax.optimization_barrier((over_y[:half], over_x[half:]) + before)[:2]
    parts = (swap(over_y, "x"), swap(over_x, "y"))
    return jnp.concatenate(lax.optimization_barrier(parts + later)[:2], axis=0)


def plane_pieces(block, sides=None, corner=None):
    sides = plane_sides(block) if sides is None else sides
    corner = plane_corner(sides) if corner is None else corner
    pieces = [block, *sides, corner]
    return pieces + [swap(piece, "c") for piece in pieces]


def small_gather(block):
    for axis in ("x", "y", "c"):
        block = jnp.concatenate([block, swap(block, axis)], axis=1)
    return block


def small_group_gather(block):
    depth = lax.axis_size("z")
    order = jnp.stack(([block] + shifts(block))[::-1] * 2)
    start = (depth - 1 - lax.axis_index("z")) % depth
    total = lax.dynamic_slice_in_dim(order, start, depth, 0)[:, None, None]
    for dim, axis in ((1, "y"), (2, "c")):
        other = swap(total, axis)
        last = lax.axis_index(axis) == 1
        pair = [jnp.where(last, other, total), jnp.where(last, total, other)]
        total = jnp.concatenate(pair, axis=dim)
    return total.reshape(-1, block.shape[1])


def add(left, right):
    return rounded(left.astype(jnp.float32) + right.astype(jnp.float32))


def over_core(near, far):
    return add(near, swap(far, "c"))


def early_sums(over_x, over_y):
    half = over_x.shape[0] // 2
    return swap(over_x[:half], "x"), swap(over_y[half:], "y")


def corner_first(corner):
    half = corner.shape[0] // 2
    return swap(corner[:half], "x"), swap(corner[half:], "y")


def corner_last(over_x, over_y, first):
    half = over_x.shape[0] // 2
    over_y, over_x = add(over_y[:half], first[0]), add(over_x[half:], first[1])
    return swap(over_y, "y"), swap(over_x, "x"), over_y, over_x


def cost(micros):
    return pl.CostEstimate(flops=micros * 10**9, bytes_accessed=micros * 10**6, transcendentals=0)


def dot(left, right, dims=((1,), (0,)), precision=None):
    return lax.dot_general(
        left, right, (dims, ((), ())), precision=precision, preferred_element_type=jnp.float32
    )


WHOLE = pl.BlockSpec(memory_space=pltpu.VMEM)
IN_HBM = pl.BlockSpec(memory_space=pltpu.HBM)
SCALARS = pl.BlockSpec(memory_space=pltpu.SMEM)


def run_kernel(kernel, micros, at, operands, outs, megabytes=16, scratch=(), hbm_in=0, hbm_out=0):
    return pl.pallas_call(
        kernel,
        out_shape=[jax.ShapeDtypeStruct(shape, dtype) for shape, dtype in outs],
        in_specs=[SCALARS] + [WHOLE] * (len(operands) - hbm_in) + [IN_HBM] * hbm_in,
        out_specs=[WHOLE] * (len(outs) - hbm_out) + [IN_HBM] * hbm_out,
        scratch_shapes=scratch,
        cost_estimate=cost(micros),
        compiler_params=pltpu.CompilerParams(vmem_limit_bytes=megabytes * 2**20),
    )(at, *operands)


def place_pieces(at, refs, weight):
    depth = weight.shape[1]
    for n, ref in enumerate(refs):
        dc, dy, dx = n // 4, n // 2 % 2, n % 2
        for k in range(depth):
            z = lax.rem(at[3] + depth - k, depth)
            weight[at[2] ^ dx, z, at[0] ^ dy, at[1] ^ dc] = ref[k]


def rms_kernel(values, gain):
    inverse = lax.rsqrt(jnp.mean(values * values, axis=-1, keepdims=True) + 1e-06)
    return (values * inverse * gain).astype(jnp.bfloat16)


def rms_back(values, gain, grad):
    inverse = lax.rsqrt(jnp.mean(values * values, axis=-1, keepdims=True) + 1e-06)
    normed = values * inverse
    gain_grad = jnp.sum(grad * normed, axis=0, keepdims=True)
    grad = grad * gain
    along = jnp.mean(grad * normed, axis=-1, keepdims=True)
    return inverse * (grad - normed * along), gain_grad


def turned(values, cosine_tab, sine_tab):
    return values * cosine_tab + pltpu.roll(values, HD // 2, 1) * sine_tab


def attend_kernel(at, tokens, gain, cosine, sine, *refs):
    first_ref, query_ref, key_ref, value_ref, out_ref = refs[8:13]
    prob_out, weight_out, prob_ref, weight, sems = refs[13:]
    place_pieces(at, refs[:8], weight)
    copies = [pltpu.make_async_copy(weight, weight_out, sems.at[HK])]
    copies[0].start()
    length = tokens.shape[0]
    first_in = rms_kernel(tokens[...].astype(jnp.float32), gain[...])
    first_ref[...] = first_in
    rows = lax.broadcasted_iota(jnp.int32, (length, length), 0)
    cols = lax.broadcasted_iota(jnp.int32, (length, length), 1)
    allowed = (cols <= rows) | (cols < at[4])
    cosine_tab, sine_tab = cosine[...], sine[...]
    group_size = HQ // HK
    for group in range(HK):
        matrix = weight[group].reshape(first_in.shape[1], -1)
        qkv = dot(first_in, matrix)
        at_key = group_size * HD
        key = turned(qkv[:, at_key : at_key + HD], cosine_tab, sine_tab).astype(jnp.bfloat16)
        value = qkv[:, at_key + HD :].astype(jnp.bfloat16)
        key_ref[:, group * HD : (group + 1) * HD] = key
        value_ref[:, group * HD : (group + 1) * HD] = value
        for member in range(group_size):
            head = group * group_size + member
            here = slice(head * HD, (head + 1) * HD)
            query = turned(qkv[:, member * HD : (member + 1) * HD], cosine_tab, sine_tab)
            query = query.astype(jnp.bfloat16)
            query_ref[:, here] = query
            scores = dot(query, key, ((1,), (1,)))
            scores = jnp.where(allowed, scores * HD ** (-0.5), -1e30)
            weights = jnp.exp(scores - jnp.max(scores, axis=-1, keepdims=True))
            prob = weights * (1.0 / jnp.sum(weights, axis=-1, keepdims=True))
            prob = prob.astype(jnp.bfloat16)
            prob_ref[head] = prob
            out_ref[:, here] = dot(prob, value).astype(jnp.bfloat16)
        here = pl.ds(group * group_size, group_size)
        copies.append(
            pltpu.make_async_copy(prob_ref.at[here], prob_out.at[here], sems.at[group])
        )
        copies[-1].start()
    for copy in copies:
        copy.wait()


def project_kernel(at, tokens, gain, attended, *refs):
    resid_ref, second_ref, weight_out, weight, sem = refs[8:]
    place_pieces(at, refs[:8], weight)
    copy = pltpu.make_async_copy(weight, weight_out, sem)
    copy.start()
    heads = attended[...]
    halves = [dot(heads, weight[half].reshape(heads.shape[1], -1)) for half in range(2)]
    resid = tokens[...].astype(jnp.float32) + jnp.concatenate(halves, axis=1)
    resid_ref[...] = resid
    second_ref[...] = rms_kernel(resid, gain[...])
    copy.wait()


def one_hot(slots, capacity, dtype):
    shape = (capacity, slots.shape[1])
    return (slots == lax.broadcasted_iota(jnp.int32, shape, 0)).astype(jnp.float32).astype(dtype)


def slots_of(ids, expert, start, rows):
    named = jnp.any(ids[:, start : start + rows] == expert, axis=0, keepdims=True)
    named = named.astype(jnp.float32)
    before = lax.broadcasted_iota(jnp.int32, (rows, rows), 0)
    upto = lax.broadcasted_iota(jnp.int32, (rows, rows), 1)
    counts = dot(named.astype(jnp.bfloat16), (before <= upto).astype(jnp.float32).astype(jnp.bfloat16))
    return jnp.where(named > 0.0, counts - 1.0, -1.0).astype(jnp.int32)


def spread(picks, capacity, rows, outs):
    rows = rows.astype(jnp.bfloat16)
    block = picks[0].shape[1]
    for n in range(len(picks) // 2):
        for part in range(2):
            pick = picks[2 * n + part]
            at_row = (2 * n + part) * capacity
            tokens = dot(pick, rows[at_row : at_row + capacity], ((0,), (0,)))
            outs[n][part * block : (part + 1) * block] = tokens.astype(jnp.bfloat16)


def expert_kernel(capacity, pieces, earlier, at, ids, router, *refs):
    count = len(pieces)
    second, cot = refs[:count], refs[count : 2 * count]
    gate_w, up_w, down_w = refs[2 * count : 2 * count + 3]
    before = refs[2 * count + 3 : 2 * count + 3 + 2 * earlier]
    refs = refs[2 * count + 3 + 2 * earlier :]
    rows_in, rows_cot, gated_ref, gate_back, up_back, gates_ref = refs[:6]
    backs, gate_rows = refs[6 : 6 + count], refs[-1]
    f32, bf16 = jnp.float32, jnp.bfloat16
    length, width = second[0].shape
    wide = router.shape[1]
    half = length // 2
    picks = []
    experts = lax.broadcasted_iota(jnp.int32, (wide, length), 0)
    for n, piece in enumerate(pieces):
        tokens = second[n][...]
        named = ids[:, piece * length : (piece + 1) * length]
        chosen = functools.reduce(
            jnp.logical_or, [named[k : k + 1] == experts for k in range(named.shape[0])]
        )
        logits = jnp.where(chosen, dot(router[...], tokens, ((0,), (1,))), -1e30)
        weights = jnp.exp(logits - jnp.max(logits, axis=0, keepdims=True))
        gates = weights * (1.0 / jnp.sum(weights, axis=0, keepdims=True))
        if n == 0:
            gates_ref[...] = gates
        own = jnp.sum(jnp.where(experts == at[5], gates, 0.0), axis=0, keepdims=True)
        for part in range(2):
            here = slice(part * half, (part + 1) * half)
            place = slice((2 * n + part) * capacity, (2 * n + part + 1) * capacity)
            slots = slots_of(ids, at[5], piece * length + part * half, half)
            pick = one_hot(slots, capacity, f32)
            picks.append(pick.astype(bf16))
            rows_in[place] = dot(picks[-1], tokens[here]).astype(bf16)
            rows_cot[place] = dot(picks[-1], cot[n][here]).astype(bf16)
            gate_rows[place] = jnp.sum(pick * own[:, here], axis=1, keepdims=True)
    gate = gate_rows[...]
    gate_pre = dot(rows_in[...], gate_w[...])
    up_pre = dot(rows_in[...], up_w[...])
    cot_hidden = dot(rows_cot[...], down_w[...], ((1,), (1,)))
    scale = math.sqrt(2.0 / math.pi)
    square = gate_pre * gate_pre
    bent = jnp.tanh(scale * gate_pre * (1.0 + 0.044715 * square))
    open_part = 0.5 * (1.0 + bent)
    active = gate_pre * open_part
    slope = open_part + 0.5 * gate_pre * (1.0 - bent * bent) * scale * (
        1.0 + 3 * 0.044715 * square
    )
    hidden = active * up_pre
    gated_ref[...] = (gate * hidden).astype(bf16)
    signal = jnp.sum(hidden * cot_hidden, axis=1, keepdims=True)
    back = gate * cot_hidden
    gate_back[...] = (back * up_pre * slope).astype(bf16)
    up_back[...] = (back * active).astype(bf16)
    high = signal.astype(bf16)
    low = (signal - high.astype(f32)).astype(bf16)
    lanes = lax.broadcasted_iota(jnp.int32, (signal.shape[0], wide), 1)
    signal = jnp.where(lanes == at[5], high.astype(f32), 0.0)
    signal = jnp.where(lanes == at[5] + wide // 2, low.astype(f32), signal)
    by_rows = ((1,), (1,))
    rows = dot(gate_back[...], gate_w[...], by_rows) + dot(up_back[...], up_w[...], by_rows)
    spread(picks, capacity, jnp.concatenate([rows, signal], axis=1), backs)
    if earlier:
        lefts = [ref[...] for ref in (*before[:earlier], rows_cot)]
        rights = [ref[...] for ref in (*before[earlier:], gated_ref)]
        total = dot(jnp.concatenate(lefts, axis=0), jnp.concatenate(rights, axis=0), ((0,), (0,)))
        refs[6 + count][...] = total.astype(bf16)


def run_expert(pieces, at, ids, router, weights, second, cot, capacity, before=()):
    count = len(pieces)
    rows, wide = 2 * count * capacity, router.shape[1]
    (length, width), hidden = second[0].shape, weights[0].shape[1]
    bf16, f32 = jnp.bfloat16, jnp.float32
    outs = [(rows, width)] * 2 + [(rows, hidden)] * 3
    outs = [(shape, bf16) for shape in outs] + [((wide, length), f32)]
    outs = outs + [((length, width + wide), bf16)] * count
    if before:
        outs = outs + [((width, hidden), bf16)]
    return run_kernel(
        functools.partial(expert_kernel, capacity, pieces, len(before) // 2),
        4 * count,
        at,
        (ids, router, *second, *cot, *weights, *before),
        outs,
        4 + 3 * count + 4 * bool(before),
        [pltpu.VMEM((rows, 1), f32)],
    )


def mixture_kernel(capacity, groups, at, ids, *refs):
    gated, down_w, outs = refs[: len(groups)], refs[len(groups)], refs[len(groups) + 1 :]
    length = outs[0].shape[0]
    for pieces, rows in zip(groups, gated):
        picks = []
        for piece in pieces:
            for part in range(2):
                start = piece * length + part * length // 2
                slots = slots_of(ids, at[5], start, length // 2)
                picks.append(one_hot(slots, capacity, jnp.bfloat16))
        spread(picks, capacity, dot(rows[...], down_w[...]), [outs[piece] for piece in pieces])


def row_sum_kernel(parts, at, *refs):
    arrays = [
        jnp.concatenate([ref[...] for ref in refs[n : n + parts]], axis=0)
        for n in range(0, len(refs) - len(refs) // (parts + 1), parts)
    ]
    outs = refs[len(arrays) * parts :]
    for out, right in zip(outs, arrays[1:]):
        out[...] = dot(arrays[0], right, ((0,), (0,))).astype(jnp.bfloat16)


def row_sums(at, left, *rights):
    operands = [part for parts in (left, *rights) for part in parts]
    outs = [((left[0].shape[1], right[0].shape[1]), jnp.bfloat16) for right in rights]
    kernel = functools.partial(row_sum_kernel, len(left))
    return run_kernel(kernel, 4 * len(rights), at, operands, outs, 24 if len(rights) == 1 else 56)


def branch_back_kernel(
    at, near, far, first_x, first_y, last_y, last_x, resid, gain, second, gates, router, cot, weight, *outs
):
    resid_grad_ref, branch_ref, attended_ref, router_ref, gain_ref = outs
    f32, bf16 = jnp.float32, jnp.bfloat16
    halves = [first_x[...].astype(f32) + last_y[...], first_y[...].astype(f32) + last_x[...]]
    total = near[...].astype(f32) + far[...] + jnp.concatenate(halves, axis=0)
    width = resid.shape[1]
    signal = total[:, width:]
    signal = signal + pltpu.roll(signal, signal.shape[1] // 2, 1)
    chosen = gates[...].T
    logit_grad = chosen * (signal - jnp.sum(chosen * signal, axis=-1, keepdims=True))
    logit_grad = logit_grad.astype(bf16)
    second_grad = total[:, :width] + dot(logit_grad, router[...], ((1,), (1,)))
    norm_grad, gain_grad = rms_back(resid[...], gain[...], second_grad)
    gain_ref[...] = gain_grad
    resid_grad = cot[...].astype(f32) + norm_grad
    resid_grad_ref[...] = resid_grad
    branch = resid_grad.astype(bf16)
    branch_ref[...] = branch
    wide = weight.shape[2]
    attended_ref[...] = (
        dot(branch[:, :wide], weight[0], ((1,), (1,)))
        + dot(branch[:, wide:], weight[1], ((1,), (1,)))
    ).astype(bf16)
    router_ref[...] = dot(second[...], logit_grad, ((0,), (0,)))


def attend_back_kernel(
    at, attended, probs, queries, keys, values, cosine, sine, branch, back_ref
):
    f32, bf16 = jnp.float32, jnp.bfloat16
    cosine_tab, sine_tab = cosine[...], -sine[...]
    group_size = HQ // HK
    places, length = back_ref.shape[0], branch.shape[0]
    branch_width = branch.shape[1] // places
    width = back_ref.shape[2] - branch_width
    for place in range(places):
        here = slice(place * branch_width, (place + 1) * branch_width)
        back_ref[place, :length, width:] = branch[:, here]
        back_ref[place, length:] = jnp.zeros((back_ref.shape[1] - length, back_ref.shape[2]), bf16)
    scale = HD ** (-0.5)

    def put(position, block):
        back_ref[position // width, :length, position % width : position % width + HD] = block

    for group in range(HK):
        own = slice(group * HD, (group + 1) * HD)
        key, value = keys[:, own], values[:, own]
        key_grad = value_grad = 0.0
        start = group * (group_size + 2) * HD
        for member in range(group_size):
            head = group * group_size + member
            here = slice(head * HD, (head + 1) * HD)
            out_grad, query, prob = attended[:, here], queries[:, here], probs[head]
            prob_grad = dot(out_grad, value, ((1,), (1,)))
            prob_f = prob.astype(f32)
            inner = jnp.sum(prob_f * prob_grad, axis=-1, keepdims=True)
            score_grad = (prob_f * (prob_grad - inner)).astype(bf16)
            query_grad = turned(dot(score_grad, key) * scale, cosine_tab, sine_tab)
            put(start + member * HD, query_grad.astype(bf16))
            key_grad = key_grad + dot(score_grad, query, ((0,), (0,)))
            value_grad = value_grad + dot(prob, out_grad, ((0,), (0,)))
        key_grad = turned(key_grad * scale, cosine_tab, sine_tab)
        put(start + group_size * HD, key_grad.astype(bf16))
        put(start + (group_size + 1) * HD, value_grad.astype(bf16))


def first_back_kernel(at, back, weight, tokens, gain, resid_grad, tokens_ref, gain_ref):
    f32 = jnp.float32
    parts = back.shape[0]
    cols = weight.shape[0] * weight.shape[2] // parts
    first_grad = 0.0
    for part in range(parts):
        group, place = divmod(part * cols, weight.shape[2])
        first_grad = first_grad + dot(
            back[part, : tokens.shape[0], :cols], weight[group, :, place : place + cols], ((1,), (1,))
        )
    norm_grad, gain_grad = rms_back(tokens[...].astype(f32), gain[...], first_grad)
    gain_ref[...] = gain_grad
    tokens_ref[...] = (resid_grad[...] + norm_grad).astype(jnp.bfloat16)


def dense_grad_kernel(at, back, *refs):
    pieces, out_ref, held, sems = refs[:8], refs[8], refs[9], refs[10]
    copies = [
        pltpu.make_async_copy(piece, held.at[n], sems.at[n]) for n, piece in enumerate(pieces)
    ]
    for copy in copies:
        copy.start()
    depth, rows, cols = out_ref.shape
    length = held.shape[1] // 2
    qkv_width = cols - held.shape[2] // back.shape[0]
    narrow = sum(back[place, length:].astype(jnp.float32) for place in range(back.shape[0]))
    sums = [0.0, 0.0]
    for n, copy in enumerate(copies):
        copy.wait()
        dc, dy, dx = n // 4, n // 2 % 2, n % 2
        place = 4 * (at[0] ^ dy) + 2 * (at[1] ^ dc) + (at[2] ^ dx)
        own = back[place, :length]
        sums[0] = sums[0] + dot(held[n, length:], own[:, :qkv_width], ((0,), (0,)))
        sums[1] = sums[1] + dot(held[n, :length], own[:, qkv_width:], ((0,), (0,)))
    wide = held.shape[2] // depth
    each = 4
    for z in range(depth):
        here = slice(z * wide, (z + 1) * wide)
        both = jnp.concatenate([part[here] for part in sums], axis=1)
        out_ref[z, :wide] = both.astype(jnp.bfloat16)
        kept = [narrow[z * each : (z + 1) * each], jnp.zeros((rows - wide - each, cols), jnp.float32)]
        out_ref[z, wide:] = jnp.concatenate(kept, axis=0).astype(jnp.bfloat16)


def finish_kernel(at, sums, query_ref, key_ref, value_ref, output_ref):
    places, _, cols = sums.shape
    rows, out_width = query_ref.shape[0], output_ref.shape[1] // places
    width = cols - out_width
    for place in range(places):
        block = sums[place, :rows].astype(jnp.float32)
        output_ref[:, place * out_width : (place + 1) * out_width] = block[:, width:]
        for at_col in range(0, width, HD):
            group, head = divmod((place * width + at_col) // HD, HQ // HK + 2)
            part = block[:, at_col : at_col + HD]
            if head < HQ // HK:
                start = (group * (HQ // HK) + head) * HD
                query_ref[:, start : start + HD] = part
            elif head == HQ // HK:
                key_ref[:, group * HD : (group + 1) * HD] = part
            else:
                value_ref[:, group * HD : (group + 1) * HD] = part


def local_pairs(
    tokens,
    norm1_gain,
    w_query,
    w_key,
    w_value,
    w_out,
    norm2_gain,
    w_router,
    w_gate,
    w_up,
    w_down,
    expert_ids,
    prefix_len,
    out_grad,
):
    bf16, f32 = jnp.bfloat16, jnp.float32
    length, model_width = tokens.shape
    shard_rows = w_query.shape[0]
    local_count, _, hidden_width = w_gate.shape
    owners = lax.axis_size("x")
    depth = lax.axis_size("z")
    plane = lax.axis_size(PLANE)
    experts_all = w_router.shape[1]
    block_rows = length // MICRO
    capacity = 3 * block_rows * expert_ids.shape[1] // (2 * experts_all)
    plane_rows = plane * length
    blocks = plane_rows // block_rows
    q_cols, kv_cols = w_query.shape[1], w_key.shape[1]
    qkv_cols = q_cols + 2 * kv_cols
    q_group, out_half = q_cols // HK, model_width // 2
    y, c, x, z = (lax.axis_index(axis) for axis in ("y", "c", "x", "z"))
    own_local = 2 * y + c
    own_expert = x * local_count + own_local
    at = jnp.stack([y, c, x, z, prefix_len[0], own_expert, own_local])

    own_half = jnp.concatenate(
        [
            lax.dynamic_slice_in_dim(part, x * (part.shape[1] // 2), part.shape[1] // 2, 1)
            for part in (w_query, w_key, w_value, w_out)
        ],
        axis=1,
    )
    narrow = jnp.concatenate([w_router, norm1_gain[:, None], norm2_gain[:, None]], axis=1)
    narrow = jnp.pad(narrow, ((0, 0), (0, 128 - narrow.shape[1])))
    router_w = small_group_gather(narrow)
    ids_all = small_gather(expert_ids.T)
    column = [own_half] + shifts(own_half)
    cot_sides = plane_sides(after(out_grad, router_w, ids_all))
    qkv_half = qkv_cols // 2
    qkv_column = jnp.stack([part[:, :qkv_half] for part in column])
    out_column = jnp.stack([part[:, qkv_half:] for part in column])
    qkv_column, out_column = lax.optimization_barrier((qkv_column, out_column, *cot_sides))[:2]
    sliced = after(own_local, column[-1])
    gate_w, up_w, down_w = (
        lax.dynamic_index_in_dim(weight, sliced, 0, keepdims=False)
        for weight in (w_gate, w_up, w_down)
    )
    qkv_sides = plane_sides(qkv_column)
    gains = router_w[:, experts_all : experts_all + 2].T.astype(f32)
    gain_one, gain_two = gains[:1], gains[1:]
    qkv_corner = plane_corner(qkv_sides, (gate_w, up_w, down_w, gain_one, gain_two))
    out_sides = plane_sides(after(out_column, *qkv_sides))
    qkv_pieces = plane_pieces(qkv_column, qkv_sides, qkv_corner)
    cosine_tab, sine_tab = angles(length, HD)
    cosine_all = jnp.concatenate([cosine_tab, cosine_tab], axis=2)[:, 0]
    sine_all = jnp.concatenate([-sine_tab, sine_tab], axis=2)[:, 0]
    weight_lead = (2, depth, 2, 2, shard_rows)
    first_in, queries, keys_rot, values_b, attended, probs, qkv_w = run_kernel(
        attend_kernel,
        11,
        at,
        (tokens, gain_one, cosine_all, sine_all, *qkv_pieces),
        [
            ((length, model_width), bf16),
            ((length, q_cols), bf16),
            ((length, kv_cols), bf16),
            ((length, kv_cols), bf16),
            ((length, q_cols), bf16),
            ((HQ, length, length), bf16),
            (weight_lead + (qkv_half,), bf16),
        ],
        28,
        [
            pltpu.VMEM((HQ, length, length), bf16),
            pltpu.VMEM(weight_lead + (qkv_half,), bf16),
            pltpu.SemaphoreType.DMA((HK + 1,)),
        ],
        hbm_out=2,
    )
    out_sides = lax.optimization_barrier((*out_sides, attended))[:2]
    out_corner = plane_corner(out_sides)
    cot_corner = plane_corner(cot_sides)
    out_pieces = plane_pieces(out_column, out_sides, out_corner)
    cot_pieces = plane_pieces(out_grad, cot_sides, cot_corner)
    resid, second_in, output_w = run_kernel(
        project_kernel,
        4,
        at,
        (tokens, after(gain_two, cot_corner), attended, *out_pieces),
        [
            ((length, model_width), f32),
            ((length, model_width), bf16),
            (weight_lead + (out_half,), bf16),
        ],
        44,
        [pltpu.VMEM(weight_lead + (out_half,), bf16), pltpu.SemaphoreType.DMA],
        hbm_out=1,
    )
    qkv_w = qkv_w.reshape(HK, model_width, qkv_half)
    output_w = output_w.reshape(2, q_cols, out_half)

    expert = functools.partial(
        run_expert,
        at=at,
        ids=ids_all,
        router=router_w,
        weights=(gate_w, up_w, down_w),
        capacity=capacity,
    )
    second_sides = plane_sides(second_in)
    groups = ((0, 4), (1, 5, 2, 6), (3, 7))
    second_pieces = {0: second_in, 4: swap(second_in, "c")}

    def run_group(pieces, before=()):
        return expert(
            pieces,
            before=before,
            second=[second_pieces[piece] for piece in pieces],
            cot=[cot_pieces[piece] for piece in pieces],
        )

    stage_own = run_group(groups[0])
    second_sides = lax.optimization_barrier((*second_sides, stage_own[0]))[:2]
    for piece, block in zip((1, 2), second_sides):
        second_pieces[piece], second_pieces[piece + 4] = block, swap(block, "c")
    stage_sides = run_group(groups[1])
    second_corner = plane_corner(second_sides, later=(stage_sides[0],))
    second_pieces[3], second_pieces[7] = second_corner, swap(second_corner, "c")
    own_near, own_far = stage_own[6:]
    own_far = swap(own_far, "c")
    x_near, x_far, y_near, y_far = stage_sides[6:]
    back_x, back_y = over_core(x_near, x_far), over_core(y_near, y_far)
    first_x, first_y = early_sums(back_x, back_y)
    two = (stage_own, stage_sides)
    stage_corner = run_group(groups[2], [stage[1] for stage in two] + [stage[2] for stage in two])
    *stage_corner, down_part = stage_corner
    corner = over_core(*stage_corner[6:])
    passed = corner_first(corner)
    stages = (stage_own, stage_sides, stage_corner)
    rows_in, rows_cot, gated, gate_back, up_back = ([stage[n] for stage in stages] for n in range(5))
    gates = stage_own[5]
    last_y, last_x, *sent = corner_last(back_x, back_y, passed)
    down_sum = scatter_sum(down_part, "z")
    gate_part, up_part = row_sums(
        at, [after(rows_in[0], *sent, own_far)] + rows_in[1:], gate_back, up_back
    )
    gate_sum, up_sum = scatter_sum(gate_part, "z"), scatter_sum(up_part, "z")
    own_near = after(own_near, gate_part)

    resid_grad, branch_grad, attended_grad, router_acc, gain_two_grad = run_kernel(
        branch_back_kernel,
        6,
        at,
        (
            own_near,
            own_far,
            first_x,
            first_y,
            last_y,
            last_x,
            resid,
            gain_two,
            second_in,
            gates,
            router_w,
            out_grad,
            output_w,
        ),
        [
            ((length, model_width), f32),
            ((length, model_width), bf16),
            ((length, q_cols), bf16),
            ((model_width, 128), f32),
            ((1, model_width), f32),
        ],
        56,
    )
    qkv_width, branch_width = qkv_cols // plane, model_width // plane
    dense_cols = qkv_width + branch_width
    (back_cols,) = run_kernel(
        attend_back_kernel,
        6,
        at,
        (
            attended_grad,
            probs,
            queries,
            keys_rot,
            values_b,
            cosine_all,
            sine_all,
            branch_grad,
        ),
        [((plane, length + 16, dense_cols), bf16)],
        56,
    )
    tokens_grad, gain_one_grad = run_kernel(
        first_back_kernel,
        5,
        at,
        (back_cols, qkv_w, tokens, gain_one, resid_grad),
        [((length, model_width), bf16), ((1, model_width), f32)],
        24,
    )

    both = jnp.concatenate(
        lax.optimization_barrier((attended, first_in, last_y, last_x))[:2], axis=0
    )
    both_sides = plane_sides(both)
    narrow_part = jnp.concatenate(
        [router_acc[:, :experts_all], gain_one_grad.T, gain_two_grad.T], axis=1
    )
    narrow_cols = -(-narrow_part.shape[1] // owners) * owners
    narrow_part = jnp.pad(narrow_part, ((0, 0), (0, narrow_cols - narrow_part.shape[1])))
    narrow_part = jnp.transpose(
        narrow_part.reshape(depth, 2, 2, shard_rows, owners, narrow_cols // owners),
        (1, 2, 4, 0, 3, 5),
    ).reshape(plane, depth, shard_rows * narrow_cols // owners)
    narrow_len = narrow_part.shape[2]
    narrow_rows = -(-narrow_len // dense_cols)
    each_rows = -(-narrow_rows // 4) * 4
    narrow_part = jnp.pad(
        narrow_part, ((0, 0), (0, 0), (0, each_rows * dense_cols - narrow_len))
    ).reshape(plane, depth * each_rows, dense_cols)
    narrow_part = jnp.pad(
        narrow_part.astype(bf16), ((0, 0), (0, 16 - depth * each_rows), (0, 0))
    )
    back_cols = lax.dynamic_update_slice(back_cols, narrow_part, (0, length, 0))
    back_cols = exchange(after(back_cols, down_sum, *both_sides), PLANE)
    shares = run_kernel(
        functools.partial(mixture_kernel, capacity, groups),
        10,
        at,
        (ids_all, after(gated[0], *both_sides), *gated[1:], down_w),
        [((length, model_width), bf16)] * plane,
        56,
    )
    sides, shares = lax.optimization_barrier((both_sides, shares))
    both_corner = plane_corner(sides, (back_cols,))
    both_pieces = plane_pieces(both, both_sides, both_corner)
    def placed(total):
        total = exchange(total, ("y", "c"))
        return total.reshape(local_count, shard_rows, hidden_width).astype(f32)

    down_grad, gate_grad = placed(down_sum), placed(gate_sum)
    kept_rows = -(-narrow_rows // 16) * 16
    wide_rows = local_count * shard_rows
    dense_shape = (depth, wide_rows + kept_rows, dense_cols)
    dense_part = pl.pallas_call(
        dense_grad_kernel,
        out_shape=jax.ShapeDtypeStruct(dense_shape, bf16),
        in_specs=[SCALARS, WHOLE] + [IN_HBM] * 8,
        out_specs=WHOLE,
        scratch_shapes=[
            pltpu.VMEM((plane, 2 * length, model_width), bf16),
            pltpu.SemaphoreType.DMA((plane,)),
        ],
        cost_estimate=cost(8),
        compiler_params=pltpu.CompilerParams(vmem_limit_bytes=32 * 2**20),
    )(at, back_cols, *both_pieces)
    dense_part, up_sum = lax.optimization_barrier((dense_part, up_sum))
    dense_sum = scatter_sum(dense_part.reshape(-1, dense_cols), "z")
    mixed = [over_core(near, far) for near, far in zip(shares[:4], shares[4:])]
    early = early_sums(mixed[1], mixed[2])
    last = corner_last(mixed[1], mixed[2], corner_first(mixed[3]))[:2]
    mixture = jnp.concatenate(
        [left.astype(f32) + right.astype(f32) for left, right in zip(early, last)], axis=0
    )
    block_out = (resid + (mixture + mixed[0].astype(f32))).astype(bf16)

    dense_sum, down_grad, gate_grad, up_grad, block_out = lax.optimization_barrier(
        (dense_sum, down_grad, gate_grad, placed(up_sum), block_out)
    )
    wide_sum = dense_sum[: local_count * shard_rows].reshape(2, 2, 1, shard_rows, dense_cols)
    wide_sum = jnp.broadcast_to(wide_sum, (2, 2, owners, shard_rows, dense_cols)).reshape(
        plane, shard_rows, dense_cols
    )
    narrow_sum = dense_sum[local_count * shard_rows :][:narrow_rows]
    narrow_sum = jnp.broadcast_to(narrow_sum[None], (plane, narrow_rows, dense_cols))
    pad_rows = -(shard_rows + narrow_rows) % 16
    padding = jnp.zeros((plane, pad_rows, dense_cols), bf16)
    dense_sum = exchange(jnp.concatenate([wide_sum, narrow_sum, padding], axis=1), PLANE)
    query_grad, key_grad, value_grad, output_grad = run_kernel(
        finish_kernel,
        2,
        at,
        (dense_sum,),
        [
            ((shard_rows, q_cols), f32),
            ((shard_rows, kv_cols), f32),
            ((shard_rows, kv_cols), f32),
            ((shard_rows, model_width), f32),
        ],
    )
    narrow_sum = dense_sum[:, shard_rows : shard_rows + narrow_rows].reshape(
        2, 2, owners, narrow_rows * dense_cols
    )
    narrow_sum = narrow_sum[y, c, :, :narrow_len].reshape(owners, shard_rows, -1)
    narrow_sum = jnp.moveaxis(narrow_sum, 0, 1).reshape(shard_rows, narrow_cols).astype(f32)

    return (
        block_out,
        tokens_grad,
        narrow_sum[:, experts_all],
        query_grad,
        key_grad,
        value_grad,
        output_grad,
        narrow_sum[:, experts_all + 1],
        narrow_sum[:, :experts_all],
        gate_grad,
        up_grad,
        jnp.swapaxes(down_grad, 1, 2),
    )


def solution(mesh):
    groups, owners = mesh.shape["dp"], mesh.shape["expert"]
    grid = jax.sharding.Mesh(
        mesh.devices.reshape(groups // 4, 2, 2, owners), ("z", "y", "c", "x")
    )
    rows = P(("z", "y", "c", "x"), None)
    shard, shard_rows = P(GROUP), P(GROUP, None)
    expert = P("x", None, None)
    return jax.shard_map(
        local_pairs if owners == 2 else local_wide,
        mesh=grid,
        in_specs=(
            rows,
            shard,
            shard_rows,
            shard_rows,
            shard_rows,
            shard_rows,
            shard,
            shard_rows,
            expert,
            expert,
            expert,
            rows,
            P(("z", "y", "c", "x")),
            rows,
        ),
        out_specs=(
            rows,
            rows,
            shard,
            shard_rows,
            shard_rows,
            shard_rows,
            shard_rows,
            shard,
            shard_rows,
            P("x", GROUP, None),
            P("x", GROUP, None),
            P("x", None, GROUP),
        ),
        check_vma=False,
    )
```

```python
import functools
import math

import jax
import jax.numpy as jnp
from jax import lax
from jax.experimental import pallas as pl
from jax.experimental.pallas import tpu as pltpu
from jax.sharding import PartitionSpec as P

HQ = 12
HK = 2
HD = 128
MICRO = 2
PLANE = ("y", "c", "x")
GROUP = ("z", "y", "c")


def rms_scale(values, gain_vec):
    inverse = lax.rsqrt(jnp.mean(values * values, axis=-1, keepdims=True) + 1e-06)
    return values * inverse * gain_vec


def angles(length, head_size):
    positions = jnp.arange(length).astype(jnp.float32)
    freq_rates = jnp.exp(
        -(2.0 * jnp.arange(head_size // 2).astype(jnp.float32) / head_size) * math.log(1000000.0)
    )
    angle_tab = positions[:, None] * freq_rates[None, :]
    return (jnp.cos(angle_tab)[:, None, :], jnp.sin(angle_tab)[:, None, :])


def rotary(values, cosine_tab, sine_tab):
    half_dim = values.shape[-1] // 2
    first_half = values[..., :half_dim]
    second_half = values[..., half_dim:]
    return jnp.concatenate(
        [
            first_half * cosine_tab - second_half * sine_tab,
            second_half * cosine_tab + first_half * sine_tab,
        ],
        axis=-1,
    )


def expert_act(gate_pre, up_pre):
    return jax.nn.gelu(gate_pre, approximate=True) * up_pre


def left_product(left_mat, right_mat):
    return lax.dot_general(
        left_mat, right_mat, (((0,), (0,)), ((), ())), preferred_element_type=jnp.float32
    )


def gather(block, axes):
    return lax.all_gather(block, axes, axis=0, tiled=True)


def exchange(block, axes):
    return lax.all_to_all(block, axes, split_axis=0, concat_axis=0, tiled=True)


def scatter_sum(block, axes):
    return lax.psum_scatter(block, axes, scatter_dimension=0, tiled=True)


def by_owner(cols, parts):
    rows, total = cols.shape
    return jnp.moveaxis(cols.reshape(rows, parts, total // parts), 1, 0).reshape(
        parts * rows, total // parts
    )


def local_wide(
    tokens,
    norm1_gain,
    w_query,
    w_key,
    w_value,
    w_out,
    norm2_gain,
    w_router,
    w_gate,
    w_up,
    w_down,
    expert_ids,
    prefix_len,
    out_grad,
):
    bf16, f32 = jnp.bfloat16, jnp.float32
    length, model_width = tokens.shape
    shard_rows = w_query.shape[0]
    local_count, _, hidden_width = w_gate.shape
    owners = lax.axis_size("x")
    depth = lax.axis_size("z")
    plane = lax.axis_size(PLANE)
    experts_all = w_router.shape[1]
    top_count = expert_ids.shape[1]
    block_rows = length // MICRO
    capacity = 3 * block_rows * top_count // (2 * experts_all)
    plane_rows = plane * length
    blocks = plane_rows // block_rows
    group_size = HQ // HK
    score_scale = HD ** (-0.5)
    q_cols, kv_cols = w_query.shape[1], w_key.shape[1]
    own_local = lax.axis_index(("y", "c"))
    own_expert = lax.axis_index("x") * local_count + own_local
    own_place = lax.axis_index(PLANE)

    narrow = jnp.concatenate([w_router, norm1_gain[:, None], norm2_gain[:, None]], axis=1)
    narrow = jnp.pad(narrow, ((0, 0), (0, -narrow.shape[1] % 128)))
    packed = gather(jnp.concatenate([w_query, w_key, w_value, narrow], axis=1), GROUP)
    qkv_cols = q_cols + 2 * kv_cols
    qkv_w = packed[:, :qkv_cols]
    router_w = packed[:, qkv_cols : qkv_cols + experts_all]
    gains = packed[:, qkv_cols + experts_all : qkv_cols + experts_all + 2].T.astype(f32)
    gain_one, gain_two = gains[0], gains[1]
    output_w = gather(w_out, GROUP)

    ids_all = gather(expert_ids, PLANE)
    cot_all = gather(out_grad, PLANE)
    chosen_mask = jnp.any(
        ids_all[:, :, None] == jnp.arange(experts_all, dtype=jnp.int32)[None, None, :], axis=1
    )
    own_mask = jnp.any(ids_all == own_expert, axis=1).reshape(blocks, block_rows)
    place = jnp.cumsum(own_mask.astype(jnp.int32), axis=1) - 1
    dispatch = (
        own_mask[:, None, :]
        & (place[:, None, :] == jnp.arange(capacity, dtype=jnp.int32)[None, :, None])
    ).astype(bf16)

    cosine_tab, sine_tab = angles(length, HD)
    inputs_f = tokens.astype(f32)
    first_in = rms_scale(inputs_f, gain_one).astype(bf16)
    qkv = jnp.dot(first_in, qkv_w, preferred_element_type=f32)
    queries = (
        rotary(qkv[:, :q_cols].reshape(length, HQ, HD), cosine_tab, sine_tab)
        .astype(bf16)
        .reshape(length, HK, group_size, HD)
    )
    keys_rot = rotary(
        qkv[:, q_cols : q_cols + kv_cols].reshape(length, HK, HD), cosine_tab, sine_tab
    ).astype(bf16)
    values_b = qkv[:, q_cols + kv_cols :].astype(bf16).reshape(length, HK, HD)
    positions = jnp.arange(length)
    allowed = (positions[None, :] <= positions[:, None]) | (positions[None, :] < prefix_len[0])

    def masked_scores():
        scores = jnp.einsum("ihrd,jhd->hrij", queries, keys_rot, preferred_element_type=f32)
        return jnp.where(allowed, scores * score_scale, -1e30)

    masked = masked_scores()
    row_peak = jnp.max(masked, axis=-1, keepdims=True)
    log_total = row_peak + jnp.log(jnp.sum(jnp.exp(masked - row_peak), axis=-1, keepdims=True))
    prob_bf = jnp.exp(masked - log_total).astype(bf16)
    attended = jnp.einsum("hrij,jhd->ihrd", prob_bf, values_b, preferred_element_type=f32)
    attended = attended.reshape(length, HQ * HD).astype(bf16)
    resid = inputs_f + jnp.dot(attended, output_w, preferred_element_type=f32)
    second_in = rms_scale(resid, gain_two).astype(bf16)

    second_all = gather(second_in, PLANE)
    logits = jnp.dot(second_all, router_w, preferred_element_type=f32)
    gates_all = jax.nn.softmax(jnp.where(chosen_mask, logits, -jnp.inf), axis=-1)
    own_gates = lax.dynamic_index_in_dim(gates_all, own_expert, 1, keepdims=False)
    own_gates = own_gates.reshape(blocks, block_rows)
    gate_rows = jnp.einsum(
        "bct,bt->bc", dispatch.astype(f32), own_gates, precision=lax.Precision.HIGHEST
    )[:, :, None]
    gate_w = lax.dynamic_index_in_dim(w_gate, own_local, 0, keepdims=False)
    up_w = lax.dynamic_index_in_dim(w_up, own_local, 0, keepdims=False)
    down_w = lax.dynamic_index_in_dim(w_down, own_local, 0, keepdims=False)

    def to_rows(array):
        return jnp.einsum(
            "bct,btd->bcd",
            dispatch,
            array.reshape(blocks, block_rows, model_width),
            preferred_element_type=f32,
        ).astype(bf16)

    def to_tokens(rows):
        return (
            jnp.einsum("bct,bcd->btd", dispatch, rows.astype(bf16), preferred_element_type=f32)
            .astype(bf16)
            .reshape(plane_rows, model_width)
        )

    rows_in = to_rows(second_all)
    rows_cot = to_rows(cot_all)
    gate_pre = jnp.einsum("bcd,df->bcf", rows_in, gate_w, preferred_element_type=f32)
    up_pre = jnp.einsum("bcd,df->bcf", rows_in, up_w, preferred_element_type=f32)
    hidden, act_pull = jax.vjp(expert_act, gate_pre, up_pre)
    gated = (gate_rows * hidden).astype(bf16)
    down_part = jnp.einsum("bcd,bcf->df", rows_cot, gated, preferred_element_type=f32)
    down_sum = scatter_sum(down_part.astype(bf16), "z")
    cot_hidden = jnp.einsum("bcd,fd->bcf", rows_cot, down_w, preferred_element_type=f32)
    gate_signal_rows = jnp.sum(hidden * cot_hidden, axis=-1)
    gate_pgrad, up_pgrad = act_pull(gate_rows * cot_hidden)
    gate_pgrad = gate_pgrad.astype(bf16)
    up_pgrad = up_pgrad.astype(bf16)
    gate_part = jnp.einsum("bcd,bcf->df", rows_in, gate_pgrad, preferred_element_type=f32)
    gate_sum = scatter_sum(gate_part.astype(bf16), "z")
    up_part = jnp.einsum("bcd,bcf->df", rows_in, up_pgrad, preferred_element_type=f32)
    up_sum = scatter_sum(up_part.astype(bf16), "z")
    rows_grad = jnp.einsum("bcf,df->bcd", gate_pgrad, gate_w, preferred_element_type=f32)
    rows_grad = rows_grad + jnp.einsum("bcf,df->bcd", up_pgrad, up_w, preferred_element_type=f32)
    second_back = scatter_sum(to_tokens(rows_grad), PLANE).astype(f32)
    gate_signal = jnp.einsum(
        "bct,bc->bt", dispatch.astype(f32), gate_signal_rows, precision=lax.Precision.HIGHEST
    )
    gate_signal = exchange(gate_signal.reshape(plane, length), PLANE)
    gate_signal = jnp.transpose(
        gate_signal.reshape(local_count, owners, length), (2, 1, 0)
    ).reshape(length, experts_all)
    expert_rows = jnp.einsum("bcf,fd->bcd", gated, down_w, preferred_element_type=f32)
    mixture = scatter_sum(to_tokens(expert_rows), PLANE).astype(f32)
    block_out = (resid + mixture).astype(bf16)

    cotangent = out_grad.astype(f32)
    gate_probs = lax.dynamic_slice_in_dim(gates_all, own_place * length, length, 0)
    logit_grad = (
        gate_probs
        * (gate_signal - jnp.sum(gate_probs * gate_signal, axis=-1, keepdims=True))
    ).astype(bf16)
    router_acc = left_product(second_in, logit_grad)
    second_grad = second_back + jnp.dot(logit_grad, router_w.T, preferred_element_type=f32)
    _, norm_two_pull = jax.vjp(rms_scale, resid, gain_two)
    resid_norm_grad, gain_two_grad = norm_two_pull(second_grad)
    resid_grad = cotangent + resid_norm_grad
    branch_grad = resid_grad.astype(bf16)

    attended_all = gather(attended, PLANE)
    branch_cols = exchange(by_owner(branch_grad, plane), PLANE)
    output_part = left_product(attended_all, branch_cols)
    attended_grad = jnp.dot(branch_grad, output_w.T, preferred_element_type=f32).astype(bf16)
    attended_grad = attended_grad.reshape(length, HK, group_size, HD)
    masked = masked_scores()
    prob_full = jnp.exp(masked - log_total)
    prob_bf = prob_full.astype(bf16)
    prob_grad = jnp.einsum("ihrd,jhd->hrij", attended_grad, values_b, preferred_element_type=f32)
    row_inner = jnp.sum(prob_full * prob_grad, axis=-1, keepdims=True)
    score_grad = (prob_full * (prob_grad - row_inner)).astype(bf16)
    query_rot_grad = (
        jnp.einsum("hrij,jhd->ihrd", score_grad, keys_rot, preferred_element_type=f32)
        * score_scale
    )
    query_back = rotary(query_rot_grad.reshape(length, HQ, HD), cosine_tab, -sine_tab)
    query_back = query_back.astype(bf16).reshape(length, HQ * HD)
    key_rot_grad = (
        jnp.einsum("hrij,ihrd->jhd", score_grad, queries, preferred_element_type=f32)
        * score_scale
    )
    key_back = rotary(key_rot_grad, cosine_tab, -sine_tab).astype(bf16).reshape(length, HK * HD)
    value_back = jnp.einsum("hrij,ihrd->jhd", prob_bf, attended_grad, preferred_element_type=f32)
    value_back = value_back.astype(bf16).reshape(length, HK * HD)
    qkv_back = jnp.concatenate([query_back, key_back, value_back], axis=1)
    first_all = gather(first_in, PLANE)
    qkv_part = left_product(first_all, exchange(by_owner(qkv_back, plane), PLANE))
    first_grad = lax.dot_general(
        qkv_back, qkv_w, (((1,), (1,)), ((), ())), preferred_element_type=f32
    )
    _, norm_one_pull = jax.vjp(rms_scale, inputs_f, gain_one)
    input_norm_grad, gain_one_grad = norm_one_pull(first_grad)
    tokens_grad = (resid_grad + input_norm_grad).astype(bf16)

    narrow_part = jnp.concatenate(
        [router_acc, gain_one_grad[:, None], gain_two_grad[:, None]], axis=1
    ).astype(bf16)
    narrow_cols = narrow_part.shape[1]
    narrow_sum = lax.psum(scatter_sum(narrow_part, GROUP), "x").astype(f32)
    dense_part = jnp.concatenate([qkv_part, output_part], axis=1).astype(bf16)
    dense_sum = scatter_sum(dense_part, "z")
    dense_cols = dense_sum.shape[1]
    dense_sum = gather(dense_sum, PLANE).reshape(plane, local_count, shard_rows, dense_cols)
    dense_sum = lax.dynamic_index_in_dim(dense_sum, own_local, 1, keepdims=False).astype(f32)
    dense_sum = jnp.moveaxis(dense_sum, 0, 1)
    qkv_width = qkv_cols // plane
    qkv_sum = dense_sum[:, :, :qkv_width].reshape(shard_rows, qkv_cols)
    output_sum = dense_sum[:, :, qkv_width:].reshape(shard_rows, model_width)

    def placed(total):
        total = exchange(total, ("y", "c"))
        return total.reshape(local_count, shard_rows, hidden_width).astype(f32)

    return (
        block_out,
        tokens_grad,
        narrow_sum[:, experts_all],
        qkv_sum[:, :q_cols],
        qkv_sum[:, q_cols : q_cols + kv_cols],
        qkv_sum[:, q_cols + kv_cols :],
        output_sum,
        narrow_sum[:, experts_all + 1],
        narrow_sum[:, :experts_all],
        placed(gate_sum),
        placed(up_sum),
        jnp.swapaxes(placed(down_sum), 1, 2),
    )


def rounded(values):
    return lax.reduce_precision(values, 8, 7).astype(jnp.bfloat16)


def after(block, *others):
    return lax.optimization_barrier((block,) + others)[0]


def swap(block, axis):
    return lax.ppermute(block, axis, [(0, 1), (1, 0)])


def shifts(block):
    depth = lax.axis_size("z")
    return [
        lax.ppermute(block, "z", [(i, (i + k) % depth) for i in range(depth)])
        for k in range(1, depth)
    ]


def plane_sides(block):
    return swap(block, "x"), swap(block, "y")


def plane_corner(sides, before=(), later=()):
    over_x, over_y = sides
    half = over_x.shape[0] // 2
    over_y, over_x = lax.optimization_barrier((over_y[:half], over_x[half:]) + before)[:2]
    parts = (swap(over_y, "x"), swap(over_x, "y"))
    return jnp.concatenate(lax.optimization_barrier(parts + later)[:2], axis=0)


def plane_pieces(block, sides=None, corner=None):
    sides = plane_sides(block) if sides is None else sides
    corner = plane_corner(sides) if corner is None else corner
    pieces = [block, *sides, corner]
    return pieces + [swap(piece, "c") for piece in pieces]


def small_gather(block):
    for axis in ("x", "y", "c"):
        block = jnp.concatenate([block, swap(block, axis)], axis=1)
    return block


def small_group_gather(block):
    depth = lax.axis_size("z")
    order = jnp.stack(([block] + shifts(block))[::-1] * 2)
    start = (depth - 1 - lax.axis_index("z")) % depth
    total = lax.dynamic_slice_in_dim(order, start, depth, 0)[:, None, None]
    for dim, axis in ((1, "y"), (2, "c")):
        other = swap(total, axis)
        last = lax.axis_index(axis) == 1
        pair = [jnp.where(last, other, total), jnp.where(last, total, other)]
        total = jnp.concatenate(pair, axis=dim)
    return total.reshape(-1, block.shape[1])


def add(left, right):
    return rounded(left.astype(jnp.float32) + right.astype(jnp.float32))


def over_core(near, far):
    return add(near, swap(far, "c"))


def early_sums(over_x, over_y):
    half = over_x.shape[0] // 2
    return swap(over_x[:half], "x"), swap(over_y[half:], "y")


def corner_first(corner):
    half = corner.shape[0] // 2
    return swap(corner[:half], "x"), swap(corner[half:], "y")


def corner_last(over_x, over_y, first):
    half = over_x.shape[0] // 2
    over_y, over_x = add(over_y[:half], first[0]), add(over_x[half:], first[1])
    return swap(over_y, "y"), swap(over_x, "x"), over_y, over_x


def cost(micros):
    return pl.CostEstimate(flops=micros * 10**9, bytes_accessed=micros * 10**6, transcendentals=0)


def dot(left, right, dims=((1,), (0,)), precision=None):
    return lax.dot_general(
        left, right, (dims, ((), ())), precision=precision, preferred_element_type=jnp.float32
    )


WHOLE = pl.BlockSpec(memory_space=pltpu.VMEM)
IN_HBM = pl.BlockSpec(memory_space=pltpu.HBM)
SCALARS = pl.BlockSpec(memory_space=pltpu.SMEM)


def run_kernel(kernel, micros, at, operands, outs, megabytes=16, scratch=(), hbm_in=0, hbm_out=0):
    return pl.pallas_call(
        kernel,
        out_shape=[jax.ShapeDtypeStruct(shape, dtype) for shape, dtype in outs],
        in_specs=[SCALARS] + [WHOLE] * (len(operands) - hbm_in) + [IN_HBM] * hbm_in,
        out_specs=[WHOLE] * (len(outs) - hbm_out) + [IN_HBM] * hbm_out,
        scratch_shapes=scratch,
        cost_estimate=cost(micros),
        compiler_params=pltpu.CompilerParams(vmem_limit_bytes=megabytes * 2**20),
    )(at, *operands)


def place_pieces(at, refs, weight):
    depth = weight.shape[1]
    for n, ref in enumerate(refs):
        dc, dy, dx = n // 4, n // 2 % 2, n % 2
        for k in range(depth):
            z = lax.rem(at[3] + depth - k, depth)
            weight[at[2] ^ dx, z, at[0] ^ dy, at[1] ^ dc] = ref[k]


def rms_kernel(values, gain):
    inverse = lax.rsqrt(jnp.mean(values * values, axis=-1, keepdims=True) + 1e-06)
    return (values * inverse * gain).astype(jnp.bfloat16)


def rms_back(values, gain, grad):
    inverse = lax.rsqrt(jnp.mean(values * values, axis=-1, keepdims=True) + 1e-06)
    normed = values * inverse
    gain_grad = jnp.sum(grad * normed, axis=0, keepdims=True)
    grad = grad * gain
    along = jnp.mean(grad * normed, axis=-1, keepdims=True)
    return inverse * (grad - normed * along), gain_grad


def turned(values, cosine_tab, sine_tab):
    return values * cosine_tab + pltpu.roll(values, HD // 2, 1) * sine_tab


def attend_kernel(at, tokens, gain, cosine, sine, *refs):
    first_ref, query_ref, key_ref, value_ref, out_ref = refs[8:13]
    prob_out, weight_out, prob_ref, weight, sems = refs[13:]
    place_pieces(at, refs[:8], weight)
    copies = [pltpu.make_async_copy(weight, weight_out, sems.at[HK])]
    copies[0].start()
    length = tokens.shape[0]
    first_in = rms_kernel(tokens[...].astype(jnp.float32), gain[...])
    first_ref[...] = first_in
    rows = lax.broadcasted_iota(jnp.int32, (length, length), 0)
    cols = lax.broadcasted_iota(jnp.int32, (length, length), 1)
    allowed = (cols <= rows) | (cols < at[4])
    cosine_tab, sine_tab = cosine[...], sine[...]
    group_size = HQ // HK
    for group in range(HK):
        matrix = weight[group].reshape(first_in.shape[1], -1)
        qkv = dot(first_in, matrix)
        at_key = group_size * HD
        key = turned(qkv[:, at_key : at_key + HD], cosine_tab, sine_tab).astype(jnp.bfloat16)
        value = qkv[:, at_key + HD :].astype(jnp.bfloat16)
        key_ref[:, group * HD : (group + 1) * HD] = key
        value_ref[:, group * HD : (group + 1) * HD] = value
        for member in range(group_size):
            head = group * group_size + member
            here = slice(head * HD, (head + 1) * HD)
            query = turned(qkv[:, member * HD : (member + 1) * HD], cosine_tab, sine_tab)
            query = query.astype(jnp.bfloat16)
            query_ref[:, here] = query
            scores = dot(query, key, ((1,), (1,)))
            scores = jnp.where(allowed, scores * HD ** (-0.5), -1e30)
            weights = jnp.exp(scores - jnp.max(scores, axis=-1, keepdims=True))
            prob = weights * (1.0 / jnp.sum(weights, axis=-1, keepdims=True))
            prob = prob.astype(jnp.bfloat16)
            prob_ref[head] = prob
            out_ref[:, here] = dot(prob, value).astype(jnp.bfloat16)
        here = pl.ds(group * group_size, group_size)
        copies.append(
            pltpu.make_async_copy(prob_ref.at[here], prob_out.at[here], sems.at[group])
        )
        copies[-1].start()
    for copy in copies:
        copy.wait()


def project_kernel(at, tokens, gain, attended, *refs):
    resid_ref, second_ref, weight_out, weight, sem = refs[8:]
    place_pieces(at, refs[:8], weight)
    copy = pltpu.make_async_copy(weight, weight_out, sem)
    copy.start()
    heads = attended[...]
    halves = [dot(heads, weight[half].reshape(heads.shape[1], -1)) for half in range(2)]
    resid = tokens[...].astype(jnp.float32) + jnp.concatenate(halves, axis=1)
    resid_ref[...] = resid
    second_ref[...] = rms_kernel(resid, gain[...])
    copy.wait()


def one_hot(slots, capacity, dtype):
    shape = (capacity, slots.shape[1])
    return (slots == lax.broadcasted_iota(jnp.int32, shape, 0)).astype(jnp.float32).astype(dtype)


def slots_of(ids, expert, start, rows):
    named = jnp.any(ids[:, start : start + rows] == expert, axis=0, keepdims=True)
    named = named.astype(jnp.float32)
    before = lax.broadcasted_iota(jnp.int32, (rows, rows), 0)
    upto = lax.broadcasted_iota(jnp.int32, (rows, rows), 1)
    counts = dot(named.astype(jnp.bfloat16), (before <= upto).astype(jnp.float32).astype(jnp.bfloat16))
    return jnp.where(named > 0.0, counts - 1.0, -1.0).astype(jnp.int32)


def spread(picks, capacity, rows, outs):
    rows = rows.astype(jnp.bfloat16)
    block = picks[0].shape[1]
    for n in range(len(picks) // 2):
        for part in range(2):
            pick = picks[2 * n + part]
            at_row = (2 * n + part) * capacity
            tokens = dot(pick, rows[at_row : at_row + capacity], ((0,), (0,)))
            outs[n][part * block : (part + 1) * block] = tokens.astype(jnp.bfloat16)


def expert_kernel(capacity, pieces, earlier, at, ids, router, *refs):
    count = len(pieces)
    second, cot = refs[:count], refs[count : 2 * count]
    gate_w, up_w, down_w = refs[2 * count : 2 * count + 3]
    before = refs[2 * count + 3 : 2 * count + 3 + 2 * earlier]
    refs = refs[2 * count + 3 + 2 * earlier :]
    rows_in, rows_cot, gated_ref, gate_back, up_back, gates_ref = refs[:6]
    backs, gate_rows = refs[6 : 6 + count], refs[-1]
    f32, bf16 = jnp.float32, jnp.bfloat16
    length, width = second[0].shape
    wide = router.shape[1]
    half = length // 2
    picks = []
    experts = lax.broadcasted_iota(jnp.int32, (wide, length), 0)
    for n, piece in enumerate(pieces):
        tokens = second[n][...]
        named = ids[:, piece * length : (piece + 1) * length]
        chosen = functools.reduce(
            jnp.logical_or, [named[k : k + 1] == experts for k in range(named.shape[0])]
        )
        logits = jnp.where(chosen, dot(router[...], tokens, ((0,), (1,))), -1e30)
        weights = jnp.exp(logits - jnp.max(logits, axis=0, keepdims=True))
        gates = weights * (1.0 / jnp.sum(weights, axis=0, keepdims=True))
        if n == 0:
            gates_ref[...] = gates
        own = jnp.sum(jnp.where(experts == at[5], gates, 0.0), axis=0, keepdims=True)
        for part in range(2):
            here = slice(part * half, (part + 1) * half)
            place = slice((2 * n + part) * capacity, (2 * n + part + 1) * capacity)
            slots = slots_of(ids, at[5], piece * length + part * half, half)
            pick = one_hot(slots, capacity, f32)
            picks.append(pick.astype(bf16))
            rows_in[place] = dot(picks[-1], tokens[here]).astype(bf16)
            rows_cot[place] = dot(picks[-1], cot[n][here]).astype(bf16)
            gate_rows[place] = jnp.sum(pick * own[:, here], axis=1, keepdims=True)
    gate = gate_rows[...]
    gate_pre = dot(rows_in[...], gate_w[...])
    up_pre = dot(rows_in[...], up_w[...])
    cot_hidden = dot(rows_cot[...], down_w[...], ((1,), (1,)))
    scale = math.sqrt(2.0 / math.pi)
    square = gate_pre * gate_pre
    bent = jnp.tanh(scale * gate_pre * (1.0 + 0.044715 * square))
    open_part = 0.5 * (1.0 + bent)
    active = gate_pre * open_part
    slope = open_part + 0.5 * gate_pre * (1.0 - bent * bent) * scale * (
        1.0 + 3 * 0.044715 * square
    )
    hidden = active * up_pre
    gated_ref[...] = (gate * hidden).astype(bf16)
    signal = jnp.sum(hidden * cot_hidden, axis=1, keepdims=True)
    back = gate * cot_hidden
    gate_back[...] = (back * up_pre * slope).astype(bf16)
    up_back[...] = (back * active).astype(bf16)
    high = signal.astype(bf16)
    low = (signal - high.astype(f32)).astype(bf16)
    lanes = lax.broadcasted_iota(jnp.int32, (signal.shape[0], wide), 1)
    signal = jnp.where(lanes == at[5], high.astype(f32), 0.0)
    signal = jnp.where(lanes == at[5] + wide // 2, low.astype(f32), signal)
    by_rows = ((1,), (1,))
    rows = dot(gate_back[...], gate_w[...], by_rows) + dot(up_back[...], up_w[...], by_rows)
    spread(picks, capacity, jnp.concatenate([rows, signal], axis=1), backs)
    if earlier:
        lefts = [ref[...] for ref in (*before[:earlier], rows_cot)]
        rights = [ref[...] for ref in (*before[earlier:], gated_ref)]
        total = dot(jnp.concatenate(lefts, axis=0), jnp.concatenate(rights, axis=0), ((0,), (0,)))
        refs[6 + count][...] = total.astype(bf16)


def run_expert(pieces, at, ids, router, weights, second, cot, capacity, before=()):
    count = len(pieces)
    rows, wide = 2 * count * capacity, router.shape[1]
    (length, width), hidden = second[0].shape, weights[0].shape[1]
    bf16, f32 = jnp.bfloat16, jnp.float32
    outs = [(rows, width)] * 2 + [(rows, hidden)] * 3
    outs = [(shape, bf16) for shape in outs] + [((wide, length), f32)]
    outs = outs + [((length, width + wide), bf16)] * count
    if before:
        outs = outs + [((width, hidden), bf16)]
    return run_kernel(
        functools.partial(expert_kernel, capacity, pieces, len(before) // 2),
        4 * count,
        at,
        (ids, router, *second, *cot, *weights, *before),
        outs,
        4 + 3 * count + 4 * bool(before),
        [pltpu.VMEM((rows, 1), f32)],
    )


def mixture_kernel(capacity, groups, at, ids, *refs):
    gated, down_w, outs = refs[: len(groups)], refs[len(groups)], refs[len(groups) + 1 :]
    length = outs[0].shape[0]
    for pieces, rows in zip(groups, gated):
        picks = []
        for piece in pieces:
            for part in range(2):
                start = piece * length + part * length // 2
                slots = slots_of(ids, at[5], start, length // 2)
                picks.append(one_hot(slots, capacity, jnp.bfloat16))
        spread(picks, capacity, dot(rows[...], down_w[...]), [outs[piece] for piece in pieces])


def row_sum_kernel(parts, at, *refs):
    arrays = [
        jnp.concatenate([ref[...] for ref in refs[n : n + parts]], axis=0)
        for n in range(0, len(refs) - len(refs) // (parts + 1), parts)
    ]
    outs = refs[len(arrays) * parts :]
    for out, right in zip(outs, arrays[1:]):
        out[...] = dot(arrays[0], right, ((0,), (0,))).astype(jnp.bfloat16)


def row_sums(at, left, *rights):
    operands = [part for parts in (left, *rights) for part in parts]
    outs = [((left[0].shape[1], right[0].shape[1]), jnp.bfloat16) for right in rights]
    kernel = functools.partial(row_sum_kernel, len(left))
    return run_kernel(kernel, 4 * len(rights), at, operands, outs, 24 if len(rights) == 1 else 56)


def branch_back_kernel(
    at, near, far, first_x, first_y, last_y, last_x, resid, gain, second, gates, router, cot, weight, *outs
):
    resid_grad_ref, branch_ref, attended_ref, router_ref, gain_ref = outs
    f32, bf16 = jnp.float32, jnp.bfloat16
    halves = [first_x[...].astype(f32) + last_y[...], first_y[...].astype(f32) + last_x[...]]
    total = near[...].astype(f32) + far[...] + jnp.concatenate(halves, axis=0)
    width = resid.shape[1]
    signal = total[:, width:]
    signal = signal + pltpu.roll(signal, signal.shape[1] // 2, 1)
    chosen = gates[...].T
    logit_grad = chosen * (signal - jnp.sum(chosen * signal, axis=-1, keepdims=True))
    logit_grad = logit_grad.astype(bf16)
    second_grad = total[:, :width] + dot(logit_grad, router[...], ((1,), (1,)))
    norm_grad, gain_grad = rms_back(resid[...], gain[...], second_grad)
    gain_ref[...] = gain_grad
    resid_grad = cot[...].astype(f32) + norm_grad
    resid_grad_ref[...] = resid_grad
    branch = resid_grad.astype(bf16)
    branch_ref[...] = branch
    wide = weight.shape[2]
    attended_ref[...] = (
        dot(branch[:, :wide], weight[0], ((1,), (1,)))
        + dot(branch[:, wide:], weight[1], ((1,), (1,)))
    ).astype(bf16)
    router_ref[...] = dot(second[...], logit_grad, ((0,), (0,)))


def attend_back_kernel(
    at, attended, probs, queries, keys, values, cosine, sine, branch, back_ref
):
    f32, bf16 = jnp.float32, jnp.bfloat16
    cosine_tab, sine_tab = cosine[...], -sine[...]
    group_size = HQ // HK
    places, length = back_ref.shape[0], branch.shape[0]
    branch_width = branch.shape[1] // places
    width = back_ref.shape[2] - branch_width
    for place in range(places):
        here = slice(place * branch_width, (place + 1) * branch_width)
        back_ref[place, :length, width:] = branch[:, here]
        back_ref[place, length:] = jnp.zeros((back_ref.shape[1] - length, back_ref.shape[2]), bf16)
    scale = HD ** (-0.5)

    def put(position, block):
        back_ref[position // width, :length, position % width : position % width + HD] = block

    for group in range(HK):
        own = slice(group * HD, (group + 1) * HD)
        key, value = keys[:, own], values[:, own]
        key_grad = value_grad = 0.0
        start = group * (group_size + 2) * HD
        for member in range(group_size):
            head = group * group_size + member
            here = slice(head * HD, (head + 1) * HD)
            out_grad, query, prob = attended[:, here], queries[:, here], probs[head]
            prob_grad = dot(out_grad, value, ((1,), (1,)))
            prob_f = prob.astype(f32)
            inner = jnp.sum(prob_f * prob_grad, axis=-1, keepdims=True)
            score_grad = (prob_f * (prob_grad - inner)).astype(bf16)
            query_grad = turned(dot(score_grad, key) * scale, cosine_tab, sine_tab)
            put(start + member * HD, query_grad.astype(bf16))
            key_grad = key_grad + dot(score_grad, query, ((0,), (0,)))
            value_grad = value_grad + dot(prob, out_grad, ((0,), (0,)))
        key_grad = turned(key_grad * scale, cosine_tab, sine_tab)
        put(start + group_size * HD, key_grad.astype(bf16))
        put(start + (group_size + 1) * HD, value_grad.astype(bf16))


def first_back_kernel(at, back, weight, tokens, gain, resid_grad, tokens_ref, gain_ref):
    f32 = jnp.float32
    parts = back.shape[0]
    cols = weight.shape[0] * weight.shape[2] // parts
    first_grad = 0.0
    for part in range(parts):
        group, place = divmod(part * cols, weight.shape[2])
        first_grad = first_grad + dot(
            back[part, : tokens.shape[0], :cols], weight[group, :, place : place + cols], ((1,), (1,))
        )
    norm_grad, gain_grad = rms_back(tokens[...].astype(f32), gain[...], first_grad)
    gain_ref[...] = gain_grad
    tokens_ref[...] = (resid_grad[...] + norm_grad).astype(jnp.bfloat16)


def dense_grad_kernel(at, back, *refs):
    pieces, out_ref, held, sems = refs[:8], refs[8], refs[9], refs[10]
    copies = [
        pltpu.make_async_copy(piece, held.at[n], sems.at[n]) for n, piece in enumerate(pieces)
    ]
    for copy in copies:
        copy.start()
    depth, rows, cols = out_ref.shape
    length = held.shape[1] // 2
    qkv_width = cols - held.shape[2] // back.shape[0]
    narrow = sum(back[place, length:].astype(jnp.float32) for place in range(back.shape[0]))
    sums = [0.0, 0.0]
    for n, copy in enumerate(copies):
        copy.wait()
        dc, dy, dx = n // 4, n // 2 % 2, n % 2
        place = 4 * (at[0] ^ dy) + 2 * (at[1] ^ dc) + (at[2] ^ dx)
        own = back[place, :length]
        sums[0] = sums[0] + dot(held[n, length:], own[:, :qkv_width], ((0,), (0,)))
        sums[1] = sums[1] + dot(held[n, :length], own[:, qkv_width:], ((0,), (0,)))
    wide = held.shape[2] // depth
    each = 4
    for z in range(depth):
        here = slice(z * wide, (z + 1) * wide)
        both = jnp.concatenate([part[here] for part in sums], axis=1)
        out_ref[z, :wide] = both.astype(jnp.bfloat16)
        kept = [narrow[z * each : (z + 1) * each], jnp.zeros((rows - wide - each, cols), jnp.float32)]
        out_ref[z, wide:] = jnp.concatenate(kept, axis=0).astype(jnp.bfloat16)


def finish_kernel(at, sums, query_ref, key_ref, value_ref, output_ref):
    places, _, cols = sums.shape
    rows, out_width = query_ref.shape[0], output_ref.shape[1] // places
    width = cols - out_width
    for place in range(places):
        block = sums[place, :rows].astype(jnp.float32)
        output_ref[:, place * out_width : (place + 1) * out_width] = block[:, width:]
        for at_col in range(0, width, HD):
            group, head = divmod((place * width + at_col) // HD, HQ // HK + 2)
            part = block[:, at_col : at_col + HD]
            if head < HQ // HK:
                start = (group * (HQ // HK) + head) * HD
                query_ref[:, start : start + HD] = part
            elif head == HQ // HK:
                key_ref[:, group * HD : (group + 1) * HD] = part
            else:
                value_ref[:, group * HD : (group + 1) * HD] = part


def local_pairs(
    tokens,
    norm1_gain,
    w_query,
    w_key,
    w_value,
    w_out,
    norm2_gain,
    w_router,
    w_gate,
    w_up,
    w_down,
    expert_ids,
    prefix_len,
    out_grad,
):
    bf16, f32 = jnp.bfloat16, jnp.float32
    length, model_width = tokens.shape
    shard_rows = w_query.shape[0]
    local_count, _, hidden_width = w_gate.shape
    owners = lax.axis_size("x")
    depth = lax.axis_size("z")
    plane = lax.axis_size(PLANE)
    experts_all = w_router.shape[1]
    block_rows = length // MICRO
    capacity = 3 * block_rows * expert_ids.shape[1] // (2 * experts_all)
    plane_rows = plane * length
    blocks = plane_rows // block_rows
    q_cols, kv_cols = w_query.shape[1], w_key.shape[1]
    qkv_cols = q_cols + 2 * kv_cols
    q_group, out_half = q_cols // HK, model_width // 2
    y, c, x, z = (lax.axis_index(axis) for axis in ("y", "c", "x", "z"))
    own_local = 2 * y + c
    own_expert = x * local_count + own_local
    at = jnp.stack([y, c, x, z, prefix_len[0], own_expert, own_local])

    own_half = jnp.concatenate(
        [
            lax.dynamic_slice_in_dim(part, x * (part.shape[1] // 2), part.shape[1] // 2, 1)
            for part in (w_query, w_key, w_value, w_out)
        ],
        axis=1,
    )
    narrow = jnp.concatenate([w_router, norm1_gain[:, None], norm2_gain[:, None]], axis=1)
    narrow = jnp.pad(narrow, ((0, 0), (0, 128 - narrow.shape[1])))
    router_w = small_group_gather(narrow)
    ids_all = small_gather(expert_ids.T)
    column = [own_half] + shifts(own_half)
    cot_sides = plane_sides(after(out_grad, router_w, ids_all))
    qkv_half = qkv_cols // 2
    qkv_column = jnp.stack([part[:, :qkv_half] for part in column])
    out_column = jnp.stack([part[:, qkv_half:] for part in column])
    qkv_column, out_column = lax.optimization_barrier((qkv_column, out_column, *cot_sides))[:2]
    sliced = after(own_local, column[-1])
    gate_w, up_w, down_w = (
        lax.dynamic_index_in_dim(weight, sliced, 0, keepdims=False)
        for weight in (w_gate, w_up, w_down)
    )
    qkv_sides = plane_sides(qkv_column)
    gains = router_w[:, experts_all : experts_all + 2].T.astype(f32)
    gain_one, gain_two = gains[:1], gains[1:]
    qkv_corner = plane_corner(qkv_sides, (gate_w, up_w, down_w, gain_one, gain_two))
    out_sides = plane_sides(after(out_column, *qkv_sides))
    qkv_pieces = plane_pieces(qkv_column, qkv_sides, qkv_corner)
    cosine_tab, sine_tab = angles(length, HD)
    cosine_all = jnp.concatenate([cosine_tab, cosine_tab], axis=2)[:, 0]
    sine_all = jnp.concatenate([-sine_tab, sine_tab], axis=2)[:, 0]
    weight_lead = (2, depth, 2, 2, shard_rows)
    first_in, queries, keys_rot, values_b, attended, probs, qkv_w = run_kernel(
        attend_kernel,
        11,
        at,
        (tokens, gain_one, cosine_all, sine_all, *qkv_pieces),
        [
            ((length, model_width), bf16),
            ((length, q_cols), bf16),
            ((length, kv_cols), bf16),
            ((length, kv_cols), bf16),
            ((length, q_cols), bf16),
            ((HQ, length, length), bf16),
            (weight_lead + (qkv_half,), bf16),
        ],
        28,
        [
            pltpu.VMEM((HQ, length, length), bf16),
            pltpu.VMEM(weight_lead + (qkv_half,), bf16),
            pltpu.SemaphoreType.DMA((HK + 1,)),
        ],
        hbm_out=2,
    )
    out_sides = lax.optimization_barrier((*out_sides, attended))[:2]
    out_corner = plane_corner(out_sides)
    cot_corner = plane_corner(cot_sides)
    out_pieces = plane_pieces(out_column, out_sides, out_corner)
    cot_pieces = plane_pieces(out_grad, cot_sides, cot_corner)
    resid, second_in, output_w = run_kernel(
        project_kernel,
        4,
        at,
        (tokens, after(gain_two, cot_corner), attended, *out_pieces),
        [
            ((length, model_width), f32),
            ((length, model_width), bf16),
            (weight_lead + (out_half,), bf16),
        ],
        44,
        [pltpu.VMEM(weight_lead + (out_half,), bf16), pltpu.SemaphoreType.DMA],
        hbm_out=1,
    )
    qkv_w = qkv_w.reshape(HK, model_width, qkv_half)
    output_w = output_w.reshape(2, q_cols, out_half)

    expert = functools.partial(
        run_expert,
        at=at,
        ids=ids_all,
        router=router_w,
        weights=(gate_w, up_w, down_w),
        capacity=capacity,
    )
    second_sides = plane_sides(second_in)
    groups = ((0, 4), (1, 5, 2, 6), (3, 7))
    second_pieces = {0: second_in, 4: swap(second_in, "c")}

    def run_group(pieces, before=()):
        return expert(
            pieces,
            before=before,
            second=[second_pieces[piece] for piece in pieces],
            cot=[cot_pieces[piece] for piece in pieces],
        )

    stage_own = run_group(groups[0])
    second_sides = lax.optimization_barrier((*second_sides, stage_own[0]))[:2]
    for piece, block in zip((1, 2), second_sides):
        second_pieces[piece], second_pieces[piece + 4] = block, swap(block, "c")
    stage_sides = run_group(groups[1])
    second_corner = plane_corner(second_sides, later=(stage_sides[0],))
    second_pieces[3], second_pieces[7] = second_corner, swap(second_corner, "c")
    own_near, own_far = stage_own[6:]
    own_far = swap(own_far, "c")
    x_near, x_far, y_near, y_far = stage_sides[6:]
    back_x, back_y = over_core(x_near, x_far), over_core(y_near, y_far)
    first_x, first_y = early_sums(back_x, back_y)
    two = (stage_own, stage_sides)
    stage_corner = run_group(groups[2], [stage[1] for stage in two] + [stage[2] for stage in two])
    *stage_corner, down_part = stage_corner
    corner = over_core(*stage_corner[6:])
    passed = corner_first(corner)
    stages = (stage_own, stage_sides, stage_corner)
    rows_in, rows_cot, gated, gate_back, up_back = ([stage[n] for stage in stages] for n in range(5))
    gates = stage_own[5]
    last_y, last_x = corner_last(back_x, back_y, passed)[:2]
    down_sum = scatter_sum(down_part, "z")

    resid_grad, branch_grad, attended_grad, router_acc, gain_two_grad = run_kernel(
        branch_back_kernel,
        6,
        at,
        (
            own_near,
            own_far,
            first_x,
            first_y,
            last_y,
            last_x,
            resid,
            gain_two,
            second_in,
            gates,
            router_w,
            out_grad,
            output_w,
        ),
        [
            ((length, model_width), f32),
            ((length, model_width), bf16),
            ((length, q_cols), bf16),
            ((model_width, 128), f32),
            ((1, model_width), f32),
        ],
        56,
    )
    gate_part, up_part = row_sums(
        at, [after(rows_in[0], resid_grad)] + rows_in[1:], gate_back, up_back
    )
    gate_sum, up_sum = scatter_sum(gate_part, "z"), scatter_sum(up_part, "z")
    attended_grad = after(attended_grad, gate_part)
    qkv_width, branch_width = qkv_cols // plane, model_width // plane
    dense_cols = qkv_width + branch_width
    (back_cols,) = run_kernel(
        attend_back_kernel,
        6,
        at,
        (
            attended_grad,
            probs,
            queries,
            keys_rot,
            values_b,
            cosine_all,
            sine_all,
            branch_grad,
        ),
        [((plane, length + 16, dense_cols), bf16)],
        56,
    )
    tokens_grad, gain_one_grad = run_kernel(
        first_back_kernel,
        5,
        at,
        (back_cols, qkv_w, tokens, gain_one, resid_grad),
        [((length, model_width), bf16), ((1, model_width), f32)],
        24,
    )

    both = jnp.concatenate(
        lax.optimization_barrier((attended, first_in, last_y, last_x))[:2], axis=0
    )
    both_sides = plane_sides(both)
    narrow_part = jnp.concatenate(
        [router_acc[:, :experts_all], gain_one_grad.T, gain_two_grad.T], axis=1
    )
    narrow_cols = -(-narrow_part.shape[1] // owners) * owners
    narrow_part = jnp.pad(narrow_part, ((0, 0), (0, narrow_cols - narrow_part.shape[1])))
    narrow_part = jnp.transpose(
        narrow_part.reshape(depth, 2, 2, shard_rows, owners, narrow_cols // owners),
        (1, 2, 4, 0, 3, 5),
    ).reshape(plane, depth, shard_rows * narrow_cols // owners)
    narrow_len = narrow_part.shape[2]
    narrow_rows = -(-narrow_len // dense_cols)
    each_rows = -(-narrow_rows // 4) * 4
    narrow_part = jnp.pad(
        narrow_part, ((0, 0), (0, 0), (0, each_rows * dense_cols - narrow_len))
    ).reshape(plane, depth * each_rows, dense_cols)
    narrow_part = jnp.pad(
        narrow_part.astype(bf16), ((0, 0), (0, 16 - depth * each_rows), (0, 0))
    )
    back_cols = lax.dynamic_update_slice(back_cols, narrow_part, (0, length, 0))
    back_cols = exchange(after(back_cols, down_sum, *both_sides), PLANE)
    shares = run_kernel(
        functools.partial(mixture_kernel, capacity, groups),
        10,
        at,
        (ids_all, after(gated[0], *both_sides), *gated[1:], down_w),
        [((length, model_width), bf16)] * plane,
        56,
    )
    sides, shares = lax.optimization_barrier((both_sides, shares))
    both_corner = plane_corner(sides, (back_cols,))
    both_pieces = plane_pieces(both, both_sides, both_corner)
    def placed(total):
        total = exchange(total, ("y", "c"))
        return total.reshape(local_count, shard_rows, hidden_width).astype(f32)

    down_grad, gate_grad = placed(down_sum), placed(gate_sum)
    kept_rows = -(-narrow_rows // 16) * 16
    wide_rows = local_count * shard_rows
    dense_shape = (depth, wide_rows + kept_rows, dense_cols)
    dense_part = pl.pallas_call(
        dense_grad_kernel,
        out_shape=jax.ShapeDtypeStruct(dense_shape, bf16),
        in_specs=[SCALARS, WHOLE] + [IN_HBM] * 8,
        out_specs=WHOLE,
        scratch_shapes=[
            pltpu.VMEM((plane, 2 * length, model_width), bf16),
            pltpu.SemaphoreType.DMA((plane,)),
        ],
        cost_estimate=cost(8),
        compiler_params=pltpu.CompilerParams(vmem_limit_bytes=32 * 2**20),
    )(at, back_cols, *both_pieces)
    dense_part, up_sum = lax.optimization_barrier((dense_part, up_sum))
    dense_sum = scatter_sum(dense_part.reshape(-1, dense_cols), "z")
    mixed = [over_core(near, far) for near, far in zip(shares[:4], shares[4:])]
    early = early_sums(mixed[1], mixed[2])
    first, down_grad, gate_grad = lax.optimization_barrier(
        (corner_first(mixed[3]), down_grad, gate_grad)
    )
    last, up_grad = lax.optimization_barrier(
        (corner_last(mixed[1], mixed[2], first)[:2], placed(up_sum))
    )
    mixture = jnp.concatenate(
        [left.astype(f32) + right.astype(f32) for left, right in zip(early, last)], axis=0
    )
    block_out = (resid + (mixture + mixed[0].astype(f32))).astype(bf16)

    wide_sum = dense_sum[: local_count * shard_rows].reshape(2, 2, 1, shard_rows, dense_cols)
    wide_sum = jnp.broadcast_to(wide_sum, (2, 2, owners, shard_rows, dense_cols)).reshape(
        plane, shard_rows, dense_cols
    )
    narrow_sum = dense_sum[local_count * shard_rows :][:narrow_rows]
    narrow_sum = jnp.broadcast_to(narrow_sum[None], (plane, narrow_rows, dense_cols))
    pad_rows = -(shard_rows + narrow_rows) % 16
    padding = jnp.zeros((plane, pad_rows, dense_cols), bf16)
    dense_sum = exchange(jnp.concatenate([wide_sum, narrow_sum, padding], axis=1), PLANE)
    query_grad, key_grad, value_grad, output_grad = run_kernel(
        finish_kernel,
        2,
        at,
        (dense_sum,),
        [
            ((shard_rows, q_cols), f32),
            ((shard_rows, kv_cols), f32),
            ((shard_rows, kv_cols), f32),
            ((shard_rows, model_width), f32),
        ],
    )
    narrow_sum = dense_sum[:, shard_rows : shard_rows + narrow_rows].reshape(
        2, 2, owners, narrow_rows * dense_cols
    )
    narrow_sum = narrow_sum[y, c, :, :narrow_len].reshape(owners, shard_rows, -1)
    narrow_sum = jnp.moveaxis(narrow_sum, 0, 1).reshape(shard_rows, narrow_cols).astype(f32)

    return (
        block_out,
        tokens_grad,
        narrow_sum[:, experts_all],
        query_grad,
        key_grad,
        value_grad,
        output_grad,
        narrow_sum[:, experts_all + 1],
        narrow_sum[:, :experts_all],
        gate_grad,
        up_grad,
        jnp.swapaxes(down_grad, 1, 2),
    )


def solution(mesh):
    groups, owners = mesh.shape["dp"], mesh.shape["expert"]
    grid = jax.sharding.Mesh(
        mesh.devices.reshape(groups // 4, 2, 2, owners), ("z", "y", "c", "x")
    )
    rows = P(("z", "y", "c", "x"), None)
    shard, shard_rows = P(GROUP), P(GROUP, None)
    expert = P("x", None, None)
    return jax.shard_map(
        local_pairs if owners == 2 else local_wide,
        mesh=grid,
        in_specs=(
            rows,
            shard,
            shard_rows,
            shard_rows,
            shard_rows,
            shard_rows,
            shard,
            shard_rows,
            expert,
            expert,
            expert,
            rows,
            P(("z", "y", "c", "x")),
            rows,
        ),
        out_specs=(
            rows,
            rows,
            shard,
            shard_rows,
            shard_rows,
            shard_rows,
            shard_rows,
            shard,
            shard_rows,
            P("x", GROUP, None),
            P("x", GROUP, None),
            P("x", None, GROUP),
        ),
        check_vma=False,
    )
```

```python
import functools
import math

import jax
import jax.numpy as jnp
from jax import lax
from jax.experimental import pallas as pl
from jax.experimental.pallas import tpu as pltpu
from jax.sharding import PartitionSpec as P

HQ = 12
HK = 2
HD = 128
MICRO = 2
PLANE = ("y", "c", "x")
GROUP = ("z", "y", "c")


def rms_scale(values, gain_vec):
    inverse = lax.rsqrt(jnp.mean(values * values, axis=-1, keepdims=True) + 1e-06)
    return values * inverse * gain_vec


def angles(length, head_size):
    positions = jnp.arange(length).astype(jnp.float32)
    freq_rates = jnp.exp(
        -(2.0 * jnp.arange(head_size // 2).astype(jnp.float32) / head_size) * math.log(1000000.0)
    )
    angle_tab = positions[:, None] * freq_rates[None, :]
    return (jnp.cos(angle_tab)[:, None, :], jnp.sin(angle_tab)[:, None, :])


def rotary(values, cosine_tab, sine_tab):
    half_dim = values.shape[-1] // 2
    first_half = values[..., :half_dim]
    second_half = values[..., half_dim:]
    return jnp.concatenate(
        [
            first_half * cosine_tab - second_half * sine_tab,
            second_half * cosine_tab + first_half * sine_tab,
        ],
        axis=-1,
    )


def expert_act(gate_pre, up_pre):
    return jax.nn.gelu(gate_pre, approximate=True) * up_pre


def left_product(left_mat, right_mat):
    return lax.dot_general(
        left_mat, right_mat, (((0,), (0,)), ((), ())), preferred_element_type=jnp.float32
    )


def gather(block, axes):
    return lax.all_gather(block, axes, axis=0, tiled=True)


def exchange(block, axes):
    return lax.all_to_all(block, axes, split_axis=0, concat_axis=0, tiled=True)


def scatter_sum(block, axes):
    return lax.psum_scatter(block, axes, scatter_dimension=0, tiled=True)


def by_owner(cols, parts):
    rows, total = cols.shape
    return jnp.moveaxis(cols.reshape(rows, parts, total // parts), 1, 0).reshape(
        parts * rows, total // parts
    )


def local_wide(
    tokens,
    norm1_gain,
    w_query,
    w_key,
    w_value,
    w_out,
    norm2_gain,
    w_router,
    w_gate,
    w_up,
    w_down,
    expert_ids,
    prefix_len,
    out_grad,
):
    bf16, f32 = jnp.bfloat16, jnp.float32
    length, model_width = tokens.shape
    shard_rows = w_query.shape[0]
    local_count, _, hidden_width = w_gate.shape
    owners = lax.axis_size("x")
    depth = lax.axis_size("z")
    plane = lax.axis_size(PLANE)
    experts_all = w_router.shape[1]
    top_count = expert_ids.shape[1]
    block_rows = length // MICRO
    capacity = 3 * block_rows * top_count // (2 * experts_all)
    plane_rows = plane * length
    blocks = plane_rows // block_rows
    group_size = HQ // HK
    score_scale = HD ** (-0.5)
    q_cols, kv_cols = w_query.shape[1], w_key.shape[1]
    own_local = lax.axis_index(("y", "c"))
    own_expert = lax.axis_index("x") * local_count + own_local
    own_place = lax.axis_index(PLANE)

    narrow = jnp.concatenate([w_router, norm1_gain[:, None], norm2_gain[:, None]], axis=1)
    narrow = jnp.pad(narrow, ((0, 0), (0, -narrow.shape[1] % 128)))
    packed = gather(jnp.concatenate([w_query, w_key, w_value, narrow], axis=1), GROUP)
    qkv_cols = q_cols + 2 * kv_cols
    qkv_w = packed[:, :qkv_cols]
    router_w = packed[:, qkv_cols : qkv_cols + experts_all]
    gains = packed[:, qkv_cols + experts_all : qkv_cols + experts_all + 2].T.astype(f32)
    gain_one, gain_two = gains[0], gains[1]
    output_w = gather(w_out, GROUP)

    ids_all = gather(expert_ids, PLANE)
    cot_all = gather(out_grad, PLANE)
    chosen_mask = jnp.any(
        ids_all[:, :, None] == jnp.arange(experts_all, dtype=jnp.int32)[None, None, :], axis=1
    )
    own_mask = jnp.any(ids_all == own_expert, axis=1).reshape(blocks, block_rows)
    place = jnp.cumsum(own_mask.astype(jnp.int32), axis=1) - 1
    dispatch = (
        own_mask[:, None, :]
        & (place[:, None, :] == jnp.arange(capacity, dtype=jnp.int32)[None, :, None])
    ).astype(bf16)

    cosine_tab, sine_tab = angles(length, HD)
    inputs_f = tokens.astype(f32)
    first_in = rms_scale(inputs_f, gain_one).astype(bf16)
    qkv = jnp.dot(first_in, qkv_w, preferred_element_type=f32)
    queries = (
        rotary(qkv[:, :q_cols].reshape(length, HQ, HD), cosine_tab, sine_tab)
        .astype(bf16)
        .reshape(length, HK, group_size, HD)
    )
    keys_rot = rotary(
        qkv[:, q_cols : q_cols + kv_cols].reshape(length, HK, HD), cosine_tab, sine_tab
    ).astype(bf16)
    values_b = qkv[:, q_cols + kv_cols :].astype(bf16).reshape(length, HK, HD)
    positions = jnp.arange(length)
    allowed = (positions[None, :] <= positions[:, None]) | (positions[None, :] < prefix_len[0])

    def masked_scores():
        scores = jnp.einsum("ihrd,jhd->hrij", queries, keys_rot, preferred_element_type=f32)
        return jnp.where(allowed, scores * score_scale, -1e30)

    masked = masked_scores()
    row_peak = jnp.max(masked, axis=-1, keepdims=True)
    log_total = row_peak + jnp.log(jnp.sum(jnp.exp(masked - row_peak), axis=-1, keepdims=True))
    prob_bf = jnp.exp(masked - log_total).astype(bf16)
    attended = jnp.einsum("hrij,jhd->ihrd", prob_bf, values_b, preferred_element_type=f32)
    attended = attended.reshape(length, HQ * HD).astype(bf16)
    resid = inputs_f + jnp.dot(attended, output_w, preferred_element_type=f32)
    second_in = rms_scale(resid, gain_two).astype(bf16)

    second_all = gather(second_in, PLANE)
    logits = jnp.dot(second_all, router_w, preferred_element_type=f32)
    gates_all = jax.nn.softmax(jnp.where(chosen_mask, logits, -jnp.inf), axis=-1)
    own_gates = lax.dynamic_index_in_dim(gates_all, own_expert, 1, keepdims=False)
    own_gates = own_gates.reshape(blocks, block_rows)
    gate_rows = jnp.einsum(
        "bct,bt->bc", dispatch.astype(f32), own_gates, precision=lax.Precision.HIGHEST
    )[:, :, None]
    gate_w = lax.dynamic_index_in_dim(w_gate, own_local, 0, keepdims=False)
    up_w = lax.dynamic_index_in_dim(w_up, own_local, 0, keepdims=False)
    down_w = lax.dynamic_index_in_dim(w_down, own_local, 0, keepdims=False)

    def to_rows(array):
        return jnp.einsum(
            "bct,btd->bcd",
            dispatch,
            array.reshape(blocks, block_rows, model_width),
            preferred_element_type=f32,
        ).astype(bf16)

    def to_tokens(rows):
        return (
            jnp.einsum("bct,bcd->btd", dispatch, rows.astype(bf16), preferred_element_type=f32)
            .astype(bf16)
            .reshape(plane_rows, model_width)
        )

    rows_in = to_rows(second_all)
    rows_cot = to_rows(cot_all)
    gate_pre = jnp.einsum("bcd,df->bcf", rows_in, gate_w, preferred_element_type=f32)
    up_pre = jnp.einsum("bcd,df->bcf", rows_in, up_w, preferred_element_type=f32)
    hidden, act_pull = jax.vjp(expert_act, gate_pre, up_pre)
    gated = (gate_rows * hidden).astype(bf16)
    down_part = jnp.einsum("bcd,bcf->df", rows_cot, gated, preferred_element_type=f32)
    down_sum = scatter_sum(down_part.astype(bf16), "z")
    cot_hidden = jnp.einsum("bcd,fd->bcf", rows_cot, down_w, preferred_element_type=f32)
    gate_signal_rows = jnp.sum(hidden * cot_hidden, axis=-1)
    gate_pgrad, up_pgrad = act_pull(gate_rows * cot_hidden)
    gate_pgrad = gate_pgrad.astype(bf16)
    up_pgrad = up_pgrad.astype(bf16)
    gate_part = jnp.einsum("bcd,bcf->df", rows_in, gate_pgrad, preferred_element_type=f32)
    gate_sum = scatter_sum(gate_part.astype(bf16), "z")
    up_part = jnp.einsum("bcd,bcf->df", rows_in, up_pgrad, preferred_element_type=f32)
    up_sum = scatter_sum(up_part.astype(bf16), "z")
    rows_grad = jnp.einsum("bcf,df->bcd", gate_pgrad, gate_w, preferred_element_type=f32)
    rows_grad = rows_grad + jnp.einsum("bcf,df->bcd", up_pgrad, up_w, preferred_element_type=f32)
    second_back = scatter_sum(to_tokens(rows_grad), PLANE).astype(f32)
    gate_signal = jnp.einsum(
        "bct,bc->bt", dispatch.astype(f32), gate_signal_rows, precision=lax.Precision.HIGHEST
    )
    gate_signal = exchange(gate_signal.reshape(plane, length), PLANE)
    gate_signal = jnp.transpose(
        gate_signal.reshape(local_count, owners, length), (2, 1, 0)
    ).reshape(length, experts_all)
    expert_rows = jnp.einsum("bcf,fd->bcd", gated, down_w, preferred_element_type=f32)
    mixture = scatter_sum(to_tokens(expert_rows), PLANE).astype(f32)
    block_out = (resid + mixture).astype(bf16)

    cotangent = out_grad.astype(f32)
    gate_probs = lax.dynamic_slice_in_dim(gates_all, own_place * length, length, 0)
    logit_grad = (
        gate_probs
        * (gate_signal - jnp.sum(gate_probs * gate_signal, axis=-1, keepdims=True))
    ).astype(bf16)
    router_acc = left_product(second_in, logit_grad)
    second_grad = second_back + jnp.dot(logit_grad, router_w.T, preferred_element_type=f32)
    _, norm_two_pull = jax.vjp(rms_scale, resid, gain_two)
    resid_norm_grad, gain_two_grad = norm_two_pull(second_grad)
    resid_grad = cotangent + resid_norm_grad
    branch_grad = resid_grad.astype(bf16)

    attended_all = gather(attended, PLANE)
    branch_cols = exchange(by_owner(branch_grad, plane), PLANE)
    output_part = left_product(attended_all, branch_cols)
    attended_grad = jnp.dot(branch_grad, output_w.T, preferred_element_type=f32).astype(bf16)
    attended_grad = attended_grad.reshape(length, HK, group_size, HD)
    masked = masked_scores()
    prob_full = jnp.exp(masked - log_total)
    prob_bf = prob_full.astype(bf16)
    prob_grad = jnp.einsum("ihrd,jhd->hrij", attended_grad, values_b, preferred_element_type=f32)
    row_inner = jnp.sum(prob_full * prob_grad, axis=-1, keepdims=True)
    score_grad = (prob_full * (prob_grad - row_inner)).astype(bf16)
    query_rot_grad = (
        jnp.einsum("hrij,jhd->ihrd", score_grad, keys_rot, preferred_element_type=f32)
        * score_scale
    )
    query_back = rotary(query_rot_grad.reshape(length, HQ, HD), cosine_tab, -sine_tab)
    query_back = query_back.astype(bf16).reshape(length, HQ * HD)
    key_rot_grad = (
        jnp.einsum("hrij,ihrd->jhd", score_grad, queries, preferred_element_type=f32)
        * score_scale
    )
    key_back = rotary(key_rot_grad, cosine_tab, -sine_tab).astype(bf16).reshape(length, HK * HD)
    value_back = jnp.einsum("hrij,ihrd->jhd", prob_bf, attended_grad, preferred_element_type=f32)
    value_back = value_back.astype(bf16).reshape(length, HK * HD)
    qkv_back = jnp.concatenate([query_back, key_back, value_back], axis=1)
    first_all = gather(first_in, PLANE)
    qkv_part = left_product(first_all, exchange(by_owner(qkv_back, plane), PLANE))
    first_grad = lax.dot_general(
        qkv_back, qkv_w, (((1,), (1,)), ((), ())), preferred_element_type=f32
    )
    _, norm_one_pull = jax.vjp(rms_scale, inputs_f, gain_one)
    input_norm_grad, gain_one_grad = norm_one_pull(first_grad)
    tokens_grad = (resid_grad + input_norm_grad).astype(bf16)

    narrow_part = jnp.concatenate(
        [router_acc, gain_one_grad[:, None], gain_two_grad[:, None]], axis=1
    ).astype(bf16)
    narrow_cols = narrow_part.shape[1]
    narrow_sum = lax.psum(scatter_sum(narrow_part, GROUP), "x").astype(f32)
    dense_part = jnp.concatenate([qkv_part, output_part], axis=1).astype(bf16)
    dense_sum = scatter_sum(dense_part, "z")
    dense_cols = dense_sum.shape[1]
    dense_sum = gather(dense_sum, PLANE).reshape(plane, local_count, shard_rows, dense_cols)
    dense_sum = lax.dynamic_index_in_dim(dense_sum, own_local, 1, keepdims=False).astype(f32)
    dense_sum = jnp.moveaxis(dense_sum, 0, 1)
    qkv_width = qkv_cols // plane
    qkv_sum = dense_sum[:, :, :qkv_width].reshape(shard_rows, qkv_cols)
    output_sum = dense_sum[:, :, qkv_width:].reshape(shard_rows, model_width)

    def placed(total):
        total = exchange(total, ("y", "c"))
        return total.reshape(local_count, shard_rows, hidden_width).astype(f32)

    return (
        block_out,
        tokens_grad,
        narrow_sum[:, experts_all],
        qkv_sum[:, :q_cols],
        qkv_sum[:, q_cols : q_cols + kv_cols],
        qkv_sum[:, q_cols + kv_cols :],
        output_sum,
        narrow_sum[:, experts_all + 1],
        narrow_sum[:, :experts_all],
        placed(gate_sum),
        placed(up_sum),
        jnp.swapaxes(placed(down_sum), 1, 2),
    )


def rounded(values):
    return lax.reduce_precision(values, 8, 7).astype(jnp.bfloat16)


def after(block, *others):
    return lax.optimization_barrier((block,) + others)[0]


def swap(block, axis):
    return lax.ppermute(block, axis, [(0, 1), (1, 0)])


def shifts(block):
    depth = lax.axis_size("z")
    return [
        lax.ppermute(block, "z", [(i, (i + k) % depth) for i in range(depth)])
        for k in range(1, depth)
    ]


def plane_sides(block):
    return swap(block, "x"), swap(block, "y")


def plane_corner(sides, before=(), later=()):
    over_x, over_y = sides
    half = over_x.shape[0] // 2
    over_y, over_x = lax.optimization_barrier((over_y[:half], over_x[half:]) + before)[:2]
    parts = (swap(over_y, "x"), swap(over_x, "y"))
    return jnp.concatenate(lax.optimization_barrier(parts + later)[:2], axis=0)


def plane_pieces(block, sides=None, corner=None):
    sides = plane_sides(block) if sides is None else sides
    corner = plane_corner(sides) if corner is None else corner
    pieces = [block, *sides, corner]
    return pieces + [swap(piece, "c") for piece in pieces]


def small_gather(block):
    for axis in ("x", "y", "c"):
        block = jnp.concatenate([block, swap(block, axis)], axis=1)
    return block


def small_group_gather(block):
    depth = lax.axis_size("z")
    order = jnp.stack(([block] + shifts(block))[::-1] * 2)
    start = (depth - 1 - lax.axis_index("z")) % depth
    total = lax.dynamic_slice_in_dim(order, start, depth, 0)[:, None, None]
    for dim, axis in ((1, "y"), (2, "c")):
        other = swap(total, axis)
        last = lax.axis_index(axis) == 1
        pair = [jnp.where(last, other, total), jnp.where(last, total, other)]
        total = jnp.concatenate(pair, axis=dim)
    return total.reshape(-1, block.shape[1])


def add(left, right):
    return rounded(left.astype(jnp.float32) + right.astype(jnp.float32))


def over_core(near, far):
    return add(near, swap(far, "c"))


def early_sums(over_x, over_y):
    half = over_x.shape[0] // 2
    return swap(over_x[:half], "x"), swap(over_y[half:], "y")


def corner_first(corner):
    half = corner.shape[0] // 2
    return swap(corner[:half], "x"), swap(corner[half:], "y")


def corner_last(over_x, over_y, first):
    half = over_x.shape[0] // 2
    over_y, over_x = add(over_y[:half], first[0]), add(over_x[half:], first[1])
    return swap(over_y, "y"), swap(over_x, "x"), over_y, over_x


def cost(micros):
    return pl.CostEstimate(flops=micros * 10**9, bytes_accessed=micros * 10**6, transcendentals=0)


def dot(left, right, dims=((1,), (0,)), precision=None):
    return lax.dot_general(
        left, right, (dims, ((), ())), precision=precision, preferred_element_type=jnp.float32
    )


WHOLE = pl.BlockSpec(memory_space=pltpu.VMEM)
IN_HBM = pl.BlockSpec(memory_space=pltpu.HBM)
SCALARS = pl.BlockSpec(memory_space=pltpu.SMEM)


def run_kernel(kernel, micros, at, operands, outs, megabytes=16, scratch=(), hbm_in=0, hbm_out=0):
    return pl.pallas_call(
        kernel,
        out_shape=[jax.ShapeDtypeStruct(shape, dtype) for shape, dtype in outs],
        in_specs=[SCALARS] + [WHOLE] * (len(operands) - hbm_in) + [IN_HBM] * hbm_in,
        out_specs=[WHOLE] * (len(outs) - hbm_out) + [IN_HBM] * hbm_out,
        scratch_shapes=scratch,
        cost_estimate=cost(micros),
        compiler_params=pltpu.CompilerParams(vmem_limit_bytes=megabytes * 2**20),
    )(at, *operands)


def place_pieces(at, refs, weight):
    depth = weight.shape[1]
    for n, ref in enumerate(refs):
        dc, dy, dx = n // 4, n // 2 % 2, n % 2
        for k in range(depth):
            z = lax.rem(at[3] + depth - k, depth)
            weight[at[2] ^ dx, z, at[0] ^ dy, at[1] ^ dc] = ref[k]


def rms_kernel(values, gain):
    inverse = lax.rsqrt(jnp.mean(values * values, axis=-1, keepdims=True) + 1e-06)
    return (values * inverse * gain).astype(jnp.bfloat16)


def rms_back(values, gain, grad):
    inverse = lax.rsqrt(jnp.mean(values * values, axis=-1, keepdims=True) + 1e-06)
    normed = values * inverse
    gain_grad = jnp.sum(grad * normed, axis=0, keepdims=True)
    grad = grad * gain
    along = jnp.mean(grad * normed, axis=-1, keepdims=True)
    return inverse * (grad - normed * along), gain_grad


def turned(values, cosine_tab, sine_tab):
    return values * cosine_tab + pltpu.roll(values, HD // 2, 1) * sine_tab


def attend_kernel(at, tokens, gain, cosine, sine, *refs):
    first_ref, query_ref, key_ref, value_ref, out_ref = refs[8:13]
    prob_out, weight_out, prob_ref, weight, sems = refs[13:]
    place_pieces(at, refs[:8], weight)
    copies = [pltpu.make_async_copy(weight, weight_out, sems.at[HK])]
    copies[0].start()
    length = tokens.shape[0]
    first_in = rms_kernel(tokens[...].astype(jnp.float32), gain[...])
    first_ref[...] = first_in
    rows = lax.broadcasted_iota(jnp.int32, (length, length), 0)
    cols = lax.broadcasted_iota(jnp.int32, (length, length), 1)
    allowed = (cols <= rows) | (cols < at[4])
    cosine_tab, sine_tab = cosine[...], sine[...]
    group_size = HQ // HK
    for group in range(HK):
        matrix = weight[group].reshape(first_in.shape[1], -1)
        qkv = dot(first_in, matrix)
        at_key = group_size * HD
        key = turned(qkv[:, at_key : at_key + HD], cosine_tab, sine_tab).astype(jnp.bfloat16)
        value = qkv[:, at_key + HD :].astype(jnp.bfloat16)
        key_ref[:, group * HD : (group + 1) * HD] = key
        value_ref[:, group * HD : (group + 1) * HD] = value
        for member in range(group_size):
            head = group * group_size + member
            here = slice(head * HD, (head + 1) * HD)
            query = turned(qkv[:, member * HD : (member + 1) * HD], cosine_tab, sine_tab)
            query = query.astype(jnp.bfloat16)
            query_ref[:, here] = query
            scores = dot(query, key, ((1,), (1,)))
            scores = jnp.where(allowed, scores * HD ** (-0.5), -1e30)
            weights = jnp.exp(scores - jnp.max(scores, axis=-1, keepdims=True))
            prob = weights * (1.0 / jnp.sum(weights, axis=-1, keepdims=True))
            prob = prob.astype(jnp.bfloat16)
            prob_ref[head] = prob
            out_ref[:, here] = dot(prob, value).astype(jnp.bfloat16)
        here = pl.ds(group * group_size, group_size)
        copies.append(
            pltpu.make_async_copy(prob_ref.at[here], prob_out.at[here], sems.at[group])
        )
        copies[-1].start()
    for copy in copies:
        copy.wait()


def project_kernel(at, tokens, gain, attended, *refs):
    resid_ref, second_ref, weight_out, weight, sem = refs[8:]
    place_pieces(at, refs[:8], weight)
    copy = pltpu.make_async_copy(weight, weight_out, sem)
    copy.start()
    heads = attended[...]
    halves = [dot(heads, weight[half].reshape(heads.shape[1], -1)) for half in range(2)]
    resid = tokens[...].astype(jnp.float32) + jnp.concatenate(halves, axis=1)
    resid_ref[...] = resid
    second_ref[...] = rms_kernel(resid, gain[...])
    copy.wait()


def one_hot(slots, capacity, dtype):
    shape = (capacity, slots.shape[1])
    return (slots == lax.broadcasted_iota(jnp.int32, shape, 0)).astype(jnp.float32).astype(dtype)


def slots_of(ids, expert, start, rows):
    named = jnp.any(ids[:, start : start + rows] == expert, axis=0, keepdims=True)
    named = named.astype(jnp.float32)
    before = lax.broadcasted_iota(jnp.int32, (rows, rows), 0)
    upto = lax.broadcasted_iota(jnp.int32, (rows, rows), 1)
    counts = dot(named.astype(jnp.bfloat16), (before <= upto).astype(jnp.float32).astype(jnp.bfloat16))
    return jnp.where(named > 0.0, counts - 1.0, -1.0).astype(jnp.int32)


def spread(picks, capacity, rows, outs):
    rows = rows.astype(jnp.bfloat16)
    block = picks[0].shape[1]
    for n in range(len(picks) // 2):
        for part in range(2):
            pick = picks[2 * n + part]
            at_row = (2 * n + part) * capacity
            tokens = dot(pick, rows[at_row : at_row + capacity], ((0,), (0,)))
            outs[n][part * block : (part + 1) * block] = tokens.astype(jnp.bfloat16)


def expert_kernel(capacity, pieces, earlier, at, ids, router, *refs):
    count = len(pieces)
    second, cot = refs[:count], refs[count : 2 * count]
    gate_w, up_w, down_w = refs[2 * count : 2 * count + 3]
    before = refs[2 * count + 3 : 2 * count + 3 + 2 * earlier]
    refs = refs[2 * count + 3 + 2 * earlier :]
    rows_in, rows_cot, gated_ref, gate_back, up_back, gates_ref = refs[:6]
    backs, gate_rows = refs[6 : 6 + count], refs[-1]
    f32, bf16 = jnp.float32, jnp.bfloat16
    length, width = second[0].shape
    wide = router.shape[1]
    half = length // 2
    picks = []
    experts = lax.broadcasted_iota(jnp.int32, (wide, length), 0)
    for n, piece in enumerate(pieces):
        tokens = second[n][...]
        named = ids[:, piece * length : (piece + 1) * length]
        chosen = functools.reduce(
            jnp.logical_or, [named[k : k + 1] == experts for k in range(named.shape[0])]
        )
        logits = jnp.where(chosen, dot(router[...], tokens, ((0,), (1,))), -1e30)
        weights = jnp.exp(logits - jnp.max(logits, axis=0, keepdims=True))
        gates = weights * (1.0 / jnp.sum(weights, axis=0, keepdims=True))
        if n == 0:
            gates_ref[...] = gates
        own = jnp.sum(jnp.where(experts == at[5], gates, 0.0), axis=0, keepdims=True)
        for part in range(2):
            here = slice(part * half, (part + 1) * half)
            place = slice((2 * n + part) * capacity, (2 * n + part + 1) * capacity)
            slots = slots_of(ids, at[5], piece * length + part * half, half)
            pick = one_hot(slots, capacity, f32)
            picks.append(pick.astype(bf16))
            rows_in[place] = dot(picks[-1], tokens[here]).astype(bf16)
            rows_cot[place] = dot(picks[-1], cot[n][here]).astype(bf16)
            gate_rows[place] = jnp.sum(pick * own[:, here], axis=1, keepdims=True)
    gate = gate_rows[...]
    gate_pre = dot(rows_in[...], gate_w[...])
    up_pre = dot(rows_in[...], up_w[...])
    cot_hidden = dot(rows_cot[...], down_w[...], ((1,), (1,)))
    scale = math.sqrt(2.0 / math.pi)
    square = gate_pre * gate_pre
    bent = jnp.tanh(scale * gate_pre * (1.0 + 0.044715 * square))
    open_part = 0.5 * (1.0 + bent)
    active = gate_pre * open_part
    slope = open_part + 0.5 * gate_pre * (1.0 - bent * bent) * scale * (
        1.0 + 3 * 0.044715 * square
    )
    hidden = active * up_pre
    gated_ref[...] = (gate * hidden).astype(bf16)
    signal = jnp.sum(hidden * cot_hidden, axis=1, keepdims=True)
    back = gate * cot_hidden
    gate_back[...] = (back * up_pre * slope).astype(bf16)
    up_back[...] = (back * active).astype(bf16)
    high = signal.astype(bf16)
    low = (signal - high.astype(f32)).astype(bf16)
    lanes = lax.broadcasted_iota(jnp.int32, (signal.shape[0], wide), 1)
    signal = jnp.where(lanes == at[5], high.astype(f32), 0.0)
    signal = jnp.where(lanes == at[5] + wide // 2, low.astype(f32), signal)
    by_rows = ((1,), (1,))
    rows = dot(gate_back[...], gate_w[...], by_rows) + dot(up_back[...], up_w[...], by_rows)
    spread(picks, capacity, jnp.concatenate([rows, signal], axis=1), backs)
    if earlier:
        lefts = [ref[...] for ref in (*before[:earlier], rows_cot)]
        rights = [ref[...] for ref in (*before[earlier:], gated_ref)]
        total = dot(jnp.concatenate(lefts, axis=0), jnp.concatenate(rights, axis=0), ((0,), (0,)))
        refs[6 + count][...] = total.astype(bf16)


def run_expert(pieces, at, ids, router, weights, second, cot, capacity, before=()):
    count = len(pieces)
    rows, wide = 2 * count * capacity, router.shape[1]
    (length, width), hidden = second[0].shape, weights[0].shape[1]
    bf16, f32 = jnp.bfloat16, jnp.float32
    outs = [(rows, width)] * 2 + [(rows, hidden)] * 3
    outs = [(shape, bf16) for shape in outs] + [((wide, length), f32)]
    outs = outs + [((length, width + wide), bf16)] * count
    if before:
        outs = outs + [((width, hidden), bf16)]
    return run_kernel(
        functools.partial(expert_kernel, capacity, pieces, len(before) // 2),
        4 * count,
        at,
        (ids, router, *second, *cot, *weights, *before),
        outs,
        4 + 3 * count + 4 * bool(before),
        [pltpu.VMEM((rows, 1), f32)],
    )


def mixture_kernel(capacity, groups, at, ids, *refs):
    gated, down_w, outs = refs[: len(groups)], refs[len(groups)], refs[len(groups) + 1 :]
    length = outs[0].shape[0]
    for pieces, rows in zip(groups, gated):
        picks = []
        for piece in pieces:
            for part in range(2):
                start = piece * length + part * length // 2
                slots = slots_of(ids, at[5], start, length // 2)
                picks.append(one_hot(slots, capacity, jnp.bfloat16))
        spread(picks, capacity, dot(rows[...], down_w[...]), [outs[piece] for piece in pieces])


def row_sum_kernel(parts, at, *refs):
    arrays = [
        jnp.concatenate([ref[...] for ref in refs[n : n + parts]], axis=0)
        for n in range(0, len(refs) - len(refs) // (parts + 1), parts)
    ]
    outs = refs[len(arrays) * parts :]
    for out, right in zip(outs, arrays[1:]):
        out[...] = dot(arrays[0], right, ((0,), (0,))).astype(jnp.bfloat16)


def row_sums(at, left, *rights):
    operands = [part for parts in (left, *rights) for part in parts]
    outs = [((left[0].shape[1], right[0].shape[1]), jnp.bfloat16) for right in rights]
    kernel = functools.partial(row_sum_kernel, len(left))
    return run_kernel(kernel, 4 * len(rights), at, operands, outs, 24 if len(rights) == 1 else 56)


def branch_back_kernel(
    at, near, far, first_x, first_y, last_y, last_x, resid, gain, second, gates, router, cot, weight, *outs
):
    resid_grad_ref, branch_ref, attended_ref, router_ref, gain_ref = outs
    f32, bf16 = jnp.float32, jnp.bfloat16
    halves = [first_x[...].astype(f32) + last_y[...], first_y[...].astype(f32) + last_x[...]]
    total = near[...].astype(f32) + far[...] + jnp.concatenate(halves, axis=0)
    width = resid.shape[1]
    signal = total[:, width:]
    signal = signal + pltpu.roll(signal, signal.shape[1] // 2, 1)
    chosen = gates[...].T
    logit_grad = chosen * (signal - jnp.sum(chosen * signal, axis=-1, keepdims=True))
    logit_grad = logit_grad.astype(bf16)
    second_grad = total[:, :width] + dot(logit_grad, router[...], ((1,), (1,)))
    norm_grad, gain_grad = rms_back(resid[...], gain[...], second_grad)
    gain_ref[...] = gain_grad
    resid_grad = cot[...].astype(f32) + norm_grad
    resid_grad_ref[...] = resid_grad
    branch = resid_grad.astype(bf16)
    branch_ref[...] = branch
    wide = weight.shape[2]
    attended_ref[...] = (
        dot(branch[:, :wide], weight[0], ((1,), (1,)))
        + dot(branch[:, wide:], weight[1], ((1,), (1,)))
    ).astype(bf16)
    router_ref[...] = dot(second[...], logit_grad, ((0,), (0,)))


def attend_back_kernel(
    at, attended, probs, queries, keys, values, cosine, sine, branch, back_ref
):
    f32, bf16 = jnp.float32, jnp.bfloat16
    cosine_tab, sine_tab = cosine[...], -sine[...]
    group_size = HQ // HK
    places, length = back_ref.shape[0], branch.shape[0]
    branch_width = branch.shape[1] // places
    width = back_ref.shape[2] - branch_width
    for place in range(places):
        here = slice(place * branch_width, (place + 1) * branch_width)
        back_ref[place, :length, width:] = branch[:, here]
        back_ref[place, length:] = jnp.zeros((back_ref.shape[1] - length, back_ref.shape[2]), bf16)
    scale = HD ** (-0.5)

    def put(position, block):
        back_ref[position // width, :length, position % width : position % width + HD] = block

    for group in range(HK):
        own = slice(group * HD, (group + 1) * HD)
        key, value = keys[:, own], values[:, own]
        key_grad = value_grad = 0.0
        start = group * (group_size + 2) * HD
        for member in range(group_size):
            head = group * group_size + member
            here = slice(head * HD, (head + 1) * HD)
            out_grad, query, prob = attended[:, here], queries[:, here], probs[head]
            prob_grad = dot(out_grad, value, ((1,), (1,)))
            prob_f = prob.astype(f32)
            inner = jnp.sum(prob_f * prob_grad, axis=-1, keepdims=True)
            score_grad = (prob_f * (prob_grad - inner)).astype(bf16)
            query_grad = turned(dot(score_grad, key) * scale, cosine_tab, sine_tab)
            put(start + member * HD, query_grad.astype(bf16))
            key_grad = key_grad + dot(score_grad, query, ((0,), (0,)))
            value_grad = value_grad + dot(prob, out_grad, ((0,), (0,)))
        key_grad = turned(key_grad * scale, cosine_tab, sine_tab)
        put(start + group_size * HD, key_grad.astype(bf16))
        put(start + (group_size + 1) * HD, value_grad.astype(bf16))


def first_back_kernel(at, back, weight, tokens, gain, resid_grad, tokens_ref, gain_ref):
    f32 = jnp.float32
    parts = back.shape[0]
    cols = weight.shape[0] * weight.shape[2] // parts
    first_grad = 0.0
    for part in range(parts):
        group, place = divmod(part * cols, weight.shape[2])
        first_grad = first_grad + dot(
            back[part, : tokens.shape[0], :cols], weight[group, :, place : place + cols], ((1,), (1,))
        )
    norm_grad, gain_grad = rms_back(tokens[...].astype(f32), gain[...], first_grad)
    gain_ref[...] = gain_grad
    tokens_ref[...] = (resid_grad[...] + norm_grad).astype(jnp.bfloat16)


def dense_grad_kernel(at, back, *refs):
    pieces, out_ref, held, sems = refs[:8], refs[8], refs[9], refs[10]
    copies = [
        pltpu.make_async_copy(piece, held.at[n], sems.at[n]) for n, piece in enumerate(pieces)
    ]
    for copy in copies:
        copy.start()
    depth, rows, cols = out_ref.shape
    length = held.shape[1] // 2
    qkv_width = cols - held.shape[2] // back.shape[0]
    narrow = sum(back[place, length:].astype(jnp.float32) for place in range(back.shape[0]))
    sums = [0.0, 0.0]
    for n, copy in enumerate(copies):
        copy.wait()
        dc, dy, dx = n // 4, n // 2 % 2, n % 2
        place = 4 * (at[0] ^ dy) + 2 * (at[1] ^ dc) + (at[2] ^ dx)
        own = back[place, :length]
        sums[0] = sums[0] + dot(held[n, length:], own[:, :qkv_width], ((0,), (0,)))
        sums[1] = sums[1] + dot(held[n, :length], own[:, qkv_width:], ((0,), (0,)))
    wide = held.shape[2] // depth
    each = 4
    for z in range(depth):
        here = slice(z * wide, (z + 1) * wide)
        both = jnp.concatenate([part[here] for part in sums], axis=1)
        out_ref[z, :wide] = both.astype(jnp.bfloat16)
        kept = [narrow[z * each : (z + 1) * each], jnp.zeros((rows - wide - each, cols), jnp.float32)]
        out_ref[z, wide:] = jnp.concatenate(kept, axis=0).astype(jnp.bfloat16)


def finish_kernel(at, sums, query_ref, key_ref, value_ref, output_ref):
    places, _, cols = sums.shape
    rows, out_width = query_ref.shape[0], output_ref.shape[1] // places
    width = cols - out_width
    for place in range(places):
        block = sums[place, :rows].astype(jnp.float32)
        output_ref[:, place * out_width : (place + 1) * out_width] = block[:, width:]
        for at_col in range(0, width, HD):
            group, head = divmod((place * width + at_col) // HD, HQ // HK + 2)
            part = block[:, at_col : at_col + HD]
            if head < HQ // HK:
                start = (group * (HQ // HK) + head) * HD
                query_ref[:, start : start + HD] = part
            elif head == HQ // HK:
                key_ref[:, group * HD : (group + 1) * HD] = part
            else:
                value_ref[:, group * HD : (group + 1) * HD] = part


def local_pairs(
    tokens,
    norm1_gain,
    w_query,
    w_key,
    w_value,
    w_out,
    norm2_gain,
    w_router,
    w_gate,
    w_up,
    w_down,
    expert_ids,
    prefix_len,
    out_grad,
):
    bf16, f32 = jnp.bfloat16, jnp.float32
    length, model_width = tokens.shape
    shard_rows = w_query.shape[0]
    local_count, _, hidden_width = w_gate.shape
    owners = lax.axis_size("x")
    depth = lax.axis_size("z")
    plane = lax.axis_size(PLANE)
    experts_all = w_router.shape[1]
    block_rows = length // MICRO
    capacity = 3 * block_rows * expert_ids.shape[1] // (2 * experts_all)
    plane_rows = plane * length
    blocks = plane_rows // block_rows
    q_cols, kv_cols = w_query.shape[1], w_key.shape[1]
    qkv_cols = q_cols + 2 * kv_cols
    q_group, out_half = q_cols // HK, model_width // 2
    y, c, x, z = (lax.axis_index(axis) for axis in ("y", "c", "x", "z"))
    own_local = 2 * y + c
    own_expert = x * local_count + own_local
    at = jnp.stack([y, c, x, z, prefix_len[0], own_expert, own_local])

    own_half = jnp.concatenate(
        [
            lax.dynamic_slice_in_dim(part, x * (part.shape[1] // 2), part.shape[1] // 2, 1)
            for part in (w_query, w_key, w_value, w_out)
        ],
        axis=1,
    )
    narrow = jnp.concatenate([w_router, norm1_gain[:, None], norm2_gain[:, None]], axis=1)
    narrow = jnp.pad(narrow, ((0, 0), (0, 128 - narrow.shape[1])))
    router_w = small_group_gather(narrow)
    ids_all = small_gather(expert_ids.T)
    column = [own_half] + shifts(own_half)
    cot_sides = plane_sides(after(out_grad, router_w, ids_all))
    qkv_half = qkv_cols // 2
    qkv_column = jnp.stack([part[:, :qkv_half] for part in column])
    out_column = jnp.stack([part[:, qkv_half:] for part in column])
    qkv_column, out_column = lax.optimization_barrier((qkv_column, out_column, *cot_sides))[:2]
    sliced = after(own_local, column[-1])
    gate_w, up_w, down_w = (
        lax.dynamic_index_in_dim(weight, sliced, 0, keepdims=False)
        for weight in (w_gate, w_up, w_down)
    )
    qkv_sides = plane_sides(qkv_column)
    gains = router_w[:, experts_all : experts_all + 2].T.astype(f32)
    gain_one, gain_two = gains[:1], gains[1:]
    qkv_corner = plane_corner(qkv_sides, (gate_w, up_w, down_w, gain_one, gain_two))
    out_sides = plane_sides(after(out_column, *qkv_sides))
    qkv_pieces = plane_pieces(qkv_column, qkv_sides, qkv_corner)
    cosine_tab, sine_tab = angles(length, HD)
    cosine_all = jnp.concatenate([cosine_tab, cosine_tab], axis=2)[:, 0]
    sine_all = jnp.concatenate([-sine_tab, sine_tab], axis=2)[:, 0]
    weight_lead = (2, depth, 2, 2, shard_rows)
    first_in, queries, keys_rot, values_b, attended, probs, qkv_w = run_kernel(
        attend_kernel,
        11,
        at,
        (tokens, gain_one, cosine_all, sine_all, *qkv_pieces),
        [
            ((length, model_width), bf16),
            ((length, q_cols), bf16),
            ((length, kv_cols), bf16),
            ((length, kv_cols), bf16),
            ((length, q_cols), bf16),
            ((HQ, length, length), bf16),
            (weight_lead + (qkv_half,), bf16),
        ],
        28,
        [
            pltpu.VMEM((HQ, length, length), bf16),
            pltpu.VMEM(weight_lead + (qkv_half,), bf16),
            pltpu.SemaphoreType.DMA((HK + 1,)),
        ],
        hbm_out=2,
    )
    out_sides = lax.optimization_barrier((*out_sides, attended))[:2]
    out_corner = plane_corner(out_sides)
    cot_corner = plane_corner(cot_sides)
    out_pieces = plane_pieces(out_column, out_sides, out_corner)
    cot_pieces = plane_pieces(out_grad, cot_sides, cot_corner)
    resid, second_in, output_w = run_kernel(
        project_kernel,
        4,
        at,
        (tokens, after(gain_two, cot_corner), attended, *out_pieces),
        [
            ((length, model_width), f32),
            ((length, model_width), bf16),
            (weight_lead + (out_half,), bf16),
        ],
        44,
        [pltpu.VMEM(weight_lead + (out_half,), bf16), pltpu.SemaphoreType.DMA],
        hbm_out=1,
    )
    qkv_w = qkv_w.reshape(HK, model_width, qkv_half)
    output_w = output_w.reshape(2, q_cols, out_half)

    expert = functools.partial(
        run_expert,
        at=at,
        ids=ids_all,
        router=router_w,
        weights=(gate_w, up_w, down_w),
        capacity=capacity,
    )
    second_sides = plane_sides(second_in)
    groups = ((0, 4), (1, 5, 2, 6), (3, 7))
    second_pieces = {0: second_in, 4: swap(second_in, "c")}

    def run_group(pieces, before=()):
        return expert(
            pieces,
            before=before,
            second=[second_pieces[piece] for piece in pieces],
            cot=[cot_pieces[piece] for piece in pieces],
        )

    stage_own = run_group(groups[0])
    second_sides = lax.optimization_barrier((*second_sides, stage_own[0]))[:2]
    for piece, block in zip((1, 2), second_sides):
        second_pieces[piece], second_pieces[piece + 4] = block, swap(block, "c")
    stage_sides = run_group(groups[1])
    second_corner = plane_corner(second_sides, later=(stage_sides[0],))
    second_pieces[3], second_pieces[7] = second_corner, swap(second_corner, "c")
    own_near, own_far = stage_own[6:]
    own_far = swap(own_far, "c")
    x_near, x_far, y_near, y_far = stage_sides[6:]
    back_x, back_y = over_core(x_near, x_far), over_core(y_near, y_far)
    first_x, first_y = early_sums(back_x, back_y)
    two = (stage_own, stage_sides)
    stage_corner = run_group(groups[2], [stage[1] for stage in two] + [stage[2] for stage in two])
    *stage_corner, down_part = stage_corner
    corner = over_core(*stage_corner[6:])
    passed = corner_first(corner)
    stages = (stage_own, stage_sides, stage_corner)
    rows_in, rows_cot, gated, gate_back, up_back = ([stage[n] for stage in stages] for n in range(5))
    gates = stage_own[5]
    last_y, last_x = corner_last(back_x, back_y, passed)[:2]
    down_sum = scatter_sum(down_part, "z")

    resid_grad, branch_grad, attended_grad, router_acc, gain_two_grad = run_kernel(
        branch_back_kernel,
        6,
        at,
        (
            own_near,
            own_far,
            first_x,
            first_y,
            last_y,
            last_x,
            resid,
            gain_two,
            second_in,
            gates,
            router_w,
            out_grad,
            output_w,
        ),
        [
            ((length, model_width), f32),
            ((length, model_width), bf16),
            ((length, q_cols), bf16),
            ((model_width, 128), f32),
            ((1, model_width), f32),
        ],
        56,
    )
    gate_part, up_part = row_sums(
        at, [after(rows_in[0], resid_grad)] + rows_in[1:], gate_back, up_back
    )
    gate_sum, up_sum = scatter_sum(gate_part, "z"), scatter_sum(up_part, "z")
    attended_grad = after(attended_grad, gate_part)
    qkv_width, branch_width = qkv_cols // plane, model_width // plane
    dense_cols = qkv_width + branch_width
    (back_cols,) = run_kernel(
        attend_back_kernel,
        6,
        at,
        (
            attended_grad,
            probs,
            queries,
            keys_rot,
            values_b,
            cosine_all,
            sine_all,
            branch_grad,
        ),
        [((plane, length + 16, dense_cols), bf16)],
        56,
    )
    both = jnp.concatenate(
        lax.optimization_barrier((attended, first_in, last_y, last_x))[:2], axis=0
    )
    both_sides = plane_sides(both)
    *both_sides, tokens_late = lax.optimization_barrier((*both_sides, tokens))
    tokens_grad, gain_one_grad = run_kernel(
        first_back_kernel,
        5,
        at,
        (back_cols, qkv_w, tokens_late, gain_one, resid_grad),
        [((length, model_width), bf16), ((1, model_width), f32)],
        24,
    )

    narrow_part = jnp.concatenate(
        [router_acc[:, :experts_all], gain_one_grad.T, gain_two_grad.T], axis=1
    )
    narrow_cols = -(-narrow_part.shape[1] // owners) * owners
    narrow_part = jnp.pad(narrow_part, ((0, 0), (0, narrow_cols - narrow_part.shape[1])))
    narrow_part = jnp.transpose(
        narrow_part.reshape(depth, 2, 2, shard_rows, owners, narrow_cols // owners),
        (1, 2, 4, 0, 3, 5),
    ).reshape(plane, depth, shard_rows * narrow_cols // owners)
    narrow_len = narrow_part.shape[2]
    narrow_rows = -(-narrow_len // dense_cols)
    each_rows = -(-narrow_rows // 4) * 4
    narrow_part = jnp.pad(
        narrow_part, ((0, 0), (0, 0), (0, each_rows * dense_cols - narrow_len))
    ).reshape(plane, depth * each_rows, dense_cols)
    narrow_part = jnp.pad(
        narrow_part.astype(bf16), ((0, 0), (0, 16 - depth * each_rows), (0, 0))
    )
    back_cols = lax.dynamic_update_slice(back_cols, narrow_part, (0, length, 0))
    back_cols = exchange(after(back_cols, down_sum, *both_sides), PLANE)
    shares = run_kernel(
        functools.partial(mixture_kernel, capacity, groups),
        10,
        at,
        (ids_all, after(gated[0], *both_sides), *gated[1:], down_w),
        [((length, model_width), bf16)] * plane,
        56,
    )
    sides, shares = lax.optimization_barrier((both_sides, shares))
    both_corner = plane_corner(sides, (back_cols,))
    both_pieces = plane_pieces(both, both_sides, both_corner)
    def placed(total):
        total = exchange(total, ("y", "c"))
        return total.reshape(local_count, shard_rows, hidden_width).astype(f32)

    down_grad, gate_grad = placed(down_sum), placed(gate_sum)
    kept_rows = -(-narrow_rows // 16) * 16
    wide_rows = local_count * shard_rows
    dense_shape = (depth, wide_rows + kept_rows, dense_cols)
    dense_part = pl.pallas_call(
        dense_grad_kernel,
        out_shape=jax.ShapeDtypeStruct(dense_shape, bf16),
        in_specs=[SCALARS, WHOLE] + [IN_HBM] * 8,
        out_specs=WHOLE,
        scratch_shapes=[
            pltpu.VMEM((plane, 2 * length, model_width), bf16),
            pltpu.SemaphoreType.DMA((plane,)),
        ],
        cost_estimate=cost(8),
        compiler_params=pltpu.CompilerParams(vmem_limit_bytes=32 * 2**20),
    )(at, back_cols, *both_pieces)
    mixed = [over_core(near, far) for near, far in zip(shares[:4], shares[4:])]
    dense_part, up_sum, mixed = lax.optimization_barrier((dense_part, up_sum, mixed))
    dense_sum = scatter_sum(dense_part.reshape(-1, dense_cols), "z")
    early = early_sums(mixed[1], mixed[2])
    first, down_grad, gate_grad = lax.optimization_barrier(
        (corner_first(mixed[3]), down_grad, gate_grad)
    )
    last, up_grad = lax.optimization_barrier(
        (corner_last(mixed[1], mixed[2], first)[:2], placed(up_sum))
    )
    mixture = jnp.concatenate(
        [left.astype(f32) + right.astype(f32) for left, right in zip(early, last)], axis=0
    )
    block_out = (resid + (mixture + mixed[0].astype(f32))).astype(bf16)

    wide_sum = dense_sum[: local_count * shard_rows].reshape(2, 2, 1, shard_rows, dense_cols)
    wide_sum = jnp.broadcast_to(wide_sum, (2, 2, owners, shard_rows, dense_cols)).reshape(
        plane, shard_rows, dense_cols
    )
    narrow_sum = dense_sum[local_count * shard_rows :][:narrow_rows]
    narrow_sum = jnp.broadcast_to(narrow_sum[None], (plane, narrow_rows, dense_cols))
    pad_rows = -(shard_rows + narrow_rows) % 16
    padding = jnp.zeros((plane, pad_rows, dense_cols), bf16)
    dense_sum = exchange(jnp.concatenate([wide_sum, narrow_sum, padding], axis=1), PLANE)
    query_grad, key_grad, value_grad, output_grad = run_kernel(
        finish_kernel,
        2,
        at,
        (dense_sum,),
        [
            ((shard_rows, q_cols), f32),
            ((shard_rows, kv_cols), f32),
            ((shard_rows, kv_cols), f32),
            ((shard_rows, model_width), f32),
        ],
    )
    narrow_sum = dense_sum[:, shard_rows : shard_rows + narrow_rows].reshape(
        2, 2, owners, narrow_rows * dense_cols
    )
    narrow_sum = narrow_sum[y, c, :, :narrow_len].reshape(owners, shard_rows, -1)
    narrow_sum = jnp.moveaxis(narrow_sum, 0, 1).reshape(shard_rows, narrow_cols).astype(f32)

    return (
        block_out,
        tokens_grad,
        narrow_sum[:, experts_all],
        query_grad,
        key_grad,
        value_grad,
        output_grad,
        narrow_sum[:, experts_all + 1],
        narrow_sum[:, :experts_all],
        gate_grad,
        up_grad,
        jnp.swapaxes(down_grad, 1, 2),
    )


def solution(mesh):
    groups, owners = mesh.shape["dp"], mesh.shape["expert"]
    grid = jax.sharding.Mesh(
        mesh.devices.reshape(groups // 4, 2, 2, owners), ("z", "y", "c", "x")
    )
    rows = P(("z", "y", "c", "x"), None)
    shard, shard_rows = P(GROUP), P(GROUP, None)
    expert = P("x", None, None)
    return jax.shard_map(
        local_pairs if owners == 2 else local_wide,
        mesh=grid,
        in_specs=(
            rows,
            shard,
            shard_rows,
            shard_rows,
            shard_rows,
            shard_rows,
            shard,
            shard_rows,
            expert,
            expert,
            expert,
            rows,
            P(("z", "y", "c", "x")),
            rows,
        ),
        out_specs=(
            rows,
            rows,
            shard,
            shard_rows,
            shard_rows,
            shard_rows,
            shard_rows,
            shard,
            shard_rows,
            P("x", GROUP, None),
            P("x", GROUP, None),
            P("x", None, GROUP),
        ),
        check_vma=False,
    )
```

```python
import functools
import math

import jax
import jax.numpy as jnp
from jax import lax
from jax.experimental import pallas as pl
from jax.experimental.pallas import tpu as pltpu
from jax.sharding import PartitionSpec as P

HQ = 12
HK = 2
HD = 128
MICRO = 2
PLANE = ("y", "c", "x")
GROUP = ("z", "y", "c")


def rms_scale(values, gain_vec):
    inverse = lax.rsqrt(jnp.mean(values * values, axis=-1, keepdims=True) + 1e-06)
    return values * inverse * gain_vec


def angles(length, head_size):
    positions = jnp.arange(length).astype(jnp.float32)
    freq_rates = jnp.exp(
        -(2.0 * jnp.arange(head_size // 2).astype(jnp.float32) / head_size) * math.log(1000000.0)
    )
    angle_tab = positions[:, None] * freq_rates[None, :]
    return (jnp.cos(angle_tab)[:, None, :], jnp.sin(angle_tab)[:, None, :])


def rotary(values, cosine_tab, sine_tab):
    half_dim = values.shape[-1] // 2
    first_half = values[..., :half_dim]
    second_half = values[..., half_dim:]
    return jnp.concatenate(
        [
            first_half * cosine_tab - second_half * sine_tab,
            second_half * cosine_tab + first_half * sine_tab,
        ],
        axis=-1,
    )


def expert_act(gate_pre, up_pre):
    return jax.nn.gelu(gate_pre, approximate=True) * up_pre


def left_product(left_mat, right_mat):
    return lax.dot_general(
        left_mat, right_mat, (((0,), (0,)), ((), ())), preferred_element_type=jnp.float32
    )


def gather(block, axes):
    return lax.all_gather(block, axes, axis=0, tiled=True)


def exchange(block, axes):
    return lax.all_to_all(block, axes, split_axis=0, concat_axis=0, tiled=True)


def scatter_sum(block, axes):
    return lax.psum_scatter(block, axes, scatter_dimension=0, tiled=True)


def by_owner(cols, parts):
    rows, total = cols.shape
    return jnp.moveaxis(cols.reshape(rows, parts, total // parts), 1, 0).reshape(
        parts * rows, total // parts
    )


def local_wide(
    tokens,
    norm1_gain,
    w_query,
    w_key,
    w_value,
    w_out,
    norm2_gain,
    w_router,
    w_gate,
    w_up,
    w_down,
    expert_ids,
    prefix_len,
    out_grad,
):
    bf16, f32 = jnp.bfloat16, jnp.float32
    length, model_width = tokens.shape
    shard_rows = w_query.shape[0]
    local_count, _, hidden_width = w_gate.shape
    owners = lax.axis_size("x")
    depth = lax.axis_size("z")
    plane = lax.axis_size(PLANE)
    experts_all = w_router.shape[1]
    top_count = expert_ids.shape[1]
    block_rows = length // MICRO
    capacity = 3 * block_rows * top_count // (2 * experts_all)
    plane_rows = plane * length
    blocks = plane_rows // block_rows
    group_size = HQ // HK
    score_scale = HD ** (-0.5)
    q_cols, kv_cols = w_query.shape[1], w_key.shape[1]
    own_local = lax.axis_index(("y", "c"))
    own_expert = lax.axis_index("x") * local_count + own_local
    own_place = lax.axis_index(PLANE)

    narrow = jnp.concatenate([w_router, norm1_gain[:, None], norm2_gain[:, None]], axis=1)
    narrow = jnp.pad(narrow, ((0, 0), (0, -narrow.shape[1] % 128)))
    packed = gather(jnp.concatenate([w_query, w_key, w_value, narrow], axis=1), GROUP)
    qkv_cols = q_cols + 2 * kv_cols
    qkv_w = packed[:, :qkv_cols]
    router_w = packed[:, qkv_cols : qkv_cols + experts_all]
    gains = packed[:, qkv_cols + experts_all : qkv_cols + experts_all + 2].T.astype(f32)
    gain_one, gain_two = gains[0], gains[1]
    output_w = gather(w_out, GROUP)

    ids_all = gather(expert_ids, PLANE)
    cot_all = gather(out_grad, PLANE)
    chosen_mask = jnp.any(
        ids_all[:, :, None] == jnp.arange(experts_all, dtype=jnp.int32)[None, None, :], axis=1
    )
    own_mask = jnp.any(ids_all == own_expert, axis=1).reshape(blocks, block_rows)
    place = jnp.cumsum(own_mask.astype(jnp.int32), axis=1) - 1
    dispatch = (
        own_mask[:, None, :]
        & (place[:, None, :] == jnp.arange(capacity, dtype=jnp.int32)[None, :, None])
    ).astype(bf16)

    cosine_tab, sine_tab = angles(length, HD)
    inputs_f = tokens.astype(f32)
    first_in = rms_scale(inputs_f, gain_one).astype(bf16)
    qkv = jnp.dot(first_in, qkv_w, preferred_element_type=f32)
    queries = (
        rotary(qkv[:, :q_cols].reshape(length, HQ, HD), cosine_tab, sine_tab)
        .astype(bf16)
        .reshape(length, HK, group_size, HD)
    )
    keys_rot = rotary(
        qkv[:, q_cols : q_cols + kv_cols].reshape(length, HK, HD), cosine_tab, sine_tab
    ).astype(bf16)
    values_b = qkv[:, q_cols + kv_cols :].astype(bf16).reshape(length, HK, HD)
    positions = jnp.arange(length)
    allowed = (positions[None, :] <= positions[:, None]) | (positions[None, :] < prefix_len[0])

    def masked_scores():
        scores = jnp.einsum("ihrd,jhd->hrij", queries, keys_rot, preferred_element_type=f32)
        return jnp.where(allowed, scores * score_scale, -1e30)

    masked = masked_scores()
    row_peak = jnp.max(masked, axis=-1, keepdims=True)
    log_total = row_peak + jnp.log(jnp.sum(jnp.exp(masked - row_peak), axis=-1, keepdims=True))
    prob_bf = jnp.exp(masked - log_total).astype(bf16)
    attended = jnp.einsum("hrij,jhd->ihrd", prob_bf, values_b, preferred_element_type=f32)
    attended = attended.reshape(length, HQ * HD).astype(bf16)
    resid = inputs_f + jnp.dot(attended, output_w, preferred_element_type=f32)
    second_in = rms_scale(resid, gain_two).astype(bf16)

    second_all = gather(second_in, PLANE)
    logits = jnp.dot(second_all, router_w, preferred_element_type=f32)
    gates_all = jax.nn.softmax(jnp.where(chosen_mask, logits, -jnp.inf), axis=-1)
    own_gates = lax.dynamic_index_in_dim(gates_all, own_expert, 1, keepdims=False)
    own_gates = own_gates.reshape(blocks, block_rows)
    gate_rows = jnp.einsum(
        "bct,bt->bc", dispatch.astype(f32), own_gates, precision=lax.Precision.HIGHEST
    )[:, :, None]
    gate_w = lax.dynamic_index_in_dim(w_gate, own_local, 0, keepdims=False)
    up_w = lax.dynamic_index_in_dim(w_up, own_local, 0, keepdims=False)
    down_w = lax.dynamic_index_in_dim(w_down, own_local, 0, keepdims=False)

    def to_rows(array):
        return jnp.einsum(
            "bct,btd->bcd",
            dispatch,
            array.reshape(blocks, block_rows, model_width),
            preferred_element_type=f32,
        ).astype(bf16)

    def to_tokens(rows):
        return (
            jnp.einsum("bct,bcd->btd", dispatch, rows.astype(bf16), preferred_element_type=f32)
            .astype(bf16)
            .reshape(plane_rows, model_width)
        )

    rows_in = to_rows(second_all)
    rows_cot = to_rows(cot_all)
    gate_pre = jnp.einsum("bcd,df->bcf", rows_in, gate_w, preferred_element_type=f32)
    up_pre = jnp.einsum("bcd,df->bcf", rows_in, up_w, preferred_element_type=f32)
    hidden, act_pull = jax.vjp(expert_act, gate_pre, up_pre)
    gated = (gate_rows * hidden).astype(bf16)
    down_part = jnp.einsum("bcd,bcf->df", rows_cot, gated, preferred_element_type=f32)
    down_sum = scatter_sum(down_part.astype(bf16), "z")
    cot_hidden = jnp.einsum("bcd,fd->bcf", rows_cot, down_w, preferred_element_type=f32)
    gate_signal_rows = jnp.sum(hidden * cot_hidden, axis=-1)
    gate_pgrad, up_pgrad = act_pull(gate_rows * cot_hidden)
    gate_pgrad = gate_pgrad.astype(bf16)
    up_pgrad = up_pgrad.astype(bf16)
    gate_part = jnp.einsum("bcd,bcf->df", rows_in, gate_pgrad, preferred_element_type=f32)
    gate_sum = scatter_sum(gate_part.astype(bf16), "z")
    up_part = jnp.einsum("bcd,bcf->df", rows_in, up_pgrad, preferred_element_type=f32)
    up_sum = scatter_sum(up_part.astype(bf16), "z")
    rows_grad = jnp.einsum("bcf,df->bcd", gate_pgrad, gate_w, preferred_element_type=f32)
    rows_grad = rows_grad + jnp.einsum("bcf,df->bcd", up_pgrad, up_w, preferred_element_type=f32)
    second_back = scatter_sum(to_tokens(rows_grad), PLANE).astype(f32)
    gate_signal = jnp.einsum(
        "bct,bc->bt", dispatch.astype(f32), gate_signal_rows, precision=lax.Precision.HIGHEST
    )
    gate_signal = exchange(gate_signal.reshape(plane, length), PLANE)
    gate_signal = jnp.transpose(
        gate_signal.reshape(local_count, owners, length), (2, 1, 0)
    ).reshape(length, experts_all)
    expert_rows = jnp.einsum("bcf,fd->bcd", gated, down_w, preferred_element_type=f32)
    mixture = scatter_sum(to_tokens(expert_rows), PLANE).astype(f32)
    block_out = (resid + mixture).astype(bf16)

    cotangent = out_grad.astype(f32)
    gate_probs = lax.dynamic_slice_in_dim(gates_all, own_place * length, length, 0)
    logit_grad = (
        gate_probs
        * (gate_signal - jnp.sum(gate_probs * gate_signal, axis=-1, keepdims=True))
    ).astype(bf16)
    router_acc = left_product(second_in, logit_grad)
    second_grad = second_back + jnp.dot(logit_grad, router_w.T, preferred_element_type=f32)
    _, norm_two_pull = jax.vjp(rms_scale, resid, gain_two)
    resid_norm_grad, gain_two_grad = norm_two_pull(second_grad)
    resid_grad = cotangent + resid_norm_grad
    branch_grad = resid_grad.astype(bf16)

    attended_all = gather(attended, PLANE)
    branch_cols = exchange(by_owner(branch_grad, plane), PLANE)
    output_part = left_product(attended_all, branch_cols)
    attended_grad = jnp.dot(branch_grad, output_w.T, preferred_element_type=f32).astype(bf16)
    attended_grad = attended_grad.reshape(length, HK, group_size, HD)
    masked = masked_scores()
    prob_full = jnp.exp(masked - log_total)
    prob_bf = prob_full.astype(bf16)
    prob_grad = jnp.einsum("ihrd,jhd->hrij", attended_grad, values_b, preferred_element_type=f32)
    row_inner = jnp.sum(prob_full * prob_grad, axis=-1, keepdims=True)
    score_grad = (prob_full * (prob_grad - row_inner)).astype(bf16)
    query_rot_grad = (
        jnp.einsum("hrij,jhd->ihrd", score_grad, keys_rot, preferred_element_type=f32)
        * score_scale
    )
    query_back = rotary(query_rot_grad.reshape(length, HQ, HD), cosine_tab, -sine_tab)
    query_back = query_back.astype(bf16).reshape(length, HQ * HD)
    key_rot_grad = (
        jnp.einsum("hrij,ihrd->jhd", score_grad, queries, preferred_element_type=f32)
        * score_scale
    )
    key_back = rotary(key_rot_grad, cosine_tab, -sine_tab).astype(bf16).reshape(length, HK * HD)
    value_back = jnp.einsum("hrij,ihrd->jhd", prob_bf, attended_grad, preferred_element_type=f32)
    value_back = value_back.astype(bf16).reshape(length, HK * HD)
    qkv_back = jnp.concatenate([query_back, key_back, value_back], axis=1)
    first_all = gather(first_in, PLANE)
    qkv_part = left_product(first_all, exchange(by_owner(qkv_back, plane), PLANE))
    first_grad = lax.dot_general(
        qkv_back, qkv_w, (((1,), (1,)), ((), ())), preferred_element_type=f32
    )
    _, norm_one_pull = jax.vjp(rms_scale, inputs_f, gain_one)
    input_norm_grad, gain_one_grad = norm_one_pull(first_grad)
    tokens_grad = (resid_grad + input_norm_grad).astype(bf16)

    narrow_part = jnp.concatenate(
        [router_acc, gain_one_grad[:, None], gain_two_grad[:, None]], axis=1
    ).astype(bf16)
    narrow_cols = narrow_part.shape[1]
    narrow_sum = lax.psum(scatter_sum(narrow_part, GROUP), "x").astype(f32)
    dense_part = jnp.concatenate([qkv_part, output_part], axis=1).astype(bf16)
    dense_sum = scatter_sum(dense_part, "z")
    dense_cols = dense_sum.shape[1]
    dense_sum = gather(dense_sum, PLANE).reshape(plane, local_count, shard_rows, dense_cols)
    dense_sum = lax.dynamic_index_in_dim(dense_sum, own_local, 1, keepdims=False).astype(f32)
    dense_sum = jnp.moveaxis(dense_sum, 0, 1)
    qkv_width = qkv_cols // plane
    qkv_sum = dense_sum[:, :, :qkv_width].reshape(shard_rows, qkv_cols)
    output_sum = dense_sum[:, :, qkv_width:].reshape(shard_rows, model_width)

    def placed(total):
        total = exchange(total, ("y", "c"))
        return total.reshape(local_count, shard_rows, hidden_width).astype(f32)

    return (
        block_out,
        tokens_grad,
        narrow_sum[:, experts_all],
        qkv_sum[:, :q_cols],
        qkv_sum[:, q_cols : q_cols + kv_cols],
        qkv_sum[:, q_cols + kv_cols :],
        output_sum,
        narrow_sum[:, experts_all + 1],
        narrow_sum[:, :experts_all],
        placed(gate_sum),
        placed(up_sum),
        jnp.swapaxes(placed(down_sum), 1, 2),
    )


def rounded(values):
    return lax.reduce_precision(values, 8, 7).astype(jnp.bfloat16)


def after(block, *others):
    return lax.optimization_barrier((block,) + others)[0]


def swap(block, axis):
    return lax.ppermute(block, axis, [(0, 1), (1, 0)])


def shifts(block):
    depth = lax.axis_size("z")
    return [
        lax.ppermute(block, "z", [(i, (i + k) % depth) for i in range(depth)])
        for k in range(1, depth)
    ]


def plane_sides(block):
    return swap(block, "x"), swap(block, "y")


def plane_corner(sides, before=(), later=()):
    over_x, over_y = sides
    half = over_x.shape[0] // 2
    over_y, over_x = lax.optimization_barrier((over_y[:half], over_x[half:]) + before)[:2]
    parts = (swap(over_y, "x"), swap(over_x, "y"))
    return jnp.concatenate(lax.optimization_barrier(parts + later)[:2], axis=0)


def plane_pieces(block, sides=None, corner=None):
    sides = plane_sides(block) if sides is None else sides
    corner = plane_corner(sides) if corner is None else corner
    pieces = [block, *sides, corner]
    return pieces + [swap(piece, "c") for piece in pieces]


def small_gather(block):
    for axis in ("x", "y", "c"):
        block = jnp.concatenate([block, swap(block, axis)], axis=1)
    return block


def small_group_gather(block):
    depth = lax.axis_size("z")
    order = jnp.stack(([block] + shifts(block))[::-1] * 2)
    start = (depth - 1 - lax.axis_index("z")) % depth
    total = lax.dynamic_slice_in_dim(order, start, depth, 0)[:, None, None]
    for dim, axis in ((1, "y"), (2, "c")):
        other = swap(total, axis)
        last = lax.axis_index(axis) == 1
        pair = [jnp.where(last, other, total), jnp.where(last, total, other)]
        total = jnp.concatenate(pair, axis=dim)
    return total.reshape(-1, block.shape[1])


def add(left, right):
    return rounded(left.astype(jnp.float32) + right.astype(jnp.float32))


def over_core(near, far):
    return add(near, swap(far, "c"))


def early_sums(over_x, over_y):
    half = over_x.shape[0] // 2
    return swap(over_x[:half], "x"), swap(over_y[half:], "y")


def corner_first(corner):
    half = corner.shape[0] // 2
    return swap(corner[:half], "x"), swap(corner[half:], "y")


def corner_last(over_x, over_y, first):
    half = over_x.shape[0] // 2
    over_y, over_x = add(over_y[:half], first[0]), add(over_x[half:], first[1])
    return swap(over_y, "y"), swap(over_x, "x"), over_y, over_x


def cost(micros):
    return pl.CostEstimate(flops=micros * 10**9, bytes_accessed=micros * 10**6, transcendentals=0)


def dot(left, right, dims=((1,), (0,)), precision=None):
    return lax.dot_general(
        left, right, (dims, ((), ())), precision=precision, preferred_element_type=jnp.float32
    )


WHOLE = pl.BlockSpec(memory_space=pltpu.VMEM)
IN_HBM = pl.BlockSpec(memory_space=pltpu.HBM)
SCALARS = pl.BlockSpec(memory_space=pltpu.SMEM)


def run_kernel(kernel, micros, at, operands, outs, megabytes=16, scratch=(), hbm_in=0, hbm_out=0):
    return pl.pallas_call(
        kernel,
        out_shape=[jax.ShapeDtypeStruct(shape, dtype) for shape, dtype in outs],
        in_specs=[SCALARS] + [WHOLE] * (len(operands) - hbm_in) + [IN_HBM] * hbm_in,
        out_specs=[WHOLE] * (len(outs) - hbm_out) + [IN_HBM] * hbm_out,
        scratch_shapes=scratch,
        cost_estimate=cost(micros),
        compiler_params=pltpu.CompilerParams(vmem_limit_bytes=megabytes * 2**20),
    )(at, *operands)


def place_pieces(at, refs, weight):
    depth = weight.shape[1]
    for n, ref in enumerate(refs):
        dc, dy, dx = n // 4, n // 2 % 2, n % 2
        for k in range(depth):
            z = lax.rem(at[3] + depth - k, depth)
            weight[at[2] ^ dx, z, at[0] ^ dy, at[1] ^ dc] = ref[k]


def rms_kernel(values, gain):
    inverse = lax.rsqrt(jnp.mean(values * values, axis=-1, keepdims=True) + 1e-06)
    return (values * inverse * gain).astype(jnp.bfloat16)


def rms_back(values, gain, grad):
    inverse = lax.rsqrt(jnp.mean(values * values, axis=-1, keepdims=True) + 1e-06)
    normed = values * inverse
    gain_grad = jnp.sum(grad * normed, axis=0, keepdims=True)
    grad = grad * gain
    along = jnp.mean(grad * normed, axis=-1, keepdims=True)
    return inverse * (grad - normed * along), gain_grad


def turned(values, cosine_tab, sine_tab):
    return values * cosine_tab + pltpu.roll(values, HD // 2, 1) * sine_tab


def attend_kernel(at, tokens, gain, cosine, sine, *refs):
    first_ref, query_ref, key_ref, value_ref, out_ref = refs[8:13]
    prob_out, weight_out, prob_ref, weight, sems = refs[13:]
    place_pieces(at, refs[:8], weight)
    copies = [pltpu.make_async_copy(weight, weight_out, sems.at[HK])]
    copies[0].start()
    length = tokens.shape[0]
    first_in = rms_kernel(tokens[...].astype(jnp.float32), gain[...])
    first_ref[...] = first_in
    rows = lax.broadcasted_iota(jnp.int32, (length, length), 0)
    cols = lax.broadcasted_iota(jnp.int32, (length, length), 1)
    allowed = (cols <= rows) | (cols < at[4])
    cosine_tab, sine_tab = cosine[...], sine[...]
    group_size = HQ // HK
    for group in range(HK):
        matrix = weight[group].reshape(first_in.shape[1], -1)
        qkv = dot(first_in, matrix)
        at_key = group_size * HD
        key = turned(qkv[:, at_key : at_key + HD], cosine_tab, sine_tab).astype(jnp.bfloat16)
        value = qkv[:, at_key + HD :].astype(jnp.bfloat16)
        key_ref[:, group * HD : (group + 1) * HD] = key
        value_ref[:, group * HD : (group + 1) * HD] = value
        for member in range(group_size):
            head = group * group_size + member
            here = slice(head * HD, (head + 1) * HD)
            query = turned(qkv[:, member * HD : (member + 1) * HD], cosine_tab, sine_tab)
            query = query.astype(jnp.bfloat16)
            query_ref[:, here] = query
            scores = dot(query, key, ((1,), (1,)))
            scores = jnp.where(allowed, scores * HD ** (-0.5), -1e30)
            weights = jnp.exp(scores - jnp.max(scores, axis=-1, keepdims=True))
            prob = weights * (1.0 / jnp.sum(weights, axis=-1, keepdims=True))
            prob = prob.astype(jnp.bfloat16)
            prob_ref[head] = prob
            out_ref[:, here] = dot(prob, value).astype(jnp.bfloat16)
        here = pl.ds(group * group_size, group_size)
        copies.append(
            pltpu.make_async_copy(prob_ref.at[here], prob_out.at[here], sems.at[group])
        )
        copies[-1].start()
    for copy in copies:
        copy.wait()


def project_kernel(at, tokens, gain, attended, *refs):
    resid_ref, second_ref, weight_out, weight, sem = refs[8:]
    place_pieces(at, refs[:8], weight)
    copy = pltpu.make_async_copy(weight, weight_out, sem)
    copy.start()
    heads = attended[...]
    halves = [dot(heads, weight[half].reshape(heads.shape[1], -1)) for half in range(2)]
    resid = tokens[...].astype(jnp.float32) + jnp.concatenate(halves, axis=1)
    resid_ref[...] = resid
    second_ref[...] = rms_kernel(resid, gain[...])
    copy.wait()


def one_hot(slots, capacity, dtype):
    shape = (capacity, slots.shape[1])
    return (slots == lax.broadcasted_iota(jnp.int32, shape, 0)).astype(jnp.float32).astype(dtype)


def slots_of(ids, expert, start, rows):
    named = jnp.any(ids[:, start : start + rows] == expert, axis=0, keepdims=True)
    named = named.astype(jnp.float32)
    before = lax.broadcasted_iota(jnp.int32, (rows, rows), 0)
    upto = lax.broadcasted_iota(jnp.int32, (rows, rows), 1)
    counts = dot(named.astype(jnp.bfloat16), (before <= upto).astype(jnp.float32).astype(jnp.bfloat16))
    return jnp.where(named > 0.0, counts - 1.0, -1.0).astype(jnp.int32)


def spread(picks, capacity, rows, outs):
    rows = rows.astype(jnp.bfloat16)
    block = picks[0].shape[1]
    for n in range(len(picks) // 2):
        for part in range(2):
            pick = picks[2 * n + part]
            at_row = (2 * n + part) * capacity
            tokens = dot(pick, rows[at_row : at_row + capacity], ((0,), (0,)))
            outs[n][part * block : (part + 1) * block] = tokens.astype(jnp.bfloat16)


def expert_kernel(capacity, pieces, earlier, at, ids, router, *refs):
    count = len(pieces)
    second, cot = refs[:count], refs[count : 2 * count]
    gate_w, up_w, down_w = refs[2 * count : 2 * count + 3]
    before = refs[2 * count + 3 : 2 * count + 3 + 2 * earlier]
    refs = refs[2 * count + 3 + 2 * earlier :]
    rows_in, rows_cot, gated_ref, gate_back, up_back, gates_ref = refs[:6]
    backs, gate_rows = refs[6 : 6 + count], refs[-1]
    f32, bf16 = jnp.float32, jnp.bfloat16
    length, width = second[0].shape
    wide = router.shape[1]
    half = length // 2
    picks = []
    experts = lax.broadcasted_iota(jnp.int32, (wide, length), 0)
    for n, piece in enumerate(pieces):
        tokens = second[n][...]
        named = ids[:, piece * length : (piece + 1) * length]
        chosen = functools.reduce(
            jnp.logical_or, [named[k : k + 1] == experts for k in range(named.shape[0])]
        )
        logits = jnp.where(chosen, dot(router[...], tokens, ((0,), (1,))), -1e30)
        weights = jnp.exp(logits - jnp.max(logits, axis=0, keepdims=True))
        gates = weights * (1.0 / jnp.sum(weights, axis=0, keepdims=True))
        if n == 0:
            gates_ref[...] = gates
        own = jnp.sum(jnp.where(experts == at[5], gates, 0.0), axis=0, keepdims=True)
        for part in range(2):
            here = slice(part * half, (part + 1) * half)
            place = slice((2 * n + part) * capacity, (2 * n + part + 1) * capacity)
            slots = slots_of(ids, at[5], piece * length + part * half, half)
            pick = one_hot(slots, capacity, f32)
            picks.append(pick.astype(bf16))
            rows_in[place] = dot(picks[-1], tokens[here]).astype(bf16)
            rows_cot[place] = dot(picks[-1], cot[n][here]).astype(bf16)
            gate_rows[place] = jnp.sum(pick * own[:, here], axis=1, keepdims=True)
    gate = gate_rows[...]
    gate_pre = dot(rows_in[...], gate_w[...])
    up_pre = dot(rows_in[...], up_w[...])
    cot_hidden = dot(rows_cot[...], down_w[...], ((1,), (1,)))
    scale = math.sqrt(2.0 / math.pi)
    square = gate_pre * gate_pre
    bent = jnp.tanh(scale * gate_pre * (1.0 + 0.044715 * square))
    open_part = 0.5 * (1.0 + bent)
    active = gate_pre * open_part
    slope = open_part + 0.5 * gate_pre * (1.0 - bent * bent) * scale * (
        1.0 + 3 * 0.044715 * square
    )
    hidden = active * up_pre
    gated_ref[...] = (gate * hidden).astype(bf16)
    signal = jnp.sum(hidden * cot_hidden, axis=1, keepdims=True)
    back = gate * cot_hidden
    gate_back[...] = (back * up_pre * slope).astype(bf16)
    up_back[...] = (back * active).astype(bf16)
    high = signal.astype(bf16)
    low = (signal - high.astype(f32)).astype(bf16)
    lanes = lax.broadcasted_iota(jnp.int32, (signal.shape[0], wide), 1)
    signal = jnp.where(lanes == at[5], high.astype(f32), 0.0)
    signal = jnp.where(lanes == at[5] + wide // 2, low.astype(f32), signal)
    by_rows = ((1,), (1,))
    rows = dot(gate_back[...], gate_w[...], by_rows) + dot(up_back[...], up_w[...], by_rows)
    spread(picks, capacity, jnp.concatenate([rows, signal], axis=1), backs)
    if earlier:
        lefts = [ref[...] for ref in (*before[:earlier], rows_cot)]
        rights = [ref[...] for ref in (*before[earlier:], gated_ref)]
        total = dot(jnp.concatenate(lefts, axis=0), jnp.concatenate(rights, axis=0), ((0,), (0,)))
        refs[6 + count][...] = total.astype(bf16)


def run_expert(pieces, at, ids, router, weights, second, cot, capacity, before=()):
    count = len(pieces)
    rows, wide = 2 * count * capacity, router.shape[1]
    (length, width), hidden = second[0].shape, weights[0].shape[1]
    bf16, f32 = jnp.bfloat16, jnp.float32
    outs = [(rows, width)] * 2 + [(rows, hidden)] * 3
    outs = [(shape, bf16) for shape in outs] + [((wide, length), f32)]
    outs = outs + [((length, width + wide), bf16)] * count
    if before:
        outs = outs + [((width, hidden), bf16)]
    return run_kernel(
        functools.partial(expert_kernel, capacity, pieces, len(before) // 2),
        4 * count,
        at,
        (ids, router, *second, *cot, *weights, *before),
        outs,
        4 + 3 * count + 4 * bool(before),
        [pltpu.VMEM((rows, 1), f32)],
    )


def mixture_kernel(capacity, groups, at, ids, *refs):
    gated, down_w, outs = refs[: len(groups)], refs[len(groups)], refs[len(groups) + 1 :]
    length = outs[0].shape[0]
    for pieces, rows in zip(groups, gated):
        picks = []
        for piece in pieces:
            for part in range(2):
                start = piece * length + part * length // 2
                slots = slots_of(ids, at[5], start, length // 2)
                picks.append(one_hot(slots, capacity, jnp.bfloat16))
        spread(picks, capacity, dot(rows[...], down_w[...]), [outs[piece] for piece in pieces])


def row_sum_kernel(parts, at, *refs):
    arrays = [
        jnp.concatenate([ref[...] for ref in refs[n : n + parts]], axis=0)
        for n in range(0, len(refs) - len(refs) // (parts + 1), parts)
    ]
    outs = refs[len(arrays) * parts :]
    for out, right in zip(outs, arrays[1:]):
        out[...] = dot(arrays[0], right, ((0,), (0,))).astype(jnp.bfloat16)


def row_sums(at, left, *rights):
    operands = [part for parts in (left, *rights) for part in parts]
    outs = [((left[0].shape[1], right[0].shape[1]), jnp.bfloat16) for right in rights]
    kernel = functools.partial(row_sum_kernel, len(left))
    return run_kernel(kernel, 4 * len(rights), at, operands, outs, 24 if len(rights) == 1 else 56)


def branch_back_kernel(
    at, near, far, first_x, first_y, last_y, last_x, resid, gain, second, gates, router, cot, weight, *outs
):
    resid_grad_ref, branch_ref, attended_ref, router_ref, gain_ref = outs
    f32, bf16 = jnp.float32, jnp.bfloat16
    halves = [first_x[...].astype(f32) + last_y[...], first_y[...].astype(f32) + last_x[...]]
    total = near[...].astype(f32) + far[...] + jnp.concatenate(halves, axis=0)
    width = resid.shape[1]
    signal = total[:, width:]
    signal = signal + pltpu.roll(signal, signal.shape[1] // 2, 1)
    chosen = gates[...].T
    logit_grad = chosen * (signal - jnp.sum(chosen * signal, axis=-1, keepdims=True))
    logit_grad = logit_grad.astype(bf16)
    second_grad = total[:, :width] + dot(logit_grad, router[...], ((1,), (1,)))
    norm_grad, gain_grad = rms_back(resid[...], gain[...], second_grad)
    gain_ref[...] = gain_grad
    resid_grad = cot[...].astype(f32) + norm_grad
    resid_grad_ref[...] = resid_grad
    branch = resid_grad.astype(bf16)
    branch_ref[...] = branch
    wide = weight.shape[2]
    attended_ref[...] = (
        dot(branch[:, :wide], weight[0], ((1,), (1,)))
        + dot(branch[:, wide:], weight[1], ((1,), (1,)))
    ).astype(bf16)
    router_ref[...] = dot(second[...], logit_grad, ((0,), (0,)))


def attend_back_kernel(
    at, attended, probs, queries, keys, values, cosine, sine, branch, back_ref
):
    f32, bf16 = jnp.float32, jnp.bfloat16
    cosine_tab, sine_tab = cosine[...], -sine[...]
    group_size = HQ // HK
    places, length = back_ref.shape[0], branch.shape[0]
    branch_width = branch.shape[1] // places
    width = back_ref.shape[2] - branch_width
    for place in range(places):
        here = slice(place * branch_width, (place + 1) * branch_width)
        back_ref[place, :length, width:] = branch[:, here]
        back_ref[place, length:] = jnp.zeros((back_ref.shape[1] - length, back_ref.shape[2]), bf16)
    scale = HD ** (-0.5)

    def put(position, block):
        back_ref[position // width, :length, position % width : position % width + HD] = block

    for group in range(HK):
        own = slice(group * HD, (group + 1) * HD)
        key, value = keys[:, own], values[:, own]
        key_grad = value_grad = 0.0
        start = group * (group_size + 2) * HD
        for member in range(group_size):
            head = group * group_size + member
            here = slice(head * HD, (head + 1) * HD)
            out_grad, query, prob = attended[:, here], queries[:, here], probs[head]
            prob_grad = dot(out_grad, value, ((1,), (1,)))
            prob_f = prob.astype(f32)
            inner = jnp.sum(prob_f * prob_grad, axis=-1, keepdims=True)
            score_grad = (prob_f * (prob_grad - inner)).astype(bf16)
            query_grad = turned(dot(score_grad, key) * scale, cosine_tab, sine_tab)
            put(start + member * HD, query_grad.astype(bf16))
            key_grad = key_grad + dot(score_grad, query, ((0,), (0,)))
            value_grad = value_grad + dot(prob, out_grad, ((0,), (0,)))
        key_grad = turned(key_grad * scale, cosine_tab, sine_tab)
        put(start + group_size * HD, key_grad.astype(bf16))
        put(start + (group_size + 1) * HD, value_grad.astype(bf16))


def first_back_kernel(at, back, weight, tokens, gain, resid_grad, tokens_ref, gain_ref):
    f32 = jnp.float32
    parts = back.shape[0]
    cols = weight.shape[0] * weight.shape[2] // parts
    first_grad = 0.0
    for part in range(parts):
        group, place = divmod(part * cols, weight.shape[2])
        first_grad = first_grad + dot(
            back[part, : tokens.shape[0], :cols], weight[group, :, place : place + cols], ((1,), (1,))
        )
    norm_grad, gain_grad = rms_back(tokens[...].astype(f32), gain[...], first_grad)
    gain_ref[...] = gain_grad
    tokens_ref[...] = (resid_grad[...] + norm_grad).astype(jnp.bfloat16)


def dense_grad_kernel(at, back, *refs):
    pieces, out_ref, held, sems = refs[:8], refs[8], refs[9], refs[10]
    copies = [
        pltpu.make_async_copy(piece, held.at[n], sems.at[n]) for n, piece in enumerate(pieces)
    ]
    for copy in copies:
        copy.start()
    depth, rows, cols = out_ref.shape
    length = held.shape[1] // 2
    qkv_width = cols - held.shape[2] // back.shape[0]
    narrow = sum(back[place, length:].astype(jnp.float32) for place in range(back.shape[0]))
    sums = [0.0, 0.0]
    for n, copy in enumerate(copies):
        copy.wait()
        dc, dy, dx = n // 4, n // 2 % 2, n % 2
        place = 4 * (at[0] ^ dy) + 2 * (at[1] ^ dc) + (at[2] ^ dx)
        own = back[place, :length]
        sums[0] = sums[0] + dot(held[n, length:], own[:, :qkv_width], ((0,), (0,)))
        sums[1] = sums[1] + dot(held[n, :length], own[:, qkv_width:], ((0,), (0,)))
    wide = held.shape[2] // depth
    each = 4
    for z in range(depth):
        here = slice(z * wide, (z + 1) * wide)
        both = jnp.concatenate([part[here] for part in sums], axis=1)
        out_ref[z, :wide] = both.astype(jnp.bfloat16)
        kept = [narrow[z * each : (z + 1) * each], jnp.zeros((rows - wide - each, cols), jnp.float32)]
        out_ref[z, wide:] = jnp.concatenate(kept, axis=0).astype(jnp.bfloat16)


def finish_kernel(at, sums, query_ref, key_ref, value_ref, output_ref):
    places, _, cols = sums.shape
    rows, out_width = query_ref.shape[0], output_ref.shape[1] // places
    width = cols - out_width
    for place in range(places):
        block = sums[place, :rows].astype(jnp.float32)
        output_ref[:, place * out_width : (place + 1) * out_width] = block[:, width:]
        for at_col in range(0, width, HD):
            group, head = divmod((place * width + at_col) // HD, HQ // HK + 2)
            part = block[:, at_col : at_col + HD]
            if head < HQ // HK:
                start = (group * (HQ // HK) + head) * HD
                query_ref[:, start : start + HD] = part
            elif head == HQ // HK:
                key_ref[:, group * HD : (group + 1) * HD] = part
            else:
                value_ref[:, group * HD : (group + 1) * HD] = part


def local_pairs(
    tokens,
    norm1_gain,
    w_query,
    w_key,
    w_value,
    w_out,
    norm2_gain,
    w_router,
    w_gate,
    w_up,
    w_down,
    expert_ids,
    prefix_len,
    out_grad,
):
    bf16, f32 = jnp.bfloat16, jnp.float32
    length, model_width = tokens.shape
    shard_rows = w_query.shape[0]
    local_count, _, hidden_width = w_gate.shape
    owners = lax.axis_size("x")
    depth = lax.axis_size("z")
    plane = lax.axis_size(PLANE)
    experts_all = w_router.shape[1]
    block_rows = length // MICRO
    capacity = 3 * block_rows * expert_ids.shape[1] // (2 * experts_all)
    plane_rows = plane * length
    blocks = plane_rows // block_rows
    q_cols, kv_cols = w_query.shape[1], w_key.shape[1]
    qkv_cols = q_cols + 2 * kv_cols
    q_group, out_half = q_cols // HK, model_width // 2
    y, c, x, z = (lax.axis_index(axis) for axis in ("y", "c", "x", "z"))
    own_local = 2 * y + c
    own_expert = x * local_count + own_local
    at = jnp.stack([y, c, x, z, prefix_len[0], own_expert, own_local])

    own_half = jnp.concatenate(
        [
            lax.dynamic_slice_in_dim(part, x * (part.shape[1] // 2), part.shape[1] // 2, 1)
            for part in (w_query, w_key, w_value, w_out)
        ],
        axis=1,
    )
    narrow = jnp.concatenate([w_router, norm1_gain[:, None], norm2_gain[:, None]], axis=1)
    narrow = jnp.pad(narrow, ((0, 0), (0, 128 - narrow.shape[1])))
    router_w = small_group_gather(narrow)
    ids_all = small_gather(expert_ids.T)
    column = [own_half] + shifts(own_half)
    cot_sides = plane_sides(after(out_grad, router_w, ids_all))
    qkv_half = qkv_cols // 2
    qkv_column = jnp.stack([part[:, :qkv_half] for part in column])
    out_column = jnp.stack([part[:, qkv_half:] for part in column])
    qkv_column, out_column = lax.optimization_barrier((qkv_column, out_column, *cot_sides))[:2]
    sliced = after(own_local, column[-1])
    gate_w, up_w, down_w = (
        lax.dynamic_index_in_dim(weight, sliced, 0, keepdims=False)
        for weight in (w_gate, w_up, w_down)
    )
    qkv_sides = plane_sides(qkv_column)
    gains = router_w[:, experts_all : experts_all + 2].T.astype(f32)
    gain_one, gain_two = gains[:1], gains[1:]
    qkv_corner = plane_corner(qkv_sides, (gate_w, up_w, down_w, gain_one, gain_two))
    out_sides = plane_sides(after(out_column, *qkv_sides))
    qkv_pieces = plane_pieces(qkv_column, qkv_sides, qkv_corner)
    cosine_tab, sine_tab = angles(length, HD)
    cosine_all = jnp.concatenate([cosine_tab, cosine_tab], axis=2)[:, 0]
    sine_all = jnp.concatenate([-sine_tab, sine_tab], axis=2)[:, 0]
    weight_lead = (2, depth, 2, 2, shard_rows)
    first_in, queries, keys_rot, values_b, attended, probs, qkv_w = run_kernel(
        attend_kernel,
        11,
        at,
        (tokens, gain_one, cosine_all, sine_all, *qkv_pieces),
        [
            ((length, model_width), bf16),
            ((length, q_cols), bf16),
            ((length, kv_cols), bf16),
            ((length, kv_cols), bf16),
            ((length, q_cols), bf16),
            ((HQ, length, length), bf16),
            (weight_lead + (qkv_half,), bf16),
        ],
        28,
        [
            pltpu.VMEM((HQ, length, length), bf16),
            pltpu.VMEM(weight_lead + (qkv_half,), bf16),
            pltpu.SemaphoreType.DMA((HK + 1,)),
        ],
        hbm_out=2,
    )
    out_sides = lax.optimization_barrier((*out_sides, attended))[:2]
    out_corner = plane_corner(out_sides)
    cot_corner = plane_corner(cot_sides)
    out_pieces = plane_pieces(out_column, out_sides, out_corner)
    cot_pieces = plane_pieces(out_grad, cot_sides, cot_corner)
    resid, second_in, output_w = run_kernel(
        project_kernel,
        4,
        at,
        (tokens, after(gain_two, cot_corner), attended, *out_pieces),
        [
            ((length, model_width), f32),
            ((length, model_width), bf16),
            (weight_lead + (out_half,), bf16),
        ],
        44,
        [pltpu.VMEM(weight_lead + (out_half,), bf16), pltpu.SemaphoreType.DMA],
        hbm_out=1,
    )
    qkv_w = qkv_w.reshape(HK, model_width, qkv_half)
    output_w = output_w.reshape(2, q_cols, out_half)

    expert = functools.partial(
        run_expert,
        at=at,
        ids=ids_all,
        router=router_w,
        weights=(gate_w, up_w, down_w),
        capacity=capacity,
    )
    second_sides = plane_sides(second_in)
    groups = ((0, 4), (1, 5, 2, 6), (3, 7))
    second_pieces = {0: second_in, 4: swap(second_in, "c")}

    def run_group(pieces, before=()):
        return expert(
            pieces,
            before=before,
            second=[second_pieces[piece] for piece in pieces],
            cot=[cot_pieces[piece] for piece in pieces],
        )

    stage_own = run_group(groups[0])
    second_sides = lax.optimization_barrier((*second_sides, stage_own[0]))[:2]
    for piece, block in zip((1, 2), second_sides):
        second_pieces[piece], second_pieces[piece + 4] = block, swap(block, "c")
    stage_sides = run_group(groups[1])
    second_corner = plane_corner(second_sides, later=(stage_sides[0],))
    second_pieces[3], second_pieces[7] = second_corner, swap(second_corner, "c")
    own_near, own_far = stage_own[6:]
    own_far = swap(own_far, "c")
    x_near, x_far, y_near, y_far = stage_sides[6:]
    back_x, back_y = over_core(x_near, x_far), over_core(y_near, y_far)
    first_x, first_y = early_sums(back_x, back_y)
    two = (stage_own, stage_sides)
    stage_corner = run_group(groups[2], [stage[1] for stage in two] + [stage[2] for stage in two])
    *stage_corner, down_part = stage_corner
    corner = over_core(*stage_corner[6:])
    passed = corner_first(corner)
    stages = (stage_own, stage_sides, stage_corner)
    rows_in, rows_cot, gated, gate_back, up_back = ([stage[n] for stage in stages] for n in range(5))
    gates = stage_own[5]
    last_y, last_x = corner_last(back_x, back_y, passed)[:2]
    down_sum = scatter_sum(down_part, "z")

    resid_grad, branch_grad, attended_grad, router_acc, gain_two_grad = run_kernel(
        branch_back_kernel,
        6,
        at,
        (
            own_near,
            own_far,
            first_x,
            first_y,
            last_y,
            last_x,
            resid,
            gain_two,
            second_in,
            gates,
            router_w,
            out_grad,
            output_w,
        ),
        [
            ((length, model_width), f32),
            ((length, model_width), bf16),
            ((length, q_cols), bf16),
            ((model_width, 128), f32),
            ((1, model_width), f32),
        ],
        56,
    )
    gate_part, up_part = row_sums(
        at, [after(rows_in[0], resid_grad)] + rows_in[1:], gate_back, up_back
    )
    gate_sum, up_sum = scatter_sum(gate_part, "z"), scatter_sum(up_part, "z")
    attended_grad = after(attended_grad, gate_part)
    qkv_width, branch_width = qkv_cols // plane, model_width // plane
    dense_cols = qkv_width + branch_width
    (back_cols,) = run_kernel(
        attend_back_kernel,
        6,
        at,
        (
            attended_grad,
            probs,
            queries,
            keys_rot,
            values_b,
            cosine_all,
            sine_all,
            branch_grad,
        ),
        [((plane, length + 16, dense_cols), bf16)],
        56,
    )
    tokens_grad, gain_one_grad = run_kernel(
        first_back_kernel,
        5,
        at,
        (back_cols, qkv_w, tokens, gain_one, resid_grad),
        [((length, model_width), bf16), ((1, model_width), f32)],
        24,
    )

    both = jnp.concatenate(
        lax.optimization_barrier((attended, first_in, last_y, last_x))[:2], axis=0
    )
    both_sides = plane_sides(both)
    narrow_part = jnp.concatenate(
        [router_acc[:, :experts_all], gain_one_grad.T, gain_two_grad.T], axis=1
    )
    narrow_cols = -(-narrow_part.shape[1] // owners) * owners
    narrow_part = jnp.pad(narrow_part, ((0, 0), (0, narrow_cols - narrow_part.shape[1])))
    narrow_part = jnp.transpose(
        narrow_part.reshape(depth, 2, 2, shard_rows, owners, narrow_cols // owners),
        (1, 2, 4, 0, 3, 5),
    ).reshape(plane, depth, shard_rows * narrow_cols // owners)
    narrow_len = narrow_part.shape[2]
    narrow_rows = -(-narrow_len // dense_cols)
    each_rows = -(-narrow_rows // 4) * 4
    narrow_part = jnp.pad(
        narrow_part, ((0, 0), (0, 0), (0, each_rows * dense_cols - narrow_len))
    ).reshape(plane, depth * each_rows, dense_cols)
    narrow_part = jnp.pad(
        narrow_part.astype(bf16), ((0, 0), (0, 16 - depth * each_rows), (0, 0))
    )
    back_cols = lax.dynamic_update_slice(back_cols, narrow_part, (0, length, 0))
    back_cols = exchange(after(back_cols, down_sum), PLANE)
    shares = run_kernel(
        functools.partial(mixture_kernel, capacity, groups),
        10,
        at,
        (ids_all, after(gated[0], *both_sides), *gated[1:], down_w),
        [((length, model_width), bf16)] * plane,
        56,
    )
    sides, shares = lax.optimization_barrier((both_sides, shares))
    both_corner = plane_corner(sides, (back_cols,))
    both_pieces = plane_pieces(both, both_sides, both_corner)
    def placed(total):
        total = exchange(total, ("y", "c"))
        return total.reshape(local_count, shard_rows, hidden_width).astype(f32)

    kept_rows = -(-narrow_rows // 16) * 16
    wide_rows = local_count * shard_rows
    dense_shape = (depth, wide_rows + kept_rows, dense_cols)
    dense_part = pl.pallas_call(
        dense_grad_kernel,
        out_shape=jax.ShapeDtypeStruct(dense_shape, bf16),
        in_specs=[SCALARS, WHOLE] + [IN_HBM] * 8,
        out_specs=WHOLE,
        scratch_shapes=[
            pltpu.VMEM((plane, 2 * length, model_width), bf16),
            pltpu.SemaphoreType.DMA((plane,)),
        ],
        cost_estimate=cost(8),
        compiler_params=pltpu.CompilerParams(vmem_limit_bytes=32 * 2**20),
    )(at, back_cols, *both_pieces)
    dense_part, down_sum, gate_sum, up_sum = lax.optimization_barrier(
        (dense_part, down_sum, gate_sum, up_sum)
    )
    down_grad, gate_grad = placed(down_sum), placed(gate_sum)
    dense_sum = scatter_sum(dense_part.reshape(-1, dense_cols), "z")
    mixed = [over_core(near, far) for near, far in zip(shares[:4], shares[4:])]
    early = early_sums(mixed[1], mixed[2])
    first, down_grad, gate_grad = lax.optimization_barrier(
        (corner_first(mixed[3]), down_grad, gate_grad)
    )
    last, up_grad = lax.optimization_barrier(
        (corner_last(mixed[1], mixed[2], first)[:2], placed(up_sum))
    )
    mixture = jnp.concatenate(
        [left.astype(f32) + right.astype(f32) for left, right in zip(early, last)], axis=0
    )
    block_out = (resid + (mixture + mixed[0].astype(f32))).astype(bf16)

    wide_sum = dense_sum[: local_count * shard_rows].reshape(2, 2, 1, shard_rows, dense_cols)
    wide_sum = jnp.broadcast_to(wide_sum, (2, 2, owners, shard_rows, dense_cols)).reshape(
        plane, shard_rows, dense_cols
    )
    narrow_sum = dense_sum[local_count * shard_rows :][:narrow_rows]
    narrow_sum = jnp.broadcast_to(narrow_sum[None], (plane, narrow_rows, dense_cols))
    pad_rows = -(shard_rows + narrow_rows) % 16
    padding = jnp.zeros((plane, pad_rows, dense_cols), bf16)
    dense_sum = exchange(jnp.concatenate([wide_sum, narrow_sum, padding], axis=1), PLANE)
    query_grad, key_grad, value_grad, output_grad = run_kernel(
        finish_kernel,
        2,
        at,
        (dense_sum,),
        [
            ((shard_rows, q_cols), f32),
            ((shard_rows, kv_cols), f32),
            ((shard_rows, kv_cols), f32),
            ((shard_rows, model_width), f32),
        ],
    )
    narrow_sum = dense_sum[:, shard_rows : shard_rows + narrow_rows].reshape(
        2, 2, owners, narrow_rows * dense_cols
    )
    narrow_sum = narrow_sum[y, c, :, :narrow_len].reshape(owners, shard_rows, -1)
    narrow_sum = jnp.moveaxis(narrow_sum, 0, 1).reshape(shard_rows, narrow_cols).astype(f32)

    return (
        block_out,
        tokens_grad,
        narrow_sum[:, experts_all],
        query_grad,
        key_grad,
        value_grad,
        output_grad,
        narrow_sum[:, experts_all + 1],
        narrow_sum[:, :experts_all],
        gate_grad,
        up_grad,
        jnp.swapaxes(down_grad, 1, 2),
    )


def solution(mesh):
    groups, owners = mesh.shape["dp"], mesh.shape["expert"]
    grid = jax.sharding.Mesh(
        mesh.devices.reshape(groups // 4, 2, 2, owners), ("z", "y", "c", "x")
    )
    rows = P(("z", "y", "c", "x"), None)
    shard, shard_rows = P(GROUP), P(GROUP, None)
    expert = P("x", None, None)
    return jax.shard_map(
        local_pairs if owners == 2 else local_wide,
        mesh=grid,
        in_specs=(
            rows,
            shard,
            shard_rows,
            shard_rows,
            shard_rows,
            shard_rows,
            shard,
            shard_rows,
            expert,
            expert,
            expert,
            rows,
            P(("z", "y", "c", "x")),
            rows,
        ),
        out_specs=(
            rows,
            rows,
            shard,
            shard_rows,
            shard_rows,
            shard_rows,
            shard_rows,
            shard,
            shard_rows,
            P("x", GROUP, None),
            P("x", GROUP, None),
            P("x", None, GROUP),
        ),
        check_vma=False,
    )
```

```python
import functools
import math

import jax
import jax.numpy as jnp
from jax import lax
from jax.experimental import pallas as pl
from jax.experimental.pallas import tpu as pltpu
from jax.sharding import PartitionSpec as P

HQ = 12
HK = 2
HD = 128
MICRO = 2
PLANE = ("y", "c", "x")
GROUP = ("z", "y", "c")


def rms_scale(values, gain_vec):
    inverse = lax.rsqrt(jnp.mean(values * values, axis=-1, keepdims=True) + 1e-06)
    return values * inverse * gain_vec


def angles(length, head_size):
    positions = jnp.arange(length).astype(jnp.float32)
    freq_rates = jnp.exp(
        -(2.0 * jnp.arange(head_size // 2).astype(jnp.float32) / head_size) * math.log(1000000.0)
    )
    angle_tab = positions[:, None] * freq_rates[None, :]
    return (jnp.cos(angle_tab)[:, None, :], jnp.sin(angle_tab)[:, None, :])


def rotary(values, cosine_tab, sine_tab):
    half_dim = values.shape[-1] // 2
    first_half = values[..., :half_dim]
    second_half = values[..., half_dim:]
    return jnp.concatenate(
        [
            first_half * cosine_tab - second_half * sine_tab,
            second_half * cosine_tab + first_half * sine_tab,
        ],
        axis=-1,
    )


def expert_act(gate_pre, up_pre):
    return jax.nn.gelu(gate_pre, approximate=True) * up_pre


def left_product(left_mat, right_mat):
    return lax.dot_general(
        left_mat, right_mat, (((0,), (0,)), ((), ())), preferred_element_type=jnp.float32
    )


def gather(block, axes):
    return lax.all_gather(block, axes, axis=0, tiled=True)


def exchange(block, axes):
    return lax.all_to_all(block, axes, split_axis=0, concat_axis=0, tiled=True)


def scatter_sum(block, axes):
    return lax.psum_scatter(block, axes, scatter_dimension=0, tiled=True)


def by_owner(cols, parts):
    rows, total = cols.shape
    return jnp.moveaxis(cols.reshape(rows, parts, total // parts), 1, 0).reshape(
        parts * rows, total // parts
    )


def local_wide(
    tokens,
    norm1_gain,
    w_query,
    w_key,
    w_value,
    w_out,
    norm2_gain,
    w_router,
    w_gate,
    w_up,
    w_down,
    expert_ids,
    prefix_len,
    out_grad,
):
    bf16, f32 = jnp.bfloat16, jnp.float32
    length, model_width = tokens.shape
    shard_rows = w_query.shape[0]
    local_count, _, hidden_width = w_gate.shape
    owners = lax.axis_size("x")
    depth = lax.axis_size("z")
    plane = lax.axis_size(PLANE)
    experts_all = w_router.shape[1]
    top_count = expert_ids.shape[1]
    block_rows = length // MICRO
    capacity = 3 * block_rows * top_count // (2 * experts_all)
    plane_rows = plane * length
    blocks = plane_rows // block_rows
    group_size = HQ // HK
    score_scale = HD ** (-0.5)
    q_cols, kv_cols = w_query.shape[1], w_key.shape[1]
    own_local = lax.axis_index(("y", "c"))
    own_expert = lax.axis_index("x") * local_count + own_local
    own_place = lax.axis_index(PLANE)

    narrow = jnp.concatenate([w_router, norm1_gain[:, None], norm2_gain[:, None]], axis=1)
    narrow = jnp.pad(narrow, ((0, 0), (0, -narrow.shape[1] % 128)))
    packed = gather(jnp.concatenate([w_query, w_key, w_value, narrow], axis=1), GROUP)
    qkv_cols = q_cols + 2 * kv_cols
    qkv_w = packed[:, :qkv_cols]
    router_w = packed[:, qkv_cols : qkv_cols + experts_all]
    gains = packed[:, qkv_cols + experts_all : qkv_cols + experts_all + 2].T.astype(f32)
    gain_one, gain_two = gains[0], gains[1]
    output_w = gather(w_out, GROUP)

    ids_all = gather(expert_ids, PLANE)
    cot_all = gather(out_grad, PLANE)
    chosen_mask = jnp.any(
        ids_all[:, :, None] == jnp.arange(experts_all, dtype=jnp.int32)[None, None, :], axis=1
    )
    own_mask = jnp.any(ids_all == own_expert, axis=1).reshape(blocks, block_rows)
    place = jnp.cumsum(own_mask.astype(jnp.int32), axis=1) - 1
    dispatch = (
        own_mask[:, None, :]
        & (place[:, None, :] == jnp.arange(capacity, dtype=jnp.int32)[None, :, None])
    ).astype(bf16)

    cosine_tab, sine_tab = angles(length, HD)
    inputs_f = tokens.astype(f32)
    first_in = rms_scale(inputs_f, gain_one).astype(bf16)
    qkv = jnp.dot(first_in, qkv_w, preferred_element_type=f32)
    queries = (
        rotary(qkv[:, :q_cols].reshape(length, HQ, HD), cosine_tab, sine_tab)
        .astype(bf16)
        .reshape(length, HK, group_size, HD)
    )
    keys_rot = rotary(
        qkv[:, q_cols : q_cols + kv_cols].reshape(length, HK, HD), cosine_tab, sine_tab
    ).astype(bf16)
    values_b = qkv[:, q_cols + kv_cols :].astype(bf16).reshape(length, HK, HD)
    positions = jnp.arange(length)
    allowed = (positions[None, :] <= positions[:, None]) | (positions[None, :] < prefix_len[0])

    def masked_scores():
        scores = jnp.einsum("ihrd,jhd->hrij", queries, keys_rot, preferred_element_type=f32)
        return jnp.where(allowed, scores * score_scale, -1e30)

    masked = masked_scores()
    row_peak = jnp.max(masked, axis=-1, keepdims=True)
    log_total = row_peak + jnp.log(jnp.sum(jnp.exp(masked - row_peak), axis=-1, keepdims=True))
    prob_bf = jnp.exp(masked - log_total).astype(bf16)
    attended = jnp.einsum("hrij,jhd->ihrd", prob_bf, values_b, preferred_element_type=f32)
    attended = attended.reshape(length, HQ * HD).astype(bf16)
    resid = inputs_f + jnp.dot(attended, output_w, preferred_element_type=f32)
    second_in = rms_scale(resid, gain_two).astype(bf16)

    second_all = gather(second_in, PLANE)
    logits = jnp.dot(second_all, router_w, preferred_element_type=f32)
    gates_all = jax.nn.softmax(jnp.where(chosen_mask, logits, -jnp.inf), axis=-1)
    own_gates = lax.dynamic_index_in_dim(gates_all, own_expert, 1, keepdims=False)
    own_gates = own_gates.reshape(blocks, block_rows)
    gate_rows = jnp.einsum(
        "bct,bt->bc", dispatch.astype(f32), own_gates, precision=lax.Precision.HIGHEST
    )[:, :, None]
    gate_w = lax.dynamic_index_in_dim(w_gate, own_local, 0, keepdims=False)
    up_w = lax.dynamic_index_in_dim(w_up, own_local, 0, keepdims=False)
    down_w = lax.dynamic_index_in_dim(w_down, own_local, 0, keepdims=False)

    def to_rows(array):
        return jnp.einsum(
            "bct,btd->bcd",
            dispatch,
            array.reshape(blocks, block_rows, model_width),
            preferred_element_type=f32,
        ).astype(bf16)

    def to_tokens(rows):
        return (
            jnp.einsum("bct,bcd->btd", dispatch, rows.astype(bf16), preferred_element_type=f32)
            .astype(bf16)
            .reshape(plane_rows, model_width)
        )

    rows_in = to_rows(second_all)
    rows_cot = to_rows(cot_all)
    gate_pre = jnp.einsum("bcd,df->bcf", rows_in, gate_w, preferred_element_type=f32)
    up_pre = jnp.einsum("bcd,df->bcf", rows_in, up_w, preferred_element_type=f32)
    hidden, act_pull = jax.vjp(expert_act, gate_pre, up_pre)
    gated = (gate_rows * hidden).astype(bf16)
    down_part = jnp.einsum("bcd,bcf->df", rows_cot, gated, preferred_element_type=f32)
    down_sum = scatter_sum(down_part.astype(bf16), "z")
    cot_hidden = jnp.einsum("bcd,fd->bcf", rows_cot, down_w, preferred_element_type=f32)
    gate_signal_rows = jnp.sum(hidden * cot_hidden, axis=-1)
    gate_pgrad, up_pgrad = act_pull(gate_rows * cot_hidden)
    gate_pgrad = gate_pgrad.astype(bf16)
    up_pgrad = up_pgrad.astype(bf16)
    gate_part = jnp.einsum("bcd,bcf->df", rows_in, gate_pgrad, preferred_element_type=f32)
    gate_sum = scatter_sum(gate_part.astype(bf16), "z")
    up_part = jnp.einsum("bcd,bcf->df", rows_in, up_pgrad, preferred_element_type=f32)
    up_sum = scatter_sum(up_part.astype(bf16), "z")
    rows_grad = jnp.einsum("bcf,df->bcd", gate_pgrad, gate_w, preferred_element_type=f32)
    rows_grad = rows_grad + jnp.einsum("bcf,df->bcd", up_pgrad, up_w, preferred_element_type=f32)
    second_back = scatter_sum(to_tokens(rows_grad), PLANE).astype(f32)
    gate_signal = jnp.einsum(
        "bct,bc->bt", dispatch.astype(f32), gate_signal_rows, precision=lax.Precision.HIGHEST
    )
    gate_signal = exchange(gate_signal.reshape(plane, length), PLANE)
    gate_signal = jnp.transpose(
        gate_signal.reshape(local_count, owners, length), (2, 1, 0)
    ).reshape(length, experts_all)
    expert_rows = jnp.einsum("bcf,fd->bcd", gated, down_w, preferred_element_type=f32)
    mixture = scatter_sum(to_tokens(expert_rows), PLANE).astype(f32)
    block_out = (resid + mixture).astype(bf16)

    cotangent = out_grad.astype(f32)
    gate_probs = lax.dynamic_slice_in_dim(gates_all, own_place * length, length, 0)
    logit_grad = (
        gate_probs
        * (gate_signal - jnp.sum(gate_probs * gate_signal, axis=-1, keepdims=True))
    ).astype(bf16)
    router_acc = left_product(second_in, logit_grad)
    second_grad = second_back + jnp.dot(logit_grad, router_w.T, preferred_element_type=f32)
    _, norm_two_pull = jax.vjp(rms_scale, resid, gain_two)
    resid_norm_grad, gain_two_grad = norm_two_pull(second_grad)
    resid_grad = cotangent + resid_norm_grad
    branch_grad = resid_grad.astype(bf16)

    attended_all = gather(attended, PLANE)
    branch_cols = exchange(by_owner(branch_grad, plane), PLANE)
    output_part = left_product(attended_all, branch_cols)
    attended_grad = jnp.dot(branch_grad, output_w.T, preferred_element_type=f32).astype(bf16)
    attended_grad = attended_grad.reshape(length, HK, group_size, HD)
    masked = masked_scores()
    prob_full = jnp.exp(masked - log_total)
    prob_bf = prob_full.astype(bf16)
    prob_grad = jnp.einsum("ihrd,jhd->hrij", attended_grad, values_b, preferred_element_type=f32)
    row_inner = jnp.sum(prob_full * prob_grad, axis=-1, keepdims=True)
    score_grad = (prob_full * (prob_grad - row_inner)).astype(bf16)
    query_rot_grad = (
        jnp.einsum("hrij,jhd->ihrd", score_grad, keys_rot, preferred_element_type=f32)
        * score_scale
    )
    query_back = rotary(query_rot_grad.reshape(length, HQ, HD), cosine_tab, -sine_tab)
    query_back = query_back.astype(bf16).reshape(length, HQ * HD)
    key_rot_grad = (
        jnp.einsum("hrij,ihrd->jhd", score_grad, queries, preferred_element_type=f32)
        * score_scale
    )
    key_back = rotary(key_rot_grad, cosine_tab, -sine_tab).astype(bf16).reshape(length, HK * HD)
    value_back = jnp.einsum("hrij,ihrd->jhd", prob_bf, attended_grad, preferred_element_type=f32)
    value_back = value_back.astype(bf16).reshape(length, HK * HD)
    qkv_back = jnp.concatenate([query_back, key_back, value_back], axis=1)
    first_all = gather(first_in, PLANE)
    qkv_part = left_product(first_all, exchange(by_owner(qkv_back, plane), PLANE))
    first_grad = lax.dot_general(
        qkv_back, qkv_w, (((1,), (1,)), ((), ())), preferred_element_type=f32
    )
    _, norm_one_pull = jax.vjp(rms_scale, inputs_f, gain_one)
    input_norm_grad, gain_one_grad = norm_one_pull(first_grad)
    tokens_grad = (resid_grad + input_norm_grad).astype(bf16)

    narrow_part = jnp.concatenate(
        [router_acc, gain_one_grad[:, None], gain_two_grad[:, None]], axis=1
    ).astype(bf16)
    narrow_cols = narrow_part.shape[1]
    narrow_sum = lax.psum(scatter_sum(narrow_part, GROUP), "x").astype(f32)
    dense_part = jnp.concatenate([qkv_part, output_part], axis=1).astype(bf16)
    dense_sum = scatter_sum(dense_part, "z")
    dense_cols = dense_sum.shape[1]
    dense_sum = gather(dense_sum, PLANE).reshape(plane, local_count, shard_rows, dense_cols)
    dense_sum = lax.dynamic_index_in_dim(dense_sum, own_local, 1, keepdims=False).astype(f32)
    dense_sum = jnp.moveaxis(dense_sum, 0, 1)
    qkv_width = qkv_cols // plane
    qkv_sum = dense_sum[:, :, :qkv_width].reshape(shard_rows, qkv_cols)
    output_sum = dense_sum[:, :, qkv_width:].reshape(shard_rows, model_width)

    def placed(total):
        total = exchange(total, ("y", "c"))
        return total.reshape(local_count, shard_rows, hidden_width).astype(f32)

    return (
        block_out,
        tokens_grad,
        narrow_sum[:, experts_all],
        qkv_sum[:, :q_cols],
        qkv_sum[:, q_cols : q_cols + kv_cols],
        qkv_sum[:, q_cols + kv_cols :],
        output_sum,
        narrow_sum[:, experts_all + 1],
        narrow_sum[:, :experts_all],
        placed(gate_sum),
        placed(up_sum),
        jnp.swapaxes(placed(down_sum), 1, 2),
    )


def rounded(values):
    return lax.reduce_precision(values, 8, 7).astype(jnp.bfloat16)


def after(block, *others):
    return lax.optimization_barrier((block,) + others)[0]


def swap(block, axis):
    return lax.ppermute(block, axis, [(0, 1), (1, 0)])


def shifts(block):
    depth = lax.axis_size("z")
    return [
        lax.ppermute(block, "z", [(i, (i + k) % depth) for i in range(depth)])
        for k in range(1, depth)
    ]


def plane_sides(block):
    return swap(block, "x"), swap(block, "y")


def plane_corner(sides, before=(), later=()):
    over_x, over_y = sides
    half = over_x.shape[0] // 2
    over_y, over_x = lax.optimization_barrier((over_y[:half], over_x[half:]) + before)[:2]
    parts = (swap(over_y, "x"), swap(over_x, "y"))
    return jnp.concatenate(lax.optimization_barrier(parts + later)[:2], axis=0)


def plane_pieces(block, sides=None, corner=None):
    sides = plane_sides(block) if sides is None else sides
    corner = plane_corner(sides) if corner is None else corner
    pieces = [block, *sides, corner]
    return pieces + [swap(piece, "c") for piece in pieces]


def small_gather(block):
    for axis in ("x", "y", "c"):
        block = jnp.concatenate([block, swap(block, axis)], axis=1)
    return block


def small_group_gather(block):
    depth = lax.axis_size("z")
    order = jnp.stack(([block] + shifts(block))[::-1] * 2)
    start = (depth - 1 - lax.axis_index("z")) % depth
    total = lax.dynamic_slice_in_dim(order, start, depth, 0)[:, None, None]
    for dim, axis in ((1, "y"), (2, "c")):
        other = swap(total, axis)
        last = lax.axis_index(axis) == 1
        pair = [jnp.where(last, other, total), jnp.where(last, total, other)]
        total = jnp.concatenate(pair, axis=dim)
    return total.reshape(-1, block.shape[1])


def add(left, right):
    return rounded(left.astype(jnp.float32) + right.astype(jnp.float32))


def over_core(near, far):
    return add(near, swap(far, "c"))


def early_sums(over_x, over_y):
    half = over_x.shape[0] // 2
    return swap(over_x[:half], "x"), swap(over_y[half:], "y")


def corner_first(corner):
    half = corner.shape[0] // 2
    return swap(corner[:half], "x"), swap(corner[half:], "y")


def corner_sums(over_x, over_y, first):
    half = over_x.shape[0] // 2
    return add(over_y[:half], first[0]), add(over_x[half:], first[1])


def corner_last(sums):
    return swap(sums[0], "y"), swap(sums[1], "x")


def cost(micros):
    return pl.CostEstimate(flops=micros * 10**9, bytes_accessed=micros * 10**6, transcendentals=0)


def dot(left, right, dims=((1,), (0,)), precision=None):
    return lax.dot_general(
        left, right, (dims, ((), ())), precision=precision, preferred_element_type=jnp.float32
    )


WHOLE = pl.BlockSpec(memory_space=pltpu.VMEM)
IN_HBM = pl.BlockSpec(memory_space=pltpu.HBM)
SCALARS = pl.BlockSpec(memory_space=pltpu.SMEM)


def run_kernel(kernel, micros, at, operands, outs, megabytes=16, scratch=(), hbm_in=0, hbm_out=0):
    return pl.pallas_call(
        kernel,
        out_shape=[jax.ShapeDtypeStruct(shape, dtype) for shape, dtype in outs],
        in_specs=[SCALARS] + [WHOLE] * (len(operands) - hbm_in) + [IN_HBM] * hbm_in,
        out_specs=[WHOLE] * (len(outs) - hbm_out) + [IN_HBM] * hbm_out,
        scratch_shapes=scratch,
        cost_estimate=cost(micros),
        compiler_params=pltpu.CompilerParams(vmem_limit_bytes=megabytes * 2**20),
    )(at, *operands)


def place_pieces(at, refs, weight):
    depth = weight.shape[1]
    for n, ref in enumerate(refs):
        dc, dy, dx = n // 4, n // 2 % 2, n % 2
        for k in range(depth):
            z = lax.rem(at[3] + depth - k, depth)
            weight[at[2] ^ dx, z, at[0] ^ dy, at[1] ^ dc] = ref[k]


def rms_kernel(values, gain):
    inverse = lax.rsqrt(jnp.mean(values * values, axis=-1, keepdims=True) + 1e-06)
    return (values * inverse * gain).astype(jnp.bfloat16)


def rms_back(values, gain, grad):
    inverse = lax.rsqrt(jnp.mean(values * values, axis=-1, keepdims=True) + 1e-06)
    normed = values * inverse
    gain_grad = jnp.sum(grad * normed, axis=0, keepdims=True)
    grad = grad * gain
    along = jnp.mean(grad * normed, axis=-1, keepdims=True)
    return inverse * (grad - normed * along), gain_grad


def turned(values, cosine_tab, sine_tab):
    return values * cosine_tab + pltpu.roll(values, HD // 2, 1) * sine_tab


def attend_kernel(at, tokens, gain, cosine, sine, *refs):
    first_ref, query_ref, key_ref, value_ref, out_ref = refs[8:13]
    prob_out, weight_out, prob_ref, weight, sems = refs[13:]
    place_pieces(at, refs[:8], weight)
    copies = [pltpu.make_async_copy(weight, weight_out, sems.at[HK])]
    copies[0].start()
    length = tokens.shape[0]
    first_in = rms_kernel(tokens[...].astype(jnp.float32), gain[...])
    first_ref[...] = first_in
    rows = lax.broadcasted_iota(jnp.int32, (length, length), 0)
    cols = lax.broadcasted_iota(jnp.int32, (length, length), 1)
    allowed = (cols <= rows) | (cols < at[4])
    cosine_tab, sine_tab = cosine[...], sine[...]
    group_size = HQ // HK
    for group in range(HK):
        matrix = weight[group].reshape(first_in.shape[1], -1)
        qkv = dot(first_in, matrix)
        at_key = group_size * HD
        key = turned(qkv[:, at_key : at_key + HD], cosine_tab, sine_tab).astype(jnp.bfloat16)
        value = qkv[:, at_key + HD :].astype(jnp.bfloat16)
        key_ref[:, group * HD : (group + 1) * HD] = key
        value_ref[:, group * HD : (group + 1) * HD] = value
        for member in range(group_size):
            head = group * group_size + member
            here = slice(head * HD, (head + 1) * HD)
            query = turned(qkv[:, member * HD : (member + 1) * HD], cosine_tab, sine_tab)
            query = query.astype(jnp.bfloat16)
            query_ref[:, here] = query
            scores = dot(query, key, ((1,), (1,)))
            scores = jnp.where(allowed, scores * HD ** (-0.5), -1e30)
            weights = jnp.exp(scores - jnp.max(scores, axis=-1, keepdims=True))
            prob = weights * (1.0 / jnp.sum(weights, axis=-1, keepdims=True))
            prob = prob.astype(jnp.bfloat16)
            prob_ref[head] = prob
            out_ref[:, here] = dot(prob, value).astype(jnp.bfloat16)
        here = pl.ds(group * group_size, group_size)
        copies.append(
            pltpu.make_async_copy(prob_ref.at[here], prob_out.at[here], sems.at[group])
        )
        copies[-1].start()
    for copy in copies:
        copy.wait()


def project_kernel(at, tokens, gain, attended, *refs):
    resid_ref, second_ref, weight_out, weight, sem = refs[8:]
    place_pieces(at, refs[:8], weight)
    copy = pltpu.make_async_copy(weight, weight_out, sem)
    copy.start()
    heads = attended[...]
    halves = [dot(heads, weight[half].reshape(heads.shape[1], -1)) for half in range(2)]
    resid = tokens[...].astype(jnp.float32) + jnp.concatenate(halves, axis=1)
    resid_ref[...] = resid
    second_ref[...] = rms_kernel(resid, gain[...])
    copy.wait()


def one_hot(slots, capacity, dtype):
    shape = (capacity, slots.shape[1])
    return (slots == lax.broadcasted_iota(jnp.int32, shape, 0)).astype(jnp.float32).astype(dtype)


def slots_of(ids, expert, start, rows):
    named = jnp.any(ids[:, start : start + rows] == expert, axis=0, keepdims=True)
    named = named.astype(jnp.float32)
    before = lax.broadcasted_iota(jnp.int32, (rows, rows), 0)
    upto = lax.broadcasted_iota(jnp.int32, (rows, rows), 1)
    counts = dot(named.astype(jnp.bfloat16), (before <= upto).astype(jnp.float32).astype(jnp.bfloat16))
    return jnp.where(named > 0.0, counts - 1.0, -1.0).astype(jnp.int32)


def spread(picks, capacity, rows, outs):
    rows = rows.astype(jnp.bfloat16)
    block = picks[0].shape[1]
    for n in range(len(picks) // 2):
        for part in range(2):
            pick = picks[2 * n + part]
            at_row = (2 * n + part) * capacity
            tokens = dot(pick, rows[at_row : at_row + capacity], ((0,), (0,)))
            outs[n][part * block : (part + 1) * block] = tokens.astype(jnp.bfloat16)


def expert_kernel(capacity, pieces, earlier, at, ids, router, *refs):
    count = len(pieces)
    second, cot = refs[:count], refs[count : 2 * count]
    gate_w, up_w, down_w = refs[2 * count : 2 * count + 3]
    before = refs[2 * count + 3 : 2 * count + 3 + 2 * earlier]
    refs = refs[2 * count + 3 + 2 * earlier :]
    rows_in, rows_cot, gated_ref, gate_back, up_back, gates_ref = refs[:6]
    backs, gate_rows = refs[6 : 6 + count], refs[-1]
    f32, bf16 = jnp.float32, jnp.bfloat16
    length, width = second[0].shape
    wide = router.shape[1]
    half = length // 2
    picks = []
    experts = lax.broadcasted_iota(jnp.int32, (wide, length), 0)
    for n, piece in enumerate(pieces):
        tokens = second[n][...]
        named = ids[:, piece * length : (piece + 1) * length]
        chosen = functools.reduce(
            jnp.logical_or, [named[k : k + 1] == experts for k in range(named.shape[0])]
        )
        logits = jnp.where(chosen, dot(router[...], tokens, ((0,), (1,))), -1e30)
        weights = jnp.exp(logits - jnp.max(logits, axis=0, keepdims=True))
        gates = weights * (1.0 / jnp.sum(weights, axis=0, keepdims=True))
        if n == 0:
            gates_ref[...] = gates
        own = jnp.sum(jnp.where(experts == at[5], gates, 0.0), axis=0, keepdims=True)
        for part in range(2):
            here = slice(part * half, (part + 1) * half)
            place = slice((2 * n + part) * capacity, (2 * n + part + 1) * capacity)
            slots = slots_of(ids, at[5], piece * length + part * half, half)
            pick = one_hot(slots, capacity, f32)
            picks.append(pick.astype(bf16))
            rows_in[place] = dot(picks[-1], tokens[here]).astype(bf16)
            rows_cot[place] = dot(picks[-1], cot[n][here]).astype(bf16)
            gate_rows[place] = jnp.sum(pick * own[:, here], axis=1, keepdims=True)
    gate = gate_rows[...]
    gate_pre = dot(rows_in[...], gate_w[...])
    up_pre = dot(rows_in[...], up_w[...])
    cot_hidden = dot(rows_cot[...], down_w[...], ((1,), (1,)))
    scale = math.sqrt(2.0 / math.pi)
    square = gate_pre * gate_pre
    bent = jnp.tanh(scale * gate_pre * (1.0 + 0.044715 * square))
    open_part = 0.5 * (1.0 + bent)
    active = gate_pre * open_part
    slope = open_part + 0.5 * gate_pre * (1.0 - bent * bent) * scale * (
        1.0 + 3 * 0.044715 * square
    )
    hidden = active * up_pre
    gated_ref[...] = (gate * hidden).astype(bf16)
    signal = jnp.sum(hidden * cot_hidden, axis=1, keepdims=True)
    back = gate * cot_hidden
    gate_back[...] = (back * up_pre * slope).astype(bf16)
    up_back[...] = (back * active).astype(bf16)
    high = signal.astype(bf16)
    low = (signal - high.astype(f32)).astype(bf16)
    lanes = lax.broadcasted_iota(jnp.int32, (signal.shape[0], wide), 1)
    signal = jnp.where(lanes == at[5], high.astype(f32), 0.0)
    signal = jnp.where(lanes == at[5] + wide // 2, low.astype(f32), signal)
    by_rows = ((1,), (1,))
    rows = dot(gate_back[...], gate_w[...], by_rows) + dot(up_back[...], up_w[...], by_rows)
    spread(picks, capacity, jnp.concatenate([rows, signal], axis=1), backs)
    if earlier:
        lefts = [ref[...] for ref in (*before[:earlier], rows_cot)]
        rights = [ref[...] for ref in (*before[earlier:], gated_ref)]
        total = dot(jnp.concatenate(lefts, axis=0), jnp.concatenate(rights, axis=0), ((0,), (0,)))
        refs[6 + count][...] = total.astype(bf16)


def run_expert(pieces, at, ids, router, weights, second, cot, capacity, before=()):
    count = len(pieces)
    rows, wide = 2 * count * capacity, router.shape[1]
    (length, width), hidden = second[0].shape, weights[0].shape[1]
    bf16, f32 = jnp.bfloat16, jnp.float32
    outs = [(rows, width)] * 2 + [(rows, hidden)] * 3
    outs = [(shape, bf16) for shape in outs] + [((wide, length), f32)]
    outs = outs + [((length, width + wide), bf16)] * count
    if before:
        outs = outs + [((width, hidden), bf16)]
    return run_kernel(
        functools.partial(expert_kernel, capacity, pieces, len(before) // 2),
        4 * count,
        at,
        (ids, router, *second, *cot, *weights, *before),
        outs,
        4 + 3 * count + 4 * bool(before),
        [pltpu.VMEM((rows, 1), f32)],
    )


def mixture_kernel(capacity, groups, at, ids, *refs):
    gated, down_w, outs = refs[: len(groups)], refs[len(groups)], refs[len(groups) + 1 :]
    length = outs[0].shape[0]
    for pieces, rows in zip(groups, gated):
        picks = []
        for piece in pieces:
            for part in range(2):
                start = piece * length + part * length // 2
                slots = slots_of(ids, at[5], start, length // 2)
                picks.append(one_hot(slots, capacity, jnp.bfloat16))
        spread(picks, capacity, dot(rows[...], down_w[...]), [outs[piece] for piece in pieces])


def row_sum_kernel(parts, at, *refs):
    arrays = [
        jnp.concatenate([ref[...] for ref in refs[n : n + parts]], axis=0)
        for n in range(0, len(refs) - len(refs) // (parts + 1), parts)
    ]
    outs = refs[len(arrays) * parts :]
    for out, right in zip(outs, arrays[1:]):
        out[...] = dot(arrays[0], right, ((0,), (0,))).astype(jnp.bfloat16)


def row_sums(at, left, *rights):
    operands = [part for parts in (left, *rights) for part in parts]
    outs = [((left[0].shape[1], right[0].shape[1]), jnp.bfloat16) for right in rights]
    kernel = functools.partial(row_sum_kernel, len(left))
    return run_kernel(kernel, 4 * len(rights), at, operands, outs, 24 if len(rights) == 1 else 56)


def branch_back_kernel(
    at, near, far, first_x, first_y, last_y, last_x, resid, gain, second, gates, router, cot, weight, *outs
):
    resid_grad_ref, branch_ref, attended_ref, router_ref, gain_ref = outs
    f32, bf16 = jnp.float32, jnp.bfloat16
    halves = [first_x[...].astype(f32) + last_y[...], first_y[...].astype(f32) + last_x[...]]
    total = near[...].astype(f32) + far[...] + jnp.concatenate(halves, axis=0)
    width = resid.shape[1]
    signal = total[:, width:]
    signal = signal + pltpu.roll(signal, signal.shape[1] // 2, 1)
    chosen = gates[...].T
    logit_grad = chosen * (signal - jnp.sum(chosen * signal, axis=-1, keepdims=True))
    logit_grad = logit_grad.astype(bf16)
    second_grad = total[:, :width] + dot(logit_grad, router[...], ((1,), (1,)))
    norm_grad, gain_grad = rms_back(resid[...], gain[...], second_grad)
    gain_ref[...] = gain_grad
    resid_grad = cot[...].astype(f32) + norm_grad
    resid_grad_ref[...] = resid_grad
    branch = resid_grad.astype(bf16)
    branch_ref[...] = branch
    wide = weight.shape[2]
    attended_ref[...] = (
        dot(branch[:, :wide], weight[0], ((1,), (1,)))
        + dot(branch[:, wide:], weight[1], ((1,), (1,)))
    ).astype(bf16)
    router_ref[...] = dot(second[...], logit_grad, ((0,), (0,)))


def attend_back_kernel(
    at, attended, probs, queries, keys, values, cosine, sine, branch, back_ref
):
    f32, bf16 = jnp.float32, jnp.bfloat16
    cosine_tab, sine_tab = cosine[...], -sine[...]
    group_size = HQ // HK
    places, length = back_ref.shape[0], branch.shape[0]
    branch_width = branch.shape[1] // places
    width = back_ref.shape[2] - branch_width
    for place in range(places):
        here = slice(place * branch_width, (place + 1) * branch_width)
        back_ref[place, :length, width:] = branch[:, here]
        back_ref[place, length:] = jnp.zeros((back_ref.shape[1] - length, back_ref.shape[2]), bf16)
    scale = HD ** (-0.5)

    def put(position, block):
        back_ref[position // width, :length, position % width : position % width + HD] = block

    for group in range(HK):
        own = slice(group * HD, (group + 1) * HD)
        key, value = keys[:, own], values[:, own]
        key_grad = value_grad = 0.0
        start = group * (group_size + 2) * HD
        for member in range(group_size):
            head = group * group_size + member
            here = slice(head * HD, (head + 1) * HD)
            out_grad, query, prob = attended[:, here], queries[:, here], probs[head]
            prob_grad = dot(out_grad, value, ((1,), (1,)))
            prob_f = prob.astype(f32)
            inner = jnp.sum(prob_f * prob_grad, axis=-1, keepdims=True)
            score_grad = (prob_f * (prob_grad - inner)).astype(bf16)
            query_grad = turned(dot(score_grad, key) * scale, cosine_tab, sine_tab)
            put(start + member * HD, query_grad.astype(bf16))
            key_grad = key_grad + dot(score_grad, query, ((0,), (0,)))
            value_grad = value_grad + dot(prob, out_grad, ((0,), (0,)))
        key_grad = turned(key_grad * scale, cosine_tab, sine_tab)
        put(start + group_size * HD, key_grad.astype(bf16))
        put(start + (group_size + 1) * HD, value_grad.astype(bf16))


def first_back_kernel(at, back, weight, tokens, gain, resid_grad, tokens_ref, gain_ref):
    f32 = jnp.float32
    parts = back.shape[0]
    cols = weight.shape[0] * weight.shape[2] // parts
    first_grad = 0.0
    for part in range(parts):
        group, place = divmod(part * cols, weight.shape[2])
        first_grad = first_grad + dot(
            back[part, : tokens.shape[0], :cols], weight[group, :, place : place + cols], ((1,), (1,))
        )
    norm_grad, gain_grad = rms_back(tokens[...].astype(f32), gain[...], first_grad)
    gain_ref[...] = gain_grad
    tokens_ref[...] = (resid_grad[...] + norm_grad).astype(jnp.bfloat16)


def dense_grad_kernel(at, back, *refs):
    pieces, out_ref, held, sems = refs[:8], refs[8], refs[9], refs[10]
    copies = [
        pltpu.make_async_copy(piece, held.at[n], sems.at[n]) for n, piece in enumerate(pieces)
    ]
    for copy in copies:
        copy.start()
    depth, rows, cols = out_ref.shape
    length = held.shape[1] // 2
    qkv_width = cols - held.shape[2] // back.shape[0]
    narrow = sum(back[place, length:].astype(jnp.float32) for place in range(back.shape[0]))
    sums = [0.0, 0.0]
    for n, copy in enumerate(copies):
        copy.wait()
        dc, dy, dx = n // 4, n // 2 % 2, n % 2
        place = 4 * (at[0] ^ dy) + 2 * (at[1] ^ dc) + (at[2] ^ dx)
        own = back[place, :length]
        sums[0] = sums[0] + dot(held[n, length:], own[:, :qkv_width], ((0,), (0,)))
        sums[1] = sums[1] + dot(held[n, :length], own[:, qkv_width:], ((0,), (0,)))
    wide = held.shape[2] // depth
    each = 4
    for z in range(depth):
        here = slice(z * wide, (z + 1) * wide)
        both = jnp.concatenate([part[here] for part in sums], axis=1)
        out_ref[z, :wide] = both.astype(jnp.bfloat16)
        kept = [narrow[z * each : (z + 1) * each], jnp.zeros((rows - wide - each, cols), jnp.float32)]
        out_ref[z, wide:] = jnp.concatenate(kept, axis=0).astype(jnp.bfloat16)


def finish_kernel(at, sums, query_ref, key_ref, value_ref, output_ref):
    places, _, cols = sums.shape
    rows, out_width = query_ref.shape[0], output_ref.shape[1] // places
    width = cols - out_width
    for place in range(places):
        block = sums[place, :rows].astype(jnp.float32)
        output_ref[:, place * out_width : (place + 1) * out_width] = block[:, width:]
        for at_col in range(0, width, HD):
            group, head = divmod((place * width + at_col) // HD, HQ // HK + 2)
            part = block[:, at_col : at_col + HD]
            if head < HQ // HK:
                start = (group * (HQ // HK) + head) * HD
                query_ref[:, start : start + HD] = part
            elif head == HQ // HK:
                key_ref[:, group * HD : (group + 1) * HD] = part
            else:
                value_ref[:, group * HD : (group + 1) * HD] = part


def local_pairs(
    tokens,
    norm1_gain,
    w_query,
    w_key,
    w_value,
    w_out,
    norm2_gain,
    w_router,
    w_gate,
    w_up,
    w_down,
    expert_ids,
    prefix_len,
    out_grad,
):
    bf16, f32 = jnp.bfloat16, jnp.float32
    length, model_width = tokens.shape
    shard_rows = w_query.shape[0]
    local_count, _, hidden_width = w_gate.shape
    owners = lax.axis_size("x")
    depth = lax.axis_size("z")
    plane = lax.axis_size(PLANE)
    experts_all = w_router.shape[1]
    block_rows = length // MICRO
    capacity = 3 * block_rows * expert_ids.shape[1] // (2 * experts_all)
    plane_rows = plane * length
    blocks = plane_rows // block_rows
    q_cols, kv_cols = w_query.shape[1], w_key.shape[1]
    qkv_cols = q_cols + 2 * kv_cols
    q_group, out_half = q_cols // HK, model_width // 2
    y, c, x, z = (lax.axis_index(axis) for axis in ("y", "c", "x", "z"))
    own_local = 2 * y + c
    own_expert = x * local_count + own_local
    at = jnp.stack([y, c, x, z, prefix_len[0], own_expert, own_local])

    own_half = jnp.concatenate(
        [
            lax.dynamic_slice_in_dim(part, x * (part.shape[1] // 2), part.shape[1] // 2, 1)
            for part in (w_query, w_key, w_value, w_out)
        ],
        axis=1,
    )
    narrow = jnp.concatenate([w_router, norm1_gain[:, None], norm2_gain[:, None]], axis=1)
    narrow = jnp.pad(narrow, ((0, 0), (0, 128 - narrow.shape[1])))
    router_w = small_group_gather(narrow)
    ids_all = small_gather(expert_ids.T)
    column = [own_half] + shifts(own_half)
    cot_sides = plane_sides(after(out_grad, router_w, ids_all))
    qkv_half = qkv_cols // 2
    qkv_column = jnp.stack([part[:, :qkv_half] for part in column])
    out_column = jnp.stack([part[:, qkv_half:] for part in column])
    qkv_column, out_column = lax.optimization_barrier((qkv_column, out_column, *cot_sides))[:2]
    sliced = after(own_local, column[-1])
    gate_w, up_w, down_w = (
        lax.dynamic_index_in_dim(weight, sliced, 0, keepdims=False)
        for weight in (w_gate, w_up, w_down)
    )
    qkv_sides = plane_sides(qkv_column)
    gains = router_w[:, experts_all : experts_all + 2].T.astype(f32)
    gain_one, gain_two = gains[:1], gains[1:]
    qkv_corner = plane_corner(qkv_sides, (gate_w, up_w, down_w, gain_one, gain_two))
    out_sides = plane_sides(after(out_column, *qkv_sides))
    qkv_pieces = plane_pieces(qkv_column, qkv_sides, qkv_corner)
    cosine_tab, sine_tab = angles(length, HD)
    cosine_all = jnp.concatenate([cosine_tab, cosine_tab], axis=2)[:, 0]
    sine_all = jnp.concatenate([-sine_tab, sine_tab], axis=2)[:, 0]
    weight_lead = (2, depth, 2, 2, shard_rows)
    first_in, queries, keys_rot, values_b, attended, probs, qkv_w = run_kernel(
        attend_kernel,
        11,
        at,
        (tokens, gain_one, cosine_all, sine_all, *qkv_pieces),
        [
            ((length, model_width), bf16),
            ((length, q_cols), bf16),
            ((length, kv_cols), bf16),
            ((length, kv_cols), bf16),
            ((length, q_cols), bf16),
            ((HQ, length, length), bf16),
            (weight_lead + (qkv_half,), bf16),
        ],
        28,
        [
            pltpu.VMEM((HQ, length, length), bf16),
            pltpu.VMEM(weight_lead + (qkv_half,), bf16),
            pltpu.SemaphoreType.DMA((HK + 1,)),
        ],
        hbm_out=2,
    )
    out_sides = lax.optimization_barrier((*out_sides, attended))[:2]
    out_corner = plane_corner(out_sides)
    cot_corner = plane_corner(cot_sides)
    out_pieces = plane_pieces(out_column, out_sides, out_corner)
    cot_pieces = plane_pieces(out_grad, cot_sides, cot_corner)
    resid, second_in, output_w = run_kernel(
        project_kernel,
        4,
        at,
        (tokens, after(gain_two, cot_corner), attended, *out_pieces),
        [
            ((length, model_width), f32),
            ((length, model_width), bf16),
            (weight_lead + (out_half,), bf16),
        ],
        44,
        [pltpu.VMEM(weight_lead + (out_half,), bf16), pltpu.SemaphoreType.DMA],
        hbm_out=1,
    )
    qkv_w = qkv_w.reshape(HK, model_width, qkv_half)
    output_w = output_w.reshape(2, q_cols, out_half)

    expert = functools.partial(
        run_expert,
        at=at,
        ids=ids_all,
        router=router_w,
        weights=(gate_w, up_w, down_w),
        capacity=capacity,
    )
    second_sides = plane_sides(second_in)
    groups = ((0, 4), (1, 5, 2, 6), (3, 7))
    second_pieces = {0: second_in, 4: swap(second_in, "c")}

    def run_group(pieces, before=()):
        return expert(
            pieces,
            before=before,
            second=[second_pieces[piece] for piece in pieces],
            cot=[cot_pieces[piece] for piece in pieces],
        )

    stage_own = run_group(groups[0])
    second_sides = lax.optimization_barrier((*second_sides, stage_own[0]))[:2]
    for piece, block in zip((1, 2), second_sides):
        second_pieces[piece], second_pieces[piece + 4] = block, swap(block, "c")
    stage_sides = run_group(groups[1])
    second_corner = plane_corner(second_sides, later=(stage_sides[0],))
    second_pieces[3], second_pieces[7] = second_corner, swap(second_corner, "c")
    own_near, own_far = stage_own[6:]
    own_far = swap(own_far, "c")
    x_near, x_far, y_near, y_far = stage_sides[6:]
    back_x, back_y = over_core(x_near, x_far), over_core(y_near, y_far)
    first_x, first_y = early_sums(back_x, back_y)
    two = (stage_own, stage_sides)
    stage_corner = run_group(groups[2], [stage[1] for stage in two] + [stage[2] for stage in two])
    *stage_corner, down_part = stage_corner
    corner = over_core(*stage_corner[6:])
    passed = corner_first(corner)
    stages = (stage_own, stage_sides, stage_corner)
    rows_in, rows_cot, gated, gate_back, up_back = ([stage[n] for stage in stages] for n in range(5))
    gates = stage_own[5]
    last_y, last_x = corner_last(corner_sums(back_x, back_y, passed))
    down_sum = scatter_sum(down_part, "z")

    resid_grad, branch_grad, attended_grad, router_acc, gain_two_grad = run_kernel(
        branch_back_kernel,
        6,
        at,
        (
            own_near,
            own_far,
            first_x,
            first_y,
            last_y,
            last_x,
            resid,
            gain_two,
            second_in,
            gates,
            router_w,
            out_grad,
            output_w,
        ),
        [
            ((length, model_width), f32),
            ((length, model_width), bf16),
            ((length, q_cols), bf16),
            ((model_width, 128), f32),
            ((1, model_width), f32),
        ],
        56,
    )
    gate_part, up_part = row_sums(
        at, [after(rows_in[0], resid_grad)] + rows_in[1:], gate_back, up_back
    )
    gate_sum, up_sum = scatter_sum(gate_part, "z"), scatter_sum(up_part, "z")
    attended_grad = after(attended_grad, gate_part)
    qkv_width, branch_width = qkv_cols // plane, model_width // plane
    dense_cols = qkv_width + branch_width
    (back_cols,) = run_kernel(
        attend_back_kernel,
        6,
        at,
        (
            attended_grad,
            probs,
            queries,
            keys_rot,
            values_b,
            cosine_all,
            sine_all,
            branch_grad,
        ),
        [((plane, length + 16, dense_cols), bf16)],
        56,
    )
    tokens_grad, gain_one_grad = run_kernel(
        first_back_kernel,
        5,
        at,
        (back_cols, qkv_w, tokens, gain_one, resid_grad),
        [((length, model_width), bf16), ((1, model_width), f32)],
        24,
    )

    both = jnp.concatenate(
        lax.optimization_barrier((attended, first_in, last_y, last_x))[:2], axis=0
    )
    both_sides = plane_sides(both)
    narrow_part = jnp.concatenate(
        [router_acc[:, :experts_all], gain_one_grad.T, gain_two_grad.T], axis=1
    )
    narrow_cols = -(-narrow_part.shape[1] // owners) * owners
    narrow_part = jnp.pad(narrow_part, ((0, 0), (0, narrow_cols - narrow_part.shape[1])))
    narrow_part = jnp.transpose(
        narrow_part.reshape(depth, 2, 2, shard_rows, owners, narrow_cols // owners),
        (1, 2, 4, 0, 3, 5),
    ).reshape(plane, depth, shard_rows * narrow_cols // owners)
    narrow_len = narrow_part.shape[2]
    narrow_rows = -(-narrow_len // dense_cols)
    each_rows = -(-narrow_rows // 4) * 4
    narrow_part = jnp.pad(
        narrow_part, ((0, 0), (0, 0), (0, each_rows * dense_cols - narrow_len))
    ).reshape(plane, depth * each_rows, dense_cols)
    narrow_part = jnp.pad(
        narrow_part.astype(bf16), ((0, 0), (0, 16 - depth * each_rows), (0, 0))
    )
    back_cols = lax.dynamic_update_slice(back_cols, narrow_part, (0, length, 0))
    back_cols = exchange(after(back_cols, down_sum), PLANE)
    shares = run_kernel(
        functools.partial(mixture_kernel, capacity, groups),
        10,
        at,
        (ids_all, after(gated[0], *both_sides), *gated[1:], down_w),
        [((length, model_width), bf16)] * plane,
        56,
    )
    sides, shares = lax.optimization_barrier((both_sides, shares))
    both_corner = plane_corner(sides, (back_cols,))
    both_pieces = plane_pieces(both, both_sides, both_corner)
    def placed(total):
        total = exchange(total, ("y", "c"))
        return total.reshape(local_count, shard_rows, hidden_width).astype(f32)

    kept_rows = -(-narrow_rows // 16) * 16
    wide_rows = local_count * shard_rows
    dense_shape = (depth, wide_rows + kept_rows, dense_cols)
    dense_part = pl.pallas_call(
        dense_grad_kernel,
        out_shape=jax.ShapeDtypeStruct(dense_shape, bf16),
        in_specs=[SCALARS, WHOLE] + [IN_HBM] * 8,
        out_specs=WHOLE,
        scratch_shapes=[
            pltpu.VMEM((plane, 2 * length, model_width), bf16),
            pltpu.SemaphoreType.DMA((plane,)),
        ],
        cost_estimate=cost(8),
        compiler_params=pltpu.CompilerParams(vmem_limit_bytes=32 * 2**20),
    )(at, back_cols, *both_pieces)
    dense_part, down_sum, gate_sum, up_sum = lax.optimization_barrier(
        (dense_part, down_sum, gate_sum, up_sum)
    )
    down_grad, gate_grad = placed(down_sum), placed(gate_sum)
    dense_sum = scatter_sum(dense_part.reshape(-1, dense_cols), "z")
    mixed = [over_core(near, far) for near, far in zip(shares[:4], shares[4:])]
    early = early_sums(mixed[1], mixed[2])
    first, down_grad, gate_grad = lax.optimization_barrier(
        (corner_first(mixed[3]), down_grad, gate_grad)
    )
    sums, up_grad, dense_sum = lax.optimization_barrier(
        (corner_sums(mixed[1], mixed[2], first), placed(up_sum), dense_sum)
    )
    last = corner_last(sums)
    mixture = jnp.concatenate(
        [left.astype(f32) + right.astype(f32) for left, right in zip(early, last)], axis=0
    )
    block_out = (resid + (mixture + mixed[0].astype(f32))).astype(bf16)

    wide_sum = dense_sum[: local_count * shard_rows].reshape(2, 2, 1, shard_rows, dense_cols)
    wide_sum = jnp.broadcast_to(wide_sum, (2, 2, owners, shard_rows, dense_cols)).reshape(
        plane, shard_rows, dense_cols
    )
    narrow_sum = dense_sum[local_count * shard_rows :][:narrow_rows]
    narrow_sum = jnp.broadcast_to(narrow_sum[None], (plane, narrow_rows, dense_cols))
    pad_rows = -(shard_rows + narrow_rows) % 16
    padding = jnp.zeros((plane, pad_rows, dense_cols), bf16)
    dense_sum = exchange(jnp.concatenate([wide_sum, narrow_sum, padding], axis=1), PLANE)
    query_grad, key_grad, value_grad, output_grad = run_kernel(
        finish_kernel,
        2,
        at,
        (dense_sum,),
        [
            ((shard_rows, q_cols), f32),
            ((shard_rows, kv_cols), f32),
            ((shard_rows, kv_cols), f32),
            ((shard_rows, model_width), f32),
        ],
    )
    narrow_sum = dense_sum[:, shard_rows : shard_rows + narrow_rows].reshape(
        2, 2, owners, narrow_rows * dense_cols
    )
    narrow_sum = narrow_sum[y, c, :, :narrow_len].reshape(owners, shard_rows, -1)
    narrow_sum = jnp.moveaxis(narrow_sum, 0, 1).reshape(shard_rows, narrow_cols).astype(f32)

    return (
        block_out,
        tokens_grad,
        narrow_sum[:, experts_all],
        query_grad,
        key_grad,
        value_grad,
        output_grad,
        narrow_sum[:, experts_all + 1],
        narrow_sum[:, :experts_all],
        gate_grad,
        up_grad,
        jnp.swapaxes(down_grad, 1, 2),
    )


def solution(mesh):
    groups, owners = mesh.shape["dp"], mesh.shape["expert"]
    grid = jax.sharding.Mesh(
        mesh.devices.reshape(groups // 4, 2, 2, owners), ("z", "y", "c", "x")
    )
    rows = P(("z", "y", "c", "x"), None)
    shard, shard_rows = P(GROUP), P(GROUP, None)
    expert = P("x", None, None)
    return jax.shard_map(
        local_pairs if owners == 2 else local_wide,
        mesh=grid,
        in_specs=(
            rows,
            shard,
            shard_rows,
            shard_rows,
            shard_rows,
            shard_rows,
            shard,
            shard_rows,
            expert,
            expert,
            expert,
            rows,
            P(("z", "y", "c", "x")),
            rows,
        ),
        out_specs=(
            rows,
            rows,
            shard,
            shard_rows,
            shard_rows,
            shard_rows,
            shard_rows,
            shard,
            shard_rows,
            P("x", GROUP, None),
            P("x", GROUP, None),
            P("x", None, GROUP),
        ),
        check_vma=False,
    )
```

```python
import functools
import math

import jax
import jax.numpy as jnp
from jax import lax
from jax.experimental import pallas as pl
from jax.experimental.pallas import tpu as pltpu
from jax.sharding import PartitionSpec as P

HQ = 12
HK = 2
HD = 128
MICRO = 2
PLANE = ("y", "c", "x")
GROUP = ("z", "y", "c")


def rms_scale(values, gain_vec):
    inverse = lax.rsqrt(jnp.mean(values * values, axis=-1, keepdims=True) + 1e-06)
    return values * inverse * gain_vec


def angles(length, head_size):
    positions = jnp.arange(length).astype(jnp.float32)
    freq_rates = jnp.exp(
        -(2.0 * jnp.arange(head_size // 2).astype(jnp.float32) / head_size) * math.log(1000000.0)
    )
    angle_tab = positions[:, None] * freq_rates[None, :]
    return (jnp.cos(angle_tab)[:, None, :], jnp.sin(angle_tab)[:, None, :])


def rotary(values, cosine_tab, sine_tab):
    half_dim = values.shape[-1] // 2
    first_half = values[..., :half_dim]
    second_half = values[..., half_dim:]
    return jnp.concatenate(
        [
            first_half * cosine_tab - second_half * sine_tab,
            second_half * cosine_tab + first_half * sine_tab,
        ],
        axis=-1,
    )


def expert_act(gate_pre, up_pre):
    return jax.nn.gelu(gate_pre, approximate=True) * up_pre


def left_product(left_mat, right_mat):
    return lax.dot_general(
        left_mat, right_mat, (((0,), (0,)), ((), ())), preferred_element_type=jnp.float32
    )


def gather(block, axes):
    return lax.all_gather(block, axes, axis=0, tiled=True)


def exchange(block, axes):
    return lax.all_to_all(block, axes, split_axis=0, concat_axis=0, tiled=True)


def scatter_sum(block, axes):
    return lax.psum_scatter(block, axes, scatter_dimension=0, tiled=True)


def by_owner(cols, parts):
    rows, total = cols.shape
    return jnp.moveaxis(cols.reshape(rows, parts, total // parts), 1, 0).reshape(
        parts * rows, total // parts
    )


def local_wide(
    tokens,
    norm1_gain,
    w_query,
    w_key,
    w_value,
    w_out,
    norm2_gain,
    w_router,
    w_gate,
    w_up,
    w_down,
    expert_ids,
    prefix_len,
    out_grad,
):
    bf16, f32 = jnp.bfloat16, jnp.float32
    length, model_width = tokens.shape
    shard_rows = w_query.shape[0]
    local_count, _, hidden_width = w_gate.shape
    owners = lax.axis_size("x")
    depth = lax.axis_size("z")
    plane = lax.axis_size(PLANE)
    experts_all = w_router.shape[1]
    top_count = expert_ids.shape[1]
    block_rows = length // MICRO
    capacity = 3 * block_rows * top_count // (2 * experts_all)
    plane_rows = plane * length
    blocks = plane_rows // block_rows
    group_size = HQ // HK
    score_scale = HD ** (-0.5)
    q_cols, kv_cols = w_query.shape[1], w_key.shape[1]
    own_local = lax.axis_index(("y", "c"))
    own_expert = lax.axis_index("x") * local_count + own_local
    own_place = lax.axis_index(PLANE)

    narrow = jnp.concatenate([w_router, norm1_gain[:, None], norm2_gain[:, None]], axis=1)
    narrow = jnp.pad(narrow, ((0, 0), (0, -narrow.shape[1] % 128)))
    packed = gather(jnp.concatenate([w_query, w_key, w_value, narrow], axis=1), GROUP)
    qkv_cols = q_cols + 2 * kv_cols
    qkv_w = packed[:, :qkv_cols]
    router_w = packed[:, qkv_cols : qkv_cols + experts_all]
    gains = packed[:, qkv_cols + experts_all : qkv_cols + experts_all + 2].T.astype(f32)
    gain_one, gain_two = gains[0], gains[1]
    output_w = gather(w_out, GROUP)

    ids_all = gather(expert_ids, PLANE)
    cot_all = gather(out_grad, PLANE)
    chosen_mask = jnp.any(
        ids_all[:, :, None] == jnp.arange(experts_all, dtype=jnp.int32)[None, None, :], axis=1
    )
    own_mask = jnp.any(ids_all == own_expert, axis=1).reshape(blocks, block_rows)
    place = jnp.cumsum(own_mask.astype(jnp.int32), axis=1) - 1
    dispatch = (
        own_mask[:, None, :]
        & (place[:, None, :] == jnp.arange(capacity, dtype=jnp.int32)[None, :, None])
    ).astype(bf16)

    cosine_tab, sine_tab = angles(length, HD)
    inputs_f = tokens.astype(f32)
    first_in = rms_scale(inputs_f, gain_one).astype(bf16)
    qkv = jnp.dot(first_in, qkv_w, preferred_element_type=f32)
    queries = (
        rotary(qkv[:, :q_cols].reshape(length, HQ, HD), cosine_tab, sine_tab)
        .astype(bf16)
        .reshape(length, HK, group_size, HD)
    )
    keys_rot = rotary(
        qkv[:, q_cols : q_cols + kv_cols].reshape(length, HK, HD), cosine_tab, sine_tab
    ).astype(bf16)
    values_b = qkv[:, q_cols + kv_cols :].astype(bf16).reshape(length, HK, HD)
    positions = jnp.arange(length)
    allowed = (positions[None, :] <= positions[:, None]) | (positions[None, :] < prefix_len[0])

    def masked_scores():
        scores = jnp.einsum("ihrd,jhd->hrij", queries, keys_rot, preferred_element_type=f32)
        return jnp.where(allowed, scores * score_scale, -1e30)

    masked = masked_scores()
    row_peak = jnp.max(masked, axis=-1, keepdims=True)
    log_total = row_peak + jnp.log(jnp.sum(jnp.exp(masked - row_peak), axis=-1, keepdims=True))
    prob_bf = jnp.exp(masked - log_total).astype(bf16)
    attended = jnp.einsum("hrij,jhd->ihrd", prob_bf, values_b, preferred_element_type=f32)
    attended = attended.reshape(length, HQ * HD).astype(bf16)
    resid = inputs_f + jnp.dot(attended, output_w, preferred_element_type=f32)
    second_in = rms_scale(resid, gain_two).astype(bf16)

    second_all = gather(second_in, PLANE)
    logits = jnp.dot(second_all, router_w, preferred_element_type=f32)
    gates_all = jax.nn.softmax(jnp.where(chosen_mask, logits, -jnp.inf), axis=-1)
    own_gates = lax.dynamic_index_in_dim(gates_all, own_expert, 1, keepdims=False)
    own_gates = own_gates.reshape(blocks, block_rows)
    gate_rows = jnp.einsum(
        "bct,bt->bc", dispatch.astype(f32), own_gates, precision=lax.Precision.HIGHEST
    )[:, :, None]
    gate_w = lax.dynamic_index_in_dim(w_gate, own_local, 0, keepdims=False)
    up_w = lax.dynamic_index_in_dim(w_up, own_local, 0, keepdims=False)
    down_w = lax.dynamic_index_in_dim(w_down, own_local, 0, keepdims=False)

    def to_rows(array):
        return jnp.einsum(
            "bct,btd->bcd",
            dispatch,
            array.reshape(blocks, block_rows, model_width),
            preferred_element_type=f32,
        ).astype(bf16)

    def to_tokens(rows):
        return (
            jnp.einsum("bct,bcd->btd", dispatch, rows.astype(bf16), preferred_element_type=f32)
            .astype(bf16)
            .reshape(plane_rows, model_width)
        )

    rows_in = to_rows(second_all)
    rows_cot = to_rows(cot_all)
    gate_pre = jnp.einsum("bcd,df->bcf", rows_in, gate_w, preferred_element_type=f32)
    up_pre = jnp.einsum("bcd,df->bcf", rows_in, up_w, preferred_element_type=f32)
    hidden, act_pull = jax.vjp(expert_act, gate_pre, up_pre)
    gated = (gate_rows * hidden).astype(bf16)
    down_part = jnp.einsum("bcd,bcf->df", rows_cot, gated, preferred_element_type=f32)
    down_sum = scatter_sum(down_part.astype(bf16), "z")
    cot_hidden = jnp.einsum("bcd,fd->bcf", rows_cot, down_w, preferred_element_type=f32)
    gate_signal_rows = jnp.sum(hidden * cot_hidden, axis=-1)
    gate_pgrad, up_pgrad = act_pull(gate_rows * cot_hidden)
    gate_pgrad = gate_pgrad.astype(bf16)
    up_pgrad = up_pgrad.astype(bf16)
    gate_part = jnp.einsum("bcd,bcf->df", rows_in, gate_pgrad, preferred_element_type=f32)
    gate_sum = scatter_sum(gate_part.astype(bf16), "z")
    up_part = jnp.einsum("bcd,bcf->df", rows_in, up_pgrad, preferred_element_type=f32)
    up_sum = scatter_sum(up_part.astype(bf16), "z")
    rows_grad = jnp.einsum("bcf,df->bcd", gate_pgrad, gate_w, preferred_element_type=f32)
    rows_grad = rows_grad + jnp.einsum("bcf,df->bcd", up_pgrad, up_w, preferred_element_type=f32)
    second_back = scatter_sum(to_tokens(rows_grad), PLANE).astype(f32)
    gate_signal = jnp.einsum(
        "bct,bc->bt", dispatch.astype(f32), gate_signal_rows, precision=lax.Precision.HIGHEST
    )
    gate_signal = exchange(gate_signal.reshape(plane, length), PLANE)
    gate_signal = jnp.transpose(
        gate_signal.reshape(local_count, owners, length), (2, 1, 0)
    ).reshape(length, experts_all)
    expert_rows = jnp.einsum("bcf,fd->bcd", gated, down_w, preferred_element_type=f32)
    mixture = scatter_sum(to_tokens(expert_rows), PLANE).astype(f32)
    block_out = (resid + mixture).astype(bf16)

    cotangent = out_grad.astype(f32)
    gate_probs = lax.dynamic_slice_in_dim(gates_all, own_place * length, length, 0)
    logit_grad = (
        gate_probs
        * (gate_signal - jnp.sum(gate_probs * gate_signal, axis=-1, keepdims=True))
    ).astype(bf16)
    router_acc = left_product(second_in, logit_grad)
    second_grad = second_back + jnp.dot(logit_grad, router_w.T, preferred_element_type=f32)
    _, norm_two_pull = jax.vjp(rms_scale, resid, gain_two)
    resid_norm_grad, gain_two_grad = norm_two_pull(second_grad)
    resid_grad = cotangent + resid_norm_grad
    branch_grad = resid_grad.astype(bf16)

    attended_all = gather(attended, PLANE)
    branch_cols = exchange(by_owner(branch_grad, plane), PLANE)
    output_part = left_product(attended_all, branch_cols)
    attended_grad = jnp.dot(branch_grad, output_w.T, preferred_element_type=f32).astype(bf16)
    attended_grad = attended_grad.reshape(length, HK, group_size, HD)
    masked = masked_scores()
    prob_full = jnp.exp(masked - log_total)
    prob_bf = prob_full.astype(bf16)
    prob_grad = jnp.einsum("ihrd,jhd->hrij", attended_grad, values_b, preferred_element_type=f32)
    row_inner = jnp.sum(prob_full * prob_grad, axis=-1, keepdims=True)
    score_grad = (prob_full * (prob_grad - row_inner)).astype(bf16)
    query_rot_grad = (
        jnp.einsum("hrij,jhd->ihrd", score_grad, keys_rot, preferred_element_type=f32)
        * score_scale
    )
    query_back = rotary(query_rot_grad.reshape(length, HQ, HD), cosine_tab, -sine_tab)
    query_back = query_back.astype(bf16).reshape(length, HQ * HD)
    key_rot_grad = (
        jnp.einsum("hrij,ihrd->jhd", score_grad, queries, preferred_element_type=f32)
        * score_scale
    )
    key_back = rotary(key_rot_grad, cosine_tab, -sine_tab).astype(bf16).reshape(length, HK * HD)
    value_back = jnp.einsum("hrij,ihrd->jhd", prob_bf, attended_grad, preferred_element_type=f32)
    value_back = value_back.astype(bf16).reshape(length, HK * HD)
    qkv_back = jnp.concatenate([query_back, key_back, value_back], axis=1)
    first_all = gather(first_in, PLANE)
    qkv_part = left_product(first_all, exchange(by_owner(qkv_back, plane), PLANE))
    first_grad = lax.dot_general(
        qkv_back, qkv_w, (((1,), (1,)), ((), ())), preferred_element_type=f32
    )
    _, norm_one_pull = jax.vjp(rms_scale, inputs_f, gain_one)
    input_norm_grad, gain_one_grad = norm_one_pull(first_grad)
    tokens_grad = (resid_grad + input_norm_grad).astype(bf16)

    narrow_part = jnp.concatenate(
        [router_acc, gain_one_grad[:, None], gain_two_grad[:, None]], axis=1
    ).astype(bf16)
    narrow_cols = narrow_part.shape[1]
    narrow_sum = lax.psum(scatter_sum(narrow_part, GROUP), "x").astype(f32)
    dense_part = jnp.concatenate([qkv_part, output_part], axis=1).astype(bf16)
    dense_sum = scatter_sum(dense_part, "z")
    dense_cols = dense_sum.shape[1]
    dense_sum = gather(dense_sum, PLANE).reshape(plane, local_count, shard_rows, dense_cols)
    dense_sum = lax.dynamic_index_in_dim(dense_sum, own_local, 1, keepdims=False).astype(f32)
    dense_sum = jnp.moveaxis(dense_sum, 0, 1)
    qkv_width = qkv_cols // plane
    qkv_sum = dense_sum[:, :, :qkv_width].reshape(shard_rows, qkv_cols)
    output_sum = dense_sum[:, :, qkv_width:].reshape(shard_rows, model_width)

    def placed(total):
        total = exchange(total, ("y", "c"))
        return total.reshape(local_count, shard_rows, hidden_width).astype(f32)

    return (
        block_out,
        tokens_grad,
        narrow_sum[:, experts_all],
        qkv_sum[:, :q_cols],
        qkv_sum[:, q_cols : q_cols + kv_cols],
        qkv_sum[:, q_cols + kv_cols :],
        output_sum,
        narrow_sum[:, experts_all + 1],
        narrow_sum[:, :experts_all],
        placed(gate_sum),
        placed(up_sum),
        jnp.swapaxes(placed(down_sum), 1, 2),
    )


def rounded(values):
    return lax.reduce_precision(values, 8, 7).astype(jnp.bfloat16)


def after(block, *others):
    return lax.optimization_barrier((block,) + others)[0]


def swap(block, axis):
    return lax.ppermute(block, axis, [(0, 1), (1, 0)])


def shifts(block):
    depth = lax.axis_size("z")
    return [
        lax.ppermute(block, "z", [(i, (i + k) % depth) for i in range(depth)])
        for k in range(1, depth)
    ]


def plane_sides(block):
    return swap(block, "x"), swap(block, "y")


def plane_corner(sides, before=(), later=()):
    over_x, over_y = sides
    half = over_x.shape[0] // 2
    over_y, over_x = lax.optimization_barrier((over_y[:half], over_x[half:]) + before)[:2]
    parts = (swap(over_y, "x"), swap(over_x, "y"))
    return jnp.concatenate(lax.optimization_barrier(parts + later)[:2], axis=0)


def plane_pieces(block, sides=None, corner=None):
    sides = plane_sides(block) if sides is None else sides
    corner = plane_corner(sides) if corner is None else corner
    pieces = [block, *sides, corner]
    return pieces + [swap(piece, "c") for piece in pieces]


def small_gather(block):
    for axis in ("x", "y", "c"):
        block = jnp.concatenate([block, swap(block, axis)], axis=1)
    return block


def small_group_gather(block):
    depth = lax.axis_size("z")
    order = jnp.stack(([block] + shifts(block))[::-1] * 2)
    start = (depth - 1 - lax.axis_index("z")) % depth
    total = lax.dynamic_slice_in_dim(order, start, depth, 0)[:, None, None]
    for dim, axis in ((1, "y"), (2, "c")):
        other = swap(total, axis)
        last = lax.axis_index(axis) == 1
        pair = [jnp.where(last, other, total), jnp.where(last, total, other)]
        total = jnp.concatenate(pair, axis=dim)
    return total.reshape(-1, block.shape[1])


def add(left, right):
    return rounded(left.astype(jnp.float32) + right.astype(jnp.float32))


def over_core(near, far):
    return add(near, swap(far, "c"))


def early_sums(over_x, over_y):
    half = over_x.shape[0] // 2
    return swap(over_x[:half], "x"), swap(over_y[half:], "y")


def corner_first(corner):
    half = corner.shape[0] // 2
    return swap(corner[:half], "x"), swap(corner[half:], "y")


def corner_last(over_x, over_y, first):
    half = over_x.shape[0] // 2
    over_y, over_x = add(over_y[:half], first[0]), add(over_x[half:], first[1])
    return swap(over_y, "y"), swap(over_x, "x"), over_y, over_x


def cost(micros):
    return pl.CostEstimate(flops=micros * 10**9, bytes_accessed=micros * 10**6, transcendentals=0)


def dot(left, right, dims=((1,), (0,)), precision=None):
    return lax.dot_general(
        left, right, (dims, ((), ())), precision=precision, preferred_element_type=jnp.float32
    )


WHOLE = pl.BlockSpec(memory_space=pltpu.VMEM)
IN_HBM = pl.BlockSpec(memory_space=pltpu.HBM)
SCALARS = pl.BlockSpec(memory_space=pltpu.SMEM)


def run_kernel(kernel, micros, at, operands, outs, megabytes=16, scratch=(), hbm_in=0, hbm_out=0):
    return pl.pallas_call(
        kernel,
        out_shape=[jax.ShapeDtypeStruct(shape, dtype) for shape, dtype in outs],
        in_specs=[SCALARS] + [WHOLE] * (len(operands) - hbm_in) + [IN_HBM] * hbm_in,
        out_specs=[WHOLE] * (len(outs) - hbm_out) + [IN_HBM] * hbm_out,
        scratch_shapes=scratch,
        cost_estimate=cost(micros),
        compiler_params=pltpu.CompilerParams(vmem_limit_bytes=megabytes * 2**20),
    )(at, *operands)


def place_pieces(at, refs, weight):
    depth = weight.shape[1]
    for n, ref in enumerate(refs):
        dc, dy, dx = n // 4, n // 2 % 2, n % 2
        for k in range(depth):
            z = lax.rem(at[3] + depth - k, depth)
            weight[at[2] ^ dx, z, at[0] ^ dy, at[1] ^ dc] = ref[k]


def rms_kernel(values, gain):
    inverse = lax.rsqrt(jnp.mean(values * values, axis=-1, keepdims=True) + 1e-06)
    return (values * inverse * gain).astype(jnp.bfloat16)


def rms_back(values, gain, grad):
    inverse = lax.rsqrt(jnp.mean(values * values, axis=-1, keepdims=True) + 1e-06)
    normed = values * inverse
    gain_grad = jnp.sum(grad * normed, axis=0, keepdims=True)
    grad = grad * gain
    along = jnp.mean(grad * normed, axis=-1, keepdims=True)
    return inverse * (grad - normed * along), gain_grad


def turned(values, cosine_tab, sine_tab):
    return values * cosine_tab + pltpu.roll(values, HD // 2, 1) * sine_tab


def attend_kernel(at, tokens, gain, cosine, sine, *refs):
    first_ref, query_ref, key_ref, value_ref, out_ref = refs[8:13]
    prob_out, weight_out, prob_ref, weight, sems = refs[13:]
    place_pieces(at, refs[:8], weight)
    copies = [pltpu.make_async_copy(weight, weight_out, sems.at[HK])]
    copies[0].start()
    length = tokens.shape[0]
    first_in = rms_kernel(tokens[...].astype(jnp.float32), gain[...])
    first_ref[...] = first_in
    rows = lax.broadcasted_iota(jnp.int32, (length, length), 0)
    cols = lax.broadcasted_iota(jnp.int32, (length, length), 1)
    allowed = (cols <= rows) | (cols < at[4])
    cosine_tab, sine_tab = cosine[...], sine[...]
    group_size = HQ // HK
    for group in range(HK):
        matrix = weight[group].reshape(first_in.shape[1], -1)
        qkv = dot(first_in, matrix)
        at_key = group_size * HD
        key = turned(qkv[:, at_key : at_key + HD], cosine_tab, sine_tab).astype(jnp.bfloat16)
        value = qkv[:, at_key + HD :].astype(jnp.bfloat16)
        key_ref[:, group * HD : (group + 1) * HD] = key
        value_ref[:, group * HD : (group + 1) * HD] = value
        for member in range(group_size):
            head = group * group_size + member
            here = slice(head * HD, (head + 1) * HD)
            query = turned(qkv[:, member * HD : (member + 1) * HD], cosine_tab, sine_tab)
            query = query.astype(jnp.bfloat16)
            query_ref[:, here] = query
            scores = dot(query, key, ((1,), (1,)))
            scores = jnp.where(allowed, scores * HD ** (-0.5), -1e30)
            weights = jnp.exp(scores - jnp.max(scores, axis=-1, keepdims=True))
            prob = weights * (1.0 / jnp.sum(weights, axis=-1, keepdims=True))
            prob = prob.astype(jnp.bfloat16)
            prob_ref[head] = prob
            out_ref[:, here] = dot(prob, value).astype(jnp.bfloat16)
        here = pl.ds(group * group_size, group_size)
        copies.append(
            pltpu.make_async_copy(prob_ref.at[here], prob_out.at[here], sems.at[group])
        )
        copies[-1].start()
    for copy in copies:
        copy.wait()


def project_kernel(at, tokens, gain, attended, *refs):
    resid_ref, second_ref, weight_out, weight, sem = refs[8:]
    place_pieces(at, refs[:8], weight)
    copy = pltpu.make_async_copy(weight, weight_out, sem)
    copy.start()
    heads = attended[...]
    halves = [dot(heads, weight[half].reshape(heads.shape[1], -1)) for half in range(2)]
    resid = tokens[...].astype(jnp.float32) + jnp.concatenate(halves, axis=1)
    resid_ref[...] = resid
    second_ref[...] = rms_kernel(resid, gain[...])
    copy.wait()


def one_hot(slots, capacity, dtype):
    shape = (capacity, slots.shape[1])
    return (slots == lax.broadcasted_iota(jnp.int32, shape, 0)).astype(jnp.float32).astype(dtype)


def slots_of(ids, expert, start, rows):
    named = jnp.any(ids[:, start : start + rows] == expert, axis=0, keepdims=True)
    named = named.astype(jnp.float32)
    before = lax.broadcasted_iota(jnp.int32, (rows, rows), 0)
    upto = lax.broadcasted_iota(jnp.int32, (rows, rows), 1)
    counts = dot(named.astype(jnp.bfloat16), (before <= upto).astype(jnp.float32).astype(jnp.bfloat16))
    return jnp.where(named > 0.0, counts - 1.0, -1.0).astype(jnp.int32)


def spread(picks, capacity, rows, outs):
    rows = rows.astype(jnp.bfloat16)
    block = picks[0].shape[1]
    for n in range(len(picks) // 2):
        for part in range(2):
            pick = picks[2 * n + part]
            at_row = (2 * n + part) * capacity
            tokens = dot(pick, rows[at_row : at_row + capacity], ((0,), (0,)))
            outs[n][part * block : (part + 1) * block] = tokens.astype(jnp.bfloat16)


def expert_kernel(capacity, pieces, earlier, at, ids, router, *refs):
    count = len(pieces)
    second, cot = refs[:count], refs[count : 2 * count]
    gate_w, up_w, down_w = refs[2 * count : 2 * count + 3]
    before = refs[2 * count + 3 : 2 * count + 3 + 2 * earlier]
    refs = refs[2 * count + 3 + 2 * earlier :]
    rows_in, rows_cot, gated_ref, gate_back, up_back, gates_ref = refs[:6]
    backs, gate_rows = refs[6 : 6 + count], refs[-1]
    f32, bf16 = jnp.float32, jnp.bfloat16
    length, width = second[0].shape
    wide = router.shape[1]
    half = length // 2
    picks = []
    experts = lax.broadcasted_iota(jnp.int32, (wide, length), 0)
    for n, piece in enumerate(pieces):
        tokens = second[n][...]
        named = ids[:, piece * length : (piece + 1) * length]
        chosen = functools.reduce(
            jnp.logical_or, [named[k : k + 1] == experts for k in range(named.shape[0])]
        )
        logits = jnp.where(chosen, dot(router[...], tokens, ((0,), (1,))), -1e30)
        weights = jnp.exp(logits - jnp.max(logits, axis=0, keepdims=True))
        gates = weights * (1.0 / jnp.sum(weights, axis=0, keepdims=True))
        if n == 0:
            gates_ref[...] = gates
        own = jnp.sum(jnp.where(experts == at[5], gates, 0.0), axis=0, keepdims=True)
        for part in range(2):
            here = slice(part * half, (part + 1) * half)
            place = slice((2 * n + part) * capacity, (2 * n + part + 1) * capacity)
            slots = slots_of(ids, at[5], piece * length + part * half, half)
            pick = one_hot(slots, capacity, f32)
            picks.append(pick.astype(bf16))
            rows_in[place] = dot(picks[-1], tokens[here]).astype(bf16)
            rows_cot[place] = dot(picks[-1], cot[n][here]).astype(bf16)
            gate_rows[place] = jnp.sum(pick * own[:, here], axis=1, keepdims=True)
    gate = gate_rows[...]
    gate_pre = dot(rows_in[...], gate_w[...])
    up_pre = dot(rows_in[...], up_w[...])
    cot_hidden = dot(rows_cot[...], down_w[...], ((1,), (1,)))
    scale = math.sqrt(2.0 / math.pi)
    square = gate_pre * gate_pre
    bent = jnp.tanh(scale * gate_pre * (1.0 + 0.044715 * square))
    open_part = 0.5 * (1.0 + bent)
    active = gate_pre * open_part
    slope = open_part + 0.5 * gate_pre * (1.0 - bent * bent) * scale * (
        1.0 + 3 * 0.044715 * square
    )
    hidden = active * up_pre
    gated_ref[...] = (gate * hidden).astype(bf16)
    signal = jnp.sum(hidden * cot_hidden, axis=1, keepdims=True)
    back = gate * cot_hidden
    gate_back[...] = (back * up_pre * slope).astype(bf16)
    up_back[...] = (back * active).astype(bf16)
    high = signal.astype(bf16)
    low = (signal - high.astype(f32)).astype(bf16)
    lanes = lax.broadcasted_iota(jnp.int32, (signal.shape[0], wide), 1)
    signal = jnp.where(lanes == at[5], high.astype(f32), 0.0)
    signal = jnp.where(lanes == at[5] + wide // 2, low.astype(f32), signal)
    by_rows = ((1,), (1,))
    rows = dot(gate_back[...], gate_w[...], by_rows) + dot(up_back[...], up_w[...], by_rows)
    spread(picks, capacity, jnp.concatenate([rows, signal], axis=1), backs)
    if earlier:
        lefts = [ref[...] for ref in (*before[:earlier], rows_cot)]
        rights = [ref[...] for ref in (*before[earlier:], gated_ref)]
        total = dot(jnp.concatenate(lefts, axis=0), jnp.concatenate(rights, axis=0), ((0,), (0,)))
        refs[6 + count][...] = total.astype(bf16)


def run_expert(pieces, at, ids, router, weights, second, cot, capacity, before=()):
    count = len(pieces)
    rows, wide = 2 * count * capacity, router.shape[1]
    (length, width), hidden = second[0].shape, weights[0].shape[1]
    bf16, f32 = jnp.bfloat16, jnp.float32
    outs = [(rows, width)] * 2 + [(rows, hidden)] * 3
    outs = [(shape, bf16) for shape in outs] + [((wide, length), f32)]
    outs = outs + [((length, width + wide), bf16)] * count
    if before:
        outs = outs + [((width, hidden), bf16)]
    return run_kernel(
        functools.partial(expert_kernel, capacity, pieces, len(before) // 2),
        4 * count,
        at,
        (ids, router, *second, *cot, *weights, *before),
        outs,
        4 + 3 * count + 4 * bool(before),
        [pltpu.VMEM((rows, 1), f32)],
    )


def mixture_kernel(capacity, groups, at, ids, *refs):
    gated, down_w, outs = refs[: len(groups)], refs[len(groups)], refs[len(groups) + 1 :]
    length = outs[0].shape[0]
    for pieces, rows in zip(groups, gated):
        picks = []
        for piece in pieces:
            for part in range(2):
                start = piece * length + part * length // 2
                slots = slots_of(ids, at[5], start, length // 2)
                picks.append(one_hot(slots, capacity, jnp.bfloat16))
        spread(picks, capacity, dot(rows[...], down_w[...]), [outs[piece] for piece in pieces])


def row_sum_kernel(parts, at, *refs):
    arrays = [
        jnp.concatenate([ref[...] for ref in refs[n : n + parts]], axis=0)
        for n in range(0, len(refs) - len(refs) // (parts + 1), parts)
    ]
    outs = refs[len(arrays) * parts :]
    for out, right in zip(outs, arrays[1:]):
        out[...] = dot(arrays[0], right, ((0,), (0,))).astype(jnp.bfloat16)


def row_sums(at, left, *rights):
    operands = [part for parts in (left, *rights) for part in parts]
    outs = [((left[0].shape[1], right[0].shape[1]), jnp.bfloat16) for right in rights]
    kernel = functools.partial(row_sum_kernel, len(left))
    return run_kernel(kernel, 4 * len(rights), at, operands, outs, 24 if len(rights) == 1 else 56)


def branch_back_kernel(
    at, near, far, first_x, first_y, last_y, last_x, resid, gain, second, gates, router, cot, weight, *outs
):
    resid_grad_ref, branch_ref, attended_ref, router_ref, gain_ref = outs
    f32, bf16 = jnp.float32, jnp.bfloat16
    halves = [first_x[...].astype(f32) + last_y[...], first_y[...].astype(f32) + last_x[...]]
    total = near[...].astype(f32) + far[...] + jnp.concatenate(halves, axis=0)
    width = resid.shape[1]
    signal = total[:, width:]
    signal = signal + pltpu.roll(signal, signal.shape[1] // 2, 1)
    chosen = gates[...].T
    logit_grad = chosen * (signal - jnp.sum(chosen * signal, axis=-1, keepdims=True))
    logit_grad = logit_grad.astype(bf16)
    second_grad = total[:, :width] + dot(logit_grad, router[...], ((1,), (1,)))
    norm_grad, gain_grad = rms_back(resid[...], gain[...], second_grad)
    gain_ref[...] = gain_grad
    resid_grad = cot[...].astype(f32) + norm_grad
    resid_grad_ref[...] = resid_grad
    branch = resid_grad.astype(bf16)
    branch_ref[...] = branch
    wide = weight.shape[2]
    attended_ref[...] = (
        dot(branch[:, :wide], weight[0], ((1,), (1,)))
        + dot(branch[:, wide:], weight[1], ((1,), (1,)))
    ).astype(bf16)
    router_ref[...] = dot(second[...], logit_grad, ((0,), (0,)))


def attend_back_kernel(
    at, attended, probs, queries, keys, values, cosine, sine, branch, back_ref
):
    f32, bf16 = jnp.float32, jnp.bfloat16
    cosine_tab, sine_tab = cosine[...], -sine[...]
    group_size = HQ // HK
    places, length = back_ref.shape[0], branch.shape[0]
    branch_width = branch.shape[1] // places
    width = back_ref.shape[2] - branch_width
    for place in range(places):
        here = slice(place * branch_width, (place + 1) * branch_width)
        back_ref[place, :length, width:] = branch[:, here]
        back_ref[place, length:] = jnp.zeros((back_ref.shape[1] - length, back_ref.shape[2]), bf16)
    scale = HD ** (-0.5)

    def put(position, block):
        back_ref[position // width, :length, position % width : position % width + HD] = block

    for group in range(HK):
        own = slice(group * HD, (group + 1) * HD)
        key, value = keys[:, own], values[:, own]
        key_grad = value_grad = 0.0
        start = group * (group_size + 2) * HD
        for member in range(group_size):
            head = group * group_size + member
            here = slice(head * HD, (head + 1) * HD)
            out_grad, query, prob = attended[:, here], queries[:, here], probs[head]
            prob_grad = dot(out_grad, value, ((1,), (1,)))
            prob_f = prob.astype(f32)
            inner = jnp.sum(prob_f * prob_grad, axis=-1, keepdims=True)
            score_grad = (prob_f * (prob_grad - inner)).astype(bf16)
            query_grad = turned(dot(score_grad, key) * scale, cosine_tab, sine_tab)
            put(start + member * HD, query_grad.astype(bf16))
            key_grad = key_grad + dot(score_grad, query, ((0,), (0,)))
            value_grad = value_grad + dot(prob, out_grad, ((0,), (0,)))
        key_grad = turned(key_grad * scale, cosine_tab, sine_tab)
        put(start + group_size * HD, key_grad.astype(bf16))
        put(start + (group_size + 1) * HD, value_grad.astype(bf16))


def first_back_kernel(at, back, weight, tokens, gain, resid_grad, tokens_ref, gain_ref):
    f32 = jnp.float32
    parts = back.shape[0]
    cols = weight.shape[0] * weight.shape[2] // parts
    first_grad = 0.0
    for part in range(parts):
        group, place = divmod(part * cols, weight.shape[2])
        first_grad = first_grad + dot(
            back[part, : tokens.shape[0], :cols], weight[group, :, place : place + cols], ((1,), (1,))
        )
    norm_grad, gain_grad = rms_back(tokens[...].astype(f32), gain[...], first_grad)
    gain_ref[...] = gain_grad
    tokens_ref[...] = (resid_grad[...] + norm_grad).astype(jnp.bfloat16)


def dense_grad_kernel(at, back, *refs):
    pieces, out_ref, held, sems = refs[:8], refs[8], refs[9], refs[10]
    copies = [
        pltpu.make_async_copy(piece, held.at[n], sems.at[n]) for n, piece in enumerate(pieces)
    ]
    for copy in copies:
        copy.start()
    depth, rows, cols = out_ref.shape
    length = held.shape[1] // 2
    qkv_width = cols - held.shape[2] // back.shape[0]
    narrow = sum(back[place, length:].astype(jnp.float32) for place in range(back.shape[0]))
    sums = [0.0, 0.0]
    for n, copy in enumerate(copies):
        copy.wait()
        dc, dy, dx = n // 4, n // 2 % 2, n % 2
        place = 4 * (at[0] ^ dy) + 2 * (at[1] ^ dc) + (at[2] ^ dx)
        own = back[place, :length]
        sums[0] = sums[0] + dot(held[n, length:], own[:, :qkv_width], ((0,), (0,)))
        sums[1] = sums[1] + dot(held[n, :length], own[:, qkv_width:], ((0,), (0,)))
    wide = held.shape[2] // depth
    each = 4
    for z in range(depth):
        here = slice(z * wide, (z + 1) * wide)
        both = jnp.concatenate([part[here] for part in sums], axis=1)
        out_ref[z, :wide] = both.astype(jnp.bfloat16)
        kept = [narrow[z * each : (z + 1) * each], jnp.zeros((rows - wide - each, cols), jnp.float32)]
        out_ref[z, wide:] = jnp.concatenate(kept, axis=0).astype(jnp.bfloat16)


def finish_kernel(at, sums, query_ref, key_ref, value_ref, output_ref):
    places, _, cols = sums.shape
    rows, out_width = query_ref.shape[0], output_ref.shape[1] // places
    width = cols - out_width
    for place in range(places):
        block = sums[place, :rows].astype(jnp.float32)
        output_ref[:, place * out_width : (place + 1) * out_width] = block[:, width:]
        for at_col in range(0, width, HD):
            group, head = divmod((place * width + at_col) // HD, HQ // HK + 2)
            part = block[:, at_col : at_col + HD]
            if head < HQ // HK:
                start = (group * (HQ // HK) + head) * HD
                query_ref[:, start : start + HD] = part
            elif head == HQ // HK:
                key_ref[:, group * HD : (group + 1) * HD] = part
            else:
                value_ref[:, group * HD : (group + 1) * HD] = part


def local_pairs(
    tokens,
    norm1_gain,
    w_query,
    w_key,
    w_value,
    w_out,
    norm2_gain,
    w_router,
    w_gate,
    w_up,
    w_down,
    expert_ids,
    prefix_len,
    out_grad,
):
    bf16, f32 = jnp.bfloat16, jnp.float32
    length, model_width = tokens.shape
    shard_rows = w_query.shape[0]
    local_count, _, hidden_width = w_gate.shape
    owners = lax.axis_size("x")
    depth = lax.axis_size("z")
    plane = lax.axis_size(PLANE)
    experts_all = w_router.shape[1]
    block_rows = length // MICRO
    capacity = 3 * block_rows * expert_ids.shape[1] // (2 * experts_all)
    plane_rows = plane * length
    blocks = plane_rows // block_rows
    q_cols, kv_cols = w_query.shape[1], w_key.shape[1]
    qkv_cols = q_cols + 2 * kv_cols
    q_group, out_half = q_cols // HK, model_width // 2
    y, c, x, z = (lax.axis_index(axis) for axis in ("y", "c", "x", "z"))
    own_local = 2 * y + c
    own_expert = x * local_count + own_local
    at = jnp.stack([y, c, x, z, prefix_len[0], own_expert, own_local])

    own_half = jnp.concatenate(
        [
            lax.dynamic_slice_in_dim(part, x * (part.shape[1] // 2), part.shape[1] // 2, 1)
            for part in (w_query, w_key, w_value, w_out)
        ],
        axis=1,
    )
    narrow = jnp.concatenate([w_router, norm1_gain[:, None], norm2_gain[:, None]], axis=1)
    narrow = jnp.pad(narrow, ((0, 0), (0, 128 - narrow.shape[1])))
    router_w = small_group_gather(narrow)
    ids_all = small_gather(expert_ids.T)
    column = [own_half] + shifts(own_half)
    cot_sides = plane_sides(after(out_grad, router_w, ids_all))
    qkv_half = qkv_cols // 2
    qkv_column = jnp.stack([part[:, :qkv_half] for part in column])
    out_column = jnp.stack([part[:, qkv_half:] for part in column])
    qkv_column, out_column = lax.optimization_barrier((qkv_column, out_column, *cot_sides))[:2]
    sliced = after(own_local, column[-1])
    gate_w, up_w, down_w = (
        lax.dynamic_index_in_dim(weight, sliced, 0, keepdims=False)
        for weight in (w_gate, w_up, w_down)
    )
    qkv_sides = plane_sides(qkv_column)
    gains = router_w[:, experts_all : experts_all + 2].T.astype(f32)
    gain_one, gain_two = gains[:1], gains[1:]
    qkv_corner = plane_corner(qkv_sides, (gate_w, up_w, down_w, gain_one, gain_two))
    out_sides = plane_sides(after(out_column, *qkv_sides))
    qkv_pieces = plane_pieces(qkv_column, qkv_sides, qkv_corner)
    cosine_tab, sine_tab = angles(length, HD)
    cosine_all = jnp.concatenate([cosine_tab, cosine_tab], axis=2)[:, 0]
    sine_all = jnp.concatenate([-sine_tab, sine_tab], axis=2)[:, 0]
    weight_lead = (2, depth, 2, 2, shard_rows)
    first_in, queries, keys_rot, values_b, attended, probs, qkv_w = run_kernel(
        attend_kernel,
        11,
        at,
        (tokens, gain_one, cosine_all, sine_all, *qkv_pieces),
        [
            ((length, model_width), bf16),
            ((length, q_cols), bf16),
            ((length, kv_cols), bf16),
            ((length, kv_cols), bf16),
            ((length, q_cols), bf16),
            ((HQ, length, length), bf16),
            (weight_lead + (qkv_half,), bf16),
        ],
        28,
        [
            pltpu.VMEM((HQ, length, length), bf16),
            pltpu.VMEM(weight_lead + (qkv_half,), bf16),
            pltpu.SemaphoreType.DMA((HK + 1,)),
        ],
        hbm_out=2,
    )
    out_sides = lax.optimization_barrier((*out_sides, attended))[:2]
    out_corner = plane_corner(out_sides)
    cot_corner = plane_corner(cot_sides)
    out_pieces = plane_pieces(out_column, out_sides, out_corner)
    cot_pieces = plane_pieces(out_grad, cot_sides, cot_corner)
    resid, second_in, output_w = run_kernel(
        project_kernel,
        4,
        at,
        (tokens, after(gain_two, cot_corner), attended, *out_pieces),
        [
            ((length, model_width), f32),
            ((length, model_width), bf16),
            (weight_lead + (out_half,), bf16),
        ],
        44,
        [pltpu.VMEM(weight_lead + (out_half,), bf16), pltpu.SemaphoreType.DMA],
        hbm_out=1,
    )
    qkv_w = qkv_w.reshape(HK, model_width, qkv_half)
    output_w = output_w.reshape(2, q_cols, out_half)

    expert = functools.partial(
        run_expert,
        at=at,
        ids=ids_all,
        router=router_w,
        weights=(gate_w, up_w, down_w),
        capacity=capacity,
    )
    second_sides = plane_sides(second_in)
    groups = ((0, 4), (1, 5, 2, 6), (3, 7))
    second_pieces = {0: second_in, 4: swap(second_in, "c")}

    def run_group(pieces, before=()):
        return expert(
            pieces,
            before=before,
            second=[second_pieces[piece] for piece in pieces],
            cot=[cot_pieces[piece] for piece in pieces],
        )

    stage_own = run_group(groups[0])
    second_sides = lax.optimization_barrier((*second_sides, stage_own[0]))[:2]
    for piece, block in zip((1, 2), second_sides):
        second_pieces[piece], second_pieces[piece + 4] = block, swap(block, "c")
    stage_sides = run_group(groups[1])
    second_corner = plane_corner(second_sides, later=(stage_sides[0],))
    second_pieces[3], second_pieces[7] = second_corner, swap(second_corner, "c")
    own_near, own_far = stage_own[6:]
    own_far = swap(own_far, "c")
    x_near, x_far, y_near, y_far = stage_sides[6:]
    back_x, back_y = over_core(x_near, x_far), over_core(y_near, y_far)
    first_x, first_y = early_sums(back_x, back_y)
    two = (stage_own, stage_sides)
    stage_corner = run_group(groups[2], [stage[1] for stage in two] + [stage[2] for stage in two])
    *stage_corner, down_part = stage_corner
    corner = over_core(*stage_corner[6:])
    passed = corner_first(corner)
    stages = (stage_own, stage_sides, stage_corner)
    rows_in, rows_cot, gated, gate_back, up_back = ([stage[n] for stage in stages] for n in range(5))
    gates = stage_own[5]
    last_y, last_x = corner_last(back_x, back_y, passed)[:2]
    down_sum = scatter_sum(down_part, "z")

    resid_grad, branch_grad, attended_grad, router_acc, gain_two_grad = run_kernel(
        branch_back_kernel,
        6,
        at,
        (
            own_near,
            own_far,
            first_x,
            first_y,
            last_y,
            last_x,
            resid,
            gain_two,
            second_in,
            gates,
            router_w,
            out_grad,
            output_w,
        ),
        [
            ((length, model_width), f32),
            ((length, model_width), bf16),
            ((length, q_cols), bf16),
            ((model_width, 128), f32),
            ((1, model_width), f32),
        ],
        56,
    )
    gate_part, up_part = row_sums(
        at, [after(rows_in[0], resid_grad)] + rows_in[1:], gate_back, up_back
    )
    gate_sum, up_sum = scatter_sum(gate_part, "z"), scatter_sum(up_part, "z")
    attended_grad = after(attended_grad, gate_part)
    qkv_width, branch_width = qkv_cols // plane, model_width // plane
    dense_cols = qkv_width + branch_width
    (back_cols,) = run_kernel(
        attend_back_kernel,
        6,
        at,
        (
            attended_grad,
            probs,
            queries,
            keys_rot,
            values_b,
            cosine_all,
            sine_all,
            branch_grad,
        ),
        [((plane, length + 16, dense_cols), bf16)],
        56,
    )
    tokens_grad, gain_one_grad = run_kernel(
        first_back_kernel,
        5,
        at,
        (back_cols, qkv_w, tokens, gain_one, resid_grad),
        [((length, model_width), bf16), ((1, model_width), f32)],
        24,
    )

    both = jnp.concatenate(
        lax.optimization_barrier((attended, first_in, last_y, last_x))[:2], axis=0
    )
    both_sides = plane_sides(both)
    narrow_part = jnp.concatenate(
        [router_acc[:, :experts_all], gain_one_grad.T, gain_two_grad.T], axis=1
    )
    narrow_cols = -(-narrow_part.shape[1] // owners) * owners
    narrow_part = jnp.pad(narrow_part, ((0, 0), (0, narrow_cols - narrow_part.shape[1])))
    narrow_part = jnp.transpose(
        narrow_part.reshape(depth, 2, 2, shard_rows, owners, narrow_cols // owners),
        (1, 2, 4, 0, 3, 5),
    ).reshape(plane, depth, shard_rows * narrow_cols // owners)
    narrow_len = narrow_part.shape[2]
    narrow_rows = -(-narrow_len // dense_cols)
    each_rows = -(-narrow_rows // 4) * 4
    narrow_part = jnp.pad(
        narrow_part, ((0, 0), (0, 0), (0, each_rows * dense_cols - narrow_len))
    ).reshape(plane, depth * each_rows, dense_cols)
    narrow_part = jnp.pad(
        narrow_part.astype(bf16), ((0, 0), (0, 16 - depth * each_rows), (0, 0))
    )
    back_cols = lax.dynamic_update_slice(back_cols, narrow_part, (0, length, 0))
    back_cols = exchange(after(back_cols, down_sum), PLANE)
    shares = run_kernel(
        functools.partial(mixture_kernel, capacity, groups),
        10,
        at,
        (ids_all, after(gated[0], *both_sides), *gated[1:], down_w),
        [((length, model_width), bf16)] * plane,
        56,
    )
    sides, shares = lax.optimization_barrier((both_sides, shares))
    both_corner = plane_corner(sides, (back_cols,))
    both_pieces = plane_pieces(both, both_sides, both_corner)
    def placed(total):
        total = exchange(total, ("y", "c"))
        return total.reshape(local_count, shard_rows, hidden_width).astype(f32)

    kept_rows = -(-narrow_rows // 16) * 16
    wide_rows = local_count * shard_rows
    dense_shape = (depth, wide_rows + kept_rows, dense_cols)
    dense_part = pl.pallas_call(
        dense_grad_kernel,
        out_shape=jax.ShapeDtypeStruct(dense_shape, bf16),
        in_specs=[SCALARS, WHOLE] + [IN_HBM] * 8,
        out_specs=WHOLE,
        scratch_shapes=[
            pltpu.VMEM((plane, 2 * length, model_width), bf16),
            pltpu.SemaphoreType.DMA((plane,)),
        ],
        cost_estimate=cost(8),
        compiler_params=pltpu.CompilerParams(vmem_limit_bytes=32 * 2**20),
    )(at, back_cols, *both_pieces)
    dense_part, down_sum, gate_sum, up_sum = lax.optimization_barrier(
        (dense_part, down_sum, gate_sum, up_sum)
    )
    down_grad, gate_grad = placed(down_sum), placed(gate_sum)
    dense_sum = scatter_sum(dense_part.reshape(-1, dense_cols), "z")
    mixed = [over_core(near, far) for near, far in zip(shares[:4], shares[4:])]
    early = early_sums(mixed[1], mixed[2])
    first, down_grad, gate_grad = lax.optimization_barrier(
        (corner_first(mixed[3]), down_grad, gate_grad)
    )
    last, up_grad = lax.optimization_barrier(
        (corner_last(mixed[1], mixed[2], first)[:2], placed(up_sum))
    )
    wide_sum = dense_sum[: local_count * shard_rows].reshape(2, 2, 1, shard_rows, dense_cols)
    wide_sum = jnp.broadcast_to(wide_sum, (2, 2, owners, shard_rows, dense_cols)).reshape(
        plane, shard_rows, dense_cols
    )
    narrow_sum = dense_sum[local_count * shard_rows :][:narrow_rows]
    narrow_sum = jnp.broadcast_to(narrow_sum[None], (plane, narrow_rows, dense_cols))
    pad_rows = -(shard_rows + narrow_rows) % 16
    padding = jnp.zeros((plane, pad_rows, dense_cols), bf16)
    dense_sum = exchange(jnp.concatenate([wide_sum, narrow_sum, padding], axis=1), PLANE)
    dense_sum, early, last = lax.optimization_barrier((dense_sum, early, last))
    mixture = jnp.concatenate(
        [left.astype(f32) + right.astype(f32) for left, right in zip(early, last)], axis=0
    )
    block_out = (resid + (mixture + mixed[0].astype(f32))).astype(bf16)

    query_grad, key_grad, value_grad, output_grad = run_kernel(
        finish_kernel,
        2,
        at,
        (dense_sum,),
        [
            ((shard_rows, q_cols), f32),
            ((shard_rows, kv_cols), f32),
            ((shard_rows, kv_cols), f32),
            ((shard_rows, model_width), f32),
        ],
    )
    narrow_sum = dense_sum[:, shard_rows : shard_rows + narrow_rows].reshape(
        2, 2, owners, narrow_rows * dense_cols
    )
    narrow_sum = narrow_sum[y, c, :, :narrow_len].reshape(owners, shard_rows, -1)
    narrow_sum = jnp.moveaxis(narrow_sum, 0, 1).reshape(shard_rows, narrow_cols).astype(f32)

    return (
        block_out,
        tokens_grad,
        narrow_sum[:, experts_all],
        query_grad,
        key_grad,
        value_grad,
        output_grad,
        narrow_sum[:, experts_all + 1],
        narrow_sum[:, :experts_all],
        gate_grad,
        up_grad,
        jnp.swapaxes(down_grad, 1, 2),
    )


def solution(mesh):
    groups, owners = mesh.shape["dp"], mesh.shape["expert"]
    grid = jax.sharding.Mesh(
        mesh.devices.reshape(groups // 4, 2, 2, owners), ("z", "y", "c", "x")
    )
    rows = P(("z", "y", "c", "x"), None)
    shard, shard_rows = P(GROUP), P(GROUP, None)
    expert = P("x", None, None)
    return jax.shard_map(
        local_pairs if owners == 2 else local_wide,
        mesh=grid,
        in_specs=(
            rows,
            shard,
            shard_rows,
            shard_rows,
            shard_rows,
            shard_rows,
            shard,
            shard_rows,
            expert,
            expert,
            expert,
            rows,
            P(("z", "y", "c", "x")),
            rows,
        ),
        out_specs=(
            rows,
            rows,
            shard,
            shard_rows,
            shard_rows,
            shard_rows,
            shard_rows,
            shard,
            shard_rows,
            P("x", GROUP, None),
            P("x", GROUP, None),
            P("x", None, GROUP),
        ),
        check_vma=False,
    )
```
